32 devices in a mesh: seq: 8 (over z, y), fsdp: 4 (over x, core).
Axes of the slice: x: 2, y: 2, z: 4, core: 2. Of those that a mesh axis runs over, the one named last changes fastest.
Arguments:
- tokens: bfloat16 [65536, 1280], P(('seq', 'fsdp')), may hold values from -6 to 6
- input_mask: int32 [65536], P(('seq', 'fsdp')), may hold values from 0 to 1
- doc_lengths: int32 [129], replicated, may hold values from 1 to 1022, as said below
- cotangent: bfloat16 [65536, 1280], P(('seq', 'fsdp')), may hold values from -6 to 6
- w_in: float32 [1280, 640], P('fsdp'), may hold values from -0.15625 to 0.15625
- w_conv: float32 [3200, 640], P('fsdp'), may hold values from -0.109375 to 0.109375
- w_out: float32 [640, 1280], P('fsdp'), may hold values from -0.25 to 0.25
- norm_params: float32 [2, 2560], replicated, may hold values from -0.6 to 2.3, as said below
- row_in: float32 [1280], P('fsdp'), may hold values from 6160.384 to 24641.535
- col_in: float32 [640], replicated, may hold values from 6160.384 to 24641.535
- row_conv: float32 [3200], P('fsdp'), may hold values from 6160.384 to 24641.535
- col_conv: float32 [640], replicated, may hold values from 6160.384 to 24641.535
- row_out: float32 [640], P('fsdp'), may hold values from 6160.384 to 24641.535
- col_out: float32 [1280], replicated, may hold values from 6160.384 to 24641.535
- norm_second: float32 [2, 2560], replicated, may hold values from 4915.2 to 19660.8
Outputs:
- block_out: bfloat16 [65536, 1280], P(('seq', 'fsdp'))
- input_grad: float32 [65536, 1280], P(('seq', 'fsdp'))
- grad_in: float32 [1280, 640], P('fsdp')
- grad_conv: float32 [3200, 640], P('fsdp')
- grad_out: float32 [640, 1280], P('fsdp')
- new_in: float32 [1280, 640], P('fsdp')
- new_conv: float32 [3200, 640], P('fsdp')
- new_out: float32 [640, 1280], P('fsdp')
- row_in_new: float32 [1280], P('fsdp')
- col_in_new: float32 [640], replicated
- row_conv_new: float32 [3200], P('fsdp')
- col_conv_new: float32 [640], replicated
- row_out_new: float32 [640], P('fsdp')
- col_out_new: float32 [1280], replicated
- norm_grads: float32 [2, 2560], replicated
- norm_second_new: float32 [2, 2560], replicated
- norm_new: float32 [2, 2560], replicated
The draws below stay inside these ranges and needn't reach their ends.
Inputs may be any that keep to these rules, and one draw needn't show every extreme that they name: `doc_lengths`: the proteins lie end to end and fill all 65536 tokens; each aligned run of 512 tokens holds exactly one protein end before its last token, and the last run one more at its end. `norm_params`: row 0 positive gains, row 1 shifts.
All inputs are finite; a program needn't handle non-finite values.
Results may differ from the reference program's by a relative error of at most 0.0095.
Values may be sent and summed in bfloat16 or wider, within the bound.
No kernel may reach another device: no remote copies, remote signals or barrier semaphores. Data moves between devices by JAX's collectives and lax.ppermute only.
A program may use at most 192 MiB of HBM per device.

```python
import math
import jax
import jax.numpy as jnp
from jax import lax

D = 1280
INNER = 640
KERNEL_TAPS = 5
DILATION_STEP = 128
SPAN = 512
STEP = 10
TOKENS = 65536


def draw_input_mask(key, part):
    key = jax.random.fold_in(key, 11)
    positions = jnp.arange(TOKENS, dtype=jnp.int32)
    threshold = 300 + 600 * positions // TOKENS
    random_draws = jax.random.randint(key, (TOKENS,), 0, 1000, dtype=jnp.int32)
    return (random_draws < threshold).astype(jnp.int32)


def draw_doc_lengths(key, part):
    key = jax.random.fold_in(key, 23)
    run_count = TOKENS // SPAN
    key_cuts, key_chosen = jax.random.split(key)
    cut_points = jax.random.randint(key_cuts, (run_count,), 1, SPAN, dtype=jnp.int32)
    chosen = jax.random.randint(key_chosen, (), 0, run_count - 1, dtype=jnp.int32)
    cut_points = cut_points.at[chosen].set(1)
    cut_points = cut_points.at[chosen + 1].set(SPAN - 1)
    cut_places = jnp.arange(run_count, dtype=jnp.int32) * SPAN + cut_points
    boundaries = jnp.concatenate([jnp.zeros((1,), jnp.int32), cut_places, jnp.full((1,), TOKENS, jnp.int32)])
    return boundaries[1:] - boundaries[:-1]


def ramp_gains(key, low_end):
    fraction = jnp.concatenate([jnp.arange(D, dtype=jnp.float32) / D, jnp.arange(INNER, dtype=jnp.float32) / INNER, jnp.arange(INNER, dtype=jnp.float32) / INNER])
    jitter = jax.random.uniform(key, (D + 2 * INNER,), jnp.float32, 0.85, 1.15)
    return (low_end + fraction) * jitter


def draw_norm_params(key, part):
    key = jax.random.fold_in(key, 37)
    key_gain, key_shift = jax.random.split(key)
    gains = ramp_gains(key_gain, 0.5)
    tap_shifts = jnp.clip(0.2 * jax.random.normal(key_shift, (D + 2 * INNER,), jnp.float32), -0.6, 0.6)
    return jnp.stack([gains, tap_shifts]).astype(jnp.float32)


def level_of(own_key, extent, cuts, smallest, largest):
    loudness, own = 1.0, jax.random.fold_in(own_key, 6)
    for position, shards_of in cuts:
        draws = jnp.exp(jax.random.uniform(jax.random.fold_in(own, position), (shards_of,), jnp.float32, smallest / len(cuts), largest / len(cuts)))
        loudness = loudness * jnp.repeat(draws, extent[position] // shards_of).reshape([-1 if axis == position else 1 for axis in range(len(extent))])
    return loudness


def normal_values(key, extent, deviation, most, cuts=(), kind=jnp.bfloat16):
    gain = level_of(key, extent, cuts, -0.22, 0.18) if cuts else 1.0
    drawn = jax.random.normal(key, extent, jnp.float32) * deviation * gain
    return jnp.minimum(jnp.maximum(drawn, -most), most).astype(kind)


def setup_inputs(seed: int = 0) -> dict:
    keys = jax.random.split(jax.random.key(seed), 16)
    tokens = normal_values(keys[0], (TOKENS, D), 1.0, 6.0, ((0, 32),))
    input_mask = draw_input_mask(jax.random.fold_in(keys[15], 71), 0)
    doc_lengths = draw_doc_lengths(jax.random.fold_in(keys[15], 71), 0)
    cotangent = normal_values(keys[3], (TOKENS, D), 1.0, 6.0, ((0, 32),))
    w_in = normal_values(keys[4], (D, INNER), D ** -0.5, 0.15625, ((0, 4),), jnp.float32)
    w_conv = normal_values(keys[5], (KERNEL_TAPS * INNER, INNER), (KERNEL_TAPS * INNER) ** -0.5, 0.109375, ((0, 4),), jnp.float32)
    w_out = normal_values(keys[6], (INNER, D), INNER ** -0.5, 0.25, ((0, 4),), jnp.float32)
    norm_params = draw_norm_params(jax.random.fold_in(keys[15], 71), 0)
    row_in = jnp.clip(jnp.exp(math.log(24641.535) - 1.3862944 * jax.random.uniform(keys[8], (D,), jnp.float32) ** level_of(keys[8], (D,), ((0, 4),), -0.2, 0.2)), 6160.384, 24641.535)
    col_in = jnp.clip(jnp.exp(jax.random.uniform(keys[9], (INNER,), jnp.float32, math.log(6160.384), math.log(24641.535))), 6160.384, 24641.535)
    row_conv = jnp.clip(jnp.exp(math.log(24641.535) - 1.3862944 * jax.random.uniform(keys[10], (KERNEL_TAPS * INNER,), jnp.float32) ** level_of(keys[10], (KERNEL_TAPS * INNER,), ((0, 4),), -0.2, 0.2)), 6160.384, 24641.535)
    col_conv = jnp.clip(jnp.exp(jax.random.uniform(keys[11], (INNER,), jnp.float32, math.log(6160.384), math.log(24641.535))), 6160.384, 24641.535)
    row_out = jnp.clip(jnp.exp(math.log(24641.535) - 1.3862944 * jax.random.uniform(keys[12], (INNER,), jnp.float32) ** level_of(keys[12], (INNER,), ((0, 4),), -0.2, 0.2)), 6160.384, 24641.535)
    col_out = jnp.clip(jnp.exp(jax.random.uniform(keys[13], (D,), jnp.float32, math.log(6160.384), math.log(24641.535))), 6160.384, 24641.535)
    norm_second = jnp.clip(jnp.exp(jax.random.uniform(keys[14], (2, D + 2 * INNER), jnp.float32, math.log(4915.2), math.log(19660.8))), 4915.2, 19660.8)
    return {"tokens": tokens, "input_mask": input_mask, "doc_lengths": doc_lengths, "cotangent": cotangent, "w_in": w_in, "w_conv": w_conv, "w_out": w_out, "norm_params": norm_params, "row_in": row_in, "col_in": col_in, "row_conv": row_conv, "col_conv": col_conv, "row_out": row_out, "col_out": col_out, "norm_second": norm_second}


@jax.custom_vjp
def low(v):
    return lax.optimization_barrier(v.astype(jnp.bfloat16)).astype(jnp.float32)

@jax.custom_vjp
def low_back(v):
    return v

def low_keep(v):
    return (low(v), None)

def low_pass(kept, grad):
    return (grad,)

def back_keep(v):
    return (v, None)

def back_low(kept, grad):
    return (low(grad),)
low.defvjp(low_keep, low_pass)
low_back.defvjp(back_keep, back_low)
EPSILON = 1e-05
PRECISE = lax.Precision.HIGHEST

def layer_norm(values, gain_vec, shift_vec):
    mean_val = lax.optimization_barrier(jnp.mean(values, axis=-1, keepdims=True))
    centered = values - mean_val
    variance = lax.optimization_barrier(jnp.mean(centered * centered, axis=-1, keepdims=True))
    return centered * lax.rsqrt(variance + EPSILON) * gain_vec + shift_vec

def gelu_norm(values, gain_vec, shift_vec):
    return jax.nn.gelu(layer_norm(values, gain_vec, shift_vec), approximate=False)

def forward(tokens_f32, w_in, w_conv, w_out, norm_params, live_rows, doc_id):
    gain_a = norm_params[0, :D]
    shift_a = norm_params[1, :D]
    gain_b = norm_params[0, D:D + INNER]
    shift_b = norm_params[1, D:D + INNER]
    gain_c = norm_params[0, D + INNER:]
    shift_c = norm_params[1, D + INNER:]
    low_in = low(w_in)
    low_conv = low(w_conv)
    low_out = low(w_out)
    block_len = min(4096, TOKENS)
    block_count = TOKENS // block_len
    reach_row_count = 2 * DILATION_STEP
    tap_offsets = [(tap_index - (KERNEL_TAPS - 1) // 2) * DILATION_STEP for tap_index in range(KERNEL_TAPS)]

    def first_half(pieces):
        token_block, live_block = pieces
        hidden_a = low(gelu_norm(token_block, gain_a, shift_a))
        pre_inner = low_back(jnp.dot(hidden_a, low_in, precision=PRECISE))
        return low(gelu_norm(pre_inner, gain_b, shift_b) * live_block[:, None])
    token_blocks = tokens_f32.reshape(block_count, block_len, D)
    live_blocks = live_rows.reshape(block_count, block_len)
    moved = lax.map(jax.checkpoint(first_half), (token_blocks, live_blocks))
    moved = moved.reshape(TOKENS, INNER)
    padded = jnp.pad(moved, ((reach_row_count, reach_row_count), (0, 0)))
    padded_ids = jnp.pad(doc_id, (reach_row_count, reach_row_count), constant_values=-1)

    def second_half(pieces):
        token_block, block_index = pieces
        begin = (block_index * block_len).astype(jnp.int32)
        window = lax.dynamic_slice_in_dim(padded, begin, block_len + 2 * reach_row_count, 0)
        window_ids = lax.dynamic_slice_in_dim(padded_ids, begin, block_len + 2 * reach_row_count, 0)
        center_ids = window_ids[reach_row_count:reach_row_count + block_len]
        columns = []
        for offset in tap_offsets:
            lower = reach_row_count + offset
            same_doc = window_ids[lower:lower + block_len] == center_ids
            columns.append(jnp.where(same_doc[:, None], window[lower:lower + block_len], jnp.zeros_like(window[:block_len])))
        conv_out = low_back(jnp.dot(jnp.concatenate(columns, axis=1), low_conv, precision=PRECISE))
        hidden_c = low(gelu_norm(conv_out, gain_c, shift_c))
        return token_block + jnp.dot(hidden_c, low_out, precision=PRECISE)
    outputs = lax.map(jax.checkpoint(second_half), (token_blocks, jnp.arange(block_count, dtype=jnp.int32)))
    return outputs.reshape(TOKENS, D)

def factored(weight, grad, row_state, col_state, step_rate, decay_rate):
    squares = grad * grad + 1e-30
    row_new = decay_rate * row_state + (1.0 - decay_rate) * lax.optimization_barrier(jnp.mean(squares, axis=1))
    col_new = decay_rate * col_state + (1.0 - decay_rate) * lax.optimization_barrier(jnp.mean(squares, axis=0))
    estimate = row_new[:, None] * col_new[None, :] / jnp.mean(row_new)
    return (weight - step_rate * grad * lax.rsqrt(estimate), row_new, col_new)

def reference(tokens, input_mask, doc_lengths, cotangent, w_in, w_conv, w_out, norm_params, row_in, col_in, row_conv, col_conv, row_out, col_out, norm_second):
    positions = jnp.arange(TOKENS, dtype=jnp.int32)
    doc_ends = jnp.cumsum(doc_lengths).astype(jnp.int32)
    doc_id = jnp.searchsorted(doc_ends, positions, side='right').astype(jnp.int32)
    live_rows = input_mask.astype(jnp.float32)
    tokens_f32 = tokens.astype(jnp.float32)

    def run_block(tok_arg, in_arg, conv_arg, output_argument, norm_arg):
        return forward(tok_arg, in_arg, conv_arg, output_argument, norm_arg, live_rows, doc_id)
    result, pull_back = jax.vjp(run_block, tokens_f32, w_in, w_conv, w_out, norm_params)
    input_grad, grad_in, grad_conv, grad_out, norm_grads = pull_back(cotangent.astype(jnp.float32))
    block_out = result.astype(jnp.bfloat16)
    decay_rate = 1.0 - STEP ** (-0.8)
    new_in, row_in_new, col_in_new = factored(w_in, grad_in, row_in, col_in, 0.5 / D ** 0.5, decay_rate)
    new_conv, row_conv_new, col_conv_new = factored(w_conv, grad_conv, row_conv, col_conv, 0.5 / (KERNEL_TAPS * INNER) ** 0.5, decay_rate)
    new_out, row_out_new, col_out_new = factored(w_out, grad_out, row_out, col_out, 0.5 / INNER ** 0.5, decay_rate)
    norm_second_new = decay_rate * norm_second + (1.0 - decay_rate) * (norm_grads * norm_grads + 1e-30)
    norm_new = norm_params - 0.2 * norm_grads * lax.rsqrt(norm_second_new)
    return (block_out, input_grad, grad_in, grad_conv, grad_out, new_in, new_conv, new_out, row_in_new, col_in_new, row_conv_new, col_conv_new, row_out_new, col_out_new, norm_grads, norm_second_new, norm_new)
```

```python
import functools
import math

import jax
import jax.numpy as jnp
from jax import lax
from jax.experimental import pallas as pl
from jax.experimental.pallas import tpu as pltpu
from jax.sharding import PartitionSpec as P

D = 1280
INNER = 640
KERNEL_TAPS = 5
DILATION_STEP = 128
STEP = 10
EPSILON = 1e-05
DECAY = 1.0 - STEP ** (-0.8)

REACH = (KERNEL_TAPS - 1) // 2 * DILATION_STEP
MID = (KERNEL_TAPS - 1) // 2
F32 = jnp.float32
BF16 = jnp.bfloat16
SUB, LANE = 16, 128
AXES = ("seq", "fsdp")
NT = (((1,), (1,)), ((), ()))
TN = (((0,), (0,)), ((), ()))
NN = (((1,), (0,)), ((), ()))
VMEM_LIMIT = 58 * 1024 * 1024


def call(kernel, grid, in_specs, out_specs, out_shape, scratch=(), flops=0, moved=0, scalars=None):
    params = pltpu.CompilerParams(
        vmem_limit_bytes=VMEM_LIMIT, dimension_semantics=("arbitrary",) * len(grid)
    )
    return pl.pallas_call(
        kernel,
        grid=grid,
        in_specs=in_specs,
        out_specs=out_specs,
        out_shape=out_shape,
        scratch_shapes=list(scratch),
        compiler_params=params,
        cost_estimate=pl.CostEstimate(flops=flops, bytes_accessed=moved, transcendentals=0),
    )


def shape(dims, dtype):
    return jax.ShapeDtypeStruct(dims, dtype)


def rows_spec(tile, width):
    return pl.BlockSpec((tile, width), lambda i: (i, 0))


def whole(*dims):
    return pl.BlockSpec(dims, lambda *_: (0,) * len(dims))


ANY = pl.BlockSpec(memory_space=pl.ANY)
SMEM = pl.BlockSpec(memory_space=pltpu.SMEM)


def normed(values):
    width = values.shape[-1]
    mean = jnp.sum(values, axis=-1, keepdims=True) * (1.0 / width)
    centered = values - mean
    variance = jnp.sum(centered * centered, axis=-1, keepdims=True) * (1.0 / width)
    rstd = lax.rsqrt(variance + EPSILON)
    return centered * rstd, rstd


def gelu_and_slope(y):
    cdf = 0.5 * lax.erf(y * math.sqrt(0.5)) + 0.5
    pdf = jnp.exp(y * y * -0.5) * (1.0 / math.sqrt(2.0 * math.pi))
    return y * cdf, cdf + y * pdf


def norm_back(dy, xhat, rstd, gain):
    width = dy.shape[-1]
    dxhat = dy * gain
    mean_d = jnp.sum(dxhat, axis=-1, keepdims=True) * (1.0 / width)
    mean_dx = jnp.sum(dxhat * xhat, axis=-1, keepdims=True) * (1.0 / width)
    return (dxhat - mean_d - xhat * mean_dx) * rstd


def fold(values):
    total = values[0:8]
    for k in range(8, values.shape[0], 8):
        total = total + values[k : k + 8]
    return total


def row_loop(count, step, body, init, unroll=2):
    def at(i, carry):
        return body(pl.ds(pl.multiple_of(i * step, step), step), carry)

    return lax.fori_loop(0, count // step, at, init, unroll=unroll)


def write_sums(out_ref, acc_ref, sums, step, steps):
    width = out_ref.shape[-1]

    @pl.when(step == 0)
    def _():
        acc_ref[...] = jnp.zeros_like(acc_ref)

    acc_ref[0:8, :] += sums[0]
    acc_ref[8:16, :] += sums[1]

    @pl.when(step == steps - 1)
    def _():
        out_ref[0:1, :] = jnp.sum(acc_ref[0:8, :], axis=0, keepdims=True)
        out_ref[1:2, :] = jnp.sum(acc_ref[8:16, :], axis=0, keepdims=True)


def run_copies(copies):
    for copy in copies:
        copy.start()
    for copy in copies:
        copy.wait()


def norm_a_kernel(tok_ref, np_ref, hid_ref, slope_ref):
    gain, shift = np_ref[0:1, 0:D], np_ref[1:2, 0:D]

    def body(rows, carry):
        xhat, _ = normed(tok_ref[rows, :].astype(F32))
        hidden, slope = gelu_and_slope(xhat * gain + shift)
        hid_ref[rows, :] = hidden.astype(BF16)
        slope_ref[rows, :] = slope.astype(BF16)
        return carry

    row_loop(tok_ref.shape[0], SUB, body, 0)


def in_kernel(pieces, place_ref, ends_ref, hid_ref, live_ref, np_ref, *refs):
    piece_refs = refs[:pieces]
    pre_ref, mov_ref, slope_ref, mask_ref, first_ref, last_ref, w_ref, sem = refs[pieces:]
    step, steps = pl.program_id(0), pl.num_programs(0)
    tile = hid_ref.shape[0]
    rows_each = w_ref.shape[0] // pieces

    @pl.when(step == 0)
    def _():
        me = place_ref[0]
        run_copies(
            [
                pltpu.make_async_copy(
                    piece,
                    w_ref.at[pl.ds(pl.multiple_of((me ^ k) * rows_each, SUB), rows_each), :],
                    sem.at[k],
                )
                for k, piece in enumerate(piece_refs)
            ]
        )

    pre_ref[...] = lax.dot_general(hid_ref[...], w_ref[...], NN, preferred_element_type=F32)

    first = place_ref[1] + step * tile
    at = (first + lax.broadcasted_iota(jnp.int32, (tile, 1), 0)).astype(F32)
    ends = ends_ref[...]
    begin = jnp.max(jnp.where(ends <= at, ends, 0.0), axis=1, keepdims=True)
    end = jnp.min(jnp.where(ends > at, ends, 1e9), axis=1, keepdims=True)
    lanes = lax.broadcasted_iota(jnp.int32, (tile, 8), 1)
    offsets = (lanes - MID) * DILATION_STEP
    there = at + offsets.astype(F32)
    same = jnp.where((there >= begin) & (there < end), 1.0, 0.0)
    mask_ref[...] = jnp.where(lanes == MID, live_ref[...], same)

    gain, shift = np_ref[0:1, D : D + INNER], np_ref[1:2, D : D + INNER]

    def body(rows, carry):
        xhat, _ = normed(pre_ref[rows, :])
        hidden, slope = gelu_and_slope(xhat * gain + shift)
        mov_ref[rows, :] = (hidden * live_ref[rows, :]).astype(BF16)
        slope_ref[rows, :] = slope.astype(BF16)
        return carry

    row_loop(tile, SUB, body, 0)

    @pl.when(step == 0)
    def _():
        first_ref[...] = mov_ref[0:REACH, :]

    @pl.when(step == steps - 1)
    def _():
        last_ref[...] = mov_ref[tile - REACH :, :]


def load_window(low, mid, high, ext_ref, sem):
    rows = mid.shape[0]
    return [
        pltpu.make_async_copy(low, ext_ref.at[0:REACH, :], sem.at[0]),
        pltpu.make_async_copy(mid, ext_ref.at[REACH : REACH + rows, :], sem.at[1]),
        pltpu.make_async_copy(high, ext_ref.at[REACH + rows : 2 * REACH + rows, :], sem.at[2]),
    ]


def fill_taps(taps_ref, ext_ref, mask_ref, start):
    tile = taps_ref.shape[0]
    for j in range(KERNEL_TAPS):
        rows = pl.ds(pl.multiple_of(start + j * DILATION_STEP, DILATION_STEP), tile)
        picked = ext_ref[rows, :]
        if j != MID:
            picked = picked * mask_ref[:, j : j + 1].astype(BF16)
        taps_ref[:, j * INNER : (j + 1) * INNER] = picked


def conv_kernel(pieces, place_ref, low_ref, mov_ref, high_ref, mask_ref, cot_ref, np_ref, *refs):
    conv_pieces, out_pieces = refs[:pieces], refs[pieces : 2 * pieces]
    (hid_ref, dconv_ref, first_ref, last_ref, sums_ref) = refs[2 * pieces : 2 * pieces + 5]
    ext_ref, wc_ref, wo_ref, taps_ref, pre_ref, dh_ref, acc_ref, sem = refs[2 * pieces + 5 :]
    step, steps = pl.program_id(0), pl.num_programs(0)
    tile = taps_ref.shape[0]

    @pl.when(step == 0)
    def _():
        me = place_ref[0]
        copies = load_window(low_ref, mov_ref, high_ref, ext_ref, sem)
        for n, (full, parts) in enumerate(((wc_ref, conv_pieces), (wo_ref, out_pieces))):
            each = full.shape[0] // pieces
            for k, piece in enumerate(parts):
                rows = pl.ds(pl.multiple_of((me ^ k) * each, SUB), each)
                copies.append(
                    pltpu.make_async_copy(piece, full.at[rows, :], sem.at[3 + n * pieces + k])
                )
        run_copies(copies)

    fill_taps(taps_ref, ext_ref, mask_ref, step * tile)
    pre_ref[...] = lax.dot_general(taps_ref[...], wc_ref[...], NN, preferred_element_type=F32)
    dh_ref[...] = lax.dot_general(cot_ref[...], wo_ref[...], NT, preferred_element_type=F32)
    gain, shift = np_ref[0:1, D + INNER :], np_ref[1:2, D + INNER :]

    def body(rows, carry):
        xhat, rstd = normed(pre_ref[rows, :])
        hidden, slope = gelu_and_slope(xhat * gain + shift)
        hid_ref[rows, :] = hidden.astype(BF16)
        dy = dh_ref[rows, :] * slope
        dconv_ref[rows, :] = norm_back(dy, xhat, rstd, gain).astype(BF16)
        return carry[0] + fold(dy * xhat), carry[1] + fold(dy)

    zero = jnp.zeros((8, INNER), F32)
    sums = row_loop(tile, SUB, body, (zero, zero))
    write_sums(sums_ref, acc_ref, sums, step, steps)

    @pl.when(step == 0)
    def _():
        first_ref[...] = dconv_ref[0:REACH, :]

    @pl.when(step == steps - 1)
    def _():
        last_ref[...] = dconv_ref[tile - REACH :, :]


def put_tiles(ref, lead, first, value):
    blocks = value.shape[1] // LANE
    for g in range(value.shape[0] // SUB):
        for b in range(blocks):
            tile = value[g * SUB : (g + 1) * SUB, b * LANE : (b + 1) * LANE]
            ref[lead, first + g * blocks + b] = tile.astype(ref.dtype)


def split_by_owner(value, first_row, rows_each, core, keep_ref, send_ref, base):
    blocks = value.shape[1] // LANE
    unit = math.gcd(value.shape[0], rows_each)
    for m in range(value.shape[0] // unit):
        row = first_row + m * unit
        owner = lax.div(row, rows_each)
        first = base + lax.div(lax.rem(row, rows_each), SUB) * blocks
        part = value[m * unit : (m + 1) * unit, :]

        @pl.when(lax.rem(owner, 2) == core)
        def _(part=part, owner=owner, first=first):
            put_tiles(keep_ref, lax.div(owner, 2), first, part)

        @pl.when(lax.rem(owner, 2) != core)
        def _(part=part, owner=owner, first=first):
            put_tiles(send_ref, lax.div(owner, 2), first, part)


def grad_conv_kernel(rows_each, place_ref, low_ref, mov_ref, high_ref, mask_ref, d_ref, *refs):
    keep_ref, send_ref, ext_ref, lhs_ref, sem = refs
    tap = pl.program_id(0)
    rows = d_ref.shape[0]

    @pl.when(tap == 0)
    def _():
        run_copies(load_window(low_ref, mov_ref, high_ref, ext_ref, sem))
        keep_ref[...] = jnp.zeros_like(keep_ref)
        send_ref[...] = jnp.zeros_like(send_ref)

    lanes = lax.broadcasted_iota(jnp.int32, (rows, 8), 1)
    chosen = jnp.where((lanes == tap) & (tap != MID), mask_ref[...], 0.0)
    factor = jnp.sum(chosen, axis=1, keepdims=True) + jnp.where(tap == MID, 1.0, 0.0)
    start = pl.multiple_of(tap * DILATION_STEP, DILATION_STEP)
    lhs_ref[...] = ext_ref[pl.ds(start, rows), :] * factor.astype(BF16)
    grad = lax.dot_general(lhs_ref[...], d_ref[...], TN, preferred_element_type=F32)
    split_by_owner(grad, tap * INNER, rows_each, lax.rem(place_ref[0], 2), keep_ref, send_ref, 0)


def grad_plain_kernel(rows_each, place_ref, lhs_ref, rhs_ref, keep_ref, send_ref):
    keep_ref[...] = jnp.zeros_like(keep_ref)
    send_ref[...] = jnp.zeros_like(send_ref)
    grad = lax.dot_general(lhs_ref[...], rhs_ref[...], TN, preferred_element_type=F32)
    split_by_owner(grad, 0, rows_each, lax.rem(place_ref[0], 2), keep_ref, send_ref, 0)


def back_conv_kernel(
    pieces, place_ref, low_ref, d_ref, high_ref, mask_ref, pre_ref, slope_ref, np_ref, *refs
):
    conv_pieces = refs[:pieces]
    dpre_ref, sums_ref, ext_ref, wt_ref, taps_ref, dmov_ref, acc_ref, sem, wsem = refs[pieces:]
    step, steps = pl.program_id(0), pl.num_programs(0)
    tile = taps_ref.shape[0]

    @pl.when(step == 0)
    def _():
        me = place_ref[0]
        copies = load_window(low_ref, d_ref, high_ref, ext_ref, sem)
        each = KERNEL_TAPS * INNER // pieces
        unit = math.gcd(each, INNER)
        per = each // unit
        for k, piece in enumerate(conv_pieces):
            for m in range(per):
                row = ((me ^ k) * per + m) * unit
                tap = lax.div(row, INNER)
                lane = (KERNEL_TAPS - 1 - tap) * INNER
                target = wt_ref.at[
                    pl.ds(pl.multiple_of(lax.rem(row, INNER), SUB), unit),
                    pl.ds(pl.multiple_of(lane, LANE), INNER),
                ]
                source = piece.at[m * unit : (m + 1) * unit, :]
                copies.append(pltpu.make_async_copy(source, target, wsem.at[k * per + m]))
        run_copies(copies)

    fill_taps(taps_ref, ext_ref, mask_ref, step * tile)
    dmov_ref[...] = lax.dot_general(taps_ref[...], wt_ref[...], NT, preferred_element_type=F32)
    gain = np_ref[0:1, D : D + INNER]

    def body(rows, carry):
        xhat, rstd = normed(pre_ref[rows, :])
        live = mask_ref[rows, MID : MID + 1]
        dy = dmov_ref[rows, :] * live * slope_ref[rows, :].astype(F32)
        dpre_ref[rows, :] = norm_back(dy, xhat, rstd, gain).astype(BF16)
        return carry[0] + fold(dy * xhat), carry[1] + fold(dy)

    zero = jnp.zeros((8, INNER), F32)
    sums = row_loop(tile, SUB, body, (zero, zero))
    write_sums(sums_ref, acc_ref, sums, step, steps)


def back_a_kernel(pieces, place_ref, dpre_ref, tok_ref, slope_ref, cot_ref, np_ref, *refs):
    piece_refs = refs[:pieces]
    grad_ref, sums_ref, w_ref, dh_ref, acc_ref, sem = refs[pieces:]
    step, steps = pl.program_id(0), pl.num_programs(0)
    tile = dpre_ref.shape[0]
    rows_each = w_ref.shape[0] // pieces

    @pl.when(step == 0)
    def _():
        me = place_ref[0]
        run_copies(
            [
                pltpu.make_async_copy(
                    piece,
                    w_ref.at[pl.ds(pl.multiple_of((me ^ k) * rows_each, SUB), rows_each), :],
                    sem.at[k],
                )
                for k, piece in enumerate(piece_refs)
            ]
        )

    dh_ref[...] = lax.dot_general(dpre_ref[...], w_ref[...], NT, preferred_element_type=F32)
    gain = np_ref[0:1, 0:D]

    def body(rows, carry):
        xhat, rstd = normed(tok_ref[rows, :].astype(F32))
        dy = dh_ref[rows, :] * slope_ref[rows, :].astype(F32)
        back = norm_back(dy, xhat, rstd, gain)
        grad_ref[rows, :] = cot_ref[rows, :].astype(F32) + back
        return carry[0] + fold(dy * xhat), carry[1] + fold(dy)

    zero = jnp.zeros((8, D), F32)
    sums = row_loop(tile, SUB, body, (zero, zero))
    write_sums(sums_ref, acc_ref, sums, step, steps)


def out_kernel(pieces, place_ref, hid_ref, tok_ref, *refs):
    piece_refs = refs[:pieces]
    out_ref, w_ref, sem = refs[pieces:]
    rows_each = w_ref.shape[0] // pieces

    @pl.when(pl.program_id(0) == 0)
    def _():
        me = place_ref[0]
        run_copies(
            [
                pltpu.make_async_copy(
                    piece,
                    w_ref.at[pl.ds(pl.multiple_of((me ^ k) * rows_each, SUB), rows_each), :],
                    sem.at[k],
                )
                for k, piece in enumerate(piece_refs)
            ]
        )

    branch = lax.dot_general(hid_ref[...], w_ref[...], NN, preferred_element_type=F32)
    out_ref[...] = (tok_ref[...].astype(F32) + branch).astype(BF16)


COLS = ((0, INNER), (INNER, INNER), (2 * INNER, D))


def load_pieces(copies, mine, other, full_ref, y, z, sem, first):
    outer = mine.shape[0]
    for s in range(outer):
        slot = lax.rem(z - s + outer, outer)
        copies.append(pltpu.make_async_copy(mine.at[s], full_ref.at[y, slot], sem.at[first + s]))
        copies.append(
            pltpu.make_async_copy(
                other.at[s], full_ref.at[1 - y, slot], sem.at[first + outer + s]
            )
        )


def stats_kernel(place_ref, *refs):
    (in_m, in_o, conv_m, conv_o, out_m, out_o) = refs[0:6]
    states = refs[6:9]
    sums_a, sums_b, sums_c = refs[9:12]
    grads = refs[12:15]
    row_news = refs[15:18]
    pack_ref = refs[18]
    fulls = refs[19:22]
    sem = refs[22]
    y, z = place_ref[2], place_ref[3]
    copies = []
    count = 2 * in_m.shape[0]
    for k, (mine, other) in enumerate(((in_m, in_o), (conv_m, conv_o), (out_m, out_o))):
        load_pieces(copies, mine, other, fulls[k], y, z, sem, k * count)
    run_copies(copies)
    pack_ref[...] = jnp.zeros_like(pack_ref)
    pack_ref[0:2, 0:D] = sums_a[...]
    pack_ref[0:2, D : D + INNER] = sums_b[...]
    pack_ref[0:2, D + INNER :] = sums_c[...]
    for k, (lane0, width) in enumerate(COLS):
        blocks = width // LANE
        per = fulls[k].shape[2]
        full, grad_ref, row_ref, state = fulls[k], grads[k], row_news[k], states[k]

        def body(g, carry, full=full, grad_ref=grad_ref, row_ref=row_ref, state=state, per=per, blocks=blocks, width=width):
            rows = pl.ds(pl.multiple_of(g * SUB, SUB), SUB)
            cols, total = carry
            row_sum = jnp.zeros((SUB, LANE), F32)
            new_cols = []
            for b in range(blocks):
                n = g * blocks + b
                half = lax.div(n, full.shape[1] * per)
                rest = lax.rem(n, full.shape[1] * per)
                value = full[half, lax.div(rest, per), lax.rem(rest, per)].astype(F32)
                grad_ref[rows, b * LANE : (b + 1) * LANE] = value
                square = value * value + 1e-30
                row_sum = row_sum + square
                new_cols.append(cols[b] + fold(square))
            mean = jnp.sum(row_sum, axis=1, keepdims=True) * (1.0 / width)
            row_new = DECAY * state[rows, :] + (1.0 - DECAY) * mean
            row_ref[rows, :] = row_new
            return tuple(new_cols), total + fold(row_new)

        zero = tuple(jnp.zeros((8, LANE), F32) for _ in range(blocks))
        cols, total = lax.fori_loop(
            0, grad_ref.shape[0] // SUB, body, (zero, jnp.zeros((8, 1), F32))
        )
        for b in range(blocks):
            lane = lane0 + b * LANE
            pack_ref[2:3, lane : lane + LANE] = jnp.sum(cols[b], axis=0, keepdims=True)
        sum_all = jnp.sum(total, axis=0, keepdims=True)
        lanes = lax.broadcasted_iota(jnp.int32, (1, LANE), 1)
        pack_ref[3:4, 0:LANE] += jnp.where(lanes == k, sum_all, 0.0)


def update_kernel(copies_of, pack_ref, np_ref, second_ref, *refs):
    cols_state, grads, rows_new, weights = refs[0:3], refs[3:6], refs[6:9], refs[9:12]
    news, cols_new = refs[12:15], refs[15:18]
    ngrad_ref, nsecond_ref, nnew_ref = refs[18:21]
    grad = pack_ref[0:2, :]
    second = DECAY * second_ref[...] + (1.0 - DECAY) * (grad * grad + 1e-30)
    ngrad_ref[...] = grad
    nsecond_ref[...] = second
    nnew_ref[...] = np_ref[...] - 0.2 * grad * lax.rsqrt(second)
    fans = (D, KERNEL_TAPS * INNER, INNER)
    for k, (lane0, width) in enumerate(COLS):
        fan = fans[k]
        mean_square = pack_ref[2:3, lane0 : lane0 + width] * (1.0 / (fan * copies_of))
        col_new = DECAY * cols_state[k][...] + (1.0 - DECAY) * mean_square
        cols_new[k][...] = col_new
        row_mean = pack_ref[3:4, k : k + 1] * (1.0 / (fan * copies_of))
        scaled = col_new / row_mean
        rate = 0.5 / fan**0.5
        weight, new, g_ref, row = weights[k], news[k], grads[k], rows_new[k]

        def body(rows, carry, weight=weight, new=new, g_ref=g_ref, row=row, scaled=scaled, rate=rate):
            step = g_ref[rows, :] * lax.rsqrt(row[rows, :] * scaled)
            new[rows, :] = weight[rows, :] - rate * step
            return carry

        row_loop(weight.shape[0], SUB, body, 0)


def permute(x, pairs):
    return lax.ppermute(x, AXES, pairs)


class Places:
    def __init__(self):
        self.seq, self.fsdp = lax.axis_size("seq"), lax.axis_size("fsdp")
        self.outer = self.seq // 2
        self.q = lax.axis_index("fsdp")
        s = lax.axis_index("seq")
        self.y, self.z = s % 2, s // 2
        self.core, self.x = self.q % 2, self.q // 2

    def pairs(self, move):
        found = []
        for s in range(self.seq):
            for f in range(self.fsdp):
                s2, f2 = move(s, f)
                found.append((s * self.fsdp + f, s2 * self.fsdp + f2))
        return found

    def flip_fsdp(self, x, bit):
        return permute(x, self.pairs(lambda s, f: (s, f ^ bit)))

    def flip_y(self, x):
        return permute(x, self.pairs(lambda s, f: (s ^ 1, f)))

    def shift_z(self, x, by):
        return permute(
            x, self.pairs(lambda s, f: (((s // 2 + by) % self.outer) * 2 + s % 2, f))
        )


def gather_pieces(piece, place):
    found = {0: piece}
    bit = place.fsdp // 2
    while bit:
        for k in list(found):
            found[k | bit] = place.flip_fsdp(found[k], bit)
        bit //= 2
    return [found[k] for k in range(place.fsdp)]


def pick(x, index):
    return lax.dynamic_index_in_dim(x, index, axis=0, keepdims=False)


def reduce_grad(keep, send, place):
    got = place.flip_fsdp(send, 1)
    bit, width = place.fsdp // 2, keep.shape[0]
    total, first = keep, got
    while width > 1:
        half = width // 2
        side = (place.q // bit) % 2
        shape_ = (2, half) + keep.shape[1:]
        total, first = total.reshape(shape_), first.reshape(shape_)
        away = pick(total, 1 - side).astype(F32) + pick(first, 1 - side).astype(F32)
        near = pick(total, side).astype(F32) + pick(first, side).astype(F32)
        got = place.flip_fsdp(away.astype(BF16), bit)
        total, first = near, got
        width, bit = half, bit // 2
    tiles = keep.shape[1]
    half = tiles // 2
    total = total.reshape((2, half) + keep.shape[2:])
    first = first.reshape((2, half) + keep.shape[2:])
    away = pick(total, 1 - place.y) + pick(first, 1 - place.y).astype(F32)
    near = pick(total, place.y) + pick(first, place.y).astype(F32)
    got = place.flip_y(away.astype(BF16))
    part = (near + got.astype(F32)).reshape((place.outer, half // place.outer) + keep.shape[2:])
    low = part.astype(BF16)
    mine = pick(part, place.z)
    for s in range(1, place.outer):
        mine = mine + place.shift_z(pick(low, (place.z + s) % place.outer), s).astype(F32)
    mine = mine.astype(BF16)
    line = jnp.stack([mine] + [place.shift_z(mine, s) for s in range(1, place.outer)])
    return line, place.flip_y(line)


def on_device(
    tokens, input_mask, doc_lengths, cotangent, w_in, w_conv, w_out, norm_params,
    row_in, col_in, row_conv, col_conv, row_out, col_out, norm_second,
):
    place = Places()
    rows = tokens.shape[0]
    pieces = place.fsdp
    split = place.outer * 2
    spots = jnp.stack(
        [place.q, (lax.axis_index("seq") * place.fsdp + place.q) * rows, place.y, place.z]
    ).astype(jnp.int32)
    docs = doc_lengths.shape[0]
    ends = jnp.pad(
        jnp.cumsum(doc_lengths).astype(F32), (0, -docs % LANE), constant_values=1e9
    ).reshape(1, -1)
    live = input_mask.astype(F32).reshape(rows, 1)

    in_pieces = gather_pieces(w_in.astype(BF16), place)
    out_pieces = gather_pieces(w_out.astype(BF16), place)
    conv_pieces = gather_pieces(w_conv.astype(BF16), place)

    tile_a, tile = 256, 512
    steps = rows // tile
    params_spec = whole(2, D + 2 * INNER)

    hidden_a, slope_a = call(
        norm_a_kernel,
        (rows // tile_a,),
        [rows_spec(tile_a, D), params_spec],
        [rows_spec(tile_a, D)] * 2,
        [shape((rows, D), BF16)] * 2,
        flops=40 * rows * D,
        moved=6 * rows * D,
    )(tokens, norm_params)

    dma = pltpu.SemaphoreType.DMA
    pre_inner, moved, slope_b, masks, m_first, m_last = call(
        functools.partial(in_kernel, pieces),
        (steps,),
        [SMEM, whole(*ends.shape), rows_spec(tile, D), rows_spec(tile, 1), params_spec]
        + [ANY] * pieces,
        [rows_spec(tile, INNER)] * 3
        + [rows_spec(tile, 8), whole(REACH, INNER), whole(REACH, INNER)],
        [
            shape((rows, INNER), F32),
            shape((rows, INNER), BF16),
            shape((rows, INNER), BF16),
            shape((rows, 8), F32),
            shape((REACH, INNER), BF16),
            shape((REACH, INNER), BF16),
        ],
        [pltpu.VMEM((D, INNER), BF16), dma((pieces,))],
        flops=2 * rows * D * INNER,
        moved=rows * (2 * D + 8 * INNER),
    )(spots, ends, hidden_a, live, norm_params, *in_pieces)

    total = place.seq * place.fsdp
    up = [(i, i + 1) for i in range(total - 1)]
    down = [(i + 1, i) for i in range(total - 1)]
    m_low, m_high = permute(m_last, up), permute(m_first, down)

    ext = pltpu.VMEM((rows + 2 * REACH, INNER), BF16)
    hidden_c, d_conv, d_first, d_last, sums_c = call(
        functools.partial(conv_kernel, pieces),
        (steps,),
        [SMEM, ANY, ANY, ANY, rows_spec(tile, 8), rows_spec(tile, D), params_spec]
        + [ANY] * (2 * pieces),
        [rows_spec(tile, INNER)] * 2
        + [whole(REACH, INNER), whole(REACH, INNER), whole(2, INNER)],
        [
            shape((rows, INNER), BF16),
            shape((rows, INNER), BF16),
            shape((REACH, INNER), BF16),
            shape((REACH, INNER), BF16),
            shape((2, INNER), F32),
        ],
        [
            ext,
            pltpu.VMEM((KERNEL_TAPS * INNER, INNER), BF16),
            pltpu.VMEM((INNER, D), BF16),
            pltpu.VMEM((tile, KERNEL_TAPS * INNER), BF16),
            pltpu.VMEM((tile, INNER), F32),
            pltpu.VMEM((tile, INNER), F32),
            pltpu.VMEM((16, INNER), F32),
            dma((3 + 2 * pieces,)),
        ],
        flops=2 * rows * INNER * (KERNEL_TAPS * INNER + D),
        moved=rows * (2 * D + 6 * INNER) + 2 * INNER * (KERNEL_TAPS * INNER + D),
    )(spots, m_low, moved, m_high, masks, cotangent, norm_params, *conv_pieces, *out_pieces)
    d_low, d_high = permute(d_last, up), permute(d_first, down)

    def tiles_of(weight):
        count = weight.shape[0] // SUB * (weight.shape[1] // LANE)
        return count + -count % split

    shards = place.fsdp // 2

    def halves(weight):
        dims = (shards, tiles_of(weight), SUB, LANE)
        return [shape(dims, F32), shape(dims, BF16)], [whole(*dims)] * 2

    out_shapes, out_specs = halves(w_conv)
    keep_conv, send_conv = call(
        functools.partial(grad_conv_kernel, w_conv.shape[0]),
        (KERNEL_TAPS,),
        [SMEM, ANY, ANY, ANY, whole(rows, 8), whole(rows, INNER)],
        out_specs,
        out_shapes,
        [ext, pltpu.VMEM((rows, INNER), BF16), dma((3,))],
        flops=2 * rows * KERNEL_TAPS * INNER * INNER,
        moved=6 * rows * INNER + 6 * KERNEL_TAPS * INNER * INNER,
    )(spots, m_low, moved, m_high, masks, d_conv)
    line_conv = reduce_grad(keep_conv, send_conv, place)

    out_shapes, out_specs = halves(w_out)
    keep_out, send_out = call(
        functools.partial(grad_plain_kernel, w_out.shape[0]),
        (1,),
        [SMEM, whole(rows, INNER), whole(rows, D)],
        out_specs,
        out_shapes,
        flops=2 * rows * D * INNER,
        moved=2 * rows * (D + INNER) + 6 * D * INNER,
    )(spots, hidden_c, cotangent)
    line_out = reduce_grad(keep_out, send_out, place)

    unit = math.gcd(w_conv.shape[0], INNER)
    d_pre, sums_b = call(
        functools.partial(back_conv_kernel, pieces),
        (steps,),
        [SMEM, ANY, ANY, ANY, rows_spec(tile, 8)]
        + [rows_spec(tile, INNER)] * 2
        + [params_spec]
        + [ANY] * pieces,
        [rows_spec(tile, INNER), whole(2, INNER)],
        [shape((rows, INNER), BF16), shape((2, INNER), F32)],
        [
            ext,
            pltpu.VMEM((INNER, KERNEL_TAPS * INNER), BF16),
            pltpu.VMEM((tile, KERNEL_TAPS * INNER), BF16),
            pltpu.VMEM((tile, INNER), F32),
            pltpu.VMEM((16, INNER), F32),
            dma((3,)),
            dma((KERNEL_TAPS * INNER // unit,)),
        ],
        flops=2 * rows * INNER * KERNEL_TAPS * INNER,
        moved=rows * 10 * INNER + 2 * INNER * KERNEL_TAPS * INNER,
    )(spots, d_low, d_conv, d_high, masks, pre_inner, slope_b, norm_params, *conv_pieces)

    out_shapes, out_specs = halves(w_in)
    keep_in, send_in = call(
        functools.partial(grad_plain_kernel, w_in.shape[0]),
        (1,),
        [SMEM, whole(rows, D), whole(rows, INNER)],
        out_specs,
        out_shapes,
        flops=2 * rows * D * INNER,
        moved=2 * rows * (D + INNER) + 6 * D * INNER,
    )(spots, hidden_a, d_pre)
    line_in = reduce_grad(keep_in, send_in, place)

    input_grad, sums_a = call(
        functools.partial(back_a_kernel, pieces),
        (steps,),
        [SMEM, rows_spec(tile, INNER)]
        + [rows_spec(tile, D)] * 3
        + [params_spec]
        + [ANY] * pieces,
        [rows_spec(tile, D), whole(2, D)],
        [shape((rows, D), F32), shape((2, D), F32)],
        [
            pltpu.VMEM((D, INNER), BF16),
            pltpu.VMEM((tile, D), F32),
            pltpu.VMEM((16, D), F32),
            dma((pieces,)),
        ],
        flops=2 * rows * D * INNER,
        moved=rows * (10 * D + 2 * INNER),
    )(spots, d_pre, tokens, slope_a, cotangent, norm_params, *in_pieces)

    (block_out,) = call(
        functools.partial(out_kernel, pieces),
        (steps,),
        [SMEM, rows_spec(tile, INNER), rows_spec(tile, D)] + [ANY] * pieces,
        [rows_spec(tile, D)],
        [shape((rows, D), BF16)],
        [pltpu.VMEM((INNER, D), BF16), dma((pieces,))],
        flops=2 * rows * D * INNER,
        moved=rows * (4 * D + 2 * INNER),
    )(spots, hidden_c, tokens, *out_pieces)

    lines = line_in + line_conv + line_out
    weights = (w_in, w_conv, w_out)
    columns = [(w.shape[0], 1) for w in weights]
    cols_all = D + 2 * INNER
    stats = call(
        stats_kernel,
        (1,),
        [SMEM]
        + [ANY] * 6
        + [whole(*c) for c in columns]
        + [whole(2, D), whole(2, INNER), whole(2, INNER)],
        [whole(*w.shape) for w in weights]
        + [whole(*c) for c in columns]
        + [whole(8, cols_all)],
        [shape(w.shape, F32) for w in weights]
        + [shape(c, F32) for c in columns]
        + [shape((8, cols_all), F32)],
        [
            pltpu.VMEM((2, place.outer, tiles_of(w) // split, SUB, LANE), BF16) for w in weights
        ]
        + [dma((6 * place.outer,))],
        moved=30 * 1024 * 1024,
    )(
        spots,
        *lines,
        row_in.reshape(-1, 1),
        row_conv.reshape(-1, 1),
        row_out.reshape(-1, 1),
        sums_a,
        sums_b,
        sums_c,
    )
    grads, rows_new, pack = stats[0:3], stats[3:6], stats[6]
    pack = lax.psum(pack, AXES)
    results = call(
        functools.partial(update_kernel, place.seq),
        (1,),
        [whole(8, cols_all), params_spec, params_spec]
        + [whole(1, w.shape[1]) for w in weights]
        + [whole(*w.shape) for w in weights]
        + [whole(*c) for c in columns]
        + [whole(*w.shape) for w in weights],
        [whole(*w.shape) for w in weights]
        + [whole(1, w.shape[1]) for w in weights]
        + [params_spec] * 3,
        [shape(w.shape, F32) for w in weights]
        + [shape((1, w.shape[1]), F32) for w in weights]
        + [shape((2, cols_all), F32)] * 3,
        moved=30 * 1024 * 1024,
    )(
        pack,
        norm_params,
        norm_second,
        col_in.reshape(1, -1),
        col_conv.reshape(1, -1),
        col_out.reshape(1, -1),
        *grads,
        *rows_new,
        *weights,
    )
    new_in, new_conv, new_out = results[0:3]
    cols_new = [c.reshape(-1) for c in results[3:6]]
    rows_new = [r.reshape(-1) for r in rows_new]
    return (
        block_out,
        input_grad,
        *grads,
        new_in,
        new_conv,
        new_out,
        rows_new[0],
        cols_new[0],
        rows_new[1],
        cols_new[1],
        rows_new[2],
        cols_new[2],
        results[6],
        results[7],
        results[8],
    )


def solution(mesh):
    both, rows = P(AXES, None), P("fsdp", None)
    in_specs = (
        both, P(AXES), P(), both, rows, rows, rows, P(),
        P("fsdp"), P(), P("fsdp"), P(), P("fsdp"), P(), P(),
    )
    out_specs = (
        both, both, rows, rows, rows, rows, rows, rows,
        P("fsdp"), P(), P("fsdp"), P(), P("fsdp"), P(), P(), P(), P(),
    )
    return jax.shard_map(
        on_device, mesh=mesh, in_specs=in_specs, out_specs=out_specs, check_vma=False
    )
```

```python
import functools
import math

import jax
import jax.numpy as jnp
from jax import lax
from jax.experimental import pallas as pl
from jax.experimental.pallas import tpu as pltpu
from jax.sharding import PartitionSpec as P

D = 1280
INNER = 640
KERNEL_TAPS = 5
DILATION_STEP = 128
STEP = 10
EPSILON = 1e-05
DECAY = 1.0 - STEP ** (-0.8)

REACH = (KERNEL_TAPS - 1) // 2 * DILATION_STEP
MID = (KERNEL_TAPS - 1) // 2
F32 = jnp.float32
BF16 = jnp.bfloat16
SUB, LANE = 16, 128
AXES = ("seq", "fsdp")
NT = (((1,), (1,)), ((), ()))
TN = (((0,), (0,)), ((), ()))
NN = (((1,), (0,)), ((), ()))
VMEM_LIMIT = 58 * 1024 * 1024


def call(kernel, grid, in_specs, out_specs, out_shape, scratch=(), flops=0, moved=0, scalars=None):
    params = pltpu.CompilerParams(
        vmem_limit_bytes=VMEM_LIMIT, dimension_semantics=("arbitrary",) * len(grid)
    )
    return pl.pallas_call(
        kernel,
        grid=grid,
        in_specs=in_specs,
        out_specs=out_specs,
        out_shape=out_shape,
        scratch_shapes=list(scratch),
        compiler_params=params,
        cost_estimate=pl.CostEstimate(flops=flops, bytes_accessed=moved, transcendentals=0),
    )


def shape(dims, dtype):
    return jax.ShapeDtypeStruct(dims, dtype)


def rows_spec(tile, width):
    return pl.BlockSpec((tile, width), lambda i: (i, 0))


def whole(*dims):
    return pl.BlockSpec(dims, lambda *_: (0,) * len(dims))


ANY = pl.BlockSpec(memory_space=pl.ANY)
SMEM = pl.BlockSpec(memory_space=pltpu.SMEM)


ERFC_P = 0.47 / math.sqrt(2.0)
ERFC_C = (
    0.12357219400743558,
    0.1999878668208835,
    -0.08033356004356296,
    0.3660253986657854,
    -0.1092519747040215,
)
LOG2E = 1.4426950408889634


def gelu_and_slope(y):
    t = pltpu.reciprocal(1.0 + ERFC_P * jnp.abs(y), approx=True)
    bell = jnp.exp2(y * y * (-0.5 * LOG2E))
    poly = ERFC_C[4] * t + ERFC_C[3]
    for c in ERFC_C[2::-1]:
        poly = poly * t + c
    tail = poly * t * bell
    cdf = jnp.where(y > 0.0, 1.0 - tail, tail)
    return y * cdf, cdf + y * (bell * (1.0 / math.sqrt(2.0 * math.pi)))


def lane_blocks(width):
    return [slice(k, k + LANE) for k in range(0, width, LANE)]


def row_stats(ref, rows):
    width = ref.shape[-1]
    blocks = lane_blocks(width)
    total = ref[rows, blocks[0]].astype(F32)
    for b in blocks[1:]:
        total = total + ref[rows, b].astype(F32)
    mean = jnp.sum(total, axis=-1, keepdims=True) * (1.0 / width)
    square = None
    for b in blocks:
        centered = ref[rows, b].astype(F32) - mean
        square = centered * centered if square is None else square + centered * centered
    variance = jnp.sum(square, axis=-1, keepdims=True) * (1.0 / width)
    return mean, lax.rsqrt(variance + EPSILON)


def fold(values):
    total = values[0:8]
    for k in range(8, values.shape[0], 8):
        total = total + values[k : k + 8]
    return total


def row_loop(count, step, body, unroll=1):
    def at(i, carry):
        body(pl.ds(pl.multiple_of(i * step, step), step))
        return carry

    lax.fori_loop(0, count // step, at, 0, unroll=unroll)


def norm_back(rows, dxhat_ref, xhat_ref, sums, rstd, put):
    width = dxhat_ref.shape[-1]
    mean_d = jnp.sum(sums[0], axis=-1, keepdims=True) * (1.0 / width)
    mean_dx = jnp.sum(sums[1], axis=-1, keepdims=True) * (1.0 / width)
    for b in lane_blocks(width):
        xhat = xhat_ref[rows, b].astype(F32)
        put(b, (dxhat_ref[rows, b] - mean_d - xhat * mean_dx) * rstd)


def add_terms(acc_ref, b, dy, xhat):
    acc_ref[0:8, b] += fold(dy * xhat)
    acc_ref[8:16, b] += fold(dy)


def open_sums(acc_ref):
    @pl.when(pl.program_id(0) == 0)
    def _():
        acc_ref[...] = jnp.zeros_like(acc_ref)


def close_sums(out_ref, acc_ref):
    @pl.when(pl.program_id(0) == pl.num_programs(0) - 1)
    def _():
        out_ref[0:1, :] = jnp.sum(acc_ref[0:8, :], axis=0, keepdims=True)
        out_ref[1:2, :] = jnp.sum(acc_ref[8:16, :], axis=0, keepdims=True)


def run_copies(copies):
    for copy in copies:
        copy.start()
    for copy in copies:
        copy.wait()


def piece_copies(pieces, full_ref, me, sem, first=0):
    each = full_ref.shape[0] // len(pieces)
    return [
        pltpu.make_async_copy(
            piece,
            full_ref.at[pl.ds(pl.multiple_of((me ^ k) * each, SUB), each), :],
            sem.at[first + k],
        )
        for k, piece in enumerate(pieces)
    ]


def column(row):
    return jnp.transpose(jnp.broadcast_to(row, (LANE, LANE)))


CHUNK = 64


def norm_a_kernel(tok_ref, np_ref, hid_ref, slope_ref, xhat_ref, rstd_ref):
    def body(rows):
        mean, rstd = row_stats(tok_ref, rows)
        rstd_ref[rows, :] = rstd
        for b in lane_blocks(D):
            xhat = (tok_ref[rows, b].astype(F32) - mean) * rstd
            hidden, slope = gelu_and_slope(xhat * np_ref[0:1, b] + np_ref[1:2, b])
            hid_ref[rows, b] = hidden.astype(BF16)
            slope_ref[rows, b] = slope.astype(BF16)
            xhat_ref[rows, b] = xhat.astype(BF16)

    row_loop(tok_ref.shape[0], CHUNK, body)


def in_kernel(pieces, place_ref, ends_ref, hid_ref, live_ref, np_ref, *refs):
    piece_refs = refs[:pieces]
    mov_ref, slope_ref, xhat_ref, rstd_ref, mask_ref, first_ref, last_ref = refs[pieces : pieces + 7]
    w_ref, pre_ref, sem = refs[pieces + 7 :]
    step, steps = pl.program_id(0), pl.num_programs(0)
    tile = hid_ref.shape[0]

    @pl.when(step == 0)
    def _():
        run_copies(piece_copies(piece_refs, w_ref, place_ref[0], sem))

    pre_ref[...] = lax.dot_general(hid_ref[...], w_ref[...], NN, preferred_element_type=F32)

    first = place_ref[1] + step * tile
    ends = ends_ref[...]
    lanes = lax.broadcasted_iota(jnp.int32, (LANE, 8), 1)
    offsets = ((lanes - MID) * DILATION_STEP).astype(F32)
    for k in range(tile // LANE):
        at = (first + k * LANE + lax.broadcasted_iota(jnp.int32, (LANE, 1), 0)).astype(F32)
        begin = jnp.max(jnp.where(ends <= at, ends, 0.0), axis=1, keepdims=True)
        end = jnp.min(jnp.where(ends > at, ends, 1e9), axis=1, keepdims=True)
        there = at + offsets
        same = jnp.where((there >= begin) & (there < end), 1.0, 0.0)
        live = column(live_ref[pl.ds(step * (tile // LANE) + k, 1), :].astype(F32))
        mask_ref[k * LANE : (k + 1) * LANE, :] = jnp.where(lanes == MID, live[:, 0:8], same)

    def body(rows):
        mean, rstd = row_stats(pre_ref, rows)
        rstd_ref[rows, :] = rstd
        live = mask_ref[rows, MID : MID + 1]
        for b in lane_blocks(INNER):
            gains = slice(D + b.start, D + b.stop)
            xhat = (pre_ref[rows, b] - mean) * rstd
            hidden, slope = gelu_and_slope(xhat * np_ref[0:1, gains] + np_ref[1:2, gains])
            mov_ref[rows, b] = (hidden * live).astype(BF16)
            slope_ref[rows, b] = slope.astype(BF16)
            xhat_ref[rows, b] = xhat.astype(BF16)

    row_loop(tile, CHUNK, body)

    @pl.when(step == 0)
    def _():
        first_ref[...] = mov_ref[0:REACH, :]

    @pl.when(step == steps - 1)
    def _():
        last_ref[...] = mov_ref[tile - REACH :, :]


def load_window(low, mid, high, ext_ref, sem):
    rows = mid.shape[0]
    return [
        pltpu.make_async_copy(low, ext_ref.at[0:REACH, :], sem.at[0]),
        pltpu.make_async_copy(mid, ext_ref.at[REACH : REACH + rows, :], sem.at[1]),
        pltpu.make_async_copy(high, ext_ref.at[REACH + rows : 2 * REACH + rows, :], sem.at[2]),
    ]


def fill_taps(taps_ref, ext_ref, mask_ref, start):
    tile = taps_ref.shape[0]
    for j in range(KERNEL_TAPS):
        rows = pl.ds(pl.multiple_of(start + j * DILATION_STEP, DILATION_STEP), tile)
        picked = ext_ref[rows, :]
        if j != MID:
            picked = picked * mask_ref[:, j : j + 1].astype(BF16)
        taps_ref[:, j * INNER : (j + 1) * INNER] = picked


def conv_kernel(pieces, place_ref, low_ref, mov_ref, high_ref, mask_ref, cot_ref, np_ref, *refs):
    conv_pieces, out_pieces = refs[:pieces], refs[pieces : 2 * pieces]
    (hid_ref, dconv_ref, first_ref, last_ref, sums_ref) = refs[2 * pieces : 2 * pieces + 5]
    ext_ref, wc_ref, wo_ref, wt_ref, taps_ref, pre_ref, dh_ref, xhat_ref, acc_ref, sem = refs[
        2 * pieces + 5 :
    ]
    step, steps = pl.program_id(0), pl.num_programs(0)
    tile = taps_ref.shape[0]
    open_sums(acc_ref)

    @pl.when(step == 0)
    def _():
        me = place_ref[0]
        outs = piece_copies(out_pieces, wo_ref, me, sem, 3)
        rest = load_window(low_ref, mov_ref, high_ref, ext_ref, sem)
        rest += piece_copies(conv_pieces, wc_ref, me, sem, 3 + pieces)
        for copy in outs + rest:
            copy.start()
        for copy in outs:
            copy.wait()
        for k in range(0, D, 256):
            wt_ref[k : k + 256, :] = jnp.transpose(wo_ref[:, k : k + 256])
        for copy in rest:
            copy.wait()

    fill_taps(taps_ref, ext_ref, mask_ref, step * tile)
    pre_ref[...] = lax.dot_general(taps_ref[...], wc_ref[...], NN, preferred_element_type=F32)
    dh_ref[...] = lax.dot_general(cot_ref[...], wt_ref[...], NN, preferred_element_type=F32)

    def body(rows):
        mean, rstd = row_stats(pre_ref, rows)
        sums = [0.0, 0.0]
        for b in lane_blocks(INNER):
            gains = slice(D + INNER + b.start, D + INNER + b.stop)
            gain = np_ref[0:1, gains]
            xhat = (pre_ref[rows, b] - mean) * rstd
            hidden, slope = gelu_and_slope(xhat * gain + np_ref[1:2, gains])
            hid_ref[rows, b] = hidden.astype(BF16)
            dy = dh_ref[rows, b] * slope
            add_terms(acc_ref, b, dy, xhat)
            dxhat = dy * gain
            xhat_ref[rows, b] = xhat
            dh_ref[rows, b] = dxhat
            sums = [sums[0] + dxhat, sums[1] + dxhat * xhat]

        def put(b, value):
            dconv_ref[rows, b] = value.astype(BF16)

        norm_back(rows, dh_ref, xhat_ref, sums, rstd, put)

    row_loop(tile, CHUNK, body)
    close_sums(sums_ref, acc_ref)

    @pl.when(step == 0)
    def _():
        first_ref[...] = dconv_ref[0:REACH, :]

    @pl.when(step == steps - 1)
    def _():
        last_ref[...] = dconv_ref[tile - REACH :, :]


def put_tiles(ref, lead, first, value):
    blocks = value.shape[1] // LANE
    for g in range(value.shape[0] // SUB):
        for b in range(blocks):
            tile = value[g * SUB : (g + 1) * SUB, b * LANE : (b + 1) * LANE]
            ref[lead, first + g * blocks + b] = tile.astype(ref.dtype)


def split_by_owner(grad_ref, rows_each, core, keep_ref, send_ref, base):
    blocks = grad_ref.shape[1] // LANE
    owners = grad_ref.shape[0] // rows_each
    groups = rows_each // SUB
    for owner in range(owners):

        def body(g, carry, owner=owner):
            row = pl.multiple_of(owner * rows_each + g * SUB, SUB)
            part = grad_ref[pl.ds(row, SUB), :]

            @pl.when(core == owner % 2)
            def _():
                put_tiles(keep_ref, owner // 2, base + g * blocks, part)

            @pl.when(core != owner % 2)
            def _():
                put_tiles(send_ref, owner // 2, base + g * blocks, part)

            return carry

        lax.fori_loop(0, groups, body, 0)


def clear_rest(refs, used):
    for ref in refs:
        if used < ref.shape[1]:
            ref[:, used:] = jnp.zeros((ref.shape[0], ref.shape[1] - used, SUB, LANE), ref.dtype)


def grads_kernel(
    rows_conv, rows_out, place_ref, low_ref, mov_ref, high_ref, mask_ref, d_ref, hid_ref, cot_ref, *refs
):
    keep_ref, send_ref, ext_ref, gc_ref, go_ref, sem = refs
    step, steps = pl.program_id(0), pl.num_programs(0)
    tile = d_ref.shape[0]

    @pl.when(step == 0)
    def _():
        copies = load_window(low_ref, mov_ref, high_ref, ext_ref, sem)
        for copy in copies:
            copy.start()
        go_ref[...] = jnp.zeros_like(go_ref)
        gc_ref[...] = jnp.zeros_like(gc_ref)
        for copy in copies:
            copy.wait()

    go_ref[...] += lax.dot_general(hid_ref[...], cot_ref[...], TN, preferred_element_type=F32)
    for j in range(KERNEL_TAPS):
        rows = pl.ds(pl.multiple_of(step * tile + j * DILATION_STEP, DILATION_STEP), tile)
        lhs = ext_ref[rows, :]
        if j != MID:
            lhs = lhs * mask_ref[:, j : j + 1].astype(BF16)
        gc_ref[j * INNER : (j + 1) * INNER, :] += lax.dot_general(
            lhs, d_ref[...], TN, preferred_element_type=F32
        )

    @pl.when(step == steps - 1)
    def _():
        core = lax.rem(place_ref[0], 2)
        conv_tiles = rows_conv // SUB * (INNER // LANE)
        out_tiles = rows_out // SUB * (D // LANE)
        clear_rest((keep_ref, send_ref), conv_tiles + out_tiles)
        split_by_owner(gc_ref, rows_conv, core, keep_ref, send_ref, 0)
        split_by_owner(go_ref, rows_out, core, keep_ref, send_ref, conv_tiles)


def back_conv_kernel(
    pieces, rows_in, place_ref, low_ref, d_ref, high_ref, mask_ref, xhat_ref, rstd_ref, slope_ref, hid_ref, np_ref, *refs
):
    conv_pieces = refs[:pieces]
    dpre_ref, sums_ref, keep_ref, send_ref = refs[pieces : pieces + 4]
    ext_ref, wc_ref, wt_ref, taps_ref, dmov_ref, grad_ref, acc_ref, sem = refs[pieces + 4 :]
    step, steps = pl.program_id(0), pl.num_programs(0)
    tile = taps_ref.shape[0]
    open_sums(acc_ref)

    @pl.when(step == 0)
    def _():
        weights = piece_copies(conv_pieces, wc_ref, place_ref[0], sem, 3)
        window = load_window(low_ref, d_ref, high_ref, ext_ref, sem)
        for copy in weights + window:
            copy.start()
        grad_ref[...] = jnp.zeros_like(grad_ref)
        for copy in weights:
            copy.wait()
        for j in range(KERNEL_TAPS):
            source = wc_ref[j * INNER : (j + 1) * INNER, :]
            at = (KERNEL_TAPS - 1 - j) * INNER
            wt_ref[at : at + INNER, :] = jnp.transpose(source)
        for copy in window:
            copy.wait()

    fill_taps(taps_ref, ext_ref, mask_ref, step * tile)
    dmov_ref[...] = lax.dot_general(taps_ref[...], wt_ref[...], NN, preferred_element_type=F32)

    def body(rows):
        live = mask_ref[rows, MID : MID + 1]
        sums = [0.0, 0.0]
        for b in lane_blocks(INNER):
            xhat = xhat_ref[rows, b].astype(F32)
            dy = dmov_ref[rows, b] * live * slope_ref[rows, b].astype(F32)
            add_terms(acc_ref, b, dy, xhat)
            dxhat = dy * np_ref[0:1, D + b.start : D + b.stop]
            dmov_ref[rows, b] = dxhat
            sums = [sums[0] + dxhat, sums[1] + dxhat * xhat]

        def put(b, value):
            dpre_ref[rows, b] = value.astype(BF16)

        norm_back(rows, dmov_ref, xhat_ref, sums, rstd_ref[rows, :], put)

    row_loop(tile, CHUNK, body)
    close_sums(sums_ref, acc_ref)
    grad_ref[...] += lax.dot_general(hid_ref[...], dpre_ref[...], TN, preferred_element_type=F32)

    @pl.when(step == steps - 1)
    def _():
        clear_rest((keep_ref, send_ref), rows_in // SUB * (INNER // LANE))
        core = lax.rem(place_ref[0], 2)
        split_by_owner(grad_ref, rows_in, core, keep_ref, send_ref, 0)


def back_a_kernel(pieces, place_ref, dpre_ref, xhat_ref, rstd_ref, slope_ref, cot_ref, np_ref, *refs):
    piece_refs = refs[:pieces]
    grad_ref, sums_ref, w_ref, wt_ref, dh_ref, acc_ref, sem = refs[pieces:]
    open_sums(acc_ref)

    @pl.when(pl.program_id(0) == 0)
    def _():
        run_copies(piece_copies(piece_refs, w_ref, place_ref[0], sem))
        for k in range(0, D, 256):
            wt_ref[:, k : k + 256] = jnp.transpose(w_ref[k : k + 256, :])

    dh_ref[...] = lax.dot_general(dpre_ref[...], wt_ref[...], NN, preferred_element_type=F32)

    def body(rows):
        sums = [0.0, 0.0]
        for b in lane_blocks(D):
            xhat = xhat_ref[rows, b].astype(F32)
            dy = dh_ref[rows, b] * slope_ref[rows, b].astype(F32)
            add_terms(acc_ref, b, dy, xhat)
            dxhat = dy * np_ref[0:1, b]
            dh_ref[rows, b] = dxhat
            sums = [sums[0] + dxhat, sums[1] + dxhat * xhat]

        def put(b, value):
            grad_ref[rows, b] = cot_ref[rows, b].astype(F32) + value

        norm_back(rows, dh_ref, xhat_ref, sums, rstd_ref[rows, :], put)

    row_loop(dpre_ref.shape[0], CHUNK, body)
    close_sums(sums_ref, acc_ref)


def out_kernel(pieces, place_ref, hid_ref, tok_ref, *refs):
    piece_refs = refs[:pieces]
    out_ref, w_ref, sem = refs[pieces:]

    @pl.when(pl.program_id(0) == 0)
    def _():
        run_copies(piece_copies(piece_refs, w_ref, place_ref[0], sem))

    branch = lax.dot_general(hid_ref[...], w_ref[...], NN, preferred_element_type=F32)
    out_ref[...] = (tok_ref[...].astype(F32) + branch).astype(BF16)


COLS = ((0, INNER), (INNER, INNER), (2 * INNER, D))


def pack_kernel(counts, place_ref, conv_out_ref, in_ref, *refs):
    states = refs[0:3]
    sums = refs[3:6]
    pack_ref, acc_ref = refs[6:8]
    pack_ref[...] = jnp.zeros_like(pack_ref)
    for k, lane0, lane1 in ((0, 0, D), (1, D, D + INNER), (2, D + INNER, D + 2 * INNER)):
        pack_ref[0:2, lane0:lane1] = sums[k][...]
    lanes = lax.broadcasted_iota(jnp.int32, (1, LANE), 1)
    for k in range(3):
        total = jnp.sum(states[k][...], axis=1, keepdims=True)
        pack_ref[3:4, 0:LANE] += jnp.where(lanes == k, total, 0.0)
    acc_ref[...] = jnp.zeros_like(acc_ref)
    n_in, n_conv, n_out = counts
    per_inner, per_d = INNER // LANE, D // LANE
    spare = acc_ref.shape[0] - 1

    def add(ref, slot_of):
        start = place_ref[2] * ref.shape[0]

        def body(k, carry):
            value = ref[k].astype(F32)
            acc_ref[slot_of(start + k)] += value * value + 1e-30
            return carry

        lax.fori_loop(0, ref.shape[0], body, 0, unroll=4)

    add(in_ref, lambda n: jnp.where(n < n_in, lax.rem(n, per_inner), spare))

    def conv_out(n):
        rest = n - n_conv
        out = jnp.where(rest < n_out, 2 * per_inner + lax.rem(jnp.maximum(rest, 0), per_d), spare)
        return jnp.where(n < n_conv, per_inner + lax.rem(n, per_inner), out)

    add(conv_out_ref, conv_out)
    for slot in range(spare):
        pack_ref[2:3, slot * LANE : (slot + 1) * LANE] = jnp.sum(acc_ref[slot], axis=0, keepdims=True)


def update_kernel(copies_of, pack_ref, np_ref, second_ref, in_ref, conv_out_ref, *refs):
    weights, row_states, col_states = refs[0:3], refs[3:6], refs[6:9]
    grads, news, rows_new, cols_new = refs[9:12], refs[12:15], refs[15:18], refs[18:21]
    ngrad_ref, nsecond_ref, nnew_ref = refs[21:24]
    line_ref, state_ref, new_ref = refs[24:27]
    grad = pack_ref[0:2, :]
    second = DECAY * second_ref[...] + (1.0 - DECAY) * (grad * grad + 1e-30)
    ngrad_ref[...] = grad
    nsecond_ref[...] = second
    nnew_ref[...] = np_ref[...] - 0.2 * grad * lax.rsqrt(second)
    fans = (D, KERNEL_TAPS * INNER, INNER)
    firsts = (0, 0, weights[1].shape[0] // SUB * (INNER // LANE))
    line_ref[...] = jnp.zeros_like(line_ref)
    for k, (lane0, width) in enumerate(COLS):
        fan, blocks = fans[k], width // LANE
        rows_here = weights[k].shape[0]
        squares = pack_ref[2:3, lane0 : lane0 + width]
        col_new = DECAY * col_states[k][...] + (1.0 - DECAY) * (squares * (1.0 / fan))
        cols_new[k][...] = col_new
        total = DECAY * pack_ref[3:4, k : k + 1] * (1.0 / copies_of)
        total = total + (1.0 - DECAY) * (1.0 / width) * jnp.sum(squares, axis=1, keepdims=True)
        scaled = col_new / (total * (1.0 / fan))
        rate = 0.5 / fan**0.5
        line_ref[0:1, 0:rows_here] = row_states[k][...]
        whole_rows = rows_here + -rows_here % LANE
        for c in range(0, whole_rows, LANE):
            state_ref[c : c + LANE, :] = column(line_ref[0:1, c : c + LANE])
        tiles, first = (in_ref, conv_out_ref, conv_out_ref)[k], firsts[k]
        weight, new, grad_ref = weights[k], news[k], grads[k]

        def body(g, carry, k=k, blocks=blocks, tiles=tiles, first=first, weight=weight, new=new, grad_ref=grad_ref, scaled=scaled, rate=rate, width=width):
            rows = pl.ds(pl.multiple_of(g * SUB, SUB), SUB)
            square = 0.0
            for b in range(blocks):
                value = tiles[first + g * blocks + b].astype(F32)
                grad_ref[rows, b * LANE : (b + 1) * LANE] = value
                square = square + (value * value + 1e-30)
            mean = jnp.sum(square, axis=1, keepdims=True) * (1.0 / width)
            row_new = DECAY * state_ref[rows, :] + (1.0 - DECAY) * mean
            new_ref[rows, :] = row_new
            for b in range(blocks):
                lanes = slice(b * LANE, (b + 1) * LANE)
                value = tiles[first + g * blocks + b].astype(F32)
                step = value * lax.rsqrt(row_new * scaled[:, lanes])
                new[rows, lanes] = weight[rows, lanes] - rate * step
            return carry

        lax.fori_loop(0, rows_here // SUB, body, 0, unroll=5)
        for c in range(0, rows_here, LANE):
            width_here = min(LANE, rows_here - c)
            turned = jnp.transpose(new_ref[c : c + LANE, :])
            rows_new[k][0:1, c : c + width_here] = turned[0:1, 0:width_here]


class Places:
    def __init__(self):
        self.seq, self.fsdp = lax.axis_size("seq"), lax.axis_size("fsdp")
        self.q = lax.axis_index("fsdp")
        self.s = lax.axis_index("seq")

    def flip(self, x, axis, bit):
        pairs = []
        for s in range(self.seq):
            for f in range(self.fsdp):
                s2, f2 = (s ^ bit, f) if axis == "seq" else (s, f ^ bit)
                pairs.append((s * self.fsdp + f, s2 * self.fsdp + f2))
        return lax.ppermute(x, AXES, pairs)


def bits_of(count):
    return [1 << k for k in range(count.bit_length() - 1)]


def gather_pieces(piece, place):
    found = {0: piece}
    for bit in reversed(bits_of(place.fsdp)):
        for k in list(found):
            found[k | bit] = place.flip(found[k], "fsdp", bit)
    return [found[k] for k in range(place.fsdp)]


def sum_everywhere(x, place):
    for axis, count in (("fsdp", place.fsdp), ("seq", place.seq)):
        for bit in bits_of(count):
            x = x + place.flip(x, axis, bit)
    return x


def pick(x, index):
    return lax.dynamic_index_in_dim(x, index, axis=0, keepdims=False)


def reduce_grad(keep, send, place):
    got = place.flip(send, "fsdp", 1)
    bit, total, width = place.fsdp // 2, keep, keep.shape[0]
    while width > 1:
        half = width // 2
        side = (place.q // bit) % 2
        parts = (2, half) + keep.shape[1:]
        total, got = total.reshape(parts), got.reshape(parts)
        away = pick(total, 1 - side) + pick(got, 1 - side).astype(F32)
        near = pick(total, side) + pick(got, side).astype(F32)
        total, got = near, place.flip(away.astype(BF16), "fsdp", bit)
        width, bit = half, bit // 2
    total = (total + got.astype(F32)).astype(BF16).reshape(keep.shape[1:])
    return lax.psum_scatter(total, "seq", scatter_dimension=0, tiled=True)


def on_device(
    tokens, input_mask, doc_lengths, cotangent, w_in, w_conv, w_out, norm_params,
    row_in, col_in, row_conv, col_conv, row_out, col_out, norm_second,
):
    place = Places()
    rows = tokens.shape[0]
    pieces = place.fsdp
    spots = jnp.stack([place.q, (place.s * place.fsdp + place.q) * rows, place.s]).astype(jnp.int32)
    docs = doc_lengths.shape[0]
    ends = jnp.pad(
        jnp.cumsum(doc_lengths).astype(F32), (0, -docs % LANE), constant_values=1e9
    ).reshape(1, -1)
    live = input_mask.reshape(-1, LANE)

    in_pieces = gather_pieces(w_in.astype(BF16), place)
    low_conv, low_out, *in_pieces = lax.optimization_barrier(
        (w_conv.astype(BF16), w_out.astype(BF16), *in_pieces)
    )
    conv_pieces = gather_pieces(low_conv, place)
    out_pieces = gather_pieces(low_out, place)

    tile_a, tile = 256, 512
    steps = rows // tile
    params_spec = whole(2, D + 2 * INNER)
    dma = pltpu.SemaphoreType.DMA

    hidden_a, slope_a, xhat_a, rstd_a = call(
        norm_a_kernel,
        (rows // tile_a,),
        [rows_spec(tile_a, D), params_spec],
        [rows_spec(tile_a, D)] * 3 + [rows_spec(tile_a, 1)],
        [shape((rows, D), BF16)] * 3 + [shape((rows, 1), F32)],
        flops=40 * rows * D,
        moved=8 * rows * D,
    )(tokens, norm_params)

    moved, slope_b, xhat_b, rstd_b, masks, m_first, m_last = call(
        functools.partial(in_kernel, pieces),
        (steps,),
        [SMEM, whole(*ends.shape), rows_spec(tile, D), whole(*live.shape), params_spec]
        + [ANY] * pieces,
        [rows_spec(tile, INNER)] * 3
        + [rows_spec(tile, 1), rows_spec(tile, 8), whole(REACH, INNER), whole(REACH, INNER)],
        [shape((rows, INNER), BF16)] * 3
        + [
            shape((rows, 1), F32),
            shape((rows, 8), F32),
            shape((REACH, INNER), BF16),
            shape((REACH, INNER), BF16),
        ],
        [pltpu.VMEM((D, INNER), BF16), pltpu.VMEM((tile, INNER), F32), dma((pieces,))],
        flops=2 * rows * D * INNER,
        moved=rows * (2 * D + 8 * INNER),
    )(spots, ends, hidden_a, live, norm_params, *in_pieces)

    total = place.seq * place.fsdp
    up = [(i, i + 1) for i in range(total - 1)]
    down = [(i + 1, i) for i in range(total - 1)]
    m_low, m_high = lax.ppermute(m_last, AXES, up), lax.ppermute(m_first, AXES, down)

    ext = pltpu.VMEM((rows + 2 * REACH, INNER), BF16)
    hidden_c, d_conv, d_first, d_last, sums_c = call(
        functools.partial(conv_kernel, pieces),
        (steps,),
        [SMEM, ANY, ANY, ANY, rows_spec(tile, 8), rows_spec(tile, D), params_spec]
        + [ANY] * (2 * pieces),
        [rows_spec(tile, INNER)] * 2
        + [whole(REACH, INNER), whole(REACH, INNER), whole(2, INNER)],
        [
            shape((rows, INNER), BF16),
            shape((rows, INNER), BF16),
            shape((REACH, INNER), BF16),
            shape((REACH, INNER), BF16),
            shape((2, INNER), F32),
        ],
        [
            ext,
            pltpu.VMEM((KERNEL_TAPS * INNER, INNER), BF16),
            pltpu.VMEM((INNER, D), BF16),
            pltpu.VMEM((D, INNER), BF16),
            pltpu.VMEM((tile, KERNEL_TAPS * INNER), BF16),
            pltpu.VMEM((tile, INNER), F32),
            pltpu.VMEM((tile, INNER), F32),
            pltpu.VMEM((tile, INNER), F32),
            pltpu.VMEM((16, INNER), F32),
            dma((3 + 2 * pieces,)),
        ],
        flops=2 * rows * INNER * (KERNEL_TAPS * INNER + D),
        moved=rows * (2 * D + 6 * INNER) + 2 * INNER * (KERNEL_TAPS * INNER + D),
    )(spots, m_low, moved, m_high, masks, cotangent, norm_params, *conv_pieces, *out_pieces)
    d_low, d_high = lax.ppermute(d_last, AXES, up), lax.ppermute(d_first, AXES, down)

    shards = place.fsdp // 2

    def count_of(weight):
        return weight.shape[0] // SUB * (weight.shape[1] // LANE)

    def halves(count):
        dims = (shards, count + -count % place.seq, SUB, LANE)
        return [whole(*dims)] * 2, [shape(dims, F32), shape(dims, BF16)]

    half_specs, half_shapes = halves(count_of(w_conv) + count_of(w_out))
    keep_co, send_co = call(
        functools.partial(grads_kernel, w_conv.shape[0], w_out.shape[0]),
        (steps,),
        [SMEM, ANY, ANY, ANY, rows_spec(tile, 8)]
        + [rows_spec(tile, INNER)] * 2
        + [rows_spec(tile, D)],
        half_specs,
        half_shapes,
        [
            ext,
            pltpu.VMEM((KERNEL_TAPS * INNER, INNER), F32),
            pltpu.VMEM((INNER, D), F32),
            dma((3,)),
        ],
        flops=2 * rows * INNER * (KERNEL_TAPS * INNER + D),
        moved=rows * (6 * INNER + 2 * D) + 6 * INNER * (KERNEL_TAPS * INNER + D),
    )(spots, m_low, moved, m_high, masks, d_conv, hidden_c, cotangent)
    part_co = reduce_grad(keep_co, send_co, place)

    half_specs, half_shapes = halves(count_of(w_in))
    d_pre, sums_b, keep_in, send_in = call(
        functools.partial(back_conv_kernel, pieces, w_in.shape[0]),
        (steps,),
        [SMEM, ANY, ANY, ANY, rows_spec(tile, 8), rows_spec(tile, INNER), rows_spec(tile, 1)]
        + [rows_spec(tile, INNER), rows_spec(tile, D), params_spec]
        + [ANY] * pieces,
        [rows_spec(tile, INNER), whole(2, INNER)] + half_specs,
        [shape((rows, INNER), BF16), shape((2, INNER), F32)] + half_shapes,
        [
            ext,
            pltpu.VMEM((KERNEL_TAPS * INNER, INNER), BF16),
            pltpu.VMEM((KERNEL_TAPS * INNER, INNER), BF16),
            pltpu.VMEM((tile, KERNEL_TAPS * INNER), BF16),
            pltpu.VMEM((tile, INNER), F32),
            pltpu.VMEM((D, INNER), F32),
            pltpu.VMEM((16, INNER), F32),
            dma((3 + pieces,)),
        ],
        flops=2 * rows * INNER * (KERNEL_TAPS * INNER + D),
        moved=rows * (10 * INNER + 2 * D) + 2 * INNER * KERNEL_TAPS * INNER,
    )(
        spots, d_low, d_conv, d_high, masks, xhat_b, rstd_b, slope_b, hidden_a, norm_params,
        *conv_pieces,
    )
    part_in = reduce_grad(keep_in, send_in, place)

    input_grad, sums_a = call(
        functools.partial(back_a_kernel, pieces),
        (steps,),
        [SMEM, rows_spec(tile, INNER), rows_spec(tile, D), rows_spec(tile, 1)]
        + [rows_spec(tile, D)] * 2
        + [params_spec]
        + [ANY] * pieces,
        [rows_spec(tile, D), whole(2, D)],
        [shape((rows, D), F32), shape((2, D), F32)],
        [
            pltpu.VMEM((D, INNER), BF16),
            pltpu.VMEM((INNER, D), BF16),
            pltpu.VMEM((tile, D), F32),
            pltpu.VMEM((16, D), F32),
            dma((pieces,)),
        ],
        flops=2 * rows * D * INNER,
        moved=rows * (10 * D + 2 * INNER),
    )(spots, d_pre, xhat_a, rstd_a, slope_a, cotangent, norm_params, *in_pieces)

    (block_out,) = call(
        functools.partial(out_kernel, pieces),
        (steps,),
        [SMEM, rows_spec(tile, INNER), rows_spec(tile, D)] + [ANY] * pieces,
        [rows_spec(tile, D)],
        [shape((rows, D), BF16)],
        [pltpu.VMEM((INNER, D), BF16), dma((pieces,))],
        flops=2 * rows * D * INNER,
        moved=rows * (4 * D + 2 * INNER),
    )(spots, hidden_c, tokens, *out_pieces)

    full_co = lax.all_gather(part_co, "seq", axis=0, tiled=True)
    full_in = lax.all_gather(part_in, "seq", axis=0, tiled=True)
    weights = (w_in, w_conv, w_out)
    row_states = [r.reshape(1, -1) for r in (row_in, row_conv, row_out)]
    col_states = [c.reshape(1, -1) for c in (col_in, col_conv, col_out)]
    row_specs = [whole(*r.shape) for r in row_states]
    col_specs = [whole(*c.shape) for c in col_states]
    cols_all = D + 2 * INNER
    (pack,) = call(
        functools.partial(pack_kernel, tuple(count_of(w) for w in weights)),
        (1,),
        [SMEM, whole(*part_co.shape), whole(*part_in.shape)]
        + row_specs
        + [whole(2, D), whole(2, INNER), whole(2, INNER)],
        [whole(4, cols_all)],
        [shape((4, cols_all), F32)],
        [pltpu.VMEM((cols_all // LANE + 1, SUB, LANE), F32)],
        moved=1024 * 1024,
    )(spots, part_co, part_in, *row_states, sums_a, sums_b, sums_c)
    pack = sum_everywhere(pack, place)
    weight_specs = [whole(*w.shape) for w in weights]
    lines = max(w.shape[0] + -w.shape[0] % LANE for w in weights)
    results = call(
        functools.partial(update_kernel, place.seq),
        (1,),
        [whole(4, cols_all), params_spec, params_spec, whole(*full_in.shape), whole(*full_co.shape)]
        + weight_specs
        + row_specs
        + col_specs,
        weight_specs * 2 + row_specs + col_specs + [params_spec] * 3,
        [shape(w.shape, F32) for w in weights] * 2
        + [shape(r.shape, F32) for r in row_states + col_states]
        + [shape((2, cols_all), F32)] * 3,
        [pltpu.VMEM((8, lines), F32), pltpu.VMEM((lines, LANE), F32), pltpu.VMEM((lines, LANE), F32)],
        moved=16 * 1024 * 1024,
    )(pack, norm_params, norm_second, full_in, full_co, *weights, *row_states, *col_states)
    grads, news = results[0:3], results[3:6]
    rows_new = [r.reshape(-1) for r in results[6:9]]
    cols_new = [c.reshape(-1) for c in results[9:12]]
    return (
        block_out,
        input_grad,
        *grads,
        *news,
        rows_new[0],
        cols_new[0],
        rows_new[1],
        cols_new[1],
        rows_new[2],
        cols_new[2],
        *results[12:15],
    )


def solution(mesh):
    both, rows = P(AXES, None), P("fsdp", None)
    in_specs = (
        both, P(AXES), P(), both, rows, rows, rows, P(),
        P("fsdp"), P(), P("fsdp"), P(), P("fsdp"), P(), P(),
    )
    out_specs = (
        both, both, rows, rows, rows, rows, rows, rows,
        P("fsdp"), P(), P("fsdp"), P(), P("fsdp"), P(), P(), P(), P(),
    )
    return jax.shard_map(
        on_device, mesh=mesh, in_specs=in_specs, out_specs=out_specs, check_vma=False
    )
```

```python
import functools
import math

import jax
import jax.numpy as jnp
from jax import lax
from jax.experimental import pallas as pl
from jax.experimental.pallas import tpu as pltpu
from jax.sharding import PartitionSpec as P

D = 1280
INNER = 640
KERNEL_TAPS = 5
DILATION_STEP = 128
STEP = 10
EPSILON = 1e-05
DECAY = 1.0 - STEP ** (-0.8)

REACH = (KERNEL_TAPS - 1) // 2 * DILATION_STEP
MID = (KERNEL_TAPS - 1) // 2
F32 = jnp.float32
BF16 = jnp.bfloat16
SUB, LANE = 16, 128
AXES = ("seq", "fsdp")
NT = (((1,), (1,)), ((), ()))
TN = (((0,), (0,)), ((), ()))
NN = (((1,), (0,)), ((), ()))
VMEM_LIMIT = 58 * 1024 * 1024


def call(kernel, grid, in_specs, out_specs, out_shape, scratch=(), us=1.0):
    params = pltpu.CompilerParams(
        vmem_limit_bytes=VMEM_LIMIT, dimension_semantics=("arbitrary",) * len(grid)
    )
    return pl.pallas_call(
        kernel,
        grid=grid,
        in_specs=in_specs,
        out_specs=out_specs,
        out_shape=out_shape,
        scratch_shapes=list(scratch),
        compiler_params=params,
        cost_estimate=pl.CostEstimate(
                flops=int(us * 1.1e9), bytes_accessed=int(us * 3.4e6), transcendentals=0
        ),
    )


def shape(dims, dtype):
    return jax.ShapeDtypeStruct(dims, dtype)


def rows_spec(tile, width):
    return pl.BlockSpec((tile, width), lambda i: (i, 0))


def whole(*dims):
    return pl.BlockSpec(dims, lambda *_: (0,) * len(dims))


ANY = pl.BlockSpec(memory_space=pl.ANY)
SMEM = pl.BlockSpec(memory_space=pltpu.SMEM)


ERFC_P = 0.47 / math.sqrt(2.0)
ERFC_C = (
    0.12357219400743558,
    0.1999878668208835,
    -0.08033356004356296,
    0.3660253986657854,
    -0.1092519747040215,
)
LOG2E = 1.4426950408889634


def gelu_and_slope(y):
    t = pltpu.reciprocal(1.0 + ERFC_P * jnp.abs(y), approx=True)
    bell = jnp.exp2(y * y * (-0.5 * LOG2E))
    poly = ERFC_C[4] * t + ERFC_C[3]
    for c in ERFC_C[2::-1]:
        poly = poly * t + c
    tail = poly * t * bell
    cdf = jnp.where(y > 0.0, 1.0 - tail, tail)
    return y * cdf, cdf + y * (bell * (1.0 / math.sqrt(2.0 * math.pi)))


def lane_blocks(width):
    return [slice(k, k + LANE) for k in range(0, width, LANE)]


def row_stats(ref, rows):
    width = ref.shape[-1]
    blocks = lane_blocks(width)
    total = ref[rows, blocks[0]].astype(F32)
    for b in blocks[1:]:
        total = total + ref[rows, b].astype(F32)
    mean = jnp.sum(total, axis=-1, keepdims=True) * (1.0 / width)
    square = None
    for b in blocks:
        centered = ref[rows, b].astype(F32) - mean
        square = centered * centered if square is None else square + centered * centered
    variance = jnp.sum(square, axis=-1, keepdims=True) * (1.0 / width)
    return mean, lax.rsqrt(variance + EPSILON)


def fold(values):
    total = values[0:8]
    for k in range(8, values.shape[0], 8):
        total = total + values[k : k + 8]
    return total


def in_stages(count, stages):
    chunks = [slice(k, k + CHUNK) for k in range(0, count, CHUNK)]
    kept = {}
    for t in range(len(chunks) + len(stages) - 1):
        for n, stage in enumerate(stages):
            if 0 <= t - n < len(chunks):
                kept[n, t - n] = stage(chunks[t - n], kept.get((n - 1, t - n)))


def row_means(sums, width):
    return [jnp.sum(x, axis=-1, keepdims=True) * (1.0 / width) for x in sums]


def norm_back(rows, dxhat_ref, xhat_ref, means, put):
    mean_d, mean_dx, rstd = means
    for b in lane_blocks(dxhat_ref.shape[-1]):
        xhat = xhat_ref[rows, b].astype(F32)
        put(b, (dxhat_ref[rows, b] - mean_d - xhat * mean_dx) * rstd)


def add_terms(acc_ref, b, dy, xhat):
    acc_ref[0:8, b] += fold(dy * xhat)
    acc_ref[8:16, b] += fold(dy)


def open_sums(acc_ref):
    @pl.when(pl.program_id(0) == 0)
    def _():
        acc_ref[...] = jnp.zeros_like(acc_ref)


def close_sums(out_ref, acc_ref):
    @pl.when(pl.program_id(0) == pl.num_programs(0) - 1)
    def _():
        out_ref[0:1, :] = jnp.sum(acc_ref[0:8, :], axis=0, keepdims=True)
        out_ref[1:2, :] = jnp.sum(acc_ref[8:16, :], axis=0, keepdims=True)


def run_copies(copies):
    for copy in copies:
        copy.start()
    for copy in copies:
        copy.wait()


def piece_copies(pieces, full_ref, me, sem, first=0):
    each = full_ref.shape[0] // len(pieces)
    return [
        pltpu.make_async_copy(
            piece,
            full_ref.at[pl.ds(pl.multiple_of((me ^ k) * each, SUB), each), :],
            sem.at[first + k],
        )
        for k, piece in enumerate(pieces)
    ]


def column(row):
    return jnp.transpose(jnp.broadcast_to(row, (LANE, LANE)))


CHUNK = 64


def norm_a_kernel(tok_ref, np_ref, hid_ref, slope_ref, xhat_ref, rstd_ref):
    def stats(rows, _):
        mean, rstd = row_stats(tok_ref, rows)
        rstd_ref[rows, :] = rstd
        return mean, rstd

    def work(rows, kept):
        mean, rstd = kept
        for b in lane_blocks(D):
            xhat = (tok_ref[rows, b].astype(F32) - mean) * rstd
            hidden, slope = gelu_and_slope(xhat * np_ref[0:1, b] + np_ref[1:2, b])
            hid_ref[rows, b] = hidden.astype(BF16)
            slope_ref[rows, b] = slope.astype(BF16)
            xhat_ref[rows, b] = xhat.astype(BF16)

    in_stages(tok_ref.shape[0], [stats, work])


def in_kernel(pieces, place_ref, ends_ref, hid_ref, live_ref, np_ref, *refs):
    piece_refs = refs[:pieces]
    mov_ref, slope_ref, xhat_ref, rstd_ref, mask_ref, first_ref, last_ref = refs[pieces : pieces + 7]
    w_ref, pre_ref, sem = refs[pieces + 7 :]
    step, steps = pl.program_id(0), pl.num_programs(0)
    tile = hid_ref.shape[0]

    @pl.when(step == 0)
    def _():
        run_copies(piece_copies(piece_refs, w_ref, place_ref[0], sem))

    pre_ref[...] = lax.dot_general(hid_ref[...], w_ref[...], NN, preferred_element_type=F32)

    first = place_ref[1] + step * tile
    ends = ends_ref[...]
    lanes = lax.broadcasted_iota(jnp.int32, (LANE, 8), 1)
    offsets = ((lanes - MID) * DILATION_STEP).astype(F32)
    for k in range(tile // LANE):
        at = (first + k * LANE + lax.broadcasted_iota(jnp.int32, (LANE, 1), 0)).astype(F32)
        begin = jnp.max(jnp.where(ends <= at, ends, 0.0), axis=1, keepdims=True)
        end = jnp.min(jnp.where(ends > at, ends, 1e9), axis=1, keepdims=True)
        there = at + offsets
        same = jnp.where((there >= begin) & (there < end), 1.0, 0.0)
        live = column(live_ref[pl.ds(step * (tile // LANE) + k, 1), :].astype(F32))
        mask_ref[k * LANE : (k + 1) * LANE, :] = jnp.where(lanes == MID, live[:, 0:8], same)

    def stats(rows, _):
        mean, rstd = row_stats(pre_ref, rows)
        rstd_ref[rows, :] = rstd
        return mean, rstd

    def work(rows, kept):
        mean, rstd = kept
        live = mask_ref[rows, MID : MID + 1]
        for b in lane_blocks(INNER):
            gains = slice(D + b.start, D + b.stop)
            xhat = (pre_ref[rows, b] - mean) * rstd
            hidden, slope = gelu_and_slope(xhat * np_ref[0:1, gains] + np_ref[1:2, gains])
            mov_ref[rows, b] = (hidden * live).astype(BF16)
            slope_ref[rows, b] = slope.astype(BF16)
            xhat_ref[rows, b] = xhat.astype(BF16)

    in_stages(tile, [stats, work])

    @pl.when(step == 0)
    def _():
        first_ref[...] = mov_ref[0:REACH, :]

    @pl.when(step == steps - 1)
    def _():
        last_ref[...] = mov_ref[tile - REACH :, :]


def load_window(low, mid, high, ext_ref, sem):
    rows = mid.shape[0]
    return [
        pltpu.make_async_copy(low, ext_ref.at[0:REACH, :], sem.at[0]),
        pltpu.make_async_copy(mid, ext_ref.at[REACH : REACH + rows, :], sem.at[1]),
        pltpu.make_async_copy(high, ext_ref.at[REACH + rows : 2 * REACH + rows, :], sem.at[2]),
    ]


def fill_taps(taps_ref, ext_ref, mask_ref, start):
    tile = taps_ref.shape[0]
    for j in range(KERNEL_TAPS):
        rows = pl.ds(pl.multiple_of(start + j * DILATION_STEP, DILATION_STEP), tile)
        picked = ext_ref[rows, :]
        if j != MID:
            picked = picked * mask_ref[:, j : j + 1].astype(BF16)
        taps_ref[:, j * INNER : (j + 1) * INNER] = picked


def conv_kernel(pieces, place_ref, low_ref, mov_ref, high_ref, mask_ref, cot_ref, np_ref, *refs):
    conv_pieces, out_pieces = refs[:pieces], refs[pieces : 2 * pieces]
    hid_ref, dconv_ref, first_ref, last_ref, sums_ref = refs[2 * pieces : 2 * pieces + 5]
    ext_ref, wc_ref, wo_ref, wt_ref, taps_ref, pre_ref, dh_ref, xhat_ref, acc_ref, sem = refs[
        2 * pieces + 5 :
    ]
    step, steps = pl.program_id(0), pl.num_programs(0)
    tile = taps_ref.shape[0]
    open_sums(acc_ref)

    @pl.when(step == 0)
    def _():
        me = place_ref[0]
        outs = piece_copies(out_pieces, wo_ref, me, sem, 3)
        rest = load_window(low_ref, mov_ref, high_ref, ext_ref, sem)
        rest += piece_copies(conv_pieces, wc_ref, me, sem, 3 + pieces)
        for copy in outs + rest:
            copy.start()
        for copy in outs:
            copy.wait()
        for k in range(0, D, 256):
            wt_ref[k : k + 256, :] = jnp.transpose(wo_ref[:, k : k + 256])
        for copy in rest:
            copy.wait()

    fill_taps(taps_ref, ext_ref, mask_ref, step * tile)
    pre_ref[...] = lax.dot_general(taps_ref[...], wc_ref[...], NN, preferred_element_type=F32)
    dh_ref[...] = lax.dot_general(cot_ref[...], wt_ref[...], NN, preferred_element_type=F32)

    def stats(rows, _):
        return row_stats(pre_ref, rows)

    def work(rows, kept):
        mean, rstd = kept
        sums = [0.0, 0.0]
        for b in lane_blocks(INNER):
            gains = slice(D + INNER + b.start, D + INNER + b.stop)
            gain = np_ref[0:1, gains]
            xhat = (pre_ref[rows, b] - mean) * rstd
            hidden, slope = gelu_and_slope(xhat * gain + np_ref[1:2, gains])
            hid_ref[rows, b] = hidden.astype(BF16)
            dy = dh_ref[rows, b] * slope
            add_terms(acc_ref, b, dy, xhat)
            dxhat = dy * gain
            xhat_ref[rows, b] = xhat
            dh_ref[rows, b] = dxhat
            sums = [sums[0] + dxhat, sums[1] + dxhat * xhat]
        return row_means(sums, INNER) + [rstd]

    def finish(rows, means):
        def put(b, value):
            dconv_ref[rows, b] = value.astype(BF16)

        norm_back(rows, dh_ref, xhat_ref, means, put)

    in_stages(tile, [stats, work, finish])
    close_sums(sums_ref, acc_ref)

    @pl.when(step == 0)
    def _():
        first_ref[...] = dconv_ref[0:REACH, :]

    @pl.when(step == steps - 1)
    def _():
        last_ref[...] = dconv_ref[tile - REACH :, :]


def put_tiles(ref, lead, first, value):
    blocks = value.shape[1] // LANE
    for g in range(value.shape[0] // SUB):
        for b in range(blocks):
            tile = value[g * SUB : (g + 1) * SUB, b * LANE : (b + 1) * LANE]
            ref[lead, first + g * blocks + b] = tile.astype(ref.dtype)


def split_by_owner(grad_ref, rows_each, core, keep_ref, send_ref, base):
    blocks = grad_ref.shape[1] // LANE
    owners = grad_ref.shape[0] // rows_each
    groups = rows_each // SUB
    for owner in range(owners):

        def body(g, carry, owner=owner):
            row = pl.multiple_of(owner * rows_each + g * SUB, SUB)
            part = grad_ref[pl.ds(row, SUB), :]

            @pl.when(core == owner % 2)
            def _():
                put_tiles(keep_ref, owner // 2, base + g * blocks, part)

            @pl.when(core != owner % 2)
            def _():
                put_tiles(send_ref, owner // 2, base + g * blocks, part)

            return carry

        lax.fori_loop(0, groups, body, 0)


def clear_rest(refs, used):
    for ref in refs:
        if used < ref.shape[1]:
            ref[:, used:] = jnp.zeros((ref.shape[0], ref.shape[1] - used, SUB, LANE), ref.dtype)


def grads_kernel(
    rows_conv, rows_out, place_ref, low_ref, mov_ref, high_ref, mask_ref, d_ref, *refs
):
    if rows_out:
        hid_ref, cot_ref, keep_ref, send_ref, ext_ref, gc_ref, go_ref, sem = refs
    else:
        keep_ref, send_ref, ext_ref, gc_ref, sem = refs
    step, steps = pl.program_id(0), pl.num_programs(0)
    tile = d_ref.shape[0]

    @pl.when(step == 0)
    def _():
        copies = load_window(low_ref, mov_ref, high_ref, ext_ref, sem)
        for copy in copies:
            copy.start()
        if rows_out:
            go_ref[...] = jnp.zeros_like(go_ref)
        gc_ref[...] = jnp.zeros_like(gc_ref)
        for copy in copies:
            copy.wait()

    if rows_out:
        go_ref[...] += lax.dot_general(hid_ref[...], cot_ref[...], TN, preferred_element_type=F32)
    for j in range(KERNEL_TAPS):
        rows = pl.ds(pl.multiple_of(step * tile + j * DILATION_STEP, DILATION_STEP), tile)
        lhs = ext_ref[rows, :]
        if j != MID:
            lhs = lhs * mask_ref[:, j : j + 1].astype(BF16)
        gc_ref[j * INNER : (j + 1) * INNER, :] += lax.dot_general(
            lhs, d_ref[...], TN, preferred_element_type=F32
        )

    @pl.when(step == steps - 1)
    def _():
        core = lax.rem(place_ref[0], 2)
        conv_tiles = rows_conv // SUB * (gc_ref.shape[1] // LANE)
        out_tiles = rows_out // SUB * (D // LANE)
        clear_rest((keep_ref, send_ref), conv_tiles + out_tiles)
        split_by_owner(gc_ref, rows_conv, core, keep_ref, send_ref, 0)
        if rows_out:
            split_by_owner(go_ref, rows_out, core, keep_ref, send_ref, conv_tiles)


def back_conv_kernel(
    pieces, rows_in, place_ref, low_ref, d_ref, high_ref, mask_ref, xhat_ref, rstd_ref, slope_ref, hid_ref, np_ref, *refs
):
    conv_pieces = refs[:pieces]
    dpre_ref, sums_ref, keep_ref, send_ref = refs[pieces : pieces + 4]
    ext_ref, wc_ref, wt_ref, taps_ref, dmov_ref, grad_ref, acc_ref, sem = refs[pieces + 4 :]
    step, steps = pl.program_id(0), pl.num_programs(0)
    tile = taps_ref.shape[0]
    open_sums(acc_ref)

    @pl.when(step == 0)
    def _():
        weights = piece_copies(conv_pieces, wc_ref, place_ref[0], sem, 3)
        window = load_window(low_ref, d_ref, high_ref, ext_ref, sem)
        for copy in weights + window:
            copy.start()
        grad_ref[...] = jnp.zeros_like(grad_ref)
        for copy in weights:
            copy.wait()
        for j in range(KERNEL_TAPS):
            source = wc_ref[j * INNER : (j + 1) * INNER, :]
            at = (KERNEL_TAPS - 1 - j) * INNER
            wt_ref[at : at + INNER, :] = jnp.transpose(source)
        for copy in window:
            copy.wait()

    fill_taps(taps_ref, ext_ref, mask_ref, step * tile)
    dmov_ref[...] = lax.dot_general(taps_ref[...], wt_ref[...], NN, preferred_element_type=F32)

    def work(rows, _):
        live = mask_ref[rows, MID : MID + 1]
        sums = [0.0, 0.0]
        for b in lane_blocks(INNER):
            xhat = xhat_ref[rows, b].astype(F32)
            dy = dmov_ref[rows, b] * live * slope_ref[rows, b].astype(F32)
            add_terms(acc_ref, b, dy, xhat)
            dxhat = dy * np_ref[0:1, D + b.start : D + b.stop]
            dmov_ref[rows, b] = dxhat
            sums = [sums[0] + dxhat, sums[1] + dxhat * xhat]
        return row_means(sums, INNER) + [rstd_ref[rows, :]]

    def finish(rows, means):
        def put(b, value):
            dpre_ref[rows, b] = value.astype(BF16)

        norm_back(rows, dmov_ref, xhat_ref, means, put)

    in_stages(tile, [work, finish])
    close_sums(sums_ref, acc_ref)
    grad_ref[...] += lax.dot_general(hid_ref[...], dpre_ref[...], TN, preferred_element_type=F32)

    @pl.when(step == steps - 1)
    def _():
        clear_rest((keep_ref, send_ref), rows_in // SUB * (INNER // LANE))
        core = lax.rem(place_ref[0], 2)
        split_by_owner(grad_ref, rows_in, core, keep_ref, send_ref, 0)


def back_a_kernel(pieces, place_ref, dpre_ref, xhat_ref, rstd_ref, slope_ref, cot_ref, np_ref, *refs):
    piece_refs = refs[:pieces]
    grad_ref, sums_ref, w_ref, wt_ref, dh_ref, acc_ref, sem = refs[pieces:]
    open_sums(acc_ref)

    @pl.when(pl.program_id(0) == 0)
    def _():
        run_copies(piece_copies(piece_refs, w_ref, place_ref[0], sem))
        for k in range(0, D, 256):
            wt_ref[:, k : k + 256] = jnp.transpose(w_ref[k : k + 256, :])

    dh_ref[...] = lax.dot_general(dpre_ref[...], wt_ref[...], NN, preferred_element_type=F32)

    def work(rows, _):
        sums = [0.0, 0.0]
        for b in lane_blocks(D):
            xhat = xhat_ref[rows, b].astype(F32)
            dy = dh_ref[rows, b] * slope_ref[rows, b].astype(F32)
            add_terms(acc_ref, b, dy, xhat)
            dxhat = dy * np_ref[0:1, b]
            dh_ref[rows, b] = dxhat
            sums = [sums[0] + dxhat, sums[1] + dxhat * xhat]
        return row_means(sums, D) + [rstd_ref[rows, :]]

    def finish(rows, means):
        def put(b, value):
            grad_ref[rows, b] = cot_ref[rows, b].astype(F32) + value

        norm_back(rows, dh_ref, xhat_ref, means, put)

    in_stages(dpre_ref.shape[0], [work, finish])
    close_sums(sums_ref, acc_ref)


def out_kernel(pieces, place_ref, hid_ref, tok_ref, *refs):
    piece_refs = refs[:pieces]
    out_ref, w_ref, sem = refs[pieces:]

    @pl.when(pl.program_id(0) == 0)
    def _():
        run_copies(piece_copies(piece_refs, w_ref, place_ref[0], sem))

    branch = lax.dot_general(hid_ref[...], w_ref[...], NN, preferred_element_type=F32)
    out_ref[...] = (tok_ref[...].astype(F32) + branch).astype(BF16)


WIDTHS = (INNER, INNER, D)
LANE0 = (0, INNER, 2 * INNER)
CUT = 2 * LANE
CHUNKS = (((1, 0, CUT), (2, 0, D)), ((1, CUT, INNER - CUT),), ((0, 0, INNER),))


def spans(chunk, rows):
    found, first = [], 0
    for weight, col, cols in chunk:
        tiles = rows[weight] // SUB * (cols // LANE)
        found.append((weight, col // LANE, cols // LANE, first, tiles))
        first += tiles
    return found, first


def pack_kernel(rows, place_ref, *refs):
    parts, states, sums = refs[0:3], refs[3:6], refs[6:9]
    pack_ref, acc_ref = refs[9:11]
    pack_ref[...] = jnp.zeros_like(pack_ref)
    for k, lane0, lane1 in ((0, 0, D), (1, D, D + INNER), (2, D + INNER, D + 2 * INNER)):
        pack_ref[0:2, lane0:lane1] = sums[k][...]
    lanes = lax.broadcasted_iota(jnp.int32, (1, LANE), 1)
    for k in range(3):
        total = jnp.sum(states[k][...].reshape(1, -1), axis=1, keepdims=True)
        pack_ref[3:4, 0:LANE] += jnp.where(lanes == k, total, 0.0)
    acc_ref[...] = jnp.zeros_like(acc_ref)
    spare = acc_ref.shape[0] - 1
    for ref, chunk in zip(parts, CHUNKS):
        start = place_ref[2] * ref.shape[0]
        found, _ = spans(chunk, rows)

        def body(k, carry, ref=ref, start=start, found=found):
            n = start + k
            slot = spare
            for weight, block0, blocks, first, tiles in found:
                here = LANE0[weight] // LANE + block0 + lax.rem(jnp.maximum(n - first, 0), blocks)
                slot = jnp.where((n >= first) & (n < first + tiles), here, slot)
            value = ref[k].astype(F32)
            acc_ref[slot] += value * value + 1e-30
            return carry

        lax.fori_loop(0, ref.shape[0], body, 0, unroll=2)
    for slot in range(spare):
        pack_ref[2:3, slot * LANE : (slot + 1) * LANE] = jnp.sum(acc_ref[slot], axis=0, keepdims=True)


def update_kernel(copies_of, pack_ref, np_ref, second_ref, *refs):
    chunk_refs, weights, row_states, col_states = refs[0:3], refs[3:6], refs[6:9], refs[9:12]
    grads, news, rows_new, cols_new = refs[12:15], refs[15:18], refs[18:21], refs[21:24]
    ngrad_ref, nsecond_ref, nnew_ref = refs[24:27]
    line_ref, state_ref, new_ref = refs[27:30]
    grad = pack_ref[0:2, :]
    second = DECAY * second_ref[...] + (1.0 - DECAY) * (grad * grad + 1e-30)
    ngrad_ref[...] = grad
    nsecond_ref[...] = second
    nnew_ref[...] = np_ref[...] - 0.2 * grad * lax.rsqrt(second)
    fans = (D, KERNEL_TAPS * INNER, INNER)
    line_ref[...] = jnp.zeros_like(line_ref)
    rows_of = [w.shape[0] for w in weights]
    sources = {0: [], 1: [], 2: []}
    for ref, chunk in zip(chunk_refs, CHUNKS):
        for weight, block0, blocks, first, _ in spans(chunk, rows_of)[0]:
            sources[weight].append((ref, block0, blocks, first))
    for k, width in enumerate(WIDTHS):
        fan, lane0 = fans[k], LANE0[k]
        rows_here = rows_of[k]
        squares = pack_ref[2:3, lane0 : lane0 + width]
        col_new = DECAY * col_states[k][...].reshape(1, -1) + (1.0 - DECAY) * (squares * (1.0 / fan))
        cols_new[k][...] = col_new.reshape(-1)
        total = DECAY * pack_ref[3:4, k : k + 1] * (1.0 / copies_of)
        total = total + (1.0 - DECAY) * (1.0 / width) * jnp.sum(squares, axis=1, keepdims=True)
        scaled = col_new / (total * (1.0 / fan))
        rate = 0.5 / fan**0.5
        line_ref[0:1, 0:rows_here] = row_states[k][...].reshape(1, -1)
        whole_rows = rows_here + -rows_here % LANE
        for c in range(0, whole_rows, LANE):
            state_ref[c : c + LANE, :] = column(line_ref[0:1, c : c + LANE])
        weight, new, grad_ref, source = weights[k], news[k], grads[k], sources[k]

        def body(g, carry, source=source, weight=weight, new=new, grad_ref=grad_ref, scaled=scaled, rate=rate, width=width):
            rows = pl.ds(pl.multiple_of(g * SUB, SUB), SUB)
            square = 0.0
            for ref, block0, blocks, first in source:
                for b in range(blocks):
                    value = ref[first + g * blocks + b].astype(F32)
                    grad_ref[rows, (block0 + b) * LANE : (block0 + b + 1) * LANE] = value
                    square = square + (value * value + 1e-30)
            mean = jnp.sum(square, axis=1, keepdims=True) * (1.0 / width)
            row_new = DECAY * state_ref[rows, :] + (1.0 - DECAY) * mean
            new_ref[rows, :] = row_new
            for ref, block0, blocks, first in source:
                for b in range(blocks):
                    lanes = slice((block0 + b) * LANE, (block0 + b + 1) * LANE)
                    value = ref[first + g * blocks + b].astype(F32)
                    step = value * lax.rsqrt(row_new * scaled[:, lanes])
                    new[rows, lanes] = weight[rows, lanes] - rate * step
            return carry

        lax.fori_loop(0, rows_here // SUB, body, 0, unroll=5)
        for c in range(0, whole_rows, LANE):
            line_ref[0:1, c : c + LANE] = jnp.transpose(new_ref[c : c + LANE, :])[0:1, :]
        rows_new[k][...] = line_ref[0:1, 0:rows_here].reshape(-1)


class Places:
    def __init__(self):
        self.seq, self.fsdp = lax.axis_size("seq"), lax.axis_size("fsdp")
        self.q = lax.axis_index("fsdp")
        self.s = lax.axis_index("seq")

    def flip(self, x, axis, bit):
        pairs = []
        for s in range(self.seq):
            for f in range(self.fsdp):
                s2, f2 = (s ^ bit, f) if axis == "seq" else (s, f ^ bit)
                pairs.append((s * self.fsdp + f, s2 * self.fsdp + f2))
        return lax.ppermute(x, AXES, pairs)


def bits_of(count):
    return [1 << k for k in range(count.bit_length() - 1)]


def gather_pieces(piece, place, after=None):
    found = {0: piece}
    for bit in reversed(bits_of(place.fsdp)):
        for k in list(found):
            found[k | bit] = place.flip(found[k], "fsdp", bit)
        if after is not None and bit > 1:
            for k in found:
                found[k], _ = lax.optimization_barrier((found[k], after))
    return [found[k] for k in range(place.fsdp)]


def sum_everywhere(x, place):
    for axis, count in (("fsdp", place.fsdp), ("seq", place.seq)):
        for bit in bits_of(count):
            x = x + place.flip(x, axis, bit)
    return x


def pick(x, index):
    return lax.dynamic_index_in_dim(x, index, axis=0, keepdims=False)


def reduce_grad(keep, send, place):
    got = place.flip(send, "fsdp", 1)
    bit, total, width = place.fsdp // 2, keep, keep.shape[0]
    while width > 1:
        half = width // 2
        side = (place.q // bit) % 2
        parts = (2, half) + keep.shape[1:]
        total, got = total.reshape(parts), got.reshape(parts)
        away = pick(total, 1 - side) + pick(got, 1 - side).astype(F32)
        near = pick(total, side) + pick(got, side).astype(F32)
        total, got = near, place.flip(away.astype(BF16), "fsdp", bit)
        width, bit = half, bit // 2
    total = (total + got.astype(F32)).astype(BF16)
    total = total.reshape((place.seq, -1) + keep.shape[2:])
    got = lax.all_to_all(total, "seq", split_axis=0, concat_axis=0)
    return jnp.sum(got.astype(F32), axis=0).astype(BF16)


def spread(part, place):
    copies = jnp.broadcast_to(part[None], (place.seq,) + part.shape)
    got = lax.all_to_all(copies, "seq", split_axis=0, concat_axis=0)
    return got.reshape((-1,) + part.shape[1:])


def on_device(
    tokens, input_mask, doc_lengths, cotangent, w_in, w_conv, w_out, norm_params,
    row_in, col_in, row_conv, col_conv, row_out, col_out, norm_second,
):
    place = Places()
    rows = tokens.shape[0]
    pieces = place.fsdp
    spots = jnp.stack([place.q, (place.s * place.fsdp + place.q) * rows, place.s]).astype(jnp.int32)
    docs = doc_lengths.shape[0]
    ends = jnp.pad(
        jnp.cumsum(doc_lengths).astype(F32), (0, -docs % LANE), constant_values=1e9
    ).reshape(1, -1)
    live = input_mask.reshape(-1, LANE)

    in_pieces = gather_pieces(w_in.astype(BF16), place)
    low_conv, low_out, *in_pieces = lax.optimization_barrier(
        (w_conv.astype(BF16), w_out.astype(BF16), *in_pieces)
    )

    tile_a, tile = 256, 512
    steps = rows // tile
    params_spec = whole(2, D + 2 * INNER)
    dma = pltpu.SemaphoreType.DMA

    hidden_a, slope_a, xhat_a, rstd_a = call(
        norm_a_kernel,
        (rows // tile_a,),
        [rows_spec(tile_a, D), params_spec],
        [rows_spec(tile_a, D)] * 3 + [rows_spec(tile_a, 1)],
        [shape((rows, D), BF16)] * 3 + [shape((rows, 1), F32)],
        us=20,
    )(tokens, norm_params)
    conv_pieces = gather_pieces(low_conv, place, hidden_a)
    out_pieces = gather_pieces(low_out, place, conv_pieces[place.fsdp // 2])

    moved, slope_b, xhat_b, rstd_b, masks, m_first, m_last = call(
        functools.partial(in_kernel, pieces),
        (steps,),
        [SMEM, whole(*ends.shape), rows_spec(tile, D), whole(*live.shape), params_spec]
        + [ANY] * pieces,
        [rows_spec(tile, INNER)] * 3
        + [rows_spec(tile, 1), rows_spec(tile, 8), whole(REACH, INNER), whole(REACH, INNER)],
        [shape((rows, INNER), BF16)] * 3
        + [
            shape((rows, 1), F32),
            shape((rows, 8), F32),
            shape((REACH, INNER), BF16),
            shape((REACH, INNER), BF16),
        ],
        [pltpu.VMEM((D, INNER), BF16), pltpu.VMEM((tile, INNER), F32), dma((pieces,))],
        us=20,
    )(spots, ends, hidden_a, live, norm_params, *in_pieces)

    total = place.seq * place.fsdp
    up = [(i, i + 1) for i in range(total - 1)]
    down = [(i + 1, i) for i in range(total - 1)]
    m_low, m_high = lax.ppermute(m_last, AXES, up), lax.ppermute(m_first, AXES, down)

    ext = pltpu.VMEM((rows + 2 * REACH, INNER), BF16)
    hidden_c, d_conv, d_first, d_last, sums_c = call(
        functools.partial(conv_kernel, pieces),
        (steps,),
        [SMEM, ANY, ANY, ANY, rows_spec(tile, 8), rows_spec(tile, D), params_spec]
        + [ANY] * (2 * pieces),
        [rows_spec(tile, INNER)] * 2
        + [whole(REACH, INNER), whole(REACH, INNER), whole(2, INNER)],
        [
            shape((rows, INNER), BF16),
            shape((rows, INNER), BF16),
            shape((REACH, INNER), BF16),
            shape((REACH, INNER), BF16),
            shape((2, INNER), F32),
        ],
        [
            ext,
            pltpu.VMEM((KERNEL_TAPS * INNER, INNER), BF16),
            pltpu.VMEM((INNER, D), BF16),
            pltpu.VMEM((D, INNER), BF16),
            pltpu.VMEM((tile, KERNEL_TAPS * INNER), BF16),
            pltpu.VMEM((tile, INNER), F32),
            pltpu.VMEM((tile, INNER), F32),
            pltpu.VMEM((tile, INNER), F32),
            pltpu.VMEM((16, INNER), F32),
            dma((3 + 2 * pieces,)),
        ],
        us=35,
    )(spots, m_low, moved, m_high, masks, cotangent, norm_params, *conv_pieces, *out_pieces)
    d_low, d_high = lax.ppermute(d_last, AXES, up), lax.ppermute(d_first, AXES, down)

    shards = place.fsdp // 2
    weights = (w_in, w_conv, w_out)
    rows_of = [w.shape[0] for w in weights]

    def halves(chunk):
        count = spans(chunk, rows_of)[1]
        dims = (shards, count + -count % place.seq, SUB, LANE)
        return [whole(*dims)] * 2, [shape(dims, F32), shape(dims, BF16)]

    parts = []
    for chunk, d_cols in zip(CHUNKS, (d_conv[:, :CUT], d_conv[:, CUT:])):
        half_specs, half_shapes = halves(chunk)
        cols = d_cols.shape[1]
        first = chunk[-1][0] == 2
        keep, send = call(
            functools.partial(grads_kernel, w_conv.shape[0], w_out.shape[0] if first else 0),
            (steps,),
            [SMEM, ANY, ANY, ANY, rows_spec(tile, 8), rows_spec(tile, cols)]
            + ([rows_spec(tile, INNER), rows_spec(tile, D)] if first else []),
            half_specs,
            half_shapes,
            [ext, pltpu.VMEM((KERNEL_TAPS * INNER, cols), F32)]
            + ([pltpu.VMEM((INNER, D), F32)] if first else [])
            + [dma((3,))],
            us=13,
        )(spots, m_low, moved, m_high, masks, d_cols, *((hidden_c, cotangent) if first else ()))
        parts.append(reduce_grad(keep, send, place))

    half_specs, half_shapes = halves(CHUNKS[2])
    d_pre, sums_b, keep_in, send_in = call(
        functools.partial(back_conv_kernel, pieces, w_in.shape[0]),
        (steps,),
        [SMEM, ANY, ANY, ANY, rows_spec(tile, 8), rows_spec(tile, INNER), rows_spec(tile, 1)]
        + [rows_spec(tile, INNER), rows_spec(tile, D), params_spec]
        + [ANY] * pieces,
        [rows_spec(tile, INNER), whole(2, INNER)] + half_specs,
        [shape((rows, INNER), BF16), shape((2, INNER), F32)] + half_shapes,
        [
            ext,
            pltpu.VMEM((KERNEL_TAPS * INNER, INNER), BF16),
            pltpu.VMEM((KERNEL_TAPS * INNER, INNER), BF16),
            pltpu.VMEM((tile, KERNEL_TAPS * INNER), BF16),
            pltpu.VMEM((tile, INNER), F32),
            pltpu.VMEM((D, INNER), F32),
            pltpu.VMEM((16, INNER), F32),
            dma((3 + pieces,)),
        ],
        us=36,
    )(
        spots, d_low, d_conv, d_high, masks, xhat_b, rstd_b, slope_b, hidden_a, norm_params,
        *conv_pieces,
    )
    parts.append(reduce_grad(keep_in, send_in, place))

    input_grad, sums_a = call(
        functools.partial(back_a_kernel, pieces),
        (steps,),
        [SMEM, rows_spec(tile, INNER), rows_spec(tile, D), rows_spec(tile, 1)]
        + [rows_spec(tile, D)] * 2
        + [params_spec]
        + [ANY] * pieces,
        [rows_spec(tile, D), whole(2, D)],
        [shape((rows, D), F32), shape((2, D), F32)],
        [
            pltpu.VMEM((D, INNER), BF16),
            pltpu.VMEM((INNER, D), BF16),
            pltpu.VMEM((tile, D), F32),
            pltpu.VMEM((16, D), F32),
            dma((pieces,)),
        ],
        us=18,
    )(spots, d_pre, xhat_a, rstd_a, slope_a, cotangent, norm_params, *in_pieces)

    (block_out,) = call(
        functools.partial(out_kernel, pieces),
        (steps,),
        [SMEM, rows_spec(tile, INNER), rows_spec(tile, D)] + [ANY] * pieces,
        [rows_spec(tile, D)],
        [shape((rows, D), BF16)],
        [pltpu.VMEM((INNER, D), BF16), dma((pieces,))],
        us=9,
    )(spots, hidden_c, tokens, *out_pieces)

    fulls = [spread(part, place) for part in parts]
    row_states, col_states = (row_in, row_conv, row_out), (col_in, col_conv, col_out)
    row_specs = [whole(*r.shape) for r in row_states]
    col_specs = [whole(*c.shape) for c in col_states]
    cols_all = D + 2 * INNER
    (pack,) = call(
        functools.partial(pack_kernel, rows_of),
        (1,),
        [SMEM]
        + [whole(*p.shape) for p in parts]
        + row_specs
        + [whole(2, D), whole(2, INNER), whole(2, INNER)],
        [whole(4, cols_all)],
        [shape((4, cols_all), F32)],
        [pltpu.VMEM((cols_all // LANE + 1, SUB, LANE), F32)],
        us=2,
    )(spots, *parts, *row_states, sums_a, sums_b, sums_c)
    pack = sum_everywhere(pack, place)
    weight_specs = [whole(*w.shape) for w in weights]
    lines = max(w.shape[0] + -w.shape[0] % LANE for w in weights)
    results = call(
        functools.partial(update_kernel, place.seq),
        (1,),
        [whole(4, cols_all), params_spec, params_spec]
        + [whole(*f.shape) for f in fulls]
        + weight_specs
        + row_specs
        + col_specs,
        weight_specs * 2 + row_specs + col_specs + [params_spec] * 3,
        [shape(w.shape, F32) for w in weights] * 2
        + [shape(r.shape, F32) for r in row_states + col_states]
        + [shape((2, cols_all), F32)] * 3,
        [pltpu.VMEM((8, lines), F32), pltpu.VMEM((lines, LANE), F32), pltpu.VMEM((lines, LANE), F32)],
        us=9,
    )(pack, norm_params, norm_second, *fulls, *weights, *row_states, *col_states)
    rows_new, cols_new = results[6:9], results[9:12]
    return (
        block_out,
        input_grad,
        *results[0:6],
        rows_new[0],
        cols_new[0],
        rows_new[1],
        cols_new[1],
        rows_new[2],
        cols_new[2],
        *results[12:15],
    )


def solution(mesh):
    both, rows = P(AXES, None), P("fsdp", None)
    in_specs = (
        both, P(AXES), P(), both, rows, rows, rows, P(),
        P("fsdp"), P(), P("fsdp"), P(), P("fsdp"), P(), P(),
    )
    out_specs = (
        both, both, rows, rows, rows, rows, rows, rows,
        P("fsdp"), P(), P("fsdp"), P(), P("fsdp"), P(), P(), P(), P(),
    )
    return jax.shard_map(
        on_device, mesh=mesh, in_specs=in_specs, out_specs=out_specs, check_vma=False
    )
```

```python
import functools
import math

import jax
import jax.numpy as jnp
from jax import lax
from jax.experimental import pallas as pl
from jax.experimental.pallas import tpu as pltpu
from jax.sharding import PartitionSpec as P

D = 1280
INNER = 640
KERNEL_TAPS = 5
DILATION_STEP = 128
STEP = 10
EPSILON = 1e-05
DECAY = 1.0 - STEP ** (-0.8)

REACH = (KERNEL_TAPS - 1) // 2 * DILATION_STEP
MID = (KERNEL_TAPS - 1) // 2
F32 = jnp.float32
BF16 = jnp.bfloat16
SUB, LANE = 16, 128
AXES = ("seq", "fsdp")
NT = (((1,), (1,)), ((), ()))
TN = (((0,), (0,)), ((), ()))
NN = (((1,), (0,)), ((), ()))
VMEM_LIMIT = 58 * 1024 * 1024


def call(kernel, grid, in_specs, out_specs, out_shape, scratch=(), us=1.0, aliases=None):
    params = pltpu.CompilerParams(
        vmem_limit_bytes=VMEM_LIMIT, dimension_semantics=("arbitrary",) * len(grid)
    )
    return pl.pallas_call(
        kernel,
        grid=grid,
        in_specs=in_specs,
        out_specs=out_specs,
        out_shape=out_shape,
        scratch_shapes=list(scratch),
        compiler_params=params,
        input_output_aliases=aliases or {},
        cost_estimate=pl.CostEstimate(
                flops=int(us * 1.1e9), bytes_accessed=int(us * 3.4e6), transcendentals=0
        ),
    )


def shape(dims, dtype):
    return jax.ShapeDtypeStruct(dims, dtype)


def rows_spec(tile, width):
    return pl.BlockSpec((tile, width), lambda i: (i, 0))


def whole(*dims):
    return pl.BlockSpec(dims, lambda *_: (0,) * len(dims))


ANY = pl.BlockSpec(memory_space=pl.ANY)
SMEM = pl.BlockSpec(memory_space=pltpu.SMEM)


ERFC_P = 0.47 / math.sqrt(2.0)
ERFC_C = (
    0.12357219400743558,
    0.1999878668208835,
    -0.08033356004356296,
    0.3660253986657854,
    -0.1092519747040215,
)
LOG2E = 1.4426950408889634


def gelu_and_slope(y):
    t = pltpu.reciprocal(1.0 + ERFC_P * jnp.abs(y), approx=True)
    bell = jnp.exp2(y * y * (-0.5 * LOG2E))
    poly = ERFC_C[4] * t + ERFC_C[3]
    for c in ERFC_C[2::-1]:
        poly = poly * t + c
    tail = poly * t * bell
    cdf = jnp.where(y > 0.0, 1.0 - tail, tail)
    return y * cdf, cdf + y * (bell * (1.0 / math.sqrt(2.0 * math.pi)))


def lane_blocks(width):
    return [slice(k, k + LANE) for k in range(0, width, LANE)]


def row_stats(ref, rows):
    width = ref.shape[-1]
    blocks = lane_blocks(width)
    total = ref[rows, blocks[0]].astype(F32)
    for b in blocks[1:]:
        total = total + ref[rows, b].astype(F32)
    mean = jnp.sum(total, axis=-1, keepdims=True) * (1.0 / width)
    square = None
    for b in blocks:
        centered = ref[rows, b].astype(F32) - mean
        square = centered * centered if square is None else square + centered * centered
    variance = jnp.sum(square, axis=-1, keepdims=True) * (1.0 / width)
    return mean, lax.rsqrt(variance + EPSILON)


def fold(values):
    total = values[0:8]
    for k in range(8, values.shape[0], 8):
        total = total + values[k : k + 8]
    return total


def in_stages(count, stages):
    chunks = [slice(k, k + CHUNK) for k in range(0, count, CHUNK)]
    kept = {}
    for t in range(len(chunks) + len(stages) - 1):
        for n, stage in enumerate(stages):
            if 0 <= t - n < len(chunks):
                kept[n, t - n] = stage(chunks[t - n], kept.get((n - 1, t - n)))


def halves_of(count):
    return (slice(0, count // 2), slice(count // 2, count))


def row_means(sums, width):
    return [jnp.sum(x, axis=-1, keepdims=True) * (1.0 / width) for x in sums]


def norm_back(rows, dxhat_ref, xhat_ref, means, put):
    mean_d, mean_dx, rstd = means
    for b in lane_blocks(dxhat_ref.shape[-1]):
        xhat = xhat_ref[rows, b].astype(F32)
        put(b, (dxhat_ref[rows, b] - mean_d - xhat * mean_dx) * rstd)


def add_terms(acc_ref, b, dy, xhat):
    acc_ref[0:8, b] += fold(dy * xhat)
    acc_ref[8:16, b] += fold(dy)


def open_sums(acc_ref):
    @pl.when(pl.program_id(0) == 0)
    def _():
        acc_ref[...] = jnp.zeros_like(acc_ref)


def close_sums(out_ref, acc_ref):
    @pl.when(pl.program_id(0) == pl.num_programs(0) - 1)
    def _():
        out_ref[0:1, :] = jnp.sum(acc_ref[0:8, :], axis=0, keepdims=True)
        out_ref[1:2, :] = jnp.sum(acc_ref[8:16, :], axis=0, keepdims=True)


def run_copies(copies):
    for copy in copies:
        copy.start()
    for copy in copies:
        copy.wait()


def piece_copies(pieces, full_ref, me, sem, first=0):
    each = full_ref.shape[0] // len(pieces)
    return [
        pltpu.make_async_copy(
            piece,
            full_ref.at[pl.ds(pl.multiple_of((me ^ k) * each, SUB), each), :],
            sem.at[first + k],
        )
        for k, piece in enumerate(pieces)
    ]


def column(row):
    return jnp.transpose(jnp.broadcast_to(row, (LANE, LANE)))


CHUNK = 64


def norm_a_kernel(tok_ref, np_ref, hid_ref, slope_ref, xhat_ref, rstd_ref):
    def stats(rows, _):
        mean, rstd = row_stats(tok_ref, rows)
        rstd_ref[rows, :] = rstd
        return mean, rstd

    def work(rows, kept):
        mean, rstd = kept
        for b in lane_blocks(D):
            xhat = (tok_ref[rows, b].astype(F32) - mean) * rstd
            hidden, slope = gelu_and_slope(xhat * np_ref[0:1, b] + np_ref[1:2, b])
            hid_ref[rows, b] = hidden.astype(BF16)
            slope_ref[rows, b] = slope.astype(BF16)
            xhat_ref[rows, b] = xhat.astype(BF16)

    in_stages(tok_ref.shape[0], [stats, work])


def in_kernel(pieces, place_ref, ends_ref, hid_ref, live_ref, np_ref, *refs):
    piece_refs = refs[:pieces]
    mov_ref, slope_ref, xhat_ref, rstd_ref, mask_ref, first_ref, last_ref = refs[pieces : pieces + 7]
    w_ref, pre_ref, sem = refs[pieces + 7 :]
    step, steps = pl.program_id(0), pl.num_programs(0)
    tile = hid_ref.shape[0]

    @pl.when(step == 0)
    def _():
        run_copies(piece_copies(piece_refs, w_ref, place_ref[0], sem))

    for half in halves_of(tile):
        pre_ref[half, :] = lax.dot_general(
            hid_ref[half, :], w_ref[...], NN, preferred_element_type=F32
        )

    first = place_ref[1] + step * tile
    ends = ends_ref[...]
    lanes = lax.broadcasted_iota(jnp.int32, (LANE, 8), 1)
    offsets = ((lanes - MID) * DILATION_STEP).astype(F32)
    for k in range(tile // LANE):
        at = (first + k * LANE + lax.broadcasted_iota(jnp.int32, (LANE, 1), 0)).astype(F32)
        begin = jnp.max(jnp.where(ends <= at, ends, 0.0), axis=1, keepdims=True)
        end = jnp.min(jnp.where(ends > at, ends, 1e9), axis=1, keepdims=True)
        there = at + offsets
        same = jnp.where((there >= begin) & (there < end), 1.0, 0.0)
        live = column(live_ref[pl.ds(step * (tile // LANE) + k, 1), :].astype(F32))
        mask_ref[k * LANE : (k + 1) * LANE, :] = jnp.where(lanes == MID, live[:, 0:8], same)

    def stats(rows, _):
        mean, rstd = row_stats(pre_ref, rows)
        rstd_ref[rows, :] = rstd
        return mean, rstd

    def work(rows, kept):
        mean, rstd = kept
        live = mask_ref[rows, MID : MID + 1]
        for b in lane_blocks(INNER):
            gains = slice(D + b.start, D + b.stop)
            xhat = (pre_ref[rows, b] - mean) * rstd
            hidden, slope = gelu_and_slope(xhat * np_ref[0:1, gains] + np_ref[1:2, gains])
            mov_ref[rows, b] = (hidden * live).astype(BF16)
            slope_ref[rows, b] = slope.astype(BF16)
            xhat_ref[rows, b] = xhat.astype(BF16)

    in_stages(tile, [stats, work])

    @pl.when(step == 0)
    def _():
        first_ref[...] = mov_ref[0:REACH, :]

    @pl.when(step == steps - 1)
    def _():
        last_ref[...] = mov_ref[tile - REACH :, :]


def load_window(low, mid, high, ext_ref, sem):
    rows = mid.shape[0]
    return [
        pltpu.make_async_copy(low, ext_ref.at[0:REACH, :], sem.at[0]),
        pltpu.make_async_copy(mid, ext_ref.at[REACH : REACH + rows, :], sem.at[1]),
        pltpu.make_async_copy(high, ext_ref.at[REACH + rows : 2 * REACH + rows, :], sem.at[2]),
    ]


def fill_taps(taps_ref, ext_ref, mask_ref, start):
    tile = taps_ref.shape[0]
    for j in range(KERNEL_TAPS):
        rows = pl.ds(pl.multiple_of(start + j * DILATION_STEP, DILATION_STEP), tile)
        picked = ext_ref[rows, :]
        if j != MID:
            picked = picked * mask_ref[:, j : j + 1].astype(BF16)
        taps_ref[:, j * INNER : (j + 1) * INNER] = picked


def conv_kernel(pieces, place_ref, low_ref, mov_ref, high_ref, mask_ref, cot_ref, np_ref, *refs):
    conv_pieces, out_pieces = refs[:pieces], refs[pieces : 2 * pieces]
    hid_ref, dconv_ref, taps_ref, first_ref, last_ref, sums_ref, turned_ref = refs[
        2 * pieces : 2 * pieces + 7
    ]
    ext_ref, wc_ref, wct_ref, wo_ref, wt_ref, pre_ref, dh_ref, xhat_ref, acc_ref, sem = refs[
        2 * pieces + 7 :
    ]
    step, steps = pl.program_id(0), pl.num_programs(0)
    tile = taps_ref.shape[0]
    open_sums(acc_ref)

    @pl.when(step == 0)
    def _():
        me = place_ref[0]
        outs = piece_copies(out_pieces, wo_ref, me, sem, 3)
        rest = load_window(low_ref, mov_ref, high_ref, ext_ref, sem)
        rest += piece_copies(conv_pieces, wc_ref, me, sem, 3 + pieces)
        for copy in outs + rest:
            copy.start()
        for copy in outs:
            copy.wait()
        for k in range(0, D, 256):
            wt_ref[k : k + 256, :] = jnp.transpose(wo_ref[:, k : k + 256])
        for copy in rest:
            copy.wait()

    fill_taps(taps_ref, ext_ref, mask_ref, step * tile)
    for half in halves_of(tile):
        pre_ref[half, :] = lax.dot_general(
            taps_ref[half, :], wc_ref[...], NN, preferred_element_type=F32
        )
        dh_ref[half, :] = lax.dot_general(
            cot_ref[half, :], wt_ref[...], NN, preferred_element_type=F32
        )
    each = wc_ref.shape[0] // KERNEL_TAPS
    for n in range(2):
        tap = jnp.minimum(2 * step + n, KERNEL_TAPS - 1)
        source = wc_ref[pl.ds(pl.multiple_of(tap * each, SUB), each), :]
        target = pl.multiple_of((KERNEL_TAPS - 1 - tap) * each, SUB)
        wct_ref[pl.ds(target, each), :] = jnp.transpose(source)

    def stats(rows, _):
        return row_stats(pre_ref, rows)

    def work(rows, kept):
        mean, rstd = kept
        sums = [0.0, 0.0]
        for b in lane_blocks(INNER):
            gains = slice(D + INNER + b.start, D + INNER + b.stop)
            gain = np_ref[0:1, gains]
            xhat = (pre_ref[rows, b] - mean) * rstd
            hidden, slope = gelu_and_slope(xhat * gain + np_ref[1:2, gains])
            hid_ref[rows, b] = hidden.astype(BF16)
            dy = dh_ref[rows, b] * slope
            add_terms(acc_ref, b, dy, xhat)
            dxhat = dy * gain
            xhat_ref[rows, b] = xhat
            dh_ref[rows, b] = dxhat
            sums = [sums[0] + dxhat, sums[1] + dxhat * xhat]
        return row_means(sums, INNER) + [rstd]

    def finish(rows, means):
        def put(b, value):
            dconv_ref[rows, b] = value.astype(BF16)

        norm_back(rows, dh_ref, xhat_ref, means, put)

    in_stages(tile, [stats, work, finish])
    close_sums(sums_ref, acc_ref)

    @pl.when(step == steps - 1)
    def _():
        run_copies([pltpu.make_async_copy(wct_ref, turned_ref, sem.at[0])])

    @pl.when(step == 0)
    def _():
        first_ref[...] = dconv_ref[0:REACH, :]

    @pl.when(step == steps - 1)
    def _():
        last_ref[...] = dconv_ref[tile - REACH :, :]


def stage_tiles(stage_ref, core, first_row, rows_each, base, block0, blocks, value):
    for g in range(value.shape[0] // SUB):
        row = first_row + g * SUB
        owner, inside = row // rows_each, row % rows_each // SUB
        side = core ^ (owner % 2)
        for b in range(value.shape[1] // LANE):
            tile = value[g * SUB : (g + 1) * SUB, b * LANE : (b + 1) * LANE]
            at = base + inside * blocks + block0 + b
            stage_ref[side, owner // 2, at] = tile.astype(BF16)


def stage_plain(stage_ref, core, grad_ref, rows_each, base):
    blocks = grad_ref.shape[1] // LANE
    for row in range(0, grad_ref.shape[0], SUB):
        part = grad_ref[row : row + SUB, :]
        stage_tiles(stage_ref, core, row, rows_each, base, 0, blocks, part)


def stage_turned(stage_ref, core, turned_ref, rows_each, base):
    blocks = turned_ref.shape[0] // LANE
    for row in range(0, turned_ref.shape[1], LANE):
        for b in range(blocks):
            part = jnp.transpose(turned_ref[b * LANE : (b + 1) * LANE, row : row + LANE])
            stage_tiles(stage_ref, core, row, rows_each, base, b, blocks, part)


def finish_stage(stage_ref, keep_ref, send_ref, used, sem):
    count = stage_ref.shape[2]
    if used < count:
        dims = stage_ref.shape[:2] + (count - used, SUB, LANE)
        stage_ref[:, :, used:] = jnp.zeros(dims, BF16)
    run_copies(
        [
            pltpu.make_async_copy(stage_ref.at[0], keep_ref, sem.at[0]),
            pltpu.make_async_copy(stage_ref.at[1], send_ref, sem.at[1]),
        ]
    )


def grads_kernel(cols, rows_conv, rows_out, place_ref, taps_ref, d_ref, *refs):
    if rows_out:
        hid_ref, cot_ref, keep_ref, send_ref, stage_ref, gc_ref, sem, go_ref = refs
    else:
        keep_ref, send_ref, stage_ref, gc_ref, sem = refs
    step, steps = pl.program_id(0), pl.num_programs(0)

    @pl.when(step == 0)
    def _():
        gc_ref[...] = jnp.zeros_like(gc_ref)
        if rows_out:
            go_ref[...] = jnp.zeros_like(go_ref)

    gc_ref[...] += lax.dot_general(
        d_ref[:, cols], taps_ref[...], TN, preferred_element_type=F32
    )
    if rows_out:
        go_ref[...] += lax.dot_general(hid_ref[...], cot_ref[...], TN, preferred_element_type=F32)

    @pl.when(step == steps - 1)
    def _():
        core = lax.rem(place_ref[0], 2)
        conv_tiles = rows_conv // SUB * (gc_ref.shape[0] // LANE)
        stage_turned(stage_ref, core, gc_ref, rows_conv, 0)
        if rows_out:
            stage_plain(stage_ref, core, go_ref, rows_out, conv_tiles)
        used = conv_tiles + rows_out // SUB * (D // LANE)
        finish_stage(stage_ref, keep_ref, send_ref, used, sem)


def back_conv_kernel(
    last, rows_in, place_ref, low_ref, d_ref, high_ref, turned_ref, mask_ref, xhat_ref, rstd_ref, slope_ref, hid_ref, np_ref, *refs
):
    if last:
        before_ref, dpre_ref, sums_ref, keep_ref, send_ref, stage_ref = refs[:6]
    else:
        dpre_ref, sums_ref, part_ref = refs[:3]
    ext_ref, wt_ref, taps_ref, dmov_ref, grad_ref, acc_ref, sem = refs[-7:]
    step, steps = pl.program_id(0), pl.num_programs(0)
    tile = taps_ref.shape[0]
    open_sums(acc_ref)

    @pl.when(step == 0)
    def _():
        copies = load_window(low_ref, d_ref, high_ref, ext_ref, sem)
        copies.append(pltpu.make_async_copy(turned_ref, wt_ref, sem.at[3]))
        if last:
            copies.append(pltpu.make_async_copy(before_ref, grad_ref, sem.at[4]))
        for copy in copies:
            copy.start()
        if not last:
            grad_ref[...] = jnp.zeros_like(grad_ref)
        for copy in copies:
            copy.wait()

    fill_taps(taps_ref, ext_ref, mask_ref, (steps * last + step) * tile)
    for half in halves_of(tile):
        dmov_ref[half, :] = lax.dot_general(
            taps_ref[half, :], wt_ref[...], NN, preferred_element_type=F32
        )

    def work(rows, _):
        live = mask_ref[rows, MID : MID + 1]
        sums = [0.0, 0.0]
        for b in lane_blocks(INNER):
            xhat = xhat_ref[rows, b].astype(F32)
            dy = dmov_ref[rows, b] * live * slope_ref[rows, b].astype(F32)
            add_terms(acc_ref, b, dy, xhat)
            dxhat = dy * np_ref[0:1, D + b.start : D + b.stop]
            dmov_ref[rows, b] = dxhat
            sums = [sums[0] + dxhat, sums[1] + dxhat * xhat]
        return row_means(sums, INNER) + [rstd_ref[rows, :]]

    def finish(rows, means):
        def put(b, value):
            dpre_ref[rows, b] = value.astype(BF16)

        norm_back(rows, dmov_ref, xhat_ref, means, put)

    in_stages(tile, [work, finish])
    close_sums(sums_ref, acc_ref)
    grad_ref[...] += lax.dot_general(dpre_ref[...], hid_ref[...], TN, preferred_element_type=F32)

    @pl.when(step == steps - 1)
    def _():
        if last:
            stage_turned(stage_ref, lax.rem(place_ref[0], 2), grad_ref, rows_in, 0)
            used = rows_in // SUB * (INNER // LANE)
            finish_stage(stage_ref, keep_ref, send_ref, used, sem)
        else:
            run_copies([pltpu.make_async_copy(grad_ref, part_ref, sem.at[0])])


def back_a_kernel(pieces, place_ref, dpre_ref, xhat_ref, rstd_ref, slope_ref, cot_ref, np_ref, *refs):
    piece_refs = refs[:pieces]
    grad_ref, sums_ref, w_ref, wt_ref, dh_ref, acc_ref, sem = refs[-7:]
    open_sums(acc_ref)

    @pl.when(pl.program_id(0) == 0)
    def _():
        run_copies(piece_copies(piece_refs, w_ref, place_ref[0], sem))
        for k in range(0, D, 256):
            wt_ref[:, k : k + 256] = jnp.transpose(w_ref[k : k + 256, :])

    dh_ref[...] = lax.dot_general(dpre_ref[...], wt_ref[...], NN, preferred_element_type=F32)

    def work(rows, _):
        sums = [0.0, 0.0]
        for b in lane_blocks(D):
            xhat = xhat_ref[rows, b].astype(F32)
            dy = dh_ref[rows, b] * slope_ref[rows, b].astype(F32)
            add_terms(acc_ref, b, dy, xhat)
            dxhat = dy * np_ref[0:1, b]
            dh_ref[rows, b] = dxhat
            sums = [sums[0] + dxhat, sums[1] + dxhat * xhat]
        return row_means(sums, D) + [rstd_ref[rows, :]]

    def finish(rows, means):
        def put(b, value):
            grad_ref[rows, b] = cot_ref[rows, b].astype(F32) + value

        norm_back(rows, dh_ref, xhat_ref, means, put)

    in_stages(dpre_ref.shape[0], [work, finish])
    close_sums(sums_ref, acc_ref)


def out_kernel(pieces, place_ref, hid_ref, tok_ref, *refs):
    piece_refs = refs[:pieces]
    out_ref, w_ref, sem = refs[pieces:]

    @pl.when(pl.program_id(0) == 0)
    def _():
        run_copies(piece_copies(piece_refs, w_ref, place_ref[0], sem))

    branch = lax.dot_general(hid_ref[...], w_ref[...], NN, preferred_element_type=F32)
    out_ref[...] = (tok_ref[...].astype(F32) + branch).astype(BF16)


WIDTHS = (INNER, INNER, D)
LANE0 = (0, INNER, 2 * INNER)
CUT = 2 * LANE
CHUNKS = (((1, 0, CUT), (2, 0, D)), ((1, CUT, INNER - CUT),), ((0, 0, INNER),))


def spans(chunk, rows):
    found, first = [], 0
    for weight, col, cols in chunk:
        tiles = rows[weight] // SUB * (cols // LANE)
        found.append((weight, col // LANE, cols // LANE, first, tiles))
        first += tiles
    return found, first


def add_columns(acc_ref, place_ref, ref, chunk, rows):
    start = (place_ref[2] % 2 * (place_ref[3] // 2) + place_ref[2] // 2) * ref.shape[0]
    found, _ = spans(chunk, rows)
    spare = acc_ref.shape[0] - 1

    def body(k, carry):
        n = start + k
        slot = spare
        for weight, block0, blocks, first, tiles in found:
            here = LANE0[weight] // LANE + block0 + lax.rem(jnp.maximum(n - first, 0), blocks)
            slot = jnp.where((n >= first) & (n < first + tiles), here, slot)
        value = ref[k].astype(F32)
        acc_ref[slot] += value * value + 1e-30
        return carry

    lax.fori_loop(0, ref.shape[0], body, 0, unroll=2)


def pack_kernel(rows, place_ref, *refs):
    parts, states, sums = refs[0:2], refs[2:5], refs[5:10]
    pack_ref, acc_ref = refs[10:12]
    pack_ref[...] = jnp.zeros_like(pack_ref)
    lanes_of = ((0, D), (0, D), (D, D + INNER), (D, D + INNER), (D + INNER, D + 2 * INNER))
    for part, (lane0, lane1) in zip(sums, lanes_of):
        pack_ref[0:2, lane0:lane1] += part[...]
    lanes = lax.broadcasted_iota(jnp.int32, (1, LANE), 1)
    for k in range(3):
        total = jnp.sum(states[k][...].reshape(1, -1), axis=1, keepdims=True)
        pack_ref[3:4, 0:LANE] += jnp.where(lanes == k, total, 0.0)
    acc_ref[...] = jnp.zeros_like(acc_ref)
    for ref, chunk in zip(parts, CHUNKS):
        add_columns(acc_ref, place_ref, ref, chunk, rows)
    for slot in range(acc_ref.shape[0] - 1):
        pack_ref[2:3, slot * LANE : (slot + 1) * LANE] = jnp.sum(acc_ref[slot], axis=0, keepdims=True)


def pack_in_kernel(rows, place_ref, part_ref, pack_ref, acc_ref):
    acc_ref[...] = jnp.zeros_like(acc_ref)
    add_columns(acc_ref, place_ref, part_ref, CHUNKS[2], rows)
    for slot in range(acc_ref.shape[0] - 1):
        total = jnp.sum(acc_ref[slot], axis=0, keepdims=True)
        pack_ref[:, slot * LANE : (slot + 1) * LANE] = jnp.broadcast_to(total, (8, LANE))


def update_weight(
    k, copies_of, squares, states_sum, source, weight, state, col_state, grad_ref, new, row_new_ref, col_new_ref, scratch
):
    line_ref, state_ref, new_ref = scratch
    width, fan, rows_here = WIDTHS[k], (D, KERNEL_TAPS * INNER, INNER)[k], weight.shape[0]
    col_new = DECAY * col_state[...].reshape(1, -1) + (1.0 - DECAY) * (squares * (1.0 / fan))
    col_new_ref[...] = col_new.reshape(-1)
    total = DECAY * states_sum * (1.0 / copies_of)
    total = total + (1.0 - DECAY) * (1.0 / width) * jnp.sum(squares, axis=1, keepdims=True)
    scaled = col_new / (total * (1.0 / fan))
    rate = 0.5 / fan**0.5
    line_ref[0:1, 0:rows_here] = state[...].reshape(1, -1)
    whole_rows = rows_here + -rows_here % LANE
    for c in range(0, whole_rows, LANE):
        state_ref[c : c + LANE, :] = column(line_ref[0:1, c : c + LANE])

    def body(g, carry):
        rows = pl.ds(pl.multiple_of(g * SUB, SUB), SUB)
        square = 0.0
        for ref, block0, blocks, first in source:
            for b in range(blocks):
                value = ref[first + g * blocks + b].astype(F32)
                grad_ref[rows, (block0 + b) * LANE : (block0 + b + 1) * LANE] = value
                square = square + (value * value + 1e-30)
        mean = jnp.sum(square, axis=1, keepdims=True) * (1.0 / width)
        row_new = DECAY * state_ref[rows, :] + (1.0 - DECAY) * mean
        new_ref[rows, :] = row_new
        for ref, block0, blocks, first in source:
            for b in range(blocks):
                lanes = slice((block0 + b) * LANE, (block0 + b + 1) * LANE)
                value = ref[first + g * blocks + b].astype(F32)
                step = value * lax.rsqrt(row_new * scaled[:, lanes])
                new[rows, lanes] = weight[rows, lanes] - rate * step
        return carry

    lax.fori_loop(0, rows_here // SUB, body, 0, unroll=5)
    for c in range(0, whole_rows, LANE):
        line_ref[0:1, c : c + LANE] = jnp.transpose(new_ref[c : c + LANE, :])[0:1, :]
    row_new_ref[...] = line_ref[0:1, 0:rows_here].reshape(-1)


def tile_copies(place_ref, mine, other, full_ref, sem, first):
    y = place_ref[2] % 2
    half = full_ref.shape[0] // 2
    return [
        pltpu.make_async_copy(ref, full_ref.at[pl.ds(side * half, half)], sem.at[first + n])
        for n, (ref, side) in enumerate(((mine, y), (other, 1 - y)))
    ]


def sources_of(chunk, ref, rows):
    return {w: (ref, block0, blocks, first) for w, block0, blocks, first, _ in spans(chunk, rows)[0]}


def update_kernel(copies_of, rows, place_ref, *refs):
    (m1, o1, m2, o2, pack_ref, np_ref, second_ref) = refs[0:7]
    weights, states, col_states = refs[7:9], refs[9:11], refs[11:13]
    grads, news, rows_new, cols_new = refs[13:15], refs[15:17], refs[17:19], refs[19:21]
    ngrad_ref, nsecond_ref, nnew_ref = refs[21:24]
    full1_ref, full2_ref, sem = refs[24:27]
    copies = tile_copies(place_ref, m1, o1, full1_ref, sem, 0)
    copies += tile_copies(place_ref, m2, o2, full2_ref, sem, 2)
    for copy in copies:
        copy.start()
    grad = pack_ref[0:2, :]
    second = DECAY * second_ref[...] + (1.0 - DECAY) * (grad * grad + 1e-30)
    ngrad_ref[...] = grad
    nsecond_ref[...] = second
    nnew_ref[...] = np_ref[...] - 0.2 * grad * lax.rsqrt(second)
    for copy in copies:
        copy.wait()
    from1 = sources_of(CHUNKS[0], full1_ref, rows)
    from2 = sources_of(CHUNKS[1], full2_ref, rows)
    for n, (k, source) in enumerate(((1, [from1[1], from2[1]]), (2, [from1[2]]))):
        squares = pack_ref[2:3, LANE0[k] : LANE0[k] + WIDTHS[k]]
        update_weight(
            k, copies_of, squares, pack_ref[3:4, k : k + 1], source, weights[n], states[n],
            col_states[n], grads[n], news[n], rows_new[n], cols_new[n], refs[27:30],
        )


def update_in_kernel(copies_of, rows, place_ref, mine, other, pack_in_ref, pack_ref, *refs):
    weight, state, col_state, grad_ref, new_ref, row_new_ref, col_new_ref, full_ref, sem = refs[:9]
    run_copies(tile_copies(place_ref, mine, other, full_ref, sem, 0))
    update_weight(
        0, copies_of, pack_in_ref[0:1, :], pack_ref[3:4, 0:1],
        [sources_of(CHUNKS[2], full_ref, rows)[0]], weight, state, col_state, grad_ref, new_ref,
        row_new_ref, col_new_ref, refs[9:12],
    )


class Places:
    def __init__(self):
        self.seq, self.fsdp = lax.axis_size("seq"), lax.axis_size("fsdp")
        self.q = lax.axis_index("fsdp")
        self.s = lax.axis_index("seq")

    def flip(self, x, axis, bit):
        pairs = []
        for s in range(self.seq):
            for f in range(self.fsdp):
                s2, f2 = (s ^ bit, f) if axis == "seq" else (s, f ^ bit)
                pairs.append((s * self.fsdp + f, s2 * self.fsdp + f2))
        return lax.ppermute(x, AXES, pairs)


def bits_of(count):
    return [1 << k for k in range(count.bit_length() - 1)]


def tie(x, *others):
    return lax.optimization_barrier((x, *others))[0]


def gather_pieces(piece, place, after):
    found = {0: piece}
    for bit in reversed(bits_of(place.fsdp)):
        for k in list(found):
            moving = tie(found[k], after) if bit == 1 else found[k]
            found[k | bit] = place.flip(moving, "fsdp", bit)
    return [found[k] for k in range(place.fsdp)]


def sum_everywhere(x, place):
    for axis, count in (("fsdp", place.fsdp), ("seq", place.seq)):
        for bit in bits_of(count):
            x = x + place.flip(x, axis, bit)
    return x


def pick(x, index):
    return lax.dynamic_index_in_dim(x, index, axis=0, keepdims=False)


class Reduction:
    def __init__(self, place, keep, send):
        self.place, self.near = place, keep
        self.got = place.flip(send, "fsdp", 1)
        self.shards = keep.shape[0]
        self.line = [[y + 2 * z for z in range(place.seq // 2)] for y in range(2)]

    def halve(self, axis, bit, side, after):
        parts = (2, -1) + self.near.shape[-3:] if axis == "fsdp" else (2, -1) + self.near.shape[-2:]
        near, got = self.near.reshape(parts), tie(self.got, after).reshape(parts)
        away = (pick(near, 1 - side).astype(F32) + pick(got, 1 - side).astype(F32)).astype(BF16)
        self.near = pick(near, side).astype(F32) + pick(got, side).astype(F32)
        self.got = self.place.flip(away, axis, bit)
        return away

    def x(self, after):
        place = self.place
        bit, away = place.fsdp // 2, None
        while bit > 1:
            away = self.halve("fsdp", bit, (place.q // bit) % 2, after)
            bit //= 2
        self.near, self.got = self.near.reshape(self.near.shape[-3:]), self.got.reshape(self.got.shape[-3:])
        return away

    def y(self, after):
        return self.halve("seq", 1, self.place.s % 2, after)

    def z(self, after):
        total = (self.near + tie(self.got, after).astype(F32)).astype(BF16)
        total = total.reshape((self.place.seq // 2, -1) + total.shape[1:])
        self.got = lax.all_to_all(total, "seq", 0, 0, axis_index_groups=self.line)
        return total

    def back_z(self, after):
        self.part = jnp.sum(tie(self.got, after).astype(F32), axis=0).astype(BF16)
        copies = jnp.broadcast_to(self.part[None], (self.place.seq // 2,) + self.part.shape)
        self.got = lax.all_to_all(copies, "seq", 0, 0, axis_index_groups=self.line)
        return copies

    def back_y(self, after):
        self.mine = tie(self.got, after).reshape((-1,) + self.got.shape[2:])
        self.other = self.place.flip(self.mine, "seq", 1)
        return self.mine


def on_device(
    tokens, input_mask, doc_lengths, cotangent, w_in, w_conv, w_out, norm_params,
    row_in, col_in, row_conv, col_conv, row_out, col_out, norm_second,
):
    place = Places()
    rows = tokens.shape[0]
    pieces = place.fsdp
    spots = jnp.stack(
        [place.q, (place.s * place.fsdp + place.q) * rows, place.s, place.seq]
    ).astype(jnp.int32)
    docs = doc_lengths.shape[0]
    ends = jnp.pad(
        jnp.cumsum(doc_lengths).astype(F32), (0, -docs % LANE), constant_values=1e9
    ).reshape(1, -1)
    live = input_mask.reshape(-1, LANE)
    weights = (w_in, w_conv, w_out)
    rows_of = [w.shape[0] for w in weights]

    tile_a, tile = 256, 512
    steps = rows // tile
    params_spec = whole(2, D + 2 * INNER)
    dma = pltpu.SemaphoreType.DMA

    hidden_a, slope_a, xhat_a, rstd_a = call(
        norm_a_kernel,
        (rows // tile_a,),
        [rows_spec(tile_a, D), params_spec],
        [rows_spec(tile_a, D)] * 3 + [rows_spec(tile_a, 1)],
        [shape((rows, D), BF16)] * 3 + [shape((rows, 1), F32)],
        us=17,
    )(tokens, norm_params)

    in_pieces = gather_pieces(w_in.astype(BF16), place, hidden_a)
    conv_pieces = gather_pieces(w_conv.astype(BF16), place, hidden_a)
    out_pieces = gather_pieces(w_out.astype(BF16), place, hidden_a)

    moved, slope_b, xhat_b, rstd_b, masks, m_first, m_last = call(
        functools.partial(in_kernel, pieces),
        (steps,),
        [SMEM, whole(*ends.shape), rows_spec(tile, D), whole(*live.shape), params_spec]
        + [ANY] * pieces,
        [rows_spec(tile, INNER)] * 3
        + [rows_spec(tile, 1), rows_spec(tile, 8), whole(REACH, INNER), whole(REACH, INNER)],
        [shape((rows, INNER), BF16)] * 3
        + [
            shape((rows, 1), F32),
            shape((rows, 8), F32),
            shape((REACH, INNER), BF16),
            shape((REACH, INNER), BF16),
        ],
        [pltpu.VMEM((D, INNER), BF16), pltpu.VMEM((tile, INNER), F32), dma((pieces,))],
        us=16,
    )(spots, ends, hidden_a, live, norm_params, *in_pieces)

    total = place.seq * place.fsdp
    up = [(i, i + 1) for i in range(total - 1)]
    down = [(i + 1, i) for i in range(total - 1)]
    m_low, m_high = lax.ppermute(m_last, AXES, up), lax.ppermute(m_first, AXES, down)

    ext = pltpu.VMEM((rows + 2 * REACH, INNER), BF16)
    taps_wide = KERNEL_TAPS * INNER
    wide = pltpu.VMEM((taps_wide, INNER), BF16)
    hidden_c, d_conv, taps, d_first, d_last, sums_c, turned = call(
        functools.partial(conv_kernel, pieces),
        (steps,),
        [SMEM, ANY, ANY, ANY, rows_spec(tile, 8), rows_spec(tile, D), params_spec]
        + [ANY] * (2 * pieces),
        [rows_spec(tile, INNER)] * 2
        + [rows_spec(tile, taps_wide), whole(REACH, INNER), whole(REACH, INNER), whole(2, INNER), ANY],
        [
            shape((rows, INNER), BF16),
            shape((rows, INNER), BF16),
            shape((rows, taps_wide), BF16),
            shape((REACH, INNER), BF16),
            shape((REACH, INNER), BF16),
            shape((2, INNER), F32),
            shape((taps_wide, INNER), BF16),
        ],
        [
            ext,
            wide,
            wide,
            pltpu.VMEM((INNER, D), BF16),
            pltpu.VMEM((D, INNER), BF16),
            pltpu.VMEM((tile, INNER), F32),
            pltpu.VMEM((tile, INNER), F32),
            pltpu.VMEM((tile, INNER), F32),
            pltpu.VMEM((16, INNER), F32),
            dma((3 + 2 * pieces,)),
        ],
        us=30,
    )(spots, m_low, moved, m_high, masks, cotangent, norm_params, *conv_pieces, *out_pieces)
    d_low, d_high = lax.ppermute(d_last, AXES, up), lax.ppermute(d_first, AXES, down)

    shards = place.fsdp // 2

    def half_dims(chunk):
        count = spans(chunk, rows_of)[1]
        return (shards, count + -count % place.seq, SUB, LANE)

    def gradients(chunk, cols, out_too, d_conv):
        dims = half_dims(chunk)
        return call(
            functools.partial(grads_kernel, cols, w_conv.shape[0], w_out.shape[0] if out_too else 0),
            (steps,),
            [SMEM, rows_spec(tile, taps_wide), rows_spec(tile, INNER)]
            + ([rows_spec(tile, INNER), rows_spec(tile, D)] if out_too else []),
            [ANY] * 2,
            [shape(dims, BF16)] * 2,
            [
                pltpu.VMEM((2,) + dims, BF16),
                pltpu.VMEM((cols.stop - cols.start, taps_wide), F32),
                dma((2,)),
            ]
            + ([pltpu.VMEM((INNER, D), F32)] if out_too else []),
            us=13,
        )(spots, taps, d_conv, *((hidden_c, cotangent) if out_too else ()))

    keep, send = gradients(CHUNKS[0], slice(0, CUT), True, d_conv)
    first = Reduction(place, keep, send)
    keep, send = gradients(CHUNKS[1], slice(CUT, INNER), False, tie(d_conv, send, d_low, d_high))
    second = Reduction(place, keep, send)

    def back_conv(last, spots, before):
        here = steps // 2
        at = here * last

        def here_spec(width):
            return pl.BlockSpec((tile, width), lambda i: (i + at, 0))

        dims = half_dims(CHUNKS[2])
        return call(
            functools.partial(back_conv_kernel, last, w_in.shape[0]),
            (here,),
            [SMEM] + [ANY] * 4
            + [here_spec(8), here_spec(INNER), here_spec(1), here_spec(INNER), here_spec(D)]
            + [params_spec]
            + [ANY] * last,
            [rows_spec(tile, INNER), whole(2, INNER)] + [ANY] * (1 + last),
            [shape((rows // 2, INNER), BF16), shape((2, INNER), F32)]
            + ([shape(dims, BF16)] * 2 if last else [shape((INNER, D), F32)]),
            ([pltpu.VMEM((2,) + dims, BF16)] if last else [])
            + [
                ext,
                wide,
                pltpu.VMEM((tile, taps_wide), BF16),
                pltpu.VMEM((tile, INNER), F32),
                pltpu.VMEM((INNER, D), F32),
                pltpu.VMEM((16, INNER), F32),
                dma((5,)),
            ],
            us=16,
        )(
            spots, d_low, d_conv, d_high, turned, masks, xhat_b, rstd_b, slope_b, hidden_a,
            norm_params, *before,
        )

    def back_a(last, spots, d_pre, before):
        here = steps // 2
        at = here * last

        def here_spec(width):
            return pl.BlockSpec((tile, width), lambda i: (i + at, 0))

        return call(
            functools.partial(back_a_kernel, pieces),
            (here,),
            [SMEM, rows_spec(tile, INNER), here_spec(D), here_spec(1), here_spec(D), here_spec(D)]
            + [params_spec]
            + [ANY] * (pieces + last),
            [here_spec(D), whole(2, D)],
            [shape((rows, D), F32), shape((2, D), F32)],
            [
                pltpu.VMEM((D, INNER), BF16),
                pltpu.VMEM((INNER, D), BF16),
                pltpu.VMEM((tile, D), F32),
                pltpu.VMEM((16, D), F32),
                dma((pieces,)),
            ],
            us=9,
            aliases={7 + pieces: 0} if last else None,
        )(spots, d_pre, xhat_a, rstd_a, slope_a, cotangent, norm_params, *in_pieces, *before)

    away = first.x(send)
    d_pre0, sums_b0, grad_part = back_conv(0, tie(spots, away, send), ())
    away = (first.y(d_pre0), second.x(d_pre0))
    d_pre1, sums_b1, keep, send = back_conv(1, tie(spots, *away), (grad_part,))
    third = Reduction(place, keep, send)
    away = (first.z(d_pre1), second.y(d_pre1))
    input_grad, sums_a0 = back_a(0, tie(spots, *away, send), d_pre0, ())
    away = (first.back_z(input_grad), second.z(input_grad), third.x(input_grad))
    input_grad, sums_a1 = back_a(1, tie(spots, *away), d_pre1, (input_grad,))
    away = (first.back_y(input_grad), second.back_z(input_grad), third.y(input_grad))
    (block_out,) = call(
        functools.partial(out_kernel, pieces),
        (steps,),
        [SMEM, rows_spec(tile, INNER), rows_spec(tile, D)] + [ANY] * pieces,
        [rows_spec(tile, D)],
        [shape((rows, D), BF16)],
        [pltpu.VMEM((INNER, D), BF16), dma((pieces,))],
        us=9,
    )(tie(spots, *away), hidden_c, tokens, *out_pieces)
    second.back_y(block_out)
    third.z(block_out)
    third.back_z(block_out)
    third.back_y(block_out)

    row_states, col_states = (row_in, row_conv, row_out), (col_in, col_conv, col_out)
    row_specs = [whole(*r.shape) for r in row_states]
    col_specs = [whole(*c.shape) for c in col_states]
    cols_all = D + 2 * INNER
    sums = (sums_a0, sums_a1, sums_b0, sums_b1, sums_c)
    squares = pltpu.VMEM((cols_all // LANE + 1, SUB, LANE), F32)
    (pack,) = call(
        functools.partial(pack_kernel, rows_of),
        (1,),
        [SMEM, whole(*first.part.shape), whole(*second.part.shape)]
        + row_specs
        + [whole(*x.shape) for x in sums],
        [whole(4, cols_all)],
        [shape((4, cols_all), F32)],
        [squares],
        us=2,
    )(spots, first.part, second.part, *row_states, *sums)
    pack = sum_everywhere(pack, place)
    (pack_in,) = call(
        functools.partial(pack_in_kernel, rows_of),
        (1,),
        [SMEM, whole(*third.part.shape)],
        [whole(8, INNER)],
        [shape((8, INNER), F32)],
        [pltpu.VMEM((INNER // LANE + 1, SUB, LANE), F32)],
        us=1,
    )(spots, third.part)
    pack_in = sum_everywhere(pack_in, place)

    def update_scratch(chunks, weights):
        lines = max(w.shape[0] + -w.shape[0] % LANE for w in weights)
        return (
            [pltpu.VMEM(half_dims(c)[1:], BF16) for c in chunks]
            + [dma((2 * len(chunks),))]
            + [pltpu.VMEM((8, lines), F32)]
            + [pltpu.VMEM((lines, LANE), F32)] * 2
        )

    weight_specs = [whole(*w.shape) for w in weights]
    results = call(
        functools.partial(update_kernel, place.seq, rows_of),
        (1,),
        [SMEM]
        + [ANY] * 4
        + [whole(4, cols_all), params_spec, params_spec]
        + weight_specs[1:]
        + row_specs[1:]
        + col_specs[1:],
        weight_specs[1:] * 2 + row_specs[1:] + col_specs[1:] + [params_spec] * 3,
        [shape(w.shape, F32) for w in weights[1:]] * 2
        + [shape(r.shape, F32) for r in row_states[1:] + col_states[1:]]
        + [shape((2, cols_all), F32)] * 3,
        update_scratch(CHUNKS[:2], weights[1:]),
        us=7,
    )(
        spots, first.mine, first.other, second.mine, second.other, pack, norm_params, norm_second,
        *weights[1:], *row_states[1:], *col_states[1:],
    )
    grad_conv, grad_out, new_conv, new_out, row_conv_new, row_out_new, col_conv_new, col_out_new = (
        results[0:8]
    )
    grad_in, new_in, row_in_new, col_in_new = call(
        functools.partial(update_in_kernel, place.seq, rows_of),
        (1,),
        [SMEM, ANY, ANY, whole(8, INNER), whole(4, cols_all)]
        + [weight_specs[0], row_specs[0], col_specs[0]],
        [weight_specs[0]] * 2 + [row_specs[0], col_specs[0]],
        [shape(w_in.shape, F32)] * 2 + [shape(row_in.shape, F32), shape(col_in.shape, F32)],
        update_scratch(CHUNKS[2:], weights[:1]),
        us=3,
    )(spots, third.mine, third.other, pack_in, pack, w_in, row_in, col_in)
    return (
        block_out,
        input_grad,
        grad_in,
        grad_conv,
        grad_out,
        new_in,
        new_conv,
        new_out,
        row_in_new,
        col_in_new,
        row_conv_new,
        col_conv_new,
        row_out_new,
        col_out_new,
        *results[8:11],
    )


def solution(mesh):
    both, rows = P(AXES, None), P("fsdp", None)
    in_specs = (
        both, P(AXES), P(), both, rows, rows, rows, P(),
        P("fsdp"), P(), P("fsdp"), P(), P("fsdp"), P(), P(),
    )
    out_specs = (
        both, both, rows, rows, rows, rows, rows, rows,
        P("fsdp"), P(), P("fsdp"), P(), P("fsdp"), P(), P(), P(), P(),
    )
    return jax.shard_map(
        on_device, mesh=mesh, in_specs=in_specs, out_specs=out_specs, check_vma=False
    )
```

```python
import functools
import math

import jax
import jax.numpy as jnp
from jax import lax
from jax.experimental import pallas as pl
from jax.experimental.pallas import tpu as pltpu
from jax.sharding import PartitionSpec as P

D = 1280
INNER = 640
KERNEL_TAPS = 5
DILATION_STEP = 128
STEP = 10
EPSILON = 1e-05
DECAY = 1.0 - STEP ** (-0.8)

REACH = (KERNEL_TAPS - 1) // 2 * DILATION_STEP
MID = (KERNEL_TAPS - 1) // 2
F32 = jnp.float32
BF16 = jnp.bfloat16
SUB, LANE = 16, 128
AXES = ("seq", "fsdp")
NT = (((1,), (1,)), ((), ()))
TN = (((0,), (0,)), ((), ()))
NN = (((1,), (0,)), ((), ()))
VMEM_LIMIT = 58 * 1024 * 1024


def call(kernel, grid, in_specs, out_specs, out_shape, scratch=(), us=1.0, aliases=None):
    params = pltpu.CompilerParams(
        vmem_limit_bytes=VMEM_LIMIT, dimension_semantics=("arbitrary",) * len(grid)
    )
    return pl.pallas_call(
        kernel,
        grid=grid,
        in_specs=in_specs,
        out_specs=out_specs,
        out_shape=out_shape,
        scratch_shapes=list(scratch),
        compiler_params=params,
        input_output_aliases=aliases or {},
        cost_estimate=pl.CostEstimate(
                flops=int(us * 1.1e9), bytes_accessed=int(us * 3.4e6), transcendentals=0
        ),
    )


def shape(dims, dtype):
    return jax.ShapeDtypeStruct(dims, dtype)


def rows_spec(tile, width):
    return pl.BlockSpec((tile, width), lambda i: (i, 0))


def whole(*dims):
    return pl.BlockSpec(dims, lambda *_: (0,) * len(dims))


ANY = pl.BlockSpec(memory_space=pl.ANY)
SMEM = pl.BlockSpec(memory_space=pltpu.SMEM)


ERFC_P = 0.47 / math.sqrt(2.0)
ERFC_C = (
    0.12357219400743558,
    0.1999878668208835,
    -0.08033356004356296,
    0.3660253986657854,
    -0.1092519747040215,
)
LOG2E = 1.4426950408889634


def gelu_and_slope(y):
    t = pltpu.reciprocal(1.0 + ERFC_P * jnp.abs(y), approx=True)
    bell = jnp.exp2(y * y * (-0.5 * LOG2E))
    poly = ERFC_C[4] * t + ERFC_C[3]
    for c in ERFC_C[2::-1]:
        poly = poly * t + c
    tail = poly * t * bell
    cdf = jnp.where(y > 0.0, 1.0 - tail, tail)
    return y * cdf, cdf + y * (bell * (1.0 / math.sqrt(2.0 * math.pi)))


def lane_blocks(width):
    return [slice(k, k + LANE) for k in range(0, width, LANE)]


def row_stats(ref, rows):
    width = ref.shape[-1]
    blocks = lane_blocks(width)
    total = ref[rows, blocks[0]].astype(F32)
    for b in blocks[1:]:
        total = total + ref[rows, b].astype(F32)
    mean = jnp.sum(total, axis=-1, keepdims=True) * (1.0 / width)
    square = None
    for b in blocks:
        centered = ref[rows, b].astype(F32) - mean
        square = centered * centered if square is None else square + centered * centered
    variance = jnp.sum(square, axis=-1, keepdims=True) * (1.0 / width)
    return mean, lax.rsqrt(variance + EPSILON)


def fold(values):
    total = values[0:8]
    for k in range(8, values.shape[0], 8):
        total = total + values[k : k + 8]
    return total


def in_stages(count, stages):
    chunks = [slice(k, k + CHUNK) for k in range(0, count, CHUNK)]
    kept = {}
    for t in range(len(chunks) + len(stages) - 1):
        for n, stage in enumerate(stages):
            if 0 <= t - n < len(chunks):
                kept[n, t - n] = stage(chunks[t - n], kept.get((n - 1, t - n)))


def halves_of(count):
    return (slice(0, count // 2), slice(count // 2, count))


def row_means(sums, width):
    return [jnp.sum(x, axis=-1, keepdims=True) * (1.0 / width) for x in sums]


def norm_back(rows, dxhat_ref, xhat_ref, means, put):
    mean_d, mean_dx, rstd = means
    for b in lane_blocks(dxhat_ref.shape[-1]):
        xhat = xhat_ref[rows, b].astype(F32)
        put(b, (dxhat_ref[rows, b] - mean_d - xhat * mean_dx) * rstd)


def add_terms(acc_ref, b, dy, xhat):
    acc_ref[0:8, b] += fold(dy * xhat)
    acc_ref[8:16, b] += fold(dy)


def open_sums(acc_ref):
    @pl.when(pl.program_id(0) == 0)
    def _():
        acc_ref[...] = jnp.zeros_like(acc_ref)


def close_sums(out_ref, acc_ref):
    @pl.when(pl.program_id(0) == pl.num_programs(0) - 1)
    def _():
        out_ref[0:1, :] = jnp.sum(acc_ref[0:8, :], axis=0, keepdims=True)
        out_ref[1:2, :] = jnp.sum(acc_ref[8:16, :], axis=0, keepdims=True)


def run_copies(copies):
    for copy in copies:
        copy.start()
    for copy in copies:
        copy.wait()


def piece_copies(pieces, full_ref, me, sem, first=0):
    each = full_ref.shape[0] // len(pieces)
    return [
        pltpu.make_async_copy(
            piece.at[0:each, :],
            full_ref.at[pl.ds(pl.multiple_of((me ^ k) * each, SUB), each), :],
            sem.at[first + k],
        )
        for k, piece in enumerate(pieces)
    ]


def out_copies(pieces, full_ref, me, sem, first=0):
    each, width = full_ref.shape[0] // len(pieces), full_ref.shape[1] // 2
    copies = []
    for k, piece in enumerate(pieces):
        rows = pl.ds(pl.multiple_of((me ^ k) * each, SUB), each)
        for side in range(2):
            at = piece.shape[0] - (2 - side) * each
            copies.append(
                pltpu.make_async_copy(
                    piece.at[at : at + each, :],
                    full_ref.at[rows, side * width : (side + 1) * width],
                    sem.at[first + 2 * k + side],
                )
            )
    return copies


def column(row):
    return jnp.transpose(jnp.broadcast_to(row, (LANE, LANE)))


CHUNK = 64


def norm_a_kernel(tok_ref, np_ref, hid_ref, slope_ref, xhat_ref, rstd_ref):
    def stats(rows, _):
        mean, rstd = row_stats(tok_ref, rows)
        rstd_ref[rows, :] = rstd
        return mean, rstd

    def work(rows, kept):
        mean, rstd = kept
        for b in lane_blocks(D):
            xhat = (tok_ref[rows, b].astype(F32) - mean) * rstd
            hidden, slope = gelu_and_slope(xhat * np_ref[0:1, b] + np_ref[1:2, b])
            hid_ref[rows, b] = hidden.astype(BF16)
            slope_ref[rows, b] = slope.astype(BF16)
            xhat_ref[rows, b] = xhat.astype(BF16)

    in_stages(tok_ref.shape[0], [stats, work])


def in_kernel(pieces, tiles, place_ref, ends_ref, hid_ref, live_ref, np_ref, *refs):
    piece_refs = refs[:pieces]
    edges = tiles[0] == 0
    outs = refs[-(10 if edges else 8) :]
    mov_ref, slope_ref, xhat_ref, rstd_ref, mask_ref = outs[:5]
    w_ref, pre_ref, sem = outs[-3:]
    step = pl.program_id(0)
    tile = hid_ref.shape[0]

    @pl.when(step == 0)
    def _():
        run_copies(piece_copies(piece_refs, w_ref, place_ref[0], sem))

    for half in halves_of(tile):
        pre_ref[half, :] = lax.dot_general(
            hid_ref[half, :], w_ref[...], NN, preferred_element_type=F32
        )

    at_tile = tiles[0] + step * tiles[1]
    first = place_ref[1] + at_tile * tile
    ends = ends_ref[...]
    lanes = lax.broadcasted_iota(jnp.int32, (LANE, 8), 1)
    offsets = ((lanes - MID) * DILATION_STEP).astype(F32)
    for k in range(tile // LANE):
        at = (first + k * LANE + lax.broadcasted_iota(jnp.int32, (LANE, 1), 0)).astype(F32)
        begin = jnp.max(jnp.where(ends <= at, ends, 0.0), axis=1, keepdims=True)
        end = jnp.min(jnp.where(ends > at, ends, 1e9), axis=1, keepdims=True)
        there = at + offsets
        same = jnp.where((there >= begin) & (there < end), 1.0, 0.0)
        live = column(live_ref[pl.ds(at_tile * (tile // LANE) + k, 1), :].astype(F32))
        mask_ref[k * LANE : (k + 1) * LANE, :] = jnp.where(lanes == MID, live[:, 0:8], same)

    def stats(rows, _):
        mean, rstd = row_stats(pre_ref, rows)
        rstd_ref[rows, :] = rstd
        return mean, rstd

    def work(rows, kept):
        mean, rstd = kept
        live = mask_ref[rows, MID : MID + 1]
        for b in lane_blocks(INNER):
            gains = slice(D + b.start, D + b.stop)
            xhat = (pre_ref[rows, b] - mean) * rstd
            hidden, slope = gelu_and_slope(xhat * np_ref[0:1, gains] + np_ref[1:2, gains])
            mov_ref[rows, b] = (hidden * live).astype(BF16)
            slope_ref[rows, b] = slope.astype(BF16)
            xhat_ref[rows, b] = xhat.astype(BF16)

    in_stages(tile, [stats, work])
    if edges:
        first_ref, last_ref = outs[5:7]

        @pl.when(step == 0)
        def _():
            first_ref[...] = mov_ref[0:REACH, :]

        @pl.when(step == 1)
        def _():
            last_ref[...] = mov_ref[tile - REACH :, :]


def load_window(low, mid, high, ext_ref, sem):
    rows = mid.shape[0]
    return [
        pltpu.make_async_copy(low, ext_ref.at[0:REACH, :], sem.at[0]),
        pltpu.make_async_copy(mid, ext_ref.at[REACH : REACH + rows, :], sem.at[1]),
        pltpu.make_async_copy(high, ext_ref.at[REACH + rows : 2 * REACH + rows, :], sem.at[2]),
    ]


def fill_taps(taps_ref, ext_ref, mask_ref, start):
    tile = taps_ref.shape[0]
    for j in range(KERNEL_TAPS):
        rows = pl.ds(pl.multiple_of(start + j * DILATION_STEP, DILATION_STEP), tile)
        picked = ext_ref[rows, :]
        if j != MID:
            picked = picked * mask_ref[:, j : j + 1].astype(BF16)
        taps_ref[:, j * INNER : (j + 1) * INNER] = picked


def conv_kernel(pieces, place_ref, low_ref, mov_ref, high_ref, mask_ref, cot_ref, np_ref, *refs):
    piece_refs = refs[:pieces]
    hid_ref, dconv_ref, taps_ref, first_ref, last_ref, sums_ref, turned_ref = refs[
        pieces : pieces + 7
    ]
    ext_ref, wc_ref, wct_ref, wo_ref, wt_ref, pre_ref, dh_ref, xhat_ref, acc_ref, sem = refs[
        pieces + 7 :
    ]
    step, steps = pl.program_id(0), pl.num_programs(0)
    tile = taps_ref.shape[0]
    open_sums(acc_ref)

    @pl.when(step == 0)
    def _():
        me = place_ref[0]
        outs = out_copies(piece_refs, wo_ref, me, sem, 3)
        rest = load_window(low_ref, mov_ref, high_ref, ext_ref, sem)
        rest += piece_copies(piece_refs, wc_ref, me, sem, 3 + 2 * pieces)
        for copy in outs + rest:
            copy.start()
        for copy in outs:
            copy.wait()
        for k in range(0, D, 256):
            wt_ref[k : k + 256, :] = jnp.transpose(wo_ref[:, k : k + 256])
        for copy in rest:
            copy.wait()

    fill_taps(taps_ref, ext_ref, mask_ref, step * tile)
    for half in halves_of(tile):
        pre_ref[half, :] = lax.dot_general(
            taps_ref[half, :], wc_ref[...], NN, preferred_element_type=F32
        )
        dh_ref[half, :] = lax.dot_general(
            cot_ref[half, :], wt_ref[...], NN, preferred_element_type=F32
        )
    each = wc_ref.shape[0] // KERNEL_TAPS
    for n in range(2):
        tap = jnp.minimum(2 * step + n, KERNEL_TAPS - 1)
        source = wc_ref[pl.ds(pl.multiple_of(tap * each, SUB), each), :]
        target = pl.multiple_of((KERNEL_TAPS - 1 - tap) * each, SUB)
        wct_ref[pl.ds(target, each), :] = jnp.transpose(source)

    def stats(rows, _):
        return row_stats(pre_ref, rows)

    def work(rows, kept):
        mean, rstd = kept
        sums = [0.0, 0.0]
        for b in lane_blocks(INNER):
            gains = slice(D + INNER + b.start, D + INNER + b.stop)
            gain = np_ref[0:1, gains]
            xhat = (pre_ref[rows, b] - mean) * rstd
            hidden, slope = gelu_and_slope(xhat * gain + np_ref[1:2, gains])
            hid_ref[rows, b] = hidden.astype(BF16)
            dy = dh_ref[rows, b] * slope
            add_terms(acc_ref, b, dy, xhat)
            dxhat = dy * gain
            xhat_ref[rows, b] = xhat
            dh_ref[rows, b] = dxhat
            sums = [sums[0] + dxhat, sums[1] + dxhat * xhat]
        return row_means(sums, INNER) + [rstd]

    def finish(rows, means):
        def put(b, value):
            dconv_ref[rows, b] = value.astype(BF16)

        norm_back(rows, dh_ref, xhat_ref, means, put)

    in_stages(tile, [stats, work, finish])
    close_sums(sums_ref, acc_ref)

    @pl.when(step == steps - 1)
    def _():
        run_copies([pltpu.make_async_copy(wct_ref, turned_ref, sem.at[0])])

    @pl.when(step == 0)
    def _():
        first_ref[...] = dconv_ref[0:REACH, :]

    @pl.when(step == steps - 1)
    def _():
        last_ref[...] = dconv_ref[tile - REACH :, :]


def stage_tiles(stage_ref, core, first_row, rows_each, base, block0, blocks, value):
    for g in range(value.shape[0] // SUB):
        row = first_row + g * SUB
        owner, inside = row // rows_each, row % rows_each // SUB
        side = core ^ (owner % 2)
        for b in range(value.shape[1] // LANE):
            tile = value[g * SUB : (g + 1) * SUB, b * LANE : (b + 1) * LANE]
            at = base + inside * blocks + block0 + b
            stage_ref[side, owner // 2, at] = tile.astype(BF16)


def stage_plain(stage_ref, core, grad_ref, rows_each, base):
    blocks = grad_ref.shape[1] // LANE
    for row in range(0, grad_ref.shape[0], SUB):
        part = grad_ref[row : row + SUB, :]
        stage_tiles(stage_ref, core, row, rows_each, base, 0, blocks, part)


def stage_turned(stage_ref, core, turned_ref, rows_each, base):
    blocks = turned_ref.shape[0] // LANE
    for row in range(0, turned_ref.shape[1], LANE):
        for b in range(blocks):
            part = jnp.transpose(turned_ref[b * LANE : (b + 1) * LANE, row : row + LANE])
            stage_tiles(stage_ref, core, row, rows_each, base, b, blocks, part)


def finish_stage(stage_ref, keep_ref, send_ref, used, sem):
    count = stage_ref.shape[2]
    if used < count:
        dims = stage_ref.shape[:2] + (count - used, SUB, LANE)
        stage_ref[:, :, used:] = jnp.zeros(dims, BF16)
    run_copies(
        [
            pltpu.make_async_copy(stage_ref.at[0], keep_ref, sem.at[0]),
            pltpu.make_async_copy(stage_ref.at[1], send_ref, sem.at[1]),
        ]
    )


def grads_kernel(cols, rows_conv, rows_out, place_ref, taps_ref, d_ref, *refs):
    if rows_out:
        hid_ref, cot_ref, keep_ref, send_ref, stage_ref, gc_ref, sem, go_ref = refs
    else:
        keep_ref, send_ref, stage_ref, gc_ref, sem = refs
    step, steps = pl.program_id(0), pl.num_programs(0)

    @pl.when(step == 0)
    def _():
        gc_ref[...] = jnp.zeros_like(gc_ref)
        if rows_out:
            go_ref[...] = jnp.zeros_like(go_ref)

    gc_ref[...] += lax.dot_general(
        d_ref[:, cols], taps_ref[...], TN, preferred_element_type=F32
    )
    if rows_out:
        go_ref[...] += lax.dot_general(hid_ref[...], cot_ref[...], TN, preferred_element_type=F32)

    @pl.when(step == steps - 1)
    def _():
        core = lax.rem(place_ref[0], 2)
        conv_tiles = rows_conv // SUB * (gc_ref.shape[0] // LANE)
        stage_turned(stage_ref, core, gc_ref, rows_conv, 0)
        if rows_out:
            stage_plain(stage_ref, core, go_ref, rows_out, conv_tiles)
        used = conv_tiles + rows_out // SUB * (D // LANE)
        finish_stage(stage_ref, keep_ref, send_ref, used, sem)


def back_conv_kernel(
    last, rows_in, place_ref, low_ref, d_ref, high_ref, turned_ref, mask_ref, xhat_ref, rstd_ref, slope_ref, hid_ref, np_ref, *refs
):
    if last:
        before_ref, dpre_ref, sums_ref, keep_ref, send_ref, stage_ref = refs[:6]
    else:
        dpre_ref, sums_ref, part_ref = refs[:3]
    ext_ref, wt_ref, taps_ref, dmov_ref, grad_ref, acc_ref, sem = refs[-7:]
    step, steps = pl.program_id(0), pl.num_programs(0)
    tile = taps_ref.shape[0]
    open_sums(acc_ref)

    @pl.when(step == 0)
    def _():
        copies = load_window(low_ref, d_ref, high_ref, ext_ref, sem)
        copies.append(pltpu.make_async_copy(turned_ref, wt_ref, sem.at[3]))
        if last:
            copies.append(pltpu.make_async_copy(before_ref, grad_ref, sem.at[4]))
        for copy in copies:
            copy.start()
        if not last:
            grad_ref[...] = jnp.zeros_like(grad_ref)
        for copy in copies:
            copy.wait()

    fill_taps(taps_ref, ext_ref, mask_ref, (steps * last + step) * tile)
    for half in halves_of(tile):
        dmov_ref[half, :] = lax.dot_general(
            taps_ref[half, :], wt_ref[...], NN, preferred_element_type=F32
        )

    def work(rows, _):
        live = mask_ref[rows, MID : MID + 1]
        sums = [0.0, 0.0]
        for b in lane_blocks(INNER):
            xhat = xhat_ref[rows, b].astype(F32)
            dy = dmov_ref[rows, b] * live * slope_ref[rows, b].astype(F32)
            add_terms(acc_ref, b, dy, xhat)
            dxhat = dy * np_ref[0:1, D + b.start : D + b.stop]
            dmov_ref[rows, b] = dxhat
            sums = [sums[0] + dxhat, sums[1] + dxhat * xhat]
        return row_means(sums, INNER) + [rstd_ref[rows, :]]

    def finish(rows, means):
        def put(b, value):
            dpre_ref[rows, b] = value.astype(BF16)

        norm_back(rows, dmov_ref, xhat_ref, means, put)

    in_stages(tile, [work, finish])
    close_sums(sums_ref, acc_ref)
    grad_ref[...] += lax.dot_general(dpre_ref[...], hid_ref[...], TN, preferred_element_type=F32)

    @pl.when(step == steps - 1)
    def _():
        if last:
            stage_turned(stage_ref, lax.rem(place_ref[0], 2), grad_ref, rows_in, 0)
            used = rows_in // SUB * (INNER // LANE)
            finish_stage(stage_ref, keep_ref, send_ref, used, sem)
        else:
            run_copies([pltpu.make_async_copy(grad_ref, part_ref, sem.at[0])])


def back_a_kernel(pieces, place_ref, dpre_ref, xhat_ref, rstd_ref, slope_ref, cot_ref, np_ref, *refs):
    piece_refs = refs[:pieces]
    grad_ref, sums_ref, w_ref, wt_ref, dh_ref, acc_ref, sem = refs[-7:]
    open_sums(acc_ref)

    @pl.when(pl.program_id(0) == 0)
    def _():
        run_copies(piece_copies(piece_refs, w_ref, place_ref[0], sem))
        for k in range(0, D, 256):
            wt_ref[:, k : k + 256] = jnp.transpose(w_ref[k : k + 256, :])

    dh_ref[...] = lax.dot_general(dpre_ref[...], wt_ref[...], NN, preferred_element_type=F32)

    def work(rows, _):
        sums = [0.0, 0.0]
        for b in lane_blocks(D):
            xhat = xhat_ref[rows, b].astype(F32)
            dy = dh_ref[rows, b] * slope_ref[rows, b].astype(F32)
            add_terms(acc_ref, b, dy, xhat)
            dxhat = dy * np_ref[0:1, b]
            dh_ref[rows, b] = dxhat
            sums = [sums[0] + dxhat, sums[1] + dxhat * xhat]
        return row_means(sums, D) + [rstd_ref[rows, :]]

    def finish(rows, means):
        def put(b, value):
            grad_ref[rows, b] = cot_ref[rows, b].astype(F32) + value

        norm_back(rows, dh_ref, xhat_ref, means, put)

    in_stages(dpre_ref.shape[0], [work, finish])
    close_sums(sums_ref, acc_ref)


def out_kernel(pieces, place_ref, hid_ref, tok_ref, *refs):
    piece_refs = refs[:pieces]
    out_ref, w_ref, sem = refs[pieces:]

    @pl.when(pl.program_id(0) == 0)
    def _():
        run_copies(out_copies(piece_refs, w_ref, place_ref[0], sem))

    branch = lax.dot_general(hid_ref[...], w_ref[...], NN, preferred_element_type=F32)
    out_ref[...] = (tok_ref[...].astype(F32) + branch).astype(BF16)


WIDTHS = (INNER, INNER, D)
LANE0 = (0, INNER, 2 * INNER)
CUT = 2 * LANE
CHUNKS = (((1, 0, CUT), (2, 0, D)), ((1, CUT, INNER - CUT),), ((0, 0, INNER),))


def spans(chunk, rows):
    found, first = [], 0
    for weight, col, cols in chunk:
        tiles = rows[weight] // SUB * (cols // LANE)
        found.append((weight, col // LANE, cols // LANE, first, tiles))
        first += tiles
    return found, first


def norm_tiles_kernel(parts, *refs):
    sums, out_ref, line_ref = refs[:-2], refs[-2], refs[-1]
    line_ref[...] = jnp.zeros_like(line_ref)
    lanes_of = ((0, D), (0, D), (D, D + INNER), (D, D + INNER), (D + INNER, D + 2 * INNER))
    for part, (lane0, lane1) in zip(sums, lanes_of):
        line_ref[0:2, lane0:lane1] += part[...]
    out_ref[...] = jnp.zeros_like(out_ref)
    blocks = (D + 2 * INNER) // LANE
    each = -(-2 * blocks // parts)
    for part in range(-(-2 * blocks // each)):
        rows = []
        for n in range(part * each, min((part + 1) * each, 2 * blocks)):
            row, b = n // blocks, n % blocks
            rows.append(line_ref[row : row + 1, b * LANE : (b + 1) * LANE])
        rows += [jnp.zeros((1, LANE), F32)] * (8 - len(rows))
        value = jnp.concatenate(rows, axis=0)
        high = value.astype(BF16).astype(F32)
        out_ref[part] = jnp.concatenate([high, value - high], axis=0).astype(BF16)


def high_low(total):
    value = total[..., 0:8, :] + total[..., 8:16, :]
    high = value.astype(BF16).astype(F32)
    return jnp.concatenate([high, value - high], axis=-2).astype(BF16)


def column_sums(pack_ref, row, ref, chunk, rows):
    for weight, block0, blocks, first, tiles in spans(chunk, rows)[0]:

        def body(g, carry, first=first, blocks=blocks):
            new = []
            for b in range(blocks):
                value = ref[first + g * blocks + b].astype(F32)
                new.append(carry[b] + fold(value * value + 1e-30))
            return tuple(new)

        zero = tuple(jnp.zeros((8, LANE), F32) for _ in range(blocks))
        cols = lax.fori_loop(0, tiles // blocks, body, zero, unroll=5)
        for b in range(blocks):
            lane = LANE0[weight] + (block0 + b) * LANE
            pack_ref[row : row + 1, lane : lane + LANE] = jnp.sum(cols[b], axis=0, keepdims=True)


def pack_kernel(rows, ref1, ref2, *refs):
    states, pack_ref = refs[0:3], refs[3]
    pack_ref[...] = jnp.zeros_like(pack_ref)
    lanes = lax.broadcasted_iota(jnp.int32, (1, LANE), 1)
    for k in range(3):
        total = jnp.sum(states[k][...].reshape(1, -1), axis=1, keepdims=True)
        pack_ref[1:2, 0:LANE] += jnp.where(lanes == k, total, 0.0)
    column_sums(pack_ref, 0, ref1, CHUNKS[0], rows)
    column_sums(pack_ref, 0, ref2, CHUNKS[1], rows)


def pack_in_kernel(rows, parts, ref, norms_ref, pack_ref):
    pack_ref[...] = jnp.zeros_like(pack_ref)
    blocks = (D + 2 * INNER) // LANE
    each = -(-2 * blocks // parts)
    for n in range(2 * blocks):
        part, at = n // each, n % each
        value = norms_ref[part].astype(F32)
        row, lane = n // blocks, n % blocks * LANE
        pack_ref[row : row + 1, lane : lane + LANE] = value[at : at + 1] + value[8 + at : 9 + at]
    column_sums(pack_ref, 2, ref, CHUNKS[2], rows)


def update_weight(
    k, squares, states_sum, source, weight, state, col_state, grad_ref, new, row_new_ref, col_new_ref, scratch
):
    line_ref, state_ref, new_ref = scratch
    width, fan, rows_here = WIDTHS[k], (D, KERNEL_TAPS * INNER, INNER)[k], weight.shape[0]
    col_new = DECAY * col_state[...].reshape(1, -1) + (1.0 - DECAY) * (squares * (1.0 / fan))
    col_new_ref[...] = col_new.reshape(-1)
    total = DECAY * states_sum
    total = total + (1.0 - DECAY) * (1.0 / width) * jnp.sum(squares, axis=1, keepdims=True)
    scaled = col_new / (total * (1.0 / fan))
    rate = 0.5 / fan**0.5
    line_ref[0:1, 0:rows_here] = state[...].reshape(1, -1)
    whole_rows = rows_here + -rows_here % LANE
    for c in range(0, whole_rows, LANE):
        state_ref[c : c + LANE, :] = column(line_ref[0:1, c : c + LANE])

    def body(g, carry):
        rows = pl.ds(pl.multiple_of(g * SUB, SUB), SUB)
        square = 0.0
        for ref, block0, blocks, first in source:
            for b in range(blocks):
                value = ref[first + g * blocks + b].astype(F32)
                grad_ref[rows, (block0 + b) * LANE : (block0 + b + 1) * LANE] = value
                square = square + (value * value + 1e-30)
        mean = jnp.sum(square, axis=1, keepdims=True) * (1.0 / width)
        row_new = DECAY * state_ref[rows, :] + (1.0 - DECAY) * mean
        new_ref[rows, :] = row_new
        for ref, block0, blocks, first in source:
            for b in range(blocks):
                lanes = slice((block0 + b) * LANE, (block0 + b + 1) * LANE)
                value = ref[first + g * blocks + b].astype(F32)
                step = value * lax.rsqrt(row_new * scaled[:, lanes])
                new[rows, lanes] = weight[rows, lanes] - rate * step
        return carry

    lax.fori_loop(0, rows_here // SUB, body, 0, unroll=5)
    for c in range(0, whole_rows, LANE):
        line_ref[0:1, c : c + LANE] = jnp.transpose(new_ref[c : c + LANE, :])[0:1, :]
    row_new_ref[...] = line_ref[0:1, 0:rows_here].reshape(-1)


def sources_of(chunk, ref, rows):
    return {w: (ref, block0, blocks, first) for w, block0, blocks, first, _ in spans(chunk, rows)[0]}


def update_kernel(rows, full1_ref, full2_ref, pack_ref, *refs):
    weights, states, col_states = refs[0:2], refs[2:4], refs[4:6]
    grads, news, rows_new, cols_new = refs[6:8], refs[8:10], refs[10:12], refs[12:14]
    from1 = sources_of(CHUNKS[0], full1_ref, rows)
    from2 = sources_of(CHUNKS[1], full2_ref, rows)
    for n, (k, source) in enumerate(((1, [from1[1], from2[1]]), (2, [from1[2]]))):
        squares = pack_ref[0:1, LANE0[k] : LANE0[k] + WIDTHS[k]]
        update_weight(
            k, squares, pack_ref[1:2, k : k + 1], source, weights[n], states[n],
            col_states[n], grads[n], news[n], rows_new[n], cols_new[n], refs[14:17],
        )


def update_in_kernel(rows, full_ref, pack_in_ref, pack_ref, np_ref, second_ref, *refs):
    weight, state, col_state, grad_ref, new_ref, row_new_ref, col_new_ref = refs[0:7]
    ngrad_ref, nsecond_ref, nnew_ref = refs[7:10]
    grad = pack_in_ref[0:2, :]
    second = DECAY * second_ref[...] + (1.0 - DECAY) * (grad * grad + 1e-30)
    ngrad_ref[...] = grad
    nsecond_ref[...] = second
    nnew_ref[...] = np_ref[...] - 0.2 * grad * lax.rsqrt(second)
    update_weight(
        0, pack_in_ref[2:3, 0:INNER], pack_ref[1:2, 0:1],
        [sources_of(CHUNKS[2], full_ref, rows)[0]], weight, state, col_state, grad_ref, new_ref,
        row_new_ref, col_new_ref, refs[10:13],
    )


class Places:
    def __init__(self):
        self.seq, self.fsdp = lax.axis_size("seq"), lax.axis_size("fsdp")
        self.q = lax.axis_index("fsdp")
        self.s = lax.axis_index("seq")

    def flip(self, x, axis, bit):
        pairs = []
        for s in range(self.seq):
            for f in range(self.fsdp):
                s2, f2 = (s ^ bit, f) if axis == "seq" else (s, f ^ bit)
                pairs.append((s * self.fsdp + f, s2 * self.fsdp + f2))
        return lax.ppermute(x, AXES, pairs)


def bits_of(count):
    return [1 << k for k in range(count.bit_length() - 1)]


def tie(x, *others):
    return lax.optimization_barrier((x, *others))[0]


def gather_pieces(piece, place, after):
    found = {0: piece}
    for bit in reversed(bits_of(place.fsdp)):
        for k in list(found):
            moving = tie(found[k], after) if bit == 1 else found[k]
            found[k | bit] = place.flip(moving, "fsdp", bit)
    return [found[k] for k in range(place.fsdp)]


def sum_shards(x, place):
    for bit in bits_of(place.fsdp):
        x = x + place.flip(x, "fsdp", bit)
    return x


def pick(x, index):
    return lax.dynamic_index_in_dim(x, index, axis=0, keepdims=False)


class Reduction:
    def __init__(self, place, keep, send):
        self.place, self.near = place, keep
        self.got = place.flip(send, "fsdp", 1)
        self.shards = keep.shape[0]

    def halve(self, axis, bit, side, after):
        parts = (2, -1) + self.near.shape[-3:] if axis == "fsdp" else (2, -1) + self.near.shape[-2:]
        near, got = self.near.reshape(parts), tie(self.got, after).reshape(parts)
        away = (pick(near, 1 - side).astype(F32) + pick(got, 1 - side).astype(F32)).astype(BF16)
        self.near = pick(near, side).astype(F32) + pick(got, side).astype(F32)
        self.got = self.place.flip(away, axis, bit)
        return away

    def x(self, after):
        place = self.place
        bit, away = place.fsdp // 2, None
        while bit > 1:
            away = self.halve("fsdp", bit, (place.q // bit) % 2, after)
            bit //= 2
        self.near, self.got = self.near.reshape(self.near.shape[-3:]), self.got.reshape(self.got.shape[-3:])
        return away

    def seq(self, after, extra=None):
        total = (self.near + tie(self.got, after).astype(F32)).astype(BF16)
        total = total.reshape((self.place.seq, -1) + total.shape[1:])
        if extra is not None:
            total = jnp.concatenate([total, extra[:, None]], axis=1)
        self.got = lax.all_to_all(total, "seq", 0, 0)
        return total

    def back(self, after, extra=False):
        total = jnp.sum(tie(self.got, after).astype(F32), axis=0)
        if extra:
            total = jnp.concatenate([total[:-1].astype(BF16), high_low(total[-1:])], axis=0)
        copies = jnp.broadcast_to(total.astype(BF16)[None], self.got.shape)
        self.got = lax.all_to_all(copies, "seq", 0, 0)
        return copies

    def full(self, extra=False):
        if extra:
            return self.got[:, :-1].reshape((-1,) + self.got.shape[2:]), self.got[:, -1]
        return self.got.reshape((-1,) + self.got.shape[2:])


def on_device(
    tokens, input_mask, doc_lengths, cotangent, w_in, w_conv, w_out, norm_params,
    row_in, col_in, row_conv, col_conv, row_out, col_out, norm_second,
):
    place = Places()
    rows = tokens.shape[0]
    pieces = place.fsdp
    spots = jnp.stack([place.q, (place.s * place.fsdp + place.q) * rows]).astype(jnp.int32)
    docs = doc_lengths.shape[0]
    ends = jnp.pad(
        jnp.cumsum(doc_lengths).astype(F32), (0, -docs % LANE), constant_values=1e9
    ).reshape(1, -1)
    live = input_mask.reshape(-1, LANE)
    weights = (w_in, w_conv, w_out)
    rows_of = [w.shape[0] for w in weights]

    tile_a, tile = 256, 512
    steps = rows // tile
    params_spec = whole(2, D + 2 * INNER)
    dma = pltpu.SemaphoreType.DMA

    hidden_a, slope_a, xhat_a, rstd_a = call(
        norm_a_kernel,
        (rows // tile_a,),
        [rows_spec(tile_a, D), params_spec],
        [rows_spec(tile_a, D)] * 3 + [rows_spec(tile_a, 1)],
        [shape((rows, D), BF16)] * 3 + [shape((rows, 1), F32)],
        us=17,
    )(tokens, norm_params)

    in_pieces = gather_pieces(w_in.astype(BF16), place, hidden_a)
    out_sides = (w_out[:, : D // 2], w_out[:, D // 2 :])
    conv_out = jnp.concatenate([w_conv, *out_sides], axis=0).astype(BF16)

    def in_call(tiles, count, before):
        at, stride = tiles

        def here_spec(width):
            return pl.BlockSpec((tile, width), lambda i: (at + stride * i, 0))

        out_shapes = [shape((rows, INNER), BF16)] * 3 + [shape((rows, 1), F32), shape((rows, 8), F32)]
        out_specs = [here_spec(INNER)] * 3 + [here_spec(1), here_spec(8)]
        if at == 0:
            out_shapes += [shape((REACH, INNER), BF16)] * 2
            out_specs += [whole(REACH, INNER)] * 2
        return call(
            functools.partial(in_kernel, pieces, tiles),
            (count,),
            [SMEM, whole(*ends.shape), here_spec(D), whole(*live.shape), params_spec]
            + [ANY] * (pieces + len(before)),
            out_specs,
            out_shapes,
            [pltpu.VMEM((D, INNER), BF16), pltpu.VMEM((tile, INNER), F32), dma((pieces,))],
            us=8,
            aliases={5 + pieces + k: k for k in range(len(before))},
        )(spots, ends, hidden_a, live, norm_params, *in_pieces, *before)

    *kept, m_first, m_last = in_call((0, steps - 1), 2, ())
    conv_pieces = gather_pieces(conv_out, place, m_first)
    moved, slope_b, xhat_b, rstd_b, masks = in_call((1, 1), steps - 2, kept)

    total = place.seq * place.fsdp
    up = [(i, i + 1) for i in range(total - 1)]
    down = [(i + 1, i) for i in range(total - 1)]
    m_low, m_high = lax.ppermute(m_last, AXES, up), lax.ppermute(m_first, AXES, down)

    ext = pltpu.VMEM((rows + 2 * REACH, INNER), BF16)
    taps_wide = KERNEL_TAPS * INNER
    wide = pltpu.VMEM((taps_wide, INNER), BF16)
    hidden_c, d_conv, taps, d_first, d_last, sums_c, turned = call(
        functools.partial(conv_kernel, pieces),
        (steps,),
        [SMEM, ANY, ANY, ANY, rows_spec(tile, 8), rows_spec(tile, D), params_spec]
        + [ANY] * pieces,
        [rows_spec(tile, INNER)] * 2
        + [rows_spec(tile, taps_wide), whole(REACH, INNER), whole(REACH, INNER), whole(2, INNER), ANY],
        [
            shape((rows, INNER), BF16),
            shape((rows, INNER), BF16),
            shape((rows, taps_wide), BF16),
            shape((REACH, INNER), BF16),
            shape((REACH, INNER), BF16),
            shape((2, INNER), F32),
            shape((taps_wide, INNER), BF16),
        ],
        [
            ext,
            wide,
            wide,
            pltpu.VMEM((INNER, D), BF16),
            pltpu.VMEM((D, INNER), BF16),
            pltpu.VMEM((tile, INNER), F32),
            pltpu.VMEM((tile, INNER), F32),
            pltpu.VMEM((tile, INNER), F32),
            pltpu.VMEM((16, INNER), F32),
            dma((3 + 3 * pieces,)),
        ],
        us=30,
    )(spots, m_low, moved, m_high, masks, cotangent, norm_params, *conv_pieces)
    d_low, d_high = lax.ppermute(d_last, AXES, up), lax.ppermute(d_first, AXES, down)

    shards = place.fsdp // 2

    def half_dims(chunk):
        count = spans(chunk, rows_of)[1]
        return (shards, count + -count % place.seq, SUB, LANE)

    def gradients(chunk, cols, out_too, d_conv):
        dims = half_dims(chunk)
        return call(
            functools.partial(grads_kernel, cols, w_conv.shape[0], w_out.shape[0] if out_too else 0),
            (steps,),
            [SMEM, rows_spec(tile, taps_wide), rows_spec(tile, INNER)]
            + ([rows_spec(tile, INNER), rows_spec(tile, D)] if out_too else []),
            [ANY] * 2,
            [shape(dims, BF16)] * 2,
            [
                pltpu.VMEM((2,) + dims, BF16),
                pltpu.VMEM((cols.stop - cols.start, taps_wide), F32),
                dma((2,)),
            ]
            + ([pltpu.VMEM((INNER, D), F32)] if out_too else []),
            us=13,
        )(spots, taps, d_conv, *((hidden_c, cotangent) if out_too else ()))

    keep, send = gradients(CHUNKS[0], slice(0, CUT), True, d_conv)
    first = Reduction(place, keep, send)
    keep, send = gradients(CHUNKS[1], slice(CUT, INNER), False, tie(d_conv, send, d_low, d_high))
    second = Reduction(place, keep, send)

    def back_conv(last, spots, before):
        here = steps // 2
        at = here * last

        def here_spec(width):
            return pl.BlockSpec((tile, width), lambda i: (i + at, 0))

        dims = half_dims(CHUNKS[2])
        return call(
            functools.partial(back_conv_kernel, last, w_in.shape[0]),
            (here,),
            [SMEM] + [ANY] * 4
            + [here_spec(8), here_spec(INNER), here_spec(1), here_spec(INNER), here_spec(D)]
            + [params_spec]
            + [ANY] * last,
            [rows_spec(tile, INNER), whole(2, INNER)] + [ANY] * (1 + last),
            [shape((rows // 2, INNER), BF16), shape((2, INNER), F32)]
            + ([shape(dims, BF16)] * 2 if last else [shape((INNER, D), F32)]),
            ([pltpu.VMEM((2,) + dims, BF16)] if last else [])
            + [
                ext,
                wide,
                pltpu.VMEM((tile, taps_wide), BF16),
                pltpu.VMEM((tile, INNER), F32),
                pltpu.VMEM((INNER, D), F32),
                pltpu.VMEM((16, INNER), F32),
                dma((5,)),
            ],
            us=16,
        )(
            spots, d_low, d_conv, d_high, turned, masks, xhat_b, rstd_b, slope_b, hidden_a,
            norm_params, *before,
        )

    def back_a(last, spots, d_pre, before):
        here = steps // 2
        at = here * last

        def here_spec(width):
            return pl.BlockSpec((tile, width), lambda i: (i + at, 0))

        return call(
            functools.partial(back_a_kernel, pieces),
            (here,),
            [SMEM, rows_spec(tile, INNER), here_spec(D), here_spec(1), here_spec(D), here_spec(D)]
            + [params_spec]
            + [ANY] * (pieces + last),
            [here_spec(D), whole(2, D)],
            [shape((rows, D), F32), shape((2, D), F32)],
            [
                pltpu.VMEM((D, INNER), BF16),
                pltpu.VMEM((INNER, D), BF16),
                pltpu.VMEM((tile, D), F32),
                pltpu.VMEM((16, D), F32),
                dma((pieces,)),
            ],
            us=9,
            aliases={7 + pieces: 0} if last else None,
        )(spots, d_pre, xhat_a, rstd_a, slope_a, cotangent, norm_params, *in_pieces, *before)

    away = first.x(send)
    d_pre0, sums_b0, grad_part = back_conv(0, tie(spots, away, send), ())
    away = (first.seq(d_pre0), second.x(d_pre0))
    d_pre1, sums_b1, keep, send = back_conv(1, tie(spots, *away), (grad_part,))
    third = Reduction(place, keep, send)
    away = (first.back(d_pre1), second.seq(d_pre1))
    input_grad, sums_a0 = back_a(0, tie(spots, *away, send), d_pre0, ())
    away = (second.back(input_grad), third.x(input_grad))
    input_grad, sums_a1 = back_a(1, tie(spots, *away), d_pre1, (input_grad,))

    sums = (sums_a0, sums_a1, sums_b0, sums_b1, sums_c)
    norm_tiles = call(
        functools.partial(norm_tiles_kernel, place.seq),
        (1,),
        [whole(*x.shape) for x in sums],
        whole(place.seq, SUB, LANE),
        shape((place.seq, SUB, LANE), BF16),
        [pltpu.VMEM((8, D + 2 * INNER), F32)],
        us=1,
    )(*sums)
    away = third.seq(input_grad, norm_tiles)
    (block_out,) = call(
        functools.partial(out_kernel, pieces),
        (steps,),
        [SMEM, rows_spec(tile, INNER), rows_spec(tile, D)] + [ANY] * pieces,
        [rows_spec(tile, D)],
        [shape((rows, D), BF16)],
        [pltpu.VMEM((INNER, D), BF16), dma((2 * pieces,))],
        us=9,
    )(tie(spots, away), hidden_c, tokens, *conv_pieces)
    copies = third.back(block_out, True)

    row_states, col_states = (row_in, row_conv, row_out), (col_in, col_conv, col_out)
    row_specs = [whole(*r.shape) for r in row_states]
    col_specs = [whole(*c.shape) for c in col_states]
    cols_all = D + 2 * INNER
    pack_spec = whole(4, cols_all)
    full1, full2 = first.full(), tie(second.full(), copies)
    fulls = [whole(*full1.shape), whole(*full2.shape)]
    (pack,) = call(
        functools.partial(pack_kernel, rows_of),
        (1,),
        fulls + row_specs,
        [pack_spec],
        [shape((4, cols_all), F32)],
        us=2,
    )(full1, full2, *row_states)
    pack = sum_shards(pack, place)

    def update_scratch(weights):
        lines = max(w.shape[0] + -w.shape[0] % LANE for w in weights)
        return [pltpu.VMEM((8, lines), F32)] + [pltpu.VMEM((lines, LANE), F32)] * 2

    weight_specs = [whole(*w.shape) for w in weights]
    results = call(
        functools.partial(update_kernel, rows_of),
        (1,),
        fulls + [pack_spec] + weight_specs[1:] + row_specs[1:] + col_specs[1:],
        weight_specs[1:] * 2 + row_specs[1:] + col_specs[1:],
        [shape(w.shape, F32) for w in weights[1:]] * 2
        + [shape(r.shape, F32) for r in row_states[1:] + col_states[1:]],
        update_scratch(weights[1:]),
        us=7,
    )(full1, full2, pack, *weights[1:], *row_states[1:], *col_states[1:])
    grad_conv, grad_out, new_conv, new_out, row_conv_new, row_out_new, col_conv_new, col_out_new = (
        results
    )
    full3, norms = third.full(True)
    (pack_in,) = call(
        functools.partial(pack_in_kernel, rows_of, place.seq),
        (1,),
        [whole(*full3.shape), whole(*norms.shape)],
        [pack_spec],
        [shape((4, cols_all), F32)],
        us=2,
    )(full3, norms)
    pack_in = sum_shards(pack_in, place)
    grad_in, new_in, row_in_new, col_in_new, *norm_results = call(
        functools.partial(update_in_kernel, rows_of),
        (1,),
        [whole(*full3.shape), pack_spec, pack_spec, params_spec, params_spec]
        + [weight_specs[0], row_specs[0], col_specs[0]],
        [weight_specs[0]] * 2 + [row_specs[0], col_specs[0]] + [params_spec] * 3,
        [shape(w_in.shape, F32)] * 2
        + [shape(row_in.shape, F32), shape(col_in.shape, F32)]
        + [shape((2, cols_all), F32)] * 3,
        update_scratch(weights[:1]),
        us=3,
    )(full3, pack_in, pack, norm_params, norm_second, w_in, row_in, col_in)
    return (
        block_out,
        input_grad,
        grad_in,
        grad_conv,
        grad_out,
        new_in,
        new_conv,
        new_out,
        row_in_new,
        col_in_new,
        row_conv_new,
        col_conv_new,
        row_out_new,
        col_out_new,
        *norm_results,
    )


def solution(mesh):
    both, rows = P(AXES, None), P("fsdp", None)
    in_specs = (
        both, P(AXES), P(), both, rows, rows, rows, P(),
        P("fsdp"), P(), P("fsdp"), P(), P("fsdp"), P(), P(),
    )
    out_specs = (
        both, both, rows, rows, rows, rows, rows, rows,
        P("fsdp"), P(), P("fsdp"), P(), P("fsdp"), P(), P(), P(), P(),
    )
    return jax.shard_map(
        on_device, mesh=mesh, in_specs=in_specs, out_specs=out_specs, check_vma=False
    )
```

```python
import functools
import math

import jax
import jax.numpy as jnp
from jax import lax
from jax.experimental import pallas as pl
from jax.experimental.pallas import tpu as pltpu
from jax.sharding import PartitionSpec as P

D = 1280
INNER = 640
KERNEL_TAPS = 5
DILATION_STEP = 128
STEP = 10
EPSILON = 1e-05
DECAY = 1.0 - STEP ** (-0.8)

REACH = (KERNEL_TAPS - 1) // 2 * DILATION_STEP
MID = (KERNEL_TAPS - 1) // 2
F32 = jnp.float32
BF16 = jnp.bfloat16
SUB, LANE = 16, 128
AXES = ("seq", "fsdp")
NT = (((1,), (1,)), ((), ()))
TN = (((0,), (0,)), ((), ()))
NN = (((1,), (0,)), ((), ()))
VMEM_LIMIT = 58 * 1024 * 1024


def call(kernel, grid, in_specs, out_specs, out_shape, scratch=(), us=1.0, aliases=None):
    params = pltpu.CompilerParams(
        vmem_limit_bytes=VMEM_LIMIT, dimension_semantics=("arbitrary",) * len(grid)
    )
    return pl.pallas_call(
        kernel,
        grid=grid,
        in_specs=in_specs,
        out_specs=out_specs,
        out_shape=out_shape,
        scratch_shapes=list(scratch),
        compiler_params=params,
        input_output_aliases=aliases or {},
        cost_estimate=pl.CostEstimate(
                flops=int(us * 1.1e9), bytes_accessed=int(us * 3.4e6), transcendentals=0
        ),
    )


def shape(dims, dtype):
    return jax.ShapeDtypeStruct(dims, dtype)


def rows_spec(tile, width):
    return pl.BlockSpec((tile, width), lambda i: (i, 0))


def whole(*dims):
    return pl.BlockSpec(dims, lambda *_: (0,) * len(dims))


ANY = pl.BlockSpec(memory_space=pl.ANY)
SMEM = pl.BlockSpec(memory_space=pltpu.SMEM)


ERFC_P = 0.47 / math.sqrt(2.0)
ERFC_C = (
    0.12357219400743558,
    0.1999878668208835,
    -0.08033356004356296,
    0.3660253986657854,
    -0.1092519747040215,
)
LOG2E = 1.4426950408889634


def gelu_and_slope(y):
    t = pltpu.reciprocal(1.0 + ERFC_P * jnp.abs(y), approx=True)
    bell = jnp.exp2(y * y * (-0.5 * LOG2E))
    poly = ERFC_C[4] * t + ERFC_C[3]
    for c in ERFC_C[2::-1]:
        poly = poly * t + c
    tail = poly * t * bell
    cdf = jnp.where(y > 0.0, 1.0 - tail, tail)
    return y * cdf, cdf + y * (bell * (1.0 / math.sqrt(2.0 * math.pi)))


def lane_blocks(width):
    return [slice(k, k + LANE) for k in range(0, width, LANE)]


def row_stats(ref, rows):
    width = ref.shape[-1]
    blocks = lane_blocks(width)
    total = ref[rows, blocks[0]].astype(F32)
    for b in blocks[1:]:
        total = total + ref[rows, b].astype(F32)
    mean = jnp.sum(total, axis=-1, keepdims=True) * (1.0 / width)
    square = None
    for b in blocks:
        centered = ref[rows, b].astype(F32) - mean
        square = centered * centered if square is None else square + centered * centered
    variance = jnp.sum(square, axis=-1, keepdims=True) * (1.0 / width)
    return mean, lax.rsqrt(variance + EPSILON)


def fold(values):
    total = values[0:8]
    for k in range(8, values.shape[0], 8):
        total = total + values[k : k + 8]
    return total


def in_stages(count, stages, between=()):
    chunks = [slice(k, k + CHUNK) for k in range(0, count, CHUNK)]
    kept, rounds = {}, len(chunks) + len(stages) - 1
    for t in range(rounds):
        for n, stage in enumerate(stages):
            if 0 <= t - n < len(chunks):
                kept[n, t - n] = stage(chunks[t - n], kept.get((n - 1, t - n)))
        for work in between[t * len(between) // rounds : (t + 1) * len(between) // rounds]:
            work()


def halves_of(count):
    return (slice(0, count // 2), slice(count // 2, count))


def row_means(sums, width):
    return [jnp.sum(x, axis=-1, keepdims=True) * (1.0 / width) for x in sums]


def norm_back(rows, dxhat_ref, xhat_ref, means, put):
    mean_d, mean_dx, rstd = means
    for b in lane_blocks(dxhat_ref.shape[-1]):
        xhat = xhat_ref[rows, b].astype(F32)
        put(b, (dxhat_ref[rows, b] - mean_d - xhat * mean_dx) * rstd)


def add_terms(acc_ref, b, dy, xhat):
    acc_ref[0:8, b] += fold(dy * xhat)
    acc_ref[8:16, b] += fold(dy)


def open_sums(acc_ref):
    @pl.when(pl.program_id(0) == 0)
    def _():
        acc_ref[...] = jnp.zeros_like(acc_ref)


def close_sums(out_ref, acc_ref):
    @pl.when(pl.program_id(0) == pl.num_programs(0) - 1)
    def _():
        out_ref[0:1, :] = jnp.sum(acc_ref[0:8, :], axis=0, keepdims=True)
        out_ref[1:2, :] = jnp.sum(acc_ref[8:16, :], axis=0, keepdims=True)


def run_copies(copies):
    for copy in copies:
        copy.start()
    for copy in copies:
        copy.wait()


def piece_copies(pieces, full_ref, me, sem, first=0):
    each = full_ref.shape[0] // len(pieces)
    return [
        pltpu.make_async_copy(
            piece.at[0:each, :],
            full_ref.at[pl.ds(pl.multiple_of((me ^ k) * each, SUB), each), :],
            sem.at[first + k],
        )
        for k, piece in enumerate(pieces)
    ]


def out_copies(pieces, full_ref, me, sem, first=0):
    each, width = full_ref.shape[0] // len(pieces), full_ref.shape[1] // 2
    copies = []
    for k, piece in enumerate(pieces):
        rows = pl.ds(pl.multiple_of((me ^ k) * each, SUB), each)
        for side in range(2):
            at = piece.shape[0] - (2 - side) * each
            copies.append(
                pltpu.make_async_copy(
                    piece.at[at : at + each, :],
                    full_ref.at[rows, side * width : (side + 1) * width],
                    sem.at[first + 2 * k + side],
                )
            )
    return copies


def column(row):
    return jnp.transpose(jnp.broadcast_to(row, (LANE, LANE)))


CHUNK = 64


def norm_a_kernel(tok_ref, np_ref, hid_ref, slope_ref, xhat_ref, rstd_ref):
    def stats(rows, _):
        mean, rstd = row_stats(tok_ref, rows)
        rstd_ref[rows, :] = rstd
        return mean, rstd

    def work(rows, kept):
        mean, rstd = kept
        for b in lane_blocks(D):
            xhat = (tok_ref[rows, b].astype(F32) - mean) * rstd
            hidden, slope = gelu_and_slope(xhat * np_ref[0:1, b] + np_ref[1:2, b])
            hid_ref[rows, b] = hidden.astype(BF16)
            slope_ref[rows, b] = slope.astype(BF16)
            xhat_ref[rows, b] = xhat.astype(BF16)

    in_stages(tok_ref.shape[0], [stats, work])


def in_kernel(pieces, tiles, place_ref, ends_ref, hid_ref, live_ref, np_ref, *refs):
    piece_refs = refs[:pieces]
    edges = tiles[0] == 0
    outs = refs[-(10 if edges else 8) :]
    mov_ref, slope_ref, xhat_ref, rstd_ref, mask_ref = outs[:5]
    w_ref, pre_ref, sem = outs[-3:]
    step = pl.program_id(0)
    tile = hid_ref.shape[0]

    @pl.when(step == 0)
    def _():
        run_copies(piece_copies(piece_refs, w_ref, place_ref[0], sem))

    for half in halves_of(tile):
        pre_ref[half, :] = lax.dot_general(
            hid_ref[half, :], w_ref[...], NN, preferred_element_type=F32
        )

    at_tile = tiles[0] + step * tiles[1]
    first = place_ref[1] + at_tile * tile
    ends = ends_ref[...]
    lanes = lax.broadcasted_iota(jnp.int32, (LANE, 8), 1)
    offsets = ((lanes - MID) * DILATION_STEP).astype(F32)
    for k in range(tile // LANE):
        at = (first + k * LANE + lax.broadcasted_iota(jnp.int32, (LANE, 1), 0)).astype(F32)
        begin = jnp.max(jnp.where(ends <= at, ends, 0.0), axis=1, keepdims=True)
        end = jnp.min(jnp.where(ends > at, ends, 1e9), axis=1, keepdims=True)
        there = at + offsets
        same = jnp.where((there >= begin) & (there < end), 1.0, 0.0)
        live = column(live_ref[pl.ds(at_tile * (tile // LANE) + k, 1), :].astype(F32))
        mask_ref[k * LANE : (k + 1) * LANE, :] = jnp.where(lanes == MID, live[:, 0:8], same)

    def stats(rows, _):
        mean, rstd = row_stats(pre_ref, rows)
        rstd_ref[rows, :] = rstd
        return mean, rstd

    def work(rows, kept):
        mean, rstd = kept
        live = mask_ref[rows, MID : MID + 1]
        for b in lane_blocks(INNER):
            gains = slice(D + b.start, D + b.stop)
            xhat = (pre_ref[rows, b] - mean) * rstd
            hidden, slope = gelu_and_slope(xhat * np_ref[0:1, gains] + np_ref[1:2, gains])
            mov_ref[rows, b] = (hidden * live).astype(BF16)
            slope_ref[rows, b] = slope.astype(BF16)
            xhat_ref[rows, b] = xhat.astype(BF16)

    in_stages(tile, [stats, work])
    if edges:
        first_ref, last_ref = outs[5:7]

        @pl.when(step == 0)
        def _():
            first_ref[...] = mov_ref[0:REACH, :]

        @pl.when(step == 1)
        def _():
            last_ref[...] = mov_ref[tile - REACH :, :]


def load_window(low, mid, high, ext_ref, sem):
    rows = mid.shape[0]
    return [
        pltpu.make_async_copy(low, ext_ref.at[0:REACH, :], sem.at[0]),
        pltpu.make_async_copy(mid, ext_ref.at[REACH : REACH + rows, :], sem.at[1]),
        pltpu.make_async_copy(high, ext_ref.at[REACH + rows : 2 * REACH + rows, :], sem.at[2]),
    ]


def fill_taps(taps_ref, ext_ref, mask_ref, start):
    tile = taps_ref.shape[0]
    for j in range(KERNEL_TAPS):
        rows = pl.ds(pl.multiple_of(start + j * DILATION_STEP, DILATION_STEP), tile)
        picked = ext_ref[rows, :]
        if j != MID:
            picked = picked * mask_ref[:, j : j + 1].astype(BF16)
        taps_ref[:, j * INNER : (j + 1) * INNER] = picked


def conv_kernel(
    pieces, rows_of, place_ref, low_ref, mov_ref, high_ref, mask_ref, cot_ref, before_ref, np_ref, *refs
):
    piece_refs = refs[:pieces]
    hid_ref, dconv_ref, first_ref, last_ref, sums_ref, turned_ref = refs[pieces : pieces + 6]
    outs = refs[pieces + 6 : pieces + 10]
    ext_ref, wc_ref, wct_ref, wo_ref, wt_ref, taps_ref, pre_ref, dh_ref, xhat_ref = refs[
        pieces + 10 : pieces + 19
    ]
    dt_ref, ht_ref, gc_ref, go_ref, acc_ref, stage1_ref, stage2_ref, sem = refs[pieces + 19 :]
    step, steps = pl.program_id(0), pl.num_programs(0) - 1
    tile = taps_ref.shape[1]
    slot = lax.rem(step, 2)

    @pl.when(step == 0)
    def _():
        me = place_ref[0]
        outs = out_copies(piece_refs, wo_ref, me, sem, 3)
        rest = load_window(low_ref, mov_ref, high_ref, ext_ref, sem)
        rest += piece_copies(piece_refs, wc_ref, me, sem, 3 + 2 * pieces)
        for copy in outs + rest:
            copy.start()
        for ref in (acc_ref, gc_ref, go_ref, dt_ref, ht_ref):
            ref[...] = jnp.zeros_like(ref)
        taps_ref[1] = jnp.zeros_like(taps_ref[1])
        for copy in outs:
            copy.wait()
        for k in range(0, D, 256):
            wt_ref[k : k + 256, :] = jnp.transpose(wo_ref[:, k : k + 256])
        for copy in rest:
            copy.wait()

    def grad_conv(cols):
        def work():
            gc_ref[:, cols] += lax.dot_general(
                dt_ref[...], taps_ref[1 - slot, :, cols], NN, preferred_element_type=F32
            )

        return work

    def grad_out(cols):
        def work():
            go_ref[:, cols] += lax.dot_general(
                ht_ref[...], before_ref[:, cols], NN, preferred_element_type=F32
            )

        return work

    taps_wide = KERNEL_TAPS * INNER
    products = [grad_conv(slice(k, min(k + 768, taps_wide))) for k in range(0, taps_wide, 768)]
    products += [grad_out(slice(k, min(k + 768, D))) for k in range(0, D, 768)]

    @pl.when(step < steps)
    def _():
        fill_taps(taps_ref.at[slot], ext_ref, mask_ref, step * tile)
        for half in halves_of(tile):
            pre_ref[half, :] = lax.dot_general(
                taps_ref[slot, half, :], wc_ref[...], NN, preferred_element_type=F32
            )
            dh_ref[half, :] = lax.dot_general(
                cot_ref[half, :], wt_ref[...], NN, preferred_element_type=F32
            )
        for n in range(2):
            tap = jnp.minimum(2 * step + n, KERNEL_TAPS - 1)
            source = wc_ref[pl.ds(pl.multiple_of(tap * INNER, SUB), INNER), :]
            target = pl.multiple_of((KERNEL_TAPS - 1 - tap) * INNER, SUB)
            wct_ref[pl.ds(target, INNER), :] = jnp.transpose(source)

        def stats(rows, _):
            return row_stats(pre_ref, rows)

        def work(rows, kept):
            mean, rstd = kept
            sums = [0.0, 0.0]
            for b in lane_blocks(INNER):
                gains = slice(D + INNER + b.start, D + INNER + b.stop)
                gain = np_ref[0:1, gains]
                xhat = (pre_ref[rows, b] - mean) * rstd
                hidden, slope = gelu_and_slope(xhat * gain + np_ref[1:2, gains])
                hid_ref[rows, b] = hidden.astype(BF16)
                dy = dh_ref[rows, b] * slope
                add_terms(acc_ref, b, dy, xhat)
                dxhat = dy * gain
                xhat_ref[rows, b] = xhat
                dh_ref[rows, b] = dxhat
                sums = [sums[0] + dxhat, sums[1] + dxhat * xhat]
            return row_means(sums, INNER) + [rstd]

        def finish(rows, means):
            def put(b, value):
                dconv_ref[rows, b] = value.astype(BF16)

            norm_back(rows, dh_ref, xhat_ref, means, put)

        in_stages(tile, [stats, work, finish], products)
        dt_ref[...] = jnp.transpose(dconv_ref[...])
        ht_ref[...] = jnp.transpose(hid_ref[...])

    @pl.when(step == 0)
    def _():
        first_ref[...] = dconv_ref[0:REACH, :]

    @pl.when(step == steps - 1)
    def _():
        last_ref[...] = dconv_ref[tile - REACH :, :]

    @pl.when(step == steps)
    def _():
        copy = pltpu.make_async_copy(wct_ref, turned_ref, sem.at[4])
        copy.start()
        for work in products:
            work()
        core = lax.rem(place_ref[0], 2)
        _, rows_conv, rows_out = rows_of
        stage_turned(stage1_ref, core, gc_ref, rows_conv, 0, slice(0, CUT // LANE))
        first_tiles = rows_conv // SUB * (CUT // LANE)
        stage_plain(stage1_ref, core, go_ref, rows_out, first_tiles)
        copies = stage_copies(stage1_ref, outs[0], outs[1], spans(CHUNKS[0], rows_of)[1], sem, 0)
        for each in copies:
            each.start()
        stage_turned(stage2_ref, core, gc_ref, rows_conv, 0, slice(CUT // LANE, INNER // LANE))
        more = stage_copies(stage2_ref, outs[2], outs[3], spans(CHUNKS[1], rows_of)[1], sem, 2)
        for each in more:
            each.start()
        for each in copies + more + [copy]:
            each.wait()
        sums_ref[0:1, :] = jnp.sum(acc_ref[0:8, :], axis=0, keepdims=True)
        sums_ref[1:2, :] = jnp.sum(acc_ref[8:16, :], axis=0, keepdims=True)


def stage_tiles(stage_ref, core, first_row, rows_each, base, block0, blocks, value):
    for g in range(value.shape[0] // SUB):
        row = first_row + g * SUB
        owner, inside = row // rows_each, row % rows_each // SUB
        side = core ^ (owner % 2)
        for b in range(value.shape[1] // LANE):
            tile = value[g * SUB : (g + 1) * SUB, b * LANE : (b + 1) * LANE]
            at = base + inside * blocks + block0 + b
            stage_ref[side, owner // 2, at] = tile.astype(BF16)


def stage_plain(stage_ref, core, grad_ref, rows_each, base):
    blocks = grad_ref.shape[1] // LANE
    for row in range(0, grad_ref.shape[0], SUB):
        part = grad_ref[row : row + SUB, :]
        stage_tiles(stage_ref, core, row, rows_each, base, 0, blocks, part)


def stage_turned(stage_ref, core, turned_ref, rows_each, base, blocks):
    count = blocks.stop - blocks.start
    for row in range(0, turned_ref.shape[1], LANE):
        for b in range(count):
            at = (blocks.start + b) * LANE
            part = jnp.transpose(turned_ref[at : at + LANE, row : row + LANE])
            stage_tiles(stage_ref, core, row, rows_each, base, b, count, part)


def stage_copies(stage_ref, keep_ref, send_ref, used, sem, first):
    count = stage_ref.shape[2]
    if used < count:
        dims = stage_ref.shape[:2] + (count - used, SUB, LANE)
        stage_ref[:, :, used:] = jnp.zeros(dims, BF16)
    return [
        pltpu.make_async_copy(stage_ref.at[n], ref, sem.at[first + n])
        for n, ref in enumerate((keep_ref, send_ref))
    ]


def back_conv_kernel(
    last, rows_in, place_ref, low_ref, d_ref, high_ref, turned_ref, mask_ref, xhat_ref, rstd_ref, slope_ref, hid_ref, np_ref, *refs
):
    if last:
        before_ref, dpre_ref, sums_ref, keep_ref, send_ref, stage_ref = refs[:6]
    else:
        dpre_ref, sums_ref, part_ref = refs[:3]
    ext_ref, wt_ref, taps_ref, dmov_ref, grad_ref, acc_ref, sem = refs[-7:]
    step, steps = pl.program_id(0), pl.num_programs(0)
    tile = taps_ref.shape[0]
    open_sums(acc_ref)

    @pl.when(step == 0)
    def _():
        copies = load_window(low_ref, d_ref, high_ref, ext_ref, sem)
        copies.append(pltpu.make_async_copy(turned_ref, wt_ref, sem.at[3]))
        if last:
            copies.append(pltpu.make_async_copy(before_ref, grad_ref, sem.at[4]))
        for copy in copies:
            copy.start()
        if not last:
            grad_ref[...] = jnp.zeros_like(grad_ref)
        for copy in copies:
            copy.wait()

    fill_taps(taps_ref, ext_ref, mask_ref, (steps * last + step) * tile)
    for half in halves_of(tile):
        dmov_ref[half, :] = lax.dot_general(
            taps_ref[half, :], wt_ref[...], NN, preferred_element_type=F32
        )

    def work(rows, _):
        live = mask_ref[rows, MID : MID + 1]
        sums = [0.0, 0.0]
        for b in lane_blocks(INNER):
            xhat = xhat_ref[rows, b].astype(F32)
            dy = dmov_ref[rows, b] * live * slope_ref[rows, b].astype(F32)
            add_terms(acc_ref, b, dy, xhat)
            dxhat = dy * np_ref[0:1, D + b.start : D + b.stop]
            dmov_ref[rows, b] = dxhat
            sums = [sums[0] + dxhat, sums[1] + dxhat * xhat]
        return row_means(sums, INNER) + [rstd_ref[rows, :]]

    def finish(rows, means):
        def put(b, value):
            dpre_ref[rows, b] = value.astype(BF16)

        norm_back(rows, dmov_ref, xhat_ref, means, put)

    in_stages(tile, [work, finish])
    close_sums(sums_ref, acc_ref)
    grad_ref[...] += lax.dot_general(dpre_ref[...], hid_ref[...], TN, preferred_element_type=F32)

    @pl.when(step == steps - 1)
    def _():
        if last:
            all_blocks = slice(0, INNER // LANE)
            stage_turned(stage_ref, lax.rem(place_ref[0], 2), grad_ref, rows_in, 0, all_blocks)
            used = rows_in // SUB * (INNER // LANE)
            run_copies(stage_copies(stage_ref, keep_ref, send_ref, used, sem, 0))
        else:
            run_copies([pltpu.make_async_copy(grad_ref, part_ref, sem.at[0])])


def back_a_kernel(pieces, half, place_ref, dpre0_ref, dpre1_ref, xhat_ref, rstd_ref, slope_ref, cot_ref, np_ref, *refs):
    piece_refs = refs[:pieces]
    grad_ref, sums_ref, w_ref, wt_ref, dh_ref, acc_ref, sem = refs[-7:]
    open_sums(acc_ref)

    @pl.when(pl.program_id(0) == 0)
    def _():
        run_copies(piece_copies(piece_refs, w_ref, place_ref[0], sem))
        for k in range(0, D, 256):
            wt_ref[:, k : k + 256] = jnp.transpose(w_ref[k : k + 256, :])

    second = (jnp.zeros((1, 1), jnp.int32) + pl.program_id(0)) >= half
    d_pre = jnp.where(second, dpre1_ref[...], dpre0_ref[...])
    dh_ref[...] = lax.dot_general(d_pre, wt_ref[...], NN, preferred_element_type=F32)

    def work(rows, _):
        sums = [0.0, 0.0]
        for b in lane_blocks(D):
            xhat = xhat_ref[rows, b].astype(F32)
            dy = dh_ref[rows, b] * slope_ref[rows, b].astype(F32)
            add_terms(acc_ref, b, dy, xhat)
            dxhat = dy * np_ref[0:1, b]
            dh_ref[rows, b] = dxhat
            sums = [sums[0] + dxhat, sums[1] + dxhat * xhat]
        return row_means(sums, D) + [rstd_ref[rows, :]]

    def finish(rows, means):
        def put(b, value):
            grad_ref[rows, b] = cot_ref[rows, b].astype(F32) + value

        norm_back(rows, dh_ref, xhat_ref, means, put)

    in_stages(dpre0_ref.shape[0], [work, finish])
    close_sums(sums_ref, acc_ref)


def out_kernel(pieces, place_ref, hid_ref, tok_ref, *refs):
    piece_refs = refs[:pieces]
    out_ref, w_ref, sem = refs[pieces:]

    @pl.when(pl.program_id(0) == 0)
    def _():
        run_copies(out_copies(piece_refs, w_ref, place_ref[0], sem))

    branch = lax.dot_general(hid_ref[...], w_ref[...], NN, preferred_element_type=F32)
    out_ref[...] = (tok_ref[...].astype(F32) + branch).astype(BF16)


WIDTHS = (INNER, INNER, D)
LANE0 = (0, INNER, 2 * INNER)
CUT = 2 * LANE
CHUNKS = (((1, 0, CUT), (2, 0, D)), ((1, CUT, INNER - CUT),), ((0, 0, INNER),))


def spans(chunk, rows):
    found, first = [], 0
    for weight, col, cols in chunk:
        tiles = rows[weight] // SUB * (cols // LANE)
        found.append((weight, col // LANE, cols // LANE, first, tiles))
        first += tiles
    return found, first


def norm_tiles_kernel(parts, *refs):
    sums, out_ref, line_ref = refs[:-2], refs[-2], refs[-1]
    line_ref[...] = jnp.zeros_like(line_ref)
    lanes_of = ((0, D), (D, D + INNER), (D, D + INNER), (D + INNER, D + 2 * INNER))
    for part, (lane0, lane1) in zip(sums, lanes_of):
        line_ref[0:2, lane0:lane1] += part[...]
    out_ref[...] = jnp.zeros_like(out_ref)
    blocks = (D + 2 * INNER) // LANE
    each = -(-2 * blocks // parts)
    for part in range(-(-2 * blocks // each)):
        rows = []
        for n in range(part * each, min((part + 1) * each, 2 * blocks)):
            row, b = n // blocks, n % blocks
            rows.append(line_ref[row : row + 1, b * LANE : (b + 1) * LANE])
        rows += [jnp.zeros((1, LANE), F32)] * (8 - len(rows))
        value = jnp.concatenate(rows, axis=0)
        high = value.astype(BF16).astype(F32)
        out_ref[part] = jnp.concatenate([high, value - high], axis=0).astype(BF16)


def high_low(total):
    value = total[..., 0:8, :] + total[..., 8:16, :]
    high = value.astype(BF16).astype(F32)
    return jnp.concatenate([high, value - high], axis=-2).astype(BF16)


def column_sums(pack_ref, row, ref, chunk, rows):
    for weight, block0, blocks, first, tiles in spans(chunk, rows)[0]:

        def body(g, carry, first=first, blocks=blocks):
            new = []
            for b in range(blocks):
                value = ref[first + g * blocks + b].astype(F32)
                new.append(carry[b] + fold(value * value + 1e-30))
            return tuple(new)

        zero = tuple(jnp.zeros((8, LANE), F32) for _ in range(blocks))
        cols = lax.fori_loop(0, tiles // blocks, body, zero, unroll=5)
        for b in range(blocks):
            lane = LANE0[weight] + (block0 + b) * LANE
            pack_ref[row : row + 1, lane : lane + LANE] = jnp.sum(cols[b], axis=0, keepdims=True)


def load_full(got_ref, first, full_ref, sem):
    each = full_ref.shape[0] // got_ref.shape[0]
    return [
        pltpu.make_async_copy(
            got_ref.at[p, first : first + each], full_ref.at[p * each : (p + 1) * each], sem.at[p]
        )
        for p in range(got_ref.shape[0])
    ]


def pack_kernel(rows, got1_ref, got2_ref, *refs):
    states, pack_ref, full1_ref, full2_ref, sem1, sem2 = refs[0:3], *refs[3:8]
    copies = load_full(got1_ref, 0, full1_ref, sem1) + load_full(got2_ref, 0, full2_ref, sem2)
    for copy in copies:
        copy.start()
    pack_ref[...] = jnp.zeros_like(pack_ref)
    lanes = lax.broadcasted_iota(jnp.int32, (1, LANE), 1)
    for k in range(3):
        total = jnp.sum(states[k][...].reshape(1, -1), axis=1, keepdims=True)
        pack_ref[1:2, 0:LANE] += jnp.where(lanes == k, total, 0.0)
    for copy in copies:
        copy.wait()
    column_sums(pack_ref, 0, full1_ref, CHUNKS[0], rows)
    column_sums(pack_ref, 0, full2_ref, CHUNKS[1], rows)


def pack_in_kernel(rows, got_ref, pack_ref, full_ref, norms_ref, sem, norms_sem):
    parts = got_ref.shape[0]
    count = full_ref.shape[0] // parts
    run_copies(
        load_full(got_ref, 0, full_ref, sem) + load_full(got_ref, count, norms_ref, norms_sem)
    )
    pack_ref[...] = jnp.zeros_like(pack_ref)
    blocks = (D + 2 * INNER) // LANE
    each = -(-2 * blocks // parts)
    for n in range(2 * blocks):
        part, at = n // each, n % each
        value = norms_ref[part].astype(F32)
        row, lane = n // blocks, n % blocks * LANE
        pack_ref[row : row + 1, lane : lane + LANE] = value[at : at + 1] + value[8 + at : 9 + at]
    column_sums(pack_ref, 2, full_ref, CHUNKS[2], rows)


def update_weight(
    k, squares, states_sum, source, weight, state, col_state, grad_ref, new, row_new_ref, col_new_ref, scratch
):
    line_ref, state_ref, new_ref = scratch
    width, fan, rows_here = WIDTHS[k], (D, KERNEL_TAPS * INNER, INNER)[k], weight.shape[0]
    col_new = DECAY * col_state[...].reshape(1, -1) + (1.0 - DECAY) * (squares * (1.0 / fan))
    col_new_ref[...] = col_new.reshape(-1)
    total = DECAY * states_sum
    total = total + (1.0 - DECAY) * (1.0 / width) * jnp.sum(squares, axis=1, keepdims=True)
    scaled = col_new / (total * (1.0 / fan))
    rate = 0.5 / fan**0.5
    line_ref[0:1, 0:rows_here] = state[...].reshape(1, -1)
    whole_rows = rows_here + -rows_here % LANE
    for c in range(0, whole_rows, LANE):
        state_ref[c : c + LANE, :] = column(line_ref[0:1, c : c + LANE])

    def body(g, carry):
        rows = pl.ds(pl.multiple_of(g * SUB, SUB), SUB)
        square = 0.0
        for ref, block0, blocks, first in source:
            for b in range(blocks):
                value = ref[first + g * blocks + b].astype(F32)
                grad_ref[rows, (block0 + b) * LANE : (block0 + b + 1) * LANE] = value
                square = square + (value * value + 1e-30)
        mean = jnp.sum(square, axis=1, keepdims=True) * (1.0 / width)
        row_new = DECAY * state_ref[rows, :] + (1.0 - DECAY) * mean
        new_ref[rows, :] = row_new
        for ref, block0, blocks, first in source:
            for b in range(blocks):
                lanes = slice((block0 + b) * LANE, (block0 + b + 1) * LANE)
                value = ref[first + g * blocks + b].astype(F32)
                step = value * lax.rsqrt(row_new * scaled[:, lanes])
                new[rows, lanes] = weight[rows, lanes] - rate * step
        return carry

    lax.fori_loop(0, rows_here // SUB, body, 0, unroll=5)
    for c in range(0, whole_rows, LANE):
        line_ref[0:1, c : c + LANE] = jnp.transpose(new_ref[c : c + LANE, :])[0:1, :]
    row_new_ref[...] = line_ref[0:1, 0:rows_here].reshape(-1)


def sources_of(chunk, ref, rows):
    return {w: (ref, block0, blocks, first) for w, block0, blocks, first, _ in spans(chunk, rows)[0]}


def update_kernel(rows, got1_ref, got2_ref, pack_ref, *refs):
    weights, states, col_states = refs[0:2], refs[2:4], refs[4:6]
    grads, news, rows_new, cols_new = refs[6:8], refs[8:10], refs[10:12], refs[12:14]
    full1_ref, full2_ref, sem1, sem2 = refs[17:21]
    run_copies(load_full(got1_ref, 0, full1_ref, sem1) + load_full(got2_ref, 0, full2_ref, sem2))
    from1 = sources_of(CHUNKS[0], full1_ref, rows)
    from2 = sources_of(CHUNKS[1], full2_ref, rows)
    for n, (k, source) in enumerate(((1, [from1[1], from2[1]]), (2, [from1[2]]))):
        squares = pack_ref[0:1, LANE0[k] : LANE0[k] + WIDTHS[k]]
        update_weight(
            k, squares, pack_ref[1:2, k : k + 1], source, weights[n], states[n],
            col_states[n], grads[n], news[n], rows_new[n], cols_new[n], refs[14:17],
        )


def update_in_kernel(rows, got_ref, pack_in_ref, pack_ref, np_ref, second_ref, *refs):
    weight, state, col_state, grad_ref, new_ref, row_new_ref, col_new_ref = refs[0:7]
    ngrad_ref, nsecond_ref, nnew_ref = refs[7:10]
    full_ref, sem = refs[13:15]
    copies = load_full(got_ref, 0, full_ref, sem)
    for copy in copies:
        copy.start()
    grad = pack_in_ref[0:2, :]
    second = DECAY * second_ref[...] + (1.0 - DECAY) * (grad * grad + 1e-30)
    ngrad_ref[...] = grad
    nsecond_ref[...] = second
    nnew_ref[...] = np_ref[...] - 0.2 * grad * lax.rsqrt(second)
    for copy in copies:
        copy.wait()
    update_weight(
        0, pack_in_ref[2:3, 0:INNER], pack_ref[1:2, 0:1],
        [sources_of(CHUNKS[2], full_ref, rows)[0]], weight, state, col_state, grad_ref, new_ref,
        row_new_ref, col_new_ref, refs[10:13],
    )


def sources_of(chunk, ref, rows):
    return {w: (ref, block0, blocks, first) for w, block0, blocks, first, _ in spans(chunk, rows)[0]}


class Places:
    def __init__(self):
        self.seq, self.fsdp = lax.axis_size("seq"), lax.axis_size("fsdp")
        self.q = lax.axis_index("fsdp")
        self.s = lax.axis_index("seq")

    def flip(self, x, axis, bit):
        pairs = []
        for s in range(self.seq):
            for f in range(self.fsdp):
                s2, f2 = (s ^ bit, f) if axis == "seq" else (s, f ^ bit)
                pairs.append((s * self.fsdp + f, s2 * self.fsdp + f2))
        return lax.ppermute(x, AXES, pairs)


def bits_of(count):
    return [1 << k for k in range(count.bit_length() - 1)]


def tie(x, *others):
    return lax.optimization_barrier((x, *others))[0]


def gather_pieces(piece, place, after):
    found = {0: piece}
    for bit in reversed(bits_of(place.fsdp)):
        for k in list(found):
            moving = tie(found[k], after) if bit == 1 else found[k]
            found[k | bit] = place.flip(moving, "fsdp", bit)
    return [found[k] for k in range(place.fsdp)]


def sum_shards(x, place):
    for bit in bits_of(place.fsdp):
        x = x + place.flip(x, "fsdp", bit)
    return x


def pick(x, index):
    return lax.dynamic_index_in_dim(x, index, axis=0, keepdims=False)


class Reduction:
    def __init__(self, place, keep, send):
        self.place, self.near = place, keep
        self.got = place.flip(send, "fsdp", 1)
        self.shards = keep.shape[0]

    def halve(self, axis, bit, side, after):
        parts = (2, -1) + self.near.shape[-3:] if axis == "fsdp" else (2, -1) + self.near.shape[-2:]
        near, got = self.near.reshape(parts), tie(self.got, after).reshape(parts)
        away = (pick(near, 1 - side).astype(F32) + pick(got, 1 - side).astype(F32)).astype(BF16)
        self.near = pick(near, side).astype(F32) + pick(got, side).astype(F32)
        self.got = self.place.flip(away, axis, bit)
        return away

    def x(self, after):
        place = self.place
        bit, away = place.fsdp // 2, None
        while bit > 1:
            away = self.halve("fsdp", bit, (place.q // bit) % 2, after)
            bit //= 2
        self.near, self.got = self.near.reshape(self.near.shape[-3:]), self.got.reshape(self.got.shape[-3:])
        return away

    def scatter(self, after):
        total = (self.near + tie(self.got, after).astype(F32)).astype(BF16)
        return total.reshape((self.place.seq, -1) + total.shape[1:])


def summed(got):
    return jnp.sum(got.astype(F32), axis=0)


def exchange(place, *arrays):
    sent = jnp.concatenate(arrays, axis=1) if len(arrays) > 1 else arrays[0]
    return sent, lax.all_to_all(sent, "seq", 0, 0)


def copies_for(place, part):
    return jnp.broadcast_to(part[None], (place.seq,) + part.shape)


def on_device(
    tokens, input_mask, doc_lengths, cotangent, w_in, w_conv, w_out, norm_params,
    row_in, col_in, row_conv, col_conv, row_out, col_out, norm_second,
):
    place = Places()
    rows = tokens.shape[0]
    pieces = place.fsdp
    spots = jnp.stack([place.q, (place.s * place.fsdp + place.q) * rows]).astype(jnp.int32)
    docs = doc_lengths.shape[0]
    ends = jnp.pad(
        jnp.cumsum(doc_lengths).astype(F32), (0, -docs % LANE), constant_values=1e9
    ).reshape(1, -1)
    live = input_mask.reshape(-1, LANE)
    weights = (w_in, w_conv, w_out)
    rows_of = [w.shape[0] for w in weights]

    tile_a, tile = 256, 512
    steps = rows // tile
    params_spec = whole(2, D + 2 * INNER)
    dma = pltpu.SemaphoreType.DMA

    out_sides = (w_out[:, : D // 2], w_out[:, D // 2 :])
    conv_out = jnp.concatenate([w_conv, *out_sides], axis=0).astype(BF16)
    hidden_a, slope_a, xhat_a, rstd_a = call(
        norm_a_kernel,
        (rows // tile_a,),
        [rows_spec(tile_a, D), params_spec],
        [rows_spec(tile_a, D)] * 3 + [rows_spec(tile_a, 1)],
        [shape((rows, D), BF16)] * 3 + [shape((rows, 1), F32)],
        us=17,
    )(tokens, tie(norm_params, conv_out))

    in_pieces = gather_pieces(w_in.astype(BF16), place, hidden_a)

    def in_call(tiles, count, before):
        at, stride = tiles

        def here_spec(width):
            return pl.BlockSpec((tile, width), lambda i: (at + stride * i, 0))

        out_shapes = [shape((rows, INNER), BF16)] * 3 + [shape((rows, 1), F32), shape((rows, 8), F32)]
        out_specs = [here_spec(INNER)] * 3 + [here_spec(1), here_spec(8)]
        if at == 0:
            out_shapes += [shape((REACH, INNER), BF16)] * 2
            out_specs += [whole(REACH, INNER)] * 2
        return call(
            functools.partial(in_kernel, pieces, tiles),
            (count,),
            [SMEM, whole(*ends.shape), here_spec(D), whole(*live.shape), params_spec]
            + [ANY] * (pieces + len(before)),
            out_specs,
            out_shapes,
            [pltpu.VMEM((D, INNER), BF16), pltpu.VMEM((tile, INNER), F32), dma((pieces,))],
            us=8,
            aliases={5 + pieces + k: k for k in range(len(before))},
        )(spots, ends, hidden_a, live, norm_params, *in_pieces, *before)

    *kept, m_first, m_last = in_call((0, steps - 1), 2, ())
    conv_pieces = gather_pieces(conv_out, place, m_first)
    moved, slope_b, xhat_b, rstd_b, masks = in_call((1, 1), steps - 2, kept)

    total = place.seq * place.fsdp
    up = [(i, i + 1) for i in range(total - 1)]
    down = [(i + 1, i) for i in range(total - 1)]
    m_low, m_high = lax.ppermute(m_last, AXES, up), lax.ppermute(m_first, AXES, down)

    ext = pltpu.VMEM((rows + 2 * REACH, INNER), BF16)
    taps_wide = KERNEL_TAPS * INNER
    wide = pltpu.VMEM((taps_wide, INNER), BF16)
    shards = place.fsdp // 2

    def half_dims(chunk):
        count = spans(chunk, rows_of)[1]
        return (shards, count + -count % place.seq, SUB, LANE)

    def tile_spec(width, ahead):
        return pl.BlockSpec((tile, width), lambda i: (jnp.clip(i + ahead, 0, steps - 1), 0))

    halves = [half_dims(CHUNKS[0])] * 2 + [half_dims(CHUNKS[1])] * 2
    work = pltpu.VMEM((tile, INNER), F32)
    turned_tile = pltpu.VMEM((INNER, tile), BF16)
    hidden_c, d_conv, d_first, d_last, sums_c, turned, keep1, send1, keep2, send2 = call(
        functools.partial(conv_kernel, pieces, rows_of),
        (steps + 1,),
        [SMEM, ANY, ANY, ANY, tile_spec(8, 0), tile_spec(D, 0), tile_spec(D, -1), params_spec]
        + [ANY] * pieces,
        [tile_spec(INNER, 0)] * 2
        + [whole(REACH, INNER), whole(REACH, INNER), whole(2, INNER)]
        + [ANY] * 5,
        [
            shape((rows, INNER), BF16),
            shape((rows, INNER), BF16),
            shape((REACH, INNER), BF16),
            shape((REACH, INNER), BF16),
            shape((2, INNER), F32),
            shape((taps_wide, INNER), BF16),
        ]
        + [shape(dims, BF16) for dims in halves],
        [ext, wide, wide, pltpu.VMEM((INNER, D), BF16), pltpu.VMEM((D, INNER), BF16)]
        + [pltpu.VMEM((2, tile, taps_wide), BF16), work, work, work, turned_tile, turned_tile]
        + [pltpu.VMEM((INNER, taps_wide), F32), pltpu.VMEM((INNER, D), F32)]
        + [pltpu.VMEM((16, INNER), F32)]
        + [pltpu.VMEM((2,) + halves[0], BF16), pltpu.VMEM((2,) + halves[2], BF16)]
        + [dma((3 + 3 * pieces,))],
        us=45,
    )(
        spots, m_low, moved, m_high, masks, cotangent, cotangent, norm_params, *conv_pieces
    )
    d_low, d_high = lax.ppermute(d_last, AXES, up), lax.ppermute(d_first, AXES, down)
    first, second = Reduction(place, keep1, send1), Reduction(place, keep2, send2)
    (block_out,) = call(
        functools.partial(out_kernel, pieces),
        (steps,),
        [SMEM, rows_spec(tile, INNER), rows_spec(tile, D)] + [ANY] * pieces,
        [rows_spec(tile, D)],
        [shape((rows, D), BF16)],
        [pltpu.VMEM((INNER, D), BF16), dma((2 * pieces,))],
        us=9,
    )(spots, hidden_c, tokens, *conv_pieces)

    def back_conv(last, spots, before):
        here = steps // 2
        at = here * last

        def here_spec(width):
            return pl.BlockSpec((tile, width), lambda i: (i + at, 0))

        dims = half_dims(CHUNKS[2])
        return call(
            functools.partial(back_conv_kernel, last, w_in.shape[0]),
            (here,),
            [SMEM] + [ANY] * 4
            + [here_spec(8), here_spec(INNER), here_spec(1), here_spec(INNER), here_spec(D)]
            + [params_spec]
            + [ANY] * last,
            [rows_spec(tile, INNER), whole(2, INNER)] + [ANY] * (1 + last),
            [shape((rows // 2, INNER), BF16), shape((2, INNER), F32)]
            + ([shape(dims, BF16)] * 2 if last else [shape((INNER, D), F32)]),
            ([pltpu.VMEM((2,) + dims, BF16)] if last else [])
            + [
                ext,
                wide,
                pltpu.VMEM((tile, taps_wide), BF16),
                pltpu.VMEM((tile, INNER), F32),
                pltpu.VMEM((INNER, D), F32),
                pltpu.VMEM((16, INNER), F32),
                dma((5,)),
            ],
            us=16,
        )(
            spots, d_low, d_conv, d_high, turned, masks, xhat_b, rstd_b, slope_b, hidden_a,
            norm_params, *before,
        )

    away = (first.x(block_out), second.x(block_out))
    d_pre0, sums_b0, grad_part = back_conv(0, tie(spots, *away), ())
    sent, got1 = exchange(place, first.scatter(d_pre0))
    d_pre1, sums_b1, keep, send = back_conv(1, tie(spots, sent), (grad_part,))
    third = Reduction(place, keep, send)
    n1, n2 = sent.shape[1], half_dims(CHUNKS[1])[1] // place.seq
    part1 = summed(tie(got1, d_pre1)).astype(BF16)
    sent, got2 = exchange(place, copies_for(place, part1), second.scatter(d_pre1))
    away = third.x(sent)
    input_grad, sums_a = call(
        functools.partial(back_a_kernel, pieces, steps // 2),
        (steps,),
        [SMEM]
        + [
            pl.BlockSpec((tile, INNER), lambda i: (jnp.minimum(i, steps // 2 - 1), 0)),
            pl.BlockSpec((tile, INNER), lambda i: (jnp.maximum(i - steps // 2, 0), 0)),
        ]
        + [rows_spec(tile, D), rows_spec(tile, 1), rows_spec(tile, D), rows_spec(tile, D)]
        + [params_spec]
        + [ANY] * pieces,
        [rows_spec(tile, D), whole(2, D)],
        [shape((rows, D), F32), shape((2, D), F32)],
        [
            pltpu.VMEM((D, INNER), BF16),
            pltpu.VMEM((INNER, D), BF16),
            pltpu.VMEM((tile, D), F32),
            pltpu.VMEM((16, D), F32),
            dma((pieces,)),
        ],
        us=17,
    )(
        tie(spots, away), d_pre0, d_pre1, xhat_a, rstd_a, slope_a, cotangent, norm_params, *in_pieces
    )

    sums = (sums_a, sums_b0, sums_b1, sums_c)
    norm_tiles = call(
        functools.partial(norm_tiles_kernel, place.seq),
        (1,),
        [whole(*x.shape) for x in sums],
        whole(place.seq, SUB, LANE),
        shape((place.seq, SUB, LANE), BF16),
        [pltpu.VMEM((8, D + 2 * INNER), F32)],
        us=1,
    )(*sums)
    part2 = summed(tie(got2, input_grad)[:, n1:]).astype(BF16)
    last = third.scatter(input_grad)
    n3 = last.shape[1]
    sent, got3 = exchange(place, copies_for(place, part2), last, norm_tiles[:, None])
    part3 = summed(got3[:, n2:])
    part3 = jnp.concatenate([part3[:-1].astype(BF16), high_low(part3[-1:])], axis=0)
    sent, got4 = exchange(place, copies_for(place, part3))

    row_states, col_states = (row_in, row_conv, row_out), (col_in, col_conv, col_out)
    row_specs = [whole(*r.shape) for r in row_states]
    col_specs = [whole(*c.shape) for c in col_states]
    cols_all = D + 2 * INNER
    pack_spec = whole(4, cols_all)
    fulls = [pltpu.VMEM(half_dims(c)[1:], BF16) for c in CHUNKS]
    sems = [dma((place.seq,))] * 2
    got3 = tie(got3, sent)
    (pack,) = call(
        functools.partial(pack_kernel, rows_of),
        (1,),
        [ANY, ANY] + row_specs,
        [pack_spec],
        [shape((4, cols_all), F32)],
        fulls[:2] + sems,
        us=2,
    )(got2, got3, *row_states)
    pack = sum_shards(pack, place)

    def update_scratch(weights):
        lines = max(w.shape[0] + -w.shape[0] % LANE for w in weights)
        return [pltpu.VMEM((8, lines), F32)] + [pltpu.VMEM((lines, LANE), F32)] * 2

    weight_specs = [whole(*w.shape) for w in weights]
    results = call(
        functools.partial(update_kernel, rows_of),
        (1,),
        [ANY, ANY, pack_spec] + weight_specs[1:] + row_specs[1:] + col_specs[1:],
        weight_specs[1:] * 2 + row_specs[1:] + col_specs[1:],
        [shape(w.shape, F32) for w in weights[1:]] * 2
        + [shape(r.shape, F32) for r in row_states[1:] + col_states[1:]],
        update_scratch(weights[1:]) + fulls[:2] + sems,
        us=7,
    )(got2, got3, pack, *weights[1:], *row_states[1:], *col_states[1:])
    grad_conv, grad_out, new_conv, new_out, row_conv_new, row_out_new, col_conv_new, col_out_new = (
        results
    )
    (pack_in,) = call(
        functools.partial(pack_in_kernel, rows_of),
        (1,),
        [ANY],
        [pack_spec],
        [shape((4, cols_all), F32)],
        [fulls[2], pltpu.VMEM((place.seq, SUB, LANE), BF16)] + sems,
        us=2,
    )(got4)
    pack_in = sum_shards(pack_in, place)
    grad_in, new_in, row_in_new, col_in_new, *norm_results = call(
        functools.partial(update_in_kernel, rows_of),
        (1,),
        [ANY, pack_spec, pack_spec, params_spec, params_spec]
        + [weight_specs[0], row_specs[0], col_specs[0]],
        [weight_specs[0]] * 2 + [row_specs[0], col_specs[0]] + [params_spec] * 3,
        [shape(w_in.shape, F32)] * 2
        + [shape(row_in.shape, F32), shape(col_in.shape, F32)]
        + [shape((2, cols_all), F32)] * 3,
        update_scratch(weights[:1]) + [fulls[2], sems[0]],
        us=3,
    )(got4, pack_in, pack, norm_params, norm_second, w_in, row_in, col_in)
    return (
        block_out,
        input_grad,
        grad_in,
        grad_conv,
        grad_out,
        new_in,
        new_conv,
        new_out,
        row_in_new,
        col_in_new,
        row_conv_new,
        col_conv_new,
        row_out_new,
        col_out_new,
        *norm_results,
    )


def solution(mesh):
    both, rows = P(AXES, None), P("fsdp", None)
    in_specs = (
        both, P(AXES), P(), both, rows, rows, rows, P(),
        P("fsdp"), P(), P("fsdp"), P(), P("fsdp"), P(), P(),
    )
    out_specs = (
        both, both, rows, rows, rows, rows, rows, rows,
        P("fsdp"), P(), P("fsdp"), P(), P("fsdp"), P(), P(), P(), P(),
    )
    return jax.shard_map(
        on_device, mesh=mesh, in_specs=in_specs, out_specs=out_specs, check_vma=False
    )
```

```python
import functools
import math

import jax
import jax.numpy as jnp
from jax import lax
from jax.experimental import pallas as pl
from jax.experimental.pallas import tpu as pltpu
from jax.sharding import PartitionSpec as P

D = 1280
INNER = 640
KERNEL_TAPS = 5
DILATION_STEP = 128
STEP = 10
EPSILON = 1e-05
DECAY = 1.0 - STEP ** (-0.8)

REACH = (KERNEL_TAPS - 1) // 2 * DILATION_STEP
MID = (KERNEL_TAPS - 1) // 2
F32 = jnp.float32
BF16 = jnp.bfloat16
SUB, LANE = 16, 128
AXES = ("seq", "fsdp")
NT = (((1,), (1,)), ((), ()))
TN = (((0,), (0,)), ((), ()))
NN = (((1,), (0,)), ((), ()))
VMEM_LIMIT = 58 * 1024 * 1024


def call(kernel, grid, in_specs, out_specs, out_shape, scratch=(), us=1.0, aliases=None):
    params = pltpu.CompilerParams(
        vmem_limit_bytes=VMEM_LIMIT, dimension_semantics=("arbitrary",) * len(grid)
    )
    return pl.pallas_call(
        kernel,
        grid=grid,
        in_specs=in_specs,
        out_specs=out_specs,
        out_shape=out_shape,
        scratch_shapes=list(scratch),
        compiler_params=params,
        input_output_aliases=aliases or {},
        cost_estimate=pl.CostEstimate(
                flops=int(us * 1.1e9), bytes_accessed=int(us * 3.4e6), transcendentals=0
        ),
    )


def shape(dims, dtype):
    return jax.ShapeDtypeStruct(dims, dtype)


def rows_spec(tile, width):
    return pl.BlockSpec((tile, width), lambda i: (i, 0))


def whole(*dims):
    return pl.BlockSpec(dims, lambda *_: (0,) * len(dims))


ANY = pl.BlockSpec(memory_space=pl.ANY)
SMEM = pl.BlockSpec(memory_space=pltpu.SMEM)


ERFC_P = 0.47 / math.sqrt(2.0)
ERFC_C = (
    0.12357219400743558,
    0.1999878668208835,
    -0.08033356004356296,
    0.3660253986657854,
    -0.1092519747040215,
)
LOG2E = 1.4426950408889634


def gelu_and_slope(y):
    t = pltpu.reciprocal(1.0 + ERFC_P * jnp.abs(y), approx=True)
    bell = jnp.exp2(y * y * (-0.5 * LOG2E))
    poly = ERFC_C[4] * t + ERFC_C[3]
    for c in ERFC_C[2::-1]:
        poly = poly * t + c
    tail = poly * t * bell
    cdf = jnp.where(y > 0.0, 1.0 - tail, tail)
    return y * cdf, cdf + y * (bell * (1.0 / math.sqrt(2.0 * math.pi)))


def lane_blocks(width):
    return [slice(k, k + LANE) for k in range(0, width, LANE)]


def row_stats(ref, rows):
    width = ref.shape[-1]
    blocks = lane_blocks(width)
    total = ref[rows, blocks[0]].astype(F32)
    for b in blocks[1:]:
        total = total + ref[rows, b].astype(F32)
    mean = jnp.sum(total, axis=-1, keepdims=True) * (1.0 / width)
    square = None
    for b in blocks:
        centered = ref[rows, b].astype(F32) - mean
        square = centered * centered if square is None else square + centered * centered
    variance = jnp.sum(square, axis=-1, keepdims=True) * (1.0 / width)
    return mean, lax.rsqrt(variance + EPSILON)


def fold(values):
    total = values[0:8]
    for k in range(8, values.shape[0], 8):
        total = total + values[k : k + 8]
    return total


def in_stages(count, stages, between=()):
    chunks = [slice(k, k + CHUNK) for k in range(0, count, CHUNK)]
    kept, rounds = {}, len(chunks) + len(stages) - 1
    for t in range(rounds):
        for n, stage in enumerate(stages):
            if 0 <= t - n < len(chunks):
                kept[n, t - n] = stage(chunks[t - n], kept.get((n - 1, t - n)))
        for work in between[t * len(between) // rounds : (t + 1) * len(between) // rounds]:
            work()


def halves_of(count):
    return (slice(0, count // 2), slice(count // 2, count))


def row_means(sums, width):
    return [jnp.sum(x, axis=-1, keepdims=True) * (1.0 / width) for x in sums]


def norm_back(rows, dxhat_ref, xhat_ref, means, put):
    mean_d, mean_dx, rstd = means
    for b in lane_blocks(dxhat_ref.shape[-1]):
        xhat = xhat_ref[rows, b].astype(F32)
        put(b, (dxhat_ref[rows, b] - mean_d - xhat * mean_dx) * rstd)


def add_terms(acc_ref, b, dy, xhat):
    acc_ref[0:8, b] += fold(dy * xhat)
    acc_ref[8:16, b] += fold(dy)


def open_sums(acc_ref):
    @pl.when(pl.program_id(0) == 0)
    def _():
        acc_ref[...] = jnp.zeros_like(acc_ref)


def close_sums(out_ref, acc_ref):
    @pl.when(pl.program_id(0) == pl.num_programs(0) - 1)
    def _():
        out_ref[0:1, :] = jnp.sum(acc_ref[0:8, :], axis=0, keepdims=True)
        out_ref[1:2, :] = jnp.sum(acc_ref[8:16, :], axis=0, keepdims=True)


def run_copies(copies):
    for copy in copies:
        copy.start()
    for copy in copies:
        copy.wait()


def piece_copies(pieces, full_ref, me, sem, first=0):
    each = full_ref.shape[0] // len(pieces)
    return [
        pltpu.make_async_copy(
            piece.at[0:each, :],
            full_ref.at[pl.ds(pl.multiple_of((me ^ k) * each, SUB), each), :],
            sem.at[first + k],
        )
        for k, piece in enumerate(pieces)
    ]


def out_copies(pieces, full_ref, me, sem, first=0):
    each, width = full_ref.shape[0] // len(pieces), full_ref.shape[1] // 2
    copies = []
    for k, piece in enumerate(pieces):
        rows = pl.ds(pl.multiple_of((me ^ k) * each, SUB), each)
        for side in range(2):
            at = piece.shape[0] - (2 - side) * each
            copies.append(
                pltpu.make_async_copy(
                    piece.at[at : at + each, :],
                    full_ref.at[rows, side * width : (side + 1) * width],
                    sem.at[first + 2 * k + side],
                )
            )
    return copies


def column(row):
    return jnp.transpose(jnp.broadcast_to(row, (LANE, LANE)))


CHUNK = 64


def norm_a_kernel(tok_ref, np_ref, hid_ref, slope_ref, xhat_ref, rstd_ref):
    def stats(rows, _):
        mean, rstd = row_stats(tok_ref, rows)
        rstd_ref[rows, :] = rstd
        return mean, rstd

    def work(rows, kept):
        mean, rstd = kept
        for b in lane_blocks(D):
            xhat = (tok_ref[rows, b].astype(F32) - mean) * rstd
            hidden, slope = gelu_and_slope(xhat * np_ref[0:1, b] + np_ref[1:2, b])
            hid_ref[rows, b] = hidden.astype(BF16)
            slope_ref[rows, b] = slope.astype(BF16)
            xhat_ref[rows, b] = xhat.astype(BF16)

    in_stages(tok_ref.shape[0], [stats, work])


def in_kernel(pieces, tiles, place_ref, ends_ref, hid_ref, live_ref, np_ref, *refs):
    piece_refs = refs[:pieces]
    edges = tiles[0] == 0
    outs = refs[-(10 if edges else 8) :]
    mov_ref, slope_ref, xhat_ref, rstd_ref, mask_ref = outs[:5]
    w_ref, pre_ref, sem = outs[-3:]
    step = pl.program_id(0)
    tile = hid_ref.shape[0]

    @pl.when(step == 0)
    def _():
        run_copies(piece_copies(piece_refs, w_ref, place_ref[0], sem))

    for half in halves_of(tile):
        pre_ref[half, :] = lax.dot_general(
            hid_ref[half, :], w_ref[...], NN, preferred_element_type=F32
        )

    at_tile = tiles[0] + step * tiles[1]
    first = place_ref[1] + at_tile * tile
    ends = ends_ref[...]
    lanes = lax.broadcasted_iota(jnp.int32, (LANE, 8), 1)
    offsets = ((lanes - MID) * DILATION_STEP).astype(F32)
    for k in range(tile // LANE):
        at = (first + k * LANE + lax.broadcasted_iota(jnp.int32, (LANE, 1), 0)).astype(F32)
        begin = jnp.max(jnp.where(ends <= at, ends, 0.0), axis=1, keepdims=True)
        end = jnp.min(jnp.where(ends > at, ends, 1e9), axis=1, keepdims=True)
        there = at + offsets
        same = jnp.where((there >= begin) & (there < end), 1.0, 0.0)
        live = column(live_ref[pl.ds(at_tile * (tile // LANE) + k, 1), :].astype(F32))
        mask_ref[k * LANE : (k + 1) * LANE, :] = jnp.where(lanes == MID, live[:, 0:8], same)

    def stats(rows, _):
        mean, rstd = row_stats(pre_ref, rows)
        rstd_ref[rows, :] = rstd
        return mean, rstd

    def work(rows, kept):
        mean, rstd = kept
        live = mask_ref[rows, MID : MID + 1]
        for b in lane_blocks(INNER):
            gains = slice(D + b.start, D + b.stop)
            xhat = (pre_ref[rows, b] - mean) * rstd
            hidden, slope = gelu_and_slope(xhat * np_ref[0:1, gains] + np_ref[1:2, gains])
            mov_ref[rows, b] = (hidden * live).astype(BF16)
            slope_ref[rows, b] = slope.astype(BF16)
            xhat_ref[rows, b] = xhat.astype(BF16)

    in_stages(tile, [stats, work])
    if edges:
        first_ref, last_ref = outs[5:7]

        @pl.when(step == 0)
        def _():
            first_ref[...] = mov_ref[0:REACH, :]

        @pl.when(step == 1)
        def _():
            last_ref[...] = mov_ref[tile - REACH :, :]


def load_window(low, mid, high, ext_ref, sem):
    rows = mid.shape[0]
    return [
        pltpu.make_async_copy(low, ext_ref.at[0:REACH, :], sem.at[0]),
        pltpu.make_async_copy(mid, ext_ref.at[REACH : REACH + rows, :], sem.at[1]),
        pltpu.make_async_copy(high, ext_ref.at[REACH + rows : 2 * REACH + rows, :], sem.at[2]),
    ]


def fill_taps(taps_ref, ext_ref, mask_ref, start):
    tile = taps_ref.shape[0]
    for j in range(KERNEL_TAPS):
        rows = pl.ds(pl.multiple_of(start + j * DILATION_STEP, DILATION_STEP), tile)
        picked = ext_ref[rows, :]
        if j != MID:
            picked = picked * mask_ref[:, j : j + 1].astype(BF16)
        taps_ref[:, j * INNER : (j + 1) * INNER] = picked


def conv_kernel(
    pieces, rows_of, place_ref, low_ref, mov_ref, high_ref, mask_ref, cot_ref, before_ref, np_ref, *refs
):
    piece_refs = refs[:pieces]
    hid_ref, dconv_ref, first_ref, last_ref, sums_ref, turned_ref = refs[pieces : pieces + 6]
    outs = refs[pieces + 6 : pieces + 10]
    ext_ref, wc_ref, wct_ref, wo_ref, wt_ref, taps_ref, pre_ref, dh_ref, xhat_ref = refs[
        pieces + 10 : pieces + 19
    ]
    dt_ref, ht_ref, gc_ref, go_ref, acc_ref, stage1_ref, stage2_ref, sem = refs[pieces + 19 :]
    step, steps = pl.program_id(0), pl.num_programs(0) - 1
    tile = taps_ref.shape[1]
    slot = lax.rem(step, 2)

    @pl.when(step == 0)
    def _():
        me = place_ref[0]
        outs = out_copies(piece_refs, wo_ref, me, sem, 3)
        rest = load_window(low_ref, mov_ref, high_ref, ext_ref, sem)
        rest += piece_copies(piece_refs, wc_ref, me, sem, 3 + 2 * pieces)
        for copy in outs + rest:
            copy.start()
        for ref in (acc_ref, gc_ref, go_ref, dt_ref, ht_ref):
            ref[...] = jnp.zeros_like(ref)
        taps_ref[1] = jnp.zeros_like(taps_ref[1])
        for copy in outs:
            copy.wait()
        for k in range(0, D, 256):
            wt_ref[k : k + 256, :] = jnp.transpose(wo_ref[:, k : k + 256])
        for copy in rest:
            copy.wait()

    def grad_conv(cols):
        def work():
            gc_ref[:, cols] += lax.dot_general(
                dt_ref[...], taps_ref[1 - slot, :, cols], NN, preferred_element_type=F32
            )

        return work

    def grad_out(cols):
        def work():
            go_ref[:, cols] += lax.dot_general(
                ht_ref[...], before_ref[:, cols], NN, preferred_element_type=F32
            )

        return work

    taps_wide = KERNEL_TAPS * INNER
    products = [grad_conv(slice(k, min(k + 768, taps_wide))) for k in range(0, taps_wide, 768)]
    products += [grad_out(slice(k, min(k + 768, D))) for k in range(0, D, 768)]

    @pl.when(step < steps)
    def _():
        fill_taps(taps_ref.at[slot], ext_ref, mask_ref, step * tile)
        pre_ref[...] = lax.dot_general(
            taps_ref[slot], wc_ref[...], NN, preferred_element_type=F32
        )
        dh_ref[...] = lax.dot_general(cot_ref[...], wt_ref[...], NN, preferred_element_type=F32)
        for n in range(2):
            tap = jnp.minimum(2 * step + n, KERNEL_TAPS - 1)
            source = wc_ref[pl.ds(pl.multiple_of(tap * INNER, SUB), INNER), :]
            target = pl.multiple_of((KERNEL_TAPS - 1 - tap) * INNER, SUB)
            wct_ref[pl.ds(target, INNER), :] = jnp.transpose(source)

        def stats(rows, _):
            return row_stats(pre_ref, rows)

        def work(rows, kept):
            mean, rstd = kept
            sums = [0.0, 0.0]
            for b in lane_blocks(INNER):
                gains = slice(D + INNER + b.start, D + INNER + b.stop)
                gain = np_ref[0:1, gains]
                xhat = (pre_ref[rows, b] - mean) * rstd
                hidden, slope = gelu_and_slope(xhat * gain + np_ref[1:2, gains])
                hid_ref[rows, b] = hidden.astype(BF16)
                dy = dh_ref[rows, b] * slope
                add_terms(acc_ref, b, dy, xhat)
                dxhat = dy * gain
                xhat_ref[rows, b] = xhat
                dh_ref[rows, b] = dxhat
                sums = [sums[0] + dxhat, sums[1] + dxhat * xhat]
            return row_means(sums, INNER) + [rstd]

        def finish(rows, means):
            def put(b, value):
                dconv_ref[rows, b] = value.astype(BF16)

            norm_back(rows, dh_ref, xhat_ref, means, put)

        in_stages(tile, [stats, work, finish], products)
        dt_ref[...] = jnp.transpose(dconv_ref[...])
        ht_ref[...] = jnp.transpose(hid_ref[...])

    @pl.when(step == 0)
    def _():
        first_ref[...] = dconv_ref[0:REACH, :]

    @pl.when(step == steps - 1)
    def _():
        last_ref[...] = dconv_ref[tile - REACH :, :]

    @pl.when(step == steps)
    def _():
        copy = pltpu.make_async_copy(wct_ref, turned_ref, sem.at[4])
        copy.start()
        for work in products:
            work()
        core = lax.rem(place_ref[0], 2)
        _, rows_conv, rows_out = rows_of
        stage_turned(stage1_ref, core, gc_ref, rows_conv, 0, slice(0, CUT // LANE))
        first_tiles = rows_conv // SUB * (CUT // LANE)
        stage_plain(stage1_ref, core, go_ref, rows_out, first_tiles)
        copies = stage_copies(stage1_ref, outs[0], outs[1], spans(CHUNKS[0], rows_of)[1], sem, 0)
        for each in copies:
            each.start()
        stage_turned(stage2_ref, core, gc_ref, rows_conv, 0, slice(CUT // LANE, INNER // LANE))
        more = stage_copies(stage2_ref, outs[2], outs[3], spans(CHUNKS[1], rows_of)[1], sem, 2)
        for each in more:
            each.start()
        for each in copies + more + [copy]:
            each.wait()
        sums_ref[0:1, :] = jnp.sum(acc_ref[0:8, :], axis=0, keepdims=True)
        sums_ref[1:2, :] = jnp.sum(acc_ref[8:16, :], axis=0, keepdims=True)


def stage_tiles(stage_ref, core, first_row, rows_each, base, block0, blocks, value):
    for g in range(value.shape[0] // SUB):
        row = first_row + g * SUB
        owner, inside = row // rows_each, row % rows_each // SUB
        side = core ^ (owner % 2)
        for b in range(value.shape[1] // LANE):
            tile = value[g * SUB : (g + 1) * SUB, b * LANE : (b + 1) * LANE]
            at = base + inside * blocks + block0 + b
            stage_ref[side, owner // 2, at] = tile.astype(BF16)


def stage_plain(stage_ref, core, grad_ref, rows_each, base):
    blocks = grad_ref.shape[1] // LANE
    for row in range(0, grad_ref.shape[0], SUB):
        part = grad_ref[row : row + SUB, :]
        stage_tiles(stage_ref, core, row, rows_each, base, 0, blocks, part)


def stage_turned(stage_ref, core, turned_ref, rows_each, base, blocks):
    count = blocks.stop - blocks.start
    for row in range(0, turned_ref.shape[1], LANE):
        for b in range(count):
            at = (blocks.start + b) * LANE
            part = jnp.transpose(turned_ref[at : at + LANE, row : row + LANE])
            stage_tiles(stage_ref, core, row, rows_each, base, b, count, part)


def stage_copies(stage_ref, keep_ref, send_ref, used, sem, first):
    count = stage_ref.shape[2]
    if used < count:
        dims = stage_ref.shape[:2] + (count - used, SUB, LANE)
        stage_ref[:, :, used:] = jnp.zeros(dims, BF16)
    return [
        pltpu.make_async_copy(stage_ref.at[n], ref, sem.at[first + n])
        for n, ref in enumerate((keep_ref, send_ref))
    ]


def back_conv_kernel(
    last, rows_in, place_ref, low_ref, d_ref, high_ref, turned_ref, mask_ref, xhat_ref, rstd_ref, slope_ref, hid_ref, np_ref, *refs
):
    if last:
        before_ref, dpre_ref, sums_ref, keep_ref, send_ref, stage_ref = refs[:6]
    else:
        dpre_ref, sums_ref, part_ref = refs[:3]
    ext_ref, wt_ref, taps_ref, dmov_ref, grad_ref, acc_ref, sem = refs[-7:]
    step, steps = pl.program_id(0), pl.num_programs(0)
    tile = taps_ref.shape[0]
    open_sums(acc_ref)

    @pl.when(step == 0)
    def _():
        copies = load_window(low_ref, d_ref, high_ref, ext_ref, sem)
        copies.append(pltpu.make_async_copy(turned_ref, wt_ref, sem.at[3]))
        if last:
            copies.append(pltpu.make_async_copy(before_ref, grad_ref, sem.at[4]))
        for copy in copies:
            copy.start()
        if not last:
            grad_ref[...] = jnp.zeros_like(grad_ref)
        for copy in copies:
            copy.wait()

    fill_taps(taps_ref, ext_ref, mask_ref, (steps * last + step) * tile)
    for half in halves_of(tile):
        dmov_ref[half, :] = lax.dot_general(
            taps_ref[half, :], wt_ref[...], NN, preferred_element_type=F32
        )

    def work(rows, _):
        live = mask_ref[rows, MID : MID + 1]
        sums = [0.0, 0.0]
        for b in lane_blocks(INNER):
            xhat = xhat_ref[rows, b].astype(F32)
            dy = dmov_ref[rows, b] * live * slope_ref[rows, b].astype(F32)
            add_terms(acc_ref, b, dy, xhat)
            dxhat = dy * np_ref[0:1, D + b.start : D + b.stop]
            dmov_ref[rows, b] = dxhat
            sums = [sums[0] + dxhat, sums[1] + dxhat * xhat]
        return row_means(sums, INNER) + [rstd_ref[rows, :]]

    def finish(rows, means):
        def put(b, value):
            dpre_ref[rows, b] = value.astype(BF16)

        norm_back(rows, dmov_ref, xhat_ref, means, put)

    in_stages(tile, [work, finish])
    close_sums(sums_ref, acc_ref)
    grad_ref[...] += lax.dot_general(dpre_ref[...], hid_ref[...], TN, preferred_element_type=F32)

    @pl.when(step == steps - 1)
    def _():
        if last:
            all_blocks = slice(0, INNER // LANE)
            stage_turned(stage_ref, lax.rem(place_ref[0], 2), grad_ref, rows_in, 0, all_blocks)
            used = rows_in // SUB * (INNER // LANE)
            run_copies(stage_copies(stage_ref, keep_ref, send_ref, used, sem, 0))
        else:
            run_copies([pltpu.make_async_copy(grad_ref, part_ref, sem.at[0])])


def back_a_kernel(pieces, half, place_ref, dpre0_ref, dpre1_ref, xhat_ref, rstd_ref, slope_ref, cot_ref, np_ref, *refs):
    piece_refs = refs[:pieces]
    grad_ref, sums_ref, w_ref, wt_ref, dh_ref, acc_ref, sem = refs[-7:]
    open_sums(acc_ref)

    @pl.when(pl.program_id(0) == 0)
    def _():
        run_copies(piece_copies(piece_refs, w_ref, place_ref[0], sem))
        for k in range(0, D, 256):
            wt_ref[:, k : k + 256] = jnp.transpose(w_ref[k : k + 256, :])

    second = (jnp.zeros((1, 1), jnp.int32) + pl.program_id(0)) >= half
    d_pre = jnp.where(second, dpre1_ref[...], dpre0_ref[...])
    dh_ref[...] = lax.dot_general(d_pre, wt_ref[...], NN, preferred_element_type=F32)

    def work(rows, _):
        sums = [0.0, 0.0]
        for b in lane_blocks(D):
            xhat = xhat_ref[rows, b].astype(F32)
            dy = dh_ref[rows, b] * slope_ref[rows, b].astype(F32)
            add_terms(acc_ref, b, dy, xhat)
            dxhat = dy * np_ref[0:1, b]
            dh_ref[rows, b] = dxhat
            sums = [sums[0] + dxhat, sums[1] + dxhat * xhat]
        return row_means(sums, D) + [rstd_ref[rows, :]]

    def finish(rows, means):
        def put(b, value):
            grad_ref[rows, b] = cot_ref[rows, b].astype(F32) + value

        norm_back(rows, dh_ref, xhat_ref, means, put)

    in_stages(dpre0_ref.shape[0], [work, finish])
    close_sums(sums_ref, acc_ref)


def out_kernel(pieces, place_ref, hid_ref, tok_ref, *refs):
    piece_refs = refs[:pieces]
    out_ref, w_ref, sem = refs[pieces:]

    @pl.when(pl.program_id(0) == 0)
    def _():
        run_copies(out_copies(piece_refs, w_ref, place_ref[0], sem))

    branch = lax.dot_general(hid_ref[...], w_ref[...], NN, preferred_element_type=F32)
    out_ref[...] = (tok_ref[...].astype(F32) + branch).astype(BF16)


WIDTHS = (INNER, INNER, D)
LANE0 = (0, INNER, 2 * INNER)
CUT = 2 * LANE
CHUNKS = (((1, 0, CUT), (2, 0, D)), ((1, CUT, INNER - CUT),), ((0, 0, INNER),))


def spans(chunk, rows):
    found, first = [], 0
    for weight, col, cols in chunk:
        tiles = rows[weight] // SUB * (cols // LANE)
        found.append((weight, col // LANE, cols // LANE, first, tiles))
        first += tiles
    return found, first


def column_sums(pack_ref, row, ref, chunk, rows):
    for weight, block0, blocks, first, tiles in spans(chunk, rows)[0]:

        def body(g, carry, first=first, blocks=blocks):
            new = []
            for b in range(blocks):
                value = ref[first + g * blocks + b].astype(F32)
                new.append(carry[b] + fold(value * value + 1e-30))
            return tuple(new)

        zero = tuple(jnp.zeros((8, LANE), F32) for _ in range(blocks))
        cols = lax.fori_loop(0, tiles // blocks, body, zero, unroll=5)
        for b in range(blocks):
            lane = LANE0[weight] + (block0 + b) * LANE
            pack_ref[row : row + 1, lane : lane + LANE] = jnp.sum(cols[b], axis=0, keepdims=True)


def load_full(refs, place_ref, first, full_ref, sem, at):
    pieces = refs[0].shape[0]
    each = full_ref.shape[0] // (2 * pieces)
    y = place_ref[2] % 2
    copies = []
    for n, (ref, side) in enumerate(zip(refs, (y, 1 - y))):
        for p in range(pieces):
            target = full_ref.at[pl.ds((side * pieces + p) * each, each)]
            source = ref.at[p, first : first + each]
            copies.append(pltpu.make_async_copy(source, target, sem.at[at + n * pieces + p]))
    return copies


def pack_kernel(rows, pieces, place_ref, part_ref, *refs):
    states, sums, (pack_ref, acc_ref) = refs[0:3], refs[3:7], refs[7:9]
    pack_ref[...] = jnp.zeros_like(pack_ref)
    lanes_of = ((0, D), (D, D + INNER), (D, D + INNER), (D + INNER, D + 2 * INNER))
    for part, (lane0, lane1) in zip(sums, lanes_of):
        pack_ref[0:2, lane0:lane1] += part[...]
    lanes = lax.broadcasted_iota(jnp.int32, (1, LANE), 1)
    for k in range(3):
        total = jnp.sum(states[k][...].reshape(1, -1), axis=1, keepdims=True)
        pack_ref[3:4, 0:LANE] += jnp.where(lanes == k, total, 0.0)
    acc_ref[...] = jnp.zeros_like(acc_ref)
    spare = acc_ref.shape[0] - 1
    outer = place_ref[3] // 2
    piece = place_ref[2] % 2 * outer + place_ref[2] // 2
    at = 0
    for chunk, each in zip(CHUNKS[:2], pieces):
        found, _ = spans(chunk, rows)
        start = piece * each

        def body(k, carry, found=found, start=start, at=at):
            n = start + k
            slot = spare
            for weight, block0, blocks, first, tiles in found:
                here = LANE0[weight] // LANE + block0 + lax.rem(jnp.maximum(n - first, 0), blocks)
                slot = jnp.where((n >= first) & (n < first + tiles), here, slot)
            value = part_ref[at + k].astype(F32)
            acc_ref[slot] += value * value + 1e-30
            return carry

        lax.fori_loop(0, each, body, 0, unroll=2)
        at += each
    for slot in range(spare):
        pack_ref[2:3, slot * LANE : (slot + 1) * LANE] = jnp.sum(acc_ref[slot], axis=0, keepdims=True)


def pack_in_kernel(rows, place_ref, mine_ref, other_ref, pack_ref, full_ref, sem):
    run_copies(load_full((mine_ref, other_ref), place_ref, 0, full_ref, sem, 0))
    column_sums(pack_ref, 0, full_ref, CHUNKS[2], rows)


def update_weight(
    k, squares, states_sum, source, weight, state, col_state, grad_ref, new, row_new_ref, col_new_ref, scratch
):
    line_ref, state_ref, new_ref = scratch
    width, fan, rows_here = WIDTHS[k], (D, KERNEL_TAPS * INNER, INNER)[k], weight.shape[0]
    col_new = DECAY * col_state[...].reshape(1, -1) + (1.0 - DECAY) * (squares * (1.0 / fan))
    col_new_ref[...] = col_new.reshape(-1)
    total = DECAY * states_sum
    total = total + (1.0 - DECAY) * (1.0 / width) * jnp.sum(squares, axis=1, keepdims=True)
    scaled = col_new / (total * (1.0 / fan))
    rate = 0.5 / fan**0.5
    line_ref[0:1, 0:rows_here] = state[...].reshape(1, -1)
    whole_rows = rows_here + -rows_here % LANE
    for c in range(0, whole_rows, LANE):
        state_ref[c : c + LANE, :] = column(line_ref[0:1, c : c + LANE])

    def body(g, carry):
        rows = pl.ds(pl.multiple_of(g * SUB, SUB), SUB)
        square = 0.0
        for ref, block0, blocks, first in source:
            for b in range(blocks):
                value = ref[first + g * blocks + b].astype(F32)
                grad_ref[rows, (block0 + b) * LANE : (block0 + b + 1) * LANE] = value
                square = square + (value * value + 1e-30)
        mean = jnp.sum(square, axis=1, keepdims=True) * (1.0 / width)
        row_new = DECAY * state_ref[rows, :] + (1.0 - DECAY) * mean
        new_ref[rows, :] = row_new
        for ref, block0, blocks, first in source:
            for b in range(blocks):
                lanes = slice((block0 + b) * LANE, (block0 + b + 1) * LANE)
                value = ref[first + g * blocks + b].astype(F32)
                step = value * lax.rsqrt(row_new * scaled[:, lanes])
                new[rows, lanes] = weight[rows, lanes] - rate * step
        return carry

    lax.fori_loop(0, rows_here // SUB, body, 0, unroll=5)
    for c in range(0, whole_rows, LANE):
        line_ref[0:1, c : c + LANE] = jnp.transpose(new_ref[c : c + LANE, :])[0:1, :]
    row_new_ref[...] = line_ref[0:1, 0:rows_here].reshape(-1)


def sources_of(chunk, ref, rows):
    return {w: (ref, block0, blocks, first) for w, block0, blocks, first, _ in spans(chunk, rows)[0]}


def update_kernel(rows, copies_of, place_ref, mine_ref, other_ref, pack_ref, np_ref, second_ref, *refs):
    weights, states, col_states = refs[0:2], refs[2:4], refs[4:6]
    grads, news, rows_new, cols_new = refs[6:8], refs[8:10], refs[10:12], refs[12:14]
    ngrad_ref, nsecond_ref, nnew_ref = refs[14:17]
    full1_ref, full2_ref, sem = refs[20:23]
    both = (mine_ref, other_ref)
    count = 2 * mine_ref.shape[0]
    copies = load_full(both, place_ref, 0, full1_ref, sem, 0)
    copies += load_full(both, place_ref, full1_ref.shape[0] // count, full2_ref, sem, count)
    for copy in copies:
        copy.start()
    grad = pack_ref[0:2, :]
    second = DECAY * second_ref[...] + (1.0 - DECAY) * (grad * grad + 1e-30)
    ngrad_ref[...] = grad
    nsecond_ref[...] = second
    nnew_ref[...] = np_ref[...] - 0.2 * grad * lax.rsqrt(second)
    for copy in copies:
        copy.wait()
    from1 = sources_of(CHUNKS[0], full1_ref, rows)
    from2 = sources_of(CHUNKS[1], full2_ref, rows)
    for n, (k, source) in enumerate(((1, [from1[1], from2[1]]), (2, [from1[2]]))):
        squares = pack_ref[2:3, LANE0[k] : LANE0[k] + WIDTHS[k]]
        update_weight(
            k, squares, pack_ref[3:4, k : k + 1] * (1.0 / copies_of), source, weights[n],
            states[n], col_states[n], grads[n], news[n], rows_new[n], cols_new[n], refs[17:20],
        )


def update_in_kernel(rows, copies_of, place_ref, mine_ref, other_ref, pack_in_ref, pack_ref, *refs):
    weight, state, col_state, grad_ref, new_ref, row_new_ref, col_new_ref = refs[0:7]
    full_ref, sem = refs[10:12]
    run_copies(load_full((mine_ref, other_ref), place_ref, 0, full_ref, sem, 0))
    update_weight(
        0, pack_in_ref[0:1, :], pack_ref[3:4, 0:1] * (1.0 / copies_of),
        [sources_of(CHUNKS[2], full_ref, rows)[0]], weight, state, col_state, grad_ref, new_ref,
        row_new_ref, col_new_ref, refs[7:10],
    )


class Places:
    def __init__(self):
        self.seq, self.fsdp = lax.axis_size("seq"), lax.axis_size("fsdp")
        self.q = lax.axis_index("fsdp")
        self.s = lax.axis_index("seq")

    def flip(self, x, axis, bit):
        pairs = []
        for s in range(self.seq):
            for f in range(self.fsdp):
                s2, f2 = (s ^ bit, f) if axis == "seq" else (s, f ^ bit)
                pairs.append((s * self.fsdp + f, s2 * self.fsdp + f2))
        return lax.ppermute(x, AXES, pairs)


def bits_of(count):
    return [1 << k for k in range(count.bit_length() - 1)]


def tie(x, *others):
    return lax.optimization_barrier((x, *others))[0]


def gather_pieces(piece, place, after, later=None):
    found = {0: piece}
    for bit in reversed(bits_of(place.fsdp)):
        for k in list(found):
            moving = found[k]
            if bit == 1:
                moving = tie(moving, after if k == 0 or later is None else later)
            found[k | bit] = place.flip(moving, "fsdp", bit)
    return [found[k] for k in range(place.fsdp)]


def sum_over(x, place, *axes):
    for axis in axes:
        for bit in bits_of(getattr(place, axis)):
            x = x + place.flip(x, axis, bit)
    return x


def pick(x, index, axis):
    return lax.dynamic_index_in_dim(x, index, axis=axis, keepdims=False)


class Reduction:
    def __init__(self, place, keep, send):
        self.place, self.near = place, keep
        self.got = place.flip(send, "fsdp", 1)

    def halve(self, axis, side, flip_axis, bit, after):
        dims = self.near.shape
        parts = dims[:axis] + (2, dims[axis] // 2) + dims[axis + 1 :]
        near, got = self.near.reshape(parts), tie(self.got, after).reshape(parts)
        away = pick(near, 1 - side, axis).astype(F32) + pick(got, 1 - side, axis).astype(F32)
        self.near = pick(near, side, axis).astype(F32) + pick(got, side, axis).astype(F32)
        away = away.astype(BF16)
        self.got = self.place.flip(away, flip_axis, bit)
        return away

    def x(self, after):
        bit = self.place.fsdp // 2
        while bit > 1:
            away = self.halve(0, (self.place.q // bit) % 2, "fsdp", bit, after)
            bit //= 2
        return away

    def y(self, after):
        return self.halve(1, self.place.s % 2, "seq", 1, after)

    def pieces(self, after):
        total = (self.near + tie(self.got, after).astype(F32)).astype(BF16)
        return total.reshape((self.place.seq // 2, -1) + total.shape[2:])


def summed(got):
    return jnp.sum(got.astype(F32), axis=0).astype(BF16)


def exchange(place, sent):
    line = [[y + 2 * z for z in range(place.seq // 2)] for y in range(2)]
    return lax.all_to_all(sent, "seq", 0, 0, axis_index_groups=line)


def copies_for(place, part):
    return jnp.broadcast_to(part[None], (place.seq // 2,) + part.shape)


def on_device(
    tokens, input_mask, doc_lengths, cotangent, w_in, w_conv, w_out, norm_params,
    row_in, col_in, row_conv, col_conv, row_out, col_out, norm_second,
):
    place = Places()
    rows = tokens.shape[0]
    pieces = place.fsdp
    spots = jnp.stack(
        [place.q, (place.s * place.fsdp + place.q) * rows, place.s, place.seq]
    ).astype(jnp.int32)
    docs = doc_lengths.shape[0]
    ends = jnp.pad(
        jnp.cumsum(doc_lengths).astype(F32), (0, -docs % LANE), constant_values=1e9
    ).reshape(1, -1)
    live = input_mask.reshape(-1, LANE)
    weights = (w_in, w_conv, w_out)
    rows_of = [w.shape[0] for w in weights]

    tile_a, tile = 256, 512
    steps = rows // tile
    params_spec = whole(2, D + 2 * INNER)
    dma = pltpu.SemaphoreType.DMA

    out_sides = (w_out[:, : D // 2], w_out[:, D // 2 :])
    conv_out = jnp.concatenate([w_conv, *out_sides], axis=0).astype(BF16)
    hidden_a, slope_a, xhat_a, rstd_a = call(
        norm_a_kernel,
        (rows // tile_a,),
        [rows_spec(tile_a, D), params_spec],
        [rows_spec(tile_a, D)] * 3 + [rows_spec(tile_a, 1)],
        [shape((rows, D), BF16)] * 3 + [shape((rows, 1), F32)],
        us=17,
    )(tokens, tie(norm_params, conv_out))

    in_pieces = gather_pieces(w_in.astype(BF16), place, hidden_a)

    def in_call(tiles, count, before):
        at, stride = tiles

        def here_spec(width):
            return pl.BlockSpec((tile, width), lambda i: (at + stride * i, 0))

        out_shapes = [shape((rows, INNER), BF16)] * 3 + [shape((rows, 1), F32), shape((rows, 8), F32)]
        out_specs = [here_spec(INNER)] * 3 + [here_spec(1), here_spec(8)]
        if at == 0:
            out_shapes += [shape((REACH, INNER), BF16)] * 2
            out_specs += [whole(REACH, INNER)] * 2
        return call(
            functools.partial(in_kernel, pieces, tiles),
            (count,),
            [SMEM, whole(*ends.shape), here_spec(D), whole(*live.shape), params_spec]
            + [ANY] * (pieces + len(before)),
            out_specs,
            out_shapes,
            [pltpu.VMEM((D, INNER), BF16), pltpu.VMEM((tile, INNER), F32), dma((pieces,))],
            us=8,
            aliases={5 + pieces + k: k for k in range(len(before))},
        )(spots, ends, hidden_a, live, norm_params, *in_pieces, *before)

    *kept, m_first, m_last = in_call((0, steps - 1), 2, ())
    moved, slope_b, xhat_b, rstd_b, masks = in_call((1, 1), steps - 2, kept)
    conv_pieces = gather_pieces(conv_out, place, m_first, moved)

    total = place.seq * place.fsdp
    up = [(i, i + 1) for i in range(total - 1)]
    down = [(i + 1, i) for i in range(total - 1)]
    m_low, m_high = lax.ppermute(m_last, AXES, up), lax.ppermute(m_first, AXES, down)

    ext = pltpu.VMEM((rows + 2 * REACH, INNER), BF16)
    taps_wide = KERNEL_TAPS * INNER
    wide = pltpu.VMEM((taps_wide, INNER), BF16)
    shards = place.fsdp // 2

    def half_dims(chunk):
        count = spans(chunk, rows_of)[1]
        return (shards, count + -count % place.seq, SUB, LANE)

    def tile_spec(width, ahead):
        return pl.BlockSpec((tile, width), lambda i: (jnp.clip(i + ahead, 0, steps - 1), 0))

    halves = [half_dims(CHUNKS[0])] * 2 + [half_dims(CHUNKS[1])] * 2
    work = pltpu.VMEM((tile, INNER), F32)
    turned_tile = pltpu.VMEM((INNER, tile), BF16)
    hidden_c, d_conv, d_first, d_last, sums_c, turned, keep1, send1, keep2, send2 = call(
        functools.partial(conv_kernel, pieces, rows_of),
        (steps + 1,),
        [SMEM, ANY, ANY, ANY, tile_spec(8, 0), tile_spec(D, 0), tile_spec(D, -1), params_spec]
        + [ANY] * pieces,
        [tile_spec(INNER, 0)] * 2
        + [whole(REACH, INNER), whole(REACH, INNER), whole(2, INNER)]
        + [ANY] * 5,
        [
            shape((rows, INNER), BF16),
            shape((rows, INNER), BF16),
            shape((REACH, INNER), BF16),
            shape((REACH, INNER), BF16),
            shape((2, INNER), F32),
            shape((taps_wide, INNER), BF16),
        ]
        + [shape(dims, BF16) for dims in halves],
        [ext, wide, wide, pltpu.VMEM((INNER, D), BF16), pltpu.VMEM((D, INNER), BF16)]
        + [pltpu.VMEM((2, tile, taps_wide), BF16), work, work, work, turned_tile, turned_tile]
        + [pltpu.VMEM((INNER, taps_wide), F32), pltpu.VMEM((INNER, D), F32)]
        + [pltpu.VMEM((16, INNER), F32)]
        + [pltpu.VMEM((2,) + halves[0], BF16), pltpu.VMEM((2,) + halves[2], BF16)]
        + [dma((3 + 3 * pieces,))],
        us=45,
    )(
        spots, m_low, moved, m_high, masks, cotangent, cotangent, norm_params, *conv_pieces
    )
    d_low, d_high = lax.ppermute(d_last, AXES, up), lax.ppermute(d_first, AXES, down)
    first, second = Reduction(place, keep1, send1), Reduction(place, keep2, send2)
    (block_out,) = call(
        functools.partial(out_kernel, pieces),
        (steps,),
        [SMEM, rows_spec(tile, INNER), rows_spec(tile, D)] + [ANY] * pieces,
        [rows_spec(tile, D)],
        [shape((rows, D), BF16)],
        [pltpu.VMEM((INNER, D), BF16), dma((2 * pieces,))],
        us=9,
    )(spots, hidden_c, tokens, *conv_pieces)

    def back_conv(last, spots, before):
        here = steps // 2
        at = here * last

        def here_spec(width):
            return pl.BlockSpec((tile, width), lambda i: (i + at, 0))

        dims = half_dims(CHUNKS[2])
        return call(
            functools.partial(back_conv_kernel, last, w_in.shape[0]),
            (here,),
            [SMEM] + [ANY] * 4
            + [here_spec(8), here_spec(INNER), here_spec(1), here_spec(INNER), here_spec(D)]
            + [params_spec]
            + [ANY] * last,
            [rows_spec(tile, INNER), whole(2, INNER)] + [ANY] * (1 + last),
            [shape((rows // 2, INNER), BF16), shape((2, INNER), F32)]
            + ([shape(dims, BF16)] * 2 if last else [shape((INNER, D), F32)]),
            ([pltpu.VMEM((2,) + dims, BF16)] if last else [])
            + [
                ext,
                wide,
                pltpu.VMEM((tile, taps_wide), BF16),
                pltpu.VMEM((tile, INNER), F32),
                pltpu.VMEM((INNER, D), F32),
                pltpu.VMEM((16, INNER), F32),
                dma((5,)),
            ],
            us=16,
        )(
            spots, d_low, d_conv, d_high, turned, masks, xhat_b, rstd_b, slope_b, hidden_a,
            norm_params, *before,
        )

    away = (first.x(block_out), second.y(block_out))
    d_pre0, sums_b0, grad_part = back_conv(0, tie(spots, *away), ())
    away = (first.y(d_pre0), second.x(d_pre0))
    d_pre1, sums_b1, keep, send = back_conv(1, tie(spots, *away), (grad_part,))
    third = Reduction(place, keep, send)
    sent = jnp.concatenate([first.pieces(d_pre1), second.pieces(d_pre1)], axis=1)
    got = exchange(place, sent)
    away = (sent, third.x(sent))
    input_grad, sums_a = call(
        functools.partial(back_a_kernel, pieces, steps // 2),
        (steps,),
        [SMEM]
        + [
            pl.BlockSpec((tile, INNER), lambda i: (jnp.minimum(i, steps // 2 - 1), 0)),
            pl.BlockSpec((tile, INNER), lambda i: (jnp.maximum(i - steps // 2, 0), 0)),
        ]
        + [rows_spec(tile, D), rows_spec(tile, 1), rows_spec(tile, D), rows_spec(tile, D)]
        + [params_spec]
        + [ANY] * pieces,
        [rows_spec(tile, D), whole(2, D)],
        [shape((rows, D), F32), shape((2, D), F32)],
        [
            pltpu.VMEM((D, INNER), BF16),
            pltpu.VMEM((INNER, D), BF16),
            pltpu.VMEM((tile, D), F32),
            pltpu.VMEM((16, D), F32),
            dma((pieces,)),
        ],
        us=17,
    )(
        tie(spots, *away), d_pre0, d_pre1, xhat_a, rstd_a, slope_a, cotangent, norm_params, *in_pieces
    )

    part = summed(tie(got, input_grad))
    sent = copies_for(place, part)
    mine = exchange(place, sent)
    away = third.y(sent)
    other = place.flip(mine, "seq", 1)
    sent = third.pieces(away)
    got = exchange(place, sent)
    mine_in = exchange(place, copies_for(place, summed(got)))
    other_in = place.flip(mine_in, "seq", 1)

    row_states, col_states = (row_in, row_conv, row_out), (col_in, col_conv, col_out)
    row_specs = [whole(*r.shape) for r in row_states]
    col_specs = [whole(*c.shape) for c in col_states]
    cols_all = D + 2 * INNER
    pack_spec = whole(4, cols_all)
    fulls = [pltpu.VMEM(half_dims(c)[1:], BF16) for c in CHUNKS]
    sums = (sums_a, sums_b0, sums_b1, sums_c)
    (pack,) = call(
        functools.partial(pack_kernel, rows_of, [half_dims(c)[1] // place.seq for c in CHUNKS]),
        (1,),
        [SMEM, whole(*part.shape)] + row_specs + [whole(*x.shape) for x in sums],
        [pack_spec],
        [shape((4, cols_all), F32)],
        [pltpu.VMEM((cols_all // LANE + 1, SUB, LANE), F32)],
        us=2,
    )(tie(spots, away), part, *row_states, *sums)
    pack = sum_over(pack, place, "fsdp", "seq")

    def update_scratch(weights):
        lines = max(w.shape[0] + -w.shape[0] % LANE for w in weights)
        return [pltpu.VMEM((8, lines), F32)] + [pltpu.VMEM((lines, LANE), F32)] * 2

    weight_specs = [whole(*w.shape) for w in weights]
    results = call(
        functools.partial(update_kernel, rows_of, place.seq),
        (1,),
        [SMEM, ANY, ANY, pack_spec, params_spec, params_spec]
        + weight_specs[1:]
        + row_specs[1:]
        + col_specs[1:],
        weight_specs[1:] * 2 + row_specs[1:] + col_specs[1:] + [params_spec] * 3,
        [shape(w.shape, F32) for w in weights[1:]] * 2
        + [shape(r.shape, F32) for r in row_states[1:] + col_states[1:]]
        + [shape((2, cols_all), F32)] * 3,
        update_scratch(weights[1:]) + fulls[:2] + [dma((2 * place.seq,))],
        us=8,
    )(
        spots, mine, other, pack, norm_params, norm_second, *weights[1:], *row_states[1:],
        *col_states[1:],
    )
    grad_conv, grad_out, new_conv, new_out, row_conv_new, row_out_new, col_conv_new, col_out_new = (
        results[:8]
    )
    (pack_in,) = call(
        functools.partial(pack_in_kernel, rows_of),
        (1,),
        [SMEM, ANY, ANY],
        [whole(8, INNER)],
        [shape((8, INNER), F32)],
        [fulls[2], dma((place.seq,))],
        us=2,
    )(spots, mine_in, other_in)
    pack_in = sum_over(pack_in, place, "fsdp")
    grad_in, new_in, row_in_new, col_in_new = call(
        functools.partial(update_in_kernel, rows_of, place.seq),
        (1,),
        [SMEM, ANY, ANY, whole(8, INNER), pack_spec]
        + [weight_specs[0], row_specs[0], col_specs[0]],
        [weight_specs[0]] * 2 + [row_specs[0], col_specs[0]],
        [shape(w_in.shape, F32)] * 2 + [shape(row_in.shape, F32), shape(col_in.shape, F32)],
        update_scratch(weights[:1]) + [fulls[2], dma((place.seq,))],
        us=4,
    )(spots, mine_in, other_in, pack_in, pack, w_in, row_in, col_in)
    return (
        block_out,
        input_grad,
        grad_in,
        grad_conv,
        grad_out,
        new_in,
        new_conv,
        new_out,
        row_in_new,
        col_in_new,
        row_conv_new,
        col_conv_new,
        row_out_new,
        col_out_new,
        *results[8:11],
    )


def solution(mesh):
    both, rows = P(AXES, None), P("fsdp", None)
    in_specs = (
        both, P(AXES), P(), both, rows, rows, rows, P(),
        P("fsdp"), P(), P("fsdp"), P(), P("fsdp"), P(), P(),
    )
    out_specs = (
        both, both, rows, rows, rows, rows, rows, rows,
        P("fsdp"), P(), P("fsdp"), P(), P("fsdp"), P(), P(), P(), P(),
    )
    return jax.shard_map(
        on_device, mesh=mesh, in_specs=in_specs, out_specs=out_specs, check_vma=False
    )
```

```python
import functools
import math

import jax
import jax.numpy as jnp
from jax import lax
from jax.experimental import pallas as pl
from jax.experimental.pallas import tpu as pltpu
from jax.sharding import PartitionSpec as P

D = 1280
INNER = 640
KERNEL_TAPS = 5
DILATION_STEP = 128
STEP = 10
EPSILON = 1e-05
DECAY = 1.0 - STEP ** (-0.8)

REACH = (KERNEL_TAPS - 1) // 2 * DILATION_STEP
MID = (KERNEL_TAPS - 1) // 2
F32 = jnp.float32
BF16 = jnp.bfloat16
SUB, LANE = 16, 128
AXES = ("seq", "fsdp")
NT = (((1,), (1,)), ((), ()))
TN = (((0,), (0,)), ((), ()))
NN = (((1,), (0,)), ((), ()))
VMEM_LIMIT = 58 * 1024 * 1024


def call(kernel, grid, in_specs, out_specs, out_shape, scratch=(), us=1.0, aliases=None):
    params = pltpu.CompilerParams(
        vmem_limit_bytes=VMEM_LIMIT, dimension_semantics=("arbitrary",) * len(grid)
    )
    return pl.pallas_call(
        kernel,
        grid=grid,
        in_specs=in_specs,
        out_specs=out_specs,
        out_shape=out_shape,
        scratch_shapes=list(scratch),
        compiler_params=params,
        input_output_aliases=aliases or {},
        cost_estimate=pl.CostEstimate(
                flops=int(us * 1.1e9), bytes_accessed=int(us * 3.4e6), transcendentals=0
        ),
    )


def shape(dims, dtype):
    return jax.ShapeDtypeStruct(dims, dtype)


def rows_spec(tile, width):
    return pl.BlockSpec((tile, width), lambda i: (i, 0))


def whole(*dims):
    return pl.BlockSpec(dims, lambda *_: (0,) * len(dims))


ANY = pl.BlockSpec(memory_space=pl.ANY)
SMEM = pl.BlockSpec(memory_space=pltpu.SMEM)


ERFC_P = 0.47 / math.sqrt(2.0)
ERFC_C = (
    0.12357219400743558,
    0.1999878668208835,
    -0.08033356004356296,
    0.3660253986657854,
    -0.1092519747040215,
)
LOG2E = 1.4426950408889634


def gelu_and_slope(y):
    t = pltpu.reciprocal(1.0 + ERFC_P * jnp.abs(y), approx=True)
    bell = jnp.exp2(y * y * (-0.5 * LOG2E))
    poly = ERFC_C[4] * t + ERFC_C[3]
    for c in ERFC_C[2::-1]:
        poly = poly * t + c
    tail = poly * t * bell
    cdf = jnp.where(y > 0.0, 1.0 - tail, tail)
    return y * cdf, cdf + y * (bell * (1.0 / math.sqrt(2.0 * math.pi)))


def lane_blocks(width):
    return [slice(k, k + LANE) for k in range(0, width, LANE)]


def row_stats(ref, rows):
    width = ref.shape[-1]
    blocks = lane_blocks(width)
    total = ref[rows, blocks[0]].astype(F32)
    for b in blocks[1:]:
        total = total + ref[rows, b].astype(F32)
    mean = jnp.sum(total, axis=-1, keepdims=True) * (1.0 / width)
    square = None
    for b in blocks:
        centered = ref[rows, b].astype(F32) - mean
        square = centered * centered if square is None else square + centered * centered
    variance = jnp.sum(square, axis=-1, keepdims=True) * (1.0 / width)
    return mean, lax.rsqrt(variance + EPSILON)


def fold(values):
    total = values[0:8]
    for k in range(8, values.shape[0], 8):
        total = total + values[k : k + 8]
    return total


def in_stages(count, stages, between=()):
    chunks = [slice(k, k + CHUNK) for k in range(0, count, CHUNK)]
    kept, rounds = {}, len(chunks) + len(stages) - 1
    for t in range(rounds):
        for n, stage in enumerate(stages):
            if 0 <= t - n < len(chunks):
                kept[n, t - n] = stage(chunks[t - n], kept.get((n - 1, t - n)))
        for work in between[t * len(between) // rounds : (t + 1) * len(between) // rounds]:
            work()


def halves_of(count):
    return (slice(0, count // 2), slice(count // 2, count))


def row_means(sums, width):
    return [jnp.sum(x, axis=-1, keepdims=True) * (1.0 / width) for x in sums]


def norm_back(rows, dxhat_ref, xhat_ref, means, put):
    mean_d, mean_dx, rstd = means
    for b in lane_blocks(dxhat_ref.shape[-1]):
        xhat = xhat_ref[rows, b].astype(F32)
        put(b, (dxhat_ref[rows, b] - mean_d - xhat * mean_dx) * rstd)


def add_terms(acc_ref, b, dy, xhat):
    acc_ref[0:8, b] += fold(dy * xhat)
    acc_ref[8:16, b] += fold(dy)


def open_sums(acc_ref):
    @pl.when(pl.program_id(0) == 0)
    def _():
        acc_ref[...] = jnp.zeros_like(acc_ref)


def close_sums(out_ref, acc_ref):
    @pl.when(pl.program_id(0) == pl.num_programs(0) - 1)
    def _():
        out_ref[0:1, :] = jnp.sum(acc_ref[0:8, :], axis=0, keepdims=True)
        out_ref[1:2, :] = jnp.sum(acc_ref[8:16, :], axis=0, keepdims=True)


def run_copies(copies):
    for copy in copies:
        copy.start()
    for copy in copies:
        copy.wait()


def piece_copies(pieces, full_ref, me, sem, first=0):
    each = full_ref.shape[0] // len(pieces)
    return [
        pltpu.make_async_copy(
            piece.at[0:each, :],
            full_ref.at[pl.ds(pl.multiple_of((me ^ k) * each, SUB), each), :],
            sem.at[first + k],
        )
        for k, piece in enumerate(pieces)
    ]


def out_copies(pieces, full_ref, me, sem, first=0):
    each, width = full_ref.shape[0] // len(pieces), full_ref.shape[1] // 2
    copies = []
    for k, piece in enumerate(pieces):
        rows = pl.ds(pl.multiple_of((me ^ k) * each, SUB), each)
        for side in range(2):
            at = piece.shape[0] - (2 - side) * each
            copies.append(
                pltpu.make_async_copy(
                    piece.at[at : at + each, :],
                    full_ref.at[rows, side * width : (side + 1) * width],
                    sem.at[first + 2 * k + side],
                )
            )
    return copies


def column(row):
    return jnp.transpose(jnp.broadcast_to(row, (LANE, LANE)))


CHUNK = 64


def norm_a_kernel(tok_ref, np_ref, hid_ref, slope_ref, xhat_ref, rstd_ref):
    def stats(rows, _):
        mean, rstd = row_stats(tok_ref, rows)
        rstd_ref[rows, :] = rstd
        return mean, rstd

    def work(rows, kept):
        mean, rstd = kept
        for b in lane_blocks(D):
            xhat = (tok_ref[rows, b].astype(F32) - mean) * rstd
            hidden, slope = gelu_and_slope(xhat * np_ref[0:1, b] + np_ref[1:2, b])
            hid_ref[rows, b] = hidden.astype(BF16)
            slope_ref[rows, b] = slope.astype(BF16)
            xhat_ref[rows, b] = xhat.astype(BF16)

    in_stages(tok_ref.shape[0], [stats, work])


def in_kernel(pieces, tiles, place_ref, ends_ref, hid_ref, live_ref, np_ref, *refs):
    piece_refs = refs[:pieces]
    edges = tiles[0] == 0
    outs = refs[-(10 if edges else 8) :]
    mov_ref, slope_ref, xhat_ref, rstd_ref, mask_ref = outs[:5]
    w_ref, pre_ref, sem = outs[-3:]
    step = pl.program_id(0)
    tile = hid_ref.shape[0]

    @pl.when(step == 0)
    def _():
        run_copies(piece_copies(piece_refs, w_ref, place_ref[0], sem))

    for half in halves_of(tile):
        pre_ref[half, :] = lax.dot_general(
            hid_ref[half, :], w_ref[...], NN, preferred_element_type=F32
        )

    at_tile = tiles[0] + step * tiles[1]
    first = place_ref[1] + at_tile * tile
    ends = ends_ref[...]
    lanes = lax.broadcasted_iota(jnp.int32, (LANE, 8), 1)
    offsets = ((lanes - MID) * DILATION_STEP).astype(F32)
    for k in range(tile // LANE):
        at = (first + k * LANE + lax.broadcasted_iota(jnp.int32, (LANE, 1), 0)).astype(F32)
        begin = jnp.max(jnp.where(ends <= at, ends, 0.0), axis=1, keepdims=True)
        end = jnp.min(jnp.where(ends > at, ends, 1e9), axis=1, keepdims=True)
        there = at + offsets
        same = jnp.where((there >= begin) & (there < end), 1.0, 0.0)
        live = column(live_ref[pl.ds(at_tile * (tile // LANE) + k, 1), :].astype(F32))
        mask_ref[k * LANE : (k + 1) * LANE, :] = jnp.where(lanes == MID, live[:, 0:8], same)

    def stats(rows, _):
        mean, rstd = row_stats(pre_ref, rows)
        rstd_ref[rows, :] = rstd
        return mean, rstd

    def work(rows, kept):
        mean, rstd = kept
        live = mask_ref[rows, MID : MID + 1]
        for b in lane_blocks(INNER):
            gains = slice(D + b.start, D + b.stop)
            xhat = (pre_ref[rows, b] - mean) * rstd
            hidden, slope = gelu_and_slope(xhat * np_ref[0:1, gains] + np_ref[1:2, gains])
            mov_ref[rows, b] = (hidden * live).astype(BF16)
            slope_ref[rows, b] = slope.astype(BF16)
            xhat_ref[rows, b] = xhat.astype(BF16)

    in_stages(tile, [stats, work])
    if edges:
        first_ref, last_ref = outs[5:7]

        @pl.when(step == 0)
        def _():
            first_ref[...] = mov_ref[0:REACH, :]

        @pl.when(step == 1)
        def _():
            last_ref[...] = mov_ref[tile - REACH :, :]


def load_window(low, mid, high, ext_ref, sem):
    rows = mid.shape[0]
    return [
        pltpu.make_async_copy(low, ext_ref.at[0:REACH, :], sem.at[0]),
        pltpu.make_async_copy(mid, ext_ref.at[REACH : REACH + rows, :], sem.at[1]),
        pltpu.make_async_copy(high, ext_ref.at[REACH + rows : 2 * REACH + rows, :], sem.at[2]),
    ]


def fill_taps(taps_ref, ext_ref, mask_ref, start):
    tile = taps_ref.shape[0]
    for j in range(KERNEL_TAPS):
        rows = pl.ds(pl.multiple_of(start + j * DILATION_STEP, DILATION_STEP), tile)
        picked = ext_ref[rows, :]
        if j != MID:
            picked = picked * mask_ref[:, j : j + 1].astype(BF16)
        taps_ref[:, j * INNER : (j + 1) * INNER] = picked


def conv_kernel(
    pieces, rows_of, place_ref, low_ref, mov_ref, high_ref, mask_ref, cot_ref, before_ref, np_ref, *refs
):
    piece_refs = refs[:pieces]
    hid_ref, dconv_ref, first_ref, last_ref, sums_ref, turned_ref = refs[pieces : pieces + 6]
    outs = refs[pieces + 6 : pieces + 10]
    ext_ref, wc_ref, wct_ref, wo_ref, wt_ref, taps_ref, pre_ref, dh_ref, xhat_ref = refs[
        pieces + 10 : pieces + 19
    ]
    dt_ref, ht_ref, gc_ref, go_ref, acc_ref, stage1_ref, stage2_ref, sem = refs[pieces + 19 :]
    step, steps = pl.program_id(0), pl.num_programs(0) - 1
    tile = taps_ref.shape[1]
    slot = lax.rem(step, 2)

    @pl.when(step == 0)
    def _():
        me = place_ref[0]
        outs = out_copies(piece_refs, wo_ref, me, sem, 3)
        rest = load_window(low_ref, mov_ref, high_ref, ext_ref, sem)
        rest += piece_copies(piece_refs, wc_ref, me, sem, 3 + 2 * pieces)
        for copy in outs + rest:
            copy.start()
        for ref in (acc_ref, gc_ref, go_ref, dt_ref, ht_ref):
            ref[...] = jnp.zeros_like(ref)
        taps_ref[1] = jnp.zeros_like(taps_ref[1])
        for copy in outs:
            copy.wait()
        for k in range(0, D, 256):
            wt_ref[k : k + 256, :] = jnp.transpose(wo_ref[:, k : k + 256])
        for copy in rest:
            copy.wait()

    def grad_conv(cols):
        def work():
            gc_ref[:, cols] += lax.dot_general(
                dt_ref[...], taps_ref[1 - slot, :, cols], NN, preferred_element_type=F32
            )

        return work

    def grad_out(cols):
        def work():
            go_ref[:, cols] += lax.dot_general(
                ht_ref[...], before_ref[:, cols], NN, preferred_element_type=F32
            )

        return work

    taps_wide = KERNEL_TAPS * INNER
    products = [grad_conv(slice(k, min(k + 768, taps_wide))) for k in range(0, taps_wide, 768)]
    products += [grad_out(slice(k, min(k + 768, D))) for k in range(0, D, 768)]

    @pl.when(step < steps)
    def _():
        fill_taps(taps_ref.at[slot], ext_ref, mask_ref, step * tile)
        pre_ref[...] = lax.dot_general(
            taps_ref[slot], wc_ref[...], NN, preferred_element_type=F32
        )
        dh_ref[...] = lax.dot_general(cot_ref[...], wt_ref[...], NN, preferred_element_type=F32)
        for n in range(2):
            tap = jnp.minimum(2 * step + n, KERNEL_TAPS - 1)
            source = wc_ref[pl.ds(pl.multiple_of(tap * INNER, SUB), INNER), :]
            target = pl.multiple_of((KERNEL_TAPS - 1 - tap) * INNER, SUB)
            wct_ref[pl.ds(target, INNER), :] = jnp.transpose(source)

        def stats(rows, _):
            return row_stats(pre_ref, rows)

        def work(rows, kept):
            mean, rstd = kept
            sums = [0.0, 0.0]
            for b in lane_blocks(INNER):
                gains = slice(D + INNER + b.start, D + INNER + b.stop)
                gain = np_ref[0:1, gains]
                xhat = (pre_ref[rows, b] - mean) * rstd
                hidden, slope = gelu_and_slope(xhat * gain + np_ref[1:2, gains])
                hid_ref[rows, b] = hidden.astype(BF16)
                dy = dh_ref[rows, b] * slope
                add_terms(acc_ref, b, dy, xhat)
                dxhat = dy * gain
                xhat_ref[rows, b] = xhat
                dh_ref[rows, b] = dxhat
                sums = [sums[0] + dxhat, sums[1] + dxhat * xhat]
            return row_means(sums, INNER) + [rstd]

        def finish(rows, means):
            def put(b, value):
                dconv_ref[rows, b] = value.astype(BF16)

            norm_back(rows, dh_ref, xhat_ref, means, put)

        in_stages(tile, [stats, work, finish], products)
        dt_ref[...] = jnp.transpose(dconv_ref[...])
        ht_ref[...] = jnp.transpose(hid_ref[...])

    @pl.when(step == 0)
    def _():
        first_ref[...] = dconv_ref[0:REACH, :]

    @pl.when(step == steps - 1)
    def _():
        last_ref[...] = dconv_ref[tile - REACH :, :]

    @pl.when(step == steps)
    def _():
        copy = pltpu.make_async_copy(wct_ref, turned_ref, sem.at[4])
        copy.start()
        for work in products:
            work()
        core = lax.rem(place_ref[0], 2)
        _, rows_conv, rows_out = rows_of
        stage_turned(stage1_ref, core, gc_ref, rows_conv, 0, slice(0, CUT // LANE))
        first_tiles = rows_conv // SUB * (CUT // LANE)
        stage_plain(stage1_ref, core, go_ref, rows_out, first_tiles)
        copies = stage_copies(stage1_ref, outs[0], outs[1], spans(CHUNKS[0], rows_of)[1], sem, 0)
        for each in copies:
            each.start()
        stage_turned(stage2_ref, core, gc_ref, rows_conv, 0, slice(CUT // LANE, INNER // LANE))
        more = stage_copies(stage2_ref, outs[2], outs[3], spans(CHUNKS[1], rows_of)[1], sem, 2)
        for each in more:
            each.start()
        for each in copies + more + [copy]:
            each.wait()
        sums_ref[0:1, :] = jnp.sum(acc_ref[0:8, :], axis=0, keepdims=True)
        sums_ref[1:2, :] = jnp.sum(acc_ref[8:16, :], axis=0, keepdims=True)


def stage_tiles(stage_ref, core, first_row, rows_each, base, block0, blocks, value):
    for g in range(value.shape[0] // SUB):
        row = first_row + g * SUB
        owner, inside = row // rows_each, row % rows_each // SUB
        side = core ^ (owner % 2)
        for b in range(value.shape[1] // LANE):
            tile = value[g * SUB : (g + 1) * SUB, b * LANE : (b + 1) * LANE]
            at = base + inside * blocks + block0 + b
            stage_ref[side, owner // 2, at] = tile.astype(BF16)


def stage_plain(stage_ref, core, grad_ref, rows_each, base):
    blocks = grad_ref.shape[1] // LANE
    for row in range(0, grad_ref.shape[0], SUB):
        part = grad_ref[row : row + SUB, :]
        stage_tiles(stage_ref, core, row, rows_each, base, 0, blocks, part)


def stage_turned(stage_ref, core, turned_ref, rows_each, base, blocks):
    count = blocks.stop - blocks.start
    for row in range(0, turned_ref.shape[1], LANE):
        for b in range(count):
            at = (blocks.start + b) * LANE
            part = jnp.transpose(turned_ref[at : at + LANE, row : row + LANE])
            stage_tiles(stage_ref, core, row, rows_each, base, b, count, part)


def stage_copies(stage_ref, keep_ref, send_ref, used, sem, first):
    count = stage_ref.shape[2]
    if used < count:
        dims = stage_ref.shape[:2] + (count - used, SUB, LANE)
        stage_ref[:, :, used:] = jnp.zeros(dims, BF16)
    return [
        pltpu.make_async_copy(stage_ref.at[n], ref, sem.at[first + n])
        for n, ref in enumerate((keep_ref, send_ref))
    ]


def back_conv_kernel(
    last, rows_in, place_ref, low_ref, d_ref, high_ref, turned_ref, mask_ref, xhat_ref, rstd_ref, slope_ref, hid_ref, np_ref, *refs
):
    if last:
        before_ref, dpre_ref, sums_ref, keep_ref, send_ref, stage_ref = refs[:6]
    else:
        dpre_ref, sums_ref, part_ref = refs[:3]
    ext_ref, wt_ref, taps_ref, dmov_ref, grad_ref, acc_ref, sem = refs[-7:]
    step, steps = pl.program_id(0), pl.num_programs(0)
    tile = taps_ref.shape[0]
    open_sums(acc_ref)

    @pl.when(step == 0)
    def _():
        copies = load_window(low_ref, d_ref, high_ref, ext_ref, sem)
        copies.append(pltpu.make_async_copy(turned_ref, wt_ref, sem.at[3]))
        if last:
            copies.append(pltpu.make_async_copy(before_ref, grad_ref, sem.at[4]))
        for copy in copies:
            copy.start()
        if not last:
            grad_ref[...] = jnp.zeros_like(grad_ref)
        for copy in copies:
            copy.wait()

    fill_taps(taps_ref, ext_ref, mask_ref, (steps * last + step) * tile)
    for half in halves_of(tile):
        dmov_ref[half, :] = lax.dot_general(
            taps_ref[half, :], wt_ref[...], NN, preferred_element_type=F32
        )

    def work(rows, _):
        live = mask_ref[rows, MID : MID + 1]
        sums = [0.0, 0.0]
        for b in lane_blocks(INNER):
            xhat = xhat_ref[rows, b].astype(F32)
            dy = dmov_ref[rows, b] * live * slope_ref[rows, b].astype(F32)
            add_terms(acc_ref, b, dy, xhat)
            dxhat = dy * np_ref[0:1, D + b.start : D + b.stop]
            dmov_ref[rows, b] = dxhat
            sums = [sums[0] + dxhat, sums[1] + dxhat * xhat]
        return row_means(sums, INNER) + [rstd_ref[rows, :]]

    def finish(rows, means):
        def put(b, value):
            dpre_ref[rows, b] = value.astype(BF16)

        norm_back(rows, dmov_ref, xhat_ref, means, put)

    in_stages(tile, [work, finish])
    close_sums(sums_ref, acc_ref)
    grad_ref[...] += lax.dot_general(dpre_ref[...], hid_ref[...], TN, preferred_element_type=F32)

    @pl.when(step == steps - 1)
    def _():
        if last:
            all_blocks = slice(0, INNER // LANE)
            stage_turned(stage_ref, lax.rem(place_ref[0], 2), grad_ref, rows_in, 0, all_blocks)
            used = rows_in // SUB * (INNER // LANE)
            run_copies(stage_copies(stage_ref, keep_ref, send_ref, used, sem, 0))
        else:
            run_copies([pltpu.make_async_copy(grad_ref, part_ref, sem.at[0])])


def back_a_kernel(pieces, half, place_ref, dpre0_ref, dpre1_ref, xhat_ref, rstd_ref, slope_ref, cot_ref, np_ref, *refs):
    piece_refs = refs[:pieces]
    grad_ref, sums_ref, w_ref, wt_ref, dh_ref, acc_ref, sem = refs[-7:]
    open_sums(acc_ref)

    @pl.when(pl.program_id(0) == 0)
    def _():
        run_copies(piece_copies(piece_refs, w_ref, place_ref[0], sem))
        for k in range(0, D, 256):
            wt_ref[:, k : k + 256] = jnp.transpose(w_ref[k : k + 256, :])

    second = (jnp.zeros((1, 1), jnp.int32) + pl.program_id(0)) >= half
    d_pre = jnp.where(second, dpre1_ref[...], dpre0_ref[...])
    dh_ref[...] = lax.dot_general(d_pre, wt_ref[...], NN, preferred_element_type=F32)

    def work(rows, _):
        sums = [0.0, 0.0]
        for b in lane_blocks(D):
            xhat = xhat_ref[rows, b].astype(F32)
            dy = dh_ref[rows, b] * slope_ref[rows, b].astype(F32)
            add_terms(acc_ref, b, dy, xhat)
            dxhat = dy * np_ref[0:1, b]
            dh_ref[rows, b] = dxhat
            sums = [sums[0] + dxhat, sums[1] + dxhat * xhat]
        return row_means(sums, D) + [rstd_ref[rows, :]]

    def finish(rows, means):
        def put(b, value):
            grad_ref[rows, b] = cot_ref[rows, b].astype(F32) + value

        norm_back(rows, dh_ref, xhat_ref, means, put)

    in_stages(dpre0_ref.shape[0], [work, finish])
    close_sums(sums_ref, acc_ref)


def out_kernel(pieces, place_ref, hid_ref, tok_ref, *refs):
    piece_refs = refs[:pieces]
    out_ref, w_ref, sem = refs[pieces:]

    @pl.when(pl.program_id(0) == 0)
    def _():
        run_copies(out_copies(piece_refs, w_ref, place_ref[0], sem))

    branch = lax.dot_general(hid_ref[...], w_ref[...], NN, preferred_element_type=F32)
    out_ref[...] = (tok_ref[...].astype(F32) + branch).astype(BF16)


WIDTHS = (INNER, INNER, D)
LANE0 = (0, INNER, 2 * INNER)
CUT = 2 * LANE
CHUNKS = (((1, 0, CUT), (2, 0, D)), ((1, CUT, INNER - CUT),), ((0, 0, INNER),))


def spans(chunk, rows):
    found, first = [], 0
    for weight, col, cols in chunk:
        tiles = rows[weight] // SUB * (cols // LANE)
        found.append((weight, col // LANE, cols // LANE, first, tiles))
        first += tiles
    return found, first


def column_sums(pack_ref, row, ref, chunk, rows):
    for weight, block0, blocks, first, tiles in spans(chunk, rows)[0]:

        def body(g, carry, first=first, blocks=blocks):
            new = []
            for b in range(blocks):
                value = ref[first + g * blocks + b].astype(F32)
                new.append(carry[b] + fold(value * value + 1e-30))
            return tuple(new)

        zero = tuple(jnp.zeros((8, LANE), F32) for _ in range(blocks))
        cols = lax.fori_loop(0, tiles // blocks, body, zero, unroll=5)
        for b in range(blocks):
            lane = LANE0[weight] + (block0 + b) * LANE
            pack_ref[row : row + 1, lane : lane + LANE] = jnp.sum(cols[b], axis=0, keepdims=True)


def load_full(refs, place_ref, first, full_ref, sem, at):
    pieces = refs[0].shape[0]
    each = full_ref.shape[0] // (2 * pieces)
    y = place_ref[2] % 2
    copies = []
    for n, (ref, side) in enumerate(zip(refs, (y, 1 - y))):
        for p in range(pieces):
            target = full_ref.at[pl.ds((side * pieces + p) * each, each)]
            source = ref.at[p, first : first + each]
            copies.append(pltpu.make_async_copy(source, target, sem.at[at + n * pieces + p]))
    return copies


def pack_kernel(rows, pieces, place_ref, part_ref, *refs):
    states, sums, (pack_ref, acc_ref) = refs[0:3], refs[3:7], refs[7:9]
    pack_ref[...] = jnp.zeros_like(pack_ref)
    lanes_of = ((0, D), (D, D + INNER), (D, D + INNER), (D + INNER, D + 2 * INNER))
    for part, (lane0, lane1) in zip(sums, lanes_of):
        pack_ref[0:2, lane0:lane1] += part[...]
    lanes = lax.broadcasted_iota(jnp.int32, (1, LANE), 1)
    for k in range(3):
        total = jnp.sum(states[k][...].reshape(1, -1), axis=1, keepdims=True)
        pack_ref[3:4, 0:LANE] += jnp.where(lanes == k, total, 0.0)
    acc_ref[...] = jnp.zeros_like(acc_ref)
    spare = acc_ref.shape[0] - 1
    outer = place_ref[3] // 2
    piece = place_ref[2] % 2 * outer + place_ref[2] // 2
    at = 0
    for chunk, each in zip(CHUNKS[:2], pieces):
        found, _ = spans(chunk, rows)
        start = piece * each

        def body(k, carry, found=found, start=start, at=at):
            n = start + k
            slot = spare
            for weight, block0, blocks, first, tiles in found:
                here = LANE0[weight] // LANE + block0 + lax.rem(jnp.maximum(n - first, 0), blocks)
                slot = jnp.where((n >= first) & (n < first + tiles), here, slot)
            value = part_ref[at + k].astype(F32)
            acc_ref[slot] += value * value + 1e-30
            return carry

        lax.fori_loop(0, each, body, 0, unroll=2)
        at += each
    for slot in range(spare):
        pack_ref[2:3, slot * LANE : (slot + 1) * LANE] = jnp.sum(acc_ref[slot], axis=0, keepdims=True)


def pack_in_kernel(rows, place_ref, mine_ref, other_ref, pack_ref, full_ref, sem):
    run_copies(load_full((mine_ref, other_ref), place_ref, 0, full_ref, sem, 0))
    column_sums(pack_ref, 0, full_ref, CHUNKS[2], rows)


def update_weight(
    k, squares, states_sum, source, weight, state, col_state, grad_ref, new, row_new_ref, col_new_ref, scratch
):
    line_ref, state_ref, new_ref = scratch
    width, fan, rows_here = WIDTHS[k], (D, KERNEL_TAPS * INNER, INNER)[k], weight.shape[0]
    col_new = DECAY * col_state[...].reshape(1, -1) + (1.0 - DECAY) * (squares * (1.0 / fan))
    col_new_ref[...] = col_new.reshape(-1)
    total = DECAY * states_sum
    total = total + (1.0 - DECAY) * (1.0 / width) * jnp.sum(squares, axis=1, keepdims=True)
    scaled = col_new / (total * (1.0 / fan))
    rate = 0.5 / fan**0.5
    line_ref[0:1, 0:rows_here] = state[...].reshape(1, -1)
    whole_rows = rows_here + -rows_here % LANE
    for c in range(0, whole_rows, LANE):
        state_ref[c : c + LANE, :] = column(line_ref[0:1, c : c + LANE])

    def body(g, carry):
        rows = pl.ds(pl.multiple_of(g * SUB, SUB), SUB)
        square = 0.0
        for ref, block0, blocks, first in source:
            for b in range(blocks):
                value = ref[first + g * blocks + b].astype(F32)
                grad_ref[rows, (block0 + b) * LANE : (block0 + b + 1) * LANE] = value
                square = square + (value * value + 1e-30)
        mean = jnp.sum(square, axis=1, keepdims=True) * (1.0 / width)
        row_new = DECAY * state_ref[rows, :] + (1.0 - DECAY) * mean
        new_ref[rows, :] = row_new
        for ref, block0, blocks, first in source:
            for b in range(blocks):
                lanes = slice((block0 + b) * LANE, (block0 + b + 1) * LANE)
                value = ref[first + g * blocks + b].astype(F32)
                step = value * lax.rsqrt(row_new * scaled[:, lanes])
                new[rows, lanes] = weight[rows, lanes] - rate * step
        return carry

    lax.fori_loop(0, rows_here // SUB, body, 0, unroll=5)
    for c in range(0, whole_rows, LANE):
        line_ref[0:1, c : c + LANE] = jnp.transpose(new_ref[c : c + LANE, :])[0:1, :]
    row_new_ref[...] = line_ref[0:1, 0:rows_here].reshape(-1)


def sources_of(chunk, ref, rows):
    return {w: (ref, block0, blocks, first) for w, block0, blocks, first, _ in spans(chunk, rows)[0]}


def update_kernel(rows, copies_of, place_ref, mine_ref, other_ref, pack_ref, np_ref, second_ref, *refs):
    weights, states, col_states = refs[0:2], refs[2:4], refs[4:6]
    grads, news, rows_new, cols_new = refs[6:8], refs[8:10], refs[10:12], refs[12:14]
    ngrad_ref, nsecond_ref, nnew_ref = refs[14:17]
    full1_ref, full2_ref, sem = refs[20:23]
    both = (mine_ref, other_ref)
    count = 2 * mine_ref.shape[0]
    copies = load_full(both, place_ref, 0, full1_ref, sem, 0)
    copies += load_full(both, place_ref, full1_ref.shape[0] // count, full2_ref, sem, count)
    for copy in copies:
        copy.start()
    grad = pack_ref[0:2, :]
    second = DECAY * second_ref[...] + (1.0 - DECAY) * (grad * grad + 1e-30)
    ngrad_ref[...] = grad
    nsecond_ref[...] = second
    nnew_ref[...] = np_ref[...] - 0.2 * grad * lax.rsqrt(second)
    for copy in copies:
        copy.wait()
    from1 = sources_of(CHUNKS[0], full1_ref, rows)
    from2 = sources_of(CHUNKS[1], full2_ref, rows)
    for n, (k, source) in enumerate(((1, [from1[1], from2[1]]), (2, [from1[2]]))):
        squares = pack_ref[2:3, LANE0[k] : LANE0[k] + WIDTHS[k]]
        update_weight(
            k, squares, pack_ref[3:4, k : k + 1] * (1.0 / copies_of), source, weights[n],
            states[n], col_states[n], grads[n], news[n], rows_new[n], cols_new[n], refs[17:20],
        )


def update_in_kernel(rows, copies_of, place_ref, mine_ref, other_ref, pack_in_ref, pack_ref, *refs):
    weight, state, col_state, grad_ref, new_ref, row_new_ref, col_new_ref = refs[0:7]
    full_ref, sem = refs[10:12]
    run_copies(load_full((mine_ref, other_ref), place_ref, 0, full_ref, sem, 0))
    update_weight(
        0, pack_in_ref[0:1, :], pack_ref[3:4, 0:1] * (1.0 / copies_of),
        [sources_of(CHUNKS[2], full_ref, rows)[0]], weight, state, col_state, grad_ref, new_ref,
        row_new_ref, col_new_ref, refs[7:10],
    )


class Places:
    def __init__(self):
        self.seq, self.fsdp = lax.axis_size("seq"), lax.axis_size("fsdp")
        self.q = lax.axis_index("fsdp")
        self.s = lax.axis_index("seq")

    def flip(self, x, axis, bit):
        pairs = []
        for s in range(self.seq):
            for f in range(self.fsdp):
                s2, f2 = (s ^ bit, f) if axis == "seq" else (s, f ^ bit)
                pairs.append((s * self.fsdp + f, s2 * self.fsdp + f2))
        return lax.ppermute(x, AXES, pairs)


def bits_of(count):
    return [1 << k for k in range(count.bit_length() - 1)]


def tie(x, *others):
    return lax.optimization_barrier((x, *others))[0]


def gather_pieces(piece, place, after, later=()):
    found = {0: piece}
    for bit in reversed(bits_of(place.fsdp)):
        for k in list(found):
            moving = found[k]
            if bit == 1:
                moving = tie(moving, *((after,) if k == 0 or not later else later))
            found[k | bit] = place.flip(moving, "fsdp", bit)
    return [found[k] for k in range(place.fsdp)]


def sum_over(x, place, *axes):
    for axis in axes:
        for bit in bits_of(getattr(place, axis)):
            x = x + place.flip(x, axis, bit)
    return x


def pick(x, index, axis):
    return lax.dynamic_index_in_dim(x, index, axis=axis, keepdims=False)


class Reduction:
    def __init__(self, place, keep, send):
        self.place, self.near = place, keep
        self.got = place.flip(send, "fsdp", 1)

    def halve(self, axis, side, flip_axis, bit):
        dims = self.near.shape
        parts = dims[:axis] + (2, dims[axis] // 2) + dims[axis + 1 :]
        near, got = self.near.reshape(parts), self.got.reshape(parts)
        away = pick(near, 1 - side, axis).astype(F32) + pick(got, 1 - side, axis).astype(F32)
        self.near = pick(near, side, axis).astype(F32) + pick(got, side, axis).astype(F32)
        away = away.astype(BF16)
        self.got = self.place.flip(away, flip_axis, bit)
        return away

    def x(self):
        bit = self.place.fsdp // 2
        while bit > 1:
            away = self.halve(0, (self.place.q // bit) % 2, "fsdp", bit)
            bit //= 2
        return away

    def y(self):
        return self.halve(1, self.place.s % 2, "seq", 1)

    def pieces(self):
        total = (self.near + self.got.astype(F32)).astype(BF16)
        return total.reshape((self.place.seq // 2, -1) + total.shape[2:])


def arrive(result, *reductions):
    result, *gots = lax.optimization_barrier((result, *[r.got for r in reductions]))
    for reduction, got in zip(reductions, gots):
        reduction.got = got
    return result


def summed(got):
    return jnp.sum(got.astype(F32), axis=0).astype(BF16)


def exchange(place, sent):
    line = [[y + 2 * z for z in range(place.seq // 2)] for y in range(2)]
    return lax.all_to_all(sent, "seq", 0, 0, axis_index_groups=line)


def copies_for(place, part):
    return jnp.broadcast_to(part[None], (place.seq // 2,) + part.shape)


def on_device(
    tokens, input_mask, doc_lengths, cotangent, w_in, w_conv, w_out, norm_params,
    row_in, col_in, row_conv, col_conv, row_out, col_out, norm_second,
):
    place = Places()
    rows = tokens.shape[0]
    pieces = place.fsdp
    spots = jnp.stack(
        [place.q, (place.s * place.fsdp + place.q) * rows, place.s, place.seq]
    ).astype(jnp.int32)
    docs = doc_lengths.shape[0]
    ends = jnp.pad(
        jnp.cumsum(doc_lengths).astype(F32), (0, -docs % LANE), constant_values=1e9
    ).reshape(1, -1)
    live = input_mask.reshape(-1, LANE)
    weights = (w_in, w_conv, w_out)
    rows_of = [w.shape[0] for w in weights]

    tile_a, tile = 256, 512
    steps = rows // tile
    params_spec = whole(2, D + 2 * INNER)
    dma = pltpu.SemaphoreType.DMA

    out_sides = (w_out[:, : D // 2], w_out[:, D // 2 :])
    conv_out = jnp.concatenate([w_conv, *out_sides], axis=0).astype(BF16)
    hidden_a, slope_a, xhat_a, rstd_a = call(
        norm_a_kernel,
        (rows // tile_a,),
        [rows_spec(tile_a, D), params_spec],
        [rows_spec(tile_a, D)] * 3 + [rows_spec(tile_a, 1)],
        [shape((rows, D), BF16)] * 3 + [shape((rows, 1), F32)],
        us=17,
    )(tokens, tie(norm_params, conv_out))

    in_pieces = gather_pieces(w_in.astype(BF16), place, hidden_a)

    def in_call(tiles, count, before):
        at, stride = tiles

        def here_spec(width):
            return pl.BlockSpec((tile, width), lambda i: (at + stride * i, 0))

        out_shapes = [shape((rows, INNER), BF16)] * 3 + [shape((rows, 1), F32), shape((rows, 8), F32)]
        out_specs = [here_spec(INNER)] * 3 + [here_spec(1), here_spec(8)]
        if at == 0:
            out_shapes += [shape((REACH, INNER), BF16)] * 2
            out_specs += [whole(REACH, INNER)] * 2
        return call(
            functools.partial(in_kernel, pieces, tiles),
            (count,),
            [SMEM, whole(*ends.shape), here_spec(D), whole(*live.shape), params_spec]
            + [ANY] * (pieces + len(before)),
            out_specs,
            out_shapes,
            [pltpu.VMEM((D, INNER), BF16), pltpu.VMEM((tile, INNER), F32), dma((pieces,))],
            us=8,
            aliases={5 + pieces + k: k for k in range(len(before))},
        )(spots, ends, hidden_a, live, norm_params, *in_pieces, *before)

    *kept, m_first, m_last = in_call((0, steps - 1), 2, ())
    moved, slope_b, xhat_b, rstd_b, masks = in_call((1, 1), steps - 2, kept)

    total = place.seq * place.fsdp
    up = [(i, i + 1) for i in range(total - 1)]
    down = [(i + 1, i) for i in range(total - 1)]
    m_low, m_high = lax.ppermute(m_last, AXES, up), lax.ppermute(m_first, AXES, down)
    conv_pieces = gather_pieces(conv_out, place, m_first, (moved, m_low, m_high))

    ext = pltpu.VMEM((rows + 2 * REACH, INNER), BF16)
    taps_wide = KERNEL_TAPS * INNER
    wide = pltpu.VMEM((taps_wide, INNER), BF16)
    shards = place.fsdp // 2

    def half_dims(chunk):
        count = spans(chunk, rows_of)[1]
        return (shards, count + -count % place.seq, SUB, LANE)

    def tile_spec(width, ahead):
        return pl.BlockSpec((tile, width), lambda i: (jnp.clip(i + ahead, 0, steps - 1), 0))

    halves = [half_dims(CHUNKS[0])] * 2 + [half_dims(CHUNKS[1])] * 2
    work = pltpu.VMEM((tile, INNER), F32)
    turned_tile = pltpu.VMEM((INNER, tile), BF16)
    hidden_c, d_conv, d_first, d_last, sums_c, turned, keep1, send1, keep2, send2 = call(
        functools.partial(conv_kernel, pieces, rows_of),
        (steps + 1,),
        [SMEM, ANY, ANY, ANY, tile_spec(8, 0), tile_spec(D, 0), tile_spec(D, -1), params_spec]
        + [ANY] * pieces,
        [tile_spec(INNER, 0)] * 2
        + [whole(REACH, INNER), whole(REACH, INNER), whole(2, INNER)]
        + [ANY] * 5,
        [
            shape((rows, INNER), BF16),
            shape((rows, INNER), BF16),
            shape((REACH, INNER), BF16),
            shape((REACH, INNER), BF16),
            shape((2, INNER), F32),
            shape((taps_wide, INNER), BF16),
        ]
        + [shape(dims, BF16) for dims in halves],
        [ext, wide, wide, pltpu.VMEM((INNER, D), BF16), pltpu.VMEM((D, INNER), BF16)]
        + [pltpu.VMEM((2, tile, taps_wide), BF16), work, work, work, turned_tile, turned_tile]
        + [pltpu.VMEM((INNER, taps_wide), F32), pltpu.VMEM((INNER, D), F32)]
        + [pltpu.VMEM((16, INNER), F32)]
        + [pltpu.VMEM((2,) + halves[0], BF16), pltpu.VMEM((2,) + halves[2], BF16)]
        + [dma((3 + 3 * pieces,))],
        us=45,
    )(
        spots, m_low, moved, m_high, masks, cotangent, cotangent, norm_params, *conv_pieces
    )
    d_low, d_high = lax.ppermute(d_last, AXES, up), lax.ppermute(d_first, AXES, down)
    first, second = Reduction(place, keep1, send1), Reduction(place, keep2, send2)
    (block_out,) = call(
        functools.partial(out_kernel, pieces),
        (steps,),
        [SMEM, rows_spec(tile, INNER), rows_spec(tile, D)] + [ANY] * pieces,
        [rows_spec(tile, D)],
        [shape((rows, D), BF16)],
        [pltpu.VMEM((INNER, D), BF16), dma((2 * pieces,))],
        us=9,
    )(spots, hidden_c, tokens, *conv_pieces)

    def back_conv(last, spots, before):
        here = steps // 2
        at = here * last

        def here_spec(width):
            return pl.BlockSpec((tile, width), lambda i: (i + at, 0))

        dims = half_dims(CHUNKS[2])
        return call(
            functools.partial(back_conv_kernel, last, w_in.shape[0]),
            (here,),
            [SMEM] + [ANY] * 4
            + [here_spec(8), here_spec(INNER), here_spec(1), here_spec(INNER), here_spec(D)]
            + [params_spec]
            + [ANY] * last,
            [rows_spec(tile, INNER), whole(2, INNER)] + [ANY] * (1 + last),
            [shape((rows // 2, INNER), BF16), shape((2, INNER), F32)]
            + ([shape(dims, BF16)] * 2 if last else [shape((INNER, D), F32)]),
            ([pltpu.VMEM((2,) + dims, BF16)] if last else [])
            + [
                ext,
                wide,
                pltpu.VMEM((tile, taps_wide), BF16),
                pltpu.VMEM((tile, INNER), F32),
                pltpu.VMEM((INNER, D), F32),
                pltpu.VMEM((16, INNER), F32),
                dma((5,)),
            ],
            us=16,
        )(
            spots, d_low, d_conv, d_high, turned, masks, xhat_b, rstd_b, slope_b, hidden_a,
            norm_params, *before,
        )

    block_out = arrive(block_out, first, second)
    away = (first.x(), second.y())
    d_pre0, sums_b0, grad_part = back_conv(0, tie(spots, *away), ())
    d_pre0 = arrive(d_pre0, first, second)
    away = (first.y(), second.x())
    d_pre1, sums_b1, keep, send = back_conv(1, tie(spots, *away), (grad_part,))
    send = arrive(send, first, second)
    third = Reduction(place, keep, send)
    sent = jnp.concatenate([first.pieces(), second.pieces()], axis=1)
    got = exchange(place, sent)
    third.got = tie(third.got, sent)
    away = (sent, third.x())
    input_grad, sums_a = call(
        functools.partial(back_a_kernel, pieces, steps // 2),
        (steps,),
        [SMEM]
        + [
            pl.BlockSpec((tile, INNER), lambda i: (jnp.minimum(i, steps // 2 - 1), 0)),
            pl.BlockSpec((tile, INNER), lambda i: (jnp.maximum(i - steps // 2, 0), 0)),
        ]
        + [rows_spec(tile, D), rows_spec(tile, 1), rows_spec(tile, D), rows_spec(tile, D)]
        + [params_spec]
        + [ANY] * pieces,
        [rows_spec(tile, D), whole(2, D)],
        [shape((rows, D), F32), shape((2, D), F32)],
        [
            pltpu.VMEM((D, INNER), BF16),
            pltpu.VMEM((INNER, D), BF16),
            pltpu.VMEM((tile, D), F32),
            pltpu.VMEM((16, D), F32),
            dma((pieces,)),
        ],
        us=17,
    )(
        tie(spots, *away), d_pre0, d_pre1, xhat_a, rstd_a, slope_a, cotangent, norm_params, *in_pieces
    )

    got, third.got, input_grad = lax.optimization_barrier((got, third.got, input_grad))
    part = summed(got)
    sent = copies_for(place, part)
    mine = exchange(place, sent)
    third.got = tie(third.got, sent)
    away = third.y()

    row_states, col_states = (row_in, row_conv, row_out), (col_in, col_conv, col_out)
    row_specs = [whole(*r.shape) for r in row_states]
    col_specs = [whole(*c.shape) for c in col_states]
    cols_all = D + 2 * INNER
    pack_spec = whole(4, cols_all)
    fulls = [pltpu.VMEM(half_dims(c)[1:], BF16) for c in CHUNKS]
    sums = (sums_a, sums_b0, sums_b1, sums_c)
    (pack,) = call(
        functools.partial(pack_kernel, rows_of, [half_dims(c)[1] // place.seq for c in CHUNKS]),
        (1,),
        [SMEM, whole(*part.shape)] + row_specs + [whole(*x.shape) for x in sums],
        [pack_spec],
        [shape((4, cols_all), F32)],
        [pltpu.VMEM((cols_all // LANE + 1, SUB, LANE), F32)],
        us=2,
    )(tie(spots, away), part, *row_states, *sums)
    pack = sum_over(pack, place, "fsdp")
    mine, third.got, pack = lax.optimization_barrier((mine, third.got, pack))
    other = place.flip(mine, "seq", 1)
    got = exchange(place, third.pieces())
    pack = sum_over(pack, place, "seq")
    mine_in = exchange(place, copies_for(place, summed(got)))
    mine_in, other, pack = lax.optimization_barrier((mine_in, other, pack))
    other_in = place.flip(mine_in, "seq", 1)

    def update_scratch(weights):
        lines = max(w.shape[0] + -w.shape[0] % LANE for w in weights)
        return [pltpu.VMEM((8, lines), F32)] + [pltpu.VMEM((lines, LANE), F32)] * 2

    weight_specs = [whole(*w.shape) for w in weights]
    results = call(
        functools.partial(update_kernel, rows_of, place.seq),
        (1,),
        [SMEM, ANY, ANY, pack_spec, params_spec, params_spec]
        + weight_specs[1:]
        + row_specs[1:]
        + col_specs[1:],
        weight_specs[1:] * 2 + row_specs[1:] + col_specs[1:] + [params_spec] * 3,
        [shape(w.shape, F32) for w in weights[1:]] * 2
        + [shape(r.shape, F32) for r in row_states[1:] + col_states[1:]]
        + [shape((2, cols_all), F32)] * 3,
        update_scratch(weights[1:]) + fulls[:2] + [dma((2 * place.seq,))],
        us=8,
    )(
        spots, mine, other, pack, norm_params, norm_second, *weights[1:], *row_states[1:],
        *col_states[1:],
    )
    grad_conv, grad_out, new_conv, new_out, row_conv_new, row_out_new, col_conv_new, col_out_new = (
        results[:8]
    )
    (pack_in,) = call(
        functools.partial(pack_in_kernel, rows_of),
        (1,),
        [SMEM, ANY, ANY],
        [whole(8, INNER)],
        [shape((8, INNER), F32)],
        [fulls[2], dma((place.seq,))],
        us=2,
    )(spots, mine_in, other_in)
    pack_in = sum_over(pack_in, place, "fsdp")
    grad_in, new_in, row_in_new, col_in_new = call(
        functools.partial(update_in_kernel, rows_of, place.seq),
        (1,),
        [SMEM, ANY, ANY, whole(8, INNER), pack_spec]
        + [weight_specs[0], row_specs[0], col_specs[0]],
        [weight_specs[0]] * 2 + [row_specs[0], col_specs[0]],
        [shape(w_in.shape, F32)] * 2 + [shape(row_in.shape, F32), shape(col_in.shape, F32)],
        update_scratch(weights[:1]) + [fulls[2], dma((place.seq,))],
        us=4,
    )(spots, mine_in, other_in, pack_in, pack, w_in, row_in, col_in)
    return (
        block_out,
        input_grad,
        grad_in,
        grad_conv,
        grad_out,
        new_in,
        new_conv,
        new_out,
        row_in_new,
        col_in_new,
        row_conv_new,
        col_conv_new,
        row_out_new,
        col_out_new,
        *results[8:11],
    )


def solution(mesh):
    both, rows = P(AXES, None), P("fsdp", None)
    in_specs = (
        both, P(AXES), P(), both, rows, rows, rows, P(),
        P("fsdp"), P(), P("fsdp"), P(), P("fsdp"), P(), P(),
    )
    out_specs = (
        both, both, rows, rows, rows, rows, rows, rows,
        P("fsdp"), P(), P("fsdp"), P(), P("fsdp"), P(), P(), P(), P(),
    )
    return jax.shard_map(
        on_device, mesh=mesh, in_specs=in_specs, out_specs=out_specs, check_vma=False
    )
```

```python
import functools
import math

import jax
import jax.numpy as jnp
from jax import lax
from jax.experimental import pallas as pl
from jax.experimental.pallas import tpu as pltpu
from jax.sharding import PartitionSpec as P

D = 1280
INNER = 640
KERNEL_TAPS = 5
DILATION_STEP = 128
STEP = 10
EPSILON = 1e-05
DECAY = 1.0 - STEP ** (-0.8)

REACH = (KERNEL_TAPS - 1) // 2 * DILATION_STEP
MID = (KERNEL_TAPS - 1) // 2
F32 = jnp.float32
BF16 = jnp.bfloat16
SUB, LANE = 16, 128
AXES = ("seq", "fsdp")
NT = (((1,), (1,)), ((), ()))
TN = (((0,), (0,)), ((), ()))
NN = (((1,), (0,)), ((), ()))
VMEM_LIMIT = 58 * 1024 * 1024


def call(kernel, grid, in_specs, out_specs, out_shape, scratch=(), us=1.0, aliases=None):
    params = pltpu.CompilerParams(
        vmem_limit_bytes=VMEM_LIMIT, dimension_semantics=("arbitrary",) * len(grid)
    )
    return pl.pallas_call(
        kernel,
        grid=grid,
        in_specs=in_specs,
        out_specs=out_specs,
        out_shape=out_shape,
        scratch_shapes=list(scratch),
        compiler_params=params,
        input_output_aliases=aliases or {},
        cost_estimate=pl.CostEstimate(
                flops=int(us * 1.1e9), bytes_accessed=int(us * 3.4e6), transcendentals=0
        ),
    )


def shape(dims, dtype):
    return jax.ShapeDtypeStruct(dims, dtype)


def rows_spec(tile, width):
    return pl.BlockSpec((tile, width), lambda i: (i, 0))


def whole(*dims):
    return pl.BlockSpec(dims, lambda *_: (0,) * len(dims))


ANY = pl.BlockSpec(memory_space=pl.ANY)
SMEM = pl.BlockSpec(memory_space=pltpu.SMEM)


ERFC_P = 0.47 / math.sqrt(2.0)
ERFC_C = (
    0.12357219400743558,
    0.1999878668208835,
    -0.08033356004356296,
    0.3660253986657854,
    -0.1092519747040215,
)
LOG2E = 1.4426950408889634


def gelu_and_slope(y):
    t = pltpu.reciprocal(1.0 + ERFC_P * jnp.abs(y), approx=True)
    bell = jnp.exp2(y * y * (-0.5 * LOG2E))
    poly = ERFC_C[4] * t + ERFC_C[3]
    for c in ERFC_C[2::-1]:
        poly = poly * t + c
    tail = poly * t * bell
    cdf = jnp.where(y > 0.0, 1.0 - tail, tail)
    return y * cdf, cdf + y * (bell * (1.0 / math.sqrt(2.0 * math.pi)))


def lane_blocks(width):
    return [slice(k, k + LANE) for k in range(0, width, LANE)]


def row_stats(ref, rows):
    width = ref.shape[-1]
    blocks = lane_blocks(width)
    total = ref[rows, blocks[0]].astype(F32)
    for b in blocks[1:]:
        total = total + ref[rows, b].astype(F32)
    mean = jnp.sum(total, axis=-1, keepdims=True) * (1.0 / width)
    square = None
    for b in blocks:
        centered = ref[rows, b].astype(F32) - mean
        square = centered * centered if square is None else square + centered * centered
    variance = jnp.sum(square, axis=-1, keepdims=True) * (1.0 / width)
    return mean, lax.rsqrt(variance + EPSILON)


def fold(values):
    total = values[0:8]
    for k in range(8, values.shape[0], 8):
        total = total + values[k : k + 8]
    return total


def in_stages(count, stages, between=()):
    chunks = [slice(k, k + CHUNK) for k in range(0, count, CHUNK)]
    kept, rounds = {}, len(chunks) + len(stages) - 1
    for t in range(rounds):
        for n, stage in enumerate(stages):
            if 0 <= t - n < len(chunks):
                kept[n, t - n] = stage(chunks[t - n], kept.get((n - 1, t - n)))
        for work in between[t * len(between) // rounds : (t + 1) * len(between) // rounds]:
            work()


def halves_of(count):
    return (slice(0, count // 2), slice(count // 2, count))


def row_means(sums, width):
    return [jnp.sum(x, axis=-1, keepdims=True) * (1.0 / width) for x in sums]


def norm_back(rows, dxhat_ref, xhat_ref, means, put):
    mean_d, mean_dx, rstd = means
    for b in lane_blocks(dxhat_ref.shape[-1]):
        xhat = xhat_ref[rows, b].astype(F32)
        put(b, (dxhat_ref[rows, b] - mean_d - xhat * mean_dx) * rstd)


def add_terms(acc_ref, b, dy, xhat):
    acc_ref[0:8, b] += fold(dy * xhat)
    acc_ref[8:16, b] += fold(dy)


def open_sums(acc_ref):
    @pl.when(pl.program_id(0) == 0)
    def _():
        acc_ref[...] = jnp.zeros_like(acc_ref)


def close_sums(out_ref, acc_ref):
    @pl.when(pl.program_id(0) == pl.num_programs(0) - 1)
    def _():
        out_ref[0:1, :] = jnp.sum(acc_ref[0:8, :], axis=0, keepdims=True)
        out_ref[1:2, :] = jnp.sum(acc_ref[8:16, :], axis=0, keepdims=True)


def run_copies(copies):
    for copy in copies:
        copy.start()
    for copy in copies:
        copy.wait()


def piece_copies(pieces, full_ref, me, sem, first=0):
    each = full_ref.shape[0] // len(pieces)
    return [
        pltpu.make_async_copy(
            piece.at[0:each, :],
            full_ref.at[pl.ds(pl.multiple_of((me ^ k) * each, SUB), each), :],
            sem.at[first + k],
        )
        for k, piece in enumerate(pieces)
    ]


def out_copies(pieces, full_ref, me, sem, first=0):
    each, width = full_ref.shape[0] // len(pieces), full_ref.shape[1] // 2
    copies = []
    for k, piece in enumerate(pieces):
        rows = pl.ds(pl.multiple_of((me ^ k) * each, SUB), each)
        for side in range(2):
            at = piece.shape[0] - (2 - side) * each
            copies.append(
                pltpu.make_async_copy(
                    piece.at[at : at + each, :],
                    full_ref.at[rows, side * width : (side + 1) * width],
                    sem.at[first + 2 * k + side],
                )
            )
    return copies


def column(row):
    return jnp.transpose(jnp.broadcast_to(row, (LANE, LANE)))


CHUNK = 64


def norm_a_kernel(tok_ref, np_ref, hid_ref, slope_ref, xhat_ref, rstd_ref):
    def stats(rows, _):
        mean, rstd = row_stats(tok_ref, rows)
        rstd_ref[rows, :] = rstd
        return mean, rstd

    def work(rows, kept):
        mean, rstd = kept
        for b in lane_blocks(D):
            xhat = (tok_ref[rows, b].astype(F32) - mean) * rstd
            hidden, slope = gelu_and_slope(xhat * np_ref[0:1, b] + np_ref[1:2, b])
            hid_ref[rows, b] = hidden.astype(BF16)
            slope_ref[rows, b] = slope.astype(BF16)
            xhat_ref[rows, b] = xhat.astype(BF16)

    in_stages(tok_ref.shape[0], [stats, work])


def running_ends(ends_ref, lengths_ref):
    docs, width = lengths_ref.shape[0], ends_ref.shape[1]
    ends_ref[...] = jnp.zeros_like(ends_ref)
    ends_ref[0:1, 0:docs] = lengths_ref[...].reshape(1, -1).astype(F32)
    before = jnp.zeros((1, 1), F32)
    row = lax.broadcasted_iota(jnp.int32, (LANE, LANE), 0)
    lane = lax.broadcasted_iota(jnp.int32, (LANE, LANE), 1)
    for k in range(0, width, LANE):
        line = ends_ref[0:1, k : k + LANE]
        sums = jnp.sum(jnp.where(row <= lane, column(line), 0.0), axis=0, keepdims=True) + before
        ends_ref[0:1, k : k + LANE] = jnp.where(lane[0:1] + k < docs, sums, 1e9)
        before = before + jnp.sum(line, axis=1, keepdims=True)


def in_kernel(pieces, tiles, place_ref, lengths_ref, hid_ref, live_ref, np_ref, *refs):
    piece_refs = refs[:pieces]
    edges = tiles[0] == 0
    outs = refs[-(11 if edges else 9) :]
    mov_ref, slope_ref, xhat_ref, rstd_ref, mask_ref = outs[:5]
    w_ref, pre_ref, ends_ref, sem = outs[-4:]
    step = pl.program_id(0)
    tile = hid_ref.shape[0]

    @pl.when(step == 0)
    def _():
        copies = piece_copies(piece_refs, w_ref, place_ref[0], sem)
        for copy in copies:
            copy.start()
        running_ends(ends_ref, lengths_ref)
        for copy in copies:
            copy.wait()

    for half in halves_of(tile):
        pre_ref[half, :] = lax.dot_general(
            hid_ref[half, :], w_ref[...], NN, preferred_element_type=F32
        )

    at_tile = tiles[0] + step * tiles[1]
    first = place_ref[1] + at_tile * tile
    ends = ends_ref[0:1, :]
    lanes = lax.broadcasted_iota(jnp.int32, (LANE, 8), 1)
    offsets = ((lanes - MID) * DILATION_STEP).astype(F32)
    for k in range(tile // LANE):
        at = (first + k * LANE + lax.broadcasted_iota(jnp.int32, (LANE, 1), 0)).astype(F32)
        begin = jnp.max(jnp.where(ends <= at, ends, 0.0), axis=1, keepdims=True)
        end = jnp.min(jnp.where(ends > at, ends, 1e9), axis=1, keepdims=True)
        there = at + offsets
        same = jnp.where((there >= begin) & (there < end), 1.0, 0.0)
        live = column(live_ref[pl.ds(at_tile * (tile // LANE) + k, 1), :].astype(F32))
        mask_ref[k * LANE : (k + 1) * LANE, :] = jnp.where(lanes == MID, live[:, 0:8], same)

    def stats(rows, _):
        mean, rstd = row_stats(pre_ref, rows)
        rstd_ref[rows, :] = rstd
        return mean, rstd

    def work(rows, kept):
        mean, rstd = kept
        live = mask_ref[rows, MID : MID + 1]
        for b in lane_blocks(INNER):
            gains = slice(D + b.start, D + b.stop)
            xhat = (pre_ref[rows, b] - mean) * rstd
            hidden, slope = gelu_and_slope(xhat * np_ref[0:1, gains] + np_ref[1:2, gains])
            mov_ref[rows, b] = (hidden * live).astype(BF16)
            slope_ref[rows, b] = slope.astype(BF16)
            xhat_ref[rows, b] = xhat.astype(BF16)

    in_stages(tile, [stats, work])
    if edges:
        first_ref, last_ref = outs[5:7]

        @pl.when(step == 0)
        def _():
            first_ref[...] = mov_ref[0:REACH, :]

        @pl.when(step == 1)
        def _():
            last_ref[...] = mov_ref[tile - REACH :, :]


def load_window(low, mid, high, ext_ref, sem):
    rows = mid.shape[0]
    return [
        pltpu.make_async_copy(low, ext_ref.at[0:REACH, :], sem.at[0]),
        pltpu.make_async_copy(mid, ext_ref.at[REACH : REACH + rows, :], sem.at[1]),
        pltpu.make_async_copy(high, ext_ref.at[REACH + rows : 2 * REACH + rows, :], sem.at[2]),
    ]


def fill_taps(taps_ref, ext_ref, mask_ref, start):
    tile = taps_ref.shape[0]
    for j in range(KERNEL_TAPS):
        rows = pl.ds(pl.multiple_of(start + j * DILATION_STEP, DILATION_STEP), tile)
        picked = ext_ref[rows, :]
        if j != MID:
            picked = picked * mask_ref[:, j : j + 1].astype(BF16)
        taps_ref[:, j * INNER : (j + 1) * INNER] = picked


def conv_kernel(
    pieces, rows_of, place_ref, low_ref, mov_ref, high_ref, mask_ref, cot_ref, before_ref, np_ref, *refs
):
    piece_refs = refs[:pieces]
    hid_ref, dconv_ref, first_ref, last_ref, sums_ref, turned_ref = refs[pieces : pieces + 6]
    outs = refs[pieces + 6 : pieces + 10]
    ext_ref, wc_ref, wct_ref, wo_ref, wt_ref, taps_ref, pre_ref, dh_ref, xhat_ref = refs[
        pieces + 10 : pieces + 19
    ]
    dt_ref, ht_ref, gc_ref, go_ref, acc_ref, stage1_ref, stage2_ref, sem = refs[pieces + 19 :]
    step, steps = pl.program_id(0), pl.num_programs(0) - 1
    tile = taps_ref.shape[1]
    slot = lax.rem(step, 2)

    @pl.when(step == 0)
    def _():
        me = place_ref[0]
        outs = out_copies(piece_refs, wo_ref, me, sem, 3)
        rest = load_window(low_ref, mov_ref, high_ref, ext_ref, sem)
        rest += piece_copies(piece_refs, wc_ref, me, sem, 3 + 2 * pieces)
        for copy in outs + rest:
            copy.start()
        for ref in (acc_ref, gc_ref, go_ref, dt_ref, ht_ref):
            ref[...] = jnp.zeros_like(ref)
        taps_ref[1] = jnp.zeros_like(taps_ref[1])
        for copy in outs:
            copy.wait()
        for k in range(0, D, 256):
            wt_ref[k : k + 256, :] = jnp.transpose(wo_ref[:, k : k + 256])
        for copy in rest:
            copy.wait()

    def grad_conv(cols):
        def work():
            gc_ref[:, cols] += lax.dot_general(
                dt_ref[...], taps_ref[1 - slot, :, cols], NN, preferred_element_type=F32
            )

        return work

    def grad_out(cols):
        def work():
            go_ref[:, cols] += lax.dot_general(
                ht_ref[...], before_ref[:, cols], NN, preferred_element_type=F32
            )

        return work

    taps_wide = KERNEL_TAPS * INNER
    products = [grad_conv(slice(k, min(k + 768, taps_wide))) for k in range(0, taps_wide, 768)]
    products += [grad_out(slice(k, min(k + 768, D))) for k in range(0, D, 768)]

    @pl.when(step < steps)
    def _():
        fill_taps(taps_ref.at[slot], ext_ref, mask_ref, step * tile)
        pre_ref[...] = lax.dot_general(
            taps_ref[slot], wc_ref[...], NN, preferred_element_type=F32
        )
        dh_ref[...] = lax.dot_general(cot_ref[...], wt_ref[...], NN, preferred_element_type=F32)
        for n in range(2):
            tap = jnp.minimum(2 * step + n, KERNEL_TAPS - 1)
            source = wc_ref[pl.ds(pl.multiple_of(tap * INNER, SUB), INNER), :]
            target = pl.multiple_of((KERNEL_TAPS - 1 - tap) * INNER, SUB)
            wct_ref[pl.ds(target, INNER), :] = jnp.transpose(source)

        def stats(rows, _):
            return row_stats(pre_ref, rows)

        def work(rows, kept):
            mean, rstd = kept
            sums = [0.0, 0.0]
            for b in lane_blocks(INNER):
                gains = slice(D + INNER + b.start, D + INNER + b.stop)
                gain = np_ref[0:1, gains]
                xhat = (pre_ref[rows, b] - mean) * rstd
                hidden, slope = gelu_and_slope(xhat * gain + np_ref[1:2, gains])
                hid_ref[rows, b] = hidden.astype(BF16)
                dy = dh_ref[rows, b] * slope
                add_terms(acc_ref, b, dy, xhat)
                dxhat = dy * gain
                xhat_ref[rows, b] = xhat
                dh_ref[rows, b] = dxhat
                sums = [sums[0] + dxhat, sums[1] + dxhat * xhat]
            return row_means(sums, INNER) + [rstd]

        def finish(rows, means):
            def put(b, value):
                dconv_ref[rows, b] = value.astype(BF16)

            norm_back(rows, dh_ref, xhat_ref, means, put)

        in_stages(tile, [stats, work, finish], products)
        dt_ref[...] = jnp.transpose(dconv_ref[...])
        ht_ref[...] = jnp.transpose(hid_ref[...])

    @pl.when(step == 0)
    def _():
        first_ref[...] = dconv_ref[0:REACH, :]

    @pl.when(step == steps - 1)
    def _():
        last_ref[...] = dconv_ref[tile - REACH :, :]

    @pl.when(step == steps)
    def _():
        copy = pltpu.make_async_copy(wct_ref, turned_ref, sem.at[4])
        copy.start()
        for work in products:
            work()
        core = lax.rem(place_ref[0], 2)
        _, rows_conv, rows_out = rows_of
        stage_turned(stage1_ref, core, gc_ref, rows_conv, 0, slice(0, CUT // LANE))
        first_tiles = rows_conv // SUB * (CUT // LANE)
        stage_plain(stage1_ref, core, go_ref, rows_out, first_tiles)
        copies = stage_copies(stage1_ref, outs[0], outs[1], spans(CHUNKS[0], rows_of)[1], sem, 0)
        for each in copies:
            each.start()
        stage_turned(stage2_ref, core, gc_ref, rows_conv, 0, slice(CUT // LANE, INNER // LANE))
        more = stage_copies(stage2_ref, outs[2], outs[3], spans(CHUNKS[1], rows_of)[1], sem, 2)
        for each in more:
            each.start()
        for each in copies + more + [copy]:
            each.wait()
        sums_ref[0:1, :] = jnp.sum(acc_ref[0:8, :], axis=0, keepdims=True)
        sums_ref[1:2, :] = jnp.sum(acc_ref[8:16, :], axis=0, keepdims=True)


def stage_tiles(stage_ref, core, first_row, rows_each, base, block0, blocks, value):
    for g in range(value.shape[0] // SUB):
        row = first_row + g * SUB
        owner, inside = row // rows_each, row % rows_each // SUB
        side = core ^ (owner % 2)
        for b in range(value.shape[1] // LANE):
            tile = value[g * SUB : (g + 1) * SUB, b * LANE : (b + 1) * LANE]
            at = base + inside * blocks + block0 + b
            stage_ref[side, owner // 2, at] = tile.astype(BF16)


def stage_plain(stage_ref, core, grad_ref, rows_each, base):
    blocks = grad_ref.shape[1] // LANE
    for row in range(0, grad_ref.shape[0], SUB):
        part = grad_ref[row : row + SUB, :]
        stage_tiles(stage_ref, core, row, rows_each, base, 0, blocks, part)


def stage_turned(stage_ref, core, turned_ref, rows_each, base, blocks):
    count = blocks.stop - blocks.start
    for row in range(0, turned_ref.shape[1], LANE):
        for b in range(count):
            at = (blocks.start + b) * LANE
            part = jnp.transpose(turned_ref[at : at + LANE, row : row + LANE].astype(BF16))
            stage_tiles(stage_ref, core, row, rows_each, base, b, count, part)


def stage_copies(stage_ref, keep_ref, send_ref, used, sem, first):
    count = stage_ref.shape[2]
    if used < count:
        dims = stage_ref.shape[:2] + (count - used, SUB, LANE)
        stage_ref[:, :, used:] = jnp.zeros(dims, BF16)
    return [
        pltpu.make_async_copy(stage_ref.at[n], ref, sem.at[first + n])
        for n, ref in enumerate((keep_ref, send_ref))
    ]


def back_conv_kernel(
    at, tokens, rows_in, place_ref, low_ref, d_ref, high_ref, turned_ref, mask_ref, xhat_ref, rstd_ref, slope_ref, np_ref, *refs
):
    ext_ref, wt_ref, taps_ref, dmov_ref, acc_ref, sem = refs[-6:]
    step, steps = pl.program_id(0), pl.num_programs(0)
    tile = taps_ref.shape[0]
    first, rows = at * tile, ext_ref.shape[0] - 2 * REACH
    last = first + rows == tokens
    if last:
        hid_ref, before_ref, dpre_ref, sums_ref, keep_ref, send_ref = refs[:6]
        stage_ref, all_ref, held_ref, grad_ref = refs[6:10]
        gather = [
            pltpu.make_async_copy(before_ref.at[0:first, :], all_ref.at[0:first, :], sem.at[4]),
            pltpu.make_async_copy(hid_ref, held_ref, sem.at[5]),
        ]
    else:
        dpre_ref, sums_ref = refs[at > 0 :][:2]
    open_sums(acc_ref)

    @pl.when(step == 0)
    def _():
        begin, end = max(first - REACH, 0), min(first + rows + REACH, tokens)
        offset = begin - (first - REACH)
        copies = [
            pltpu.make_async_copy(turned_ref, wt_ref, sem.at[0]),
            pltpu.make_async_copy(
                d_ref.at[begin:end, :], ext_ref.at[offset : offset + end - begin, :], sem.at[1]
            ),
        ]
        if first == 0:
            copies.append(pltpu.make_async_copy(low_ref, ext_ref.at[0:REACH, :], sem.at[2]))
        if last:
            target = ext_ref.at[REACH + rows : 2 * REACH + rows, :]
            copies.append(pltpu.make_async_copy(high_ref, target, sem.at[3]))
        for copy in copies:
            copy.start()
        if last:
            for copy in gather:
                copy.start()
        for copy in copies:
            copy.wait()

    fill_taps(taps_ref, ext_ref, mask_ref, step * tile)
    dmov_ref[...] = lax.dot_general(taps_ref[...], wt_ref[...], NN, preferred_element_type=F32)

    def work(rows, _):
        live = mask_ref[rows, MID : MID + 1]
        sums = [0.0, 0.0]
        for b in lane_blocks(INNER):
            xhat = xhat_ref[rows, b].astype(F32)
            dy = dmov_ref[rows, b] * live * slope_ref[rows, b].astype(F32)
            add_terms(acc_ref, b, dy, xhat)
            dxhat = dy * np_ref[0:1, D + b.start : D + b.stop]
            dmov_ref[rows, b] = dxhat
            sums = [sums[0] + dxhat, sums[1] + dxhat * xhat]
        return row_means(sums, INNER) + [rstd_ref[rows, :]]

    def finish(rows, means):
        def put(b, value):
            dpre_ref[rows, b] = value.astype(BF16)

        norm_back(rows, dmov_ref, xhat_ref, means, put)

    in_stages(tile, [work, finish])
    close_sums(sums_ref, acc_ref)
    if last:
        all_ref[pl.ds(first + step * tile, tile), :] = dpre_ref[...]

        @pl.when(step == steps - 1)
        def _():
            for copy in gather:
                copy.wait()
            grad_ref[...] = lax.dot_general(
                all_ref[...], held_ref[...], TN, preferred_element_type=F32
            )
            all_blocks = slice(0, INNER // LANE)
            stage_turned(stage_ref, lax.rem(place_ref[0], 2), grad_ref, rows_in, 0, all_blocks)
            used = rows_in // SUB * (INNER // LANE)
            run_copies(stage_copies(stage_ref, keep_ref, send_ref, used, sem, 0))


def back_a_kernel(pieces, place_ref, dpre_ref, xhat_ref, rstd_ref, slope_ref, cot_ref, np_ref, *refs):
    piece_refs = refs[:pieces]
    grad_ref, sums_ref, w_ref, wt_ref, dh_ref, acc_ref, sem = refs[-7:]
    open_sums(acc_ref)

    @pl.when(pl.program_id(0) == 0)
    def _():
        run_copies(piece_copies(piece_refs, w_ref, place_ref[0], sem))
        for k in range(0, D, 256):
            wt_ref[:, k : k + 256] = jnp.transpose(w_ref[k : k + 256, :])

    dh_ref[...] = lax.dot_general(dpre_ref[...], wt_ref[...], NN, preferred_element_type=F32)

    def work(rows, _):
        sums = [0.0, 0.0]
        for b in lane_blocks(D):
            xhat = xhat_ref[rows, b].astype(F32)
            dy = dh_ref[rows, b] * slope_ref[rows, b].astype(F32)
            add_terms(acc_ref, b, dy, xhat)
            dxhat = dy * np_ref[0:1, b]
            dh_ref[rows, b] = dxhat
            sums = [sums[0] + dxhat, sums[1] + dxhat * xhat]
        return row_means(sums, D) + [rstd_ref[rows, :]]

    def finish(rows, means):
        def put(b, value):
            grad_ref[rows, b] = cot_ref[rows, b].astype(F32) + value

        norm_back(rows, dh_ref, xhat_ref, means, put)

    in_stages(dpre_ref.shape[0], [work, finish])
    close_sums(sums_ref, acc_ref)


def out_kernel(pieces, place_ref, hid_ref, tok_ref, *refs):
    piece_refs = refs[:pieces]
    out_ref, w_ref, sem = refs[pieces:]

    @pl.when(pl.program_id(0) == 0)
    def _():
        run_copies(out_copies(piece_refs, w_ref, place_ref[0], sem))

    branch = lax.dot_general(hid_ref[...], w_ref[...], NN, preferred_element_type=F32)
    out_ref[...] = (tok_ref[...].astype(F32) + branch).astype(BF16)


WIDTHS = (INNER, INNER, D)
LANE0 = (0, INNER, 2 * INNER)
CUT = 2 * LANE
CHUNKS = (((1, 0, CUT), (2, 0, D)), ((1, CUT, INNER - CUT),), ((0, 0, INNER),))


def spans(chunk, rows):
    found, first = [], 0
    for weight, col, cols in chunk:
        tiles = rows[weight] // SUB * (cols // LANE)
        found.append((weight, col // LANE, cols // LANE, first, tiles))
        first += tiles
    return found, first


def column_sums(pack_ref, row, ref, chunk, rows):
    for weight, block0, blocks, first, tiles in spans(chunk, rows)[0]:

        def body(g, carry, first=first, blocks=blocks):
            new = []
            for b in range(blocks):
                value = ref[first + g * blocks + b].astype(F32)
                new.append(carry[b] + fold(value * value + 1e-30))
            return tuple(new)

        zero = tuple(jnp.zeros((8, LANE), F32) for _ in range(blocks))
        cols = lax.fori_loop(0, tiles // blocks, body, zero, unroll=5)
        for b in range(blocks):
            lane = LANE0[weight] + (block0 + b) * LANE
            pack_ref[row : row + 1, lane : lane + LANE] = jnp.sum(cols[b], axis=0, keepdims=True)


def load_full(refs, place_ref, first, full_ref, sem, at):
    pieces = refs[0].shape[0]
    each = full_ref.shape[0] // (len(refs) * pieces)
    outer = pieces if len(refs) == 2 else pieces // 2
    y = place_ref[2] % 2
    copies = []
    for n, (ref, side) in enumerate(zip(refs, (y, 1 - y))):
        for p in range(pieces):
            index = side * outer + p if len(refs) == 2 else p % 2 * outer + p // 2
            target = full_ref.at[pl.ds(index * each, each)]
            source = ref.at[p, first : first + each]
            copies.append(pltpu.make_async_copy(source, target, sem.at[at + n * pieces + p]))
    return copies


def pack_kernel(rows, pieces, place_ref, part_ref, *refs):
    states, (pack_ref, acc_ref) = refs[0:3], refs[3:5]
    pack_ref[...] = jnp.zeros_like(pack_ref)
    lanes = lax.broadcasted_iota(jnp.int32, (1, LANE), 1)
    for k in range(3):
        total = jnp.sum(states[k][...].reshape(1, -1), axis=1, keepdims=True)
        pack_ref[3:4, 0:LANE] += jnp.where(lanes == k, total, 0.0)
    acc_ref[...] = jnp.zeros_like(acc_ref)
    spare = acc_ref.shape[0] - 1
    piece = place_ref[2] % 2 * (place_ref[3] // 2) + place_ref[2] // 2
    at = 0
    for chunk, each in zip(CHUNKS[:2], pieces):
        found, _ = spans(chunk, rows)
        start = piece * each

        def body(k, carry, found=found, start=start, at=at):
            n = start + k
            slot = spare
            for weight, block0, blocks, first, tiles in found:
                here = LANE0[weight] // LANE + block0 + lax.rem(jnp.maximum(n - first, 0), blocks)
                slot = jnp.where((n >= first) & (n < first + tiles), here, slot)
            value = part_ref[at + k].astype(F32)
            acc_ref[slot] += value * value + 1e-30
            return carry

        lax.fori_loop(0, each, body, 0, unroll=2)
        at += each
    for slot in range(spare):
        pack_ref[2:3, slot * LANE : (slot + 1) * LANE] = jnp.sum(acc_ref[slot], axis=0, keepdims=True)


def pack_norms_kernel(pack_ref, *refs):
    sums, out_ref = refs[:-1], refs[-1]
    out_ref[...] = pack_ref[...]
    lanes_of = ((0, D), (D, D + INNER), (D, D + INNER), (D, D + INNER), (D + INNER, D + 2 * INNER))
    for part, (lane0, lane1) in zip(sums, lanes_of):
        out_ref[0:2, lane0:lane1] += part[...]


def pack_in_kernel(rows, place_ref, got_ref, pack_ref, out_ref, full_ref, sem):
    run_copies(load_full((got_ref,), place_ref, 0, full_ref, sem, 0))
    out_ref[...] = pack_ref[...]
    column_sums(out_ref, 2, full_ref, CHUNKS[2], rows)


def update_weight(
    k, squares, states_sum, source, weight, state, col_state, grad_ref, new, row_new_ref, col_new_ref, scratch
):
    line_ref, state_ref, new_ref = scratch
    width, fan, rows_here = WIDTHS[k], (D, KERNEL_TAPS * INNER, INNER)[k], weight.shape[0]
    col_new = DECAY * col_state[...].reshape(1, -1) + (1.0 - DECAY) * (squares * (1.0 / fan))
    col_new_ref[...] = col_new.reshape(-1)
    total = DECAY * states_sum
    total = total + (1.0 - DECAY) * (1.0 / width) * jnp.sum(squares, axis=1, keepdims=True)
    scaled = col_new / (total * (1.0 / fan))
    rate = 0.5 / fan**0.5
    line_ref[0:1, 0:rows_here] = state[...].reshape(1, -1)
    whole_rows = rows_here + -rows_here % LANE
    for c in range(0, whole_rows, LANE):
        state_ref[c : c + LANE, :] = column(line_ref[0:1, c : c + LANE])

    def body(g, carry):
        rows = pl.ds(pl.multiple_of(g * SUB, SUB), SUB)
        square = 0.0
        for ref, block0, blocks, first in source:
            for b in range(blocks):
                value = ref[first + g * blocks + b].astype(F32)
                grad_ref[rows, (block0 + b) * LANE : (block0 + b + 1) * LANE] = value
                square = square + (value * value + 1e-30)
        mean = jnp.sum(square, axis=1, keepdims=True) * (1.0 / width)
        row_new = DECAY * state_ref[rows, :] + (1.0 - DECAY) * mean
        new_ref[rows, :] = row_new
        for ref, block0, blocks, first in source:
            for b in range(blocks):
                lanes = slice((block0 + b) * LANE, (block0 + b + 1) * LANE)
                value = ref[first + g * blocks + b].astype(F32)
                step = value * lax.rsqrt(row_new * scaled[:, lanes])
                new[rows, lanes] = weight[rows, lanes] - rate * step
        return carry

    lax.fori_loop(0, rows_here // SUB, body, 0, unroll=5)
    for c in range(0, whole_rows, LANE):
        line_ref[0:1, c : c + LANE] = jnp.transpose(new_ref[c : c + LANE, :])[0:1, :]
    row_new_ref[...] = line_ref[0:1, 0:rows_here].reshape(-1)


def update_kernel(rows, copies_of, place_ref, mine_ref, other_ref, pack_ref, *refs):
    weights, states, col_states = refs[0:2], refs[2:4], refs[4:6]
    grads, news, rows_new, cols_new = refs[6:8], refs[8:10], refs[10:12], refs[12:14]
    full1_ref, full2_ref, sem = refs[17:20]
    both = (mine_ref, other_ref)
    count = 2 * mine_ref.shape[0]
    copies = load_full(both, place_ref, 0, full1_ref, sem, 0)
    copies += load_full(both, place_ref, full1_ref.shape[0] // count, full2_ref, sem, count)
    run_copies(copies)
    from1 = sources_of(CHUNKS[0], full1_ref, rows)
    from2 = sources_of(CHUNKS[1], full2_ref, rows)
    for n, (k, source) in enumerate(((1, [from1[1], from2[1]]), (2, [from1[2]]))):
        squares = pack_ref[2:3, LANE0[k] : LANE0[k] + WIDTHS[k]]
        update_weight(
            k, squares, pack_ref[3:4, k : k + 1] * (1.0 / copies_of), source, weights[n],
            states[n], col_states[n], grads[n], news[n], rows_new[n], cols_new[n], refs[14:17],
        )


def update_in_kernel(
    rows, copies_of, place_ref, got_ref, pack_in_ref, pack_ref, np_ref, second_ref, *refs
):
    weight, state, col_state, grad_ref, new_ref, row_new_ref, col_new_ref = refs[0:7]
    ngrad_ref, nsecond_ref, nnew_ref = refs[7:10]
    full_ref, sem = refs[13:15]
    copies = load_full((got_ref,), place_ref, 0, full_ref, sem, 0)
    for copy in copies:
        copy.start()
    grad = pack_in_ref[0:2, :]
    second = DECAY * second_ref[...] + (1.0 - DECAY) * (grad * grad + 1e-30)
    ngrad_ref[...] = grad
    nsecond_ref[...] = second
    nnew_ref[...] = np_ref[...] - 0.2 * grad * lax.rsqrt(second)
    for copy in copies:
        copy.wait()
    update_weight(
        0, pack_in_ref[2:3, 0:INNER], pack_ref[3:4, 0:1] * (1.0 / copies_of),
        [sources_of(CHUNKS[2], full_ref, rows)[0]], weight, state, col_state, grad_ref, new_ref,
        row_new_ref, col_new_ref, refs[10:13],
    )


def sources_of(chunk, ref, rows):
    return {w: (ref, block0, blocks, first) for w, block0, blocks, first, _ in spans(chunk, rows)[0]}


class Places:
    def __init__(self):
        self.seq, self.fsdp = lax.axis_size("seq"), lax.axis_size("fsdp")
        self.q = lax.axis_index("fsdp")
        self.s = lax.axis_index("seq")

    def flip(self, x, axis, bit):
        pairs = []
        for s in range(self.seq):
            for f in range(self.fsdp):
                s2, f2 = (s ^ bit, f) if axis == "seq" else (s, f ^ bit)
                pairs.append((s * self.fsdp + f, s2 * self.fsdp + f2))
        return lax.ppermute(x, AXES, pairs)


def bits_of(count):
    return [1 << k for k in range(count.bit_length() - 1)]


def tie(x, *others):
    return lax.optimization_barrier((x, *others))[0]


def gather_pieces(piece, place, after, later=()):
    found = {0: piece}
    for bit in reversed(bits_of(place.fsdp)):
        for k in list(found):
            moving = found[k]
            if bit == 1:
                moving = tie(moving, *((after,) if k == 0 or not later else later))
            found[k | bit] = place.flip(moving, "fsdp", bit)
    return [found[k] for k in range(place.fsdp)]


def sum_over(x, place, *axes):
    for axis in axes:
        for bit in bits_of(getattr(place, axis)):
            x = x + place.flip(x, axis, bit)
    return x


def pick(x, index, axis):
    return lax.dynamic_index_in_dim(x, index, axis=axis, keepdims=False)


class Reduction:
    def __init__(self, place, keep, send):
        self.place, self.near = place, keep
        self.got = place.flip(send, "fsdp", 1)

    def halve(self, axis, side, flip_axis, bit):
        dims = self.near.shape
        parts = dims[:axis] + (2, dims[axis] // 2) + dims[axis + 1 :]
        near, got = self.near.reshape(parts), self.got.reshape(parts)
        away = pick(near, 1 - side, axis).astype(F32) + pick(got, 1 - side, axis).astype(F32)
        self.near = pick(near, side, axis).astype(F32) + pick(got, side, axis).astype(F32)
        away = away.astype(BF16)
        self.got = self.place.flip(away, flip_axis, bit)
        return away

    def x(self):
        bit = self.place.fsdp // 2
        while bit > 1:
            away = self.halve(0, (self.place.q // bit) % 2, "fsdp", bit)
            bit //= 2
        return away

    def y(self):
        return self.halve(1, self.place.s % 2, "seq", 1)

    def pieces(self):
        total = (self.near + self.got.astype(F32)).astype(BF16)
        return total.reshape((self.place.seq // 2, -1) + total.shape[2:])

    def all_pieces(self):
        total = (self.near + self.got.astype(F32)).astype(BF16)
        total = total.reshape((2, self.place.seq // 2, -1) + total.shape[2:])
        return jnp.swapaxes(total, 0, 1).reshape((self.place.seq,) + total.shape[2:])


def arrive(result, *reductions):
    result, *gots = lax.optimization_barrier((result, *[r.got for r in reductions]))
    for reduction, got in zip(reductions, gots):
        reduction.got = got
    return result


def summed(got):
    return jnp.sum(got.astype(F32), axis=0).astype(BF16)


def exchange_all(sent):
    return lax.all_to_all(sent, "seq", 0, 0)


def exchange(place, sent):
    line = [[y + 2 * z for z in range(place.seq // 2)] for y in range(2)]
    return lax.all_to_all(sent, "seq", 0, 0, axis_index_groups=line)


def copies_for(count, part):
    return jnp.broadcast_to(part[None], (count,) + part.shape)


def on_device(
    tokens, input_mask, doc_lengths, cotangent, w_in, w_conv, w_out, norm_params,
    row_in, col_in, row_conv, col_conv, row_out, col_out, norm_second,
):
    place = Places()
    rows = tokens.shape[0]
    pieces = place.fsdp
    spots = jnp.stack(
        [place.q, (place.s * place.fsdp + place.q) * rows, place.s, place.seq]
    ).astype(jnp.int32)
    docs = doc_lengths.shape[0]
    live = input_mask.reshape(-1, LANE)
    weights = (w_in, w_conv, w_out)
    rows_of = [w.shape[0] for w in weights]

    tile_a, tile = 256, 512
    steps = rows // tile
    params_spec = whole(2, D + 2 * INNER)
    dma = pltpu.SemaphoreType.DMA

    out_sides = (w_out[:, : D // 2], w_out[:, D // 2 :])
    conv_out = jnp.concatenate([w_conv, *out_sides], axis=0).astype(BF16)
    hidden_a, slope_a, xhat_a, rstd_a = call(
        norm_a_kernel,
        (rows // tile_a,),
        [rows_spec(tile_a, D), params_spec],
        [rows_spec(tile_a, D)] * 3 + [rows_spec(tile_a, 1)],
        [shape((rows, D), BF16)] * 3 + [shape((rows, 1), F32)],
        us=17,
    )(tokens, tie(norm_params, conv_out))

    in_pieces = gather_pieces(w_in.astype(BF16), place, hidden_a)

    def in_call(tiles, count, before):
        at, stride = tiles

        def here_spec(width):
            return pl.BlockSpec((tile, width), lambda i: (at + stride * i, 0))

        out_shapes = [shape((rows, INNER), BF16)] * 3 + [shape((rows, 1), F32), shape((rows, 8), F32)]
        out_specs = [here_spec(INNER)] * 3 + [here_spec(1), here_spec(8)]
        if at == 0:
            out_shapes += [shape((REACH, INNER), BF16)] * 2
            out_specs += [whole(REACH, INNER)] * 2
        return call(
            functools.partial(in_kernel, pieces, tiles),
            (count,),
            [SMEM, whole(docs), here_spec(D), whole(*live.shape), params_spec]
            + [ANY] * (pieces + len(before)),
            out_specs,
            out_shapes,
            [pltpu.VMEM((D, INNER), BF16), pltpu.VMEM((tile, INNER), F32)]
            + [pltpu.VMEM((8, docs + -docs % LANE), F32), dma((pieces,))],
            us=8,
            aliases={5 + pieces + k: k for k in range(len(before))},
        )(spots, doc_lengths, hidden_a, live, norm_params, *in_pieces, *before)

    *kept, m_first, m_last = in_call((0, steps - 1), 2, ())
    moved, slope_b, xhat_b, rstd_b, masks = in_call((1, 1), steps - 2, kept)

    total = place.seq * place.fsdp
    up = [(i, i + 1) for i in range(total - 1)]
    down = [(i + 1, i) for i in range(total - 1)]
    m_low, m_high = lax.ppermute(m_last, AXES, up), lax.ppermute(m_first, AXES, down)
    conv_pieces = gather_pieces(conv_out, place, m_first, (moved, m_low, m_high))

    ext = pltpu.VMEM((rows + 2 * REACH, INNER), BF16)
    taps_wide = KERNEL_TAPS * INNER
    wide = pltpu.VMEM((taps_wide, INNER), BF16)
    shards = place.fsdp // 2

    def half_dims(chunk):
        count = spans(chunk, rows_of)[1]
        return (shards, count + -count % place.seq, SUB, LANE)

    def tile_spec(width, ahead):
        return pl.BlockSpec((tile, width), lambda i: (jnp.clip(i + ahead, 0, steps - 1), 0))

    halves = [half_dims(CHUNKS[0])] * 2 + [half_dims(CHUNKS[1])] * 2
    work = pltpu.VMEM((tile, INNER), F32)
    turned_tile = pltpu.VMEM((INNER, tile), BF16)
    hidden_c, d_conv, d_first, d_last, sums_c, turned, keep1, send1, keep2, send2 = call(
        functools.partial(conv_kernel, pieces, rows_of),
        (steps + 1,),
        [SMEM, ANY, ANY, ANY, tile_spec(8, 0), tile_spec(D, 0), tile_spec(D, -1), params_spec]
        + [ANY] * pieces,
        [tile_spec(INNER, 0)] * 2
        + [whole(REACH, INNER), whole(REACH, INNER), whole(2, INNER)]
        + [ANY] * 5,
        [
            shape((rows, INNER), BF16),
            shape((rows, INNER), BF16),
            shape((REACH, INNER), BF16),
            shape((REACH, INNER), BF16),
            shape((2, INNER), F32),
            shape((taps_wide, INNER), BF16),
        ]
        + [shape(dims, BF16) for dims in halves],
        [ext, wide, wide, pltpu.VMEM((INNER, D), BF16), pltpu.VMEM((D, INNER), BF16)]
        + [pltpu.VMEM((2, tile, taps_wide), BF16), work, work, work, turned_tile, turned_tile]
        + [pltpu.VMEM((INNER, taps_wide), F32), pltpu.VMEM((INNER, D), F32)]
        + [pltpu.VMEM((16, INNER), F32)]
        + [pltpu.VMEM((2,) + halves[0], BF16), pltpu.VMEM((2,) + halves[2], BF16)]
        + [dma((3 + 3 * pieces,))],
        us=45,
    )(
        spots, m_low, moved, m_high, masks, cotangent, cotangent, norm_params, *conv_pieces
    )
    d_low, d_high = lax.ppermute(d_last, AXES, up), lax.ppermute(d_first, AXES, down)
    first, second = Reduction(place, keep1, send1), Reduction(place, keep2, send2)
    (block_out,) = call(
        functools.partial(out_kernel, pieces),
        (steps,),
        [SMEM, rows_spec(tile, INNER), rows_spec(tile, D)] + [ANY] * pieces,
        [rows_spec(tile, D)],
        [shape((rows, D), BF16)],
        [pltpu.VMEM((INNER, D), BF16), dma((2 * pieces,))],
        us=9,
    )(spots, hidden_c, tokens, *conv_pieces)

    def back_conv(at, count, spots, before):
        def here_spec(width):
            return pl.BlockSpec((tile, width), lambda i: (i + at, 0))

        dims = half_dims(CHUNKS[2])
        last = at + count == steps
        return call(
            functools.partial(back_conv_kernel, at, rows, w_in.shape[0]),
            (count,),
            [SMEM] + [ANY] * 4
            + [here_spec(8), here_spec(INNER), here_spec(1), here_spec(INNER)]
            + [params_spec]
            + [ANY] * (last + len(before)),
            [here_spec(INNER), whole(2, INNER)] + [ANY] * (2 * last),
            [shape((rows, INNER), BF16), shape((2, INNER), F32)] + [shape(dims, BF16)] * (2 * last),
            (
                [
                    pltpu.VMEM((2,) + dims, BF16),
                    pltpu.VMEM((rows, INNER), BF16),
                    pltpu.VMEM((rows, D), BF16),
                    pltpu.VMEM((INNER, D), F32),
                ]
                if last
                else []
            )
            + [
                pltpu.VMEM((count * tile + 2 * REACH, INNER), BF16),
                wide,
                pltpu.VMEM((tile, taps_wide), BF16),
                pltpu.VMEM((tile, INNER), F32),
                pltpu.VMEM((16, INNER), F32),
                dma((6,)),
            ],
            us=7 * count + 6 * last,
            aliases={10 + last: 0} if before else None,
        )(
            spots, d_low, d_conv, d_high, turned, masks, xhat_b, rstd_b, slope_b, norm_params,
            *([hidden_a] if last else []), *before,
        )

    row_states, col_states = (row_in, row_conv, row_out), (col_in, col_conv, col_out)
    row_specs = [whole(*r.shape) for r in row_states]
    col_specs = [whole(*c.shape) for c in col_states]
    cols_all = D + 2 * INNER
    pack_spec, pack_shape = whole(4, cols_all), shape((4, cols_all), F32)
    fulls = [pltpu.VMEM(half_dims(c)[1:], BF16) for c in CHUNKS]

    block_out = arrive(block_out, first, second)
    away = (first.x(), second.y())
    d_pre, sums_b0 = back_conv(0, steps - 2, tie(spots, *away), ())
    d_pre = arrive(d_pre, first, second)
    away = (first.y(), second.x())
    d_pre, sums_b1 = back_conv(steps - 2, 1, tie(spots, *away), (d_pre,))
    d_pre = arrive(d_pre, first, second)
    sent = jnp.concatenate([first.pieces(), second.pieces()], axis=1)
    got = exchange(place, sent)
    d_pre, sums_b2, keep, send = back_conv(steps - 1, 1, tie(spots, sent), (d_pre,))
    got, send = lax.optimization_barrier((got, send))
    third = Reduction(place, keep, send)
    part = summed(got)
    sent = copies_for(place.seq // 2, part)
    mine = exchange(place, sent)
    third.got = tie(third.got, sent)
    away = third.x()
    (pack,) = call(
        functools.partial(pack_kernel, rows_of, [half_dims(c)[1] // place.seq for c in CHUNKS]),
        (1,),
        [SMEM, whole(*part.shape)] + row_specs,
        [pack_spec],
        [pack_shape],
        [pltpu.VMEM((cols_all // LANE + 1, SUB, LANE), F32)],
        us=1,
    )(tie(spots, away), part, *row_states)
    core_sum = pack + place.flip(pack, "fsdp", 1)

    input_grad, sums_a = call(
        functools.partial(back_a_kernel, pieces),
        (steps,),
        [SMEM, rows_spec(tile, INNER), rows_spec(tile, D), rows_spec(tile, 1)]
        + [rows_spec(tile, D)] * 2
        + [params_spec]
        + [ANY] * pieces,
        [rows_spec(tile, D), whole(2, D)],
        [shape((rows, D), F32), shape((2, D), F32)],
        [
            pltpu.VMEM((D, INNER), BF16),
            pltpu.VMEM((INNER, D), BF16),
            pltpu.VMEM((tile, D), F32),
            pltpu.VMEM((16, D), F32),
            dma((pieces,)),
        ],
        us=17,
    )(
        tie(spots, core_sum), d_pre, xhat_a, rstd_a, slope_a, cotangent, norm_params, *in_pieces
    )
    pack = core_sum
    for bit in bits_of(place.fsdp)[1:]:
        flipped = place.flip(pack, "fsdp", bit)
        pack = pack + (tie(flipped, input_grad) if bit == 2 else flipped)
    mine, third.got, input_grad, pack = lax.optimization_barrier(
        (mine, third.got, input_grad, pack)
    )
    other = place.flip(mine, "seq", 1)
    got = exchange_all(third.all_pieces())
    sums = (sums_a, sums_b0, sums_b1, sums_b2, sums_c)
    (pack,) = call(
        pack_norms_kernel,
        (1,),
        [pack_spec] + [whole(*x.shape) for x in sums],
        [pack_spec],
        [pack_shape],
        us=1,
    )(pack, *sums)
    seq_bits = bits_of(place.seq)
    for bit in seq_bits[:-1]:
        pack = pack + place.flip(pack, "seq", bit)
    got, pack = lax.optimization_barrier((got, pack))
    got_in = exchange_all(copies_for(place.seq, summed(got)))
    pack = pack + place.flip(pack, "seq", seq_bits[-1])
    other, pack = lax.optimization_barrier((other, pack))

    def update_scratch(weights):
        lines = max(w.shape[0] + -w.shape[0] % LANE for w in weights)
        return [pltpu.VMEM((8, lines), F32)] + [pltpu.VMEM((lines, LANE), F32)] * 2

    weight_specs = [whole(*w.shape) for w in weights]
    results = call(
        functools.partial(update_kernel, rows_of, place.seq),
        (1,),
        [SMEM, ANY, ANY, pack_spec] + weight_specs[1:] + row_specs[1:] + col_specs[1:],
        weight_specs[1:] * 2 + row_specs[1:] + col_specs[1:],
        [shape(w.shape, F32) for w in weights[1:]] * 2
        + [shape(r.shape, F32) for r in row_states[1:] + col_states[1:]],
        update_scratch(weights[1:]) + fulls[:2] + [dma((2 * place.seq,))],
        us=8,
    )(spots, mine, other, pack, *weights[1:], *row_states[1:], *col_states[1:])
    grad_conv, grad_out, new_conv, new_out, row_conv_new, row_out_new, col_conv_new, col_out_new = (
        results
    )
    got_in, grad_out = lax.optimization_barrier((got_in, grad_out))
    (pack_in,) = call(
        functools.partial(pack_in_kernel, rows_of),
        (1,),
        [SMEM, ANY, pack_spec],
        [pack_spec],
        [pack_shape],
        [fulls[2], dma((place.seq,))],
        us=2,
    )(spots, got_in, pack)
    pack_in = sum_over(pack_in, place, "fsdp")
    grad_in, new_in, row_in_new, col_in_new, *norm_results = call(
        functools.partial(update_in_kernel, rows_of, place.seq),
        (1,),
        [SMEM, ANY, pack_spec, pack_spec, params_spec, params_spec]
        + [weight_specs[0], row_specs[0], col_specs[0]],
        [weight_specs[0]] * 2 + [row_specs[0], col_specs[0]] + [params_spec] * 3,
        [shape(w_in.shape, F32)] * 2
        + [shape(row_in.shape, F32), shape(col_in.shape, F32)]
        + [shape((2, cols_all), F32)] * 3,
        update_scratch(weights[:1]) + [fulls[2], dma((place.seq,))],
        us=4,
    )(spots, got_in, pack_in, pack, norm_params, norm_second, w_in, row_in, col_in)
    return (
        block_out,
        input_grad,
        grad_in,
        grad_conv,
        grad_out,
        new_in,
        new_conv,
        new_out,
        row_in_new,
        col_in_new,
        row_conv_new,
        col_conv_new,
        row_out_new,
        col_out_new,
        *norm_results,
    )


def solution(mesh):
    both, rows = P(AXES, None), P("fsdp", None)
    in_specs = (
        both, P(AXES), P(), both, rows, rows, rows, P(),
        P("fsdp"), P(), P("fsdp"), P(), P("fsdp"), P(), P(),
    )
    out_specs = (
        both, both, rows, rows, rows, rows, rows, rows,
        P("fsdp"), P(), P("fsdp"), P(), P("fsdp"), P(), P(), P(), P(),
    )
    return jax.shard_map(
        on_device, mesh=mesh, in_specs=in_specs, out_specs=out_specs, check_vma=False
    )
```

```python
import functools
import math

import jax
import jax.numpy as jnp
from jax import lax
from jax.experimental import pallas as pl
from jax.experimental.pallas import tpu as pltpu
from jax.sharding import PartitionSpec as P

D = 1280
INNER = 640
KERNEL_TAPS = 5
DILATION_STEP = 128
STEP = 10
EPSILON = 1e-05
DECAY = 1.0 - STEP ** (-0.8)

REACH = (KERNEL_TAPS - 1) // 2 * DILATION_STEP
MID = (KERNEL_TAPS - 1) // 2
F32 = jnp.float32
BF16 = jnp.bfloat16
SUB, LANE = 16, 128
AXES = ("seq", "fsdp")
NT = (((1,), (1,)), ((), ()))
TN = (((0,), (0,)), ((), ()))
NN = (((1,), (0,)), ((), ()))
VMEM_LIMIT = 58 * 1024 * 1024


def call(kernel, grid, in_specs, out_specs, out_shape, scratch=(), us=1.0, aliases=None):
    params = pltpu.CompilerParams(
        vmem_limit_bytes=VMEM_LIMIT, dimension_semantics=("arbitrary",) * len(grid)
    )
    return pl.pallas_call(
        kernel,
        grid=grid,
        in_specs=in_specs,
        out_specs=out_specs,
        out_shape=out_shape,
        scratch_shapes=list(scratch),
        compiler_params=params,
        input_output_aliases=aliases or {},
        cost_estimate=pl.CostEstimate(
                flops=int(us * 1e8), bytes_accessed=int(us * 3e5), transcendentals=0
        ),
    )


def shape(dims, dtype):
    return jax.ShapeDtypeStruct(dims, dtype)


def rows_spec(tile, width):
    return pl.BlockSpec((tile, width), lambda i: (i, 0))


def whole(*dims):
    return pl.BlockSpec(dims, lambda *_: (0,) * len(dims))


ANY = pl.BlockSpec(memory_space=pl.ANY)
SMEM = pl.BlockSpec(memory_space=pltpu.SMEM)


ERFC_P = 0.47 / math.sqrt(2.0)
ERFC_C = (
    0.12357219400743558,
    0.1999878668208835,
    -0.08033356004356296,
    0.3660253986657854,
    -0.1092519747040215,
)
LOG2E = 1.4426950408889634


def gelu_and_slope(y):
    t = pltpu.reciprocal(1.0 + ERFC_P * jnp.abs(y), approx=True)
    bell = jnp.exp2(y * y * (-0.5 * LOG2E))
    poly = ERFC_C[4] * t + ERFC_C[3]
    for c in ERFC_C[2::-1]:
        poly = poly * t + c
    tail = poly * t * bell
    cdf = jnp.where(y > 0.0, 1.0 - tail, tail)
    return y * cdf, cdf + y * (bell * (1.0 / math.sqrt(2.0 * math.pi)))


def lane_blocks(width):
    return [slice(k, k + LANE) for k in range(0, width, LANE)]


def row_stats(ref, rows):
    width = ref.shape[-1]
    blocks = lane_blocks(width)
    total = ref[rows, blocks[0]].astype(F32)
    for b in blocks[1:]:
        total = total + ref[rows, b].astype(F32)
    mean = jnp.sum(total, axis=-1, keepdims=True) * (1.0 / width)
    square = None
    for b in blocks:
        centered = ref[rows, b].astype(F32) - mean
        square = centered * centered if square is None else square + centered * centered
    variance = jnp.sum(square, axis=-1, keepdims=True) * (1.0 / width)
    return mean, lax.rsqrt(variance + EPSILON)


def fold(values):
    total = values[0:8]
    for k in range(8, values.shape[0], 8):
        total = total + values[k : k + 8]
    return total


def in_stages(count, stages, between=()):
    chunks = [slice(k, k + CHUNK) for k in range(0, count, CHUNK)]
    kept, rounds = {}, len(chunks) + len(stages) - 1
    for t in range(rounds):
        for n, stage in enumerate(stages):
            if 0 <= t - n < len(chunks):
                kept[n, t - n] = stage(chunks[t - n], kept.get((n - 1, t - n)))
        for work in between[t * len(between) // rounds : (t + 1) * len(between) // rounds]:
            work()


def halves_of(count):
    return (slice(0, count // 2), slice(count // 2, count))


def row_means(sums, width):
    return [jnp.sum(x, axis=-1, keepdims=True) * (1.0 / width) for x in sums]


def norm_back(rows, dxhat_ref, xhat_ref, means, put):
    mean_d, mean_dx, rstd = means
    for b in lane_blocks(dxhat_ref.shape[-1]):
        xhat = xhat_ref[rows, b].astype(F32)
        put(b, (dxhat_ref[rows, b] - mean_d - xhat * mean_dx) * rstd)


def add_terms(acc_ref, b, dy, xhat):
    acc_ref[0:8, b] += fold(dy * xhat)
    acc_ref[8:16, b] += fold(dy)


def open_sums(acc_ref):
    @pl.when(pl.program_id(0) == 0)
    def _():
        acc_ref[...] = jnp.zeros_like(acc_ref)


def close_sums(out_ref, acc_ref):
    @pl.when(pl.program_id(0) == pl.num_programs(0) - 1)
    def _():
        out_ref[0:1, :] = jnp.sum(acc_ref[0:8, :], axis=0, keepdims=True)
        out_ref[1:2, :] = jnp.sum(acc_ref[8:16, :], axis=0, keepdims=True)


def run_copies(copies):
    for copy in copies:
        copy.start()
    for copy in copies:
        copy.wait()


def piece_copies(pieces, full_ref, me, sem, first=0):
    each = full_ref.shape[0] // len(pieces)
    return [
        pltpu.make_async_copy(
            piece.at[0:each, :],
            full_ref.at[pl.ds(pl.multiple_of((me ^ k) * each, SUB), each), :],
            sem.at[first + k],
        )
        for k, piece in enumerate(pieces)
    ]


def out_copies(pieces, full_ref, me, sem, first=0):
    each, width = full_ref.shape[0] // len(pieces), full_ref.shape[1] // 2
    copies = []
    for k, piece in enumerate(pieces):
        rows = pl.ds(pl.multiple_of((me ^ k) * each, SUB), each)
        for side in range(2):
            at = piece.shape[0] - (2 - side) * each
            copies.append(
                pltpu.make_async_copy(
                    piece.at[at : at + each, :],
                    full_ref.at[rows, side * width : (side + 1) * width],
                    sem.at[first + 2 * k + side],
                )
            )
    return copies


def column(row):
    return jnp.transpose(jnp.broadcast_to(row, (LANE, LANE)))


CHUNK = 64


def norm_a_kernel(tok_ref, np_ref, hid_ref, slope_ref, xhat_ref, rstd_ref):
    def stats(rows, _):
        mean, rstd = row_stats(tok_ref, rows)
        rstd_ref[rows, :] = rstd
        return mean, rstd

    def work(rows, kept):
        mean, rstd = kept
        for b in lane_blocks(D):
            xhat = (tok_ref[rows, b].astype(F32) - mean) * rstd
            hidden, slope = gelu_and_slope(xhat * np_ref[0:1, b] + np_ref[1:2, b])
            hid_ref[rows, b] = hidden.astype(BF16)
            slope_ref[rows, b] = slope.astype(BF16)
            xhat_ref[rows, b] = xhat.astype(BF16)

    in_stages(tok_ref.shape[0], [stats, work])


def running_ends(ends_ref, lengths_ref):
    docs, width = lengths_ref.shape[0], ends_ref.shape[1]
    ends_ref[...] = jnp.zeros_like(ends_ref)
    ends_ref[0:1, 0:docs] = lengths_ref[...].reshape(1, -1).astype(F32)
    before = jnp.zeros((1, 1), F32)
    row = lax.broadcasted_iota(jnp.int32, (LANE, LANE), 0)
    lane = lax.broadcasted_iota(jnp.int32, (LANE, LANE), 1)
    for k in range(0, width, LANE):
        line = ends_ref[0:1, k : k + LANE]
        sums = jnp.sum(jnp.where(row <= lane, column(line), 0.0), axis=0, keepdims=True) + before
        ends_ref[0:1, k : k + LANE] = jnp.where(lane[0:1] + k < docs, sums, 1e9)
        before = before + jnp.sum(line, axis=1, keepdims=True)


def in_kernel(pieces, tiles, place_ref, lengths_ref, hid_ref, live_ref, np_ref, *refs):
    piece_refs = refs[:pieces]
    edges = tiles[0] == 0
    outs = refs[-(11 if edges else 9) :]
    mov_ref, slope_ref, xhat_ref, rstd_ref, mask_ref = outs[:5]
    w_ref, pre_ref, ends_ref, sem = outs[-4:]
    step = pl.program_id(0)
    tile = hid_ref.shape[0]

    @pl.when(step == 0)
    def _():
        copies = piece_copies(piece_refs, w_ref, place_ref[0], sem)
        for copy in copies:
            copy.start()
        running_ends(ends_ref, lengths_ref)
        for copy in copies:
            copy.wait()

    for half in halves_of(tile):
        pre_ref[half, :] = lax.dot_general(
            hid_ref[half, :], w_ref[...], NN, preferred_element_type=F32
        )

    at_tile = tiles[0] + step * tiles[1]
    first = place_ref[1] + at_tile * tile
    ends = ends_ref[0:1, :]
    lanes = lax.broadcasted_iota(jnp.int32, (LANE, 8), 1)
    offsets = ((lanes - MID) * DILATION_STEP).astype(F32)
    for k in range(tile // LANE):
        at = (first + k * LANE + lax.broadcasted_iota(jnp.int32, (LANE, 1), 0)).astype(F32)
        begin = jnp.max(jnp.where(ends <= at, ends, 0.0), axis=1, keepdims=True)
        end = jnp.min(jnp.where(ends > at, ends, 1e9), axis=1, keepdims=True)
        there = at + offsets
        same = jnp.where((there >= begin) & (there < end), 1.0, 0.0)
        live = column(live_ref[pl.ds(at_tile * (tile // LANE) + k, 1), :].astype(F32))
        mask_ref[k * LANE : (k + 1) * LANE, :] = jnp.where(lanes == MID, live[:, 0:8], same)

    def stats(rows, _):
        mean, rstd = row_stats(pre_ref, rows)
        rstd_ref[rows, :] = rstd
        return mean, rstd

    def work(rows, kept):
        mean, rstd = kept
        live = mask_ref[rows, MID : MID + 1]
        for b in lane_blocks(INNER):
            gains = slice(D + b.start, D + b.stop)
            xhat = (pre_ref[rows, b] - mean) * rstd
            hidden, slope = gelu_and_slope(xhat * np_ref[0:1, gains] + np_ref[1:2, gains])
            mov_ref[rows, b] = (hidden * live).astype(BF16)
            slope_ref[rows, b] = slope.astype(BF16)
            xhat_ref[rows, b] = xhat.astype(BF16)

    in_stages(tile, [stats, work])
    if edges:
        first_ref, last_ref = outs[5:7]

        @pl.when(step == 0)
        def _():
            first_ref[...] = mov_ref[0:REACH, :]

        @pl.when(step == 1)
        def _():
            last_ref[...] = mov_ref[tile - REACH :, :]


def load_window(low, mid, high, ext_ref, sem):
    rows = mid.shape[0]
    return [
        pltpu.make_async_copy(low, ext_ref.at[0:REACH, :], sem.at[0]),
        pltpu.make_async_copy(mid, ext_ref.at[REACH : REACH + rows, :], sem.at[1]),
        pltpu.make_async_copy(high, ext_ref.at[REACH + rows : 2 * REACH + rows, :], sem.at[2]),
    ]


def fill_taps(taps_ref, ext_ref, mask_ref, start):
    tile = taps_ref.shape[0]
    for j in range(KERNEL_TAPS):
        rows = pl.ds(pl.multiple_of(start + j * DILATION_STEP, DILATION_STEP), tile)
        picked = ext_ref[rows, :]
        if j != MID:
            picked = picked * mask_ref[:, j : j + 1].astype(BF16)
        taps_ref[:, j * INNER : (j + 1) * INNER] = picked


def conv_kernel(
    pieces, rows_of, place_ref, low_ref, mov_ref, high_ref, mask_ref, cot_ref, before_ref, np_ref, *refs
):
    piece_refs = refs[:pieces]
    hid_ref, dconv_ref, first_ref, last_ref, sums_ref, turned_ref = refs[pieces : pieces + 6]
    outs = refs[pieces + 6 : pieces + 10]
    ext_ref, wc_ref, wct_ref, wo_ref, wt_ref, taps_ref, pre_ref, dh_ref, xhat_ref = refs[
        pieces + 10 : pieces + 19
    ]
    dt_ref, ht_ref, gc_ref, go_ref, acc_ref, stage1_ref, stage2_ref, sem = refs[pieces + 19 :]
    step, steps = pl.program_id(0), pl.num_programs(0) - 1
    tile = taps_ref.shape[1]
    slot = lax.rem(step, 2)

    @pl.when(step == 0)
    def _():
        me = place_ref[0]
        outs = out_copies(piece_refs, wo_ref, me, sem, 3)
        rest = load_window(low_ref, mov_ref, high_ref, ext_ref, sem)
        rest += piece_copies(piece_refs, wc_ref, me, sem, 3 + 2 * pieces)
        for copy in outs + rest:
            copy.start()
        for ref in (acc_ref, gc_ref, go_ref, dt_ref, ht_ref):
            ref[...] = jnp.zeros_like(ref)
        taps_ref[1] = jnp.zeros_like(taps_ref[1])
        for copy in outs:
            copy.wait()
        for k in range(0, D, 256):
            wt_ref[k : k + 256, :] = jnp.transpose(wo_ref[:, k : k + 256])
        for copy in rest:
            copy.wait()

    def grad_conv(cols):
        def work():
            gc_ref[:, cols] += lax.dot_general(
                dt_ref[...], taps_ref[1 - slot, :, cols], NN, preferred_element_type=F32
            )

        return work

    def grad_out(cols):
        def work():
            go_ref[:, cols] += lax.dot_general(
                ht_ref[...], before_ref[:, cols], NN, preferred_element_type=F32
            )

        return work

    taps_wide = KERNEL_TAPS * INNER
    products = [grad_conv(slice(k, min(k + 768, taps_wide))) for k in range(0, taps_wide, 768)]
    products += [grad_out(slice(k, min(k + 768, D))) for k in range(0, D, 768)]

    @pl.when(step < steps)
    def _():
        fill_taps(taps_ref.at[slot], ext_ref, mask_ref, step * tile)
        pre_ref[...] = lax.dot_general(
            taps_ref[slot], wc_ref[...], NN, preferred_element_type=F32
        )
        dh_ref[...] = lax.dot_general(cot_ref[...], wt_ref[...], NN, preferred_element_type=F32)
        for n in range(2):
            tap = jnp.minimum(2 * step + n, KERNEL_TAPS - 1)
            source = wc_ref[pl.ds(pl.multiple_of(tap * INNER, SUB), INNER), :]
            target = pl.multiple_of((KERNEL_TAPS - 1 - tap) * INNER, SUB)
            wct_ref[pl.ds(target, INNER), :] = jnp.transpose(source)

        def stats(rows, _):
            return row_stats(pre_ref, rows)

        def work(rows, kept):
            mean, rstd = kept
            sums = [0.0, 0.0]
            for b in lane_blocks(INNER):
                gains = slice(D + INNER + b.start, D + INNER + b.stop)
                gain = np_ref[0:1, gains]
                xhat = (pre_ref[rows, b] - mean) * rstd
                hidden, slope = gelu_and_slope(xhat * gain + np_ref[1:2, gains])
                hid_ref[rows, b] = hidden.astype(BF16)
                dy = dh_ref[rows, b] * slope
                add_terms(acc_ref, b, dy, xhat)
                dxhat = dy * gain
                xhat_ref[rows, b] = xhat
                dh_ref[rows, b] = dxhat
                sums = [sums[0] + dxhat, sums[1] + dxhat * xhat]
            return row_means(sums, INNER) + [rstd]

        def finish(rows, means):
            def put(b, value):
                dconv_ref[rows, b] = value.astype(BF16)

            norm_back(rows, dh_ref, xhat_ref, means, put)

        in_stages(tile, [stats, work, finish], products)
        dt_ref[...] = jnp.transpose(dconv_ref[...])
        ht_ref[...] = jnp.transpose(hid_ref[...])

    @pl.when(step == 0)
    def _():
        first_ref[...] = dconv_ref[0:REACH, :]

    @pl.when(step == steps - 1)
    def _():
        last_ref[...] = dconv_ref[tile - REACH :, :]

    @pl.when(step == steps)
    def _():
        copy = pltpu.make_async_copy(wct_ref, turned_ref, sem.at[4])
        copy.start()
        for work in products:
            work()
        core = lax.rem(place_ref[0], 2)
        _, rows_conv, rows_out = rows_of
        stage_turned(stage1_ref, core, gc_ref, rows_conv, 0, slice(0, CUT // LANE))
        first_tiles = rows_conv // SUB * (CUT // LANE)
        stage_plain(stage1_ref, core, go_ref, rows_out, first_tiles)
        copies = stage_copies(stage1_ref, outs[0], outs[1], spans(CHUNKS[0], rows_of)[1], sem, 0)
        for each in copies:
            each.start()
        stage_turned(stage2_ref, core, gc_ref, rows_conv, 0, slice(CUT // LANE, INNER // LANE))
        more = stage_copies(stage2_ref, outs[2], outs[3], spans(CHUNKS[1], rows_of)[1], sem, 2)
        for each in more:
            each.start()
        for each in copies + more + [copy]:
            each.wait()
        sums_ref[0:1, :] = jnp.sum(acc_ref[0:8, :], axis=0, keepdims=True)
        sums_ref[1:2, :] = jnp.sum(acc_ref[8:16, :], axis=0, keepdims=True)


def stage_tiles(stage_ref, core, first_row, rows_each, base, block0, blocks, value):
    for g in range(value.shape[0] // SUB):
        row = first_row + g * SUB
        owner, inside = row // rows_each, row % rows_each // SUB
        side = core ^ (owner % 2)
        for b in range(value.shape[1] // LANE):
            tile = value[g * SUB : (g + 1) * SUB, b * LANE : (b + 1) * LANE]
            at = base + inside * blocks + block0 + b
            stage_ref[side, owner // 2, at] = tile.astype(BF16)


def stage_plain(stage_ref, core, grad_ref, rows_each, base):
    blocks = grad_ref.shape[1] // LANE
    for row in range(0, grad_ref.shape[0], SUB):
        part = grad_ref[row : row + SUB, :]
        stage_tiles(stage_ref, core, row, rows_each, base, 0, blocks, part)


def stage_turned(stage_ref, core, turned_ref, rows_each, base, blocks):
    count = blocks.stop - blocks.start
    for row in range(0, turned_ref.shape[1], LANE):
        for b in range(count):
            at = (blocks.start + b) * LANE
            part = jnp.transpose(turned_ref[at : at + LANE, row : row + LANE].astype(BF16))
            stage_tiles(stage_ref, core, row, rows_each, base, b, count, part)


def stage_copies(stage_ref, keep_ref, send_ref, used, sem, first):
    count = stage_ref.shape[2]
    if used < count:
        dims = stage_ref.shape[:2] + (count - used, SUB, LANE)
        stage_ref[:, :, used:] = jnp.zeros(dims, BF16)
    return [
        pltpu.make_async_copy(stage_ref.at[n], ref, sem.at[first + n])
        for n, ref in enumerate((keep_ref, send_ref))
    ]


def back_conv_kernel(
    at, tokens, rows_in, place_ref, low_ref, d_ref, high_ref, turned_ref, mask_ref, xhat_ref, rstd_ref, slope_ref, np_ref, *refs
):
    ext_ref, wt_ref, taps_ref, dmov_ref, acc_ref, sem = refs[-6:]
    step, steps = pl.program_id(0), pl.num_programs(0)
    tile = taps_ref.shape[0]
    first, rows = at * tile, ext_ref.shape[0] - 2 * REACH
    last = first + rows == tokens
    if last:
        hid_ref, before_ref, dpre_ref, sums_ref, keep_ref, send_ref = refs[:6]
        stage_ref, all_ref, held_ref, grad_ref = refs[6:10]
        gather = [
            pltpu.make_async_copy(before_ref.at[0:first, :], all_ref.at[0:first, :], sem.at[4]),
            pltpu.make_async_copy(hid_ref, held_ref, sem.at[5]),
        ]
    else:
        dpre_ref, sums_ref = refs[at > 0 :][:2]
    open_sums(acc_ref)

    @pl.when(step == 0)
    def _():
        begin, end = max(first - REACH, 0), min(first + rows + REACH, tokens)
        offset = begin - (first - REACH)
        copies = [
            pltpu.make_async_copy(turned_ref, wt_ref, sem.at[0]),
            pltpu.make_async_copy(
                d_ref.at[begin:end, :], ext_ref.at[offset : offset + end - begin, :], sem.at[1]
            ),
        ]
        if first == 0:
            copies.append(pltpu.make_async_copy(low_ref, ext_ref.at[0:REACH, :], sem.at[2]))
        if last:
            target = ext_ref.at[REACH + rows : 2 * REACH + rows, :]
            copies.append(pltpu.make_async_copy(high_ref, target, sem.at[3]))
        for copy in copies:
            copy.start()
        if last:
            for copy in gather:
                copy.start()
        for copy in copies:
            copy.wait()

    fill_taps(taps_ref, ext_ref, mask_ref, step * tile)
    dmov_ref[...] = lax.dot_general(taps_ref[...], wt_ref[...], NN, preferred_element_type=F32)

    def work(rows, _):
        live = mask_ref[rows, MID : MID + 1]
        sums = [0.0, 0.0]
        for b in lane_blocks(INNER):
            xhat = xhat_ref[rows, b].astype(F32)
            dy = dmov_ref[rows, b] * live * slope_ref[rows, b].astype(F32)
            add_terms(acc_ref, b, dy, xhat)
            dxhat = dy * np_ref[0:1, D + b.start : D + b.stop]
            dmov_ref[rows, b] = dxhat
            sums = [sums[0] + dxhat, sums[1] + dxhat * xhat]
        return row_means(sums, INNER) + [rstd_ref[rows, :]]

    def finish(rows, means):
        def put(b, value):
            dpre_ref[rows, b] = value.astype(BF16)

        norm_back(rows, dmov_ref, xhat_ref, means, put)

    in_stages(tile, [work, finish])
    close_sums(sums_ref, acc_ref)
    if last:
        all_ref[pl.ds(first + step * tile, tile), :] = dpre_ref[...]

        @pl.when(step == steps - 1)
        def _():
            for copy in gather:
                copy.wait()
            grad_ref[...] = lax.dot_general(
                all_ref[...], held_ref[...], TN, preferred_element_type=F32
            )
            all_blocks = slice(0, INNER // LANE)
            stage_turned(stage_ref, lax.rem(place_ref[0], 2), grad_ref, rows_in, 0, all_blocks)
            used = rows_in // SUB * (INNER // LANE)
            run_copies(stage_copies(stage_ref, keep_ref, send_ref, used, sem, 0))


def back_a_kernel(pieces, place_ref, dpre_ref, xhat_ref, rstd_ref, slope_ref, cot_ref, np_ref, *refs):
    piece_refs = refs[:pieces]
    grad_ref, sums_ref, w_ref, wt_ref, dh_ref, acc_ref, sem = refs[-7:]
    open_sums(acc_ref)

    @pl.when(pl.program_id(0) == 0)
    def _():
        run_copies(piece_copies(piece_refs, w_ref, place_ref[0], sem))
        for k in range(0, D, 256):
            wt_ref[:, k : k + 256] = jnp.transpose(w_ref[k : k + 256, :])

    dh_ref[...] = lax.dot_general(dpre_ref[...], wt_ref[...], NN, preferred_element_type=F32)

    def work(rows, _):
        sums = [0.0, 0.0]
        for b in lane_blocks(D):
            xhat = xhat_ref[rows, b].astype(F32)
            dy = dh_ref[rows, b] * slope_ref[rows, b].astype(F32)
            add_terms(acc_ref, b, dy, xhat)
            dxhat = dy * np_ref[0:1, b]
            dh_ref[rows, b] = dxhat
            sums = [sums[0] + dxhat, sums[1] + dxhat * xhat]
        return row_means(sums, D) + [rstd_ref[rows, :]]

    def finish(rows, means):
        def put(b, value):
            grad_ref[rows, b] = cot_ref[rows, b].astype(F32) + value

        norm_back(rows, dh_ref, xhat_ref, means, put)

    in_stages(dpre_ref.shape[0], [work, finish])
    close_sums(sums_ref, acc_ref)


def out_kernel(pieces, place_ref, hid_ref, tok_ref, *refs):
    piece_refs = refs[:pieces]
    out_ref, w_ref, sem = refs[pieces:]

    @pl.when(pl.program_id(0) == 0)
    def _():
        run_copies(out_copies(piece_refs, w_ref, place_ref[0], sem))

    branch = lax.dot_general(hid_ref[...], w_ref[...], NN, preferred_element_type=F32)
    out_ref[...] = (tok_ref[...].astype(F32) + branch).astype(BF16)


WIDTHS = (INNER, INNER, D)
LANE0 = (0, INNER, 2 * INNER)
CUT = 2 * LANE
CHUNKS = (((1, 0, CUT), (2, 0, D)), ((1, CUT, INNER - CUT),), ((0, 0, INNER),))


def spans(chunk, rows):
    found, first = [], 0
    for weight, col, cols in chunk:
        tiles = rows[weight] // SUB * (cols // LANE)
        found.append((weight, col // LANE, cols // LANE, first, tiles))
        first += tiles
    return found, first


def column_sums(pack_ref, row, ref, chunk, rows):
    for weight, block0, blocks, first, tiles in spans(chunk, rows)[0]:

        def body(g, carry, first=first, blocks=blocks):
            new = []
            for b in range(blocks):
                value = ref[first + g * blocks + b].astype(F32)
                new.append(carry[b] + fold(value * value + 1e-30))
            return tuple(new)

        zero = tuple(jnp.zeros((8, LANE), F32) for _ in range(blocks))
        cols = lax.fori_loop(0, tiles // blocks, body, zero, unroll=5)
        for b in range(blocks):
            lane = LANE0[weight] + (block0 + b) * LANE
            pack_ref[row : row + 1, lane : lane + LANE] = jnp.sum(cols[b], axis=0, keepdims=True)


def load_full(refs, place_ref, first, full_ref, sem, at):
    pieces = refs[0].shape[0]
    each = full_ref.shape[0] // (len(refs) * pieces)
    outer = pieces if len(refs) == 2 else pieces // 2
    y = place_ref[2] % 2
    copies = []
    for n, (ref, side) in enumerate(zip(refs, (y, 1 - y))):
        for p in range(pieces):
            index = side * outer + p if len(refs) == 2 else p % 2 * outer + p // 2
            target = full_ref.at[pl.ds(index * each, each)]
            source = ref.at[p, first : first + each]
            copies.append(pltpu.make_async_copy(source, target, sem.at[at + n * pieces + p]))
    return copies


def pack_kernel(rows, place_ref, mine_ref, *refs):
    states, (pack_ref, acc_ref) = refs[0:3], refs[3:5]
    pack_ref[...] = jnp.zeros_like(pack_ref)
    lanes = lax.broadcasted_iota(jnp.int32, (1, LANE), 1)
    for k in range(3):
        total = jnp.sum(states[k][...].reshape(1, -1), axis=1, keepdims=True)
        pack_ref[1:2, 0:LANE] += jnp.where(lanes == k, total, 0.0)
    acc_ref[...] = jnp.zeros_like(acc_ref)
    spare = acc_ref.shape[0] - 1
    outer, at = mine_ref.shape[0], 0
    for chunk in CHUNKS[:2]:
        found, count = spans(chunk, rows)
        each = (count + -count % (2 * outer)) // (2 * outer)
        for p in range(outer):
            start = (place_ref[2] % 2 * outer + p) * each

            def body(k, carry, found=found, start=start, at=at, p=p):
                n = start + k
                slot = spare
                for weight, block0, blocks, first, tiles in found:
                    here = lax.rem(jnp.maximum(n - first, 0), blocks)
                    here = LANE0[weight] // LANE + block0 + here
                    slot = jnp.where((n >= first) & (n < first + tiles), here, slot)
                value = mine_ref[p, at + k].astype(F32)
                acc_ref[slot] += value * value + 1e-30
                return carry

            lax.fori_loop(0, each, body, 0, unroll=2)
        at += each
    for slot in range(spare):
        pack_ref[0:1, slot * LANE : (slot + 1) * LANE] = jnp.sum(acc_ref[slot], axis=0, keepdims=True)


def norm_tiles_kernel(parts, *refs):
    sums, out_ref, line_ref = refs[:-2], refs[-2], refs[-1]
    line_ref[...] = jnp.zeros_like(line_ref)
    lanes_of = ((0, D), (D, D + INNER), (D, D + INNER), (D, D + INNER), (D + INNER, D + 2 * INNER))
    for part, (lane0, lane1) in zip(sums, lanes_of):
        line_ref[0:2, lane0:lane1] += part[...]
    out_ref[...] = jnp.zeros_like(out_ref)
    blocks = (D + 2 * INNER) // LANE
    each = -(-2 * blocks // parts)
    for part in range(-(-2 * blocks // each)):
        rows = []
        for n in range(part * each, min((part + 1) * each, 2 * blocks)):
            row, b = n // blocks, n % blocks
            rows.append(line_ref[row : row + 1, b * LANE : (b + 1) * LANE])
        rows += [jnp.zeros((1, LANE), F32)] * (8 - len(rows))
        value = jnp.concatenate(rows, axis=0)
        high = value.astype(BF16).astype(F32)
        out_ref[part] = jnp.concatenate([high, value - high], axis=0).astype(BF16)


def high_low(total):
    value = total[..., 0:8, :] + total[..., 8:16, :]
    high = value.astype(BF16).astype(F32)
    return jnp.concatenate([high, value - high], axis=-2).astype(BF16)


def pack_in_kernel(rows, place_ref, got_ref, out_ref, full_ref, norms_ref, sem, norms_sem):
    parts = got_ref.shape[0]
    each = full_ref.shape[0] // parts
    copies = load_full((got_ref,), place_ref, 0, full_ref, sem, 0)
    copies += [
        pltpu.make_async_copy(got_ref.at[p, each], norms_ref.at[p], norms_sem.at[p])
        for p in range(parts)
    ]
    run_copies(copies)
    out_ref[...] = jnp.zeros_like(out_ref)
    blocks = (D + 2 * INNER) // LANE
    rows_each = -(-2 * blocks // parts)
    for n in range(2 * blocks):
        part, at = n // rows_each, n % rows_each
        value = norms_ref[part].astype(F32)
        row, lane = n // blocks, n % blocks * LANE
        out_ref[row : row + 1, lane : lane + LANE] = value[at : at + 1] + value[8 + at : 9 + at]
    column_sums(out_ref, 2, full_ref, CHUNKS[2], rows)


def update_weight(
    k, squares, states_sum, source, weight, state, col_state, grad_ref, new, row_new_ref, col_new_ref, scratch
):
    line_ref, state_ref, new_ref = scratch
    width, fan, rows_here = WIDTHS[k], (D, KERNEL_TAPS * INNER, INNER)[k], weight.shape[0]
    col_new = DECAY * col_state[...].reshape(1, -1) + (1.0 - DECAY) * (squares * (1.0 / fan))
    col_new_ref[...] = col_new.reshape(-1)
    total = DECAY * states_sum
    total = total + (1.0 - DECAY) * (1.0 / width) * jnp.sum(squares, axis=1, keepdims=True)
    scaled = col_new / (total * (1.0 / fan))
    rate = 0.5 / fan**0.5
    line_ref[0:1, 0:rows_here] = state[...].reshape(1, -1)
    whole_rows = rows_here + -rows_here % LANE
    for c in range(0, whole_rows, LANE):
        state_ref[c : c + LANE, :] = column(line_ref[0:1, c : c + LANE])

    def body(g, carry):
        rows = pl.ds(pl.multiple_of(g * SUB, SUB), SUB)
        square = 0.0
        for ref, block0, blocks, first in source:
            for b in range(blocks):
                value = ref[first + g * blocks + b].astype(F32)
                grad_ref[rows, (block0 + b) * LANE : (block0 + b + 1) * LANE] = value
                square = square + (value * value + 1e-30)
        mean = jnp.sum(square, axis=1, keepdims=True) * (1.0 / width)
        row_new = DECAY * state_ref[rows, :] + (1.0 - DECAY) * mean
        new_ref[rows, :] = row_new
        for ref, block0, blocks, first in source:
            for b in range(blocks):
                lanes = slice((block0 + b) * LANE, (block0 + b + 1) * LANE)
                value = ref[first + g * blocks + b].astype(F32)
                step = value * lax.rsqrt(row_new * scaled[:, lanes])
                new[rows, lanes] = weight[rows, lanes] - rate * step
        return carry

    lax.fori_loop(0, rows_here // SUB, body, 0, unroll=5)
    for c in range(0, whole_rows, LANE):
        line_ref[0:1, c : c + LANE] = jnp.transpose(new_ref[c : c + LANE, :])[0:1, :]
    row_new_ref[...] = line_ref[0:1, 0:rows_here].reshape(-1)


def update_kernel(rows, copies_of, place_ref, mine_ref, other_ref, pack_ref, *refs):
    weights, states, col_states = refs[0:2], refs[2:4], refs[4:6]
    grads, news, rows_new, cols_new = refs[6:8], refs[8:10], refs[10:12], refs[12:14]
    full1_ref, full2_ref, sem = refs[17:20]
    both = (mine_ref, other_ref)
    count = 2 * mine_ref.shape[0]
    copies = load_full(both, place_ref, 0, full1_ref, sem, 0)
    copies += load_full(both, place_ref, full1_ref.shape[0] // count, full2_ref, sem, count)
    run_copies(copies)
    from1 = sources_of(CHUNKS[0], full1_ref, rows)
    from2 = sources_of(CHUNKS[1], full2_ref, rows)
    for n, (k, source) in enumerate(((1, [from1[1], from2[1]]), (2, [from1[2]]))):
        squares = pack_ref[0:1, LANE0[k] : LANE0[k] + WIDTHS[k]]
        update_weight(
            k, squares, pack_ref[1:2, k : k + 1] * (1.0 / copies_of), source, weights[n],
            states[n], col_states[n], grads[n], news[n], rows_new[n], cols_new[n], refs[14:17],
        )


def update_in_kernel(
    rows, copies_of, place_ref, got_ref, pack_in_ref, pack_ref, np_ref, second_ref, *refs
):
    weight, state, col_state, grad_ref, new_ref, row_new_ref, col_new_ref = refs[0:7]
    ngrad_ref, nsecond_ref, nnew_ref = refs[7:10]
    full_ref, sem = refs[13:15]
    copies = load_full((got_ref,), place_ref, 0, full_ref, sem, 0)
    for copy in copies:
        copy.start()
    grad = pack_in_ref[0:2, :]
    second = DECAY * second_ref[...] + (1.0 - DECAY) * (grad * grad + 1e-30)
    ngrad_ref[...] = grad
    nsecond_ref[...] = second
    nnew_ref[...] = np_ref[...] - 0.2 * grad * lax.rsqrt(second)
    for copy in copies:
        copy.wait()
    update_weight(
        0, pack_in_ref[2:3, 0:INNER], pack_ref[1:2, 0:1] * (1.0 / copies_of),
        [sources_of(CHUNKS[2], full_ref, rows)[0]], weight, state, col_state, grad_ref, new_ref,
        row_new_ref, col_new_ref, refs[10:13],
    )


def sources_of(chunk, ref, rows):
    return {w: (ref, block0, blocks, first) for w, block0, blocks, first, _ in spans(chunk, rows)[0]}


class Places:
    def __init__(self):
        self.seq, self.fsdp = lax.axis_size("seq"), lax.axis_size("fsdp")
        self.q = lax.axis_index("fsdp")
        self.s = lax.axis_index("seq")

    def flip(self, x, axis, bit):
        pairs = []
        for s in range(self.seq):
            for f in range(self.fsdp):
                s2, f2 = (s ^ bit, f) if axis == "seq" else (s, f ^ bit)
                pairs.append((s * self.fsdp + f, s2 * self.fsdp + f2))
        return lax.ppermute(x, AXES, pairs)


def bits_of(count):
    return [1 << k for k in range(count.bit_length() - 1)]


def tie(x, *others):
    return lax.optimization_barrier((x, *others))[0]


def gather_pieces(piece, place, after, later=()):
    found = {0: piece}
    for bit in reversed(bits_of(place.fsdp)):
        for k in list(found):
            moving = found[k]
            if bit == 1:
                moving = tie(moving, *((after,) if k == 0 or not later else later))
            found[k | bit] = place.flip(moving, "fsdp", bit)
    return [found[k] for k in range(place.fsdp)]


def sum_over(x, place, *axes):
    for axis in axes:
        for bit in bits_of(getattr(place, axis)):
            x = x + place.flip(x, axis, bit)
    return x


def pick(x, index, axis):
    return lax.dynamic_index_in_dim(x, index, axis=axis, keepdims=False)


class Reduction:
    def __init__(self, place, keep, send):
        self.place, self.near = place, keep
        self.got = place.flip(send, "fsdp", 1)

    def halve(self, axis, side, flip_axis, bit):
        dims = self.near.shape
        parts = dims[:axis] + (2, dims[axis] // 2) + dims[axis + 1 :]
        near, got = self.near.reshape(parts), self.got.reshape(parts)
        away = pick(near, 1 - side, axis).astype(F32) + pick(got, 1 - side, axis).astype(F32)
        self.near = pick(near, side, axis).astype(F32) + pick(got, side, axis).astype(F32)
        away = away.astype(BF16)
        self.got = self.place.flip(away, flip_axis, bit)
        return away

    def x(self):
        bit = self.place.fsdp // 2
        while bit > 1:
            away = self.halve(0, (self.place.q // bit) % 2, "fsdp", bit)
            bit //= 2
        return away

    def y(self):
        return self.halve(1, self.place.s % 2, "seq", 1)

    def pieces(self):
        total = (self.near + self.got.astype(F32)).astype(BF16)
        return total.reshape((self.place.seq // 2, -1) + total.shape[2:])

    def all_pieces(self):
        total = (self.near + self.got.astype(F32)).astype(BF16)
        total = total.reshape((2, self.place.seq // 2, -1) + total.shape[2:])
        return jnp.swapaxes(total, 0, 1).reshape((self.place.seq,) + total.shape[2:])


def arrive(result, *reductions):
    result, *gots = lax.optimization_barrier((result, *[r.got for r in reductions]))
    for reduction, got in zip(reductions, gots):
        reduction.got = got
    return result


def summed_f32(got):
    return jnp.sum(got.astype(F32), axis=0)


def summed(got):
    return summed_f32(got).astype(BF16)


def exchange_all(sent):
    return lax.all_to_all(sent, "seq", 0, 0)


def exchange(place, sent):
    line = [[y + 2 * z for z in range(place.seq // 2)] for y in range(2)]
    return lax.all_to_all(sent, "seq", 0, 0, axis_index_groups=line)


def copies_for(count, part):
    return jnp.broadcast_to(part[None], (count,) + part.shape)


def on_device(
    tokens, input_mask, doc_lengths, cotangent, w_in, w_conv, w_out, norm_params,
    row_in, col_in, row_conv, col_conv, row_out, col_out, norm_second,
):
    place = Places()
    rows = tokens.shape[0]
    pieces = place.fsdp
    spots = jnp.stack(
        [place.q, (place.s * place.fsdp + place.q) * rows, place.s, place.seq]
    ).astype(jnp.int32)
    docs = doc_lengths.shape[0]
    live = input_mask.reshape(-1, LANE)
    weights = (w_in, w_conv, w_out)
    rows_of = [w.shape[0] for w in weights]

    tile_a, tile = 256, 512
    steps = rows // tile
    params_spec = whole(2, D + 2 * INNER)
    dma = pltpu.SemaphoreType.DMA

    out_sides = (w_out[:, : D // 2], w_out[:, D // 2 :])
    conv_out = jnp.concatenate([w_conv, *out_sides], axis=0).astype(BF16)
    hidden_a, slope_a, xhat_a, rstd_a = call(
        norm_a_kernel,
        (rows // tile_a,),
        [rows_spec(tile_a, D), params_spec],
        [rows_spec(tile_a, D)] * 3 + [rows_spec(tile_a, 1)],
        [shape((rows, D), BF16)] * 3 + [shape((rows, 1), F32)],
        us=17,
    )(tokens, tie(norm_params, conv_out))

    in_pieces = gather_pieces(w_in.astype(BF16), place, hidden_a)

    def in_call(tiles, count, before):
        at, stride = tiles

        def here_spec(width):
            return pl.BlockSpec((tile, width), lambda i: (at + stride * i, 0))

        out_shapes = [shape((rows, INNER), BF16)] * 3 + [shape((rows, 1), F32), shape((rows, 8), F32)]
        out_specs = [here_spec(INNER)] * 3 + [here_spec(1), here_spec(8)]
        if at == 0:
            out_shapes += [shape((REACH, INNER), BF16)] * 2
            out_specs += [whole(REACH, INNER)] * 2
        return call(
            functools.partial(in_kernel, pieces, tiles),
            (count,),
            [SMEM, whole(docs), here_spec(D), whole(*live.shape), params_spec]
            + [ANY] * (pieces + len(before)),
            out_specs,
            out_shapes,
            [pltpu.VMEM((D, INNER), BF16), pltpu.VMEM((tile, INNER), F32)]
            + [pltpu.VMEM((8, docs + -docs % LANE), F32), dma((pieces,))],
            us=8,
            aliases={5 + pieces + k: k for k in range(len(before))},
        )(spots, doc_lengths, hidden_a, live, norm_params, *in_pieces, *before)

    *kept, m_first, m_last = in_call((0, steps - 1), 2, ())
    moved, slope_b, xhat_b, rstd_b, masks = in_call((1, 1), steps - 2, kept)

    total = place.seq * place.fsdp
    up = [(i, i + 1) for i in range(total - 1)]
    down = [(i + 1, i) for i in range(total - 1)]
    m_low, m_high = lax.ppermute(m_last, AXES, up), lax.ppermute(m_first, AXES, down)
    conv_pieces = gather_pieces(conv_out, place, m_first, (moved, m_low, m_high))

    ext = pltpu.VMEM((rows + 2 * REACH, INNER), BF16)
    taps_wide = KERNEL_TAPS * INNER
    wide = pltpu.VMEM((taps_wide, INNER), BF16)
    shards = place.fsdp // 2

    def half_dims(chunk):
        count = spans(chunk, rows_of)[1]
        return (shards, count + -count % place.seq, SUB, LANE)

    def tile_spec(width, ahead):
        return pl.BlockSpec((tile, width), lambda i: (jnp.clip(i + ahead, 0, steps - 1), 0))

    halves = [half_dims(CHUNKS[0])] * 2 + [half_dims(CHUNKS[1])] * 2
    work = pltpu.VMEM((tile, INNER), F32)
    turned_tile = pltpu.VMEM((INNER, tile), BF16)
    hidden_c, d_conv, d_first, d_last, sums_c, turned, keep1, send1, keep2, send2 = call(
        functools.partial(conv_kernel, pieces, rows_of),
        (steps + 1,),
        [SMEM, ANY, ANY, ANY, tile_spec(8, 0), tile_spec(D, 0), tile_spec(D, -1), params_spec]
        + [ANY] * pieces,
        [tile_spec(INNER, 0)] * 2
        + [whole(REACH, INNER), whole(REACH, INNER), whole(2, INNER)]
        + [ANY] * 5,
        [
            shape((rows, INNER), BF16),
            shape((rows, INNER), BF16),
            shape((REACH, INNER), BF16),
            shape((REACH, INNER), BF16),
            shape((2, INNER), F32),
            shape((taps_wide, INNER), BF16),
        ]
        + [shape(dims, BF16) for dims in halves],
        [ext, wide, wide, pltpu.VMEM((INNER, D), BF16), pltpu.VMEM((D, INNER), BF16)]
        + [pltpu.VMEM((2, tile, taps_wide), BF16), work, work, work, turned_tile, turned_tile]
        + [pltpu.VMEM((INNER, taps_wide), F32), pltpu.VMEM((INNER, D), F32)]
        + [pltpu.VMEM((16, INNER), F32)]
        + [pltpu.VMEM((2,) + halves[0], BF16), pltpu.VMEM((2,) + halves[2], BF16)]
        + [dma((3 + 3 * pieces,))],
        us=45,
    )(
        spots, m_low, moved, m_high, masks, cotangent, cotangent, norm_params, *conv_pieces
    )
    d_low, d_high = lax.ppermute(d_last, AXES, up), lax.ppermute(d_first, AXES, down)
    first, second = Reduction(place, keep1, send1), Reduction(place, keep2, send2)
    (block_out,) = call(
        functools.partial(out_kernel, pieces),
        (steps,),
        [SMEM, rows_spec(tile, INNER), rows_spec(tile, D)] + [ANY] * pieces,
        [rows_spec(tile, D)],
        [shape((rows, D), BF16)],
        [pltpu.VMEM((INNER, D), BF16), dma((2 * pieces,))],
        us=9,
    )(spots, hidden_c, tokens, *conv_pieces)

    def back_conv(at, count, spots, before):
        def here_spec(width):
            return pl.BlockSpec((tile, width), lambda i: (i + at, 0))

        dims = half_dims(CHUNKS[2])
        last = at + count == steps
        return call(
            functools.partial(back_conv_kernel, at, rows, w_in.shape[0]),
            (count,),
            [SMEM] + [ANY] * 4
            + [here_spec(8), here_spec(INNER), here_spec(1), here_spec(INNER)]
            + [params_spec]
            + [ANY] * (last + len(before)),
            [here_spec(INNER), whole(2, INNER)] + [ANY] * (2 * last),
            [shape((rows, INNER), BF16), shape((2, INNER), F32)] + [shape(dims, BF16)] * (2 * last),
            (
                [
                    pltpu.VMEM((2,) + dims, BF16),
                    pltpu.VMEM((rows, INNER), BF16),
                    pltpu.VMEM((rows, D), BF16),
                    pltpu.VMEM((INNER, D), F32),
                ]
                if last
                else []
            )
            + [
                pltpu.VMEM((count * tile + 2 * REACH, INNER), BF16),
                wide,
                pltpu.VMEM((tile, taps_wide), BF16),
                pltpu.VMEM((tile, INNER), F32),
                pltpu.VMEM((16, INNER), F32),
                dma((6,)),
            ],
            us=7 * count + 6 * last,
            aliases={10 + last: 0} if before else None,
        )(
            spots, d_low, d_conv, d_high, turned, masks, xhat_b, rstd_b, slope_b, norm_params,
            *([hidden_a] if last else []), *before,
        )

    row_states, col_states = (row_in, row_conv, row_out), (col_in, col_conv, col_out)
    row_specs = [whole(*r.shape) for r in row_states]
    col_specs = [whole(*c.shape) for c in col_states]
    cols_all = D + 2 * INNER
    pack_spec, pack_shape = whole(4, cols_all), shape((4, cols_all), F32)
    fulls = [pltpu.VMEM(half_dims(c)[1:], BF16) for c in CHUNKS]

    block_out, d_low, d_high = arrive((block_out, d_low, d_high), first, second)
    away = (first.x(), second.y())
    d_pre, sums_b0 = back_conv(0, steps - 2, tie(spots, *away), ())
    d_pre = arrive(d_pre, first, second)
    away = (first.y(), second.x())
    d_pre, sums_b1 = back_conv(steps - 2, 1, tie(spots, *away), (d_pre,))
    d_pre = arrive(d_pre, first, second)
    sent = jnp.concatenate([first.pieces(), second.pieces()], axis=1)
    got = exchange(place, sent)
    d_pre, sums_b2, keep, send = back_conv(steps - 1, 1, tie(spots, sent), (d_pre,))
    got, send = lax.optimization_barrier((got, send))
    third = Reduction(place, keep, send)
    part = summed(got)
    sent = copies_for(place.seq // 2, part)
    mine = exchange(place, sent)
    third.got = tie(third.got, sent)
    away = third.x()
    input_grad, sums_a = call(
        functools.partial(back_a_kernel, pieces),
        (steps,),
        [SMEM, rows_spec(tile, INNER), rows_spec(tile, D), rows_spec(tile, 1)]
        + [rows_spec(tile, D)] * 2
        + [params_spec]
        + [ANY] * pieces,
        [rows_spec(tile, D), whole(2, D)],
        [shape((rows, D), F32), shape((2, D), F32)],
        [
            pltpu.VMEM((D, INNER), BF16),
            pltpu.VMEM((INNER, D), BF16),
            pltpu.VMEM((tile, D), F32),
            pltpu.VMEM((16, D), F32),
            dma((pieces,)),
        ],
        us=17,
    )(
        tie(spots, away), d_pre, xhat_a, rstd_a, slope_a, cotangent, norm_params, *in_pieces
    )
    sums = (sums_a, sums_b0, sums_b1, sums_b2, sums_c)
    norm_tiles = call(
        functools.partial(norm_tiles_kernel, place.seq),
        (1,),
        [whole(*x.shape) for x in sums],
        whole(place.seq, SUB, LANE),
        shape((place.seq, SUB, LANE), BF16),
        [pltpu.VMEM((8, cols_all), F32)],
        us=1,
    )(*sums)
    mine, third.got, norm_tiles = lax.optimization_barrier((mine, third.got, norm_tiles))
    other = place.flip(mine, "seq", 1)
    sent = jnp.concatenate([third.all_pieces(), norm_tiles[:, None]], axis=1)
    got = exchange_all(sent)
    (pack,) = call(
        functools.partial(pack_kernel, rows_of),
        (1,),
        [SMEM, whole(*mine.shape)] + row_specs,
        [pack_spec],
        [pack_shape],
        [pltpu.VMEM((cols_all // LANE + 1, SUB, LANE), F32)],
        us=2,
    )(tie(spots, sent), mine, *row_states)
    pack = sum_over(pack, place, "fsdp")
    got, pack = lax.optimization_barrier((got, pack))
    part = summed_f32(got)
    part = jnp.concatenate([part[:-1].astype(BF16), high_low(part[-1:])], axis=0)
    got_in = exchange_all(copies_for(place.seq, part))
    pack = pack + place.flip(pack, "seq", 1)
    other, pack = lax.optimization_barrier((other, pack))

    def update_scratch(weights):
        lines = max(w.shape[0] + -w.shape[0] % LANE for w in weights)
        return [pltpu.VMEM((8, lines), F32)] + [pltpu.VMEM((lines, LANE), F32)] * 2

    weight_specs = [whole(*w.shape) for w in weights]
    results = call(
        functools.partial(update_kernel, rows_of, 2),
        (1,),
        [SMEM, ANY, ANY, pack_spec] + weight_specs[1:] + row_specs[1:] + col_specs[1:],
        weight_specs[1:] * 2 + row_specs[1:] + col_specs[1:],
        [shape(w.shape, F32) for w in weights[1:]] * 2
        + [shape(r.shape, F32) for r in row_states[1:] + col_states[1:]],
        update_scratch(weights[1:]) + fulls[:2] + [dma((2 * place.seq,))],
        us=8,
    )(spots, mine, other, pack, *weights[1:], *row_states[1:], *col_states[1:])
    grad_conv, grad_out, new_conv, new_out, row_conv_new, row_out_new, col_conv_new, col_out_new = (
        results
    )
    got_in, grad_out = lax.optimization_barrier((got_in, grad_out))
    (pack_in,) = call(
        functools.partial(pack_in_kernel, rows_of),
        (1,),
        [SMEM, ANY],
        [pack_spec],
        [pack_shape],
        [fulls[2], pltpu.VMEM((place.seq, SUB, LANE), BF16)] + [dma((place.seq,))] * 2,
        us=2,
    )(spots, got_in)
    pack_in = sum_over(pack_in, place, "fsdp")
    grad_in, new_in, row_in_new, col_in_new, *norm_results = call(
        functools.partial(update_in_kernel, rows_of, 2),
        (1,),
        [SMEM, ANY, pack_spec, pack_spec, params_spec, params_spec]
        + [weight_specs[0], row_specs[0], col_specs[0]],
        [weight_specs[0]] * 2 + [row_specs[0], col_specs[0]] + [params_spec] * 3,
        [shape(w_in.shape, F32)] * 2
        + [shape(row_in.shape, F32), shape(col_in.shape, F32)]
        + [shape((2, cols_all), F32)] * 3,
        update_scratch(weights[:1]) + [fulls[2], dma((place.seq,))],
        us=4,
    )(spots, got_in, pack_in, pack, norm_params, norm_second, w_in, row_in, col_in)
    return (
        block_out,
        input_grad,
        grad_in,
        grad_conv,
        grad_out,
        new_in,
        new_conv,
        new_out,
        row_in_new,
        col_in_new,
        row_conv_new,
        col_conv_new,
        row_out_new,
        col_out_new,
        *norm_results,
    )


def solution(mesh):
    both, rows = P(AXES, None), P("fsdp", None)
    in_specs = (
        both, P(AXES), P(), both, rows, rows, rows, P(),
        P("fsdp"), P(), P("fsdp"), P(), P("fsdp"), P(), P(),
    )
    out_specs = (
        both, both, rows, rows, rows, rows, rows, rows,
        P("fsdp"), P(), P("fsdp"), P(), P("fsdp"), P(), P(), P(), P(),
    )
    return jax.shard_map(
        on_device, mesh=mesh, in_specs=in_specs, out_specs=out_specs, check_vma=False
    )
```

```python
import functools
import math

import jax
import jax.numpy as jnp
from jax import lax
from jax.experimental import pallas as pl
from jax.experimental.pallas import tpu as pltpu
from jax.sharding import PartitionSpec as P

D = 1280
INNER = 640
KERNEL_TAPS = 5
DILATION_STEP = 128
STEP = 10
EPSILON = 1e-05
DECAY = 1.0 - STEP ** (-0.8)

REACH = (KERNEL_TAPS - 1) // 2 * DILATION_STEP
MID = (KERNEL_TAPS - 1) // 2
F32 = jnp.float32
BF16 = jnp.bfloat16
SUB, LANE = 16, 128
AXES = ("seq", "fsdp")
NT = (((1,), (1,)), ((), ()))
TN = (((0,), (0,)), ((), ()))
NN = (((1,), (0,)), ((), ()))
VMEM_LIMIT = 58 * 1024 * 1024


def call(kernel, grid, in_specs, out_specs, out_shape, scratch=(), us=1.0, aliases=None):
    params = pltpu.CompilerParams(
        vmem_limit_bytes=VMEM_LIMIT, dimension_semantics=("arbitrary",) * len(grid)
    )
    return pl.pallas_call(
        kernel,
        grid=grid,
        in_specs=in_specs,
        out_specs=out_specs,
        out_shape=out_shape,
        scratch_shapes=list(scratch),
        compiler_params=params,
        input_output_aliases=aliases or {},
        cost_estimate=pl.CostEstimate(
                flops=int(us * 1e8), bytes_accessed=int(us * 3e5), transcendentals=0
        ),
    )


def shape(dims, dtype):
    return jax.ShapeDtypeStruct(dims, dtype)


def rows_spec(tile, width):
    return pl.BlockSpec((tile, width), lambda i: (i, 0))


def whole(*dims):
    return pl.BlockSpec(dims, lambda *_: (0,) * len(dims))


ANY = pl.BlockSpec(memory_space=pl.ANY)
SMEM = pl.BlockSpec(memory_space=pltpu.SMEM)


ERFC_P = 0.47 / math.sqrt(2.0)
ERFC_C = (
    0.12357219400743558,
    0.1999878668208835,
    -0.08033356004356296,
    0.3660253986657854,
    -0.1092519747040215,
)
LOG2E = 1.4426950408889634


def gelu_and_slope(y):
    t = pltpu.reciprocal(1.0 + ERFC_P * jnp.abs(y), approx=True)
    bell = jnp.exp2(y * y * (-0.5 * LOG2E))
    poly = ERFC_C[4] * t + ERFC_C[3]
    for c in ERFC_C[2::-1]:
        poly = poly * t + c
    tail = poly * t * bell
    cdf = jnp.where(y > 0.0, 1.0 - tail, tail)
    return y * cdf, cdf + y * (bell * (1.0 / math.sqrt(2.0 * math.pi)))


def lane_blocks(width):
    return [slice(k, k + LANE) for k in range(0, width, LANE)]


def row_stats(ref, rows):
    width = ref.shape[-1]
    blocks = lane_blocks(width)
    total = ref[rows, blocks[0]].astype(F32)
    for b in blocks[1:]:
        total = total + ref[rows, b].astype(F32)
    mean = jnp.sum(total, axis=-1, keepdims=True) * (1.0 / width)
    square = None
    for b in blocks:
        centered = ref[rows, b].astype(F32) - mean
        square = centered * centered if square is None else square + centered * centered
    variance = jnp.sum(square, axis=-1, keepdims=True) * (1.0 / width)
    return mean, lax.rsqrt(variance + EPSILON)


def fold(values):
    total = values[0:8]
    for k in range(8, values.shape[0], 8):
        total = total + values[k : k + 8]
    return total


def in_stages(count, stages, between=()):
    chunks = [slice(k, k + CHUNK) for k in range(0, count, CHUNK)]
    kept, rounds = {}, len(chunks) + len(stages) - 1
    for t in range(rounds):
        for n, stage in enumerate(stages):
            if 0 <= t - n < len(chunks):
                kept[n, t - n] = stage(chunks[t - n], kept.get((n - 1, t - n)))
        for work in between[t * len(between) // rounds : (t + 1) * len(between) // rounds]:
            work()


def halves_of(count):
    return (slice(0, count // 2), slice(count // 2, count))


def row_means(sums, width):
    return [jnp.sum(x, axis=-1, keepdims=True) * (1.0 / width) for x in sums]


def norm_back(rows, dxhat_ref, xhat_ref, means, put):
    mean_d, mean_dx, rstd = means
    for b in lane_blocks(dxhat_ref.shape[-1]):
        xhat = xhat_ref[rows, b].astype(F32)
        put(b, (dxhat_ref[rows, b] - mean_d - xhat * mean_dx) * rstd)


def add_terms(acc_ref, b, dy, xhat):
    acc_ref[0:8, b] += fold(dy * xhat)
    acc_ref[8:16, b] += fold(dy)


def open_sums(acc_ref):
    @pl.when(pl.program_id(0) == 0)
    def _():
        acc_ref[...] = jnp.zeros_like(acc_ref)


def close_sums(out_ref, acc_ref):
    @pl.when(pl.program_id(0) == pl.num_programs(0) - 1)
    def _():
        out_ref[0:1, :] = jnp.sum(acc_ref[0:8, :], axis=0, keepdims=True)
        out_ref[1:2, :] = jnp.sum(acc_ref[8:16, :], axis=0, keepdims=True)


def run_copies(copies):
    for copy in copies:
        copy.start()
    for copy in copies:
        copy.wait()


def piece_copies(pieces, full_ref, me, sem, first=0):
    each = full_ref.shape[0] // len(pieces)
    return [
        pltpu.make_async_copy(
            piece.at[0:each, :],
            full_ref.at[pl.ds(pl.multiple_of((me ^ k) * each, SUB), each), :],
            sem.at[first + k],
        )
        for k, piece in enumerate(pieces)
    ]


def out_copies(pieces, full_ref, me, sem, first=0):
    each, width = full_ref.shape[0] // len(pieces), full_ref.shape[1] // 2
    copies = []
    for k, piece in enumerate(pieces):
        rows = pl.ds(pl.multiple_of((me ^ k) * each, SUB), each)
        for side in range(2):
            at = piece.shape[0] - (2 - side) * each
            copies.append(
                pltpu.make_async_copy(
                    piece.at[at : at + each, :],
                    full_ref.at[rows, side * width : (side + 1) * width],
                    sem.at[first + 2 * k + side],
                )
            )
    return copies


def column(row):
    return jnp.transpose(jnp.broadcast_to(row, (LANE, LANE)))


CHUNK = 64


def norm_a_kernel(tok_ref, np_ref, *refs):
    hid_ref, slope_ref, xhat_ref, rstd_ref = refs[-4:]

    def stats(rows, _):
        mean, rstd = row_stats(tok_ref, rows)
        rstd_ref[rows, :] = rstd
        return mean, rstd

    def work(rows, kept):
        mean, rstd = kept
        for b in lane_blocks(D):
            xhat = (tok_ref[rows, b].astype(F32) - mean) * rstd
            hidden, slope = gelu_and_slope(xhat * np_ref[0:1, b] + np_ref[1:2, b])
            hid_ref[rows, b] = hidden.astype(BF16)
            slope_ref[rows, b] = slope.astype(BF16)
            xhat_ref[rows, b] = xhat.astype(BF16)

    in_stages(tok_ref.shape[0], [stats, work])


def running_ends(ends_ref, lengths_ref):
    docs, width = lengths_ref.shape[0], ends_ref.shape[1]
    ends_ref[...] = jnp.zeros_like(ends_ref)
    ends_ref[0:1, 0:docs] = lengths_ref[...].reshape(1, -1).astype(F32)
    before = jnp.zeros((1, 1), F32)
    row = lax.broadcasted_iota(jnp.int32, (LANE, LANE), 0)
    lane = lax.broadcasted_iota(jnp.int32, (LANE, LANE), 1)
    for k in range(0, width, LANE):
        line = ends_ref[0:1, k : k + LANE]
        sums = jnp.sum(jnp.where(row <= lane, column(line), 0.0), axis=0, keepdims=True) + before
        ends_ref[0:1, k : k + LANE] = jnp.where(lane[0:1] + k < docs, sums, 1e9)
        before = before + jnp.sum(line, axis=1, keepdims=True)


def in_kernel(pieces, tiles, place_ref, lengths_ref, hid_ref, live_ref, np_ref, *refs):
    piece_refs = refs[:pieces]
    edges = tiles[0] == 0
    outs = refs[-(11 if edges else 9) :]
    mov_ref, slope_ref, xhat_ref, rstd_ref, mask_ref = outs[:5]
    w_ref, pre_ref, ends_ref, sem = outs[-4:]
    step = pl.program_id(0)
    tile = hid_ref.shape[0]

    @pl.when(step == 0)
    def _():
        copies = piece_copies(piece_refs, w_ref, place_ref[0], sem)
        for copy in copies:
            copy.start()
        running_ends(ends_ref, lengths_ref)
        for copy in copies:
            copy.wait()

    for half in halves_of(tile):
        pre_ref[half, :] = lax.dot_general(
            hid_ref[half, :], w_ref[...], NN, preferred_element_type=F32
        )

    at_tile = tiles[0] + step * tiles[1]
    first = place_ref[1] + at_tile * tile
    ends = ends_ref[0:1, :]
    lanes = lax.broadcasted_iota(jnp.int32, (LANE, 8), 1)
    offsets = ((lanes - MID) * DILATION_STEP).astype(F32)
    for k in range(tile // LANE):
        at = (first + k * LANE + lax.broadcasted_iota(jnp.int32, (LANE, 1), 0)).astype(F32)
        begin = jnp.max(jnp.where(ends <= at, ends, 0.0), axis=1, keepdims=True)
        end = jnp.min(jnp.where(ends > at, ends, 1e9), axis=1, keepdims=True)
        there = at + offsets
        same = jnp.where((there >= begin) & (there < end), 1.0, 0.0)
        live = column(live_ref[pl.ds(at_tile * (tile // LANE) + k, 1), :].astype(F32))
        mask_ref[k * LANE : (k + 1) * LANE, :] = jnp.where(lanes == MID, live[:, 0:8], same)

    def stats(rows, _):
        mean, rstd = row_stats(pre_ref, rows)
        rstd_ref[rows, :] = rstd
        return mean, rstd

    def work(rows, kept):
        mean, rstd = kept
        live = mask_ref[rows, MID : MID + 1]
        for b in lane_blocks(INNER):
            gains = slice(D + b.start, D + b.stop)
            xhat = (pre_ref[rows, b] - mean) * rstd
            hidden, slope = gelu_and_slope(xhat * np_ref[0:1, gains] + np_ref[1:2, gains])
            mov_ref[rows, b] = (hidden * live).astype(BF16)
            slope_ref[rows, b] = slope.astype(BF16)
            xhat_ref[rows, b] = xhat.astype(BF16)

    in_stages(tile, [stats, work])
    if edges:
        first_ref, last_ref = outs[5:7]

        @pl.when(step == 0)
        def _():
            first_ref[...] = mov_ref[0:REACH, :]

        @pl.when(step == 1)
        def _():
            last_ref[...] = mov_ref[tile - REACH :, :]


def load_window(low, mid, high, ext_ref, sem):
    rows = mid.shape[0]
    return [
        pltpu.make_async_copy(low, ext_ref.at[0:REACH, :], sem.at[0]),
        pltpu.make_async_copy(mid, ext_ref.at[REACH : REACH + rows, :], sem.at[1]),
        pltpu.make_async_copy(high, ext_ref.at[REACH + rows : 2 * REACH + rows, :], sem.at[2]),
    ]


def fill_taps(taps_ref, ext_ref, mask_ref, start):
    tile = taps_ref.shape[0]
    for j in range(KERNEL_TAPS):
        rows = pl.ds(pl.multiple_of(start + j * DILATION_STEP, DILATION_STEP), tile)
        picked = ext_ref[rows, :]
        if j != MID:
            picked = picked * mask_ref[:, j : j + 1].astype(BF16)
        taps_ref[:, j * INNER : (j + 1) * INNER] = picked


def conv_kernel(
    pieces, rows_of, place_ref, low_ref, mov_ref, high_ref, mask_ref, cot_ref, before_ref, np_ref, *refs
):
    piece_refs = refs[:pieces]
    hid_ref, dconv_ref, first_ref, last_ref, sums_ref, turned_ref = refs[pieces : pieces + 6]
    outs = refs[pieces + 6 : pieces + 10]
    ext_ref, wc_ref, wct_ref, wo_ref, wt_ref, taps_ref, pre_ref, dh_ref, xhat_ref = refs[
        pieces + 10 : pieces + 19
    ]
    dt_ref, ht_ref, gc_ref, go_ref, acc_ref, stage1_ref, stage2_ref, sem = refs[pieces + 19 :]
    step, steps = pl.program_id(0), pl.num_programs(0) - 1
    tile = taps_ref.shape[1]
    slot = lax.rem(step, 2)

    @pl.when(step == 0)
    def _():
        me = place_ref[0]
        outs = out_copies(piece_refs, wo_ref, me, sem, 3)
        rest = load_window(low_ref, mov_ref, high_ref, ext_ref, sem)
        rest += piece_copies(piece_refs, wc_ref, me, sem, 3 + 2 * pieces)
        for copy in outs + rest:
            copy.start()
        for ref in (acc_ref, gc_ref, go_ref, dt_ref, ht_ref):
            ref[...] = jnp.zeros_like(ref)
        taps_ref[1] = jnp.zeros_like(taps_ref[1])
        for copy in outs:
            copy.wait()
        for k in range(0, D, 256):
            wt_ref[k : k + 256, :] = jnp.transpose(wo_ref[:, k : k + 256])
        for copy in rest:
            copy.wait()

    def grad_conv(cols):
        def work():
            gc_ref[:, cols] += lax.dot_general(
                dt_ref[...], taps_ref[1 - slot, :, cols], NN, preferred_element_type=F32
            )

        return work

    def grad_out(cols):
        def work():
            go_ref[:, cols] += lax.dot_general(
                ht_ref[...], before_ref[:, cols], NN, preferred_element_type=F32
            )

        return work

    taps_wide = KERNEL_TAPS * INNER
    products = [grad_conv(slice(k, min(k + 768, taps_wide))) for k in range(0, taps_wide, 768)]
    products += [grad_out(slice(k, min(k + 768, D))) for k in range(0, D, 768)]

    @pl.when(step < steps)
    def _():
        fill_taps(taps_ref.at[slot], ext_ref, mask_ref, step * tile)
        pre_ref[...] = lax.dot_general(
            taps_ref[slot], wc_ref[...], NN, preferred_element_type=F32
        )
        dh_ref[...] = lax.dot_general(cot_ref[...], wt_ref[...], NN, preferred_element_type=F32)
        for n in range(2):
            tap = jnp.minimum(2 * step + n, KERNEL_TAPS - 1)
            source = wc_ref[pl.ds(pl.multiple_of(tap * INNER, SUB), INNER), :]
            target = pl.multiple_of((KERNEL_TAPS - 1 - tap) * INNER, SUB)
            wct_ref[pl.ds(target, INNER), :] = jnp.transpose(source)

        def stats(rows, _):
            return row_stats(pre_ref, rows)

        def work(rows, kept):
            mean, rstd = kept
            sums = [0.0, 0.0]
            for b in lane_blocks(INNER):
                gains = slice(D + INNER + b.start, D + INNER + b.stop)
                gain = np_ref[0:1, gains]
                xhat = (pre_ref[rows, b] - mean) * rstd
                hidden, slope = gelu_and_slope(xhat * gain + np_ref[1:2, gains])
                hid_ref[rows, b] = hidden.astype(BF16)
                dy = dh_ref[rows, b] * slope
                add_terms(acc_ref, b, dy, xhat)
                dxhat = dy * gain
                xhat_ref[rows, b] = xhat
                dh_ref[rows, b] = dxhat
                sums = [sums[0] + dxhat, sums[1] + dxhat * xhat]
            return row_means(sums, INNER) + [rstd]

        def finish(rows, means):
            def put(b, value):
                dconv_ref[rows, b] = value.astype(BF16)

            norm_back(rows, dh_ref, xhat_ref, means, put)

        in_stages(tile, [stats, work, finish], products)
        dt_ref[...] = jnp.transpose(dconv_ref[...])
        ht_ref[...] = jnp.transpose(hid_ref[...])

    @pl.when(step == 0)
    def _():
        first_ref[...] = dconv_ref[0:REACH, :]

    @pl.when(step == steps - 1)
    def _():
        last_ref[...] = dconv_ref[tile - REACH :, :]

    @pl.when(step == steps)
    def _():
        copy = pltpu.make_async_copy(wct_ref, turned_ref, sem.at[4])
        copy.start()
        for work in products:
            work()
        core = lax.rem(place_ref[0], 2)
        _, rows_conv, rows_out = rows_of
        stage_turned(stage1_ref, core, gc_ref, rows_conv, 0, slice(0, CUT // LANE))
        first_tiles = rows_conv // SUB * (CUT // LANE)
        stage_plain(stage1_ref, core, go_ref, rows_out, first_tiles)
        copies = stage_copies(stage1_ref, outs[0], outs[1], spans(CHUNKS[0], rows_of)[1], sem, 0)
        for each in copies:
            each.start()
        stage_turned(stage2_ref, core, gc_ref, rows_conv, 0, slice(CUT // LANE, INNER // LANE))
        more = stage_copies(stage2_ref, outs[2], outs[3], spans(CHUNKS[1], rows_of)[1], sem, 2)
        for each in more:
            each.start()
        for each in copies + more + [copy]:
            each.wait()
        sums_ref[0:1, :] = jnp.sum(acc_ref[0:8, :], axis=0, keepdims=True)
        sums_ref[1:2, :] = jnp.sum(acc_ref[8:16, :], axis=0, keepdims=True)


def stage_tiles(stage_ref, core, first_row, rows_each, base, block0, blocks, value):
    for g in range(value.shape[0] // SUB):
        row = first_row + g * SUB
        owner, inside = row // rows_each, row % rows_each // SUB
        side = core ^ (owner % 2)
        for b in range(value.shape[1] // LANE):
            tile = value[g * SUB : (g + 1) * SUB, b * LANE : (b + 1) * LANE]
            at = base + inside * blocks + block0 + b
            stage_ref[side, owner // 2, at] = tile.astype(BF16)


def stage_plain(stage_ref, core, grad_ref, rows_each, base):
    blocks = grad_ref.shape[1] // LANE
    for row in range(0, grad_ref.shape[0], SUB):
        part = grad_ref[row : row + SUB, :]
        stage_tiles(stage_ref, core, row, rows_each, base, 0, blocks, part)


def stage_turned(stage_ref, core, turned_ref, rows_each, base, blocks):
    count = blocks.stop - blocks.start
    for row in range(0, turned_ref.shape[1], LANE):
        for b in range(count):
            at = (blocks.start + b) * LANE
            part = jnp.transpose(turned_ref[at : at + LANE, row : row + LANE].astype(BF16))
            stage_tiles(stage_ref, core, row, rows_each, base, b, count, part)


def stage_copies(stage_ref, keep_ref, send_ref, used, sem, first):
    count = stage_ref.shape[2]
    if used < count:
        dims = stage_ref.shape[:2] + (count - used, SUB, LANE)
        stage_ref[:, :, used:] = jnp.zeros(dims, BF16)
    return [
        pltpu.make_async_copy(stage_ref.at[n], ref, sem.at[first + n])
        for n, ref in enumerate((keep_ref, send_ref))
    ]


def back_conv_kernel(
    at, tokens, rows_in, place_ref, low_ref, d_ref, high_ref, turned_ref, mask_ref, xhat_ref, rstd_ref, slope_ref, np_ref, *refs
):
    ext_ref, wt_ref, taps_ref, dmov_ref, acc_ref, sem = refs[-6:]
    step, steps = pl.program_id(0), pl.num_programs(0)
    tile = taps_ref.shape[0]
    first, rows = at * tile, ext_ref.shape[0] - 2 * REACH
    last = first + rows == tokens
    if last:
        hid_ref, before_ref, dpre_ref, sums_ref, keep_ref, send_ref = refs[:6]
        stage_ref, all_ref, held_ref, grad_ref = refs[6:10]
        gather = [
            pltpu.make_async_copy(before_ref.at[0:first, :], all_ref.at[0:first, :], sem.at[4]),
            pltpu.make_async_copy(hid_ref, held_ref, sem.at[5]),
        ]
    else:
        dpre_ref, sums_ref = refs[at > 0 :][:2]
    open_sums(acc_ref)

    @pl.when(step == 0)
    def _():
        begin, end = max(first - REACH, 0), min(first + rows + REACH, tokens)
        offset = begin - (first - REACH)
        copies = [
            pltpu.make_async_copy(turned_ref, wt_ref, sem.at[0]),
            pltpu.make_async_copy(
                d_ref.at[begin:end, :], ext_ref.at[offset : offset + end - begin, :], sem.at[1]
            ),
        ]
        if first == 0:
            copies.append(pltpu.make_async_copy(low_ref, ext_ref.at[0:REACH, :], sem.at[2]))
        if last:
            target = ext_ref.at[REACH + rows : 2 * REACH + rows, :]
            copies.append(pltpu.make_async_copy(high_ref, target, sem.at[3]))
        for copy in copies:
            copy.start()
        if last:
            for copy in gather:
                copy.start()
        for copy in copies:
            copy.wait()

    fill_taps(taps_ref, ext_ref, mask_ref, step * tile)
    dmov_ref[...] = lax.dot_general(taps_ref[...], wt_ref[...], NN, preferred_element_type=F32)

    def work(rows, _):
        live = mask_ref[rows, MID : MID + 1]
        sums = [0.0, 0.0]
        for b in lane_blocks(INNER):
            xhat = xhat_ref[rows, b].astype(F32)
            dy = dmov_ref[rows, b] * live * slope_ref[rows, b].astype(F32)
            add_terms(acc_ref, b, dy, xhat)
            dxhat = dy * np_ref[0:1, D + b.start : D + b.stop]
            dmov_ref[rows, b] = dxhat
            sums = [sums[0] + dxhat, sums[1] + dxhat * xhat]
        return row_means(sums, INNER) + [rstd_ref[rows, :]]

    def finish(rows, means):
        def put(b, value):
            dpre_ref[rows, b] = value.astype(BF16)

        norm_back(rows, dmov_ref, xhat_ref, means, put)

    in_stages(tile, [work, finish])
    close_sums(sums_ref, acc_ref)
    if last:
        all_ref[pl.ds(first + step * tile, tile), :] = dpre_ref[...]

        @pl.when(step == steps - 1)
        def _():
            for copy in gather:
                copy.wait()
            grad_ref[...] = lax.dot_general(
                all_ref[...], held_ref[...], TN, preferred_element_type=F32
            )
            all_blocks = slice(0, INNER // LANE)
            stage_turned(stage_ref, lax.rem(place_ref[0], 2), grad_ref, rows_in, 0, all_blocks)
            used = rows_in // SUB * (INNER // LANE)
            run_copies(stage_copies(stage_ref, keep_ref, send_ref, used, sem, 0))


def back_a_kernel(pieces, place_ref, dpre_ref, xhat_ref, rstd_ref, slope_ref, cot_ref, np_ref, *refs):
    piece_refs = refs[:pieces]
    grad_ref, sums_ref, w_ref, wt_ref, dh_ref, acc_ref, sem = refs[-7:]
    open_sums(acc_ref)

    @pl.when(pl.program_id(0) == 0)
    def _():
        run_copies(piece_copies(piece_refs, w_ref, place_ref[0], sem))
        for k in range(0, D, 256):
            wt_ref[:, k : k + 256] = jnp.transpose(w_ref[k : k + 256, :])

    dh_ref[...] = lax.dot_general(dpre_ref[...], wt_ref[...], NN, preferred_element_type=F32)

    def work(rows, _):
        sums = [0.0, 0.0]
        for b in lane_blocks(D):
            xhat = xhat_ref[rows, b].astype(F32)
            dy = dh_ref[rows, b] * slope_ref[rows, b].astype(F32)
            add_terms(acc_ref, b, dy, xhat)
            dxhat = dy * np_ref[0:1, b]
            dh_ref[rows, b] = dxhat
            sums = [sums[0] + dxhat, sums[1] + dxhat * xhat]
        return row_means(sums, D) + [rstd_ref[rows, :]]

    def finish(rows, means):
        def put(b, value):
            grad_ref[rows, b] = cot_ref[rows, b].astype(F32) + value

        norm_back(rows, dh_ref, xhat_ref, means, put)

    in_stages(dpre_ref.shape[0], [work, finish])
    close_sums(sums_ref, acc_ref)


def out_kernel(pieces, place_ref, hid_ref, tok_ref, *refs):
    piece_refs = refs[:pieces]
    out_ref, w_ref, sem = refs[pieces:]

    @pl.when(pl.program_id(0) == 0)
    def _():
        run_copies(out_copies(piece_refs, w_ref, place_ref[0], sem))

    branch = lax.dot_general(hid_ref[...], w_ref[...], NN, preferred_element_type=F32)
    out_ref[...] = (tok_ref[...].astype(F32) + branch).astype(BF16)


WIDTHS = (INNER, INNER, D)
LANE0 = (0, INNER, 2 * INNER)
CUT = 2 * LANE
CHUNKS = (((1, 0, CUT), (2, 0, D)), ((1, CUT, INNER - CUT),), ((0, 0, INNER),))


def spans(chunk, rows):
    found, first = [], 0
    for weight, col, cols in chunk:
        tiles = rows[weight] // SUB * (cols // LANE)
        found.append((weight, col // LANE, cols // LANE, first, tiles))
        first += tiles
    return found, first


def column_sums(pack_ref, row, ref, chunk, rows):
    for weight, block0, blocks, first, tiles in spans(chunk, rows)[0]:

        def body(g, carry, first=first, blocks=blocks):
            new = []
            for b in range(blocks):
                value = ref[first + g * blocks + b].astype(F32)
                new.append(carry[b] + fold(value * value + 1e-30))
            return tuple(new)

        zero = tuple(jnp.zeros((8, LANE), F32) for _ in range(blocks))
        cols = lax.fori_loop(0, tiles // blocks, body, zero, unroll=5)
        for b in range(blocks):
            lane = LANE0[weight] + (block0 + b) * LANE
            pack_ref[row : row + 1, lane : lane + LANE] = jnp.sum(cols[b], axis=0, keepdims=True)


def load_full(refs, place_ref, first, full_ref, sem, at):
    pieces = refs[0].shape[0]
    each = full_ref.shape[0] // (len(refs) * pieces)
    outer = pieces if len(refs) == 2 else pieces // 2
    y = place_ref[2] % 2
    copies = []
    for n, (ref, side) in enumerate(zip(refs, (y, 1 - y))):
        for p in range(pieces):
            index = side * outer + p if len(refs) == 2 else p % 2 * outer + p // 2
            target = full_ref.at[pl.ds(index * each, each)]
            source = ref.at[p, first : first + each]
            copies.append(pltpu.make_async_copy(source, target, sem.at[at + n * pieces + p]))
    return copies


def pack_kernel(rows, place_ref, mine_ref, *refs):
    states, (pack_ref, acc_ref) = refs[0:3], refs[3:5]
    pack_ref[...] = jnp.zeros_like(pack_ref)
    lanes = lax.broadcasted_iota(jnp.int32, (1, LANE), 1)
    for k in range(3):
        total = jnp.sum(states[k][...].reshape(1, -1), axis=1, keepdims=True)
        pack_ref[1:2, 0:LANE] += jnp.where(lanes == k, total, 0.0)
    acc_ref[...] = jnp.zeros_like(acc_ref)
    spare = acc_ref.shape[0] - 1
    outer, at = mine_ref.shape[0], 0
    for chunk in CHUNKS[:2]:
        found, count = spans(chunk, rows)
        each = (count + -count % (2 * outer)) // (2 * outer)
        for p in range(outer):
            start = (place_ref[2] % 2 * outer + p) * each

            def body(k, carry, found=found, start=start, at=at, p=p):
                n = start + k
                slot = spare
                for weight, block0, blocks, first, tiles in found:
                    here = lax.rem(jnp.maximum(n - first, 0), blocks)
                    here = LANE0[weight] // LANE + block0 + here
                    slot = jnp.where((n >= first) & (n < first + tiles), here, slot)
                value = mine_ref[p, at + k].astype(F32)
                acc_ref[slot] += value * value + 1e-30
                return carry

            lax.fori_loop(0, each, body, 0, unroll=2)
        at += each
    for slot in range(spare):
        pack_ref[0:1, slot * LANE : (slot + 1) * LANE] = jnp.sum(acc_ref[slot], axis=0, keepdims=True)


def norm_tiles_kernel(parts, *refs):
    sums, out_ref, line_ref = refs[:-2], refs[-2], refs[-1]
    line_ref[...] = jnp.zeros_like(line_ref)
    lanes_of = ((0, D), (D, D + INNER), (D, D + INNER), (D, D + INNER), (D + INNER, D + 2 * INNER))
    for part, (lane0, lane1) in zip(sums, lanes_of):
        line_ref[0:2, lane0:lane1] += part[...]
    out_ref[...] = jnp.zeros_like(out_ref)
    blocks = (D + 2 * INNER) // LANE
    each = -(-2 * blocks // parts)
    for part in range(-(-2 * blocks // each)):
        rows = []
        for n in range(part * each, min((part + 1) * each, 2 * blocks)):
            row, b = n // blocks, n % blocks
            rows.append(line_ref[row : row + 1, b * LANE : (b + 1) * LANE])
        rows += [jnp.zeros((1, LANE), F32)] * (8 - len(rows))
        value = jnp.concatenate(rows, axis=0)
        high = value.astype(BF16).astype(F32)
        out_ref[part] = jnp.concatenate([high, value - high], axis=0).astype(BF16)


def high_low(total):
    value = total[..., 0:8, :] + total[..., 8:16, :]
    high = value.astype(BF16).astype(F32)
    return jnp.concatenate([high, value - high], axis=-2).astype(BF16)


def pack_in_kernel(rows, place_ref, got_ref, out_ref, full_ref, norms_ref, sem, norms_sem):
    parts = got_ref.shape[0]
    each = full_ref.shape[0] // parts
    copies = load_full((got_ref,), place_ref, 0, full_ref, sem, 0)
    copies += [
        pltpu.make_async_copy(got_ref.at[p, each], norms_ref.at[p], norms_sem.at[p])
        for p in range(parts)
    ]
    run_copies(copies)
    out_ref[...] = jnp.zeros_like(out_ref)
    blocks = (D + 2 * INNER) // LANE
    rows_each = -(-2 * blocks // parts)
    for n in range(2 * blocks):
        part, at = n // rows_each, n % rows_each
        value = norms_ref[part].astype(F32)
        row, lane = n // blocks, n % blocks * LANE
        out_ref[row : row + 1, lane : lane + LANE] = value[at : at + 1] + value[8 + at : 9 + at]
    column_sums(out_ref, 2, full_ref, CHUNKS[2], rows)


def update_weight(
    k, squares, states_sum, source, weight, state, col_state, grad_ref, new, row_new_ref, col_new_ref, scratch
):
    line_ref, state_ref, new_ref = scratch
    width, fan, rows_here = WIDTHS[k], (D, KERNEL_TAPS * INNER, INNER)[k], weight.shape[0]
    col_new = DECAY * col_state[...].reshape(1, -1) + (1.0 - DECAY) * (squares * (1.0 / fan))
    col_new_ref[...] = col_new.reshape(-1)
    total = DECAY * states_sum
    total = total + (1.0 - DECAY) * (1.0 / width) * jnp.sum(squares, axis=1, keepdims=True)
    scaled = col_new / (total * (1.0 / fan))
    rate = 0.5 / fan**0.5
    line_ref[0:1, 0:rows_here] = state[...].reshape(1, -1)
    whole_rows = rows_here + -rows_here % LANE
    for c in range(0, whole_rows, LANE):
        state_ref[c : c + LANE, :] = column(line_ref[0:1, c : c + LANE])

    def body(g, carry):
        rows = pl.ds(pl.multiple_of(g * SUB, SUB), SUB)
        square = 0.0
        for ref, block0, blocks, first in source:
            for b in range(blocks):
                value = ref[first + g * blocks + b].astype(F32)
                grad_ref[rows, (block0 + b) * LANE : (block0 + b + 1) * LANE] = value
                square = square + (value * value + 1e-30)
        mean = jnp.sum(square, axis=1, keepdims=True) * (1.0 / width)
        row_new = DECAY * state_ref[rows, :] + (1.0 - DECAY) * mean
        new_ref[rows, :] = row_new
        for ref, block0, blocks, first in source:
            for b in range(blocks):
                lanes = slice((block0 + b) * LANE, (block0 + b + 1) * LANE)
                value = ref[first + g * blocks + b].astype(F32)
                step = value * lax.rsqrt(row_new * scaled[:, lanes])
                new[rows, lanes] = weight[rows, lanes] - rate * step
        return carry

    lax.fori_loop(0, rows_here // SUB, body, 0, unroll=5)
    for c in range(0, whole_rows, LANE):
        line_ref[0:1, c : c + LANE] = jnp.transpose(new_ref[c : c + LANE, :])[0:1, :]
    row_new_ref[...] = line_ref[0:1, 0:rows_here].reshape(-1)


def update_kernel(rows, copies_of, place_ref, mine_ref, other_ref, pack_ref, *refs):
    weights, states, col_states = refs[0:2], refs[2:4], refs[4:6]
    grads, news, rows_new, cols_new = refs[6:8], refs[8:10], refs[10:12], refs[12:14]
    full1_ref, full2_ref, sem = refs[17:20]
    both = (mine_ref, other_ref)
    count = 2 * mine_ref.shape[0]
    copies = load_full(both, place_ref, 0, full1_ref, sem, 0)
    copies += load_full(both, place_ref, full1_ref.shape[0] // count, full2_ref, sem, count)
    run_copies(copies)
    from1 = sources_of(CHUNKS[0], full1_ref, rows)
    from2 = sources_of(CHUNKS[1], full2_ref, rows)
    for n, (k, source) in enumerate(((1, [from1[1], from2[1]]), (2, [from1[2]]))):
        squares = pack_ref[0:1, LANE0[k] : LANE0[k] + WIDTHS[k]]
        update_weight(
            k, squares, pack_ref[1:2, k : k + 1] * (1.0 / copies_of), source, weights[n],
            states[n], col_states[n], grads[n], news[n], rows_new[n], cols_new[n], refs[14:17],
        )


def update_in_kernel(
    rows, copies_of, place_ref, got_ref, pack_in_ref, pack_ref, np_ref, second_ref, *refs
):
    weight, state, col_state, grad_ref, new_ref, row_new_ref, col_new_ref = refs[0:7]
    ngrad_ref, nsecond_ref, nnew_ref = refs[7:10]
    full_ref, sem = refs[13:15]
    copies = load_full((got_ref,), place_ref, 0, full_ref, sem, 0)
    for copy in copies:
        copy.start()
    grad = pack_in_ref[0:2, :]
    second = DECAY * second_ref[...] + (1.0 - DECAY) * (grad * grad + 1e-30)
    ngrad_ref[...] = grad
    nsecond_ref[...] = second
    nnew_ref[...] = np_ref[...] - 0.2 * grad * lax.rsqrt(second)
    for copy in copies:
        copy.wait()
    update_weight(
        0, pack_in_ref[2:3, 0:INNER], pack_ref[1:2, 0:1] * (1.0 / copies_of),
        [sources_of(CHUNKS[2], full_ref, rows)[0]], weight, state, col_state, grad_ref, new_ref,
        row_new_ref, col_new_ref, refs[10:13],
    )


def sources_of(chunk, ref, rows):
    return {w: (ref, block0, blocks, first) for w, block0, blocks, first, _ in spans(chunk, rows)[0]}


class Places:
    def __init__(self):
        self.seq, self.fsdp = lax.axis_size("seq"), lax.axis_size("fsdp")
        self.q = lax.axis_index("fsdp")
        self.s = lax.axis_index("seq")

    def flip(self, x, axis, bit):
        pairs = []
        for s in range(self.seq):
            for f in range(self.fsdp):
                s2, f2 = (s ^ bit, f) if axis == "seq" else (s, f ^ bit)
                pairs.append((s * self.fsdp + f, s2 * self.fsdp + f2))
        return lax.ppermute(x, AXES, pairs)


def bits_of(count):
    return [1 << k for k in range(count.bit_length() - 1)]


def tie(x, *others):
    return lax.optimization_barrier((x, *others))[0]


def gather_pieces(piece, place, after, later=()):
    found = {0: piece}
    for bit in reversed(bits_of(place.fsdp)):
        for k in list(found):
            moving = found[k]
            if bit == 1:
                moving = tie(moving, *((after,) if k == 0 or not later else later))
            found[k | bit] = place.flip(moving, "fsdp", bit)
    return [found[k] for k in range(place.fsdp)]


def sum_over(x, place, *axes):
    for axis in axes:
        for bit in bits_of(getattr(place, axis)):
            x = x + place.flip(x, axis, bit)
    return x


def pick(x, index, axis):
    return lax.dynamic_index_in_dim(x, index, axis=axis, keepdims=False)


class Reduction:
    def __init__(self, place, keep, send):
        self.place, self.near = place, keep
        self.got = place.flip(send, "fsdp", 1)

    def halve(self, axis, side, flip_axis, bit):
        dims = self.near.shape
        parts = dims[:axis] + (2, dims[axis] // 2) + dims[axis + 1 :]
        near, got = self.near.reshape(parts), self.got.reshape(parts)
        away = pick(near, 1 - side, axis).astype(F32) + pick(got, 1 - side, axis).astype(F32)
        self.near = pick(near, side, axis).astype(F32) + pick(got, side, axis).astype(F32)
        away = away.astype(BF16)
        self.got = self.place.flip(away, flip_axis, bit)
        return away

    def x(self):
        bit = self.place.fsdp // 2
        while bit > 1:
            away = self.halve(0, (self.place.q // bit) % 2, "fsdp", bit)
            bit //= 2
        return away

    def y(self):
        return self.halve(1, self.place.s % 2, "seq", 1)

    def pieces(self):
        total = (self.near + self.got.astype(F32)).astype(BF16)
        return total.reshape((self.place.seq // 2, -1) + total.shape[2:])

    def all_pieces(self):
        total = (self.near + self.got.astype(F32)).astype(BF16)
        total = total.reshape((2, self.place.seq // 2, -1) + total.shape[2:])
        return jnp.swapaxes(total, 0, 1).reshape((self.place.seq,) + total.shape[2:])


def arrive(result, *reductions):
    result, *gots = lax.optimization_barrier((result, *[r.got for r in reductions]))
    for reduction, got in zip(reductions, gots):
        reduction.got = got
    return result


def summed_f32(got):
    return jnp.sum(got.astype(F32), axis=0)


def summed(got):
    return summed_f32(got).astype(BF16)


def exchange_all(sent):
    return lax.all_to_all(sent, "seq", 0, 0)


def exchange(place, sent):
    line = [[y + 2 * z for z in range(place.seq // 2)] for y in range(2)]
    return lax.all_to_all(sent, "seq", 0, 0, axis_index_groups=line)


def copies_for(count, part):
    return jnp.broadcast_to(part[None], (count,) + part.shape)


def on_device(
    tokens, input_mask, doc_lengths, cotangent, w_in, w_conv, w_out, norm_params,
    row_in, col_in, row_conv, col_conv, row_out, col_out, norm_second,
):
    place = Places()
    rows = tokens.shape[0]
    pieces = place.fsdp
    spots = jnp.stack(
        [place.q, (place.s * place.fsdp + place.q) * rows, place.s, place.seq]
    ).astype(jnp.int32)
    docs = doc_lengths.shape[0]
    live = input_mask.reshape(-1, LANE)
    weights = (w_in, w_conv, w_out)
    rows_of = [w.shape[0] for w in weights]

    tile_a, tile = 256, 512
    steps = rows // tile
    params_spec = whole(2, D + 2 * INNER)
    dma = pltpu.SemaphoreType.DMA

    out_sides = (w_out[:, : D // 2], w_out[:, D // 2 :])
    conv_out = jnp.concatenate([w_conv, *out_sides], axis=0).astype(BF16)
    half = rows // tile_a // 2

    def norm_a(at, params, before):
        def here_spec(width):
            return pl.BlockSpec((tile_a, width), lambda i: (i + at, 0))

        return call(
            norm_a_kernel,
            (half,),
            [here_spec(D), params_spec] + [ANY] * len(before),
            [here_spec(D)] * 3 + [here_spec(1)],
            [shape((rows, D), BF16)] * 3 + [shape((rows, 1), F32)],
            us=8,
            aliases={2 + k: k for k in range(len(before))},
        )(tokens, params, *before)

    before = norm_a(0, norm_params, ())
    in_pieces = gather_pieces(w_in.astype(BF16), place, before[0])
    conv_out = tie(conv_out, in_pieces[pieces // 2], before[0])
    hidden_a, slope_a, xhat_a, rstd_a = norm_a(half, tie(norm_params, conv_out), before)

    def in_call(tiles, count, before):
        at, stride = tiles

        def here_spec(width):
            return pl.BlockSpec((tile, width), lambda i: (at + stride * i, 0))

        out_shapes = [shape((rows, INNER), BF16)] * 3 + [shape((rows, 1), F32), shape((rows, 8), F32)]
        out_specs = [here_spec(INNER)] * 3 + [here_spec(1), here_spec(8)]
        if at == 0:
            out_shapes += [shape((REACH, INNER), BF16)] * 2
            out_specs += [whole(REACH, INNER)] * 2
        return call(
            functools.partial(in_kernel, pieces, tiles),
            (count,),
            [SMEM, whole(docs), here_spec(D), whole(*live.shape), params_spec]
            + [ANY] * (pieces + len(before)),
            out_specs,
            out_shapes,
            [pltpu.VMEM((D, INNER), BF16), pltpu.VMEM((tile, INNER), F32)]
            + [pltpu.VMEM((8, docs + -docs % LANE), F32), dma((pieces,))],
            us=8,
            aliases={5 + pieces + k: k for k in range(len(before))},
        )(spots, doc_lengths, hidden_a, live, norm_params, *in_pieces, *before)

    *kept, m_first, m_last = in_call((0, steps - 1), 2, ())
    moved, slope_b, xhat_b, rstd_b, masks = in_call((1, 1), steps - 2, kept)

    total = place.seq * place.fsdp
    up = [(i, i + 1) for i in range(total - 1)]
    down = [(i + 1, i) for i in range(total - 1)]
    m_low, m_high = lax.ppermute(m_last, AXES, up), lax.ppermute(m_first, AXES, down)
    conv_pieces = gather_pieces(conv_out, place, m_first, (moved, m_low, m_high))

    ext = pltpu.VMEM((rows + 2 * REACH, INNER), BF16)
    taps_wide = KERNEL_TAPS * INNER
    wide = pltpu.VMEM((taps_wide, INNER), BF16)
    shards = place.fsdp // 2

    def half_dims(chunk):
        count = spans(chunk, rows_of)[1]
        return (shards, count + -count % place.seq, SUB, LANE)

    def tile_spec(width, ahead):
        return pl.BlockSpec((tile, width), lambda i: (jnp.clip(i + ahead, 0, steps - 1), 0))

    halves = [half_dims(CHUNKS[0])] * 2 + [half_dims(CHUNKS[1])] * 2
    work = pltpu.VMEM((tile, INNER), F32)
    turned_tile = pltpu.VMEM((INNER, tile), BF16)
    hidden_c, d_conv, d_first, d_last, sums_c, turned, keep1, send1, keep2, send2 = call(
        functools.partial(conv_kernel, pieces, rows_of),
        (steps + 1,),
        [SMEM, ANY, ANY, ANY, tile_spec(8, 0), tile_spec(D, 0), tile_spec(D, -1), params_spec]
        + [ANY] * pieces,
        [tile_spec(INNER, 0)] * 2
        + [whole(REACH, INNER), whole(REACH, INNER), whole(2, INNER)]
        + [ANY] * 5,
        [
            shape((rows, INNER), BF16),
            shape((rows, INNER), BF16),
            shape((REACH, INNER), BF16),
            shape((REACH, INNER), BF16),
            shape((2, INNER), F32),
            shape((taps_wide, INNER), BF16),
        ]
        + [shape(dims, BF16) for dims in halves],
        [ext, wide, wide, pltpu.VMEM((INNER, D), BF16), pltpu.VMEM((D, INNER), BF16)]
        + [pltpu.VMEM((2, tile, taps_wide), BF16), work, work, work, turned_tile, turned_tile]
        + [pltpu.VMEM((INNER, taps_wide), F32), pltpu.VMEM((INNER, D), F32)]
        + [pltpu.VMEM((16, INNER), F32)]
        + [pltpu.VMEM((2,) + halves[0], BF16), pltpu.VMEM((2,) + halves[2], BF16)]
        + [dma((3 + 3 * pieces,))],
        us=45,
    )(
        spots, m_low, moved, m_high, masks, cotangent, cotangent, norm_params, *conv_pieces
    )
    d_low, d_high = lax.ppermute(d_last, AXES, up), lax.ppermute(d_first, AXES, down)
    first, second = Reduction(place, keep1, send1), Reduction(place, keep2, send2)
    (block_out,) = call(
        functools.partial(out_kernel, pieces),
        (steps,),
        [SMEM, rows_spec(tile, INNER), rows_spec(tile, D)] + [ANY] * pieces,
        [rows_spec(tile, D)],
        [shape((rows, D), BF16)],
        [pltpu.VMEM((INNER, D), BF16), dma((2 * pieces,))],
        us=9,
    )(spots, hidden_c, tokens, *conv_pieces)

    def back_conv(at, count, spots, before):
        def here_spec(width):
            return pl.BlockSpec((tile, width), lambda i: (i + at, 0))

        dims = half_dims(CHUNKS[2])
        last = at + count == steps
        return call(
            functools.partial(back_conv_kernel, at, rows, w_in.shape[0]),
            (count,),
            [SMEM] + [ANY] * 4
            + [here_spec(8), here_spec(INNER), here_spec(1), here_spec(INNER)]
            + [params_spec]
            + [ANY] * (last + len(before)),
            [here_spec(INNER), whole(2, INNER)] + [ANY] * (2 * last),
            [shape((rows, INNER), BF16), shape((2, INNER), F32)] + [shape(dims, BF16)] * (2 * last),
            (
                [
                    pltpu.VMEM((2,) + dims, BF16),
                    pltpu.VMEM((rows, INNER), BF16),
                    pltpu.VMEM((rows, D), BF16),
                    pltpu.VMEM((INNER, D), F32),
                ]
                if last
                else []
            )
            + [
                pltpu.VMEM((count * tile + 2 * REACH, INNER), BF16),
                wide,
                pltpu.VMEM((tile, taps_wide), BF16),
                pltpu.VMEM((tile, INNER), F32),
                pltpu.VMEM((16, INNER), F32),
                dma((6,)),
            ],
            us=7 * count + 6 * last,
            aliases={10 + last: 0} if before else None,
        )(
            spots, d_low, d_conv, d_high, turned, masks, xhat_b, rstd_b, slope_b, norm_params,
            *([hidden_a] if last else []), *before,
        )

    row_states, col_states = (row_in, row_conv, row_out), (col_in, col_conv, col_out)
    row_specs = [whole(*r.shape) for r in row_states]
    col_specs = [whole(*c.shape) for c in col_states]
    cols_all = D + 2 * INNER
    pack_spec, pack_shape = whole(4, cols_all), shape((4, cols_all), F32)
    fulls = [pltpu.VMEM(half_dims(c)[1:], BF16) for c in CHUNKS]

    block_out, d_low, d_high = arrive((block_out, d_low, d_high), first, second)
    away = (first.x(), second.y())
    d_pre, sums_b0 = back_conv(0, steps - 2, tie(spots, *away), ())
    d_pre = arrive(d_pre, first, second)
    away = (first.y(), second.x())
    d_pre, sums_b1 = back_conv(steps - 2, 1, tie(spots, *away), (d_pre,))
    d_pre = arrive(d_pre, first, second)
    sent = jnp.concatenate([first.pieces(), second.pieces()], axis=1)
    got = exchange(place, sent)
    d_pre, sums_b2, keep, send = back_conv(steps - 1, 1, tie(spots, sent), (d_pre,))
    got, send = lax.optimization_barrier((got, send))
    third = Reduction(place, keep, send)
    part = summed(got)
    sent = copies_for(place.seq // 2, part)
    mine = exchange(place, sent)
    third.got = tie(third.got, sent)
    away = third.x()
    input_grad, sums_a = call(
        functools.partial(back_a_kernel, pieces),
        (steps,),
        [SMEM, rows_spec(tile, INNER), rows_spec(tile, D), rows_spec(tile, 1)]
        + [rows_spec(tile, D)] * 2
        + [params_spec]
        + [ANY] * pieces,
        [rows_spec(tile, D), whole(2, D)],
        [shape((rows, D), F32), shape((2, D), F32)],
        [
            pltpu.VMEM((D, INNER), BF16),
            pltpu.VMEM((INNER, D), BF16),
            pltpu.VMEM((tile, D), F32),
            pltpu.VMEM((16, D), F32),
            dma((pieces,)),
        ],
        us=17,
    )(
        tie(spots, away), d_pre, xhat_a, rstd_a, slope_a, cotangent, norm_params, *in_pieces
    )
    sums = (sums_a, sums_b0, sums_b1, sums_b2, sums_c)
    norm_tiles = call(
        functools.partial(norm_tiles_kernel, place.seq),
        (1,),
        [whole(*x.shape) for x in sums],
        whole(place.seq, SUB, LANE),
        shape((place.seq, SUB, LANE), BF16),
        [pltpu.VMEM((8, cols_all), F32)],
        us=1,
    )(*sums)
    mine, third.got, norm_tiles = lax.optimization_barrier((mine, third.got, norm_tiles))
    other = place.flip(mine, "seq", 1)
    sent = jnp.concatenate([third.all_pieces(), norm_tiles[:, None]], axis=1)
    got = exchange_all(sent)
    (pack,) = call(
        functools.partial(pack_kernel, rows_of),
        (1,),
        [SMEM, whole(*mine.shape)] + row_specs,
        [pack_spec],
        [pack_shape],
        [pltpu.VMEM((cols_all // LANE + 1, SUB, LANE), F32)],
        us=2,
    )(tie(spots, sent), mine, *row_states)
    pack = sum_over(pack, place, "fsdp")
    got, other = lax.optimization_barrier((got, other))
    part = summed_f32(got)
    part = jnp.concatenate([part[:-1].astype(BF16), high_low(part[-1:])], axis=0)
    got_in = exchange_all(copies_for(place.seq, part))
    pack = pack + place.flip(pack, "seq", 1)
    other, pack = lax.optimization_barrier((other, pack))

    def update_scratch(weights):
        lines = max(w.shape[0] + -w.shape[0] % LANE for w in weights)
        return [pltpu.VMEM((8, lines), F32)] + [pltpu.VMEM((lines, LANE), F32)] * 2

    weight_specs = [whole(*w.shape) for w in weights]
    results = call(
        functools.partial(update_kernel, rows_of, 2),
        (1,),
        [SMEM, ANY, ANY, pack_spec] + weight_specs[1:] + row_specs[1:] + col_specs[1:],
        weight_specs[1:] * 2 + row_specs[1:] + col_specs[1:],
        [shape(w.shape, F32) for w in weights[1:]] * 2
        + [shape(r.shape, F32) for r in row_states[1:] + col_states[1:]],
        update_scratch(weights[1:]) + fulls[:2] + [dma((2 * place.seq,))],
        us=8,
    )(spots, mine, other, pack, *weights[1:], *row_states[1:], *col_states[1:])
    grad_conv, grad_out, new_conv, new_out, row_conv_new, row_out_new, col_conv_new, col_out_new = (
        results
    )
    got_in, grad_out = lax.optimization_barrier((got_in, grad_out))
    (pack_in,) = call(
        functools.partial(pack_in_kernel, rows_of),
        (1,),
        [SMEM, ANY],
        [pack_spec],
        [pack_shape],
        [fulls[2], pltpu.VMEM((place.seq, SUB, LANE), BF16)] + [dma((place.seq,))] * 2,
        us=2,
    )(spots, got_in)
    pack_in = sum_over(pack_in, place, "fsdp")
    grad_in, new_in, row_in_new, col_in_new, *norm_results = call(
        functools.partial(update_in_kernel, rows_of, 2),
        (1,),
        [SMEM, ANY, pack_spec, pack_spec, params_spec, params_spec]
        + [weight_specs[0], row_specs[0], col_specs[0]],
        [weight_specs[0]] * 2 + [row_specs[0], col_specs[0]] + [params_spec] * 3,
        [shape(w_in.shape, F32)] * 2
        + [shape(row_in.shape, F32), shape(col_in.shape, F32)]
        + [shape((2, cols_all), F32)] * 3,
        update_scratch(weights[:1]) + [fulls[2], dma((place.seq,))],
        us=4,
    )(spots, got_in, pack_in, pack, norm_params, norm_second, w_in, row_in, col_in)
    return (
        block_out,
        input_grad,
        grad_in,
        grad_conv,
        grad_out,
        new_in,
        new_conv,
        new_out,
        row_in_new,
        col_in_new,
        row_conv_new,
        col_conv_new,
        row_out_new,
        col_out_new,
        *norm_results,
    )


def solution(mesh):
    both, rows = P(AXES, None), P("fsdp", None)
    in_specs = (
        both, P(AXES), P(), both, rows, rows, rows, P(),
        P("fsdp"), P(), P("fsdp"), P(), P("fsdp"), P(), P(),
    )
    out_specs = (
        both, both, rows, rows, rows, rows, rows, rows,
        P("fsdp"), P(), P("fsdp"), P(), P("fsdp"), P(), P(), P(), P(),
    )
    return jax.shard_map(
        on_device, mesh=mesh, in_specs=in_specs, out_specs=out_specs, check_vma=False
    )
```

```python
import functools
import math

import jax
import jax.numpy as jnp
from jax import lax
from jax.experimental import pallas as pl
from jax.experimental.pallas import tpu as pltpu
from jax.sharding import PartitionSpec as P

D = 1280
INNER = 640
KERNEL_TAPS = 5
DILATION_STEP = 128
STEP = 10
EPSILON = 1e-05
DECAY = 1.0 - STEP ** (-0.8)

REACH = (KERNEL_TAPS - 1) // 2 * DILATION_STEP
MID = (KERNEL_TAPS - 1) // 2
F32 = jnp.float32
BF16 = jnp.bfloat16
SUB, LANE = 16, 128
AXES = ("seq", "fsdp")
NT = (((1,), (1,)), ((), ()))
TN = (((0,), (0,)), ((), ()))
NN = (((1,), (0,)), ((), ()))
VMEM_LIMIT = 58 * 1024 * 1024


def call(kernel, grid, in_specs, out_specs, out_shape, scratch=(), us=1.0, aliases=None):
    params = pltpu.CompilerParams(
        vmem_limit_bytes=VMEM_LIMIT, dimension_semantics=("arbitrary",) * len(grid)
    )
    return pl.pallas_call(
        kernel,
        grid=grid,
        in_specs=in_specs,
        out_specs=out_specs,
        out_shape=out_shape,
        scratch_shapes=list(scratch),
        compiler_params=params,
        input_output_aliases=aliases or {},
        cost_estimate=pl.CostEstimate(
                flops=int(us * 1.1e9), bytes_accessed=int(us * 3.4e6), transcendentals=0
        ),
    )


def shape(dims, dtype):
    return jax.ShapeDtypeStruct(dims, dtype)


def rows_spec(tile, width):
    return pl.BlockSpec((tile, width), lambda i: (i, 0))


def whole(*dims):
    return pl.BlockSpec(dims, lambda *_: (0,) * len(dims))


ANY = pl.BlockSpec(memory_space=pl.ANY)
SMEM = pl.BlockSpec(memory_space=pltpu.SMEM)


ERFC_P = 0.47 / math.sqrt(2.0)
ERFC_C = (
    0.12357219400743558,
    0.1999878668208835,
    -0.08033356004356296,
    0.3660253986657854,
    -0.1092519747040215,
)
LOG2E = 1.4426950408889634


def gelu_and_slope(y):
    t = pltpu.reciprocal(1.0 + ERFC_P * jnp.abs(y), approx=True)
    bell = jnp.exp2(y * y * (-0.5 * LOG2E))
    poly = ERFC_C[4] * t + ERFC_C[3]
    for c in ERFC_C[2::-1]:
        poly = poly * t + c
    tail = poly * t * bell
    cdf = jnp.where(y > 0.0, 1.0 - tail, tail)
    return y * cdf, cdf + y * (bell * (1.0 / math.sqrt(2.0 * math.pi)))


def lane_blocks(width):
    return [slice(k, k + LANE) for k in range(0, width, LANE)]


def row_stats(ref, rows):
    width = ref.shape[-1]
    blocks = lane_blocks(width)
    total = ref[rows, blocks[0]].astype(F32)
    for b in blocks[1:]:
        total = total + ref[rows, b].astype(F32)
    mean = jnp.sum(total, axis=-1, keepdims=True) * (1.0 / width)
    square = None
    for b in blocks:
        centered = ref[rows, b].astype(F32) - mean
        square = centered * centered if square is None else square + centered * centered
    variance = jnp.sum(square, axis=-1, keepdims=True) * (1.0 / width)
    return mean, lax.rsqrt(variance + EPSILON)


def fold(values):
    total = values[0:8]
    for k in range(8, values.shape[0], 8):
        total = total + values[k : k + 8]
    return total


def in_stages(count, stages, between=()):
    chunks = [slice(k, k + CHUNK) for k in range(0, count, CHUNK)]
    kept, rounds = {}, len(chunks) + len(stages) - 1
    for t in range(rounds):
        for n, stage in enumerate(stages):
            if 0 <= t - n < len(chunks):
                kept[n, t - n] = stage(chunks[t - n], kept.get((n - 1, t - n)))
        for work in between[t * len(between) // rounds : (t + 1) * len(between) // rounds]:
            work()


def halves_of(count):
    return (slice(0, count // 2), slice(count // 2, count))


def row_means(sums, width):
    return [jnp.sum(x, axis=-1, keepdims=True) * (1.0 / width) for x in sums]


def norm_back(rows, dxhat_ref, xhat_ref, means, put):
    mean_d, mean_dx, rstd = means
    for b in lane_blocks(dxhat_ref.shape[-1]):
        xhat = xhat_ref[rows, b].astype(F32)
        put(b, (dxhat_ref[rows, b] - mean_d - xhat * mean_dx) * rstd)


def add_terms(acc_ref, b, dy, xhat):
    acc_ref[0:8, b] += fold(dy * xhat)
    acc_ref[8:16, b] += fold(dy)


def open_sums(acc_ref):
    @pl.when(pl.program_id(0) == 0)
    def _():
        acc_ref[...] = jnp.zeros_like(acc_ref)


def close_sums(out_ref, acc_ref):
    @pl.when(pl.program_id(0) == pl.num_programs(0) - 1)
    def _():
        out_ref[0:1, :] = jnp.sum(acc_ref[0:8, :], axis=0, keepdims=True)
        out_ref[1:2, :] = jnp.sum(acc_ref[8:16, :], axis=0, keepdims=True)


def run_copies(copies):
    for copy in copies:
        copy.start()
    for copy in copies:
        copy.wait()


def piece_copies(pieces, full_ref, me, sem, first=0):
    each = full_ref.shape[0] // len(pieces)
    return [
        pltpu.make_async_copy(
            piece.at[0:each, :],
            full_ref.at[pl.ds(pl.multiple_of((me ^ k) * each, SUB), each), :],
            sem.at[first + k],
        )
        for k, piece in enumerate(pieces)
    ]


def out_copies(pieces, full_ref, me, sem, first=0):
    each, width = full_ref.shape[0] // len(pieces), full_ref.shape[1] // 2
    copies = []
    for k, piece in enumerate(pieces):
        rows = pl.ds(pl.multiple_of((me ^ k) * each, SUB), each)
        for side in range(2):
            at = piece.shape[0] - (2 - side) * each
            copies.append(
                pltpu.make_async_copy(
                    piece.at[at : at + each, :],
                    full_ref.at[rows, side * width : (side + 1) * width],
                    sem.at[first + 2 * k + side],
                )
            )
    return copies


def column(row):
    return jnp.transpose(jnp.broadcast_to(row, (LANE, LANE)))


CHUNK = 64


def norm_a_kernel(tok_ref, np_ref, hid_ref, slope_ref, xhat_ref, rstd_ref):
    def stats(rows, _):
        mean, rstd = row_stats(tok_ref, rows)
        rstd_ref[rows, :] = rstd
        return mean, rstd

    def work(rows, kept):
        mean, rstd = kept
        for b in lane_blocks(D):
            xhat = (tok_ref[rows, b].astype(F32) - mean) * rstd
            hidden, slope = gelu_and_slope(xhat * np_ref[0:1, b] + np_ref[1:2, b])
            hid_ref[rows, b] = hidden.astype(BF16)
            slope_ref[rows, b] = slope.astype(BF16)
            xhat_ref[rows, b] = xhat.astype(BF16)

    in_stages(tok_ref.shape[0], [stats, work])


def running_ends(ends_ref, lengths_ref):
    docs, width = lengths_ref.shape[0], ends_ref.shape[1]
    ends_ref[...] = jnp.zeros_like(ends_ref)
    ends_ref[0:1, 0:docs] = lengths_ref[...].reshape(1, -1).astype(F32)
    before = jnp.zeros((1, 1), F32)
    row = lax.broadcasted_iota(jnp.int32, (LANE, LANE), 0)
    lane = lax.broadcasted_iota(jnp.int32, (LANE, LANE), 1)
    for k in range(0, width, LANE):
        line = ends_ref[0:1, k : k + LANE]
        sums = jnp.sum(jnp.where(row <= lane, column(line), 0.0), axis=0, keepdims=True) + before
        ends_ref[0:1, k : k + LANE] = jnp.where(lane[0:1] + k < docs, sums, 1e9)
        before = before + jnp.sum(line, axis=1, keepdims=True)


def in_kernel(pieces, tiles, place_ref, lengths_ref, hid_ref, live_ref, np_ref, *refs):
    piece_refs = refs[:pieces]
    edges = tiles[0] == 0
    outs = refs[-(11 if edges else 9) :]
    mov_ref, slope_ref, xhat_ref, rstd_ref, mask_ref = outs[:5]
    w_ref, pre_ref, ends_ref, sem = outs[-4:]
    step = pl.program_id(0)
    tile = hid_ref.shape[0]

    @pl.when(step == 0)
    def _():
        copies = piece_copies(piece_refs, w_ref, place_ref[0], sem)
        for copy in copies:
            copy.start()
        running_ends(ends_ref, lengths_ref)
        for copy in copies:
            copy.wait()

    for half in halves_of(tile):
        pre_ref[half, :] = lax.dot_general(
            hid_ref[half, :], w_ref[...], NN, preferred_element_type=F32
        )

    at_tile = tiles[0] + step * tiles[1]
    first = place_ref[1] + at_tile * tile
    ends = ends_ref[0:1, :]
    lanes = lax.broadcasted_iota(jnp.int32, (LANE, 8), 1)
    offsets = ((lanes - MID) * DILATION_STEP).astype(F32)
    for k in range(tile // LANE):
        at = (first + k * LANE + lax.broadcasted_iota(jnp.int32, (LANE, 1), 0)).astype(F32)
        begin = jnp.max(jnp.where(ends <= at, ends, 0.0), axis=1, keepdims=True)
        end = jnp.min(jnp.where(ends > at, ends, 1e9), axis=1, keepdims=True)
        there = at + offsets
        same = jnp.where((there >= begin) & (there < end), 1.0, 0.0)
        live = column(live_ref[pl.ds(at_tile * (tile // LANE) + k, 1), :].astype(F32))
        mask_ref[k * LANE : (k + 1) * LANE, :] = jnp.where(lanes == MID, live[:, 0:8], same)

    def stats(rows, _):
        mean, rstd = row_stats(pre_ref, rows)
        rstd_ref[rows, :] = rstd
        return mean, rstd

    def work(rows, kept):
        mean, rstd = kept
        live = mask_ref[rows, MID : MID + 1]
        for b in lane_blocks(INNER):
            gains = slice(D + b.start, D + b.stop)
            xhat = (pre_ref[rows, b] - mean) * rstd
            hidden, slope = gelu_and_slope(xhat * np_ref[0:1, gains] + np_ref[1:2, gains])
            mov_ref[rows, b] = (hidden * live).astype(BF16)
            slope_ref[rows, b] = slope.astype(BF16)
            xhat_ref[rows, b] = xhat.astype(BF16)

    in_stages(tile, [stats, work])
    if edges:
        put_edges(place_ref, outs[5], outs[6], mov_ref, step == 0, step == 1)


def load_window(place_ref, inner, mid, outer, ext_ref, sem):
    rows, core = mid.shape[0], lax.rem(place_ref[0], 2)
    near = pl.multiple_of((1 - core) * (REACH + rows), SUB)
    far = pl.multiple_of(core * (REACH + rows), SUB)
    return [
        pltpu.make_async_copy(inner, ext_ref.at[pl.ds(near, REACH), :], sem.at[0]),
        pltpu.make_async_copy(mid, ext_ref.at[REACH : REACH + rows, :], sem.at[1]),
        pltpu.make_async_copy(outer, ext_ref.at[pl.ds(far, REACH), :], sem.at[2]),
    ]


def put_edges(place_ref, inner_ref, outer_ref, tile_ref, at_first, at_last):
    rows, core = tile_ref.shape[0], lax.rem(place_ref[0], 2)
    for at, edge, first in ((at_first, slice(0, REACH), 0), (at_last, slice(rows - REACH, rows), 1)):

        @pl.when(at & (core == first))
        def _(edge=edge):
            outer_ref[...] = tile_ref[edge, :]

        @pl.when(at & (core != first))
        def _(edge=edge):
            inner_ref[...] = tile_ref[edge, :]


def fill_taps(taps_ref, ext_ref, mask_ref, start):
    tile = taps_ref.shape[0]
    for j in range(KERNEL_TAPS):
        rows = pl.ds(pl.multiple_of(start + j * DILATION_STEP, DILATION_STEP), tile)
        picked = ext_ref[rows, :]
        if j != MID:
            picked = picked * mask_ref[:, j : j + 1].astype(BF16)
        taps_ref[:, j * INNER : (j + 1) * INNER] = picked


def conv_kernel(
    pieces, rows_of, place_ref, low_ref, mov_ref, high_ref, mask_ref, cot_ref, before_ref, np_ref, *refs
):
    piece_refs = refs[:pieces]
    hid_ref, dconv_ref, inner_ref, outer_ref, sums_ref, turned_ref = refs[pieces : pieces + 6]
    outs = refs[pieces + 6 : pieces + 10]
    ext_ref, wc_ref, wct_ref, wo_ref, wt_ref, taps_ref, pre_ref, dh_ref, xhat_ref = refs[
        pieces + 10 : pieces + 19
    ]
    dt_ref, ht_ref, gc_ref, go_ref, acc_ref, stage1_ref, stage2_ref, sem = refs[pieces + 19 :]
    step, steps = pl.program_id(0), pl.num_programs(0) - 1
    tile = taps_ref.shape[1]
    slot = lax.rem(step, 2)

    @pl.when(step == 0)
    def _():
        me = place_ref[0]
        outs = out_copies(piece_refs, wo_ref, me, sem, 3)
        rest = load_window(place_ref, low_ref, mov_ref, high_ref, ext_ref, sem)
        rest += piece_copies(piece_refs, wc_ref, me, sem, 3 + 2 * pieces)
        for copy in outs + rest:
            copy.start()
        for ref in (acc_ref, gc_ref, go_ref, dt_ref, ht_ref):
            ref[...] = jnp.zeros_like(ref)
        taps_ref[1] = jnp.zeros_like(taps_ref[1])
        for copy in outs:
            copy.wait()
        for k in range(0, D, 256):
            wt_ref[k : k + 256, :] = jnp.transpose(wo_ref[:, k : k + 256])
        for copy in rest:
            copy.wait()

    def grad_conv(cols):
        def work():
            gc_ref[:, cols] += lax.dot_general(
                dt_ref[...], taps_ref[1 - slot, :, cols], NN, preferred_element_type=F32
            )

        return work

    def grad_out(cols):
        def work():
            go_ref[:, cols] += lax.dot_general(
                ht_ref[...], before_ref[:, cols], NN, preferred_element_type=F32
            )

        return work

    taps_wide = KERNEL_TAPS * INNER
    products = [grad_conv(slice(k, min(k + 768, taps_wide))) for k in range(0, taps_wide, 768)]
    products += [grad_out(slice(k, min(k + 768, D))) for k in range(0, D, 768)]

    @pl.when(step < steps)
    def _():
        fill_taps(taps_ref.at[slot], ext_ref, mask_ref, step * tile)
        pre_ref[...] = lax.dot_general(
            taps_ref[slot], wc_ref[...], NN, preferred_element_type=F32
        )
        dh_ref[...] = lax.dot_general(cot_ref[...], wt_ref[...], NN, preferred_element_type=F32)
        for n in range(2):
            tap = jnp.minimum(2 * step + n, KERNEL_TAPS - 1)
            source = wc_ref[pl.ds(pl.multiple_of(tap * INNER, SUB), INNER), :]
            target = pl.multiple_of((KERNEL_TAPS - 1 - tap) * INNER, SUB)
            wct_ref[pl.ds(target, INNER), :] = jnp.transpose(source)

        def stats(rows, _):
            return row_stats(pre_ref, rows)

        def work(rows, kept):
            mean, rstd = kept
            sums = [0.0, 0.0]
            for b in lane_blocks(INNER):
                gains = slice(D + INNER + b.start, D + INNER + b.stop)
                gain = np_ref[0:1, gains]
                xhat = (pre_ref[rows, b] - mean) * rstd
                hidden, slope = gelu_and_slope(xhat * gain + np_ref[1:2, gains])
                hid_ref[rows, b] = hidden.astype(BF16)
                dy = dh_ref[rows, b] * slope
                add_terms(acc_ref, b, dy, xhat)
                dxhat = dy * gain
                xhat_ref[rows, b] = xhat
                dh_ref[rows, b] = dxhat
                sums = [sums[0] + dxhat, sums[1] + dxhat * xhat]
            return row_means(sums, INNER) + [rstd]

        def finish(rows, means):
            def put(b, value):
                dconv_ref[rows, b] = value.astype(BF16)

            norm_back(rows, dh_ref, xhat_ref, means, put)

        in_stages(tile, [stats, work, finish], products)
        dt_ref[...] = jnp.transpose(dconv_ref[...])
        ht_ref[...] = jnp.transpose(hid_ref[...])

    put_edges(place_ref, inner_ref, outer_ref, dconv_ref, step == 0, step == steps - 1)

    @pl.when(step == steps)
    def _():
        copy = pltpu.make_async_copy(wct_ref, turned_ref, sem.at[4])
        copy.start()
        for work in products:
            work()
        core = lax.rem(place_ref[0], 2)
        _, rows_conv, rows_out = rows_of
        stage_turned(stage1_ref, core, gc_ref, rows_conv, 0, slice(0, CUT // LANE))
        first_tiles = rows_conv // SUB * (CUT // LANE)
        stage_plain(stage1_ref, core, go_ref, rows_out, first_tiles)
        copies = stage_copies(stage1_ref, outs[0], outs[1], spans(CHUNKS[0], rows_of)[1], sem, 0)
        for each in copies:
            each.start()
        stage_turned(stage2_ref, core, gc_ref, rows_conv, 0, slice(CUT // LANE, INNER // LANE))
        more = stage_copies(stage2_ref, outs[2], outs[3], spans(CHUNKS[1], rows_of)[1], sem, 2)
        for each in more:
            each.start()
        for each in copies + more + [copy]:
            each.wait()
        sums_ref[0:1, :] = jnp.sum(acc_ref[0:8, :], axis=0, keepdims=True)
        sums_ref[1:2, :] = jnp.sum(acc_ref[8:16, :], axis=0, keepdims=True)


def stage_tiles(stage_ref, core, first_row, rows_each, base, block0, blocks, value):
    for g in range(value.shape[0] // SUB):
        row = first_row + g * SUB
        owner, inside = row // rows_each, row % rows_each // SUB
        side = core ^ (owner % 2)
        for b in range(value.shape[1] // LANE):
            tile = value[g * SUB : (g + 1) * SUB, b * LANE : (b + 1) * LANE]
            at = base + inside * blocks + block0 + b
            stage_ref[side, owner // 2, at] = tile.astype(BF16)


def stage_plain(stage_ref, core, grad_ref, rows_each, base):
    blocks = grad_ref.shape[1] // LANE
    for row in range(0, grad_ref.shape[0], SUB):
        part = grad_ref[row : row + SUB, :]
        stage_tiles(stage_ref, core, row, rows_each, base, 0, blocks, part)


def stage_turned(stage_ref, core, turned_ref, rows_each, base, blocks):
    count = blocks.stop - blocks.start
    for row in range(0, turned_ref.shape[1], LANE):
        for b in range(count):
            at = (blocks.start + b) * LANE
            part = jnp.transpose(turned_ref[at : at + LANE, row : row + LANE].astype(BF16))
            stage_tiles(stage_ref, core, row, rows_each, base, b, count, part)


def stage_copies(stage_ref, keep_ref, send_ref, used, sem, first):
    count = stage_ref.shape[2]
    if used < count:
        dims = stage_ref.shape[:2] + (count - used, SUB, LANE)
        stage_ref[:, :, used:] = jnp.zeros(dims, BF16)
    return [
        pltpu.make_async_copy(stage_ref.at[n], ref, sem.at[first + n])
        for n, ref in enumerate((keep_ref, send_ref))
    ]


def back_conv_kernel(
    last, rows_in, place_ref, low_ref, d_ref, high_ref, turned_ref, mask_ref, xhat_ref, rstd_ref, slope_ref, hid_ref, np_ref, *refs
):
    if last:
        before_ref, dpre_ref, sums_ref, keep_ref, send_ref, stage_ref = refs[:6]
    else:
        dpre_ref, sums_ref, part_ref = refs[:3]
    ext_ref, wt_ref, taps_ref, dmov_ref, grad_ref, acc_ref, sem = refs[-7:]
    step, steps = pl.program_id(0), pl.num_programs(0)
    tile = taps_ref.shape[0]
    open_sums(acc_ref)

    @pl.when(step == 0)
    def _():
        copies = load_window(place_ref, low_ref, d_ref, high_ref, ext_ref, sem)
        copies.append(pltpu.make_async_copy(turned_ref, wt_ref, sem.at[3]))
        if last:
            copies.append(pltpu.make_async_copy(before_ref, grad_ref, sem.at[4]))
        for copy in copies:
            copy.start()
        if not last:
            grad_ref[...] = jnp.zeros_like(grad_ref)
        for copy in copies:
            copy.wait()

    fill_taps(taps_ref, ext_ref, mask_ref, (steps * last + step) * tile)
    for half in halves_of(tile):
        dmov_ref[half, :] = lax.dot_general(
            taps_ref[half, :], wt_ref[...], NN, preferred_element_type=F32
        )

    def work(rows, _):
        live = mask_ref[rows, MID : MID + 1]
        sums = [0.0, 0.0]
        for b in lane_blocks(INNER):
            xhat = xhat_ref[rows, b].astype(F32)
            dy = dmov_ref[rows, b] * live * slope_ref[rows, b].astype(F32)
            add_terms(acc_ref, b, dy, xhat)
            dxhat = dy * np_ref[0:1, D + b.start : D + b.stop]
            dmov_ref[rows, b] = dxhat
            sums = [sums[0] + dxhat, sums[1] + dxhat * xhat]
        return row_means(sums, INNER) + [rstd_ref[rows, :]]

    def finish(rows, means):
        def put(b, value):
            dpre_ref[rows, b] = value.astype(BF16)

        norm_back(rows, dmov_ref, xhat_ref, means, put)

    in_stages(tile, [work, finish])
    close_sums(sums_ref, acc_ref)
    grad_ref[...] += lax.dot_general(dpre_ref[...], hid_ref[...], TN, preferred_element_type=F32)

    @pl.when(step == steps - 1)
    def _():
        if last:
            all_blocks = slice(0, INNER // LANE)
            stage_turned(stage_ref, lax.rem(place_ref[0], 2), grad_ref, rows_in, 0, all_blocks)
            used = rows_in // SUB * (INNER // LANE)
            run_copies(stage_copies(stage_ref, keep_ref, send_ref, used, sem, 0))
        else:
            run_copies([pltpu.make_async_copy(grad_ref, part_ref, sem.at[0])])


def back_a_kernel(pieces, half, place_ref, dpre0_ref, dpre1_ref, xhat_ref, rstd_ref, slope_ref, cot_ref, np_ref, *refs):
    piece_refs = refs[:pieces]
    grad_ref, sums_ref, w_ref, wt_ref, dh_ref, acc_ref, sem = refs[-7:]
    open_sums(acc_ref)

    @pl.when(pl.program_id(0) == 0)
    def _():
        run_copies(piece_copies(piece_refs, w_ref, place_ref[0], sem))
        for k in range(0, D, 256):
            wt_ref[:, k : k + 256] = jnp.transpose(w_ref[k : k + 256, :])

    second = (jnp.zeros((1, 1), jnp.int32) + pl.program_id(0)) >= half
    d_pre = jnp.where(second, dpre1_ref[...], dpre0_ref[...])
    dh_ref[...] = lax.dot_general(d_pre, wt_ref[...], NN, preferred_element_type=F32)

    def work(rows, _):
        sums = [0.0, 0.0]
        for b in lane_blocks(D):
            xhat = xhat_ref[rows, b].astype(F32)
            dy = dh_ref[rows, b] * slope_ref[rows, b].astype(F32)
            add_terms(acc_ref, b, dy, xhat)
            dxhat = dy * np_ref[0:1, b]
            dh_ref[rows, b] = dxhat
            sums = [sums[0] + dxhat, sums[1] + dxhat * xhat]
        return row_means(sums, D) + [rstd_ref[rows, :]]

    def finish(rows, means):
        def put(b, value):
            grad_ref[rows, b] = cot_ref[rows, b].astype(F32) + value

        norm_back(rows, dh_ref, xhat_ref, means, put)

    in_stages(dpre0_ref.shape[0], [work, finish])
    close_sums(sums_ref, acc_ref)


def out_kernel(pieces, place_ref, hid_ref, tok_ref, *refs):
    piece_refs = refs[:pieces]
    out_ref, w_ref, sem = refs[pieces:]

    @pl.when(pl.program_id(0) == 0)
    def _():
        run_copies(out_copies(piece_refs, w_ref, place_ref[0], sem))

    branch = lax.dot_general(hid_ref[...], w_ref[...], NN, preferred_element_type=F32)
    out_ref[...] = (tok_ref[...].astype(F32) + branch).astype(BF16)


WIDTHS = (INNER, INNER, D)
LANE0 = (0, INNER, 2 * INNER)
CUT = 2 * LANE
CHUNKS = (((1, 0, CUT), (2, 0, D)), ((1, CUT, INNER - CUT),), ((0, 0, INNER),))


def spans(chunk, rows):
    found, first = [], 0
    for weight, col, cols in chunk:
        tiles = rows[weight] // SUB * (cols // LANE)
        found.append((weight, col // LANE, cols // LANE, first, tiles))
        first += tiles
    return found, first


def column_sums(pack_ref, row, ref, chunk, rows):
    for weight, block0, blocks, first, tiles in spans(chunk, rows)[0]:

        def body(g, carry, first=first, blocks=blocks):
            new = []
            for b in range(blocks):
                value = ref[first + g * blocks + b].astype(F32)
                new.append(carry[b] + fold(value * value + 1e-30))
            return tuple(new)

        zero = tuple(jnp.zeros((8, LANE), F32) for _ in range(blocks))
        cols = lax.fori_loop(0, tiles // blocks, body, zero, unroll=5)
        for b in range(blocks):
            lane = LANE0[weight] + (block0 + b) * LANE
            pack_ref[row : row + 1, lane : lane + LANE] = jnp.sum(cols[b], axis=0, keepdims=True)


def load_full(got_ref, place_ref, full_ref, sem):
    parts = got_ref.shape[0]
    each = full_ref.shape[0] // parts
    return [
        pltpu.make_async_copy(
            got_ref.at[p, 0:each],
            full_ref.at[pl.ds((p % 2 * (parts // 2) + p // 2) * each, each)],
            sem.at[p],
        )
        for p in range(parts)
    ]


def pack_kernel(rows, pieces, place_ref, part_ref, *refs):
    states, (pack_ref, acc_ref) = refs[0:3], refs[3:5]
    pack_ref[...] = jnp.zeros_like(pack_ref)
    lanes = lax.broadcasted_iota(jnp.int32, (1, LANE), 1)
    for k in range(3):
        total = jnp.sum(states[k][...].reshape(1, -1), axis=1, keepdims=True)
        pack_ref[1:2, 0:LANE] += jnp.where(lanes == k, total, 0.0)
    acc_ref[...] = jnp.zeros_like(acc_ref)
    spare = acc_ref.shape[0] - 1
    outer = place_ref[3] // 2
    piece = place_ref[2] % 2 * outer + place_ref[2] // 2
    at = 0
    for chunk, each in zip(CHUNKS[:2], pieces):
        found, _ = spans(chunk, rows)
        start = piece * each

        def body(k, carry, found=found, start=start, at=at):
            n = start + k
            slot = spare
            for weight, block0, blocks, first, tiles in found:
                here = LANE0[weight] // LANE + block0 + lax.rem(jnp.maximum(n - first, 0), blocks)
                slot = jnp.where((n >= first) & (n < first + tiles), here, slot)
            value = part_ref[at + k].astype(F32)
            acc_ref[slot] += value * value + 1e-30
            return carry

        lax.fori_loop(0, each, body, 0, unroll=2)
        at += each
    for slot in range(spare):
        pack_ref[0:1, slot * LANE : (slot + 1) * LANE] = jnp.sum(acc_ref[slot], axis=0, keepdims=True)


def norm_tiles_kernel(parts, *refs):
    sums, out_ref, line_ref = refs[:-2], refs[-2], refs[-1]
    line_ref[...] = jnp.zeros_like(line_ref)
    lanes_of = ((0, D), (D, D + INNER), (D, D + INNER), (D + INNER, D + 2 * INNER))
    for part, (lane0, lane1) in zip(sums, lanes_of):
        line_ref[0:2, lane0:lane1] += part[...]
    out_ref[...] = jnp.zeros_like(out_ref)
    blocks = (D + 2 * INNER) // LANE
    each = -(-2 * blocks // parts)
    for part in range(-(-2 * blocks // each)):
        rows = []
        for n in range(part * each, min((part + 1) * each, 2 * blocks)):
            row, b = n // blocks, n % blocks
            rows.append(line_ref[row : row + 1, b * LANE : (b + 1) * LANE])
        rows += [jnp.zeros((1, LANE), F32)] * (8 - len(rows))
        value = jnp.concatenate(rows, axis=0)
        high = value.astype(BF16).astype(F32)
        out_ref[part] = jnp.concatenate([high, value - high], axis=0).astype(BF16)


def high_low(total):
    value = total[..., 0:8, :] + total[..., 8:16, :]
    high = value.astype(BF16).astype(F32)
    return jnp.concatenate([high, value - high], axis=-2).astype(BF16)


def pack_in_kernel(rows, place_ref, got_ref, out_ref, full_ref, norms_ref, sem, norms_sem):
    parts = got_ref.shape[0]
    each = full_ref.shape[0] // parts
    copies = load_full(got_ref, place_ref, full_ref, sem)
    copies += [
        pltpu.make_async_copy(got_ref.at[p, each], norms_ref.at[p], norms_sem.at[p])
        for p in range(parts)
    ]
    run_copies(copies)
    out_ref[...] = jnp.zeros_like(out_ref)
    blocks = (D + 2 * INNER) // LANE
    rows_each = -(-2 * blocks // parts)
    for n in range(2 * blocks):
        part, at = n // rows_each, n % rows_each
        value = norms_ref[part].astype(F32)
        row, lane = n // blocks, n % blocks * LANE
        out_ref[row : row + 1, lane : lane + LANE] = value[at : at + 1] + value[8 + at : 9 + at]
    column_sums(out_ref, 2, full_ref, CHUNKS[2], rows)


def update_weight(
    k, squares, states_sum, source, weight, state, col_state, grad_ref, new, row_new_ref, col_new_ref, scratch
):
    line_ref, state_ref, new_ref = scratch
    width, fan, rows_here = WIDTHS[k], (D, KERNEL_TAPS * INNER, INNER)[k], weight.shape[0]
    col_new = DECAY * col_state[...].reshape(1, -1) + (1.0 - DECAY) * (squares * (1.0 / fan))
    col_new_ref[...] = col_new.reshape(-1)
    total = DECAY * states_sum
    total = total + (1.0 - DECAY) * (1.0 / width) * jnp.sum(squares, axis=1, keepdims=True)
    scaled = col_new / (total * (1.0 / fan))
    rate = 0.5 / fan**0.5
    line_ref[0:1, 0:rows_here] = state[...].reshape(1, -1)
    whole_rows = rows_here + -rows_here % LANE
    for c in range(0, whole_rows, LANE):
        state_ref[c : c + LANE, :] = column(line_ref[0:1, c : c + LANE])

    def body(g, carry):
        rows = pl.ds(pl.multiple_of(g * SUB, SUB), SUB)
        square = 0.0
        for ref, block0, blocks, first in source:
            for b in range(blocks):
                value = ref[first + g * blocks + b].astype(F32)
                grad_ref[rows, (block0 + b) * LANE : (block0 + b + 1) * LANE] = value
                square = square + (value * value + 1e-30)
        mean = jnp.sum(square, axis=1, keepdims=True) * (1.0 / width)
        row_new = DECAY * state_ref[rows, :] + (1.0 - DECAY) * mean
        new_ref[rows, :] = row_new
        for ref, block0, blocks, first in source:
            for b in range(blocks):
                lanes = slice((block0 + b) * LANE, (block0 + b + 1) * LANE)
                value = ref[first + g * blocks + b].astype(F32)
                step = value * lax.rsqrt(row_new * scaled[:, lanes])
                new[rows, lanes] = weight[rows, lanes] - rate * step
        return carry

    lax.fori_loop(0, rows_here // SUB, body, 0, unroll=5)
    for c in range(0, whole_rows, LANE):
        line_ref[0:1, c : c + LANE] = jnp.transpose(new_ref[c : c + LANE, :])[0:1, :]
    row_new_ref[...] = line_ref[0:1, 0:rows_here].reshape(-1)


def sources_of(chunk, ref, rows):
    return {w: (ref, block0, blocks, first) for w, block0, blocks, first, _ in spans(chunk, rows)[0]}


def update_kernel(rows, copies_of, place_ref, got_ref, pack_ref, *refs):
    weights, states, col_states = refs[0:2], refs[2:4], refs[4:6]
    grads, news, rows_new, cols_new = refs[6:8], refs[8:10], refs[10:12], refs[12:14]
    full1_ref, full2_ref, sem1, sem2 = refs[17:21]
    each = full1_ref.shape[0] // got_ref.shape[0]
    run_copies(
        load_full(got_ref.at[:, 0:each], place_ref, full1_ref, sem1)
        + load_full(got_ref.at[:, each:], place_ref, full2_ref, sem2)
    )
    from1 = sources_of(CHUNKS[0], full1_ref, rows)
    from2 = sources_of(CHUNKS[1], full2_ref, rows)
    for n, (k, source) in enumerate(((1, [from1[1], from2[1]]), (2, [from1[2]]))):
        squares = pack_ref[0:1, LANE0[k] : LANE0[k] + WIDTHS[k]]
        update_weight(
            k, squares, pack_ref[1:2, k : k + 1] * (1.0 / copies_of), source, weights[n],
            states[n], col_states[n], grads[n], news[n], rows_new[n], cols_new[n], refs[14:17],
        )


def update_in_kernel(
    rows, copies_of, place_ref, got_ref, pack_in_ref, pack_ref, np_ref, second_ref, *refs
):
    weight, state, col_state, grad_ref, new_ref, row_new_ref, col_new_ref = refs[0:7]
    ngrad_ref, nsecond_ref, nnew_ref = refs[7:10]
    full_ref, sem = refs[13:15]
    copies = load_full(got_ref, place_ref, full_ref, sem)
    for copy in copies:
        copy.start()
    grad = pack_in_ref[0:2, :]
    second = DECAY * second_ref[...] + (1.0 - DECAY) * (grad * grad + 1e-30)
    ngrad_ref[...] = grad
    nsecond_ref[...] = second
    nnew_ref[...] = np_ref[...] - 0.2 * grad * lax.rsqrt(second)
    for copy in copies:
        copy.wait()
    update_weight(
        0, pack_in_ref[2:3, 0:INNER], pack_ref[1:2, 0:1] * (1.0 / copies_of),
        [sources_of(CHUNKS[2], full_ref, rows)[0]], weight, state, col_state, grad_ref, new_ref,
        row_new_ref, col_new_ref, refs[10:13],
    )


class Places:
    def __init__(self):
        self.seq, self.fsdp = lax.axis_size("seq"), lax.axis_size("fsdp")
        self.q = lax.axis_index("fsdp")
        self.s = lax.axis_index("seq")

    def flip(self, x, axis, bit):
        pairs = []
        for s in range(self.seq):
            for f in range(self.fsdp):
                s2, f2 = (s ^ bit, f) if axis == "seq" else (s, f ^ bit)
                pairs.append((s * self.fsdp + f, s2 * self.fsdp + f2))
        return lax.ppermute(x, AXES, pairs)


def bits_of(count):
    return [1 << k for k in range(count.bit_length() - 1)]


def tie(x, *others):
    return lax.optimization_barrier((x, *others))[0]


def gather_pieces(piece, place, after, later=()):
    found = {0: piece}
    for bit in reversed(bits_of(place.fsdp)):
        for k in list(found):
            moving = found[k]
            if bit == 1:
                moving = tie(moving, *((after,) if k == 0 or not later else later))
            found[k | bit] = place.flip(moving, "fsdp", bit)
    return [found[k] for k in range(place.fsdp)]


def sum_over(x, place, *axes):
    for axis in axes:
        for bit in bits_of(getattr(place, axis)):
            x = x + place.flip(x, axis, bit)
    return x


def pick(x, index, axis):
    return lax.dynamic_index_in_dim(x, index, axis=axis, keepdims=False)


class Reduction:
    def __init__(self, place, keep, send):
        self.place, self.near = place, keep
        self.got = place.flip(send, "fsdp", 1)

    def halve(self, axis, side, flip_axis, bit):
        dims = self.near.shape
        parts = dims[:axis] + (2, dims[axis] // 2) + dims[axis + 1 :]
        near, got = self.near.reshape(parts), self.got.reshape(parts)
        away = pick(near, 1 - side, axis).astype(F32) + pick(got, 1 - side, axis).astype(F32)
        self.near = pick(near, side, axis).astype(F32) + pick(got, side, axis).astype(F32)
        away = away.astype(BF16)
        self.got = self.place.flip(away, flip_axis, bit)
        return away

    def x(self):
        bit = self.place.fsdp // 2
        while bit > 1:
            away = self.halve(0, (self.place.q // bit) % 2, "fsdp", bit)
            bit //= 2
        return away

    def y(self):
        return self.halve(1, self.place.s % 2, "seq", 1)

    def all_pieces(self):
        total = (self.near + self.got.astype(F32)).astype(BF16)
        total = total.reshape((2, self.place.seq // 2, -1) + total.shape[2:])
        return jnp.swapaxes(total, 0, 1).reshape((self.place.seq,) + total.shape[2:])

    def pieces(self):
        total = (self.near + self.got.astype(F32)).astype(BF16)
        return total.reshape((self.place.seq // 2, -1) + total.shape[2:])


def arrive(result, *reductions):
    result, *gots = lax.optimization_barrier((result, *[r.got for r in reductions]))
    for reduction, got in zip(reductions, gots):
        reduction.got = got
    return result


def summed_f32(got):
    return jnp.sum(got.astype(F32), axis=0)


def summed(got):
    return summed_f32(got).astype(BF16)


def exchange_all(sent):
    return lax.all_to_all(sent, "seq", 0, 0)


def exchange(place, sent):
    line = [[y + 2 * z for z in range(place.seq // 2)] for y in range(2)]
    return lax.all_to_all(sent, "seq", 0, 0, axis_index_groups=line)


def on_device(
    tokens, input_mask, doc_lengths, cotangent, w_in, w_conv, w_out, norm_params,
    row_in, col_in, row_conv, col_conv, row_out, col_out, norm_second,
):
    place = Places()
    rows = tokens.shape[0]
    pieces = place.fsdp
    spots = jnp.stack(
        [place.q, (place.s * place.fsdp + place.q) * rows, place.s, place.seq]
    ).astype(jnp.int32)
    docs = doc_lengths.shape[0]
    live = input_mask.reshape(-1, LANE)
    weights = (w_in, w_conv, w_out)
    rows_of = [w.shape[0] for w in weights]

    tile_a, tile = 256, 512
    steps = rows // tile
    params_spec = whole(2, D + 2 * INNER)
    dma = pltpu.SemaphoreType.DMA

    out_sides = (w_out[:, : D // 2], w_out[:, D // 2 :])
    conv_out = jnp.concatenate([w_conv, *out_sides], axis=0).astype(BF16)
    hidden_a, slope_a, xhat_a, rstd_a = call(
        norm_a_kernel,
        (rows // tile_a,),
        [rows_spec(tile_a, D), params_spec],
        [rows_spec(tile_a, D)] * 3 + [rows_spec(tile_a, 1)],
        [shape((rows, D), BF16)] * 3 + [shape((rows, 1), F32)],
        us=17,
    )(tokens, tie(norm_params, conv_out))

    in_pieces = gather_pieces(w_in.astype(BF16), place, hidden_a)

    def in_call(tiles, count, before):
        at, stride = tiles

        def here_spec(width):
            return pl.BlockSpec((tile, width), lambda i: (at + stride * i, 0))

        out_shapes = [shape((rows, INNER), BF16)] * 3 + [shape((rows, 1), F32), shape((rows, 8), F32)]
        out_specs = [here_spec(INNER)] * 3 + [here_spec(1), here_spec(8)]
        if at == 0:
            out_shapes += [shape((REACH, INNER), BF16)] * 2
            out_specs += [whole(REACH, INNER)] * 2
        return call(
            functools.partial(in_kernel, pieces, tiles),
            (count,),
            [SMEM, whole(docs), here_spec(D), whole(*live.shape), params_spec]
            + [ANY] * (pieces + len(before)),
            out_specs,
            out_shapes,
            [pltpu.VMEM((D, INNER), BF16), pltpu.VMEM((tile, INNER), F32)]
            + [pltpu.VMEM((8, docs + -docs % LANE), F32), dma((pieces,))],
            us=3,
            aliases={5 + pieces + k: k for k in range(len(before))},
        )(spots, doc_lengths, hidden_a, live, norm_params, *in_pieces, *before)

    *kept, m_first, m_last = in_call((0, steps - 1), 2, ())
    moved, slope_b, xhat_b, rstd_b, masks = in_call((1, 1), steps - 2, kept)

    def halo(inner, outer):
        total = place.seq * place.fsdp
        across = [(i, i + 1 if i % 2 else i - 1) for i in range(1, total - 1)]
        return place.flip(inner, "fsdp", 1), lax.ppermute(outer, AXES, across)

    m_inner, m_outer = halo(m_first, m_last)
    conv_pieces = gather_pieces(conv_out, place, m_first, (moved, m_inner, m_outer))

    ext = pltpu.VMEM((rows + 2 * REACH, INNER), BF16)
    taps_wide = KERNEL_TAPS * INNER
    wide = pltpu.VMEM((taps_wide, INNER), BF16)
    shards = place.fsdp // 2

    def half_dims(chunk):
        count = spans(chunk, rows_of)[1]
        return (shards, count + -count % place.seq, SUB, LANE)

    def tile_spec(width, ahead):
        return pl.BlockSpec((tile, width), lambda i: (jnp.clip(i + ahead, 0, steps - 1), 0))

    halves = [half_dims(CHUNKS[0])] * 2 + [half_dims(CHUNKS[1])] * 2
    work = pltpu.VMEM((tile, INNER), F32)
    turned_tile = pltpu.VMEM((INNER, tile), BF16)
    hidden_c, d_conv, d_first, d_last, sums_c, turned, keep1, send1, keep2, send2 = call(
        functools.partial(conv_kernel, pieces, rows_of),
        (steps + 1,),
        [SMEM, ANY, ANY, ANY, tile_spec(8, 0), tile_spec(D, 0), tile_spec(D, -1), params_spec]
        + [ANY] * pieces,
        [tile_spec(INNER, 0)] * 2
        + [whole(REACH, INNER), whole(REACH, INNER), whole(2, INNER)]
        + [ANY] * 5,
        [
            shape((rows, INNER), BF16),
            shape((rows, INNER), BF16),
            shape((REACH, INNER), BF16),
            shape((REACH, INNER), BF16),
            shape((2, INNER), F32),
            shape((taps_wide, INNER), BF16),
        ]
        + [shape(dims, BF16) for dims in halves],
        [ext, wide, wide, pltpu.VMEM((INNER, D), BF16), pltpu.VMEM((D, INNER), BF16)]
        + [pltpu.VMEM((2, tile, taps_wide), BF16), work, work, work, turned_tile, turned_tile]
        + [pltpu.VMEM((INNER, taps_wide), F32), pltpu.VMEM((INNER, D), F32)]
        + [pltpu.VMEM((16, INNER), F32)]
        + [pltpu.VMEM((2,) + halves[0], BF16), pltpu.VMEM((2,) + halves[2], BF16)]
        + [dma((3 + 3 * pieces,))],
        us=45,
    )(
        spots, m_inner, moved, m_outer, masks, cotangent, cotangent, norm_params, *conv_pieces
    )
    d_inner, d_outer = halo(d_first, d_last)
    first, second = Reduction(place, keep1, send1), Reduction(place, keep2, send2)
    (block_out,) = call(
        functools.partial(out_kernel, pieces),
        (steps,),
        [SMEM, rows_spec(tile, INNER), rows_spec(tile, D)] + [ANY] * pieces,
        [rows_spec(tile, D)],
        [shape((rows, D), BF16)],
        [pltpu.VMEM((INNER, D), BF16), dma((2 * pieces,))],
        us=9,
    )(spots, hidden_c, tokens, *conv_pieces)

    def back_conv(last, spots, before):
        here = steps // 2
        at = here * last

        def here_spec(width):
            return pl.BlockSpec((tile, width), lambda i: (i + at, 0))

        dims = half_dims(CHUNKS[2])
        return call(
            functools.partial(back_conv_kernel, last, w_in.shape[0]),
            (here,),
            [SMEM] + [ANY] * 4
            + [here_spec(8), here_spec(INNER), here_spec(1), here_spec(INNER), here_spec(D)]
            + [params_spec]
            + [ANY] * last,
            [rows_spec(tile, INNER), whole(2, INNER)] + [ANY] * (1 + last),
            [shape((rows // 2, INNER), BF16), shape((2, INNER), F32)]
            + ([shape(dims, BF16)] * 2 if last else [shape((INNER, D), F32)]),
            ([pltpu.VMEM((2,) + dims, BF16)] if last else [])
            + [
                ext,
                wide,
                pltpu.VMEM((tile, taps_wide), BF16),
                pltpu.VMEM((tile, INNER), F32),
                pltpu.VMEM((INNER, D), F32),
                pltpu.VMEM((16, INNER), F32),
                dma((5,)),
            ],
            us=16,
        )(
            spots, d_inner, d_conv, d_outer, turned, masks, xhat_b, rstd_b, slope_b, hidden_a,
            norm_params, *before,
        )

    block_out, d_inner, d_outer = arrive((block_out, d_inner, d_outer), first, second)
    away = (first.x(), second.y())
    d_pre0, sums_b0, grad_part = back_conv(0, tie(spots, *away), ())
    d_pre0 = arrive(d_pre0, first, second)
    away = (first.y(), second.x())
    d_pre1, sums_b1, keep, send = back_conv(1, tie(spots, *away), (grad_part,))
    send = arrive(send, first, second)
    third = Reduction(place, keep, send)
    sent = jnp.concatenate([first.pieces(), second.pieces()], axis=1)
    got = exchange(place, sent)
    third.got = tie(third.got, sent)
    away = (sent, third.x())
    input_grad, sums_a = call(
        functools.partial(back_a_kernel, pieces, steps // 2),
        (steps,),
        [SMEM]
        + [
            pl.BlockSpec((tile, INNER), lambda i: (jnp.minimum(i, steps // 2 - 1), 0)),
            pl.BlockSpec((tile, INNER), lambda i: (jnp.maximum(i - steps // 2, 0), 0)),
        ]
        + [rows_spec(tile, D), rows_spec(tile, 1), rows_spec(tile, D), rows_spec(tile, D)]
        + [params_spec]
        + [ANY] * pieces,
        [rows_spec(tile, D), whole(2, D)],
        [shape((rows, D), F32), shape((2, D), F32)],
        [
            pltpu.VMEM((D, INNER), BF16),
            pltpu.VMEM((INNER, D), BF16),
            pltpu.VMEM((tile, D), F32),
            pltpu.VMEM((16, D), F32),
            dma((pieces,)),
        ],
        us=17,
    )(
        tie(spots, *away), d_pre0, d_pre1, xhat_a, rstd_a, slope_a, cotangent, norm_params, *in_pieces
    )

    row_states, col_states = (row_in, row_conv, row_out), (col_in, col_conv, col_out)
    row_specs = [whole(*r.shape) for r in row_states]
    col_specs = [whole(*c.shape) for c in col_states]
    cols_all = D + 2 * INNER
    pack_spec = whole(4, cols_all)
    fulls = [pltpu.VMEM(half_dims(c)[1:], BF16) for c in CHUNKS]
    sums = (sums_a, sums_b0, sums_b1, sums_c)
    norm_tiles = call(
        functools.partial(norm_tiles_kernel, place.seq),
        (1,),
        [whole(*x.shape) for x in sums],
        whole(place.seq, SUB, LANE),
        shape((place.seq, SUB, LANE), BF16),
        [pltpu.VMEM((8, cols_all), F32)],
        us=1,
    )(*sums)
    got, third.got, norm_tiles = lax.optimization_barrier((got, third.got, norm_tiles))
    part = summed(got)
    sent = jnp.concatenate([third.all_pieces(), norm_tiles[:, None]], axis=1)
    got = exchange_all(sent)
    gathered = lax.all_gather(part, "seq", axis=0)
    part = tie(part, sent)
    (pack,) = call(
        functools.partial(pack_kernel, rows_of, [half_dims(c)[1] // place.seq for c in CHUNKS]),
        (1,),
        [SMEM, whole(*part.shape)] + row_specs,
        [pack_spec],
        [shape((4, cols_all), F32)],
        [pltpu.VMEM((cols_all // LANE + 1, SUB, LANE), F32)],
        us=2,
    )(spots, part, *row_states)
    pack = sum_over(pack, place, "fsdp")
    got, pack = lax.optimization_barrier((got, pack))
    last = summed_f32(got)
    last = jnp.concatenate([last[:-1].astype(BF16), high_low(last[-1:])], axis=0)
    got_in = exchange_all(jnp.broadcast_to(last[None], (place.seq,) + last.shape))
    pack = sum_over(pack, place, "seq")
    got_in, pack = lax.optimization_barrier((got_in, pack))

    def update_scratch(weights):
        lines = max(w.shape[0] + -w.shape[0] % LANE for w in weights)
        return [pltpu.VMEM((8, lines), F32)] + [pltpu.VMEM((lines, LANE), F32)] * 2

    weight_specs = [whole(*w.shape) for w in weights]
    (pack_in,) = call(
        functools.partial(pack_in_kernel, rows_of),
        (1,),
        [SMEM, ANY],
        [pack_spec],
        [shape((4, cols_all), F32)],
        [fulls[2], pltpu.VMEM((place.seq, SUB, LANE), BF16)] + [dma((place.seq,))] * 2,
        us=2,
    )(spots, got_in)
    pack_in = sum_over(pack_in, place, "fsdp")
    results = call(
        functools.partial(update_kernel, rows_of, place.seq),
        (1,),
        [SMEM, ANY, pack_spec] + weight_specs[1:] + row_specs[1:] + col_specs[1:],
        weight_specs[1:] * 2 + row_specs[1:] + col_specs[1:],
        [shape(w.shape, F32) for w in weights[1:]] * 2
        + [shape(r.shape, F32) for r in row_states[1:] + col_states[1:]],
        update_scratch(weights[1:]) + fulls[:2] + [dma((place.seq,))] * 2,
        us=8,
    )(spots, gathered, pack, *weights[1:], *row_states[1:], *col_states[1:])
    grad_conv, grad_out, new_conv, new_out, row_conv_new, row_out_new, col_conv_new, col_out_new = (
        results
    )
    grad_in, new_in, row_in_new, col_in_new, *norm_results = call(
        functools.partial(update_in_kernel, rows_of, place.seq),
        (1,),
        [SMEM, ANY, pack_spec, pack_spec, params_spec, params_spec]
        + [weight_specs[0], row_specs[0], col_specs[0]],
        [weight_specs[0]] * 2 + [row_specs[0], col_specs[0]] + [params_spec] * 3,
        [shape(w_in.shape, F32)] * 2
        + [shape(row_in.shape, F32), shape(col_in.shape, F32)]
        + [shape((2, cols_all), F32)] * 3,
        update_scratch(weights[:1]) + [fulls[2], dma((place.seq,))],
        us=4,
    )(spots, got_in, pack_in, pack, norm_params, norm_second, w_in, row_in, col_in)
    return (
        block_out,
        input_grad,
        grad_in,
        grad_conv,
        grad_out,
        new_in,
        new_conv,
        new_out,
        row_in_new,
        col_in_new,
        row_conv_new,
        col_conv_new,
        row_out_new,
        col_out_new,
        *norm_results,
    )


def solution(mesh):
    both, rows = P(AXES, None), P("fsdp", None)
    in_specs = (
        both, P(AXES), P(), both, rows, rows, rows, P(),
        P("fsdp"), P(), P("fsdp"), P(), P("fsdp"), P(), P(),
    )
    out_specs = (
        both, both, rows, rows, rows, rows, rows, rows,
        P("fsdp"), P(), P("fsdp"), P(), P("fsdp"), P(), P(), P(), P(),
    )
    return jax.shard_map(
        on_device, mesh=mesh, in_specs=in_specs, out_specs=out_specs, check_vma=False
    )
```

```python
import functools
import math

import jax
import jax.numpy as jnp
from jax import lax
from jax.experimental import pallas as pl
from jax.experimental.pallas import tpu as pltpu
from jax.sharding import PartitionSpec as P

D = 1280
INNER = 640
KERNEL_TAPS = 5
DILATION_STEP = 128
STEP = 10
EPSILON = 1e-05
DECAY = 1.0 - STEP ** (-0.8)

REACH = (KERNEL_TAPS - 1) // 2 * DILATION_STEP
MID = (KERNEL_TAPS - 1) // 2
F32 = jnp.float32
BF16 = jnp.bfloat16
SUB, LANE = 16, 128
AXES = ("seq", "fsdp")
NT = (((1,), (1,)), ((), ()))
TN = (((0,), (0,)), ((), ()))
NN = (((1,), (0,)), ((), ()))
VMEM_LIMIT = 58 * 1024 * 1024


def call(kernel, grid, in_specs, out_specs, out_shape, scratch=(), us=1.0, aliases=None):
    params = pltpu.CompilerParams(
        vmem_limit_bytes=VMEM_LIMIT, dimension_semantics=("arbitrary",) * len(grid)
    )
    return pl.pallas_call(
        kernel,
        grid=grid,
        in_specs=in_specs,
        out_specs=out_specs,
        out_shape=out_shape,
        scratch_shapes=list(scratch),
        compiler_params=params,
        input_output_aliases=aliases or {},
        cost_estimate=pl.CostEstimate(
                flops=int(us * 1.1e9), bytes_accessed=int(us * 3.4e6), transcendentals=0
        ),
    )


def shape(dims, dtype):
    return jax.ShapeDtypeStruct(dims, dtype)


def rows_spec(tile, width):
    return pl.BlockSpec((tile, width), lambda i: (i, 0))


def whole(*dims):
    return pl.BlockSpec(dims, lambda *_: (0,) * len(dims))


ANY = pl.BlockSpec(memory_space=pl.ANY)
SMEM = pl.BlockSpec(memory_space=pltpu.SMEM)


ERFC_P = 0.47 / math.sqrt(2.0)
ERFC_C = (
    0.12357219400743558,
    0.1999878668208835,
    -0.08033356004356296,
    0.3660253986657854,
    -0.1092519747040215,
)
LOG2E = 1.4426950408889634


def gelu_and_slope(y):
    t = pltpu.reciprocal(1.0 + ERFC_P * jnp.abs(y), approx=True)
    bell = jnp.exp2(y * y * (-0.5 * LOG2E))
    poly = ERFC_C[4] * t + ERFC_C[3]
    for c in ERFC_C[2::-1]:
        poly = poly * t + c
    tail = poly * t * bell
    cdf = jnp.where(y > 0.0, 1.0 - tail, tail)
    return y * cdf, cdf + y * (bell * (1.0 / math.sqrt(2.0 * math.pi)))


def lane_blocks(width):
    return [slice(k, k + LANE) for k in range(0, width, LANE)]


def row_stats(ref, rows):
    width = ref.shape[-1]
    blocks = lane_blocks(width)
    total = ref[rows, blocks[0]].astype(F32)
    for b in blocks[1:]:
        total = total + ref[rows, b].astype(F32)
    mean = jnp.sum(total, axis=-1, keepdims=True) * (1.0 / width)
    square = None
    for b in blocks:
        centered = ref[rows, b].astype(F32) - mean
        square = centered * centered if square is None else square + centered * centered
    variance = jnp.sum(square, axis=-1, keepdims=True) * (1.0 / width)
    return mean, lax.rsqrt(variance + EPSILON)


def fold(values):
    total = values[0:8]
    for k in range(8, values.shape[0], 8):
        total = total + values[k : k + 8]
    return total


def in_stages(count, stages, between=()):
    chunks = [slice(k, k + CHUNK) for k in range(0, count, CHUNK)]
    kept, rounds = {}, len(chunks) + len(stages) - 1
    for t in range(rounds):
        for n, stage in enumerate(stages):
            if 0 <= t - n < len(chunks):
                kept[n, t - n] = stage(chunks[t - n], kept.get((n - 1, t - n)))
        for work in between[t * len(between) // rounds : (t + 1) * len(between) // rounds]:
            work()


def halves_of(count):
    return (slice(0, count // 2), slice(count // 2, count))


def row_means(sums, width):
    return [jnp.sum(x, axis=-1, keepdims=True) * (1.0 / width) for x in sums]


def norm_back(rows, dxhat_ref, xhat_ref, means, put):
    mean_d, mean_dx, rstd = means
    for b in lane_blocks(dxhat_ref.shape[-1]):
        xhat = xhat_ref[rows, b].astype(F32)
        put(b, (dxhat_ref[rows, b] - mean_d - xhat * mean_dx) * rstd)


def add_terms(acc_ref, b, dy, xhat):
    acc_ref[0:8, b] += fold(dy * xhat)
    acc_ref[8:16, b] += fold(dy)


def open_sums(acc_ref):
    @pl.when(pl.program_id(0) == 0)
    def _():
        acc_ref[...] = jnp.zeros_like(acc_ref)


def close_sums(out_ref, acc_ref):
    @pl.when(pl.program_id(0) == pl.num_programs(0) - 1)
    def _():
        out_ref[0:1, :] = jnp.sum(acc_ref[0:8, :], axis=0, keepdims=True)
        out_ref[1:2, :] = jnp.sum(acc_ref[8:16, :], axis=0, keepdims=True)


def run_copies(copies):
    for copy in copies:
        copy.start()
    for copy in copies:
        copy.wait()


def piece_copies(pieces, full_ref, me, sem, first=0):
    each = full_ref.shape[0] // len(pieces)
    return [
        pltpu.make_async_copy(
            piece.at[0:each, :],
            full_ref.at[pl.ds(pl.multiple_of((me ^ k) * each, SUB), each), :],
            sem.at[first + k],
        )
        for k, piece in enumerate(pieces)
    ]


def out_copies(pieces, full_ref, me, sem, first=0):
    each, width = full_ref.shape[0] // len(pieces), full_ref.shape[1] // 2
    copies = []
    for k, piece in enumerate(pieces):
        rows = pl.ds(pl.multiple_of((me ^ k) * each, SUB), each)
        for side in range(2):
            at = piece.shape[0] - (2 - side) * each
            copies.append(
                pltpu.make_async_copy(
                    piece.at[at : at + each, :],
                    full_ref.at[rows, side * width : (side + 1) * width],
                    sem.at[first + 2 * k + side],
                )
            )
    return copies


def column(row):
    return jnp.transpose(jnp.broadcast_to(row, (LANE, LANE)))


CHUNK = 64


def norm_a_kernel(tok_ref, np_ref, hid_ref, slope_ref, xhat_ref, rstd_ref):
    def stats(rows, _):
        mean, rstd = row_stats(tok_ref, rows)
        rstd_ref[rows, :] = rstd
        return mean, rstd

    def work(rows, kept):
        mean, rstd = kept
        for b in lane_blocks(D):
            xhat = (tok_ref[rows, b].astype(F32) - mean) * rstd
            hidden, slope = gelu_and_slope(xhat * np_ref[0:1, b] + np_ref[1:2, b])
            hid_ref[rows, b] = hidden.astype(BF16)
            slope_ref[rows, b] = slope.astype(BF16)
            xhat_ref[rows, b] = xhat.astype(BF16)

    in_stages(tok_ref.shape[0], [stats, work])


def running_ends(ends_ref, lengths_ref):
    docs, width = lengths_ref.shape[0], ends_ref.shape[1]
    ends_ref[...] = jnp.zeros_like(ends_ref)
    ends_ref[0:1, 0:docs] = lengths_ref[...].reshape(1, -1).astype(F32)
    before = jnp.zeros((1, 1), F32)
    row = lax.broadcasted_iota(jnp.int32, (LANE, LANE), 0)
    lane = lax.broadcasted_iota(jnp.int32, (LANE, LANE), 1)
    for k in range(0, width, LANE):
        line = ends_ref[0:1, k : k + LANE]
        sums = jnp.sum(jnp.where(row <= lane, column(line), 0.0), axis=0, keepdims=True) + before
        ends_ref[0:1, k : k + LANE] = jnp.where(lane[0:1] + k < docs, sums, 1e9)
        before = before + jnp.sum(line, axis=1, keepdims=True)


def in_kernel(pieces, tiles, place_ref, lengths_ref, hid_ref, live_ref, np_ref, *refs):
    piece_refs = refs[:pieces]
    edges = tiles[0] == 0
    outs = refs[-(11 if edges else 9) :]
    mov_ref, slope_ref, xhat_ref, rstd_ref, mask_ref = outs[:5]
    w_ref, pre_ref, ends_ref, sem = outs[-4:]
    step = pl.program_id(0)
    tile = hid_ref.shape[0]

    @pl.when(step == 0)
    def _():
        copies = piece_copies(piece_refs, w_ref, place_ref[0], sem)
        for copy in copies:
            copy.start()
        running_ends(ends_ref, lengths_ref)
        for copy in copies:
            copy.wait()

    for half in halves_of(tile):
        pre_ref[half, :] = lax.dot_general(
            hid_ref[half, :], w_ref[...], NN, preferred_element_type=F32
        )

    at_tile = tiles[0] + step * tiles[1]
    first = place_ref[1] + at_tile * tile
    ends = ends_ref[0:1, :]
    lanes = lax.broadcasted_iota(jnp.int32, (LANE, 8), 1)
    offsets = ((lanes - MID) * DILATION_STEP).astype(F32)
    for k in range(tile // LANE):
        at = (first + k * LANE + lax.broadcasted_iota(jnp.int32, (LANE, 1), 0)).astype(F32)
        begin = jnp.max(jnp.where(ends <= at, ends, 0.0), axis=1, keepdims=True)
        end = jnp.min(jnp.where(ends > at, ends, 1e9), axis=1, keepdims=True)
        there = at + offsets
        same = jnp.where((there >= begin) & (there < end), 1.0, 0.0)
        live = column(live_ref[pl.ds(at_tile * (tile // LANE) + k, 1), :].astype(F32))
        mask_ref[k * LANE : (k + 1) * LANE, :] = jnp.where(lanes == MID, live[:, 0:8], same)

    def stats(rows, _):
        mean, rstd = row_stats(pre_ref, rows)
        rstd_ref[rows, :] = rstd
        return mean, rstd

    def work(rows, kept):
        mean, rstd = kept
        live = mask_ref[rows, MID : MID + 1]
        for b in lane_blocks(INNER):
            gains = slice(D + b.start, D + b.stop)
            xhat = (pre_ref[rows, b] - mean) * rstd
            hidden, slope = gelu_and_slope(xhat * np_ref[0:1, gains] + np_ref[1:2, gains])
            mov_ref[rows, b] = (hidden * live).astype(BF16)
            slope_ref[rows, b] = slope.astype(BF16)
            xhat_ref[rows, b] = xhat.astype(BF16)

    in_stages(tile, [stats, work])
    if edges:
        put_edges(place_ref, outs[5], outs[6], mov_ref, step == 0, step == 1)


def load_window(place_ref, inner, mid, outer, ext_ref, sem):
    rows, core = mid.shape[0], lax.rem(place_ref[0], 2)
    near = pl.multiple_of((1 - core) * (REACH + rows), SUB)
    far = pl.multiple_of(core * (REACH + rows), SUB)
    return [
        pltpu.make_async_copy(inner, ext_ref.at[pl.ds(near, REACH), :], sem.at[0]),
        pltpu.make_async_copy(mid, ext_ref.at[REACH : REACH + rows, :], sem.at[1]),
        pltpu.make_async_copy(outer, ext_ref.at[pl.ds(far, REACH), :], sem.at[2]),
    ]


def put_edges(place_ref, inner_ref, outer_ref, tile_ref, at_first, at_last):
    rows, core = tile_ref.shape[0], lax.rem(place_ref[0], 2)
    for at, edge, first in ((at_first, slice(0, REACH), 0), (at_last, slice(rows - REACH, rows), 1)):

        @pl.when(at & (core == first))
        def _(edge=edge):
            outer_ref[...] = tile_ref[edge, :]

        @pl.when(at & (core != first))
        def _(edge=edge):
            inner_ref[...] = tile_ref[edge, :]


def fill_taps(taps_ref, ext_ref, mask_ref, start):
    tile = taps_ref.shape[0]
    for j in range(KERNEL_TAPS):
        rows = pl.ds(pl.multiple_of(start + j * DILATION_STEP, DILATION_STEP), tile)
        picked = ext_ref[rows, :]
        if j != MID:
            picked = picked * mask_ref[:, j : j + 1].astype(BF16)
        taps_ref[:, j * INNER : (j + 1) * INNER] = picked


def conv_kernel(
    pieces, rows_of, place_ref, low_ref, mov_ref, high_ref, mask_ref, cot_ref, before_ref, np_ref, *refs
):
    piece_refs = refs[:pieces]
    hid_ref, dconv_ref, inner_ref, outer_ref, sums_ref, turned_ref = refs[pieces : pieces + 6]
    outs = refs[pieces + 6 : pieces + 10]
    ext_ref, wc_ref, wct_ref, wo_ref, wt_ref, taps_ref, pre_ref, dh_ref, xhat_ref = refs[
        pieces + 10 : pieces + 19
    ]
    dt_ref, ht_ref, gc_ref, go_ref, acc_ref, stage1_ref, stage2_ref, sem = refs[pieces + 19 :]
    step, steps = pl.program_id(0), pl.num_programs(0) - 1
    tile = taps_ref.shape[1]
    slot = lax.rem(step, 2)

    @pl.when(step == 0)
    def _():
        me = place_ref[0]
        outs = out_copies(piece_refs, wo_ref, me, sem, 3)
        rest = load_window(place_ref, low_ref, mov_ref, high_ref, ext_ref, sem)
        rest += piece_copies(piece_refs, wc_ref, me, sem, 3 + 2 * pieces)
        for copy in outs + rest:
            copy.start()
        for ref in (acc_ref, gc_ref, go_ref, dt_ref, ht_ref):
            ref[...] = jnp.zeros_like(ref)
        taps_ref[1] = jnp.zeros_like(taps_ref[1])
        for copy in outs:
            copy.wait()
        for k in range(0, D, 256):
            wt_ref[k : k + 256, :] = jnp.transpose(wo_ref[:, k : k + 256])
        for copy in rest:
            copy.wait()

    def grad_conv(cols):
        def work():
            gc_ref[:, cols] += lax.dot_general(
                dt_ref[...], taps_ref[1 - slot, :, cols], NN, preferred_element_type=F32
            )

        return work

    def grad_out(cols):
        def work():
            go_ref[:, cols] += lax.dot_general(
                ht_ref[...], before_ref[:, cols], NN, preferred_element_type=F32
            )

        return work

    taps_wide = KERNEL_TAPS * INNER
    products = [grad_conv(slice(k, min(k + 768, taps_wide))) for k in range(0, taps_wide, 768)]
    products += [grad_out(slice(k, min(k + 768, D))) for k in range(0, D, 768)]

    @pl.when(step < steps)
    def _():
        fill_taps(taps_ref.at[slot], ext_ref, mask_ref, step * tile)
        pre_ref[...] = lax.dot_general(
            taps_ref[slot], wc_ref[...], NN, preferred_element_type=F32
        )
        dh_ref[...] = lax.dot_general(cot_ref[...], wt_ref[...], NN, preferred_element_type=F32)
        for n in range(2):
            tap = jnp.minimum(2 * step + n, KERNEL_TAPS - 1)
            source = wc_ref[pl.ds(pl.multiple_of(tap * INNER, SUB), INNER), :]
            target = pl.multiple_of((KERNEL_TAPS - 1 - tap) * INNER, SUB)
            wct_ref[pl.ds(target, INNER), :] = jnp.transpose(source)

        def stats(rows, _):
            return row_stats(pre_ref, rows)

        def work(rows, kept):
            mean, rstd = kept
            sums = [0.0, 0.0]
            for b in lane_blocks(INNER):
                gains = slice(D + INNER + b.start, D + INNER + b.stop)
                gain = np_ref[0:1, gains]
                xhat = (pre_ref[rows, b] - mean) * rstd
                hidden, slope = gelu_and_slope(xhat * gain + np_ref[1:2, gains])
                hid_ref[rows, b] = hidden.astype(BF16)
                dy = dh_ref[rows, b] * slope
                add_terms(acc_ref, b, dy, xhat)
                dxhat = dy * gain
                xhat_ref[rows, b] = xhat
                dh_ref[rows, b] = dxhat
                sums = [sums[0] + dxhat, sums[1] + dxhat * xhat]
            return row_means(sums, INNER) + [rstd]

        def finish(rows, means):
            def put(b, value):
                dconv_ref[rows, b] = value.astype(BF16)

            norm_back(rows, dh_ref, xhat_ref, means, put)

        in_stages(tile, [stats, work, finish], products)
        dt_ref[...] = jnp.transpose(dconv_ref[...])
        ht_ref[...] = jnp.transpose(hid_ref[...])

    put_edges(place_ref, inner_ref, outer_ref, dconv_ref, step == 0, step == steps - 1)

    @pl.when(step == steps)
    def _():
        copy = pltpu.make_async_copy(wct_ref, turned_ref, sem.at[4])
        copy.start()
        for work in products:
            work()
        core = lax.rem(place_ref[0], 2)
        _, rows_conv, rows_out = rows_of
        stage_turned(stage1_ref, core, gc_ref, rows_conv, 0, slice(0, CUT // LANE))
        first_tiles = rows_conv // SUB * (CUT // LANE)
        stage_plain(stage1_ref, core, go_ref, rows_out, first_tiles)
        copies = stage_copies(stage1_ref, outs[0], outs[1], spans(CHUNKS[0], rows_of)[1], sem, 0)
        for each in copies:
            each.start()
        stage_turned(stage2_ref, core, gc_ref, rows_conv, 0, slice(CUT // LANE, INNER // LANE))
        more = stage_copies(stage2_ref, outs[2], outs[3], spans(CHUNKS[1], rows_of)[1], sem, 2)
        for each in more:
            each.start()
        for each in copies + more + [copy]:
            each.wait()
        sums_ref[0:1, :] = jnp.sum(acc_ref[0:8, :], axis=0, keepdims=True)
        sums_ref[1:2, :] = jnp.sum(acc_ref[8:16, :], axis=0, keepdims=True)


def stage_tiles(stage_ref, core, first_row, rows_each, base, block0, blocks, value):
    for g in range(value.shape[0] // SUB):
        row = first_row + g * SUB
        owner, inside = row // rows_each, row % rows_each // SUB
        side = core ^ (owner % 2)
        for b in range(value.shape[1] // LANE):
            tile = value[g * SUB : (g + 1) * SUB, b * LANE : (b + 1) * LANE]
            at = base + inside * blocks + block0 + b
            stage_ref[side, owner // 2, at] = tile.astype(BF16)


def stage_plain(stage_ref, core, grad_ref, rows_each, base):
    blocks = grad_ref.shape[1] // LANE
    for row in range(0, grad_ref.shape[0], SUB):
        part = grad_ref[row : row + SUB, :]
        stage_tiles(stage_ref, core, row, rows_each, base, 0, blocks, part)


def stage_turned(stage_ref, core, turned_ref, rows_each, base, blocks):
    count = blocks.stop - blocks.start
    for row in range(0, turned_ref.shape[1], LANE):
        for b in range(count):
            at = (blocks.start + b) * LANE
            part = jnp.transpose(turned_ref[at : at + LANE, row : row + LANE].astype(BF16))
            stage_tiles(stage_ref, core, row, rows_each, base, b, count, part)


def stage_copies(stage_ref, keep_ref, send_ref, used, sem, first):
    count = stage_ref.shape[2]
    if used < count:
        dims = stage_ref.shape[:2] + (count - used, SUB, LANE)
        stage_ref[:, :, used:] = jnp.zeros(dims, BF16)
    return [
        pltpu.make_async_copy(stage_ref.at[n], ref, sem.at[first + n])
        for n, ref in enumerate((keep_ref, send_ref))
    ]


def back_conv_kernel(
    last, rows_in, place_ref, low_ref, d_ref, high_ref, turned_ref, mask_ref, xhat_ref, rstd_ref, slope_ref, hid_ref, np_ref, *refs
):
    if last:
        before_ref, dpre_ref, sums_ref, keep_ref, send_ref, stage_ref = refs[:6]
    else:
        dpre_ref, sums_ref, part_ref = refs[:3]
    ext_ref, wt_ref, taps_ref, dmov_ref, grad_ref, acc_ref, sem = refs[-7:]
    step, steps = pl.program_id(0), pl.num_programs(0)
    tile = taps_ref.shape[0]
    open_sums(acc_ref)

    @pl.when(step == 0)
    def _():
        copies = load_window(place_ref, low_ref, d_ref, high_ref, ext_ref, sem)
        copies.append(pltpu.make_async_copy(turned_ref, wt_ref, sem.at[3]))
        if last:
            copies.append(pltpu.make_async_copy(before_ref, grad_ref, sem.at[4]))
        for copy in copies:
            copy.start()
        if not last:
            grad_ref[...] = jnp.zeros_like(grad_ref)
        for copy in copies:
            copy.wait()

    fill_taps(taps_ref, ext_ref, mask_ref, (steps * last + step) * tile)
    for half in halves_of(tile):
        dmov_ref[half, :] = lax.dot_general(
            taps_ref[half, :], wt_ref[...], NN, preferred_element_type=F32
        )

    def work(rows, _):
        live = mask_ref[rows, MID : MID + 1]
        sums = [0.0, 0.0]
        for b in lane_blocks(INNER):
            xhat = xhat_ref[rows, b].astype(F32)
            dy = dmov_ref[rows, b] * live * slope_ref[rows, b].astype(F32)
            add_terms(acc_ref, b, dy, xhat)
            dxhat = dy * np_ref[0:1, D + b.start : D + b.stop]
            dmov_ref[rows, b] = dxhat
            sums = [sums[0] + dxhat, sums[1] + dxhat * xhat]
        return row_means(sums, INNER) + [rstd_ref[rows, :]]

    def finish(rows, means):
        def put(b, value):
            dpre_ref[rows, b] = value.astype(BF16)

        norm_back(rows, dmov_ref, xhat_ref, means, put)

    in_stages(tile, [work, finish])
    close_sums(sums_ref, acc_ref)
    grad_ref[...] += lax.dot_general(dpre_ref[...], hid_ref[...], TN, preferred_element_type=F32)

    @pl.when(step == steps - 1)
    def _():
        if last:
            all_blocks = slice(0, INNER // LANE)
            stage_turned(stage_ref, lax.rem(place_ref[0], 2), grad_ref, rows_in, 0, all_blocks)
            used = rows_in // SUB * (INNER // LANE)
            run_copies(stage_copies(stage_ref, keep_ref, send_ref, used, sem, 0))
        else:
            run_copies([pltpu.make_async_copy(grad_ref, part_ref, sem.at[0])])


def back_a_kernel(pieces, half, place_ref, dpre0_ref, dpre1_ref, xhat_ref, rstd_ref, slope_ref, cot_ref, np_ref, *refs):
    piece_refs = refs[:pieces]
    grad_ref, sums_ref, w_ref, wt_ref, dh_ref, acc_ref, sem = refs[-7:]
    open_sums(acc_ref)

    @pl.when(pl.program_id(0) == 0)
    def _():
        run_copies(piece_copies(piece_refs, w_ref, place_ref[0], sem))
        for k in range(0, D, 256):
            wt_ref[:, k : k + 256] = jnp.transpose(w_ref[k : k + 256, :])

    second = (jnp.zeros((1, 1), jnp.int32) + pl.program_id(0)) >= half
    d_pre = jnp.where(second, dpre1_ref[...], dpre0_ref[...])
    dh_ref[...] = lax.dot_general(d_pre, wt_ref[...], NN, preferred_element_type=F32)

    def work(rows, _):
        sums = [0.0, 0.0]
        for b in lane_blocks(D):
            xhat = xhat_ref[rows, b].astype(F32)
            dy = dh_ref[rows, b] * slope_ref[rows, b].astype(F32)
            add_terms(acc_ref, b, dy, xhat)
            dxhat = dy * np_ref[0:1, b]
            dh_ref[rows, b] = dxhat
            sums = [sums[0] + dxhat, sums[1] + dxhat * xhat]
        return row_means(sums, D) + [rstd_ref[rows, :]]

    def finish(rows, means):
        def put(b, value):
            grad_ref[rows, b] = cot_ref[rows, b].astype(F32) + value

        norm_back(rows, dh_ref, xhat_ref, means, put)

    in_stages(dpre0_ref.shape[0], [work, finish])
    close_sums(sums_ref, acc_ref)


def out_kernel(pieces, place_ref, hid_ref, tok_ref, *refs):
    piece_refs = refs[:pieces]
    out_ref, w_ref, sem = refs[pieces:]

    @pl.when(pl.program_id(0) == 0)
    def _():
        run_copies(out_copies(piece_refs, w_ref, place_ref[0], sem))

    branch = lax.dot_general(hid_ref[...], w_ref[...], NN, preferred_element_type=F32)
    out_ref[...] = (tok_ref[...].astype(F32) + branch).astype(BF16)


WIDTHS = (INNER, INNER, D)
LANE0 = (0, INNER, 2 * INNER)
CUT = 2 * LANE
CHUNKS = (((1, 0, CUT), (2, 0, D)), ((1, CUT, INNER - CUT),), ((0, 0, INNER),))


def spans(chunk, rows):
    found, first = [], 0
    for weight, col, cols in chunk:
        tiles = rows[weight] // SUB * (cols // LANE)
        found.append((weight, col // LANE, cols // LANE, first, tiles))
        first += tiles
    return found, first


def column_sums(pack_ref, row, ref, chunk, rows):
    for weight, block0, blocks, first, tiles in spans(chunk, rows)[0]:

        def body(g, carry, first=first, blocks=blocks):
            new = []
            for b in range(blocks):
                value = ref[first + g * blocks + b].astype(F32)
                new.append(carry[b] + fold(value * value + 1e-30))
            return tuple(new)

        zero = tuple(jnp.zeros((8, LANE), F32) for _ in range(blocks))
        cols = lax.fori_loop(0, tiles // blocks, body, zero, unroll=5)
        for b in range(blocks):
            lane = LANE0[weight] + (block0 + b) * LANE
            pack_ref[row : row + 1, lane : lane + LANE] = jnp.sum(cols[b], axis=0, keepdims=True)


def load_full(refs, place_ref, first, full_ref, sem, at):
    pieces = refs[0].shape[0]
    each = full_ref.shape[0] // (len(refs) * pieces)
    outer = pieces if len(refs) == 2 else pieces // 2
    y = place_ref[2] % 2
    copies = []
    for n, (ref, side) in enumerate(zip(refs, (y, 1 - y))):
        for p in range(pieces):
            index = side * outer + p if len(refs) == 2 else p % 2 * outer + p // 2
            target = full_ref.at[pl.ds(index * each, each)]
            source = ref.at[p, first : first + each]
            copies.append(pltpu.make_async_copy(source, target, sem.at[at + n * pieces + p]))
    return copies


def pack_kernel(rows, pieces, place_ref, part_ref, *refs):
    states, (pack_ref, acc_ref) = refs[0:3], refs[3:5]
    pack_ref[...] = jnp.zeros_like(pack_ref)
    lanes = lax.broadcasted_iota(jnp.int32, (1, LANE), 1)
    for k in range(3):
        total = jnp.sum(states[k][...].reshape(1, -1), axis=1, keepdims=True)
        pack_ref[1:2, 0:LANE] += jnp.where(lanes == k, total, 0.0)
    acc_ref[...] = jnp.zeros_like(acc_ref)
    spare = acc_ref.shape[0] - 1
    outer = place_ref[3] // 2
    piece = place_ref[2] % 2 * outer + place_ref[2] // 2
    at = 0
    for chunk, each in zip(CHUNKS[:2], pieces):
        found, _ = spans(chunk, rows)
        start = piece * each

        def body(k, carry, found=found, start=start, at=at):
            n = start + k
            slot = spare
            for weight, block0, blocks, first, tiles in found:
                here = LANE0[weight] // LANE + block0 + lax.rem(jnp.maximum(n - first, 0), blocks)
                slot = jnp.where((n >= first) & (n < first + tiles), here, slot)
            value = part_ref[at + k].astype(F32)
            acc_ref[slot] += value * value + 1e-30
            return carry

        lax.fori_loop(0, each, body, 0, unroll=2)
        at += each
    for slot in range(spare):
        pack_ref[0:1, slot * LANE : (slot + 1) * LANE] = jnp.sum(acc_ref[slot], axis=0, keepdims=True)


def norm_tiles_kernel(parts, *refs):
    sums, out_ref, line_ref = refs[:-2], refs[-2], refs[-1]
    line_ref[...] = jnp.zeros_like(line_ref)
    lanes_of = ((0, D), (D, D + INNER), (D, D + INNER), (D + INNER, D + 2 * INNER))
    for part, (lane0, lane1) in zip(sums, lanes_of):
        line_ref[0:2, lane0:lane1] += part[...]
    out_ref[...] = jnp.zeros_like(out_ref)
    blocks = (D + 2 * INNER) // LANE
    each = -(-2 * blocks // parts)
    for part in range(-(-2 * blocks // each)):
        rows = []
        for n in range(part * each, min((part + 1) * each, 2 * blocks)):
            row, b = n // blocks, n % blocks
            rows.append(line_ref[row : row + 1, b * LANE : (b + 1) * LANE])
        rows += [jnp.zeros((1, LANE), F32)] * (8 - len(rows))
        value = jnp.concatenate(rows, axis=0)
        high = value.astype(BF16).astype(F32)
        out_ref[part] = jnp.concatenate([high, value - high], axis=0).astype(BF16)


def high_low(total):
    value = total[..., 0:8, :] + total[..., 8:16, :]
    high = value.astype(BF16).astype(F32)
    return jnp.concatenate([high, value - high], axis=-2).astype(BF16)


def pack_in_kernel(rows, place_ref, got_ref, out_ref, full_ref, norms_ref, sem, norms_sem):
    parts = got_ref.shape[0]
    each = full_ref.shape[0] // parts
    copies = load_full((got_ref,), place_ref, 0, full_ref, sem, 0)
    copies += [
        pltpu.make_async_copy(got_ref.at[p, each], norms_ref.at[p], norms_sem.at[p])
        for p in range(parts)
    ]
    run_copies(copies)
    out_ref[...] = jnp.zeros_like(out_ref)
    blocks = (D + 2 * INNER) // LANE
    rows_each = -(-2 * blocks // parts)
    for n in range(2 * blocks):
        part, at = n // rows_each, n % rows_each
        value = norms_ref[part].astype(F32)
        row, lane = n // blocks, n % blocks * LANE
        out_ref[row : row + 1, lane : lane + LANE] = value[at : at + 1] + value[8 + at : 9 + at]
    column_sums(out_ref, 2, full_ref, CHUNKS[2], rows)


def update_weight(
    k, squares, states_sum, source, weight, state, col_state, grad_ref, new, row_new_ref, col_new_ref, scratch
):
    line_ref, state_ref, new_ref = scratch
    width, fan, rows_here = WIDTHS[k], (D, KERNEL_TAPS * INNER, INNER)[k], weight.shape[0]
    col_new = DECAY * col_state[...].reshape(1, -1) + (1.0 - DECAY) * (squares * (1.0 / fan))
    col_new_ref[...] = col_new.reshape(-1)
    total = DECAY * states_sum
    total = total + (1.0 - DECAY) * (1.0 / width) * jnp.sum(squares, axis=1, keepdims=True)
    scaled = col_new / (total * (1.0 / fan))
    rate = 0.5 / fan**0.5
    line_ref[0:1, 0:rows_here] = state[...].reshape(1, -1)
    whole_rows = rows_here + -rows_here % LANE
    for c in range(0, whole_rows, LANE):
        state_ref[c : c + LANE, :] = column(line_ref[0:1, c : c + LANE])

    def body(g, carry):
        rows = pl.ds(pl.multiple_of(g * SUB, SUB), SUB)
        square = 0.0
        for ref, block0, blocks, first in source:
            for b in range(blocks):
                value = ref[first + g * blocks + b].astype(F32)
                grad_ref[rows, (block0 + b) * LANE : (block0 + b + 1) * LANE] = value
                square = square + (value * value + 1e-30)
        mean = jnp.sum(square, axis=1, keepdims=True) * (1.0 / width)
        row_new = DECAY * state_ref[rows, :] + (1.0 - DECAY) * mean
        new_ref[rows, :] = row_new
        for ref, block0, blocks, first in source:
            for b in range(blocks):
                lanes = slice((block0 + b) * LANE, (block0 + b + 1) * LANE)
                value = ref[first + g * blocks + b].astype(F32)
                step = value * lax.rsqrt(row_new * scaled[:, lanes])
                new[rows, lanes] = weight[rows, lanes] - rate * step
        return carry

    lax.fori_loop(0, rows_here // SUB, body, 0, unroll=5)
    for c in range(0, whole_rows, LANE):
        line_ref[0:1, c : c + LANE] = jnp.transpose(new_ref[c : c + LANE, :])[0:1, :]
    row_new_ref[...] = line_ref[0:1, 0:rows_here].reshape(-1)


def sources_of(chunk, ref, rows):
    return {w: (ref, block0, blocks, first) for w, block0, blocks, first, _ in spans(chunk, rows)[0]}


def update_kernel(rows, copies_of, place_ref, mine_ref, other_ref, pack_ref, *refs):
    weights, states, col_states = refs[0:2], refs[2:4], refs[4:6]
    grads, news, rows_new, cols_new = refs[6:8], refs[8:10], refs[10:12], refs[12:14]
    full1_ref, full2_ref, sem = refs[17:20]
    both = (mine_ref, other_ref)
    count = 2 * mine_ref.shape[0]
    copies = load_full(both, place_ref, 0, full1_ref, sem, 0)
    copies += load_full(both, place_ref, full1_ref.shape[0] // count, full2_ref, sem, count)
    run_copies(copies)
    from1 = sources_of(CHUNKS[0], full1_ref, rows)
    from2 = sources_of(CHUNKS[1], full2_ref, rows)
    for n, (k, source) in enumerate(((1, [from1[1], from2[1]]), (2, [from1[2]]))):
        squares = pack_ref[0:1, LANE0[k] : LANE0[k] + WIDTHS[k]]
        update_weight(
            k, squares, pack_ref[1:2, k : k + 1] * (1.0 / copies_of), source, weights[n],
            states[n], col_states[n], grads[n], news[n], rows_new[n], cols_new[n], refs[14:17],
        )


def update_in_kernel(
    rows, copies_of, place_ref, got_ref, pack_in_ref, pack_ref, np_ref, second_ref, *refs
):
    weight, state, col_state, grad_ref, new_ref, row_new_ref, col_new_ref = refs[0:7]
    ngrad_ref, nsecond_ref, nnew_ref = refs[7:10]
    full_ref, sem = refs[13:15]
    copies = load_full((got_ref,), place_ref, 0, full_ref, sem, 0)
    for copy in copies:
        copy.start()
    grad = pack_in_ref[0:2, :]
    second = DECAY * second_ref[...] + (1.0 - DECAY) * (grad * grad + 1e-30)
    ngrad_ref[...] = grad
    nsecond_ref[...] = second
    nnew_ref[...] = np_ref[...] - 0.2 * grad * lax.rsqrt(second)
    for copy in copies:
        copy.wait()
    update_weight(
        0, pack_in_ref[2:3, 0:INNER], pack_ref[1:2, 0:1] * (1.0 / copies_of),
        [sources_of(CHUNKS[2], full_ref, rows)[0]], weight, state, col_state, grad_ref, new_ref,
        row_new_ref, col_new_ref, refs[10:13],
    )


class Places:
    def __init__(self):
        self.seq, self.fsdp = lax.axis_size("seq"), lax.axis_size("fsdp")
        self.q = lax.axis_index("fsdp")
        self.s = lax.axis_index("seq")

    def flip(self, x, axis, bit):
        pairs = []
        for s in range(self.seq):
            for f in range(self.fsdp):
                s2, f2 = (s ^ bit, f) if axis == "seq" else (s, f ^ bit)
                pairs.append((s * self.fsdp + f, s2 * self.fsdp + f2))
        return lax.ppermute(x, AXES, pairs)


def bits_of(count):
    return [1 << k for k in range(count.bit_length() - 1)]


def tie(x, *others):
    return lax.optimization_barrier((x, *others))[0]


def gather_pieces(piece, place, after, later=()):
    found = {0: piece}
    for bit in reversed(bits_of(place.fsdp)):
        for k in list(found):
            moving = found[k]
            if bit == 1:
                moving = tie(moving, *((after,) if k == 0 or not later else later))
            found[k | bit] = place.flip(moving, "fsdp", bit)
    return [found[k] for k in range(place.fsdp)]


def sum_over(x, place, *axes):
    for axis in axes:
        for bit in bits_of(getattr(place, axis)):
            x = x + place.flip(x, axis, bit)
    return x


def pick(x, index, axis):
    return lax.dynamic_index_in_dim(x, index, axis=axis, keepdims=False)


class Reduction:
    def __init__(self, place, keep, send):
        self.place, self.near = place, keep
        self.got = place.flip(send, "fsdp", 1)

    def halve(self, axis, side, flip_axis, bit):
        dims = self.near.shape
        parts = dims[:axis] + (2, dims[axis] // 2) + dims[axis + 1 :]
        near, got = self.near.reshape(parts), self.got.reshape(parts)
        away = pick(near, 1 - side, axis).astype(F32) + pick(got, 1 - side, axis).astype(F32)
        self.near = pick(near, side, axis).astype(F32) + pick(got, side, axis).astype(F32)
        away = away.astype(BF16)
        self.got = self.place.flip(away, flip_axis, bit)
        return away

    def x(self):
        bit = self.place.fsdp // 2
        while bit > 1:
            away = self.halve(0, (self.place.q // bit) % 2, "fsdp", bit)
            bit //= 2
        return away

    def y(self):
        return self.halve(1, self.place.s % 2, "seq", 1)

    def all_pieces(self):
        total = (self.near + self.got.astype(F32)).astype(BF16)
        total = total.reshape((2, self.place.seq // 2, -1) + total.shape[2:])
        return jnp.swapaxes(total, 0, 1).reshape((self.place.seq,) + total.shape[2:])

    def pieces(self):
        total = (self.near + self.got.astype(F32)).astype(BF16)
        return total.reshape((self.place.seq // 2, -1) + total.shape[2:])


def arrive(result, *reductions):
    result, *gots = lax.optimization_barrier((result, *[r.got for r in reductions]))
    for reduction, got in zip(reductions, gots):
        reduction.got = got
    return result


def summed_f32(got):
    return jnp.sum(got.astype(F32), axis=0)


def summed(got):
    return summed_f32(got).astype(BF16)


def exchange_all(sent):
    return lax.all_to_all(sent, "seq", 0, 0)


def exchange(place, sent):
    line = [[y + 2 * z for z in range(place.seq // 2)] for y in range(2)]
    return lax.all_to_all(sent, "seq", 0, 0, axis_index_groups=line)


def on_device(
    tokens, input_mask, doc_lengths, cotangent, w_in, w_conv, w_out, norm_params,
    row_in, col_in, row_conv, col_conv, row_out, col_out, norm_second,
):
    place = Places()
    rows = tokens.shape[0]
    pieces = place.fsdp
    spots = jnp.stack(
        [place.q, (place.s * place.fsdp + place.q) * rows, place.s, place.seq]
    ).astype(jnp.int32)
    docs = doc_lengths.shape[0]
    live = input_mask.reshape(-1, LANE)
    weights = (w_in, w_conv, w_out)
    rows_of = [w.shape[0] for w in weights]

    tile_a, tile = 256, 512
    steps = rows // tile
    params_spec = whole(2, D + 2 * INNER)
    dma = pltpu.SemaphoreType.DMA

    out_sides = (w_out[:, : D // 2], w_out[:, D // 2 :])
    conv_out = jnp.concatenate([w_conv, *out_sides], axis=0).astype(BF16)
    hidden_a, slope_a, xhat_a, rstd_a = call(
        norm_a_kernel,
        (rows // tile_a,),
        [rows_spec(tile_a, D), params_spec],
        [rows_spec(tile_a, D)] * 3 + [rows_spec(tile_a, 1)],
        [shape((rows, D), BF16)] * 3 + [shape((rows, 1), F32)],
        us=17,
    )(tokens, tie(norm_params, conv_out))

    in_pieces = gather_pieces(w_in.astype(BF16), place, hidden_a)

    def in_call(tiles, count, before):
        at, stride = tiles

        def here_spec(width):
            return pl.BlockSpec((tile, width), lambda i: (at + stride * i, 0))

        out_shapes = [shape((rows, INNER), BF16)] * 3 + [shape((rows, 1), F32), shape((rows, 8), F32)]
        out_specs = [here_spec(INNER)] * 3 + [here_spec(1), here_spec(8)]
        if at == 0:
            out_shapes += [shape((REACH, INNER), BF16)] * 2
            out_specs += [whole(REACH, INNER)] * 2
        return call(
            functools.partial(in_kernel, pieces, tiles),
            (count,),
            [SMEM, whole(docs), here_spec(D), whole(*live.shape), params_spec]
            + [ANY] * (pieces + len(before)),
            out_specs,
            out_shapes,
            [pltpu.VMEM((D, INNER), BF16), pltpu.VMEM((tile, INNER), F32)]
            + [pltpu.VMEM((8, docs + -docs % LANE), F32), dma((pieces,))],
            us=3,
            aliases={5 + pieces + k: k for k in range(len(before))},
        )(spots, doc_lengths, hidden_a, live, norm_params, *in_pieces, *before)

    *kept, m_first, m_last = in_call((0, steps - 1), 2, ())
    moved, slope_b, xhat_b, rstd_b, masks = in_call((1, 1), steps - 2, kept)

    def halo(inner, outer):
        total = place.seq * place.fsdp
        across = [(i, i + 1 if i % 2 else i - 1) for i in range(1, total - 1)]
        return place.flip(inner, "fsdp", 1), lax.ppermute(outer, AXES, across)

    m_inner, m_outer = halo(m_first, m_last)
    conv_pieces = gather_pieces(conv_out, place, m_first, (moved, m_inner, m_outer))

    ext = pltpu.VMEM((rows + 2 * REACH, INNER), BF16)
    taps_wide = KERNEL_TAPS * INNER
    wide = pltpu.VMEM((taps_wide, INNER), BF16)
    shards = place.fsdp // 2

    def half_dims(chunk):
        count = spans(chunk, rows_of)[1]
        return (shards, count + -count % place.seq, SUB, LANE)

    def tile_spec(width, ahead):
        return pl.BlockSpec((tile, width), lambda i: (jnp.clip(i + ahead, 0, steps - 1), 0))

    halves = [half_dims(CHUNKS[0])] * 2 + [half_dims(CHUNKS[1])] * 2
    work = pltpu.VMEM((tile, INNER), F32)
    turned_tile = pltpu.VMEM((INNER, tile), BF16)
    hidden_c, d_conv, d_first, d_last, sums_c, turned, keep1, send1, keep2, send2 = call(
        functools.partial(conv_kernel, pieces, rows_of),
        (steps + 1,),
        [SMEM, ANY, ANY, ANY, tile_spec(8, 0), tile_spec(D, 0), tile_spec(D, -1), params_spec]
        + [ANY] * pieces,
        [tile_spec(INNER, 0)] * 2
        + [whole(REACH, INNER), whole(REACH, INNER), whole(2, INNER)]
        + [ANY] * 5,
        [
            shape((rows, INNER), BF16),
            shape((rows, INNER), BF16),
            shape((REACH, INNER), BF16),
            shape((REACH, INNER), BF16),
            shape((2, INNER), F32),
            shape((taps_wide, INNER), BF16),
        ]
        + [shape(dims, BF16) for dims in halves],
        [ext, wide, wide, pltpu.VMEM((INNER, D), BF16), pltpu.VMEM((D, INNER), BF16)]
        + [pltpu.VMEM((2, tile, taps_wide), BF16), work, work, work, turned_tile, turned_tile]
        + [pltpu.VMEM((INNER, taps_wide), F32), pltpu.VMEM((INNER, D), F32)]
        + [pltpu.VMEM((16, INNER), F32)]
        + [pltpu.VMEM((2,) + halves[0], BF16), pltpu.VMEM((2,) + halves[2], BF16)]
        + [dma((3 + 3 * pieces,))],
        us=45,
    )(
        spots, m_inner, moved, m_outer, masks, cotangent, cotangent, norm_params, *conv_pieces
    )
    d_inner, d_outer = halo(d_first, d_last)
    first, second = Reduction(place, keep1, send1), Reduction(place, keep2, send2)
    (block_out,) = call(
        functools.partial(out_kernel, pieces),
        (steps,),
        [SMEM, rows_spec(tile, INNER), rows_spec(tile, D)] + [ANY] * pieces,
        [rows_spec(tile, D)],
        [shape((rows, D), BF16)],
        [pltpu.VMEM((INNER, D), BF16), dma((2 * pieces,))],
        us=9,
    )(spots, hidden_c, tokens, *conv_pieces)

    def back_conv(last, spots, before):
        here = steps // 2
        at = here * last

        def here_spec(width):
            return pl.BlockSpec((tile, width), lambda i: (i + at, 0))

        dims = half_dims(CHUNKS[2])
        return call(
            functools.partial(back_conv_kernel, last, w_in.shape[0]),
            (here,),
            [SMEM] + [ANY] * 4
            + [here_spec(8), here_spec(INNER), here_spec(1), here_spec(INNER), here_spec(D)]
            + [params_spec]
            + [ANY] * last,
            [rows_spec(tile, INNER), whole(2, INNER)] + [ANY] * (1 + last),
            [shape((rows // 2, INNER), BF16), shape((2, INNER), F32)]
            + ([shape(dims, BF16)] * 2 if last else [shape((INNER, D), F32)]),
            ([pltpu.VMEM((2,) + dims, BF16)] if last else [])
            + [
                ext,
                wide,
                pltpu.VMEM((tile, taps_wide), BF16),
                pltpu.VMEM((tile, INNER), F32),
                pltpu.VMEM((INNER, D), F32),
                pltpu.VMEM((16, INNER), F32),
                dma((5,)),
            ],
            us=16,
        )(
            spots, d_inner, d_conv, d_outer, turned, masks, xhat_b, rstd_b, slope_b, hidden_a,
            norm_params, *before,
        )

    block_out, d_inner, d_outer = arrive((block_out, d_inner, d_outer), first, second)
    away = (first.x(), second.y())
    d_pre0, sums_b0, grad_part = back_conv(0, tie(spots, *away), ())
    d_pre0 = arrive(d_pre0, first, second)
    away = (first.y(), second.x())
    d_pre1, sums_b1, keep, send = back_conv(1, tie(spots, *away), (grad_part,))
    send = arrive(send, first, second)
    third = Reduction(place, keep, send)
    sent = jnp.concatenate([first.pieces(), second.pieces()], axis=1)
    got = exchange(place, sent)
    third.got = tie(third.got, sent)
    away = (sent, third.x())
    input_grad, sums_a = call(
        functools.partial(back_a_kernel, pieces, steps // 2),
        (steps,),
        [SMEM]
        + [
            pl.BlockSpec((tile, INNER), lambda i: (jnp.minimum(i, steps // 2 - 1), 0)),
            pl.BlockSpec((tile, INNER), lambda i: (jnp.maximum(i - steps // 2, 0), 0)),
        ]
        + [rows_spec(tile, D), rows_spec(tile, 1), rows_spec(tile, D), rows_spec(tile, D)]
        + [params_spec]
        + [ANY] * pieces,
        [rows_spec(tile, D), whole(2, D)],
        [shape((rows, D), F32), shape((2, D), F32)],
        [
            pltpu.VMEM((D, INNER), BF16),
            pltpu.VMEM((INNER, D), BF16),
            pltpu.VMEM((tile, D), F32),
            pltpu.VMEM((16, D), F32),
            dma((pieces,)),
        ],
        us=17,
    )(
        tie(spots, *away), d_pre0, d_pre1, xhat_a, rstd_a, slope_a, cotangent, norm_params, *in_pieces
    )

    row_states, col_states = (row_in, row_conv, row_out), (col_in, col_conv, col_out)
    row_specs = [whole(*r.shape) for r in row_states]
    col_specs = [whole(*c.shape) for c in col_states]
    cols_all = D + 2 * INNER
    pack_spec = whole(4, cols_all)
    fulls = [pltpu.VMEM(half_dims(c)[1:], BF16) for c in CHUNKS]
    sums = (sums_a, sums_b0, sums_b1, sums_c)
    norm_tiles = call(
        functools.partial(norm_tiles_kernel, place.seq),
        (1,),
        [whole(*x.shape) for x in sums],
        whole(place.seq, SUB, LANE),
        shape((place.seq, SUB, LANE), BF16),
        [pltpu.VMEM((8, cols_all), F32)],
        us=1,
    )(*sums)
    got, third.got, norm_tiles = lax.optimization_barrier((got, third.got, norm_tiles))
    part = summed(got)
    sent = jnp.concatenate([third.all_pieces(), norm_tiles[:, None]], axis=1)
    got = exchange_all(sent)
    mine = exchange(place, jnp.broadcast_to(part[None], (place.seq // 2,) + part.shape))
    (pack,) = call(
        functools.partial(pack_kernel, rows_of, [half_dims(c)[1] // place.seq for c in CHUNKS]),
        (1,),
        [SMEM, whole(*part.shape)] + row_specs,
        [pack_spec],
        [shape((4, cols_all), F32)],
        [pltpu.VMEM((cols_all // LANE + 1, SUB, LANE), F32)],
        us=2,
    )(spots, part, *row_states)
    pack = sum_over(pack, place, "fsdp")
    pack = pack + place.flip(pack, "seq", 1)
    mine, got, pack = lax.optimization_barrier((mine, got, pack))
    other = place.flip(mine, "seq", 1)
    last = summed_f32(got)
    last = jnp.concatenate([last[:-1].astype(BF16), high_low(last[-1:])], axis=0)
    got_in = exchange_all(jnp.broadcast_to(last[None], (place.seq,) + last.shape))
    for bit in bits_of(place.seq)[1:]:
        pack = pack + place.flip(pack, "seq", bit)
    got_in, other, pack = lax.optimization_barrier((got_in, other, pack))

    def update_scratch(weights):
        lines = max(w.shape[0] + -w.shape[0] % LANE for w in weights)
        return [pltpu.VMEM((8, lines), F32)] + [pltpu.VMEM((lines, LANE), F32)] * 2

    weight_specs = [whole(*w.shape) for w in weights]
    (pack_in,) = call(
        functools.partial(pack_in_kernel, rows_of),
        (1,),
        [SMEM, ANY],
        [pack_spec],
        [shape((4, cols_all), F32)],
        [fulls[2], pltpu.VMEM((place.seq, SUB, LANE), BF16)] + [dma((place.seq,))] * 2,
        us=2,
    )(spots, got_in)
    pack_in = sum_over(pack_in, place, "fsdp")
    results = call(
        functools.partial(update_kernel, rows_of, place.seq),
        (1,),
        [SMEM, ANY, ANY, pack_spec] + weight_specs[1:] + row_specs[1:] + col_specs[1:],
        weight_specs[1:] * 2 + row_specs[1:] + col_specs[1:],
        [shape(w.shape, F32) for w in weights[1:]] * 2
        + [shape(r.shape, F32) for r in row_states[1:] + col_states[1:]],
        update_scratch(weights[1:]) + fulls[:2] + [dma((2 * place.seq,))],
        us=8,
    )(spots, mine, other, pack, *weights[1:], *row_states[1:], *col_states[1:])
    grad_conv, grad_out, new_conv, new_out, row_conv_new, row_out_new, col_conv_new, col_out_new = (
        results
    )
    grad_in, new_in, row_in_new, col_in_new, *norm_results = call(
        functools.partial(update_in_kernel, rows_of, place.seq),
        (1,),
        [SMEM, ANY, pack_spec, pack_spec, params_spec, params_spec]
        + [weight_specs[0], row_specs[0], col_specs[0]],
        [weight_specs[0]] * 2 + [row_specs[0], col_specs[0]] + [params_spec] * 3,
        [shape(w_in.shape, F32)] * 2
        + [shape(row_in.shape, F32), shape(col_in.shape, F32)]
        + [shape((2, cols_all), F32)] * 3,
        update_scratch(weights[:1]) + [fulls[2], dma((place.seq,))],
        us=4,
    )(spots, got_in, pack_in, pack, norm_params, norm_second, w_in, row_in, col_in)
    return (
        block_out,
        input_grad,
        grad_in,
        grad_conv,
        grad_out,
        new_in,
        new_conv,
        new_out,
        row_in_new,
        col_in_new,
        row_conv_new,
        col_conv_new,
        row_out_new,
        col_out_new,
        *norm_results,
    )


def solution(mesh):
    both, rows = P(AXES, None), P("fsdp", None)
    in_specs = (
        both, P(AXES), P(), both, rows, rows, rows, P(),
        P("fsdp"), P(), P("fsdp"), P(), P("fsdp"), P(), P(),
    )
    out_specs = (
        both, both, rows, rows, rows, rows, rows, rows,
        P("fsdp"), P(), P("fsdp"), P(), P("fsdp"), P(), P(), P(), P(),
    )
    return jax.shard_map(
        on_device, mesh=mesh, in_specs=in_specs, out_specs=out_specs, check_vma=False
    )
```

```python
import functools
import math

import jax
import jax.numpy as jnp
from jax import lax
from jax.experimental import pallas as pl
from jax.experimental.pallas import tpu as pltpu
from jax.sharding import PartitionSpec as P

D = 1280
INNER = 640
KERNEL_TAPS = 5
DILATION_STEP = 128
STEP = 10
EPSILON = 1e-05
DECAY = 1.0 - STEP ** (-0.8)

REACH = (KERNEL_TAPS - 1) // 2 * DILATION_STEP
MID = (KERNEL_TAPS - 1) // 2
F32 = jnp.float32
BF16 = jnp.bfloat16
SUB, LANE = 16, 128
AXES = ("seq", "fsdp")
NT = (((1,), (1,)), ((), ()))
TN = (((0,), (0,)), ((), ()))
NN = (((1,), (0,)), ((), ()))
VMEM_LIMIT = 58 * 1024 * 1024


def call(kernel, grid, in_specs, out_specs, out_shape, scratch=(), us=1.0, aliases=None):
    params = pltpu.CompilerParams(
        vmem_limit_bytes=VMEM_LIMIT, dimension_semantics=("arbitrary",) * len(grid)
    )
    return pl.pallas_call(
        kernel,
        grid=grid,
        in_specs=in_specs,
        out_specs=out_specs,
        out_shape=out_shape,
        scratch_shapes=list(scratch),
        compiler_params=params,
        input_output_aliases=aliases or {},
        cost_estimate=pl.CostEstimate(
                flops=int(us * 1.1e9), bytes_accessed=int(us * 3.4e6), transcendentals=0
        ),
    )


def shape(dims, dtype):
    return jax.ShapeDtypeStruct(dims, dtype)


def rows_spec(tile, width):
    return pl.BlockSpec((tile, width), lambda i: (i, 0))


def whole(*dims):
    return pl.BlockSpec(dims, lambda *_: (0,) * len(dims))


ANY = pl.BlockSpec(memory_space=pl.ANY)
SMEM = pl.BlockSpec(memory_space=pltpu.SMEM)


ERFC_P = 0.47 / math.sqrt(2.0)
ERFC_C = (
    0.12357219400743558,
    0.1999878668208835,
    -0.08033356004356296,
    0.3660253986657854,
    -0.1092519747040215,
)
LOG2E = 1.4426950408889634


def gelu_and_slope(y):
    t = pltpu.reciprocal(1.0 + ERFC_P * jnp.abs(y), approx=True)
    bell = jnp.exp2(y * y * (-0.5 * LOG2E))
    poly = ERFC_C[4] * t + ERFC_C[3]
    for c in ERFC_C[2::-1]:
        poly = poly * t + c
    tail = poly * t * bell
    cdf = jnp.where(y > 0.0, 1.0 - tail, tail)
    return y * cdf, cdf + y * (bell * (1.0 / math.sqrt(2.0 * math.pi)))


def lane_blocks(width):
    return [slice(k, k + LANE) for k in range(0, width, LANE)]


def row_stats(ref, rows):
    width = ref.shape[-1]
    blocks = lane_blocks(width)
    total = ref[rows, blocks[0]].astype(F32)
    for b in blocks[1:]:
        total = total + ref[rows, b].astype(F32)
    mean = jnp.sum(total, axis=-1, keepdims=True) * (1.0 / width)
    square = None
    for b in blocks:
        centered = ref[rows, b].astype(F32) - mean
        square = centered * centered if square is None else square + centered * centered
    variance = jnp.sum(square, axis=-1, keepdims=True) * (1.0 / width)
    return mean, lax.rsqrt(variance + EPSILON)


def fold(values):
    total = values[0:8]
    for k in range(8, values.shape[0], 8):
        total = total + values[k : k + 8]
    return total


def in_stages(count, stages, base=None, chunk=None):
    chunk = chunk or CHUNK
    if base is None:
        chunks = [slice(k, k + chunk) for k in range(0, count, chunk)]
    else:
        chunks = [pl.ds(pl.multiple_of(base + k, chunk), chunk) for k in range(0, count, chunk)]
    kept = {}
    for t in range(len(chunks) + len(stages) - 1):
        for n, stage in enumerate(stages):
            if 0 <= t - n < len(chunks):
                kept[n, t - n] = stage(chunks[t - n], kept.get((n - 1, t - n)))


def halves_of(count):
    return (slice(0, count // 2), slice(count // 2, count))


def row_means(sums, width):
    return [jnp.sum(x, axis=-1, keepdims=True) * (1.0 / width) for x in sums]


def norm_back(rows, dxhat_ref, xhat_ref, means, put):
    mean_d, mean_dx, rstd = means
    for b in lane_blocks(dxhat_ref.shape[-1]):
        xhat = xhat_ref[rows, b].astype(F32)
        put(b, (dxhat_ref[rows, b] - mean_d - xhat * mean_dx) * rstd)


def add_terms(acc_ref, b, dy, xhat):
    acc_ref[0:8, b] += fold(dy * xhat)
    acc_ref[8:16, b] += fold(dy)


def open_sums(acc_ref):
    @pl.when(pl.program_id(0) == 0)
    def _():
        acc_ref[...] = jnp.zeros_like(acc_ref)


def close_sums(out_ref, acc_ref):
    @pl.when(pl.program_id(0) == pl.num_programs(0) - 1)
    def _():
        out_ref[0:1, :] = jnp.sum(acc_ref[0:8, :], axis=0, keepdims=True)
        out_ref[1:2, :] = jnp.sum(acc_ref[8:16, :], axis=0, keepdims=True)


def run_copies(copies):
    for copy in copies:
        copy.start()
    for copy in copies:
        copy.wait()


def piece_copies(pieces, full_ref, me, sem, first=0):
    each = full_ref.shape[0] // len(pieces)
    return [
        pltpu.make_async_copy(
            piece.at[0:each, :],
            full_ref.at[pl.ds(pl.multiple_of((me ^ k) * each, SUB), each), :],
            sem.at[first + k],
        )
        for k, piece in enumerate(pieces)
    ]


def out_copies(pieces, full_ref, me, sem, first=0):
    each, width = full_ref.shape[0] // len(pieces), full_ref.shape[1] // 2
    copies = []
    for k, piece in enumerate(pieces):
        rows = pl.ds(pl.multiple_of((me ^ k) * each, SUB), each)
        for side in range(2):
            at = piece.shape[0] - (2 - side) * each
            copies.append(
                pltpu.make_async_copy(
                    piece.at[at : at + each, :],
                    full_ref.at[rows, side * width : (side + 1) * width],
                    sem.at[first + 2 * k + side],
                )
            )
    return copies


def column(row):
    return jnp.transpose(jnp.broadcast_to(row, (LANE, LANE)))


CHUNK = 64


def norm_a_kernel(tok_ref, np_ref, hid_ref, slope_ref, xhat_ref, rstd_ref):
    def stats(rows, _):
        mean, rstd = row_stats(tok_ref, rows)
        rstd_ref[rows, :] = rstd
        return mean, rstd

    def work(rows, kept):
        mean, rstd = kept
        for b in lane_blocks(D):
            xhat = (tok_ref[rows, b].astype(F32) - mean) * rstd
            hidden, slope = gelu_and_slope(xhat * np_ref[0:1, b] + np_ref[1:2, b])
            hid_ref[rows, b] = hidden.astype(BF16)
            slope_ref[rows, b] = slope.astype(BF16)
            xhat_ref[rows, b] = xhat.astype(BF16)

    in_stages(tok_ref.shape[0], [stats, work], chunk=128)


def running_ends(ends_ref, lengths_ref):
    docs, width = lengths_ref.shape[0], ends_ref.shape[1]
    ends_ref[...] = jnp.zeros_like(ends_ref)
    ends_ref[0:1, 0:docs] = lengths_ref[...].reshape(1, -1).astype(F32)
    before = jnp.zeros((1, 1), F32)
    row = lax.broadcasted_iota(jnp.int32, (LANE, LANE), 0)
    lane = lax.broadcasted_iota(jnp.int32, (LANE, LANE), 1)
    for k in range(0, width, LANE):
        line = ends_ref[0:1, k : k + LANE]
        sums = jnp.sum(jnp.where(row <= lane, column(line), 0.0), axis=0, keepdims=True) + before
        ends_ref[0:1, k : k + LANE] = jnp.where(lane[0:1] + k < docs, sums, 1e9)
        before = before + jnp.sum(line, axis=1, keepdims=True)


def in_kernel(pieces, tiles, place_ref, lengths_ref, hid_ref, live_ref, np_ref, *refs):
    piece_refs = refs[:pieces]
    edges = tiles[0] == 0
    outs = refs[-(11 if edges else 9) :]
    mov_ref, slope_ref, xhat_ref, rstd_ref, mask_ref = outs[:5]
    w_ref, pre_ref, ends_ref, sem = outs[-4:]
    step = pl.program_id(0)
    tile = hid_ref.shape[0]

    @pl.when(step == 0)
    def _():
        copies = piece_copies(piece_refs, w_ref, place_ref[0], sem)
        for copy in copies:
            copy.start()
        running_ends(ends_ref, lengths_ref)
        for copy in copies:
            copy.wait()

    for half in halves_of(tile):
        pre_ref[half, :] = lax.dot_general(
            hid_ref[half, :], w_ref[...], NN, preferred_element_type=F32
        )

    at_tile = tiles[0] + step * tiles[1]
    first = place_ref[1] + at_tile * tile
    ends = ends_ref[0:1, :]
    lanes = lax.broadcasted_iota(jnp.int32, (LANE, 8), 1)
    offsets = ((lanes - MID) * DILATION_STEP).astype(F32)
    for k in range(tile // LANE):
        at = (first + k * LANE + lax.broadcasted_iota(jnp.int32, (LANE, 1), 0)).astype(F32)
        begin = jnp.max(jnp.where(ends <= at, ends, 0.0), axis=1, keepdims=True)
        end = jnp.min(jnp.where(ends > at, ends, 1e9), axis=1, keepdims=True)
        there = at + offsets
        same = jnp.where((there >= begin) & (there < end), 1.0, 0.0)
        live = column(live_ref[pl.ds(at_tile * (tile // LANE) + k, 1), :].astype(F32))
        mask_ref[k * LANE : (k + 1) * LANE, :] = jnp.where(lanes == MID, live[:, 0:8], same)

    def stats(rows, _):
        mean, rstd = row_stats(pre_ref, rows)
        rstd_ref[rows, :] = rstd
        return mean, rstd

    def work(rows, kept):
        mean, rstd = kept
        live = mask_ref[rows, MID : MID + 1]
        for b in lane_blocks(INNER):
            gains = slice(D + b.start, D + b.stop)
            xhat = (pre_ref[rows, b] - mean) * rstd
            hidden, slope = gelu_and_slope(xhat * np_ref[0:1, gains] + np_ref[1:2, gains])
            mov_ref[rows, b] = (hidden * live).astype(BF16)
            slope_ref[rows, b] = slope.astype(BF16)
            xhat_ref[rows, b] = xhat.astype(BF16)

    in_stages(tile, [stats, work])
    if edges:
        put_edges(place_ref, outs[5], outs[6], mov_ref, step == 0, step == 1)


def load_window(place_ref, inner, mid, outer, ext_ref, sem):
    rows, core = mid.shape[0], lax.rem(place_ref[0], 2)
    near = pl.multiple_of((1 - core) * (REACH + rows), SUB)
    far = pl.multiple_of(core * (REACH + rows), SUB)
    return [
        pltpu.make_async_copy(inner, ext_ref.at[pl.ds(near, REACH), :], sem.at[0]),
        pltpu.make_async_copy(mid, ext_ref.at[REACH : REACH + rows, :], sem.at[1]),
        pltpu.make_async_copy(outer, ext_ref.at[pl.ds(far, REACH), :], sem.at[2]),
    ]


def put_edges(place_ref, inner_ref, outer_ref, tile_ref, at_first, at_last):
    rows, core = tile_ref.shape[0], lax.rem(place_ref[0], 2)
    for at, edge, first in ((at_first, slice(0, REACH), 0), (at_last, slice(rows - REACH, rows), 1)):

        @pl.when(at & (core == first))
        def _(edge=edge):
            outer_ref[...] = tile_ref[edge, :]

        @pl.when(at & (core != first))
        def _(edge=edge):
            inner_ref[...] = tile_ref[edge, :]


def fill_taps(taps_ref, ext_ref, mask_ref, start):
    tile = taps_ref.shape[0]
    for j in range(KERNEL_TAPS):
        rows = pl.ds(pl.multiple_of(start + j * DILATION_STEP, DILATION_STEP), tile)
        picked = ext_ref[rows, :]
        if j != MID:
            picked = picked * mask_ref[:, j : j + 1].astype(BF16)
        taps_ref[:, j * INNER : (j + 1) * INNER] = picked


def conv_kernel(
    pieces, rows_of, place_ref, low_ref, mov_ref, high_ref, mask_ref, cot_ref, before_ref, np_ref, *refs
):
    piece_refs = refs[:pieces]
    hid_ref, dconv_ref, inner_ref, outer_ref, sums_ref, turned_ref = refs[pieces : pieces + 6]
    outs = refs[pieces + 6 : pieces + 10]
    ext_ref, wc_ref, wct_ref, wo_ref, wt_ref, taps_ref, pre_ref, dh_ref, xhat_ref = refs[
        pieces + 10 : pieces + 19
    ]
    dt_ref, ht_ref, gc_ref, go_ref, acc_ref, stage1_ref, stage2_ref, sem = refs[pieces + 19 :]
    step, steps = pl.program_id(0), pl.num_programs(0) - 1
    tile = taps_ref.shape[1]
    slot = lax.rem(step, 2)

    @pl.when(step == 0)
    def _():
        me = place_ref[0]
        outs = out_copies(piece_refs, wo_ref, me, sem, 3)
        rest = load_window(place_ref, low_ref, mov_ref, high_ref, ext_ref, sem)
        rest += piece_copies(piece_refs, wc_ref, me, sem, 3 + 2 * pieces)
        for copy in outs + rest:
            copy.start()
        for ref in (acc_ref, gc_ref, go_ref, dt_ref, ht_ref):
            ref[...] = jnp.zeros_like(ref)
        taps_ref[1] = jnp.zeros_like(taps_ref[1])
        for copy in outs:
            copy.wait()
        for k in range(0, D, 256):
            wt_ref[k : k + 256, :] = jnp.transpose(wo_ref[:, k : k + 256])
        for copy in rest:
            copy.wait()

    taps_wide, turns = KERNEL_TAPS * INNER, 4
    conv_part, out_part = 768, 256

    def grad_conv(at, width):
        cols = pl.ds(at, width)
        gc_ref[:, cols] += lax.dot_general(
            dt_ref[...], taps_ref[1 - slot, :, cols], NN, preferred_element_type=F32
        )

    def grad_out(at, width):
        cols = pl.ds(at, width)
        go_ref[:, cols] += lax.dot_general(
            ht_ref[...], before_ref[:, cols], NN, preferred_element_type=F32
        )

    def rest_of_products():
        grad_conv(turns * conv_part, taps_wide - turns * conv_part)
        grad_out(turns * out_part, D - turns * out_part)

    def product_turn(q):
        grad_conv(pl.multiple_of(q * conv_part, LANE), conv_part)
        grad_out(pl.multiple_of(q * out_part, LANE), out_part)

    @pl.when(step < steps)
    def _():
        fill_taps(taps_ref.at[slot], ext_ref, mask_ref, step * tile)
        pre_ref[...] = lax.dot_general(
            taps_ref[slot], wc_ref[...], NN, preferred_element_type=F32
        )
        dh_ref[...] = lax.dot_general(cot_ref[...], wt_ref[...], NN, preferred_element_type=F32)
        for n in range(2):
            tap = jnp.minimum(2 * step + n, KERNEL_TAPS - 1)
            source = wc_ref[pl.ds(pl.multiple_of(tap * INNER, SUB), INNER), :]
            target = pl.multiple_of((KERNEL_TAPS - 1 - tap) * INNER, SUB)
            wct_ref[pl.ds(target, INNER), :] = jnp.transpose(source)

        def stats(rows, _):
            return row_stats(pre_ref, rows)

        def work(rows, kept):
            mean, rstd = kept
            sums = [0.0, 0.0]
            for b in lane_blocks(INNER):
                gains = slice(D + INNER + b.start, D + INNER + b.stop)
                gain = np_ref[0:1, gains]
                xhat = (pre_ref[rows, b] - mean) * rstd
                hidden, slope = gelu_and_slope(xhat * gain + np_ref[1:2, gains])
                hid_ref[rows, b] = hidden.astype(BF16)
                dy = dh_ref[rows, b] * slope
                add_terms(acc_ref, b, dy, xhat)
                dxhat = dy * gain
                xhat_ref[rows, b] = xhat
                dh_ref[rows, b] = dxhat
                sums = [sums[0] + dxhat, sums[1] + dxhat * xhat]
            return row_means(sums, INNER) + [rstd]

        def finish(rows, means):
            def put(b, value):
                dconv_ref[rows, b] = value.astype(BF16)

            norm_back(rows, dh_ref, xhat_ref, means, put)

        def turn(q, carry):
            product_turn(q)
            in_stages(tile // turns, [stats, work, finish], q * (tile // turns))
            return carry

        lax.fori_loop(0, turns, turn, 0)
        rest_of_products()
        dt_ref[...] = jnp.transpose(dconv_ref[...])
        ht_ref[...] = jnp.transpose(hid_ref[...])

    put_edges(place_ref, inner_ref, outer_ref, dconv_ref, step == 0, step == steps - 1)

    @pl.when(step == steps)
    def _():
        copy = pltpu.make_async_copy(wct_ref, turned_ref, sem.at[4])
        copy.start()
        for q in range(turns):
            product_turn(q)
        rest_of_products()
        core = lax.rem(place_ref[0], 2)
        _, rows_conv, rows_out = rows_of
        stage_turned(stage1_ref, core, gc_ref, rows_conv, 0, slice(0, CUT // LANE))
        first_tiles = rows_conv // SUB * (CUT // LANE)
        stage_plain(stage1_ref, core, go_ref, rows_out, first_tiles)
        copies = stage_copies(stage1_ref, outs[0], outs[1], spans(CHUNKS[0], rows_of)[1], sem, 0)
        for each in copies:
            each.start()
        stage_turned(stage2_ref, core, gc_ref, rows_conv, 0, slice(CUT // LANE, INNER // LANE))
        more = stage_copies(stage2_ref, outs[2], outs[3], spans(CHUNKS[1], rows_of)[1], sem, 2)
        for each in more:
            each.start()
        for each in copies + more + [copy]:
            each.wait()
        sums_ref[0:1, :] = jnp.sum(acc_ref[0:8, :], axis=0, keepdims=True)
        sums_ref[1:2, :] = jnp.sum(acc_ref[8:16, :], axis=0, keepdims=True)


def stage_tiles(stage_ref, core, first_row, rows_each, base, block0, blocks, value):
    for g in range(value.shape[0] // SUB):
        row = first_row + g * SUB
        owner, inside = row // rows_each, row % rows_each // SUB
        side = core ^ (owner % 2)
        for b in range(value.shape[1] // LANE):
            tile = value[g * SUB : (g + 1) * SUB, b * LANE : (b + 1) * LANE]
            at = base + inside * blocks + block0 + b
            stage_ref[side, owner // 2, at] = tile.astype(BF16)


def stage_plain(stage_ref, core, grad_ref, rows_each, base):
    blocks = grad_ref.shape[1] // LANE
    for row in range(0, grad_ref.shape[0], SUB):
        part = grad_ref[row : row + SUB, :]
        stage_tiles(stage_ref, core, row, rows_each, base, 0, blocks, part)


def stage_turned(stage_ref, core, turned_ref, rows_each, base, blocks):
    count = blocks.stop - blocks.start
    for row in range(0, turned_ref.shape[1], LANE):
        for b in range(count):
            at = (blocks.start + b) * LANE
            part = jnp.transpose(turned_ref[at : at + LANE, row : row + LANE].astype(BF16))
            stage_tiles(stage_ref, core, row, rows_each, base, b, count, part)


def stage_copies(stage_ref, keep_ref, send_ref, used, sem, first):
    count = stage_ref.shape[2]
    if used < count:
        dims = stage_ref.shape[:2] + (count - used, SUB, LANE)
        stage_ref[:, :, used:] = jnp.zeros(dims, BF16)
    return [
        pltpu.make_async_copy(stage_ref.at[n], ref, sem.at[first + n])
        for n, ref in enumerate((keep_ref, send_ref))
    ]


def back_conv_kernel(
    last, rows_in, place_ref, low_ref, d_ref, high_ref, turned_ref, mask_ref, xhat_ref, rstd_ref, slope_ref, hid_ref, np_ref, *refs
):
    if last:
        before_ref, dpre_ref, sums_ref, keep_ref, send_ref, stage_ref = refs[:6]
    else:
        dpre_ref, sums_ref, part_ref = refs[:3]
    ext_ref, wt_ref, taps_ref, dmov_ref, grad_ref, acc_ref, sem = refs[-7:]
    step, steps = pl.program_id(0), pl.num_programs(0)
    tile = taps_ref.shape[0]
    open_sums(acc_ref)

    @pl.when(step == 0)
    def _():
        copies = load_window(place_ref, low_ref, d_ref, high_ref, ext_ref, sem)
        copies.append(pltpu.make_async_copy(turned_ref, wt_ref, sem.at[3]))
        if last:
            copies.append(pltpu.make_async_copy(before_ref, grad_ref, sem.at[4]))
        for copy in copies:
            copy.start()
        if not last:
            grad_ref[...] = jnp.zeros_like(grad_ref)
        for copy in copies:
            copy.wait()

    fill_taps(taps_ref, ext_ref, mask_ref, (steps * last + step) * tile)
    for half in halves_of(tile):
        dmov_ref[half, :] = lax.dot_general(
            taps_ref[half, :], wt_ref[...], NN, preferred_element_type=F32
        )

    def work(rows, _):
        live = mask_ref[rows, MID : MID + 1]
        sums = [0.0, 0.0]
        for b in lane_blocks(INNER):
            xhat = xhat_ref[rows, b].astype(F32)
            dy = dmov_ref[rows, b] * live * slope_ref[rows, b].astype(F32)
            add_terms(acc_ref, b, dy, xhat)
            dxhat = dy * np_ref[0:1, D + b.start : D + b.stop]
            dmov_ref[rows, b] = dxhat
            sums = [sums[0] + dxhat, sums[1] + dxhat * xhat]
        return row_means(sums, INNER) + [rstd_ref[rows, :]]

    def finish(rows, means):
        def put(b, value):
            dpre_ref[rows, b] = value.astype(BF16)

        norm_back(rows, dmov_ref, xhat_ref, means, put)

    in_stages(tile, [work, finish])
    close_sums(sums_ref, acc_ref)
    grad_ref[...] += lax.dot_general(dpre_ref[...], hid_ref[...], TN, preferred_element_type=F32)

    @pl.when(step == steps - 1)
    def _():
        if last:
            all_blocks = slice(0, INNER // LANE)
            stage_turned(stage_ref, lax.rem(place_ref[0], 2), grad_ref, rows_in, 0, all_blocks)
            used = rows_in // SUB * (INNER // LANE)
            run_copies(stage_copies(stage_ref, keep_ref, send_ref, used, sem, 0))
        else:
            run_copies([pltpu.make_async_copy(grad_ref, part_ref, sem.at[0])])


def back_a_kernel(pieces, half, place_ref, dpre0_ref, dpre1_ref, xhat_ref, rstd_ref, slope_ref, cot_ref, np_ref, *refs):
    piece_refs = refs[:pieces]
    grad_ref, sums_ref, w_ref, wt_ref, dh_ref, acc_ref, sem = refs[-7:]
    open_sums(acc_ref)

    @pl.when(pl.program_id(0) == 0)
    def _():
        run_copies(piece_copies(piece_refs, w_ref, place_ref[0], sem))
        for k in range(0, D, 256):
            wt_ref[:, k : k + 256] = jnp.transpose(w_ref[k : k + 256, :])

    second = (jnp.zeros((1, 1), jnp.int32) + pl.program_id(0)) >= half
    d_pre = jnp.where(second, dpre1_ref[...], dpre0_ref[...])
    dh_ref[...] = lax.dot_general(d_pre, wt_ref[...], NN, preferred_element_type=F32)

    def work(rows, _):
        sums = [0.0, 0.0]
        for b in lane_blocks(D):
            xhat = xhat_ref[rows, b].astype(F32)
            dy = dh_ref[rows, b] * slope_ref[rows, b].astype(F32)
            add_terms(acc_ref, b, dy, xhat)
            dxhat = dy * np_ref[0:1, b]
            dh_ref[rows, b] = dxhat
            sums = [sums[0] + dxhat, sums[1] + dxhat * xhat]
        return row_means(sums, D) + [rstd_ref[rows, :]]

    def finish(rows, means):
        def put(b, value):
            grad_ref[rows, b] = cot_ref[rows, b].astype(F32) + value

        norm_back(rows, dh_ref, xhat_ref, means, put)

    in_stages(dpre0_ref.shape[0], [work, finish])
    close_sums(sums_ref, acc_ref)


def out_kernel(pieces, place_ref, hid_ref, tok_ref, *refs):
    piece_refs = refs[:pieces]
    out_ref, w_ref, sem = refs[pieces:]

    @pl.when(pl.program_id(0) == 0)
    def _():
        run_copies(out_copies(piece_refs, w_ref, place_ref[0], sem))

    branch = lax.dot_general(hid_ref[...], w_ref[...], NN, preferred_element_type=F32)
    out_ref[...] = (tok_ref[...].astype(F32) + branch).astype(BF16)


WIDTHS = (INNER, INNER, D)
LANE0 = (0, INNER, 2 * INNER)
CUT = 2 * LANE
CHUNKS = (((1, 0, CUT), (2, 0, D)), ((1, CUT, INNER - CUT),), ((0, 0, INNER),))


def spans(chunk, rows):
    found, first = [], 0
    for weight, col, cols in chunk:
        tiles = rows[weight] // SUB * (cols // LANE)
        found.append((weight, col // LANE, cols // LANE, first, tiles))
        first += tiles
    return found, first


def column_sums(pack_ref, row, ref, chunk, rows):
    for weight, block0, blocks, first, tiles in spans(chunk, rows)[0]:

        def body(g, carry, first=first, blocks=blocks):
            new = []
            for b in range(blocks):
                value = ref[first + g * blocks + b].astype(F32)
                new.append(carry[b] + fold(value * value + 1e-30))
            return tuple(new)

        zero = tuple(jnp.zeros((8, LANE), F32) for _ in range(blocks))
        cols = lax.fori_loop(0, tiles // blocks, body, zero, unroll=5)
        for b in range(blocks):
            lane = LANE0[weight] + (block0 + b) * LANE
            pack_ref[row : row + 1, lane : lane + LANE] = jnp.sum(cols[b], axis=0, keepdims=True)


def load_full(refs, place_ref, first, full_ref, sem, at):
    pieces = refs[0].shape[0]
    each = full_ref.shape[0] // (len(refs) * pieces)
    outer = pieces if len(refs) == 2 else pieces // 2
    y = place_ref[2] % 2
    copies = []
    for n, (ref, side) in enumerate(zip(refs, (y, 1 - y))):
        for p in range(pieces):
            index = side * outer + p if len(refs) == 2 else p % 2 * outer + p // 2
            target = full_ref.at[pl.ds(index * each, each)]
            source = ref.at[p, first : first + each]
            copies.append(pltpu.make_async_copy(source, target, sem.at[at + n * pieces + p]))
    return copies


def load_list(bits, mine_ref, other_ref, place_ref, full_ref, sem):
    me, copies = place_ref[2], []
    each = full_ref.shape[0] // (1 << len(bits))
    inner = mine_ref.shape[0]
    for n in range(2 * inner):
        ref, at, k = (mine_ref, other_ref)[n // inner], n % inner, 0
        for i, bit in enumerate(bits):
            if n >> (len(bits) - 1 - i) & 1:
                k |= bit
        device, index = me ^ k, 0
        for bit in sorted(bits):
            index = index * 2 + lax.rem(lax.div(device, bit), 2)
        target = full_ref.at[pl.ds(index * each, each)]
        copies.append(pltpu.make_async_copy(ref.at[at], target, sem.at[n]))
    return copies


def pack_kernel(rows, pieces, place_ref, part_ref, *refs):
    states, sums, (pack_ref, acc_ref) = refs[0:3], refs[3:7], refs[7:9]
    pack_ref[...] = jnp.zeros_like(pack_ref)
    lanes_of = ((0, D), (D, D + INNER), (D, D + INNER), (D + INNER, D + 2 * INNER))
    for part, (lane0, lane1) in zip(sums, lanes_of):
        pack_ref[0:2, lane0:lane1] += part[...]
    lanes = lax.broadcasted_iota(jnp.int32, (1, LANE), 1)
    for k in range(3):
        total = jnp.sum(states[k][...].reshape(1, -1), axis=1, keepdims=True)
        pack_ref[3:4, 0:LANE] += jnp.where(lanes == k, total, 0.0)
    acc_ref[...] = jnp.zeros_like(acc_ref)
    spare = acc_ref.shape[0] - 1
    outer = place_ref[3] // 2
    piece = place_ref[2] % 2 * outer + place_ref[2] // 2
    at = 0
    for chunk, each in zip(CHUNKS[:2], pieces):
        found, _ = spans(chunk, rows)
        start = piece * each

        def body(k, carry, found=found, start=start, at=at):
            n = start + k
            slot = spare
            for weight, block0, blocks, first, tiles in found:
                here = LANE0[weight] // LANE + block0 + lax.rem(jnp.maximum(n - first, 0), blocks)
                slot = jnp.where((n >= first) & (n < first + tiles), here, slot)
            value = part_ref[at + k].astype(F32)
            acc_ref[slot] += value * value + 1e-30
            return carry

        lax.fori_loop(0, each, body, 0, unroll=2)
        at += each
    for slot in range(spare):
        pack_ref[2:3, slot * LANE : (slot + 1) * LANE] = jnp.sum(acc_ref[slot], axis=0, keepdims=True)


def pack_in_kernel(rows, bits, place_ref, mine_ref, other_ref, pack_ref, full_ref, sem):
    run_copies(load_list(bits, mine_ref, other_ref, place_ref, full_ref, sem))
    pack_ref[...] = jnp.zeros_like(pack_ref)
    column_sums(pack_ref, 0, full_ref, CHUNKS[2], rows)


def update_weight(
    k, squares, states_sum, source, weight, state, col_state, grad_ref, new, row_new_ref, col_new_ref, scratch
):
    line_ref, state_ref, new_ref = scratch
    width, fan, rows_here = WIDTHS[k], (D, KERNEL_TAPS * INNER, INNER)[k], weight.shape[0]
    col_new = DECAY * col_state[...].reshape(1, -1) + (1.0 - DECAY) * (squares * (1.0 / fan))
    col_new_ref[...] = col_new.reshape(-1)
    total = DECAY * states_sum
    total = total + (1.0 - DECAY) * (1.0 / width) * jnp.sum(squares, axis=1, keepdims=True)
    scaled = col_new / (total * (1.0 / fan))
    rate = 0.5 / fan**0.5
    line_ref[0:1, 0:rows_here] = state[...].reshape(1, -1)
    whole_rows = rows_here + -rows_here % LANE
    for c in range(0, whole_rows, LANE):
        state_ref[c : c + LANE, :] = column(line_ref[0:1, c : c + LANE])

    def body(g, carry):
        rows = pl.ds(pl.multiple_of(g * SUB, SUB), SUB)
        square = 0.0
        for ref, block0, blocks, first in source:
            for b in range(blocks):
                value = ref[first + g * blocks + b].astype(F32)
                grad_ref[rows, (block0 + b) * LANE : (block0 + b + 1) * LANE] = value
                square = square + (value * value + 1e-30)
        mean = jnp.sum(square, axis=1, keepdims=True) * (1.0 / width)
        row_new = DECAY * state_ref[rows, :] + (1.0 - DECAY) * mean
        new_ref[rows, :] = row_new
        for ref, block0, blocks, first in source:
            for b in range(blocks):
                lanes = slice((block0 + b) * LANE, (block0 + b + 1) * LANE)
                value = ref[first + g * blocks + b].astype(F32)
                step = value * lax.rsqrt(row_new * scaled[:, lanes])
                new[rows, lanes] = weight[rows, lanes] - rate * step
        return carry

    lax.fori_loop(0, rows_here // SUB, body, 0, unroll=5)
    for c in range(0, whole_rows, LANE):
        line_ref[0:1, c : c + LANE] = jnp.transpose(new_ref[c : c + LANE, :])[0:1, :]
    row_new_ref[...] = line_ref[0:1, 0:rows_here].reshape(-1)


def sources_of(chunk, ref, rows):
    return {w: (ref, block0, blocks, first) for w, block0, blocks, first, _ in spans(chunk, rows)[0]}


def update_kernel(rows, copies_of, place_ref, mine_ref, other_ref, pack_ref, *refs):
    weights, states, col_states = refs[0:2], refs[2:4], refs[4:6]
    grads, news, rows_new, cols_new = refs[6:8], refs[8:10], refs[10:12], refs[12:14]
    full1_ref, full2_ref, sem = refs[17:20]
    both = (mine_ref, other_ref)
    count = 2 * mine_ref.shape[0]
    copies = load_full(both, place_ref, 0, full1_ref, sem, 0)
    copies += load_full(both, place_ref, full1_ref.shape[0] // count, full2_ref, sem, count)
    run_copies(copies)
    from1 = sources_of(CHUNKS[0], full1_ref, rows)
    from2 = sources_of(CHUNKS[1], full2_ref, rows)
    for n, (k, source) in enumerate(((1, [from1[1], from2[1]]), (2, [from1[2]]))):
        squares = pack_ref[2:3, LANE0[k] : LANE0[k] + WIDTHS[k]]
        update_weight(
            k, squares, pack_ref[3:4, k : k + 1] * (1.0 / copies_of), source, weights[n],
            states[n], col_states[n], grads[n], news[n], rows_new[n], cols_new[n], refs[14:17],
        )


def update_in_kernel(
    rows, copies_of, bits, place_ref, mine_ref, other_ref, pack_in_ref, pack_ref, np_ref, second_ref, *refs
):
    weight, state, col_state, grad_ref, new_ref, row_new_ref, col_new_ref = refs[0:7]
    ngrad_ref, nsecond_ref, nnew_ref = refs[7:10]
    full_ref, sem = refs[13:15]
    copies = load_list(bits, mine_ref, other_ref, place_ref, full_ref, sem)
    for copy in copies:
        copy.start()
    grad = pack_ref[0:2, :]
    second = DECAY * second_ref[...] + (1.0 - DECAY) * (grad * grad + 1e-30)
    ngrad_ref[...] = grad
    nsecond_ref[...] = second
    nnew_ref[...] = np_ref[...] - 0.2 * grad * lax.rsqrt(second)
    for copy in copies:
        copy.wait()
    update_weight(
        0, pack_in_ref[0:1, :], pack_ref[3:4, 0:1] * (1.0 / copies_of),
        [sources_of(CHUNKS[2], full_ref, rows)[0]], weight, state, col_state, grad_ref, new_ref,
        row_new_ref, col_new_ref, refs[10:13],
    )


class Places:
    def __init__(self):
        self.seq, self.fsdp = lax.axis_size("seq"), lax.axis_size("fsdp")
        self.q = lax.axis_index("fsdp")
        self.s = lax.axis_index("seq")

    def flip(self, x, axis, bit):
        pairs = []
        for s in range(self.seq):
            for f in range(self.fsdp):
                s2, f2 = (s ^ bit, f) if axis == "seq" else (s, f ^ bit)
                pairs.append((s * self.fsdp + f, s2 * self.fsdp + f2))
        return lax.ppermute(x, AXES, pairs)


def bits_of(count):
    return [1 << k for k in range(count.bit_length() - 1)]


def tie(x, *others):
    return lax.optimization_barrier((x, *others))[0]


def gather_pieces(piece, place, after, later=()):
    found = {0: piece}
    for bit in reversed(bits_of(place.fsdp)):
        for k in list(found):
            moving = found[k]
            if bit == 1:
                moving = tie(moving, *((after,) if k == 0 or not later else later))
            found[k | bit] = place.flip(moving, "fsdp", bit)
    return [found[k] for k in range(place.fsdp)]


def sum_over(x, place, *axes):
    for axis in axes:
        for bit in bits_of(getattr(place, axis)):
            x = x + place.flip(x, axis, bit)
    return x


def pick(x, index, axis):
    return lax.dynamic_index_in_dim(x, index, axis=axis, keepdims=False)


class Reduction:
    def __init__(self, place, keep, send):
        self.place, self.near = place, keep
        self.got = place.flip(send, "fsdp", 1)

    def halve(self, axis, side, flip_axis, bit):
        dims = self.near.shape
        parts = dims[:axis] + (2, dims[axis] // 2) + dims[axis + 1 :]
        near, got = self.near.reshape(parts), self.got.reshape(parts)
        away = pick(near, 1 - side, axis).astype(F32) + pick(got, 1 - side, axis).astype(F32)
        self.near = pick(near, side, axis).astype(F32) + pick(got, side, axis).astype(F32)
        away = away.astype(BF16)
        self.got = self.place.flip(away, flip_axis, bit)
        return away

    def x(self):
        bit = self.place.fsdp // 2
        while bit > 1:
            away = self.halve(0, (self.place.q // bit) % 2, "fsdp", bit)
            bit //= 2
        return away

    def y(self):
        return self.halve(1, self.place.s % 2, "seq", 1)

    def seq_bit(self, bit):
        return self.halve(1, (self.place.s // bit) % 2, "seq", bit)

    def piece(self):
        total = (self.near + self.got.astype(F32)).astype(BF16)
        return total.reshape(total.shape[1:])

    def pieces(self):
        total = (self.near + self.got.astype(F32)).astype(BF16)
        return total.reshape((self.place.seq // 2, -1) + total.shape[2:])


def arrive(result, *reductions):
    result, *gots = lax.optimization_barrier((result, *[r.got for r in reductions]))
    for reduction, got in zip(reductions, gots):
        reduction.got = got
    return result


def summed_f32(got):
    return jnp.sum(got.astype(F32), axis=0)


def summed(got):
    return summed_f32(got).astype(BF16)


def exchange(place, sent):
    line = [[y + 2 * z for z in range(place.seq // 2)] for y in range(2)]
    return lax.all_to_all(sent, "seq", 0, 0, axis_index_groups=line)


def on_device(
    tokens, input_mask, doc_lengths, cotangent, w_in, w_conv, w_out, norm_params,
    row_in, col_in, row_conv, col_conv, row_out, col_out, norm_second,
):
    place = Places()
    rows = tokens.shape[0]
    pieces = place.fsdp
    spots = jnp.stack(
        [place.q, (place.s * place.fsdp + place.q) * rows, place.s, place.seq]
    ).astype(jnp.int32)
    docs = doc_lengths.shape[0]
    live = input_mask.reshape(-1, LANE)
    weights = (w_in, w_conv, w_out)
    rows_of = [w.shape[0] for w in weights]

    tile_a, tile = 256, 512
    steps = rows // tile
    params_spec = whole(2, D + 2 * INNER)
    dma = pltpu.SemaphoreType.DMA

    out_sides = (w_out[:, : D // 2], w_out[:, D // 2 :])
    conv_out = jnp.concatenate([w_conv, *out_sides], axis=0).astype(BF16)
    hidden_a, slope_a, xhat_a, rstd_a = call(
        norm_a_kernel,
        (rows // tile_a,),
        [rows_spec(tile_a, D), params_spec],
        [rows_spec(tile_a, D)] * 3 + [rows_spec(tile_a, 1)],
        [shape((rows, D), BF16)] * 3 + [shape((rows, 1), F32)],
        us=17,
    )(tokens, tie(norm_params, conv_out))

    in_pieces = gather_pieces(w_in.astype(BF16), place, hidden_a)

    def in_call(tiles, count, before):
        at, stride = tiles

        def here_spec(width):
            return pl.BlockSpec((tile, width), lambda i: (at + stride * i, 0))

        out_shapes = [shape((rows, INNER), BF16)] * 3 + [shape((rows, 1), F32), shape((rows, 8), F32)]
        out_specs = [here_spec(INNER)] * 3 + [here_spec(1), here_spec(8)]
        if at == 0:
            out_shapes += [shape((REACH, INNER), BF16)] * 2
            out_specs += [whole(REACH, INNER)] * 2
        return call(
            functools.partial(in_kernel, pieces, tiles),
            (count,),
            [SMEM, whole(docs), here_spec(D), whole(*live.shape), params_spec]
            + [ANY] * (pieces + len(before)),
            out_specs,
            out_shapes,
            [pltpu.VMEM((D, INNER), BF16), pltpu.VMEM((tile, INNER), F32)]
            + [pltpu.VMEM((8, docs + -docs % LANE), F32), dma((pieces,))],
            us=3,
            aliases={5 + pieces + k: k for k in range(len(before))},
        )(spots, doc_lengths, hidden_a, live, norm_params, *in_pieces, *before)

    *kept, m_first, m_last = in_call((0, steps - 1), 2, ())
    moved, slope_b, xhat_b, rstd_b, masks = in_call((1, 1), steps - 2, kept)

    def halo(inner, outer):
        total = place.seq * place.fsdp
        across = [(i, i + 1 if i % 2 else i - 1) for i in range(1, total - 1)]
        return place.flip(inner, "fsdp", 1), lax.ppermute(outer, AXES, across)

    m_inner, m_outer = halo(m_first, m_last)
    conv_pieces = gather_pieces(conv_out, place, m_first, (moved, m_inner, m_outer))

    ext = pltpu.VMEM((rows + 2 * REACH, INNER), BF16)
    taps_wide = KERNEL_TAPS * INNER
    wide = pltpu.VMEM((taps_wide, INNER), BF16)
    shards = place.fsdp // 2

    def half_dims(chunk):
        count = spans(chunk, rows_of)[1]
        return (shards, count + -count % place.seq, SUB, LANE)

    def tile_spec(width, ahead):
        return pl.BlockSpec((tile, width), lambda i: (jnp.clip(i + ahead, 0, steps - 1), 0))

    halves = [half_dims(CHUNKS[0])] * 2 + [half_dims(CHUNKS[1])] * 2
    work = pltpu.VMEM((tile, INNER), F32)
    turned_tile = pltpu.VMEM((INNER, tile), BF16)
    hidden_c, d_conv, d_first, d_last, sums_c, turned, keep1, send1, keep2, send2 = call(
        functools.partial(conv_kernel, pieces, rows_of),
        (steps + 1,),
        [SMEM, ANY, ANY, ANY, tile_spec(8, 0), tile_spec(D, 0), tile_spec(D, -1), params_spec]
        + [ANY] * pieces,
        [tile_spec(INNER, 0)] * 2
        + [whole(REACH, INNER), whole(REACH, INNER), whole(2, INNER)]
        + [ANY] * 5,
        [
            shape((rows, INNER), BF16),
            shape((rows, INNER), BF16),
            shape((REACH, INNER), BF16),
            shape((REACH, INNER), BF16),
            shape((2, INNER), F32),
            shape((taps_wide, INNER), BF16),
        ]
        + [shape(dims, BF16) for dims in halves],
        [ext, wide, wide, pltpu.VMEM((INNER, D), BF16), pltpu.VMEM((D, INNER), BF16)]
        + [pltpu.VMEM((2, tile, taps_wide), BF16), work, work, work, turned_tile, turned_tile]
        + [pltpu.VMEM((INNER, taps_wide), F32), pltpu.VMEM((INNER, D), F32)]
        + [pltpu.VMEM((16, INNER), F32)]
        + [pltpu.VMEM((2,) + halves[0], BF16), pltpu.VMEM((2,) + halves[2], BF16)]
        + [dma((3 + 3 * pieces,))],
        us=45,
    )(
        spots, m_inner, moved, m_outer, masks, cotangent, cotangent, norm_params, *conv_pieces
    )
    d_inner, d_outer = halo(d_first, d_last)
    first, second = Reduction(place, keep1, send1), Reduction(place, keep2, send2)
    (block_out,) = call(
        functools.partial(out_kernel, pieces),
        (steps,),
        [SMEM, rows_spec(tile, INNER), rows_spec(tile, D)] + [ANY] * pieces,
        [rows_spec(tile, D)],
        [shape((rows, D), BF16)],
        [pltpu.VMEM((INNER, D), BF16), dma((2 * pieces,))],
        us=9,
    )(spots, hidden_c, tokens, *conv_pieces)

    def back_conv(last, spots, before):
        here = steps // 2
        at = here * last

        def here_spec(width):
            return pl.BlockSpec((tile, width), lambda i: (i + at, 0))

        dims = half_dims(CHUNKS[2])
        return call(
            functools.partial(back_conv_kernel, last, w_in.shape[0]),
            (here,),
            [SMEM] + [ANY] * 4
            + [here_spec(8), here_spec(INNER), here_spec(1), here_spec(INNER), here_spec(D)]
            + [params_spec]
            + [ANY] * last,
            [rows_spec(tile, INNER), whole(2, INNER)] + [ANY] * (1 + last),
            [shape((rows // 2, INNER), BF16), shape((2, INNER), F32)]
            + ([shape(dims, BF16)] * 2 if last else [shape((INNER, D), F32)]),
            ([pltpu.VMEM((2,) + dims, BF16)] if last else [])
            + [
                ext,
                wide,
                pltpu.VMEM((tile, taps_wide), BF16),
                pltpu.VMEM((tile, INNER), F32),
                pltpu.VMEM((INNER, D), F32),
                pltpu.VMEM((16, INNER), F32),
                dma((5,)),
            ],
            us=16,
        )(
            spots, d_inner, d_conv, d_outer, turned, masks, xhat_b, rstd_b, slope_b, hidden_a,
            norm_params, *before,
        )

    block_out, d_inner, d_outer = arrive((block_out, d_inner, d_outer), first, second)
    away = (first.x(), second.y())
    d_pre0, sums_b0, grad_part = back_conv(0, tie(spots, *away), ())
    d_pre0 = arrive(d_pre0, first, second)
    away = (first.y(), second.x())
    d_pre1, sums_b1, keep, send = back_conv(1, tie(spots, *away), (grad_part,))
    send = arrive(send, first, second)
    third = Reduction(place, keep, send)
    sent = jnp.concatenate([first.pieces(), second.pieces()], axis=1)
    got = exchange(place, sent)
    third.got = tie(third.got, sent)
    away = (sent, third.x())
    input_grad, sums_a = call(
        functools.partial(back_a_kernel, pieces, steps // 2),
        (steps,),
        [SMEM]
        + [
            pl.BlockSpec((tile, INNER), lambda i: (jnp.minimum(i, steps // 2 - 1), 0)),
            pl.BlockSpec((tile, INNER), lambda i: (jnp.maximum(i - steps // 2, 0), 0)),
        ]
        + [rows_spec(tile, D), rows_spec(tile, 1), rows_spec(tile, D), rows_spec(tile, D)]
        + [params_spec]
        + [ANY] * pieces,
        [rows_spec(tile, D), whole(2, D)],
        [shape((rows, D), F32), shape((2, D), F32)],
        [
            pltpu.VMEM((D, INNER), BF16),
            pltpu.VMEM((INNER, D), BF16),
            pltpu.VMEM((tile, D), F32),
            pltpu.VMEM((16, D), F32),
            dma((pieces,)),
        ],
        us=17,
    )(
        tie(spots, *away), d_pre0, d_pre1, xhat_a, rstd_a, slope_a, cotangent, norm_params, *in_pieces
    )

    row_states, col_states = (row_in, row_conv, row_out), (col_in, col_conv, col_out)
    row_specs = [whole(*r.shape) for r in row_states]
    col_specs = [whole(*c.shape) for c in col_states]
    cols_all = D + 2 * INNER
    pack_spec = whole(4, cols_all)
    fulls = [pltpu.VMEM(half_dims(c)[1:], BF16) for c in CHUNKS]
    sums = (sums_a, sums_b0, sums_b1, sums_c)
    got, third.got, input_grad = lax.optimization_barrier((got, third.got, input_grad))
    part = summed(got)
    sent = jnp.broadcast_to(part[None], (place.seq // 2,) + part.shape)
    mine = exchange(place, sent)
    third.got = tie(third.got, sent)
    away = third.y()
    (pack,) = call(
        functools.partial(pack_kernel, rows_of, [half_dims(c)[1] // place.seq for c in CHUNKS]),
        (1,),
        [SMEM, whole(*part.shape)] + row_specs + [whole(*x.shape) for x in sums],
        [pack_spec],
        [shape((4, cols_all), F32)],
        [pltpu.VMEM((cols_all // LANE + 1, SUB, LANE), F32)],
        us=2,
    )(tie(spots, away), part, *row_states, *sums)
    pack = sum_over(pack, place, "fsdp")
    seq_bits = bits_of(place.seq)
    mine, third.got, pack = lax.optimization_barrier((mine, third.got, pack))
    other = place.flip(mine, "seq", 1)
    for bit in seq_bits[1:]:
        third.seq_bit(bit)
    line = third.piece()[None]
    for bit in seq_bits[:0:-1]:
        line = jnp.concatenate([line, place.flip(line, "seq", bit)], axis=0)
    for bit in seq_bits[1:] + seq_bits[:1]:
        pack = pack + place.flip(pack, "seq", bit)
    line, other, pack = lax.optimization_barrier((line, other, pack))
    line_other = place.flip(line, "seq", 1)
    list_bits = [1] + seq_bits[1:]

    def update_scratch(weights):
        lines = max(w.shape[0] + -w.shape[0] % LANE for w in weights)
        return [pltpu.VMEM((8, lines), F32)] + [pltpu.VMEM((lines, LANE), F32)] * 2

    weight_specs = [whole(*w.shape) for w in weights]
    (pack_in,) = call(
        functools.partial(pack_in_kernel, rows_of, list_bits),
        (1,),
        [SMEM, ANY, ANY],
        [whole(8, INNER)],
        [shape((8, INNER), F32)],
        [fulls[2], dma((place.seq,))],
        us=2,
    )(spots, line, line_other)
    pack_in = sum_over(pack_in, place, "fsdp")
    results = call(
        functools.partial(update_kernel, rows_of, place.seq),
        (1,),
        [SMEM, ANY, ANY, pack_spec] + weight_specs[1:] + row_specs[1:] + col_specs[1:],
        weight_specs[1:] * 2 + row_specs[1:] + col_specs[1:],
        [shape(w.shape, F32) for w in weights[1:]] * 2
        + [shape(r.shape, F32) for r in row_states[1:] + col_states[1:]],
        update_scratch(weights[1:]) + fulls[:2] + [dma((2 * place.seq,))],
        us=8,
    )(spots, mine, other, pack, *weights[1:], *row_states[1:], *col_states[1:])
    grad_conv, grad_out, new_conv, new_out, row_conv_new, row_out_new, col_conv_new, col_out_new = (
        results
    )
    grad_in, new_in, row_in_new, col_in_new, *norm_results = call(
        functools.partial(update_in_kernel, rows_of, place.seq, list_bits),
        (1,),
        [SMEM, ANY, ANY, whole(8, INNER), pack_spec, params_spec, params_spec]
        + [weight_specs[0], row_specs[0], col_specs[0]],
        [weight_specs[0]] * 2 + [row_specs[0], col_specs[0]] + [params_spec] * 3,
        [shape(w_in.shape, F32)] * 2
        + [shape(row_in.shape, F32), shape(col_in.shape, F32)]
        + [shape((2, cols_all), F32)] * 3,
        update_scratch(weights[:1]) + [fulls[2], dma((place.seq,))],
        us=4,
    )(
        spots, line, line_other, pack_in, pack, norm_params, norm_second, w_in, row_in, col_in
    )
    return (
        block_out,
        input_grad,
        grad_in,
        grad_conv,
        grad_out,
        new_in,
        new_conv,
        new_out,
        row_in_new,
        col_in_new,
        row_conv_new,
        col_conv_new,
        row_out_new,
        col_out_new,
        *norm_results,
    )


def solution(mesh):
    both, rows = P(AXES, None), P("fsdp", None)
    in_specs = (
        both, P(AXES), P(), both, rows, rows, rows, P(),
        P("fsdp"), P(), P("fsdp"), P(), P("fsdp"), P(), P(),
    )
    out_specs = (
        both, both, rows, rows, rows, rows, rows, rows,
        P("fsdp"), P(), P("fsdp"), P(), P("fsdp"), P(), P(), P(), P(),
    )
    return jax.shard_map(
        on_device, mesh=mesh, in_specs=in_specs, out_specs=out_specs, check_vma=False
    )
```

```python
import functools
import math

import jax
import jax.numpy as jnp
from jax import lax
from jax.experimental import pallas as pl
from jax.experimental.pallas import tpu as pltpu
from jax.sharding import PartitionSpec as P

D = 1280
INNER = 640
KERNEL_TAPS = 5
DILATION_STEP = 128
STEP = 10
EPSILON = 1e-05
DECAY = 1.0 - STEP ** (-0.8)

REACH = (KERNEL_TAPS - 1) // 2 * DILATION_STEP
MID = (KERNEL_TAPS - 1) // 2
F32 = jnp.float32
BF16 = jnp.bfloat16
SUB, LANE = 16, 128
AXES = ("seq", "fsdp")
NT = (((1,), (1,)), ((), ()))
TN = (((0,), (0,)), ((), ()))
NN = (((1,), (0,)), ((), ()))


def call(kernel, grid, in_specs, out_specs, out_shape, scratch=(), us=1.0, aliases=None, mib=58):
    params = pltpu.CompilerParams(
        vmem_limit_bytes=mib * 1024 * 1024, dimension_semantics=("arbitrary",) * len(grid)
    )
    return pl.pallas_call(
        kernel,
        grid=grid,
        in_specs=in_specs,
        out_specs=out_specs,
        out_shape=out_shape,
        scratch_shapes=list(scratch),
        compiler_params=params,
        input_output_aliases=aliases or {},
        cost_estimate=pl.CostEstimate(
                flops=int(us * 1.1e9), bytes_accessed=int(us * 3.4e6), transcendentals=0
        ),
    )


def shape(dims, dtype):
    return jax.ShapeDtypeStruct(dims, dtype)


def rows_spec(tile, width):
    return pl.BlockSpec((tile, width), lambda i: (i, 0))


def whole(*dims):
    return pl.BlockSpec(dims, lambda *_: (0,) * len(dims))


ANY = pl.BlockSpec(memory_space=pl.ANY)
SMEM = pl.BlockSpec(memory_space=pltpu.SMEM)


ERFC_P = 0.47 / math.sqrt(2.0)
ERFC_C = (
    0.12357219400743558,
    0.1999878668208835,
    -0.08033356004356296,
    0.3660253986657854,
    -0.1092519747040215,
)
LOG2E = 1.4426950408889634


def gelu_and_slope(y):
    t = pltpu.reciprocal(1.0 + ERFC_P * jnp.abs(y), approx=True)
    bell = jnp.exp2(y * y * (-0.5 * LOG2E))
    poly = ERFC_C[4] * t + ERFC_C[3]
    for c in ERFC_C[2::-1]:
        poly = poly * t + c
    tail = poly * t * bell
    cdf = jnp.where(y > 0.0, 1.0 - tail, tail)
    return y * cdf, cdf + y * (bell * (1.0 / math.sqrt(2.0 * math.pi)))


def lane_blocks(width):
    return [slice(k, k + LANE) for k in range(0, width, LANE)]


def row_stats(ref, rows):
    width = ref.shape[-1]
    blocks = lane_blocks(width)
    total = ref[rows, blocks[0]].astype(F32)
    for b in blocks[1:]:
        total = total + ref[rows, b].astype(F32)
    mean = jnp.sum(total, axis=-1, keepdims=True) * (1.0 / width)
    square = None
    for b in blocks:
        centered = ref[rows, b].astype(F32) - mean
        square = centered * centered if square is None else square + centered * centered
    variance = jnp.sum(square, axis=-1, keepdims=True) * (1.0 / width)
    return mean, lax.rsqrt(variance + EPSILON)


def fold(values):
    total = values[0:8]
    for k in range(8, values.shape[0], 8):
        total = total + values[k : k + 8]
    return total


def in_stages(count, stages, between=()):
    chunks = [slice(k, k + CHUNK) for k in range(0, count, CHUNK)]
    kept, rounds = {}, len(chunks) + len(stages) - 1
    for t in range(rounds):
        for n, stage in enumerate(stages):
            if 0 <= t - n < len(chunks):
                kept[n, t - n] = stage(chunks[t - n], kept.get((n - 1, t - n)))
        for work in between[t * len(between) // rounds : (t + 1) * len(between) // rounds]:
            work()


def halves_of(count):
    return (slice(0, count // 2), slice(count // 2, count))


def row_means(sums, width):
    return [jnp.sum(x, axis=-1, keepdims=True) * (1.0 / width) for x in sums]


def norm_back(rows, dxhat_ref, xhat_ref, means, put):
    mean_d, mean_dx, rstd = means
    for b in lane_blocks(dxhat_ref.shape[-1]):
        xhat = xhat_ref[rows, b].astype(F32)
        put(b, (dxhat_ref[rows, b] - mean_d - xhat * mean_dx) * rstd)


def add_terms(acc_ref, b, dy, xhat):
    acc_ref[0:8, b] += fold(dy * xhat)
    acc_ref[8:16, b] += fold(dy)


def open_sums(acc_ref):
    @pl.when(pl.program_id(0) == 0)
    def _():
        acc_ref[...] = jnp.zeros_like(acc_ref)


def close_sums(out_ref, acc_ref):
    @pl.when(pl.program_id(0) == pl.num_programs(0) - 1)
    def _():
        out_ref[0:1, :] = jnp.sum(acc_ref[0:8, :], axis=0, keepdims=True)
        out_ref[1:2, :] = jnp.sum(acc_ref[8:16, :], axis=0, keepdims=True)


def run_copies(copies):
    for copy in copies:
        copy.start()
    for copy in copies:
        copy.wait()


def piece_copies(pieces, full_ref, me, sem, first=0):
    each = full_ref.shape[0] // len(pieces)
    return [
        pltpu.make_async_copy(
            piece.at[0:each, :],
            full_ref.at[pl.ds(pl.multiple_of((me ^ k) * each, SUB), each), :],
            sem.at[first + k],
        )
        for k, piece in enumerate(pieces)
    ]


def out_copies(pieces, full_ref, me, sem, first=0):
    each, width = full_ref.shape[0] // len(pieces), full_ref.shape[1] // 2
    copies = []
    for k, piece in enumerate(pieces):
        rows = pl.ds(pl.multiple_of((me ^ k) * each, SUB), each)
        for side in range(2):
            at = piece.shape[0] - (2 - side) * each
            copies.append(
                pltpu.make_async_copy(
                    piece.at[at : at + each, :],
                    full_ref.at[rows, side * width : (side + 1) * width],
                    sem.at[first + 2 * k + side],
                )
            )
    return copies


def column(row):
    return jnp.transpose(jnp.broadcast_to(row, (LANE, LANE)))


CHUNK = 64
UPDATE_STEPS = 5


def norm_a_kernel(tok_ref, np_ref, hid_ref, slope_ref, xhat_ref, rstd_ref):
    def stats(rows, _):
        mean, rstd = row_stats(tok_ref, rows)
        rstd_ref[rows, :] = rstd
        return mean, rstd

    def work(rows, kept):
        mean, rstd = kept
        for b in lane_blocks(D):
            xhat = (tok_ref[rows, b].astype(F32) - mean) * rstd
            hidden, slope = gelu_and_slope(xhat * np_ref[0:1, b] + np_ref[1:2, b])
            hid_ref[rows, b] = hidden.astype(BF16)
            slope_ref[rows, b] = slope.astype(BF16)
            xhat_ref[rows, b] = xhat.astype(BF16)

    in_stages(tok_ref.shape[0], [stats, work])


def running_ends(ends_ref, lengths_ref):
    docs, width = lengths_ref.shape[0], ends_ref.shape[1]
    ends_ref[...] = jnp.zeros_like(ends_ref)
    ends_ref[0:1, 0:docs] = lengths_ref[...].reshape(1, -1).astype(F32)
    before = jnp.zeros((1, 1), F32)
    row = lax.broadcasted_iota(jnp.int32, (LANE, LANE), 0)
    lane = lax.broadcasted_iota(jnp.int32, (LANE, LANE), 1)
    for k in range(0, width, LANE):
        line = ends_ref[0:1, k : k + LANE]
        sums = jnp.sum(jnp.where(row <= lane, column(line), 0.0), axis=0, keepdims=True) + before
        ends_ref[0:1, k : k + LANE] = jnp.where(lane[0:1] + k < docs, sums, 1e9)
        before = before + jnp.sum(line, axis=1, keepdims=True)


def in_kernel(pieces, tiles, place_ref, lengths_ref, hid_ref, live_ref, np_ref, *refs):
    piece_refs = refs[:pieces]
    edges = tiles[0] == 0
    outs = refs[-(11 if edges else 9) :]
    mov_ref, slope_ref, xhat_ref, rstd_ref, mask_ref = outs[:5]
    w_ref, pre_ref, ends_ref, sem = outs[-4:]
    step = pl.program_id(0)
    tile = hid_ref.shape[0]

    @pl.when(step == 0)
    def _():
        copies = piece_copies(piece_refs, w_ref, place_ref[0], sem)
        for copy in copies:
            copy.start()
        running_ends(ends_ref, lengths_ref)
        for copy in copies:
            copy.wait()

    for half in halves_of(tile):
        pre_ref[half, :] = lax.dot_general(
            hid_ref[half, :], w_ref[...], NN, preferred_element_type=F32
        )

    at_tile = tiles[0] + step * tiles[1]
    first = place_ref[1] + at_tile * tile
    ends = ends_ref[0:1, :]
    lanes = lax.broadcasted_iota(jnp.int32, (LANE, 8), 1)
    offsets = ((lanes - MID) * DILATION_STEP).astype(F32)
    for k in range(tile // LANE):
        at = (first + k * LANE + lax.broadcasted_iota(jnp.int32, (LANE, 1), 0)).astype(F32)
        begin = jnp.max(jnp.where(ends <= at, ends, 0.0), axis=1, keepdims=True)
        end = jnp.min(jnp.where(ends > at, ends, 1e9), axis=1, keepdims=True)
        there = at + offsets
        same = jnp.where((there >= begin) & (there < end), 1.0, 0.0)
        live = column(live_ref[pl.ds(at_tile * (tile // LANE) + k, 1), :].astype(F32))
        mask_ref[k * LANE : (k + 1) * LANE, :] = jnp.where(lanes == MID, live[:, 0:8], same)

    def stats(rows, _):
        mean, rstd = row_stats(pre_ref, rows)
        rstd_ref[rows, :] = rstd
        return mean, rstd

    def work(rows, kept):
        mean, rstd = kept
        live = mask_ref[rows, MID : MID + 1]
        for b in lane_blocks(INNER):
            gains = slice(D + b.start, D + b.stop)
            xhat = (pre_ref[rows, b] - mean) * rstd
            hidden, slope = gelu_and_slope(xhat * np_ref[0:1, gains] + np_ref[1:2, gains])
            mov_ref[rows, b] = (hidden * live).astype(BF16)
            slope_ref[rows, b] = slope.astype(BF16)
            xhat_ref[rows, b] = xhat.astype(BF16)

    in_stages(tile, [stats, work])
    if edges:
        put_edges(place_ref, outs[5], outs[6], mov_ref, step == 0, step == 1)


def load_window(place_ref, inner, mid, outer, ext_ref, sem):
    rows, core = mid.shape[0], lax.rem(place_ref[0], 2)
    near = pl.multiple_of((1 - core) * (REACH + rows), SUB)
    far = pl.multiple_of(core * (REACH + rows), SUB)
    return [
        pltpu.make_async_copy(inner, ext_ref.at[pl.ds(near, REACH), :], sem.at[0]),
        pltpu.make_async_copy(mid, ext_ref.at[REACH : REACH + rows, :], sem.at[1]),
        pltpu.make_async_copy(outer, ext_ref.at[pl.ds(far, REACH), :], sem.at[2]),
    ]


def put_edges(place_ref, inner_ref, outer_ref, tile_ref, at_first, at_last):
    rows, core = tile_ref.shape[0], lax.rem(place_ref[0], 2)
    for at, edge, first in ((at_first, slice(0, REACH), 0), (at_last, slice(rows - REACH, rows), 1)):

        @pl.when(at & (core == first))
        def _(edge=edge):
            outer_ref[...] = tile_ref[edge, :]

        @pl.when(at & (core != first))
        def _(edge=edge):
            inner_ref[...] = tile_ref[edge, :]


def fill_taps(taps_ref, ext_ref, mask_ref, start):
    tile = taps_ref.shape[0]
    for j in range(KERNEL_TAPS):
        rows = pl.ds(pl.multiple_of(start + j * DILATION_STEP, DILATION_STEP), tile)
        picked = ext_ref[rows, :]
        if j != MID:
            picked = picked * mask_ref[:, j : j + 1].astype(BF16)
        taps_ref[:, j * INNER : (j + 1) * INNER] = picked


def conv_kernel(
    pieces, rows_of, place_ref, low_ref, mov_ref, high_ref, mask_ref, cot_ref, before_ref, np_ref, *refs
):
    piece_refs = refs[:pieces]
    hid_ref, dconv_ref, inner_ref, outer_ref, sums_ref, turned_ref = refs[pieces : pieces + 6]
    outs = refs[pieces + 6 : pieces + 10]
    ext_ref, wc_ref, wct_ref, wo_ref, wt_ref, taps_ref, pre_ref, dh_ref, xhat_ref = refs[
        pieces + 10 : pieces + 19
    ]
    dt_ref, ht_ref, gc_ref, go_ref, acc_ref, stage1_ref, stage2_ref, sem = refs[pieces + 19 :]
    step, steps = pl.program_id(0), pl.num_programs(0) - 1
    tile = taps_ref.shape[1]
    slot = lax.rem(step, 2)

    @pl.when(step == 0)
    def _():
        me = place_ref[0]
        outs = out_copies(piece_refs, wo_ref, me, sem, 3)
        rest = load_window(place_ref, low_ref, mov_ref, high_ref, ext_ref, sem)
        rest += piece_copies(piece_refs, wc_ref, me, sem, 3 + 2 * pieces)
        for copy in outs + rest:
            copy.start()
        for ref in (acc_ref, gc_ref, go_ref, dt_ref, ht_ref):
            ref[...] = jnp.zeros_like(ref)
        taps_ref[1] = jnp.zeros_like(taps_ref[1])
        for copy in outs:
            copy.wait()
        for k in range(0, D, 256):
            wt_ref[k : k + 256, :] = jnp.transpose(wo_ref[:, k : k + 256])
        for copy in rest:
            copy.wait()

    def grad_conv(cols):
        def work():
            gc_ref[:, cols] += lax.dot_general(
                dt_ref[...], taps_ref[1 - slot, :, cols], NN, preferred_element_type=F32
            )

        return work

    def grad_out(cols):
        def work():
            go_ref[:, cols] += lax.dot_general(
                ht_ref[...], before_ref[:, cols], NN, preferred_element_type=F32
            )

        return work

    taps_wide = KERNEL_TAPS * INNER
    products = [grad_conv(slice(k, min(k + 768, taps_wide))) for k in range(0, taps_wide, 768)]
    products += [grad_out(slice(k, min(k + 768, D))) for k in range(0, D, 768)]

    @pl.when(step < steps)
    def _():
        fill_taps(taps_ref.at[slot], ext_ref, mask_ref, step * tile)
        pre_ref[...] = lax.dot_general(
            taps_ref[slot], wc_ref[...], NN, preferred_element_type=F32
        )
        dh_ref[...] = lax.dot_general(cot_ref[...], wt_ref[...], NN, preferred_element_type=F32)
        for n in range(2):
            tap = jnp.minimum(2 * step + n, KERNEL_TAPS - 1)
            source = wc_ref[pl.ds(pl.multiple_of(tap * INNER, SUB), INNER), :]
            target = pl.multiple_of((KERNEL_TAPS - 1 - tap) * INNER, SUB)
            wct_ref[pl.ds(target, INNER), :] = jnp.transpose(source)

        def stats(rows, _):
            return row_stats(pre_ref, rows)

        def work(rows, kept):
            mean, rstd = kept
            sums = [0.0, 0.0]
            for b in lane_blocks(INNER):
                gains = slice(D + INNER + b.start, D + INNER + b.stop)
                gain = np_ref[0:1, gains]
                xhat = (pre_ref[rows, b] - mean) * rstd
                hidden, slope = gelu_and_slope(xhat * gain + np_ref[1:2, gains])
                hid_ref[rows, b] = hidden.astype(BF16)
                dy = dh_ref[rows, b] * slope
                add_terms(acc_ref, b, dy, xhat)
                dxhat = dy * gain
                xhat_ref[rows, b] = xhat
                dh_ref[rows, b] = dxhat
                sums = [sums[0] + dxhat, sums[1] + dxhat * xhat]
            return row_means(sums, INNER) + [rstd]

        def finish(rows, means):
            def put(b, value):
                dconv_ref[rows, b] = value.astype(BF16)

            norm_back(rows, dh_ref, xhat_ref, means, put)

        in_stages(tile, [stats, work, finish], products)
        dt_ref[...] = jnp.transpose(dconv_ref[...])
        ht_ref[...] = jnp.transpose(hid_ref[...])

    put_edges(place_ref, inner_ref, outer_ref, dconv_ref, step == 0, step == steps - 1)

    @pl.when(step == steps)
    def _():
        copy = pltpu.make_async_copy(wct_ref, turned_ref, sem.at[4])
        copy.start()
        for work in products:
            work()
        core = lax.rem(place_ref[0], 2)
        _, rows_conv, rows_out = rows_of
        stage_turned(stage1_ref, core, gc_ref, rows_conv, 0, slice(0, CUT // LANE))
        first_tiles = rows_conv // SUB * (CUT // LANE)
        stage_plain(stage1_ref, core, go_ref, rows_out, first_tiles)
        copies = stage_copies(stage1_ref, outs[0], outs[1], spans(CHUNKS[0], rows_of)[1], sem, 0)
        for each in copies:
            each.start()
        stage_turned(stage2_ref, core, gc_ref, rows_conv, 0, slice(CUT // LANE, INNER // LANE))
        more = stage_copies(stage2_ref, outs[2], outs[3], spans(CHUNKS[1], rows_of)[1], sem, 2)
        for each in more:
            each.start()
        for each in copies + more + [copy]:
            each.wait()
        sums_ref[0:1, :] = jnp.sum(acc_ref[0:8, :], axis=0, keepdims=True)
        sums_ref[1:2, :] = jnp.sum(acc_ref[8:16, :], axis=0, keepdims=True)


def stage_tiles(stage_ref, core, first_row, rows_each, base, block0, blocks, value):
    for g in range(value.shape[0] // SUB):
        row = first_row + g * SUB
        owner, inside = row // rows_each, row % rows_each // SUB
        side = core ^ (owner % 2)
        for b in range(value.shape[1] // LANE):
            tile = value[g * SUB : (g + 1) * SUB, b * LANE : (b + 1) * LANE]
            at = base + inside * blocks + block0 + b
            stage_ref[side, owner // 2, at] = tile.astype(BF16)


def stage_plain(stage_ref, core, grad_ref, rows_each, base):
    blocks = grad_ref.shape[1] // LANE
    for row in range(0, grad_ref.shape[0], SUB):
        part = grad_ref[row : row + SUB, :]
        stage_tiles(stage_ref, core, row, rows_each, base, 0, blocks, part)


def stage_turned(stage_ref, core, turned_ref, rows_each, base, blocks):
    count = blocks.stop - blocks.start
    for row in range(0, turned_ref.shape[1], LANE):
        for b in range(count):
            at = (blocks.start + b) * LANE
            part = jnp.transpose(turned_ref[at : at + LANE, row : row + LANE].astype(BF16))
            stage_tiles(stage_ref, core, row, rows_each, base, b, count, part)


def stage_copies(stage_ref, keep_ref, send_ref, used, sem, first):
    count = stage_ref.shape[2]
    if used < count:
        dims = stage_ref.shape[:2] + (count - used, SUB, LANE)
        stage_ref[:, :, used:] = jnp.zeros(dims, BF16)
    return [
        pltpu.make_async_copy(stage_ref.at[n], ref, sem.at[first + n])
        for n, ref in enumerate((keep_ref, send_ref))
    ]


def back_conv_kernel(
    last, rows_in, place_ref, low_ref, d_ref, high_ref, turned_ref, mask_ref, xhat_ref, rstd_ref, slope_ref, hid_ref, np_ref, *refs
):
    if last:
        before_ref, dpre_ref, sums_ref, keep_ref, send_ref, stage_ref = refs[:6]
    else:
        dpre_ref, sums_ref, part_ref = refs[:3]
    ext_ref, wt_ref, taps_ref, dmov_ref, grad_ref, acc_ref, sem = refs[-7:]
    step, steps = pl.program_id(0), pl.num_programs(0)
    tile = taps_ref.shape[0]
    open_sums(acc_ref)

    @pl.when(step == 0)
    def _():
        copies = load_window(place_ref, low_ref, d_ref, high_ref, ext_ref, sem)
        copies.append(pltpu.make_async_copy(turned_ref, wt_ref, sem.at[3]))
        if last:
            copies.append(pltpu.make_async_copy(before_ref, grad_ref, sem.at[4]))
        for copy in copies:
            copy.start()
        if not last:
            grad_ref[...] = jnp.zeros_like(grad_ref)
        for copy in copies:
            copy.wait()

    fill_taps(taps_ref, ext_ref, mask_ref, (steps * last + step) * tile)
    for half in halves_of(tile):
        dmov_ref[half, :] = lax.dot_general(
            taps_ref[half, :], wt_ref[...], NN, preferred_element_type=F32
        )

    def work(rows, _):
        live = mask_ref[rows, MID : MID + 1]
        sums = [0.0, 0.0]
        for b in lane_blocks(INNER):
            xhat = xhat_ref[rows, b].astype(F32)
            dy = dmov_ref[rows, b] * live * slope_ref[rows, b].astype(F32)
            add_terms(acc_ref, b, dy, xhat)
            dxhat = dy * np_ref[0:1, D + b.start : D + b.stop]
            dmov_ref[rows, b] = dxhat
            sums = [sums[0] + dxhat, sums[1] + dxhat * xhat]
        return row_means(sums, INNER) + [rstd_ref[rows, :]]

    def finish(rows, means):
        def put(b, value):
            dpre_ref[rows, b] = value.astype(BF16)

        norm_back(rows, dmov_ref, xhat_ref, means, put)

    in_stages(tile, [work, finish])
    close_sums(sums_ref, acc_ref)
    grad_ref[...] += lax.dot_general(dpre_ref[...], hid_ref[...], TN, preferred_element_type=F32)

    @pl.when(step == steps - 1)
    def _():
        if last:
            all_blocks = slice(0, INNER // LANE)
            stage_turned(stage_ref, lax.rem(place_ref[0], 2), grad_ref, rows_in, 0, all_blocks)
            used = rows_in // SUB * (INNER // LANE)
            run_copies(stage_copies(stage_ref, keep_ref, send_ref, used, sem, 0))
        else:
            run_copies([pltpu.make_async_copy(grad_ref, part_ref, sem.at[0])])


def back_a_kernel(pieces, half, place_ref, dpre0_ref, dpre1_ref, xhat_ref, rstd_ref, slope_ref, cot_ref, np_ref, *refs):
    piece_refs = refs[:pieces]
    grad_ref, sums_ref, w_ref, wt_ref, dh_ref, acc_ref, sem = refs[-7:]
    open_sums(acc_ref)

    @pl.when(pl.program_id(0) == 0)
    def _():
        run_copies(piece_copies(piece_refs, w_ref, place_ref[0], sem))
        for k in range(0, D, 256):
            wt_ref[:, k : k + 256] = jnp.transpose(w_ref[k : k + 256, :])

    second = (jnp.zeros((1, 1), jnp.int32) + pl.program_id(0)) >= half
    d_pre = jnp.where(second, dpre1_ref[...], dpre0_ref[...])
    dh_ref[...] = lax.dot_general(d_pre, wt_ref[...], NN, preferred_element_type=F32)

    def work(rows, _):
        sums = [0.0, 0.0]
        for b in lane_blocks(D):
            xhat = xhat_ref[rows, b].astype(F32)
            dy = dh_ref[rows, b] * slope_ref[rows, b].astype(F32)
            add_terms(acc_ref, b, dy, xhat)
            dxhat = dy * np_ref[0:1, b]
            dh_ref[rows, b] = dxhat
            sums = [sums[0] + dxhat, sums[1] + dxhat * xhat]
        return row_means(sums, D) + [rstd_ref[rows, :]]

    def finish(rows, means):
        def put(b, value):
            grad_ref[rows, b] = cot_ref[rows, b].astype(F32) + value

        norm_back(rows, dh_ref, xhat_ref, means, put)

    in_stages(dpre0_ref.shape[0], [work, finish])
    close_sums(sums_ref, acc_ref)


def out_kernel(pieces, place_ref, hid_ref, tok_ref, *refs):
    piece_refs = refs[:pieces]
    out_ref, w_ref, sem = refs[pieces:]

    @pl.when(pl.program_id(0) == 0)
    def _():
        run_copies(out_copies(piece_refs, w_ref, place_ref[0], sem))

    branch = lax.dot_general(hid_ref[...], w_ref[...], NN, preferred_element_type=F32)
    out_ref[...] = (tok_ref[...].astype(F32) + branch).astype(BF16)


WIDTHS = (INNER, INNER, D)
LANE0 = (0, INNER, 2 * INNER)
CUT = 2 * LANE
CHUNKS = (((1, 0, CUT), (2, 0, D)), ((1, CUT, INNER - CUT),), ((0, 0, INNER),))


def spans(chunk, rows):
    found, first = [], 0
    for weight, col, cols in chunk:
        tiles = rows[weight] // SUB * (cols // LANE)
        found.append((weight, col // LANE, cols // LANE, first, tiles))
        first += tiles
    return found, first


def column_sums(pack_ref, row, ref, chunk, rows):
    for weight, block0, blocks, first, tiles in spans(chunk, rows)[0]:

        def body(g, carry, first=first, blocks=blocks):
            new = []
            for b in range(blocks):
                value = ref[first + g * blocks + b].astype(F32)
                new.append(carry[b] + fold(value * value + 1e-30))
            return tuple(new)

        zero = tuple(jnp.zeros((8, LANE), F32) for _ in range(blocks))
        cols = lax.fori_loop(0, tiles // blocks, body, zero, unroll=5)
        for b in range(blocks):
            lane = LANE0[weight] + (block0 + b) * LANE
            pack_ref[row : row + 1, lane : lane + LANE] = jnp.sum(cols[b], axis=0, keepdims=True)


def load_full(refs, place_ref, first, full_ref, sem, at):
    pieces = refs[0].shape[0]
    each = full_ref.shape[0] // (len(refs) * pieces)
    outer = pieces if len(refs) == 2 else pieces // 2
    y = place_ref[2] % 2
    copies = []
    for n, (ref, side) in enumerate(zip(refs, (y, 1 - y))):
        for p in range(pieces):
            index = side * outer + p if len(refs) == 2 else p % 2 * outer + p // 2
            target = full_ref.at[pl.ds(index * each, each)]
            source = ref.at[p, first : first + each]
            copies.append(pltpu.make_async_copy(source, target, sem.at[at + n * pieces + p]))
    return copies


def load_list(bits, mine_ref, other_ref, place_ref, full_ref, sem):
    me, copies = place_ref[2], []
    each = full_ref.shape[0] // (1 << len(bits))
    inner = mine_ref.shape[0]
    for n in range(2 * inner):
        ref, at, k = (mine_ref, other_ref)[n // inner], n % inner, 0
        for i, bit in enumerate(bits):
            if n >> (len(bits) - 1 - i) & 1:
                k |= bit
        device, index = me ^ k, 0
        for bit in sorted(bits):
            index = index * 2 + lax.rem(lax.div(device, bit), 2)
        target = full_ref.at[pl.ds(index * each, each)]
        copies.append(pltpu.make_async_copy(ref.at[at], target, sem.at[n]))
    return copies


def pack_kernel(rows, pieces, place_ref, part_ref, *refs):
    states, sums, (pack_ref, acc_ref) = refs[0:3], refs[3:7], refs[7:9]
    pack_ref[...] = jnp.zeros_like(pack_ref)
    lanes_of = ((0, D), (D, D + INNER), (D, D + INNER), (D + INNER, D + 2 * INNER))
    for part, (lane0, lane1) in zip(sums, lanes_of):
        pack_ref[0:2, lane0:lane1] += part[...]
    lanes = lax.broadcasted_iota(jnp.int32, (1, LANE), 1)
    for k in range(3):
        total = jnp.sum(states[k][...].reshape(1, -1), axis=1, keepdims=True)
        pack_ref[3:4, 0:LANE] += jnp.where(lanes == k, total, 0.0)
    acc_ref[...] = jnp.zeros_like(acc_ref)
    spare = acc_ref.shape[0] - 1
    outer = place_ref[3] // 2
    piece = place_ref[2] % 2 * outer + place_ref[2] // 2
    at = 0
    for chunk, each in zip(CHUNKS[:2], pieces):
        found, _ = spans(chunk, rows)
        start = piece * each

        def body(k, carry, found=found, start=start, at=at):
            n = start + k
            slot = spare
            for weight, block0, blocks, first, tiles in found:
                here = LANE0[weight] // LANE + block0 + lax.rem(jnp.maximum(n - first, 0), blocks)
                slot = jnp.where((n >= first) & (n < first + tiles), here, slot)
            value = part_ref[at + k].astype(F32)
            acc_ref[slot] += value * value + 1e-30
            return carry

        lax.fori_loop(0, each, body, 0, unroll=2)
        at += each
    for slot in range(spare):
        pack_ref[2:3, slot * LANE : (slot + 1) * LANE] = jnp.sum(acc_ref[slot], axis=0, keepdims=True)


def pack_in_kernel(rows, bits, place_ref, mine_ref, other_ref, pack_ref, full_ref, sem):
    run_copies(load_list(bits, mine_ref, other_ref, place_ref, full_ref, sem))
    pack_ref[...] = jnp.zeros_like(pack_ref)
    column_sums(pack_ref, 0, full_ref, CHUNKS[2], rows)


def update_weight(
    k, squares, states_sum, source, weight, state, col_state, grad_ref, new, row_new_ref, col_new_ref, scratch, step=0, steps=1
):
    line_ref, state_ref, new_ref, scaled_ref = scratch
    width, fan, rows_here = WIDTHS[k], (D, KERNEL_TAPS * INNER, INNER)[k], state.shape[0]
    whole_rows = rows_here + -rows_here % LANE
    groups = rows_here // SUB // steps
    rate = 0.5 / fan**0.5

    def before():
        col_new = DECAY * col_state[...].reshape(1, -1) + (1.0 - DECAY) * (squares * (1.0 / fan))
        col_new_ref[...] = col_new.reshape(-1)
        total = DECAY * states_sum
        total = total + (1.0 - DECAY) * (1.0 / width) * jnp.sum(squares, axis=1, keepdims=True)
        scaled_ref[0:1, 0:width] = col_new / (total * (1.0 / fan))
        line_ref[0:1, 0:rows_here] = state[...].reshape(1, -1)
        for c in range(0, whole_rows, LANE):
            state_ref[c : c + LANE, :] = column(line_ref[0:1, c : c + LANE])

    def after():
        for c in range(0, whole_rows, LANE):
            line_ref[0:1, c : c + LANE] = jnp.transpose(new_ref[c : c + LANE, :])[0:1, :]
        row_new_ref[...] = line_ref[0:1, 0:rows_here].reshape(-1)

    def body(g, carry):
        here = pl.ds(pl.multiple_of(g * SUB, SUB), SUB)
        at = step * groups + g
        rows = pl.ds(pl.multiple_of(at * SUB, SUB), SUB)
        square = 0.0
        for ref, block0, blocks, first in source:
            for b in range(blocks):
                value = ref[first + at * blocks + b].astype(F32)
                grad_ref[here, (block0 + b) * LANE : (block0 + b + 1) * LANE] = value
                square = square + (value * value + 1e-30)
        mean = jnp.sum(square, axis=1, keepdims=True) * (1.0 / width)
        row_new = DECAY * state_ref[rows, :] + (1.0 - DECAY) * mean
        new_ref[rows, :] = row_new
        for ref, block0, blocks, first in source:
            for b in range(blocks):
                lanes = slice((block0 + b) * LANE, (block0 + b + 1) * LANE)
                value = ref[first + at * blocks + b].astype(F32)
                change = value * lax.rsqrt(row_new * scaled_ref[0:1, lanes])
                new[here, lanes] = weight[here, lanes] - rate * change
        return carry

    if steps == 1:
        before()
        lax.fori_loop(0, groups, body, 0, unroll=5)
        after()
    else:
        pl.when(step == 0)(before)
        lax.fori_loop(0, groups, body, 0, unroll=5)
        pl.when(step == steps - 1)(after)


def sources_of(chunk, ref, rows):
    return {w: (ref, block0, blocks, first) for w, block0, blocks, first, _ in spans(chunk, rows)[0]}


def update_kernel(rows, copies_of, place_ref, mine_ref, other_ref, pack_ref, *refs):
    weights, states, col_states = refs[0:2], refs[2:4], refs[4:6]
    grads, news, rows_new, cols_new = refs[6:8], refs[8:10], refs[10:12], refs[12:14]
    conv_scratch, out_scratch = refs[14:18], refs[18:22]
    full1_ref, full2_ref, sem = refs[22:25]
    both = (mine_ref, other_ref)
    count = 2 * mine_ref.shape[0]
    step, steps = pl.program_id(0), pl.num_programs(0)

    @pl.when(step == 0)
    def _():
        copies = load_full(both, place_ref, 0, full1_ref, sem, 0)
        copies += load_full(both, place_ref, full1_ref.shape[0] // count, full2_ref, sem, count)
        run_copies(copies)

    from1 = sources_of(CHUNKS[0], full1_ref, rows)
    from2 = sources_of(CHUNKS[1], full2_ref, rows)

    def update(n, k, source, scratch, *steps):
        squares = pack_ref[2:3, LANE0[k] : LANE0[k] + WIDTHS[k]]
        update_weight(
            k, squares, pack_ref[3:4, k : k + 1] * (1.0 / copies_of), source, weights[n],
            states[n], col_states[n], grads[n], news[n], rows_new[n], cols_new[n], scratch, *steps,
        )

    update(0, 1, [from1[1], from2[1]], conv_scratch, step, UPDATE_STEPS)

    @pl.when(step == steps - 1)
    def _():
        update(1, 2, [from1[2]], out_scratch)


def update_in_kernel(
    rows, copies_of, bits, place_ref, mine_ref, other_ref, pack_in_ref, pack_ref, np_ref, second_ref, *refs
):
    weight, state, col_state, grad_ref, new_ref, row_new_ref, col_new_ref = refs[0:7]
    ngrad_ref, nsecond_ref, nnew_ref = refs[7:10]
    full_ref, sem = refs[14:16]
    copies = load_list(bits, mine_ref, other_ref, place_ref, full_ref, sem)
    for copy in copies:
        copy.start()
    grad = pack_ref[0:2, :]
    second = DECAY * second_ref[...] + (1.0 - DECAY) * (grad * grad + 1e-30)
    ngrad_ref[...] = grad
    nsecond_ref[...] = second
    nnew_ref[...] = np_ref[...] - 0.2 * grad * lax.rsqrt(second)
    for copy in copies:
        copy.wait()
    update_weight(
        0, pack_in_ref[0:1, :], pack_ref[3:4, 0:1] * (1.0 / copies_of),
        [sources_of(CHUNKS[2], full_ref, rows)[0]], weight, state, col_state, grad_ref, new_ref,
        row_new_ref, col_new_ref, refs[10:14],
    )


class Places:
    def __init__(self):
        self.seq, self.fsdp = lax.axis_size("seq"), lax.axis_size("fsdp")
        self.q = lax.axis_index("fsdp")
        self.s = lax.axis_index("seq")

    def flip(self, x, axis, bit):
        pairs = []
        for s in range(self.seq):
            for f in range(self.fsdp):
                s2, f2 = (s ^ bit, f) if axis == "seq" else (s, f ^ bit)
                pairs.append((s * self.fsdp + f, s2 * self.fsdp + f2))
        return lax.ppermute(x, AXES, pairs)


def bits_of(count):
    return [1 << k for k in range(count.bit_length() - 1)]


def tie(x, *others):
    return lax.optimization_barrier((x, *others))[0]


def gather_pieces(piece, place, after, later=()):
    found = {0: piece}
    for bit in reversed(bits_of(place.fsdp)):
        for k in list(found):
            moving = found[k]
            if bit == 1:
                moving = tie(moving, *((after,) if k == 0 or not later else later))
            found[k | bit] = place.flip(moving, "fsdp", bit)
    return [found[k] for k in range(place.fsdp)]


def sum_over(x, place, *axes):
    for axis in axes:
        for bit in bits_of(getattr(place, axis)):
            x = x + place.flip(x, axis, bit)
    return x


def pick(x, index, axis):
    return lax.dynamic_index_in_dim(x, index, axis=axis, keepdims=False)


class Reduction:
    def __init__(self, place, keep, send):
        self.place, self.near = place, keep
        self.got = place.flip(send, "fsdp", 1)

    def halve(self, axis, side, flip_axis, bit):
        dims = self.near.shape
        parts = dims[:axis] + (2, dims[axis] // 2) + dims[axis + 1 :]
        near, got = self.near.reshape(parts), self.got.reshape(parts)
        away = pick(near, 1 - side, axis).astype(F32) + pick(got, 1 - side, axis).astype(F32)
        self.near = pick(near, side, axis).astype(F32) + pick(got, side, axis).astype(F32)
        away = away.astype(BF16)
        self.got = self.place.flip(away, flip_axis, bit)
        return away

    def x(self):
        bit = self.place.fsdp // 2
        while bit > 1:
            away = self.halve(0, (self.place.q // bit) % 2, "fsdp", bit)
            bit //= 2
        return away

    def y(self):
        return self.halve(1, self.place.s % 2, "seq", 1)

    def seq_bit(self, bit):
        return self.halve(1, (self.place.s // bit) % 2, "seq", bit)

    def piece(self):
        total = (self.near + self.got.astype(F32)).astype(BF16)
        return total.reshape(total.shape[1:])

    def pieces(self):
        total = (self.near + self.got.astype(F32)).astype(BF16)
        return total.reshape((self.place.seq // 2, -1) + total.shape[2:])


def arrive(result, *reductions):
    result, *gots = lax.optimization_barrier((result, *[r.got for r in reductions]))
    for reduction, got in zip(reductions, gots):
        reduction.got = got
    return result


def summed_f32(got):
    return jnp.sum(got.astype(F32), axis=0)


def summed(got):
    return summed_f32(got).astype(BF16)


def exchange(place, sent):
    line = [[y + 2 * z for z in range(place.seq // 2)] for y in range(2)]
    return lax.all_to_all(sent, "seq", 0, 0, axis_index_groups=line)


def on_device(
    tokens, input_mask, doc_lengths, cotangent, w_in, w_conv, w_out, norm_params,
    row_in, col_in, row_conv, col_conv, row_out, col_out, norm_second,
):
    place = Places()
    rows = tokens.shape[0]
    pieces = place.fsdp
    spots = jnp.stack(
        [place.q, (place.s * place.fsdp + place.q) * rows, place.s, place.seq]
    ).astype(jnp.int32)
    docs = doc_lengths.shape[0]
    live = input_mask.reshape(-1, LANE)
    weights = (w_in, w_conv, w_out)
    rows_of = [w.shape[0] for w in weights]

    tile_a, tile = 256, 512
    steps = rows // tile
    params_spec = whole(2, D + 2 * INNER)
    dma = pltpu.SemaphoreType.DMA

    out_sides = (w_out[:, : D // 2], w_out[:, D // 2 :])
    conv_out = jnp.concatenate([w_conv, *out_sides], axis=0).astype(BF16)
    hidden_a, slope_a, xhat_a, rstd_a = call(
        norm_a_kernel,
        (rows // tile_a,),
        [rows_spec(tile_a, D), params_spec],
        [rows_spec(tile_a, D)] * 3 + [rows_spec(tile_a, 1)],
        [shape((rows, D), BF16)] * 3 + [shape((rows, 1), F32)],
        us=17,
    )(tokens, tie(norm_params, conv_out))

    in_pieces = gather_pieces(w_in.astype(BF16), place, hidden_a)

    def in_call(tiles, count, before):
        at, stride = tiles

        def here_spec(width):
            return pl.BlockSpec((tile, width), lambda i: (at + stride * i, 0))

        out_shapes = [shape((rows, INNER), BF16)] * 3 + [shape((rows, 1), F32), shape((rows, 8), F32)]
        out_specs = [here_spec(INNER)] * 3 + [here_spec(1), here_spec(8)]
        if at == 0:
            out_shapes += [shape((REACH, INNER), BF16)] * 2
            out_specs += [whole(REACH, INNER)] * 2
        return call(
            functools.partial(in_kernel, pieces, tiles),
            (count,),
            [SMEM, whole(docs), here_spec(D), whole(*live.shape), params_spec]
            + [ANY] * (pieces + len(before)),
            out_specs,
            out_shapes,
            [pltpu.VMEM((D, INNER), BF16), pltpu.VMEM((tile, INNER), F32)]
            + [pltpu.VMEM((8, docs + -docs % LANE), F32), dma((pieces,))],
            us=3,
            mib=24,
            aliases={5 + pieces + k: k for k in range(len(before))},
        )(spots, doc_lengths, hidden_a, live, norm_params, *in_pieces, *before)

    *kept, m_first, m_last = in_call((0, steps - 1), 2, ())
    moved, slope_b, xhat_b, rstd_b, masks = in_call((1, 1), steps - 2, kept)

    def halo(inner, outer):
        total = place.seq * place.fsdp
        across = [(i, i + 1 if i % 2 else i - 1) for i in range(1, total - 1)]
        return place.flip(inner, "fsdp", 1), lax.ppermute(outer, AXES, across)

    m_inner, m_outer = halo(m_first, m_last)
    conv_pieces = gather_pieces(conv_out, place, m_first, (moved, m_inner, m_outer))

    ext = pltpu.VMEM((rows + 2 * REACH, INNER), BF16)
    taps_wide = KERNEL_TAPS * INNER
    wide = pltpu.VMEM((taps_wide, INNER), BF16)
    shards = place.fsdp // 2

    def half_dims(chunk):
        count = spans(chunk, rows_of)[1]
        return (shards, count + -count % place.seq, SUB, LANE)

    def tile_spec(width, ahead):
        return pl.BlockSpec((tile, width), lambda i: (jnp.clip(i + ahead, 0, steps - 1), 0))

    halves = [half_dims(CHUNKS[0])] * 2 + [half_dims(CHUNKS[1])] * 2
    work = pltpu.VMEM((tile, INNER), F32)
    turned_tile = pltpu.VMEM((INNER, tile), BF16)
    hidden_c, d_conv, d_first, d_last, sums_c, turned, keep1, send1, keep2, send2 = call(
        functools.partial(conv_kernel, pieces, rows_of),
        (steps + 1,),
        [SMEM, ANY, ANY, ANY, tile_spec(8, 0), tile_spec(D, 0), tile_spec(D, -1), params_spec]
        + [ANY] * pieces,
        [tile_spec(INNER, 0)] * 2
        + [whole(REACH, INNER), whole(REACH, INNER), whole(2, INNER)]
        + [ANY] * 5,
        [
            shape((rows, INNER), BF16),
            shape((rows, INNER), BF16),
            shape((REACH, INNER), BF16),
            shape((REACH, INNER), BF16),
            shape((2, INNER), F32),
            shape((taps_wide, INNER), BF16),
        ]
        + [shape(dims, BF16) for dims in halves],
        [ext, wide, wide, pltpu.VMEM((INNER, D), BF16), pltpu.VMEM((D, INNER), BF16)]
        + [pltpu.VMEM((2, tile, taps_wide), BF16), work, work, work, turned_tile, turned_tile]
        + [pltpu.VMEM((INNER, taps_wide), F32), pltpu.VMEM((INNER, D), F32)]
        + [pltpu.VMEM((16, INNER), F32)]
        + [pltpu.VMEM((2,) + halves[0], BF16), pltpu.VMEM((2,) + halves[2], BF16)]
        + [dma((3 + 3 * pieces,))],
        us=45,
    )(
        spots, m_inner, moved, m_outer, masks, cotangent, cotangent, norm_params, *conv_pieces
    )
    d_inner, d_outer = halo(d_first, d_last)
    first, second = Reduction(place, keep1, send1), Reduction(place, keep2, send2)
    (block_out,) = call(
        functools.partial(out_kernel, pieces),
        (steps,),
        [SMEM, rows_spec(tile, INNER), rows_spec(tile, D)] + [ANY] * pieces,
        [rows_spec(tile, D)],
        [shape((rows, D), BF16)],
        [pltpu.VMEM((INNER, D), BF16), dma((2 * pieces,))],
        us=9,
        mib=24,
    )(spots, hidden_c, tokens, *conv_pieces)

    def back_conv(last, spots, before):
        here = steps // 2
        at = here * last

        def here_spec(width):
            return pl.BlockSpec((tile, width), lambda i: (i + at, 0))

        dims = half_dims(CHUNKS[2])
        return call(
            functools.partial(back_conv_kernel, last, w_in.shape[0]),
            (here,),
            [SMEM] + [ANY] * 4
            + [here_spec(8), here_spec(INNER), here_spec(1), here_spec(INNER), here_spec(D)]
            + [params_spec]
            + [ANY] * last,
            [rows_spec(tile, INNER), whole(2, INNER)] + [ANY] * (1 + last),
            [shape((rows // 2, INNER), BF16), shape((2, INNER), F32)]
            + ([shape(dims, BF16)] * 2 if last else [shape((INNER, D), F32)]),
            ([pltpu.VMEM((2,) + dims, BF16)] if last else [])
            + [
                ext,
                wide,
                pltpu.VMEM((tile, taps_wide), BF16),
                pltpu.VMEM((tile, INNER), F32),
                pltpu.VMEM((INNER, D), F32),
                pltpu.VMEM((16, INNER), F32),
                dma((5,)),
            ],
            us=16,
            mib=40,
        )(
            spots, d_inner, d_conv, d_outer, turned, masks, xhat_b, rstd_b, slope_b, hidden_a,
            norm_params, *before,
        )

    block_out, d_inner, d_outer = arrive((block_out, d_inner, d_outer), first, second)
    away = (first.x(), second.y())
    d_pre0, sums_b0, grad_part = back_conv(0, tie(spots, *away), ())
    d_pre0 = arrive(d_pre0, first, second)
    away = (first.y(), second.x())
    d_pre1, sums_b1, keep, send = back_conv(1, tie(spots, *away), (grad_part,))
    send = arrive(send, first, second)
    third = Reduction(place, keep, send)
    sent = jnp.concatenate([first.pieces(), second.pieces()], axis=1)
    got = exchange(place, sent)
    third.got = tie(third.got, sent)
    away = (sent, third.x())
    input_grad, sums_a = call(
        functools.partial(back_a_kernel, pieces, steps // 2),
        (steps,),
        [SMEM]
        + [
            pl.BlockSpec((tile, INNER), lambda i: (jnp.minimum(i, steps // 2 - 1), 0)),
            pl.BlockSpec((tile, INNER), lambda i: (jnp.maximum(i - steps // 2, 0), 0)),
        ]
        + [rows_spec(tile, D), rows_spec(tile, 1), rows_spec(tile, D), rows_spec(tile, D)]
        + [params_spec]
        + [ANY] * pieces,
        [rows_spec(tile, D), whole(2, D)],
        [shape((rows, D), F32), shape((2, D), F32)],
        [
            pltpu.VMEM((D, INNER), BF16),
            pltpu.VMEM((INNER, D), BF16),
            pltpu.VMEM((tile, D), F32),
            pltpu.VMEM((16, D), F32),
            dma((pieces,)),
        ],
        us=17,
        mib=36,
    )(
        tie(spots, *away), d_pre0, d_pre1, xhat_a, rstd_a, slope_a, cotangent, norm_params, *in_pieces
    )

    row_states, col_states = (row_in, row_conv, row_out), (col_in, col_conv, col_out)
    row_specs = [whole(*r.shape) for r in row_states]
    col_specs = [whole(*c.shape) for c in col_states]
    cols_all = D + 2 * INNER
    pack_spec = whole(4, cols_all)
    fulls = [pltpu.VMEM(half_dims(c)[1:], BF16) for c in CHUNKS]
    sums = (sums_a, sums_b0, sums_b1, sums_c)
    got, third.got, input_grad = lax.optimization_barrier((got, third.got, input_grad))
    part = summed(got)
    sent = jnp.broadcast_to(part[None], (place.seq // 2,) + part.shape)
    mine = exchange(place, sent)
    third.got = tie(third.got, sent)
    away = third.y()
    (pack,) = call(
        functools.partial(pack_kernel, rows_of, [half_dims(c)[1] // place.seq for c in CHUNKS]),
        (1,),
        [SMEM, whole(*part.shape)] + row_specs + [whole(*x.shape) for x in sums],
        [pack_spec],
        [shape((4, cols_all), F32)],
        [pltpu.VMEM((cols_all // LANE + 1, SUB, LANE), F32)],
        us=2,
        mib=16,
    )(tie(spots, away), part, *row_states, *sums)
    pack = sum_over(pack, place, "fsdp")
    seq_bits = bits_of(place.seq)
    mine, third.got, pack = lax.optimization_barrier((mine, third.got, pack))
    other = place.flip(mine, "seq", 1)
    for bit in seq_bits[1:]:
        third.seq_bit(bit)
    line = third.piece()[None]
    for bit in seq_bits[:0:-1]:
        line = jnp.concatenate([line, place.flip(line, "seq", bit)], axis=0)
    for bit in seq_bits[1:] + seq_bits[:1]:
        pack = pack + place.flip(pack, "seq", bit)
    line, other, pack = lax.optimization_barrier((line, other, pack))
    line_other = place.flip(line, "seq", 1)
    list_bits = [1] + seq_bits[1:]

    def update_scratch(weight):
        lines = weight.shape[0] + -weight.shape[0] % LANE
        return (
            [pltpu.VMEM((8, lines), F32)]
            + [pltpu.VMEM((lines, LANE), F32)] * 2
            + [pltpu.VMEM((8, weight.shape[1]), F32)]
        )

    weight_specs = [whole(*w.shape) for w in weights]
    conv_block = pl.BlockSpec((w_conv.shape[0] // UPDATE_STEPS, INNER), lambda i: (i, 0))
    both_specs = [conv_block, weight_specs[2]]
    results = call(
        functools.partial(update_kernel, rows_of, place.seq),
        (UPDATE_STEPS,),
        [SMEM, ANY, ANY, pack_spec] + both_specs + row_specs[1:] + col_specs[1:],
        both_specs * 2 + row_specs[1:] + col_specs[1:],
        [shape(w.shape, F32) for w in weights[1:]] * 2
        + [shape(r.shape, F32) for r in row_states[1:] + col_states[1:]],
        update_scratch(w_conv)
        + update_scratch(w_out)
        + fulls[:2]
        + [dma((2 * place.seq,))],
        us=8,
        mib=32,
    )(spots, mine, other, pack, *weights[1:], *row_states[1:], *col_states[1:])
    grad_conv, grad_out, new_conv, new_out, row_conv_new, row_out_new, col_conv_new, col_out_new = (
        results
    )
    line_other, grad_out = lax.optimization_barrier((line_other, grad_out))
    (pack_in,) = call(
        functools.partial(pack_in_kernel, rows_of, list_bits),
        (1,),
        [SMEM, ANY, ANY],
        [whole(8, INNER)],
        [shape((8, INNER), F32)],
        [fulls[2], dma((place.seq,))],
        us=2,
        mib=16,
    )(spots, line, line_other)
    pack_in = sum_over(pack_in, place, "fsdp")
    grad_in, new_in, row_in_new, col_in_new, *norm_results = call(
        functools.partial(update_in_kernel, rows_of, place.seq, list_bits),
        (1,),
        [SMEM, ANY, ANY, whole(8, INNER), pack_spec, params_spec, params_spec]
        + [weight_specs[0], row_specs[0], col_specs[0]],
        [weight_specs[0]] * 2 + [row_specs[0], col_specs[0]] + [params_spec] * 3,
        [shape(w_in.shape, F32)] * 2
        + [shape(row_in.shape, F32), shape(col_in.shape, F32)]
        + [shape((2, cols_all), F32)] * 3,
        update_scratch(w_in) + [fulls[2], dma((place.seq,))],
        us=4,
        mib=24,
    )(
        spots, line, line_other, pack_in, pack, norm_params, norm_second, w_in, row_in, col_in
    )
    return (
        block_out,
        input_grad,
        grad_in,
        grad_conv,
        grad_out,
        new_in,
        new_conv,
        new_out,
        row_in_new,
        col_in_new,
        row_conv_new,
        col_conv_new,
        row_out_new,
        col_out_new,
        *norm_results,
    )


def solution(mesh):
    both, rows = P(AXES, None), P("fsdp", None)
    in_specs = (
        both, P(AXES), P(), both, rows, rows, rows, P(),
        P("fsdp"), P(), P("fsdp"), P(), P("fsdp"), P(), P(),
    )
    out_specs = (
        both, both, rows, rows, rows, rows, rows, rows,
        P("fsdp"), P(), P("fsdp"), P(), P("fsdp"), P(), P(), P(), P(),
    )
    return jax.shard_map(
        on_device, mesh=mesh, in_specs=in_specs, out_specs=out_specs, check_vma=False
    )
```

```python
import functools
import math

import jax
import jax.numpy as jnp
from jax import lax
from jax.experimental import pallas as pl
from jax.experimental.pallas import tpu as pltpu
from jax.sharding import PartitionSpec as P

D = 1280
INNER = 640
KERNEL_TAPS = 5
DILATION_STEP = 128
STEP = 10
EPSILON = 1e-05
DECAY = 1.0 - STEP ** (-0.8)

REACH = (KERNEL_TAPS - 1) // 2 * DILATION_STEP
MID = (KERNEL_TAPS - 1) // 2
F32 = jnp.float32
BF16 = jnp.bfloat16
SUB, LANE = 16, 128
AXES = ("seq", "fsdp")
NT = (((1,), (1,)), ((), ()))
TN = (((0,), (0,)), ((), ()))
NN = (((1,), (0,)), ((), ()))


def call(kernel, grid, in_specs, out_specs, out_shape, scratch=(), us=1.0, aliases=None, mib=58):
    params = pltpu.CompilerParams(
        vmem_limit_bytes=mib * 1024 * 1024, dimension_semantics=("arbitrary",) * len(grid)
    )
    return pl.pallas_call(
        kernel,
        grid=grid,
        in_specs=in_specs,
        out_specs=out_specs,
        out_shape=out_shape,
        scratch_shapes=list(scratch),
        compiler_params=params,
        input_output_aliases=aliases or {},
        cost_estimate=pl.CostEstimate(
                flops=int(us * 1.1e9), bytes_accessed=int(us * 3.4e6), transcendentals=0
        ),
    )


def shape(dims, dtype):
    return jax.ShapeDtypeStruct(dims, dtype)


def rows_spec(tile, width):
    return pl.BlockSpec((tile, width), lambda i: (i, 0))


def whole(*dims):
    return pl.BlockSpec(dims, lambda *_: (0,) * len(dims))


ANY = pl.BlockSpec(memory_space=pl.ANY)
SMEM = pl.BlockSpec(memory_space=pltpu.SMEM)


ERFC_P = 0.47 / math.sqrt(2.0)
ERFC_C = (
    0.12357219400743558,
    0.1999878668208835,
    -0.08033356004356296,
    0.3660253986657854,
    -0.1092519747040215,
)
LOG2E = 1.4426950408889634


def gelu_and_slope(y):
    t = pltpu.reciprocal(1.0 + ERFC_P * jnp.abs(y), approx=True)
    bell = jnp.exp2(y * y * (-0.5 * LOG2E))
    poly = ERFC_C[4] * t + ERFC_C[3]
    for c in ERFC_C[2::-1]:
        poly = poly * t + c
    tail = poly * t * bell
    cdf = jnp.where(y > 0.0, 1.0 - tail, tail)
    return y * cdf, cdf + y * (bell * (1.0 / math.sqrt(2.0 * math.pi)))


def lane_blocks(width):
    return [slice(k, k + LANE) for k in range(0, width, LANE)]


def row_stats(ref, rows):
    width = ref.shape[-1]
    blocks = lane_blocks(width)
    total = ref[rows, blocks[0]].astype(F32)
    for b in blocks[1:]:
        total = total + ref[rows, b].astype(F32)
    mean = jnp.sum(total, axis=-1, keepdims=True) * (1.0 / width)
    square = None
    for b in blocks:
        centered = ref[rows, b].astype(F32) - mean
        square = centered * centered if square is None else square + centered * centered
    variance = jnp.sum(square, axis=-1, keepdims=True) * (1.0 / width)
    return mean, lax.rsqrt(variance + EPSILON)


def fold(values):
    total = values[0:8]
    for k in range(8, values.shape[0], 8):
        total = total + values[k : k + 8]
    return total


def in_stages(count, stages, between=()):
    chunks = [slice(k, k + CHUNK) for k in range(0, count, CHUNK)]
    kept, rounds = {}, len(chunks) + len(stages) - 1
    for t in range(rounds):
        for n, stage in enumerate(stages):
            if 0 <= t - n < len(chunks):
                kept[n, t - n] = stage(chunks[t - n], kept.get((n - 1, t - n)))
        for work in between[t * len(between) // rounds : (t + 1) * len(between) // rounds]:
            work()


def halves_of(count):
    return (slice(0, count // 2), slice(count // 2, count))


def row_means(sums, width):
    return [jnp.sum(x, axis=-1, keepdims=True) * (1.0 / width) for x in sums]


def norm_back(rows, dxhat_ref, xhat_ref, means, put):
    mean_d, mean_dx, rstd = means
    for b in lane_blocks(dxhat_ref.shape[-1]):
        xhat = xhat_ref[rows, b].astype(F32)
        put(b, (dxhat_ref[rows, b] - mean_d - xhat * mean_dx) * rstd)


def add_terms(acc_ref, b, dy, xhat):
    acc_ref[0:8, b] += fold(dy * xhat)
    acc_ref[8:16, b] += fold(dy)


def open_sums(acc_ref):
    @pl.when(pl.program_id(0) == 0)
    def _():
        acc_ref[...] = jnp.zeros_like(acc_ref)


def close_sums(out_ref, acc_ref):
    @pl.when(pl.program_id(0) == pl.num_programs(0) - 1)
    def _():
        out_ref[0:1, :] = jnp.sum(acc_ref[0:8, :], axis=0, keepdims=True)
        out_ref[1:2, :] = jnp.sum(acc_ref[8:16, :], axis=0, keepdims=True)


def run_copies(copies):
    for copy in copies:
        copy.start()
    for copy in copies:
        copy.wait()


def piece_copies(pieces, full_ref, me, sem, first=0):
    each = full_ref.shape[0] // len(pieces)
    return [
        pltpu.make_async_copy(
            piece.at[0:each, :],
            full_ref.at[pl.ds(pl.multiple_of((me ^ k) * each, SUB), each), :],
            sem.at[first + k],
        )
        for k, piece in enumerate(pieces)
    ]


def out_copies(pieces, full_ref, me, sem, first=0):
    each, width = full_ref.shape[0] // len(pieces), full_ref.shape[1] // 2
    copies = []
    for k, piece in enumerate(pieces):
        rows = pl.ds(pl.multiple_of((me ^ k) * each, SUB), each)
        for side in range(2):
            at = piece.shape[0] - (2 - side) * each
            copies.append(
                pltpu.make_async_copy(
                    piece.at[at : at + each, :],
                    full_ref.at[rows, side * width : (side + 1) * width],
                    sem.at[first + 2 * k + side],
                )
            )
    return copies


def column(row):
    return jnp.transpose(jnp.broadcast_to(row, (LANE, LANE)))


CHUNK = 64
UPDATE_STEPS = 5


def norm_a_kernel(tok_ref, np_ref, hid_ref, slope_ref, xhat_ref, rstd_ref):
    def stats(rows, _):
        mean, rstd = row_stats(tok_ref, rows)
        rstd_ref[rows, :] = jnp.broadcast_to(rstd, (CHUNK, LANE))
        return mean, rstd

    def work(rows, kept):
        mean, rstd = kept
        for b in lane_blocks(D):
            xhat = (tok_ref[rows, b].astype(F32) - mean) * rstd
            hidden, slope = gelu_and_slope(xhat * np_ref[0:1, b] + np_ref[1:2, b])
            hid_ref[rows, b] = hidden.astype(BF16)
            slope_ref[rows, b] = slope.astype(BF16)
            xhat_ref[rows, b] = xhat.astype(BF16)

    in_stages(tok_ref.shape[0], [stats, work])


def running_ends(ends_ref, lengths_ref):
    docs, width = lengths_ref.shape[0], ends_ref.shape[1]
    ends_ref[...] = jnp.zeros_like(ends_ref)
    ends_ref[0:1, 0:docs] = lengths_ref[...].reshape(1, -1).astype(F32)
    before = jnp.zeros((1, 1), F32)
    row = lax.broadcasted_iota(jnp.int32, (LANE, LANE), 0)
    lane = lax.broadcasted_iota(jnp.int32, (LANE, LANE), 1)
    for k in range(0, width, LANE):
        line = ends_ref[0:1, k : k + LANE]
        sums = jnp.sum(jnp.where(row <= lane, column(line), 0.0), axis=0, keepdims=True) + before
        ends_ref[0:1, k : k + LANE] = jnp.where(lane[0:1] + k < docs, sums, 1e9)
        before = before + jnp.sum(line, axis=1, keepdims=True)


def in_kernel(pieces, tiles, place_ref, lengths_ref, hid_ref, live_ref, np_ref, *refs):
    piece_refs = refs[:pieces]
    edges = tiles[0] == 0
    outs = refs[-(11 if edges else 9) :]
    mov_ref, slope_ref, xhat_ref, rstd_ref, mask_ref = outs[:5]
    w_ref, pre_ref, ends_ref, sem = outs[-4:]
    step = pl.program_id(0)
    tile = hid_ref.shape[0]

    @pl.when(step == 0)
    def _():
        copies = piece_copies(piece_refs, w_ref, place_ref[0], sem)
        for copy in copies:
            copy.start()
        running_ends(ends_ref, lengths_ref)
        for copy in copies:
            copy.wait()

    for half in halves_of(tile):
        pre_ref[half, :] = lax.dot_general(
            hid_ref[half, :], w_ref[...], NN, preferred_element_type=F32
        )

    at_tile = tiles[0] + step * tiles[1]
    first = place_ref[1] + at_tile * tile
    ends = ends_ref[0:1, :]
    lanes = lax.broadcasted_iota(jnp.int32, (LANE, LANE), 1)
    offsets = ((lanes - MID) * DILATION_STEP).astype(F32)
    for k in range(tile // LANE):
        at = (first + k * LANE + lax.broadcasted_iota(jnp.int32, (LANE, 1), 0)).astype(F32)
        begin = jnp.max(jnp.where(ends <= at, ends, 0.0), axis=1, keepdims=True)
        end = jnp.min(jnp.where(ends > at, ends, 1e9), axis=1, keepdims=True)
        there = at + offsets
        same = jnp.where((there >= begin) & (there < end), 1.0, 0.0)
        live = column(live_ref[pl.ds(at_tile * (tile // LANE) + k, 1), :].astype(F32))
        mask_ref[k * LANE : (k + 1) * LANE, :] = jnp.where(lanes == MID, live, same)

    def stats(rows, _):
        mean, rstd = row_stats(pre_ref, rows)
        rstd_ref[rows, :] = jnp.broadcast_to(rstd, (CHUNK, LANE))
        return mean, rstd

    def work(rows, kept):
        mean, rstd = kept
        live = mask_ref[rows, MID : MID + 1]
        for b in lane_blocks(INNER):
            gains = slice(D + b.start, D + b.stop)
            xhat = (pre_ref[rows, b] - mean) * rstd
            hidden, slope = gelu_and_slope(xhat * np_ref[0:1, gains] + np_ref[1:2, gains])
            mov_ref[rows, b] = (hidden * live).astype(BF16)
            slope_ref[rows, b] = slope.astype(BF16)
            xhat_ref[rows, b] = xhat.astype(BF16)

    in_stages(tile, [stats, work])
    if edges:
        put_edges(place_ref, outs[5], outs[6], mov_ref, step == 0, step == 1)


def load_window(place_ref, inner, mid, outer, ext_ref, sem):
    rows, core = mid.shape[0], lax.rem(place_ref[0], 2)
    near = pl.multiple_of((1 - core) * (REACH + rows), SUB)
    far = pl.multiple_of(core * (REACH + rows), SUB)
    return [
        pltpu.make_async_copy(inner, ext_ref.at[pl.ds(near, REACH), :], sem.at[0]),
        pltpu.make_async_copy(mid, ext_ref.at[REACH : REACH + rows, :], sem.at[1]),
        pltpu.make_async_copy(outer, ext_ref.at[pl.ds(far, REACH), :], sem.at[2]),
    ]


def put_edges(place_ref, inner_ref, outer_ref, tile_ref, at_first, at_last):
    rows, core = tile_ref.shape[0], lax.rem(place_ref[0], 2)
    for at, edge, first in ((at_first, slice(0, REACH), 0), (at_last, slice(rows - REACH, rows), 1)):

        @pl.when(at & (core == first))
        def _(edge=edge):
            outer_ref[...] = tile_ref[edge, :]

        @pl.when(at & (core != first))
        def _(edge=edge):
            inner_ref[...] = tile_ref[edge, :]


def fill_taps(taps_ref, ext_ref, mask_ref, start):
    tile = taps_ref.shape[0]
    for j in range(KERNEL_TAPS):
        rows = pl.ds(pl.multiple_of(start + j * DILATION_STEP, DILATION_STEP), tile)
        picked = ext_ref[rows, :]
        if j != MID:
            picked = picked * mask_ref[:, j : j + 1].astype(BF16)
        taps_ref[:, j * INNER : (j + 1) * INNER] = picked


def conv_kernel(
    pieces, rows_of, place_ref, low_ref, mov_ref, high_ref, mask_ref, cot_ref, before_ref, np_ref, *refs
):
    piece_refs = refs[:pieces]
    hid_ref, dconv_ref, inner_ref, outer_ref, sums_ref, turned_ref = refs[pieces : pieces + 6]
    outs = refs[pieces + 6 : pieces + 10]
    ext_ref, wc_ref, wct_ref, wo_ref, wt_ref, taps_ref, pre_ref, dh_ref, xhat_ref = refs[
        pieces + 10 : pieces + 19
    ]
    dt_ref, ht_ref, gc_ref, go_ref, acc_ref, stage1_ref, stage2_ref, sem = refs[pieces + 19 :]
    step, steps = pl.program_id(0), pl.num_programs(0) - 1
    tile = taps_ref.shape[1]
    slot = lax.rem(step, 2)

    @pl.when(step == 0)
    def _():
        me = place_ref[0]
        outs = out_copies(piece_refs, wo_ref, me, sem, 3)
        rest = load_window(place_ref, low_ref, mov_ref, high_ref, ext_ref, sem)
        rest += piece_copies(piece_refs, wc_ref, me, sem, 3 + 2 * pieces)
        for copy in outs + rest:
            copy.start()
        for ref in (acc_ref, gc_ref, go_ref, dt_ref, ht_ref):
            ref[...] = jnp.zeros_like(ref)
        taps_ref[1] = jnp.zeros_like(taps_ref[1])
        for copy in outs:
            copy.wait()
        for k in range(0, D, 256):
            wt_ref[k : k + 256, :] = jnp.transpose(wo_ref[:, k : k + 256])
        for copy in rest:
            copy.wait()

    def grad_conv(cols):
        def work():
            gc_ref[:, cols] += lax.dot_general(
                dt_ref[...], taps_ref[1 - slot, :, cols], NN, preferred_element_type=F32
            )

        return work

    def grad_out(cols):
        def work():
            go_ref[:, cols] += lax.dot_general(
                ht_ref[...], before_ref[:, cols], NN, preferred_element_type=F32
            )

        return work

    taps_wide = KERNEL_TAPS * INNER
    products = [grad_conv(slice(k, min(k + 768, taps_wide))) for k in range(0, taps_wide, 768)]
    products += [grad_out(slice(k, min(k + 768, D))) for k in range(0, D, 768)]

    @pl.when(step < steps)
    def _():
        fill_taps(taps_ref.at[slot], ext_ref, mask_ref, step * tile)
        pre_ref[...] = lax.dot_general(
            taps_ref[slot], wc_ref[...], NN, preferred_element_type=F32
        )
        dh_ref[...] = lax.dot_general(cot_ref[...], wt_ref[...], NN, preferred_element_type=F32)
        for n in range(2):
            tap = jnp.minimum(2 * step + n, KERNEL_TAPS - 1)
            source = wc_ref[pl.ds(pl.multiple_of(tap * INNER, SUB), INNER), :]
            target = pl.multiple_of((KERNEL_TAPS - 1 - tap) * INNER, SUB)
            wct_ref[pl.ds(target, INNER), :] = jnp.transpose(source)

        def stats(rows, _):
            return row_stats(pre_ref, rows)

        def work(rows, kept):
            mean, rstd = kept
            sums = [0.0, 0.0]
            for b in lane_blocks(INNER):
                gains = slice(D + INNER + b.start, D + INNER + b.stop)
                gain = np_ref[0:1, gains]
                xhat = (pre_ref[rows, b] - mean) * rstd
                hidden, slope = gelu_and_slope(xhat * gain + np_ref[1:2, gains])
                hid_ref[rows, b] = hidden.astype(BF16)
                dy = dh_ref[rows, b] * slope
                add_terms(acc_ref, b, dy, xhat)
                dxhat = dy * gain
                xhat_ref[rows, b] = xhat
                dh_ref[rows, b] = dxhat
                sums = [sums[0] + dxhat, sums[1] + dxhat * xhat]
            return row_means(sums, INNER) + [rstd]

        def finish(rows, means):
            def put(b, value):
                dconv_ref[rows, b] = value.astype(BF16)

            norm_back(rows, dh_ref, xhat_ref, means, put)

        in_stages(tile, [stats, work, finish], products)
        dt_ref[...] = jnp.transpose(dconv_ref[...])
        ht_ref[...] = jnp.transpose(hid_ref[...])

    put_edges(place_ref, inner_ref, outer_ref, dconv_ref, step == 0, step == steps - 1)

    @pl.when(step == steps)
    def _():
        copy = pltpu.make_async_copy(wct_ref, turned_ref, sem.at[4])
        copy.start()
        for work in products:
            work()
        core = lax.rem(place_ref[0], 2)
        _, rows_conv, rows_out = rows_of
        stage_turned(stage1_ref, core, gc_ref, rows_conv, 0, slice(0, CUT // LANE))
        first_tiles = rows_conv // SUB * (CUT // LANE)
        stage_plain(stage1_ref, core, go_ref, rows_out, first_tiles)
        copies = stage_copies(stage1_ref, outs[0], outs[1], spans(CHUNKS[0], rows_of)[1], sem, 0)
        for each in copies:
            each.start()
        stage_turned(stage2_ref, core, gc_ref, rows_conv, 0, slice(CUT // LANE, INNER // LANE))
        more = stage_copies(stage2_ref, outs[2], outs[3], spans(CHUNKS[1], rows_of)[1], sem, 2)
        for each in more:
            each.start()
        for each in copies + more + [copy]:
            each.wait()
        sums_ref[0:1, :] = jnp.sum(acc_ref[0:8, :], axis=0, keepdims=True)
        sums_ref[1:2, :] = jnp.sum(acc_ref[8:16, :], axis=0, keepdims=True)


def stage_tiles(stage_ref, core, first_row, rows_each, base, block0, blocks, value):
    for g in range(value.shape[0] // SUB):
        row = first_row + g * SUB
        owner, inside = row // rows_each, row % rows_each // SUB
        side = core ^ (owner % 2)
        for b in range(value.shape[1] // LANE):
            tile = value[g * SUB : (g + 1) * SUB, b * LANE : (b + 1) * LANE]
            at = base + inside * blocks + block0 + b
            stage_ref[side, owner // 2, at] = tile.astype(BF16)


def stage_plain(stage_ref, core, grad_ref, rows_each, base):
    blocks = grad_ref.shape[1] // LANE
    for row in range(0, grad_ref.shape[0], SUB):
        part = grad_ref[row : row + SUB, :]
        stage_tiles(stage_ref, core, row, rows_each, base, 0, blocks, part)


def stage_turned(stage_ref, core, turned_ref, rows_each, base, blocks):
    count = blocks.stop - blocks.start
    for row in range(0, turned_ref.shape[1], LANE):
        for b in range(count):
            at = (blocks.start + b) * LANE
            part = jnp.transpose(turned_ref[at : at + LANE, row : row + LANE].astype(BF16))
            stage_tiles(stage_ref, core, row, rows_each, base, b, count, part)


def stage_copies(stage_ref, keep_ref, send_ref, used, sem, first):
    count = stage_ref.shape[2]
    if used < count:
        dims = stage_ref.shape[:2] + (count - used, SUB, LANE)
        stage_ref[:, :, used:] = jnp.zeros(dims, BF16)
    return [
        pltpu.make_async_copy(stage_ref.at[n], ref, sem.at[first + n])
        for n, ref in enumerate((keep_ref, send_ref))
    ]


def back_conv_kernel(
    last, rows_in, place_ref, low_ref, d_ref, high_ref, turned_ref, mask_ref, xhat_ref, rstd_ref, slope_ref, hid_ref, np_ref, *refs
):
    if last:
        before_ref, dpre_ref, sums_ref, keep_ref, send_ref, stage_ref = refs[:6]
    else:
        dpre_ref, sums_ref, part_ref = refs[:3]
    ext_ref, wt_ref, taps_ref, dmov_ref, grad_ref, acc_ref, sem = refs[-7:]
    step, steps = pl.program_id(0), pl.num_programs(0)
    tile = taps_ref.shape[0]
    open_sums(acc_ref)

    @pl.when(step == 0)
    def _():
        copies = load_window(place_ref, low_ref, d_ref, high_ref, ext_ref, sem)
        copies.append(pltpu.make_async_copy(turned_ref, wt_ref, sem.at[3]))
        if last:
            copies.append(pltpu.make_async_copy(before_ref, grad_ref, sem.at[4]))
        for copy in copies:
            copy.start()
        if not last:
            grad_ref[...] = jnp.zeros_like(grad_ref)
        for copy in copies:
            copy.wait()

    fill_taps(taps_ref, ext_ref, mask_ref, (steps * last + step) * tile)
    for half in halves_of(tile):
        dmov_ref[half, :] = lax.dot_general(
            taps_ref[half, :], wt_ref[...], NN, preferred_element_type=F32
        )

    def work(rows, _):
        live = mask_ref[rows, MID : MID + 1]
        sums = [0.0, 0.0]
        for b in lane_blocks(INNER):
            xhat = xhat_ref[rows, b].astype(F32)
            dy = dmov_ref[rows, b] * live * slope_ref[rows, b].astype(F32)
            add_terms(acc_ref, b, dy, xhat)
            dxhat = dy * np_ref[0:1, D + b.start : D + b.stop]
            dmov_ref[rows, b] = dxhat
            sums = [sums[0] + dxhat, sums[1] + dxhat * xhat]
        return row_means(sums, INNER) + [rstd_ref[rows, :]]

    def finish(rows, means):
        def put(b, value):
            dpre_ref[rows, b] = value.astype(BF16)

        norm_back(rows, dmov_ref, xhat_ref, means, put)

    in_stages(tile, [work, finish])
    close_sums(sums_ref, acc_ref)
    grad_ref[...] += lax.dot_general(dpre_ref[...], hid_ref[...], TN, preferred_element_type=F32)

    @pl.when(step == steps - 1)
    def _():
        if last:
            all_blocks = slice(0, INNER // LANE)
            stage_turned(stage_ref, lax.rem(place_ref[0], 2), grad_ref, rows_in, 0, all_blocks)
            used = rows_in // SUB * (INNER // LANE)
            run_copies(stage_copies(stage_ref, keep_ref, send_ref, used, sem, 0))
        else:
            run_copies([pltpu.make_async_copy(grad_ref, part_ref, sem.at[0])])


def back_a_kernel(pieces, half, place_ref, dpre0_ref, dpre1_ref, xhat_ref, rstd_ref, slope_ref, cot_ref, np_ref, *refs):
    piece_refs = refs[:pieces]
    grad_ref, sums_ref, w_ref, wt_ref, dh_ref, acc_ref, sem = refs[-7:]
    open_sums(acc_ref)

    @pl.when(pl.program_id(0) == 0)
    def _():
        run_copies(piece_copies(piece_refs, w_ref, place_ref[0], sem))
        for k in range(0, D, 256):
            wt_ref[:, k : k + 256] = jnp.transpose(w_ref[k : k + 256, :])

    second = (jnp.zeros((1, 1), jnp.int32) + pl.program_id(0)) >= half
    d_pre = jnp.where(second, dpre1_ref[...], dpre0_ref[...])
    dh_ref[...] = lax.dot_general(d_pre, wt_ref[...], NN, preferred_element_type=F32)

    def work(rows, _):
        sums = [0.0, 0.0]
        for b in lane_blocks(D):
            xhat = xhat_ref[rows, b].astype(F32)
            dy = dh_ref[rows, b] * slope_ref[rows, b].astype(F32)
            add_terms(acc_ref, b, dy, xhat)
            dxhat = dy * np_ref[0:1, b]
            dh_ref[rows, b] = dxhat
            sums = [sums[0] + dxhat, sums[1] + dxhat * xhat]
        return row_means(sums, D) + [rstd_ref[rows, :]]

    def finish(rows, means):
        def put(b, value):
            grad_ref[rows, b] = cot_ref[rows, b].astype(F32) + value

        norm_back(rows, dh_ref, xhat_ref, means, put)

    in_stages(dpre0_ref.shape[0], [work, finish])
    close_sums(sums_ref, acc_ref)


def out_kernel(pieces, place_ref, hid_ref, tok_ref, *refs):
    piece_refs = refs[:pieces]
    out_ref, w_ref, sem = refs[pieces:]

    @pl.when(pl.program_id(0) == 0)
    def _():
        run_copies(out_copies(piece_refs, w_ref, place_ref[0], sem))

    branch = lax.dot_general(hid_ref[...], w_ref[...], NN, preferred_element_type=F32)
    out_ref[...] = (tok_ref[...].astype(F32) + branch).astype(BF16)


WIDTHS = (INNER, INNER, D)
LANE0 = (0, INNER, 2 * INNER)
CUT = 2 * LANE
CHUNKS = (((1, 0, CUT), (2, 0, D)), ((1, CUT, INNER - CUT),), ((0, 0, INNER),))


def spans(chunk, rows):
    found, first = [], 0
    for weight, col, cols in chunk:
        tiles = rows[weight] // SUB * (cols // LANE)
        found.append((weight, col // LANE, cols // LANE, first, tiles))
        first += tiles
    return found, first


def column_sums(pack_ref, row, ref, chunk, rows):
    for weight, block0, blocks, first, tiles in spans(chunk, rows)[0]:

        def body(g, carry, first=first, blocks=blocks):
            new = []
            for b in range(blocks):
                value = ref[first + g * blocks + b].astype(F32)
                new.append(carry[b] + fold(value * value + 1e-30))
            return tuple(new)

        zero = tuple(jnp.zeros((8, LANE), F32) for _ in range(blocks))
        cols = lax.fori_loop(0, tiles // blocks, body, zero, unroll=5)
        for b in range(blocks):
            lane = LANE0[weight] + (block0 + b) * LANE
            pack_ref[row : row + 1, lane : lane + LANE] = jnp.sum(cols[b], axis=0, keepdims=True)


def load_full(refs, place_ref, first, full_ref, sem, at):
    pieces = refs[0].shape[0]
    each = full_ref.shape[0] // (len(refs) * pieces)
    outer = pieces if len(refs) == 2 else pieces // 2
    y = place_ref[2] % 2
    copies = []
    for n, (ref, side) in enumerate(zip(refs, (y, 1 - y))):
        for p in range(pieces):
            index = side * outer + p if len(refs) == 2 else p % 2 * outer + p // 2
            target = full_ref.at[pl.ds(index * each, each)]
            source = ref.at[p, first : first + each]
            copies.append(pltpu.make_async_copy(source, target, sem.at[at + n * pieces + p]))
    return copies


def load_list(bits, mine_ref, other_ref, place_ref, full_ref, sem):
    me, copies = place_ref[2], []
    each = full_ref.shape[0] // (1 << len(bits))
    inner = mine_ref.shape[0]
    for n in range(2 * inner):
        ref, at, k = (mine_ref, other_ref)[n // inner], n % inner, 0
        for i, bit in enumerate(bits):
            if n >> (len(bits) - 1 - i) & 1:
                k |= bit
        device, index = me ^ k, 0
        for bit in sorted(bits):
            index = index * 2 + lax.rem(lax.div(device, bit), 2)
        target = full_ref.at[pl.ds(index * each, each)]
        copies.append(pltpu.make_async_copy(ref.at[at], target, sem.at[n]))
    return copies


def pack_kernel(rows, pieces, place_ref, part_ref, *refs):
    states, sums, (pack_ref, acc_ref) = refs[0:3], refs[3:7], refs[7:9]
    pack_ref[...] = jnp.zeros_like(pack_ref)
    lanes_of = ((0, D), (D, D + INNER), (D, D + INNER), (D + INNER, D + 2 * INNER))
    for part, (lane0, lane1) in zip(sums, lanes_of):
        pack_ref[0:2, lane0:lane1] += part[...]
    lanes = lax.broadcasted_iota(jnp.int32, (1, LANE), 1)
    for k in range(3):
        total = jnp.sum(states[k][...].reshape(1, -1), axis=1, keepdims=True)
        pack_ref[3:4, 0:LANE] += jnp.where(lanes == k, total, 0.0)
    acc_ref[...] = jnp.zeros_like(acc_ref)
    spare = acc_ref.shape[0] - 1
    outer = place_ref[3] // 2
    piece = place_ref[2] % 2 * outer + place_ref[2] // 2
    at = 0
    for chunk, each in zip(CHUNKS[:2], pieces):
        found, _ = spans(chunk, rows)
        start = piece * each

        def body(k, carry, found=found, start=start, at=at):
            n = start + k
            slot = spare
            for weight, block0, blocks, first, tiles in found:
                here = LANE0[weight] // LANE + block0 + lax.rem(jnp.maximum(n - first, 0), blocks)
                slot = jnp.where((n >= first) & (n < first + tiles), here, slot)
            value = part_ref[at + k].astype(F32)
            acc_ref[slot] += value * value + 1e-30
            return carry

        lax.fori_loop(0, each, body, 0, unroll=2)
        at += each
    for slot in range(spare):
        pack_ref[2:3, slot * LANE : (slot + 1) * LANE] = jnp.sum(acc_ref[slot], axis=0, keepdims=True)


def pack_in_kernel(rows, bits, place_ref, mine_ref, other_ref, pack_ref, full_ref, sem):
    run_copies(load_list(bits, mine_ref, other_ref, place_ref, full_ref, sem))
    pack_ref[...] = jnp.zeros_like(pack_ref)
    column_sums(pack_ref, 0, full_ref, CHUNKS[2], rows)


def update_weight(
    k, squares, states_sum, source, weight, state, col_state, grad_ref, new, row_new_ref, col_new_ref, scratch, step=0, steps=1
):
    line_ref, state_ref, new_ref, scaled_ref = scratch
    width, fan, rows_here = WIDTHS[k], (D, KERNEL_TAPS * INNER, INNER)[k], state.shape[0]
    whole_rows = rows_here + -rows_here % LANE
    groups = rows_here // SUB // steps
    rate = 0.5 / fan**0.5

    def before():
        col_new = DECAY * col_state[...].reshape(1, -1) + (1.0 - DECAY) * (squares * (1.0 / fan))
        col_new_ref[...] = col_new.reshape(-1)
        total = DECAY * states_sum
        total = total + (1.0 - DECAY) * (1.0 / width) * jnp.sum(squares, axis=1, keepdims=True)
        scaled_ref[0:1, 0:width] = col_new / (total * (1.0 / fan))
        line_ref[0:1, 0:rows_here] = state[...].reshape(1, -1)
        for c in range(0, whole_rows, LANE):
            state_ref[c : c + LANE, :] = column(line_ref[0:1, c : c + LANE])

    def after():
        for c in range(0, whole_rows, LANE):
            line_ref[0:1, c : c + LANE] = jnp.transpose(new_ref[c : c + LANE, :])[0:1, :]
        row_new_ref[...] = line_ref[0:1, 0:rows_here].reshape(-1)

    def body(g, carry):
        here = pl.ds(pl.multiple_of(g * SUB, SUB), SUB)
        at = step * groups + g
        rows = pl.ds(pl.multiple_of(at * SUB, SUB), SUB)
        square = 0.0
        for ref, block0, blocks, first in source:
            for b in range(blocks):
                value = ref[first + at * blocks + b].astype(F32)
                grad_ref[here, (block0 + b) * LANE : (block0 + b + 1) * LANE] = value
                square = square + (value * value + 1e-30)
        mean = jnp.sum(square, axis=1, keepdims=True) * (1.0 / width)
        row_new = DECAY * state_ref[rows, :] + (1.0 - DECAY) * mean
        new_ref[rows, :] = row_new
        for ref, block0, blocks, first in source:
            for b in range(blocks):
                lanes = slice((block0 + b) * LANE, (block0 + b + 1) * LANE)
                value = ref[first + at * blocks + b].astype(F32)
                change = value * lax.rsqrt(row_new * scaled_ref[0:1, lanes])
                new[here, lanes] = weight[here, lanes] - rate * change
        return carry

    if steps == 1:
        before()
        lax.fori_loop(0, groups, body, 0, unroll=5)
        after()
    else:
        pl.when(step == 0)(before)
        lax.fori_loop(0, groups, body, 0, unroll=5)
        pl.when(step == steps - 1)(after)


def sources_of(chunk, ref, rows):
    return {w: (ref, block0, blocks, first) for w, block0, blocks, first, _ in spans(chunk, rows)[0]}


def update_kernel(rows, copies_of, place_ref, mine_ref, other_ref, pack_ref, *refs):
    weights, states, col_states = refs[0:2], refs[2:4], refs[4:6]
    grads, news, rows_new, cols_new = refs[6:8], refs[8:10], refs[10:12], refs[12:14]
    conv_scratch, out_scratch = refs[14:18], refs[18:22]
    full1_ref, full2_ref, sem = refs[22:25]
    both = (mine_ref, other_ref)
    count = 2 * mine_ref.shape[0]
    step, steps = pl.program_id(0), pl.num_programs(0)

    @pl.when(step == 0)
    def _():
        copies = load_full(both, place_ref, 0, full1_ref, sem, 0)
        copies += load_full(both, place_ref, full1_ref.shape[0] // count, full2_ref, sem, count)
        run_copies(copies)

    from1 = sources_of(CHUNKS[0], full1_ref, rows)
    from2 = sources_of(CHUNKS[1], full2_ref, rows)

    def update(n, k, source, scratch, *steps):
        squares = pack_ref[2:3, LANE0[k] : LANE0[k] + WIDTHS[k]]
        update_weight(
            k, squares, pack_ref[3:4, k : k + 1] * (1.0 / copies_of), source, weights[n],
            states[n], col_states[n], grads[n], news[n], rows_new[n], cols_new[n], scratch, *steps,
        )

    update(0, 1, [from1[1], from2[1]], conv_scratch, step, UPDATE_STEPS)

    @pl.when(step == steps - 1)
    def _():
        update(1, 2, [from1[2]], out_scratch)


def update_in_kernel(
    rows, copies_of, bits, place_ref, mine_ref, other_ref, pack_in_ref, pack_ref, np_ref, second_ref, *refs
):
    weight, state, col_state, grad_ref, new_ref, row_new_ref, col_new_ref = refs[0:7]
    ngrad_ref, nsecond_ref, nnew_ref = refs[7:10]
    full_ref, sem = refs[14:16]
    copies = load_list(bits, mine_ref, other_ref, place_ref, full_ref, sem)
    for copy in copies:
        copy.start()
    grad = pack_ref[0:2, :]
    second = DECAY * second_ref[...] + (1.0 - DECAY) * (grad * grad + 1e-30)
    ngrad_ref[...] = grad
    nsecond_ref[...] = second
    nnew_ref[...] = np_ref[...] - 0.2 * grad * lax.rsqrt(second)
    for copy in copies:
        copy.wait()
    update_weight(
        0, pack_in_ref[0:1, :], pack_ref[3:4, 0:1] * (1.0 / copies_of),
        [sources_of(CHUNKS[2], full_ref, rows)[0]], weight, state, col_state, grad_ref, new_ref,
        row_new_ref, col_new_ref, refs[10:14],
    )


class Places:
    def __init__(self):
        self.seq, self.fsdp = lax.axis_size("seq"), lax.axis_size("fsdp")
        self.q = lax.axis_index("fsdp")
        self.s = lax.axis_index("seq")

    def flip(self, x, axis, bit):
        pairs = []
        for s in range(self.seq):
            for f in range(self.fsdp):
                s2, f2 = (s ^ bit, f) if axis == "seq" else (s, f ^ bit)
                pairs.append((s * self.fsdp + f, s2 * self.fsdp + f2))
        return lax.ppermute(x, AXES, pairs)


def bits_of(count):
    return [1 << k for k in range(count.bit_length() - 1)]


def tie(x, *others):
    return lax.optimization_barrier((x, *others))[0]


def gather_pieces(piece, place, after, later=()):
    found = {0: piece}
    for bit in reversed(bits_of(place.fsdp)):
        for k in list(found):
            moving = found[k]
            if bit == 1:
                moving = tie(moving, *((after,) if k == 0 or not later else later))
            found[k | bit] = place.flip(moving, "fsdp", bit)
    return [found[k] for k in range(place.fsdp)]


def sum_over(x, place, *axes):
    for axis in axes:
        for bit in bits_of(getattr(place, axis)):
            x = x + place.flip(x, axis, bit)
    return x


def pick(x, index, axis):
    return lax.dynamic_index_in_dim(x, index, axis=axis, keepdims=False)


class Reduction:
    def __init__(self, place, keep, send):
        self.place, self.near = place, keep
        self.got = place.flip(send, "fsdp", 1)

    def halve(self, axis, side, flip_axis, bit):
        dims = self.near.shape
        parts = dims[:axis] + (2, dims[axis] // 2) + dims[axis + 1 :]
        near, got = self.near.reshape(parts), self.got.reshape(parts)
        away = pick(near, 1 - side, axis).astype(F32) + pick(got, 1 - side, axis).astype(F32)
        self.near = pick(near, side, axis).astype(F32) + pick(got, side, axis).astype(F32)
        away = away.astype(BF16)
        self.got = self.place.flip(away, flip_axis, bit)
        return away

    def x(self):
        bit = self.place.fsdp // 2
        while bit > 1:
            away = self.halve(0, (self.place.q // bit) % 2, "fsdp", bit)
            bit //= 2
        return away

    def y(self):
        return self.halve(1, self.place.s % 2, "seq", 1)

    def seq_bit(self, bit):
        return self.halve(1, (self.place.s // bit) % 2, "seq", bit)

    def piece(self):
        total = (self.near + self.got.astype(F32)).astype(BF16)
        return total.reshape(total.shape[1:])

    def pieces(self):
        total = (self.near + self.got.astype(F32)).astype(BF16)
        return total.reshape((self.place.seq // 2, -1) + total.shape[2:])


def arrive(result, *reductions):
    result, *gots = lax.optimization_barrier((result, *[r.got for r in reductions]))
    for reduction, got in zip(reductions, gots):
        reduction.got = got
    return result


def summed_f32(got):
    return jnp.sum(got.astype(F32), axis=0)


def summed(got):
    return summed_f32(got).astype(BF16)


def exchange(place, sent):
    line = [[y + 2 * z for z in range(place.seq // 2)] for y in range(2)]
    return lax.all_to_all(sent, "seq", 0, 0, axis_index_groups=line)


def on_device(
    tokens, input_mask, doc_lengths, cotangent, w_in, w_conv, w_out, norm_params,
    row_in, col_in, row_conv, col_conv, row_out, col_out, norm_second,
):
    place = Places()
    rows = tokens.shape[0]
    pieces = place.fsdp
    spots = jnp.stack(
        [place.q, (place.s * place.fsdp + place.q) * rows, place.s, place.seq]
    ).astype(jnp.int32)
    docs = doc_lengths.shape[0]
    live = input_mask.reshape(-1, LANE)
    weights = (w_in, w_conv, w_out)
    rows_of = [w.shape[0] for w in weights]

    tile_a, tile = 256, 512
    steps = rows // tile
    params_spec = whole(2, D + 2 * INNER)
    dma = pltpu.SemaphoreType.DMA

    out_sides = (w_out[:, : D // 2], w_out[:, D // 2 :])
    conv_out = jnp.concatenate([w_conv, *out_sides], axis=0).astype(BF16)
    hidden_a, slope_a, xhat_a, rstd_a = call(
        norm_a_kernel,
        (rows // tile_a,),
        [rows_spec(tile_a, D), params_spec],
        [rows_spec(tile_a, D)] * 3 + [rows_spec(tile_a, LANE)],
        [shape((rows, D), BF16)] * 3 + [shape((rows, LANE), F32)],
        us=17,
    )(tokens, tie(norm_params, conv_out))

    in_pieces = gather_pieces(w_in.astype(BF16), place, hidden_a)

    def in_call(tiles, count, before):
        at, stride = tiles

        def here_spec(width):
            return pl.BlockSpec((tile, width), lambda i: (at + stride * i, 0))

        out_shapes = [shape((rows, INNER), BF16)] * 3 + [shape((rows, LANE), F32)] * 2
        out_specs = [here_spec(INNER)] * 3 + [here_spec(LANE)] * 2
        if at == 0:
            out_shapes += [shape((REACH, INNER), BF16)] * 2
            out_specs += [whole(REACH, INNER)] * 2
        return call(
            functools.partial(in_kernel, pieces, tiles),
            (count,),
            [SMEM, whole(docs), here_spec(D), whole(*live.shape), params_spec]
            + [ANY] * (pieces + len(before)),
            out_specs,
            out_shapes,
            [pltpu.VMEM((D, INNER), BF16), pltpu.VMEM((tile, INNER), F32)]
            + [pltpu.VMEM((8, docs + -docs % LANE), F32), dma((pieces,))],
            us=3,
            aliases={5 + pieces + k: k for k in range(len(before))},
        )(spots, doc_lengths, hidden_a, live, norm_params, *in_pieces, *before)

    *kept, m_first, m_last = in_call((0, steps - 1), 2, ())
    moved, slope_b, xhat_b, rstd_b, masks = in_call((1, 1), steps - 2, kept)

    def halo(inner, outer):
        total = place.seq * place.fsdp
        across = [(i, i + 1 if i % 2 else i - 1) for i in range(1, total - 1)]
        return place.flip(inner, "fsdp", 1), lax.ppermute(outer, AXES, across)

    m_inner, m_outer = halo(m_first, m_last)
    conv_pieces = gather_pieces(conv_out, place, m_first, (moved, m_inner, m_outer))

    ext = pltpu.VMEM((rows + 2 * REACH, INNER), BF16)
    taps_wide = KERNEL_TAPS * INNER
    wide = pltpu.VMEM((taps_wide, INNER), BF16)
    shards = place.fsdp // 2

    def half_dims(chunk):
        count = spans(chunk, rows_of)[1]
        return (shards, count + -count % place.seq, SUB, LANE)

    def tile_spec(width, ahead):
        return pl.BlockSpec((tile, width), lambda i: (jnp.clip(i + ahead, 0, steps - 1), 0))

    halves = [half_dims(CHUNKS[0])] * 2 + [half_dims(CHUNKS[1])] * 2
    work = pltpu.VMEM((tile, INNER), F32)
    turned_tile = pltpu.VMEM((INNER, tile), BF16)
    hidden_c, d_conv, d_first, d_last, sums_c, turned, keep1, send1, keep2, send2 = call(
        functools.partial(conv_kernel, pieces, rows_of),
        (steps + 1,),
        [SMEM, ANY, ANY, ANY, tile_spec(LANE, 0), tile_spec(D, 0), tile_spec(D, -1), params_spec]
        + [ANY] * pieces,
        [tile_spec(INNER, 0)] * 2
        + [whole(REACH, INNER), whole(REACH, INNER), whole(2, INNER)]
        + [ANY] * 5,
        [
            shape((rows, INNER), BF16),
            shape((rows, INNER), BF16),
            shape((REACH, INNER), BF16),
            shape((REACH, INNER), BF16),
            shape((2, INNER), F32),
            shape((taps_wide, INNER), BF16),
        ]
        + [shape(dims, BF16) for dims in halves],
        [ext, wide, wide, pltpu.VMEM((INNER, D), BF16), pltpu.VMEM((D, INNER), BF16)]
        + [pltpu.VMEM((2, tile, taps_wide), BF16), work, work, work, turned_tile, turned_tile]
        + [pltpu.VMEM((INNER, taps_wide), F32), pltpu.VMEM((INNER, D), F32)]
        + [pltpu.VMEM((16, INNER), F32)]
        + [pltpu.VMEM((2,) + halves[0], BF16), pltpu.VMEM((2,) + halves[2], BF16)]
        + [dma((3 + 3 * pieces,))],
        us=45,
    )(
        spots, m_inner, moved, m_outer, masks, cotangent, cotangent, norm_params, *conv_pieces
    )
    d_inner, d_outer = halo(d_first, d_last)
    first, second = Reduction(place, keep1, send1), Reduction(place, keep2, send2)
    (block_out,) = call(
        functools.partial(out_kernel, pieces),
        (steps,),
        [SMEM, rows_spec(tile, INNER), rows_spec(tile, D)] + [ANY] * pieces,
        [rows_spec(tile, D)],
        [shape((rows, D), BF16)],
        [pltpu.VMEM((INNER, D), BF16), dma((2 * pieces,))],
        us=9,
    )(spots, hidden_c, tokens, *conv_pieces)

    def back_conv(last, spots, before):
        here = steps // 2
        at = here * last

        def here_spec(width):
            return pl.BlockSpec((tile, width), lambda i: (i + at, 0))

        dims = half_dims(CHUNKS[2])
        return call(
            functools.partial(back_conv_kernel, last, w_in.shape[0]),
            (here,),
            [SMEM] + [ANY] * 4
            + [here_spec(LANE), here_spec(INNER), here_spec(LANE), here_spec(INNER), here_spec(D)]
            + [params_spec]
            + [ANY] * last,
            [rows_spec(tile, INNER), whole(2, INNER)] + [ANY] * (1 + last),
            [shape((rows // 2, INNER), BF16), shape((2, INNER), F32)]
            + ([shape(dims, BF16)] * 2 if last else [shape((INNER, D), F32)]),
            ([pltpu.VMEM((2,) + dims, BF16)] if last else [])
            + [
                ext,
                wide,
                pltpu.VMEM((tile, taps_wide), BF16),
                pltpu.VMEM((tile, INNER), F32),
                pltpu.VMEM((INNER, D), F32),
                pltpu.VMEM((16, INNER), F32),
                dma((5,)),
            ],
            us=16,
        )(
            spots, d_inner, d_conv, d_outer, turned, masks, xhat_b, rstd_b, slope_b, hidden_a,
            norm_params, *before,
        )

    block_out, d_inner, d_outer = arrive((block_out, d_inner, d_outer), first, second)
    away = (first.x(), second.y())
    d_pre0, sums_b0, grad_part = back_conv(0, tie(spots, *away), ())
    d_pre0 = arrive(d_pre0, first, second)
    away = (first.y(), second.x())
    d_pre1, sums_b1, keep, send = back_conv(1, tie(spots, *away), (grad_part,))
    send = arrive(send, first, second)
    third = Reduction(place, keep, send)
    sent = jnp.concatenate([first.pieces(), second.pieces()], axis=1)
    got = exchange(place, sent)
    third.got = tie(third.got, sent)
    away = (sent, third.x())
    input_grad, sums_a = call(
        functools.partial(back_a_kernel, pieces, steps // 2),
        (steps,),
        [SMEM]
        + [
            pl.BlockSpec((tile, INNER), lambda i: (jnp.minimum(i, steps // 2 - 1), 0)),
            pl.BlockSpec((tile, INNER), lambda i: (jnp.maximum(i - steps // 2, 0), 0)),
        ]
        + [rows_spec(tile, D), rows_spec(tile, LANE), rows_spec(tile, D), rows_spec(tile, D)]
        + [params_spec]
        + [ANY] * pieces,
        [rows_spec(tile, D), whole(2, D)],
        [shape((rows, D), F32), shape((2, D), F32)],
        [
            pltpu.VMEM((D, INNER), BF16),
            pltpu.VMEM((INNER, D), BF16),
            pltpu.VMEM((tile, D), F32),
            pltpu.VMEM((16, D), F32),
            dma((pieces,)),
        ],
        us=17,
    )(
        tie(spots, *away), d_pre0, d_pre1, xhat_a, rstd_a, slope_a, cotangent, norm_params, *in_pieces
    )

    row_states, col_states = (row_in, row_conv, row_out), (col_in, col_conv, col_out)
    row_specs = [whole(*r.shape) for r in row_states]
    col_specs = [whole(*c.shape) for c in col_states]
    cols_all = D + 2 * INNER
    pack_spec = whole(4, cols_all)
    fulls = [pltpu.VMEM(half_dims(c)[1:], BF16) for c in CHUNKS]
    sums = (sums_a, sums_b0, sums_b1, sums_c)
    got, third.got, input_grad = lax.optimization_barrier((got, third.got, input_grad))
    part = summed(got)
    sent = jnp.broadcast_to(part[None], (place.seq // 2,) + part.shape)
    mine = exchange(place, sent)
    third.got = tie(third.got, sent)
    away = third.y()
    (pack,) = call(
        functools.partial(pack_kernel, rows_of, [half_dims(c)[1] // place.seq for c in CHUNKS]),
        (1,),
        [SMEM, whole(*part.shape)] + row_specs + [whole(*x.shape) for x in sums],
        [pack_spec],
        [shape((4, cols_all), F32)],
        [pltpu.VMEM((cols_all // LANE + 1, SUB, LANE), F32)],
        us=2,
        mib=16,
    )(tie(spots, away), part, *row_states, *sums)
    pack = sum_over(pack, place, "fsdp")
    seq_bits = bits_of(place.seq)
    third.seq_bit(seq_bits[1])
    mine, third.got, pack = lax.optimization_barrier((mine, third.got, pack))
    other = place.flip(mine, "seq", 1)
    for bit in seq_bits[2:]:
        third.seq_bit(bit)
    line = third.piece()[None]
    for bit in seq_bits[:0:-1]:
        line = jnp.concatenate([line, place.flip(line, "seq", bit)], axis=0)
    for bit in seq_bits[1:] + seq_bits[:1]:
        pack = pack + place.flip(pack, "seq", bit)
    line, other, pack = lax.optimization_barrier((line, other, pack))
    line_other = place.flip(line, "seq", 1)
    list_bits = [1] + seq_bits[1:]

    def update_scratch(weight):
        lines = weight.shape[0] + -weight.shape[0] % LANE
        return (
            [pltpu.VMEM((8, lines), F32)]
            + [pltpu.VMEM((lines, LANE), F32)] * 2
            + [pltpu.VMEM((8, weight.shape[1]), F32)]
        )

    weight_specs = [whole(*w.shape) for w in weights]
    conv_block = pl.BlockSpec((w_conv.shape[0] // UPDATE_STEPS, INNER), lambda i: (i, 0))
    both_specs = [conv_block, weight_specs[2]]
    results = call(
        functools.partial(update_kernel, rows_of, place.seq),
        (UPDATE_STEPS,),
        [SMEM, ANY, ANY, pack_spec] + both_specs + row_specs[1:] + col_specs[1:],
        both_specs * 2 + row_specs[1:] + col_specs[1:],
        [shape(w.shape, F32) for w in weights[1:]] * 2
        + [shape(r.shape, F32) for r in row_states[1:] + col_states[1:]],
        update_scratch(w_conv)
        + update_scratch(w_out)
        + fulls[:2]
        + [dma((2 * place.seq,))],
        us=8,
        mib=32,
    )(spots, mine, other, pack, *weights[1:], *row_states[1:], *col_states[1:])
    grad_conv, grad_out, new_conv, new_out, row_conv_new, row_out_new, col_conv_new, col_out_new = (
        results
    )
    line_other, grad_out = lax.optimization_barrier((line_other, grad_out))
    (pack_in,) = call(
        functools.partial(pack_in_kernel, rows_of, list_bits),
        (1,),
        [SMEM, ANY, ANY],
        [whole(8, INNER)],
        [shape((8, INNER), F32)],
        [fulls[2], dma((place.seq,))],
        us=2,
        mib=16,
    )(spots, line, line_other)
    pack_in = sum_over(pack_in, place, "fsdp")
    grad_in, new_in, row_in_new, col_in_new, *norm_results = call(
        functools.partial(update_in_kernel, rows_of, place.seq, list_bits),
        (1,),
        [SMEM, ANY, ANY, whole(8, INNER), pack_spec, params_spec, params_spec]
        + [weight_specs[0], row_specs[0], col_specs[0]],
        [weight_specs[0]] * 2 + [row_specs[0], col_specs[0]] + [params_spec] * 3,
        [shape(w_in.shape, F32)] * 2
        + [shape(row_in.shape, F32), shape(col_in.shape, F32)]
        + [shape((2, cols_all), F32)] * 3,
        update_scratch(w_in) + [fulls[2], dma((place.seq,))],
        us=4,
        mib=24,
    )(
        spots, line, line_other, pack_in, pack, norm_params, norm_second, w_in, row_in, col_in
    )
    return (
        block_out,
        input_grad,
        grad_in,
        grad_conv,
        grad_out,
        new_in,
        new_conv,
        new_out,
        row_in_new,
        col_in_new,
        row_conv_new,
        col_conv_new,
        row_out_new,
        col_out_new,
        *norm_results,
    )


def solution(mesh):
    both, rows = P(AXES, None), P("fsdp", None)
    in_specs = (
        both, P(AXES), P(), both, rows, rows, rows, P(),
        P("fsdp"), P(), P("fsdp"), P(), P("fsdp"), P(), P(),
    )
    out_specs = (
        both, both, rows, rows, rows, rows, rows, rows,
        P("fsdp"), P(), P("fsdp"), P(), P("fsdp"), P(), P(), P(), P(),
    )
    return jax.shard_map(
        on_device, mesh=mesh, in_specs=in_specs, out_specs=out_specs, check_vma=False
    )
```

```python
import functools
import math

import jax
import jax.numpy as jnp
from jax import lax
from jax.experimental import pallas as pl
from jax.experimental.pallas import tpu as pltpu
from jax.sharding import PartitionSpec as P

D = 1280
INNER = 640
KERNEL_TAPS = 5
DILATION_STEP = 128
STEP = 10
EPSILON = 1e-05
DECAY = 1.0 - STEP ** (-0.8)

REACH = (KERNEL_TAPS - 1) // 2 * DILATION_STEP
MID = (KERNEL_TAPS - 1) // 2
F32 = jnp.float32
BF16 = jnp.bfloat16
SUB, LANE = 16, 128
AXES = ("seq", "fsdp")
NT = (((1,), (1,)), ((), ()))
TN = (((0,), (0,)), ((), ()))
NN = (((1,), (0,)), ((), ()))


def call(kernel, grid, in_specs, out_specs, out_shape, scratch=(), us=1.0, aliases=None, mib=58):
    params = pltpu.CompilerParams(
        vmem_limit_bytes=mib * 1024 * 1024, dimension_semantics=("arbitrary",) * len(grid)
    )
    return pl.pallas_call(
        kernel,
        grid=grid,
        in_specs=in_specs,
        out_specs=out_specs,
        out_shape=out_shape,
        scratch_shapes=list(scratch),
        compiler_params=params,
        input_output_aliases=aliases or {},
        cost_estimate=pl.CostEstimate(
                flops=int(us * 1.1e9), bytes_accessed=int(us * 3.4e6), transcendentals=0
        ),
    )


def shape(dims, dtype):
    return jax.ShapeDtypeStruct(dims, dtype)


def rows_spec(tile, width):
    return pl.BlockSpec((tile, width), lambda i: (i, 0))


def whole(*dims):
    return pl.BlockSpec(dims, lambda *_: (0,) * len(dims))


ANY = pl.BlockSpec(memory_space=pl.ANY)
SMEM = pl.BlockSpec(memory_space=pltpu.SMEM)


ERFC_P = 0.47 / math.sqrt(2.0)
ERFC_C = (
    0.12357219400743558,
    0.1999878668208835,
    -0.08033356004356296,
    0.3660253986657854,
    -0.1092519747040215,
)
LOG2E = 1.4426950408889634


def gelu_and_slope(y):
    t = pltpu.reciprocal(1.0 + ERFC_P * jnp.abs(y), approx=True)
    bell = jnp.exp2(y * y * (-0.5 * LOG2E))
    poly = ERFC_C[4] * t + ERFC_C[3]
    for c in ERFC_C[2::-1]:
        poly = poly * t + c
    tail = poly * t * bell
    cdf = jnp.where(y > 0.0, 1.0 - tail, tail)
    return y * cdf, cdf + y * (bell * (1.0 / math.sqrt(2.0 * math.pi)))


def lane_blocks(width):
    return [slice(k, k + LANE) for k in range(0, width, LANE)]


def row_stats(ref, rows):
    width = ref.shape[-1]
    blocks = lane_blocks(width)
    total = ref[rows, blocks[0]].astype(F32)
    for b in blocks[1:]:
        total = total + ref[rows, b].astype(F32)
    mean = jnp.sum(total, axis=-1, keepdims=True) * (1.0 / width)
    square = None
    for b in blocks:
        centered = ref[rows, b].astype(F32) - mean
        square = centered * centered if square is None else square + centered * centered
    variance = jnp.sum(square, axis=-1, keepdims=True) * (1.0 / width)
    return mean, lax.rsqrt(variance + EPSILON)


def fold(values):
    total = values[0:8]
    for k in range(8, values.shape[0], 8):
        total = total + values[k : k + 8]
    return total


def in_stages(count, stages, between=()):
    chunks = [slice(k, k + CHUNK) for k in range(0, count, CHUNK)]
    kept, rounds = {}, len(chunks) + len(stages) - 1
    for t in range(rounds):
        for n, stage in enumerate(stages):
            if 0 <= t - n < len(chunks):
                kept[n, t - n] = stage(chunks[t - n], kept.get((n - 1, t - n)))
        for work in between[t * len(between) // rounds : (t + 1) * len(between) // rounds]:
            work()


def halves_of(count):
    return (slice(0, count // 2), slice(count // 2, count))


def row_means(sums, width):
    return [jnp.sum(x, axis=-1, keepdims=True) * (1.0 / width) for x in sums]


def norm_back(rows, dxhat_ref, xhat_ref, means, put):
    mean_d, mean_dx, rstd = means
    for b in lane_blocks(dxhat_ref.shape[-1]):
        xhat = xhat_ref[rows, b].astype(F32)
        put(b, (dxhat_ref[rows, b] - mean_d - xhat * mean_dx) * rstd)


def add_terms(acc_ref, b, dy, xhat):
    acc_ref[0:8, b] += fold(dy * xhat)
    acc_ref[8:16, b] += fold(dy)


def open_sums(acc_ref):
    @pl.when(pl.program_id(0) == 0)
    def _():
        acc_ref[...] = jnp.zeros_like(acc_ref)


def close_sums(out_ref, acc_ref):
    @pl.when(pl.program_id(0) == pl.num_programs(0) - 1)
    def _():
        out_ref[0:1, :] = jnp.sum(acc_ref[0:8, :], axis=0, keepdims=True)
        out_ref[1:2, :] = jnp.sum(acc_ref[8:16, :], axis=0, keepdims=True)


def run_copies(copies):
    for copy in copies:
        copy.start()
    for copy in copies:
        copy.wait()


def piece_copies(pieces, full_ref, me, sem, first=0):
    each = full_ref.shape[0] // len(pieces)
    return [
        pltpu.make_async_copy(
            piece.at[0:each, :],
            full_ref.at[pl.ds(pl.multiple_of((me ^ k) * each, SUB), each), :],
            sem.at[first + k],
        )
        for k, piece in enumerate(pieces)
    ]


def out_copies(pieces, full_ref, me, sem, first=0):
    each, width = full_ref.shape[0] // len(pieces), full_ref.shape[1] // 2
    copies = []
    for k, piece in enumerate(pieces):
        rows = pl.ds(pl.multiple_of((me ^ k) * each, SUB), each)
        for side in range(2):
            at = piece.shape[0] - (2 - side) * each
            copies.append(
                pltpu.make_async_copy(
                    piece.at[at : at + each, :],
                    full_ref.at[rows, side * width : (side + 1) * width],
                    sem.at[first + 2 * k + side],
                )
            )
    return copies


def column(row):
    return jnp.transpose(jnp.broadcast_to(row, (LANE, LANE)))


CHUNK = 64
UPDATE_STEPS = 5
TURNED = 2


def norm_a_kernel(tok_ref, np_ref, hid_ref, slope_ref, xhat_ref, rstd_ref):
    def stats(rows, _):
        mean, rstd = row_stats(tok_ref, rows)
        rstd_ref[rows, :] = jnp.broadcast_to(rstd, (CHUNK, LANE))
        return mean, rstd

    def work(rows, kept):
        mean, rstd = kept
        for b in lane_blocks(D):
            xhat = (tok_ref[rows, b].astype(F32) - mean) * rstd
            hidden, slope = gelu_and_slope(xhat * np_ref[0:1, b] + np_ref[1:2, b])
            hid_ref[rows, b] = hidden.astype(BF16)
            slope_ref[rows, b] = slope.astype(BF16)
            xhat_ref[rows, b] = xhat.astype(BF16)

    in_stages(tok_ref.shape[0], [stats, work])


def running_ends(ends_ref, lengths_ref):
    docs, width = lengths_ref.shape[0], ends_ref.shape[1]
    ends_ref[...] = jnp.zeros_like(ends_ref)
    ends_ref[0:1, 0:docs] = lengths_ref[...].reshape(1, -1).astype(F32)
    before = jnp.zeros((1, 1), F32)
    row = lax.broadcasted_iota(jnp.int32, (LANE, LANE), 0)
    lane = lax.broadcasted_iota(jnp.int32, (LANE, LANE), 1)
    for k in range(0, width, LANE):
        line = ends_ref[0:1, k : k + LANE]
        sums = jnp.sum(jnp.where(row <= lane, column(line), 0.0), axis=0, keepdims=True) + before
        ends_ref[0:1, k : k + LANE] = jnp.where(lane[0:1] + k < docs, sums, 1e9)
        before = before + jnp.sum(line, axis=1, keepdims=True)


def in_kernel(pieces, tiles, place_ref, lengths_ref, hid_ref, live_ref, np_ref, *refs):
    piece_refs = refs[:pieces]
    edges = tiles[0] == 0
    outs = refs[-(11 if edges else 9) :]
    mov_ref, slope_ref, xhat_ref, rstd_ref, mask_ref = outs[:5]
    w_ref, pre_ref, ends_ref, sem = outs[-4:]
    step = pl.program_id(0)
    tile = hid_ref.shape[0]

    @pl.when(step == 0)
    def _():
        copies = piece_copies(piece_refs, w_ref, place_ref[0], sem)
        for copy in copies:
            copy.start()
        running_ends(ends_ref, lengths_ref)
        for copy in copies:
            copy.wait()

    for half in halves_of(tile):
        pre_ref[half, :] = lax.dot_general(
            hid_ref[half, :], w_ref[...], NN, preferred_element_type=F32
        )

    at_tile = tiles[0] + step * tiles[1]
    first = place_ref[1] + at_tile * tile
    ends = ends_ref[0:1, :]
    lanes = lax.broadcasted_iota(jnp.int32, (LANE, LANE), 1)
    offsets = ((lanes - MID) * DILATION_STEP).astype(F32)
    for k in range(tile // LANE):
        at = (first + k * LANE + lax.broadcasted_iota(jnp.int32, (LANE, 1), 0)).astype(F32)
        begin = jnp.max(jnp.where(ends <= at, ends, 0.0), axis=1, keepdims=True)
        end = jnp.min(jnp.where(ends > at, ends, 1e9), axis=1, keepdims=True)
        there = at + offsets
        same = jnp.where((there >= begin) & (there < end), 1.0, 0.0)
        live = column(live_ref[pl.ds(at_tile * (tile // LANE) + k, 1), :].astype(F32))
        mask_ref[k * LANE : (k + 1) * LANE, :] = jnp.where(lanes == MID, live, same)

    def stats(rows, _):
        mean, rstd = row_stats(pre_ref, rows)
        rstd_ref[rows, :] = jnp.broadcast_to(rstd, (CHUNK, LANE))
        return mean, rstd

    def work(rows, kept):
        mean, rstd = kept
        live = mask_ref[rows, MID : MID + 1]
        for b in lane_blocks(INNER):
            gains = slice(D + b.start, D + b.stop)
            xhat = (pre_ref[rows, b] - mean) * rstd
            hidden, slope = gelu_and_slope(xhat * np_ref[0:1, gains] + np_ref[1:2, gains])
            mov_ref[rows, b] = (hidden * live).astype(BF16)
            slope_ref[rows, b] = slope.astype(BF16)
            xhat_ref[rows, b] = xhat.astype(BF16)

    in_stages(tile, [stats, work])
    if edges:
        put_edges(place_ref, outs[5], outs[6], mov_ref, step == 0, step == 1)


def load_window(place_ref, inner, mid, outer, ext_ref, sem):
    rows, core = mid.shape[0], lax.rem(place_ref[0], 2)
    near = pl.multiple_of((1 - core) * (REACH + rows), SUB)
    far = pl.multiple_of(core * (REACH + rows), SUB)
    return [
        pltpu.make_async_copy(inner, ext_ref.at[pl.ds(near, REACH), :], sem.at[0]),
        pltpu.make_async_copy(mid, ext_ref.at[REACH : REACH + rows, :], sem.at[1]),
        pltpu.make_async_copy(outer, ext_ref.at[pl.ds(far, REACH), :], sem.at[2]),
    ]


def put_edges(place_ref, inner_ref, outer_ref, tile_ref, at_first, at_last):
    rows, core = tile_ref.shape[0], lax.rem(place_ref[0], 2)
    for at, edge, first in ((at_first, slice(0, REACH), 0), (at_last, slice(rows - REACH, rows), 1)):

        @pl.when(at & (core == first))
        def _(edge=edge):
            outer_ref[...] = tile_ref[edge, :]

        @pl.when(at & (core != first))
        def _(edge=edge):
            inner_ref[...] = tile_ref[edge, :]


def fill_taps(taps_ref, ext_ref, mask_ref, start):
    tile = taps_ref.shape[0]
    for j in range(KERNEL_TAPS):
        rows = pl.ds(pl.multiple_of(start + j * DILATION_STEP, DILATION_STEP), tile)
        picked = ext_ref[rows, :]
        if j != MID:
            picked = picked * mask_ref[:, j : j + 1].astype(BF16)
        taps_ref[:, j * INNER : (j + 1) * INNER] = picked


def conv_kernel(
    pieces, rows_of, place_ref, low_ref, mov_ref, high_ref, mask_ref, cot_ref, before_ref, np_ref, *refs
):
    piece_refs = refs[:pieces]
    hid_ref, dconv_ref, inner_ref, outer_ref, sums_ref, turned_ref = refs[pieces : pieces + 6]
    outs = refs[pieces + 6 : pieces + 10]
    ext_ref, wc_ref, wct_ref, wo_ref, wt_ref, taps_ref, pre_ref, dh_ref, xhat_ref = refs[
        pieces + 10 : pieces + 19
    ]
    dt_ref, ht_ref, gc_ref, go_ref, acc_ref, stage1_ref, stage2_ref, sem = refs[pieces + 19 :]
    step, steps = pl.program_id(0), pl.num_programs(0) - 1
    tile = taps_ref.shape[1]
    slot = lax.rem(step, 2)

    @pl.when(step == 0)
    def _():
        me = place_ref[0]
        outs = out_copies(piece_refs, wo_ref, me, sem, 3)
        rest = load_window(place_ref, low_ref, mov_ref, high_ref, ext_ref, sem)
        rest += piece_copies(piece_refs, wc_ref, me, sem, 3 + 2 * pieces)
        for copy in outs + rest:
            copy.start()
        for ref in (acc_ref, gc_ref, go_ref):
            ref[...] = jnp.zeros_like(ref)
        for copy in outs:
            copy.wait()
        for k in range(0, D, 256):
            wt_ref[k : k + 256, :] = jnp.transpose(wo_ref[:, k : k + 256])
        for copy in rest:
            copy.wait()

    def grad_conv(cols):
        def work():
            gc_ref[:, cols] += lax.dot_general(
                dt_ref[...], taps_ref[1 - slot, :, cols], NN, preferred_element_type=F32
            )

        return work

    def grad_out(cols):
        def work():
            go_ref[:, cols] += lax.dot_general(
                ht_ref[...], before_ref[:, cols], NN, preferred_element_type=F32
            )

        return work

    taps_wide = KERNEL_TAPS * INNER
    products = [grad_conv(slice(k, min(k + 768, taps_wide))) for k in range(0, taps_wide, 768)]
    products += [grad_out(slice(k, min(k + 768, D))) for k in range(0, D, 768)]

    def tile_work(products, turned):
        fill_taps(taps_ref.at[slot], ext_ref, mask_ref, step * tile)
        pre_ref[...] = lax.dot_general(
            taps_ref[slot], wc_ref[...], NN, preferred_element_type=F32
        )
        dh_ref[...] = lax.dot_general(cot_ref[...], wt_ref[...], NN, preferred_element_type=F32)
        for n in range(turned):
            tap = jnp.minimum(turned * (step - 1) + n, KERNEL_TAPS - 1)
            source = wc_ref[pl.ds(pl.multiple_of(tap * INNER, SUB), INNER), :]
            target = pl.multiple_of((KERNEL_TAPS - 1 - tap) * INNER, SUB)
            wct_ref[pl.ds(target, INNER), :] = jnp.transpose(source)

        def stats(rows, _):
            return row_stats(pre_ref, rows)

        def work(rows, kept):
            mean, rstd = kept
            sums = [0.0, 0.0]
            for b in lane_blocks(INNER):
                gains = slice(D + INNER + b.start, D + INNER + b.stop)
                gain = np_ref[0:1, gains]
                xhat = (pre_ref[rows, b] - mean) * rstd
                hidden, slope = gelu_and_slope(xhat * gain + np_ref[1:2, gains])
                hid_ref[rows, b] = hidden.astype(BF16)
                dy = dh_ref[rows, b] * slope
                add_terms(acc_ref, b, dy, xhat)
                dxhat = dy * gain
                xhat_ref[rows, b] = xhat
                dh_ref[rows, b] = dxhat
                sums = [sums[0] + dxhat, sums[1] + dxhat * xhat]
            return row_means(sums, INNER) + [rstd]

        def finish(rows, means):
            def put(b, value):
                dconv_ref[rows, b] = value.astype(BF16)

            norm_back(rows, dh_ref, xhat_ref, means, put)

        in_stages(tile, [stats, work, finish], products)
        dt_ref[...] = jnp.transpose(dconv_ref[...])
        ht_ref[...] = jnp.transpose(hid_ref[...])

    @pl.when(step == 0)
    def _():
        tile_work([], 0)

    @pl.when((step > 0) & (step < steps))
    def _():
        tile_work(products, TURNED)

    put_edges(place_ref, inner_ref, outer_ref, dconv_ref, step == 0, step == steps - 1)

    @pl.when(step == steps)
    def _():
        copy = pltpu.make_async_copy(wct_ref, turned_ref, sem.at[4])
        copy.start()
        for work in products:
            work()
        core = lax.rem(place_ref[0], 2)
        _, rows_conv, rows_out = rows_of
        stage_turned(stage1_ref, core, gc_ref, rows_conv, 0, slice(0, CUT // LANE))
        first_tiles = rows_conv // SUB * (CUT // LANE)
        stage_plain(stage1_ref, core, go_ref, rows_out, first_tiles)
        copies = stage_copies(stage1_ref, outs[0], outs[1], spans(CHUNKS[0], rows_of)[1], sem, 0)
        for each in copies:
            each.start()
        stage_turned(stage2_ref, core, gc_ref, rows_conv, 0, slice(CUT // LANE, INNER // LANE))
        more = stage_copies(stage2_ref, outs[2], outs[3], spans(CHUNKS[1], rows_of)[1], sem, 2)
        for each in more:
            each.start()
        for each in copies + more + [copy]:
            each.wait()
        sums_ref[0:1, :] = jnp.sum(acc_ref[0:8, :], axis=0, keepdims=True)
        sums_ref[1:2, :] = jnp.sum(acc_ref[8:16, :], axis=0, keepdims=True)


def stage_tiles(stage_ref, core, first_row, rows_each, base, block0, blocks, value):
    for g in range(value.shape[0] // SUB):
        row = first_row + g * SUB
        owner, inside = row // rows_each, row % rows_each // SUB
        side = core ^ (owner % 2)
        for b in range(value.shape[1] // LANE):
            tile = value[g * SUB : (g + 1) * SUB, b * LANE : (b + 1) * LANE]
            at = base + inside * blocks + block0 + b
            stage_ref[side, owner // 2, at] = tile.astype(BF16)


def stage_plain(stage_ref, core, grad_ref, rows_each, base):
    blocks = grad_ref.shape[1] // LANE
    for row in range(0, grad_ref.shape[0], SUB):
        part = grad_ref[row : row + SUB, :]
        stage_tiles(stage_ref, core, row, rows_each, base, 0, blocks, part)


def stage_turned(stage_ref, core, turned_ref, rows_each, base, blocks):
    count = blocks.stop - blocks.start
    for row in range(0, turned_ref.shape[1], LANE):
        for b in range(count):
            at = (blocks.start + b) * LANE
            part = jnp.transpose(turned_ref[at : at + LANE, row : row + LANE].astype(BF16))
            stage_tiles(stage_ref, core, row, rows_each, base, b, count, part)


def stage_copies(stage_ref, keep_ref, send_ref, used, sem, first):
    count = stage_ref.shape[2]
    if used < count:
        dims = stage_ref.shape[:2] + (count - used, SUB, LANE)
        stage_ref[:, :, used:] = jnp.zeros(dims, BF16)
    return [
        pltpu.make_async_copy(stage_ref.at[n], ref, sem.at[first + n])
        for n, ref in enumerate((keep_ref, send_ref))
    ]


def back_conv_kernel(
    last, rows_in, place_ref, low_ref, d_ref, high_ref, turned_ref, mask_ref, xhat_ref, rstd_ref, slope_ref, hid_ref, np_ref, *refs
):
    if last:
        before_ref, dpre_ref, sums_ref, keep_ref, send_ref, stage_ref = refs[:6]
    else:
        dpre_ref, sums_ref, part_ref = refs[:3]
    ext_ref, wt_ref, taps_ref, dmov_ref, grad_ref, acc_ref, sem = refs[-7:]
    step, steps = pl.program_id(0), pl.num_programs(0)
    tile = taps_ref.shape[0]
    open_sums(acc_ref)

    @pl.when(step == 0)
    def _():
        copies = load_window(place_ref, low_ref, d_ref, high_ref, ext_ref, sem)
        copies.append(pltpu.make_async_copy(turned_ref, wt_ref, sem.at[3]))
        if last:
            copies.append(pltpu.make_async_copy(before_ref, grad_ref, sem.at[4]))
        for copy in copies:
            copy.start()
        if not last:
            grad_ref[...] = jnp.zeros_like(grad_ref)
        for copy in copies:
            copy.wait()

    fill_taps(taps_ref, ext_ref, mask_ref, (steps * last + step) * tile)
    for half in halves_of(tile):
        dmov_ref[half, :] = lax.dot_general(
            taps_ref[half, :], wt_ref[...], NN, preferred_element_type=F32
        )

    def work(rows, _):
        live = mask_ref[rows, MID : MID + 1]
        sums = [0.0, 0.0]
        for b in lane_blocks(INNER):
            xhat = xhat_ref[rows, b].astype(F32)
            dy = dmov_ref[rows, b] * live * slope_ref[rows, b].astype(F32)
            add_terms(acc_ref, b, dy, xhat)
            dxhat = dy * np_ref[0:1, D + b.start : D + b.stop]
            dmov_ref[rows, b] = dxhat
            sums = [sums[0] + dxhat, sums[1] + dxhat * xhat]
        return row_means(sums, INNER) + [rstd_ref[rows, :]]

    def finish(rows, means):
        def put(b, value):
            dpre_ref[rows, b] = value.astype(BF16)

        norm_back(rows, dmov_ref, xhat_ref, means, put)

    in_stages(tile, [work, finish])
    close_sums(sums_ref, acc_ref)
    grad_ref[...] += lax.dot_general(dpre_ref[...], hid_ref[...], TN, preferred_element_type=F32)

    @pl.when(step == steps - 1)
    def _():
        if last:
            all_blocks = slice(0, INNER // LANE)
            stage_turned(stage_ref, lax.rem(place_ref[0], 2), grad_ref, rows_in, 0, all_blocks)
            used = rows_in // SUB * (INNER // LANE)
            run_copies(stage_copies(stage_ref, keep_ref, send_ref, used, sem, 0))
        else:
            run_copies([pltpu.make_async_copy(grad_ref, part_ref, sem.at[0])])


def back_a_kernel(pieces, half, place_ref, dpre0_ref, dpre1_ref, xhat_ref, rstd_ref, slope_ref, cot_ref, np_ref, *refs):
    piece_refs = refs[:pieces]
    grad_ref, sums_ref, w_ref, wt_ref, dh_ref, acc_ref, sem = refs[-7:]
    open_sums(acc_ref)

    @pl.when(pl.program_id(0) == 0)
    def _():
        run_copies(piece_copies(piece_refs, w_ref, place_ref[0], sem))
        for k in range(0, D, 256):
            wt_ref[:, k : k + 256] = jnp.transpose(w_ref[k : k + 256, :])

    second = (jnp.zeros((1, 1), jnp.int32) + pl.program_id(0)) >= half
    d_pre = jnp.where(second, dpre1_ref[...], dpre0_ref[...])
    dh_ref[...] = lax.dot_general(d_pre, wt_ref[...], NN, preferred_element_type=F32)

    def work(rows, _):
        sums = [0.0, 0.0]
        for b in lane_blocks(D):
            xhat = xhat_ref[rows, b].astype(F32)
            dy = dh_ref[rows, b] * slope_ref[rows, b].astype(F32)
            add_terms(acc_ref, b, dy, xhat)
            dxhat = dy * np_ref[0:1, b]
            dh_ref[rows, b] = dxhat
            sums = [sums[0] + dxhat, sums[1] + dxhat * xhat]
        return row_means(sums, D) + [rstd_ref[rows, :]]

    def finish(rows, means):
        def put(b, value):
            grad_ref[rows, b] = cot_ref[rows, b].astype(F32) + value

        norm_back(rows, dh_ref, xhat_ref, means, put)

    in_stages(dpre0_ref.shape[0], [work, finish])
    close_sums(sums_ref, acc_ref)


def out_kernel(pieces, place_ref, hid_ref, tok_ref, *refs):
    piece_refs = refs[:pieces]
    out_ref, w_ref, sem = refs[pieces:]

    @pl.when(pl.program_id(0) == 0)
    def _():
        run_copies(out_copies(piece_refs, w_ref, place_ref[0], sem))

    branch = lax.dot_general(hid_ref[...], w_ref[...], NN, preferred_element_type=F32)
    out_ref[...] = (tok_ref[...].astype(F32) + branch).astype(BF16)


WIDTHS = (INNER, INNER, D)
LANE0 = (0, INNER, 2 * INNER)
CUT = 2 * LANE
CHUNKS = (((1, 0, CUT), (2, 0, D)), ((1, CUT, INNER - CUT),), ((0, 0, INNER),))


def spans(chunk, rows):
    found, first = [], 0
    for weight, col, cols in chunk:
        tiles = rows[weight] // SUB * (cols // LANE)
        found.append((weight, col // LANE, cols // LANE, first, tiles))
        first += tiles
    return found, first


def column_sums(pack_ref, row, ref, chunk, rows):
    for weight, block0, blocks, first, tiles in spans(chunk, rows)[0]:

        def body(g, carry, first=first, blocks=blocks):
            new = []
            for b in range(blocks):
                value = ref[first + g * blocks + b].astype(F32)
                new.append(carry[b] + fold(value * value + 1e-30))
            return tuple(new)

        zero = tuple(jnp.zeros((8, LANE), F32) for _ in range(blocks))
        cols = lax.fori_loop(0, tiles // blocks, body, zero, unroll=5)
        for b in range(blocks):
            lane = LANE0[weight] + (block0 + b) * LANE
            pack_ref[row : row + 1, lane : lane + LANE] = jnp.sum(cols[b], axis=0, keepdims=True)


def load_full(refs, place_ref, first, full_ref, sem, at):
    pieces = refs[0].shape[0]
    each = full_ref.shape[0] // (len(refs) * pieces)
    outer = pieces if len(refs) == 2 else pieces // 2
    y = place_ref[2] % 2
    copies = []
    for n, (ref, side) in enumerate(zip(refs, (y, 1 - y))):
        for p in range(pieces):
            index = side * outer + p if len(refs) == 2 else p % 2 * outer + p // 2
            target = full_ref.at[pl.ds(index * each, each)]
            source = ref.at[p, first : first + each]
            copies.append(pltpu.make_async_copy(source, target, sem.at[at + n * pieces + p]))
    return copies


def load_list(mine_ref, other_ref, place_ref, full_ref, sem):
    me, copies = place_ref[2], []
    outer = mine_ref.shape[0]
    each = full_ref.shape[0] // (2 * outer)
    for n in range(2 * outer):
        device = me ^ (2 * (n % outer) + n // outer)
        index = lax.rem(device, 2) * outer + lax.div(device, 2)
        target = full_ref.at[pl.ds(index * each, each)]
        source = (mine_ref, other_ref)[n // outer].at[n % outer]
        copies.append(pltpu.make_async_copy(source, target, sem.at[n]))
    return copies


def pack_kernel(rows, pieces, place_ref, part_ref, *refs):
    states, sums, (pack_ref, acc_ref) = refs[0:3], refs[3:7], refs[7:9]
    pack_ref[...] = jnp.zeros_like(pack_ref)
    lanes_of = ((0, D), (D, D + INNER), (D, D + INNER), (D + INNER, D + 2 * INNER))
    for part, (lane0, lane1) in zip(sums, lanes_of):
        pack_ref[0:2, lane0:lane1] += part[...]
    lanes = lax.broadcasted_iota(jnp.int32, (1, LANE), 1)
    for k in range(3):
        total = jnp.sum(states[k][...].reshape(1, -1), axis=1, keepdims=True)
        pack_ref[3:4, 0:LANE] += jnp.where(lanes == k, total, 0.0)
    acc_ref[...] = jnp.zeros_like(acc_ref)
    spare = acc_ref.shape[0] - 1
    outer = place_ref[3] // 2
    piece = place_ref[2] % 2 * outer + place_ref[2] // 2
    at = 0
    for chunk, each in zip(CHUNKS[:2], pieces):
        found, _ = spans(chunk, rows)
        start = piece * each

        def body(k, carry, found=found, start=start, at=at):
            n = start + k
            slot = spare
            for weight, block0, blocks, first, tiles in found:
                here = LANE0[weight] // LANE + block0 + lax.rem(jnp.maximum(n - first, 0), blocks)
                slot = jnp.where((n >= first) & (n < first + tiles), here, slot)
            value = part_ref[at + k].astype(F32)
            acc_ref[slot] += value * value + 1e-30
            return carry

        lax.fori_loop(0, each, body, 0, unroll=2)
        at += each
    for slot in range(spare):
        pack_ref[2:3, slot * LANE : (slot + 1) * LANE] = jnp.sum(acc_ref[slot], axis=0, keepdims=True)


def pack_in_kernel(rows, place_ref, mine_ref, other_ref, pack_ref, full_ref, sem):
    run_copies(load_list(mine_ref, other_ref, place_ref, full_ref, sem))
    pack_ref[...] = jnp.zeros_like(pack_ref)
    column_sums(pack_ref, 0, full_ref, CHUNKS[2], rows)


def update_weight(
    k, squares, states_sum, source, weight, state, col_state, grad_ref, new, row_new_ref, col_new_ref, scratch, step=0, steps=1
):
    line_ref, state_ref, new_ref, scaled_ref = scratch
    width, fan, rows_here = WIDTHS[k], (D, KERNEL_TAPS * INNER, INNER)[k], state.shape[0]
    whole_rows = rows_here + -rows_here % LANE
    groups = rows_here // SUB // steps
    rate = 0.5 / fan**0.5

    def before():
        col_new = DECAY * col_state[...].reshape(1, -1) + (1.0 - DECAY) * (squares * (1.0 / fan))
        col_new_ref[...] = col_new.reshape(-1)
        total = DECAY * states_sum
        total = total + (1.0 - DECAY) * (1.0 / width) * jnp.sum(squares, axis=1, keepdims=True)
        scaled_ref[0:1, 0:width] = col_new / (total * (1.0 / fan))
        line_ref[0:1, 0:rows_here] = state[...].reshape(1, -1)
        for c in range(0, whole_rows, LANE):
            state_ref[c : c + LANE, :] = column(line_ref[0:1, c : c + LANE])

    def after():
        for c in range(0, whole_rows, LANE):
            line_ref[0:1, c : c + LANE] = jnp.transpose(new_ref[c : c + LANE, :])[0:1, :]
        row_new_ref[...] = line_ref[0:1, 0:rows_here].reshape(-1)

    def body(g, carry):
        here = pl.ds(pl.multiple_of(g * SUB, SUB), SUB)
        at = step * groups + g
        rows = pl.ds(pl.multiple_of(at * SUB, SUB), SUB)
        square = 0.0
        for ref, block0, blocks, first in source:
            for b in range(blocks):
                value = ref[first + at * blocks + b].astype(F32)
                grad_ref[here, (block0 + b) * LANE : (block0 + b + 1) * LANE] = value
                square = square + (value * value + 1e-30)
        mean = jnp.sum(square, axis=1, keepdims=True) * (1.0 / width)
        row_new = DECAY * state_ref[rows, :] + (1.0 - DECAY) * mean
        new_ref[rows, :] = row_new
        for ref, block0, blocks, first in source:
            for b in range(blocks):
                lanes = slice((block0 + b) * LANE, (block0 + b + 1) * LANE)
                value = ref[first + at * blocks + b].astype(F32)
                change = value * lax.rsqrt(row_new * scaled_ref[0:1, lanes])
                new[here, lanes] = weight[here, lanes] - rate * change
        return carry

    if steps == 1:
        before()
        lax.fori_loop(0, groups, body, 0, unroll=5)
        after()
    else:
        pl.when(step == 0)(before)
        lax.fori_loop(0, groups, body, 0, unroll=5)
        pl.when(step == steps - 1)(after)


def sources_of(chunk, ref, rows):
    return {w: (ref, block0, blocks, first) for w, block0, blocks, first, _ in spans(chunk, rows)[0]}


def update_kernel(rows, copies_of, place_ref, mine_ref, other_ref, pack_ref, *refs):
    weights, states, col_states = refs[0:2], refs[2:4], refs[4:6]
    grads, news, rows_new, cols_new = refs[6:8], refs[8:10], refs[10:12], refs[12:14]
    conv_scratch, out_scratch = refs[14:18], refs[18:22]
    full1_ref, full2_ref, sem = refs[22:25]
    both = (mine_ref, other_ref)
    count = 2 * mine_ref.shape[0]
    step, steps = pl.program_id(0), pl.num_programs(0)

    @pl.when(step == 0)
    def _():
        copies = load_full(both, place_ref, 0, full1_ref, sem, 0)
        copies += load_full(both, place_ref, full1_ref.shape[0] // count, full2_ref, sem, count)
        run_copies(copies)

    from1 = sources_of(CHUNKS[0], full1_ref, rows)
    from2 = sources_of(CHUNKS[1], full2_ref, rows)

    def update(n, k, source, scratch, *steps):
        squares = pack_ref[2:3, LANE0[k] : LANE0[k] + WIDTHS[k]]
        update_weight(
            k, squares, pack_ref[3:4, k : k + 1] * (1.0 / copies_of), source, weights[n],
            states[n], col_states[n], grads[n], news[n], rows_new[n], cols_new[n], scratch, *steps,
        )

    update(0, 1, [from1[1], from2[1]], conv_scratch, step, UPDATE_STEPS)

    @pl.when(step == steps - 1)
    def _():
        update(1, 2, [from1[2]], out_scratch)


def update_in_kernel(
    rows, copies_of, place_ref, mine_ref, other_ref, pack_in_ref, pack_ref, np_ref, second_ref, *refs
):
    weight, state, col_state, grad_ref, new_ref, row_new_ref, col_new_ref = refs[0:7]
    ngrad_ref, nsecond_ref, nnew_ref = refs[7:10]
    full_ref, sem = refs[14:16]
    copies = load_list(mine_ref, other_ref, place_ref, full_ref, sem)
    for copy in copies:
        copy.start()
    grad = pack_ref[0:2, :]
    second = DECAY * second_ref[...] + (1.0 - DECAY) * (grad * grad + 1e-30)
    ngrad_ref[...] = grad
    nsecond_ref[...] = second
    nnew_ref[...] = np_ref[...] - 0.2 * grad * lax.rsqrt(second)
    for copy in copies:
        copy.wait()
    update_weight(
        0, pack_in_ref[0:1, :], pack_ref[3:4, 0:1] * (1.0 / copies_of),
        [sources_of(CHUNKS[2], full_ref, rows)[0]], weight, state, col_state, grad_ref, new_ref,
        row_new_ref, col_new_ref, refs[10:14],
    )


class Places:
    def __init__(self):
        self.seq, self.fsdp = lax.axis_size("seq"), lax.axis_size("fsdp")
        self.q = lax.axis_index("fsdp")
        self.s = lax.axis_index("seq")

    def flip(self, x, axis, bit):
        pairs = []
        for s in range(self.seq):
            for f in range(self.fsdp):
                s2, f2 = (s ^ bit, f) if axis == "seq" else (s, f ^ bit)
                pairs.append((s * self.fsdp + f, s2 * self.fsdp + f2))
        return lax.ppermute(x, AXES, pairs)


def bits_of(count):
    return [1 << k for k in range(count.bit_length() - 1)]


def tie(x, *others):
    return lax.optimization_barrier((x, *others))[0]


def gather_pieces(piece, place, after, later=()):
    found = {0: piece}
    for bit in reversed(bits_of(place.fsdp)):
        for k in list(found):
            moving = found[k]
            if bit == 1:
                moving = tie(moving, *((after,) if k == 0 or not later else later))
            found[k | bit] = place.flip(moving, "fsdp", bit)
    return [found[k] for k in range(place.fsdp)]


def sum_over(x, place, *axes):
    for axis in axes:
        for bit in bits_of(getattr(place, axis)):
            x = x + place.flip(x, axis, bit)
    return x


def pick(x, index, axis):
    return lax.dynamic_index_in_dim(x, index, axis=axis, keepdims=False)


class Reduction:
    def __init__(self, place, keep, send):
        self.place, self.near = place, keep
        self.got = place.flip(send, "fsdp", 1)

    def halve(self, axis, side, flip_axis, bit):
        dims = self.near.shape
        parts = dims[:axis] + (2, dims[axis] // 2) + dims[axis + 1 :]
        near, got = self.near.reshape(parts), self.got.reshape(parts)
        away = pick(near, 1 - side, axis).astype(F32) + pick(got, 1 - side, axis).astype(F32)
        self.near = pick(near, side, axis).astype(F32) + pick(got, side, axis).astype(F32)
        away = away.astype(BF16)
        self.got = self.place.flip(away, flip_axis, bit)
        return away

    def x(self):
        bit = self.place.fsdp // 2
        while bit > 1:
            away = self.halve(0, (self.place.q // bit) % 2, "fsdp", bit)
            bit //= 2
        return away

    def y(self):
        return self.halve(1, self.place.s % 2, "seq", 1)

    def along_z(self):
        outer, z = self.place.seq // 2, self.place.s // 2
        total = self.near + self.got.astype(F32)
        total = total.reshape((outer, -1) + total.shape[2:])
        low = total.astype(BF16)
        self.near = pick(total, z, 0)
        self.got = [self.place.flip(pick(low, z ^ k, 0), "seq", 2 * k) for k in range(1, outer)]

    def piece(self):
        total = self.near
        for got in self.got:
            total = total + got.astype(F32)
        return total.astype(BF16)

    def pieces(self):
        total = (self.near + self.got.astype(F32)).astype(BF16)
        return total.reshape((self.place.seq // 2, -1) + total.shape[2:])


def arrive(result, *reductions):
    result, *gots = lax.optimization_barrier((result, *[r.got for r in reductions]))
    for reduction, got in zip(reductions, gots):
        reduction.got = got
    return result


def summed_f32(got):
    return jnp.sum(got.astype(F32), axis=0)


def summed(got):
    return summed_f32(got).astype(BF16)


def exchange(place, sent):
    line = [[y + 2 * z for z in range(place.seq // 2)] for y in range(2)]
    return lax.all_to_all(sent, "seq", 0, 0, axis_index_groups=line)


def on_device(
    tokens, input_mask, doc_lengths, cotangent, w_in, w_conv, w_out, norm_params,
    row_in, col_in, row_conv, col_conv, row_out, col_out, norm_second,
):
    place = Places()
    rows = tokens.shape[0]
    pieces = place.fsdp
    spots = jnp.stack(
        [place.q, (place.s * place.fsdp + place.q) * rows, place.s, place.seq]
    ).astype(jnp.int32)
    docs = doc_lengths.shape[0]
    live = input_mask.reshape(-1, LANE)
    weights = (w_in, w_conv, w_out)
    rows_of = [w.shape[0] for w in weights]

    tile_a, tile = 256, 512
    steps = rows // tile
    params_spec = whole(2, D + 2 * INNER)
    dma = pltpu.SemaphoreType.DMA

    out_sides = (w_out[:, : D // 2], w_out[:, D // 2 :])
    conv_out = jnp.concatenate([w_conv, *out_sides], axis=0).astype(BF16)
    hidden_a, slope_a, xhat_a, rstd_a = call(
        norm_a_kernel,
        (rows // tile_a,),
        [rows_spec(tile_a, D), params_spec],
        [rows_spec(tile_a, D)] * 3 + [rows_spec(tile_a, LANE)],
        [shape((rows, D), BF16)] * 3 + [shape((rows, LANE), F32)],
        us=17,
    )(tokens, tie(norm_params, conv_out))

    in_pieces = gather_pieces(w_in.astype(BF16), place, hidden_a)

    def in_call(tiles, count, before):
        at, stride = tiles

        def here_spec(width):
            return pl.BlockSpec((tile, width), lambda i: (at + stride * i, 0))

        out_shapes = [shape((rows, INNER), BF16)] * 3 + [shape((rows, LANE), F32)] * 2
        out_specs = [here_spec(INNER)] * 3 + [here_spec(LANE)] * 2
        if at == 0:
            out_shapes += [shape((REACH, INNER), BF16)] * 2
            out_specs += [whole(REACH, INNER)] * 2
        return call(
            functools.partial(in_kernel, pieces, tiles),
            (count,),
            [SMEM, whole(docs), here_spec(D), whole(*live.shape), params_spec]
            + [ANY] * (pieces + len(before)),
            out_specs,
            out_shapes,
            [pltpu.VMEM((D, INNER), BF16), pltpu.VMEM((tile, INNER), F32)]
            + [pltpu.VMEM((8, docs + -docs % LANE), F32), dma((pieces,))],
            us=3,
            aliases={5 + pieces + k: k for k in range(len(before))},
        )(spots, doc_lengths, hidden_a, live, norm_params, *in_pieces, *before)

    *kept, m_first, m_last = in_call((0, steps - 1), 2, ())
    moved, slope_b, xhat_b, rstd_b, masks = in_call((1, 1), steps - 2, kept)

    def halo(inner, outer):
        total = place.seq * place.fsdp
        across = [(i, i + 1 if i % 2 else i - 1) for i in range(1, total - 1)]
        return place.flip(inner, "fsdp", 1), lax.ppermute(outer, AXES, across)

    m_inner, m_outer = halo(m_first, m_last)
    conv_pieces = gather_pieces(conv_out, place, m_first, (moved, m_inner, m_outer))

    ext = pltpu.VMEM((rows + 2 * REACH, INNER), BF16)
    taps_wide = KERNEL_TAPS * INNER
    wide = pltpu.VMEM((taps_wide, INNER), BF16)
    shards = place.fsdp // 2

    def half_dims(chunk):
        count = spans(chunk, rows_of)[1]
        return (shards, count + -count % place.seq, SUB, LANE)

    def tile_spec(width, ahead):
        return pl.BlockSpec((tile, width), lambda i: (jnp.clip(i + ahead, 0, steps - 1), 0))

    halves = [half_dims(CHUNKS[0])] * 2 + [half_dims(CHUNKS[1])] * 2
    work = pltpu.VMEM((tile, INNER), F32)
    turned_tile = pltpu.VMEM((INNER, tile), BF16)
    hidden_c, d_conv, d_first, d_last, sums_c, turned, keep1, send1, keep2, send2 = call(
        functools.partial(conv_kernel, pieces, rows_of),
        (steps + 1,),
        [SMEM, ANY, ANY, ANY, tile_spec(LANE, 0), tile_spec(D, 0), tile_spec(D, -1), params_spec]
        + [ANY] * pieces,
        [tile_spec(INNER, 0)] * 2
        + [whole(REACH, INNER), whole(REACH, INNER), whole(2, INNER)]
        + [ANY] * 5,
        [
            shape((rows, INNER), BF16),
            shape((rows, INNER), BF16),
            shape((REACH, INNER), BF16),
            shape((REACH, INNER), BF16),
            shape((2, INNER), F32),
            shape((taps_wide, INNER), BF16),
        ]
        + [shape(dims, BF16) for dims in halves],
        [ext, wide, wide, pltpu.VMEM((INNER, D), BF16), pltpu.VMEM((D, INNER), BF16)]
        + [pltpu.VMEM((2, tile, taps_wide), BF16), work, work, work, turned_tile, turned_tile]
        + [pltpu.VMEM((INNER, taps_wide), F32), pltpu.VMEM((INNER, D), F32)]
        + [pltpu.VMEM((16, INNER), F32)]
        + [pltpu.VMEM((2,) + halves[0], BF16), pltpu.VMEM((2,) + halves[2], BF16)]
        + [dma((3 + 3 * pieces,))],
        us=45,
    )(
        spots, m_inner, moved, m_outer, masks, cotangent, cotangent, norm_params, *conv_pieces
    )
    d_inner, d_outer = halo(d_first, d_last)
    first, second = Reduction(place, keep1, send1), Reduction(place, keep2, send2)
    (block_out,) = call(
        functools.partial(out_kernel, pieces),
        (steps,),
        [SMEM, rows_spec(tile, INNER), rows_spec(tile, D)] + [ANY] * pieces,
        [rows_spec(tile, D)],
        [shape((rows, D), BF16)],
        [pltpu.VMEM((INNER, D), BF16), dma((2 * pieces,))],
        us=9,
    )(spots, hidden_c, tokens, *conv_pieces)

    def back_conv(last, spots, before):
        here = steps // 2
        at = here * last

        def here_spec(width):
            return pl.BlockSpec((tile, width), lambda i: (i + at, 0))

        dims = half_dims(CHUNKS[2])
        return call(
            functools.partial(back_conv_kernel, last, w_in.shape[0]),
            (here,),
            [SMEM] + [ANY] * 4
            + [here_spec(LANE), here_spec(INNER), here_spec(LANE), here_spec(INNER), here_spec(D)]
            + [params_spec]
            + [ANY] * last,
            [rows_spec(tile, INNER), whole(2, INNER)] + [ANY] * (1 + last),
            [shape((rows // 2, INNER), BF16), shape((2, INNER), F32)]
            + ([shape(dims, BF16)] * 2 if last else [shape((INNER, D), F32)]),
            ([pltpu.VMEM((2,) + dims, BF16)] if last else [])
            + [
                ext,
                wide,
                pltpu.VMEM((tile, taps_wide), BF16),
                pltpu.VMEM((tile, INNER), F32),
                pltpu.VMEM((INNER, D), F32),
                pltpu.VMEM((16, INNER), F32),
                dma((5,)),
            ],
            us=16,
        )(
            spots, d_inner, d_conv, d_outer, turned, masks, xhat_b, rstd_b, slope_b, hidden_a,
            norm_params, *before,
        )

    block_out, d_inner, d_outer = arrive((block_out, d_inner, d_outer), first, second)
    away = (first.x(), second.y())
    d_pre0, sums_b0, grad_part = back_conv(0, tie(spots, *away), ())
    d_pre0 = arrive(d_pre0, first, second)
    away = (first.y(), second.x())
    d_pre1, sums_b1, keep, send = back_conv(1, tie(spots, *away), (grad_part,))
    send = arrive(send, first, second)
    third = Reduction(place, keep, send)
    sent = jnp.concatenate([first.pieces(), second.pieces()], axis=1)
    got = exchange(place, sent)
    third.got = tie(third.got, sent)
    away = (sent, third.x())
    input_grad, sums_a = call(
        functools.partial(back_a_kernel, pieces, steps // 2),
        (steps,),
        [SMEM]
        + [
            pl.BlockSpec((tile, INNER), lambda i: (jnp.minimum(i, steps // 2 - 1), 0)),
            pl.BlockSpec((tile, INNER), lambda i: (jnp.maximum(i - steps // 2, 0), 0)),
        ]
        + [rows_spec(tile, D), rows_spec(tile, LANE), rows_spec(tile, D), rows_spec(tile, D)]
        + [params_spec]
        + [ANY] * pieces,
        [rows_spec(tile, D), whole(2, D)],
        [shape((rows, D), F32), shape((2, D), F32)],
        [
            pltpu.VMEM((D, INNER), BF16),
            pltpu.VMEM((INNER, D), BF16),
            pltpu.VMEM((tile, D), F32),
            pltpu.VMEM((16, D), F32),
            dma((pieces,)),
        ],
        us=17,
    )(
        tie(spots, *away), d_pre0, d_pre1, xhat_a, rstd_a, slope_a, cotangent, norm_params, *in_pieces
    )

    row_states, col_states = (row_in, row_conv, row_out), (col_in, col_conv, col_out)
    row_specs = [whole(*r.shape) for r in row_states]
    col_specs = [whole(*c.shape) for c in col_states]
    cols_all = D + 2 * INNER
    pack_spec = whole(4, cols_all)
    fulls = [pltpu.VMEM(half_dims(c)[1:], BF16) for c in CHUNKS]
    sums = (sums_a, sums_b0, sums_b1, sums_c)
    got, third.got, input_grad = lax.optimization_barrier((got, third.got, input_grad))
    part = summed(got)
    sent = jnp.broadcast_to(part[None], (place.seq // 2,) + part.shape)
    mine = exchange(place, sent)
    third.got = tie(third.got, sent)
    away = third.y()
    (pack,) = call(
        functools.partial(pack_kernel, rows_of, [half_dims(c)[1] // place.seq for c in CHUNKS]),
        (1,),
        [SMEM, whole(*part.shape)] + row_specs + [whole(*x.shape) for x in sums],
        [pack_spec],
        [shape((4, cols_all), F32)],
        [pltpu.VMEM((cols_all // LANE + 1, SUB, LANE), F32)],
        us=2,
        mib=16,
    )(tie(spots, away), part, *row_states, *sums)
    core_sum = pack + place.flip(pack, "fsdp", 1)
    third.got, pack = lax.optimization_barrier((third.got, core_sum))
    for bit in bits_of(place.fsdp)[1:]:
        pack = pack + place.flip(pack, "fsdp", bit)
    third.along_z()
    steps_z = range(1, place.seq // 2)
    for flipped in [place.flip(pack, "seq", 2 * k) for k in steps_z]:
        pack = pack + flipped
    mine, third.got, pack = lax.optimization_barrier((mine, third.got, pack))
    other = place.flip(mine, "seq", 1)
    line = third.piece()
    line = jnp.stack([line] + [place.flip(line, "seq", 2 * k) for k in steps_z])
    pack = pack + place.flip(pack, "seq", 1)
    line, other, pack = lax.optimization_barrier((line, other, pack))
    line_other = place.flip(line, "seq", 1)

    def update_scratch(weight):
        lines = weight.shape[0] + -weight.shape[0] % LANE
        return (
            [pltpu.VMEM((8, lines), F32)]
            + [pltpu.VMEM((lines, LANE), F32)] * 2
            + [pltpu.VMEM((8, weight.shape[1]), F32)]
        )

    weight_specs = [whole(*w.shape) for w in weights]
    conv_block = pl.BlockSpec((w_conv.shape[0] // UPDATE_STEPS, INNER), lambda i: (i, 0))
    both_specs = [conv_block, weight_specs[2]]
    results = call(
        functools.partial(update_kernel, rows_of, place.seq),
        (UPDATE_STEPS,),
        [SMEM, ANY, ANY, pack_spec] + both_specs + row_specs[1:] + col_specs[1:],
        both_specs * 2 + row_specs[1:] + col_specs[1:],
        [shape(w.shape, F32) for w in weights[1:]] * 2
        + [shape(r.shape, F32) for r in row_states[1:] + col_states[1:]],
        update_scratch(w_conv)
        + update_scratch(w_out)
        + fulls[:2]
        + [dma((2 * place.seq,))],
        us=8,
        mib=32,
    )(spots, mine, other, pack, *weights[1:], *row_states[1:], *col_states[1:])
    grad_conv, grad_out, new_conv, new_out, row_conv_new, row_out_new, col_conv_new, col_out_new = (
        results
    )
    line_other, grad_out = lax.optimization_barrier((line_other, grad_out))
    (pack_in,) = call(
        functools.partial(pack_in_kernel, rows_of),
        (1,),
        [SMEM, ANY, ANY],
        [whole(8, INNER)],
        [shape((8, INNER), F32)],
        [fulls[2], dma((place.seq,))],
        us=2,
        mib=16,
    )(spots, line, line_other)
    pack_in = sum_over(pack_in, place, "fsdp")
    grad_in, new_in, row_in_new, col_in_new, *norm_results = call(
        functools.partial(update_in_kernel, rows_of, place.seq),
        (1,),
        [SMEM, ANY, ANY, whole(8, INNER), pack_spec, params_spec, params_spec]
        + [weight_specs[0], row_specs[0], col_specs[0]],
        [weight_specs[0]] * 2 + [row_specs[0], col_specs[0]] + [params_spec] * 3,
        [shape(w_in.shape, F32)] * 2
        + [shape(row_in.shape, F32), shape(col_in.shape, F32)]
        + [shape((2, cols_all), F32)] * 3,
        update_scratch(w_in) + [fulls[2], dma((place.seq,))],
        us=4,
        mib=24,
    )(
        spots, line, line_other, pack_in, pack, norm_params, norm_second, w_in, row_in, col_in
    )
    return (
        block_out,
        input_grad,
        grad_in,
        grad_conv,
        grad_out,
        new_in,
        new_conv,
        new_out,
        row_in_new,
        col_in_new,
        row_conv_new,
        col_conv_new,
        row_out_new,
        col_out_new,
        *norm_results,
    )


def solution(mesh):
    both, rows = P(AXES, None), P("fsdp", None)
    in_specs = (
        both, P(AXES), P(), both, rows, rows, rows, P(),
        P("fsdp"), P(), P("fsdp"), P(), P("fsdp"), P(), P(),
    )
    out_specs = (
        both, both, rows, rows, rows, rows, rows, rows,
        P("fsdp"), P(), P("fsdp"), P(), P("fsdp"), P(), P(), P(), P(),
    )
    return jax.shard_map(
        on_device, mesh=mesh, in_specs=in_specs, out_specs=out_specs, check_vma=False
    )
```

```python
import functools
import math

import jax
import jax.numpy as jnp
from jax import lax
from jax.experimental import pallas as pl
from jax.experimental.pallas import tpu as pltpu
from jax.sharding import PartitionSpec as P

D = 1280
INNER = 640
KERNEL_TAPS = 5
DILATION_STEP = 128
STEP = 10
EPSILON = 1e-05
DECAY = 1.0 - STEP ** (-0.8)

REACH = (KERNEL_TAPS - 1) // 2 * DILATION_STEP
MID = (KERNEL_TAPS - 1) // 2
F32 = jnp.float32
BF16 = jnp.bfloat16
SUB, LANE = 16, 128
AXES = ("seq", "fsdp")
NT = (((1,), (1,)), ((), ()))
TN = (((0,), (0,)), ((), ()))
NN = (((1,), (0,)), ((), ()))


def call(kernel, grid, in_specs, out_specs, out_shape, scratch=(), us=1.0, aliases=None, mib=58):
    params = pltpu.CompilerParams(
        vmem_limit_bytes=mib * 1024 * 1024, dimension_semantics=("arbitrary",) * len(grid)
    )
    return pl.pallas_call(
        kernel,
        grid=grid,
        in_specs=in_specs,
        out_specs=out_specs,
        out_shape=out_shape,
        scratch_shapes=list(scratch),
        compiler_params=params,
        input_output_aliases=aliases or {},
        cost_estimate=pl.CostEstimate(
                flops=int(us * 1.1e9), bytes_accessed=int(us * 3.4e6), transcendentals=0
        ),
    )


def shape(dims, dtype):
    return jax.ShapeDtypeStruct(dims, dtype)


def rows_spec(tile, width):
    return pl.BlockSpec((tile, width), lambda i: (i, 0))


def whole(*dims):
    return pl.BlockSpec(dims, lambda *_: (0,) * len(dims))


ANY = pl.BlockSpec(memory_space=pl.ANY)
SMEM = pl.BlockSpec(memory_space=pltpu.SMEM)


ERFC_P = 0.47 / math.sqrt(2.0)
ERFC_C = (
    0.12357219400743558,
    0.1999878668208835,
    -0.08033356004356296,
    0.3660253986657854,
    -0.1092519747040215,
)
LOG2E = 1.4426950408889634


def gelu_and_slope(y):
    t = pltpu.reciprocal(1.0 + ERFC_P * jnp.abs(y), approx=True)
    bell = jnp.exp2(y * y * (-0.5 * LOG2E))
    poly = ERFC_C[4] * t + ERFC_C[3]
    for c in ERFC_C[2::-1]:
        poly = poly * t + c
    tail = poly * t * bell
    cdf = jnp.where(y > 0.0, 1.0 - tail, tail)
    return y * cdf, cdf + y * (bell * (1.0 / math.sqrt(2.0 * math.pi)))


def lane_blocks(width):
    return [slice(k, k + LANE) for k in range(0, width, LANE)]


def row_stats(ref, rows):
    width = ref.shape[-1]
    blocks = lane_blocks(width)
    total = ref[rows, blocks[0]].astype(F32)
    for b in blocks[1:]:
        total = total + ref[rows, b].astype(F32)
    mean = jnp.sum(total, axis=-1, keepdims=True) * (1.0 / width)
    square = None
    for b in blocks:
        centered = ref[rows, b].astype(F32) - mean
        square = centered * centered if square is None else square + centered * centered
    variance = jnp.sum(square, axis=-1, keepdims=True) * (1.0 / width)
    return mean, lax.rsqrt(variance + EPSILON)


def fold(values):
    total = values[0:8]
    for k in range(8, values.shape[0], 8):
        total = total + values[k : k + 8]
    return total


def in_stages(count, stages, between=()):
    chunks = [slice(k, k + CHUNK) for k in range(0, count, CHUNK)]
    kept, rounds = {}, len(chunks) + len(stages) - 1
    for t in range(rounds):
        for n, stage in enumerate(stages):
            if 0 <= t - n < len(chunks):
                kept[n, t - n] = stage(chunks[t - n], kept.get((n - 1, t - n)))
        for work in between[t * len(between) // rounds : (t + 1) * len(between) // rounds]:
            work()


def halves_of(count):
    return (slice(0, count // 2), slice(count // 2, count))


def row_means(sums, width):
    return [jnp.sum(x, axis=-1, keepdims=True) * (1.0 / width) for x in sums]


def norm_back(rows, dxhat_ref, xhat_ref, means, put):
    mean_d, mean_dx, rstd = means
    for b in lane_blocks(dxhat_ref.shape[-1]):
        xhat = xhat_ref[rows, b].astype(F32)
        put(b, (dxhat_ref[rows, b] - mean_d - xhat * mean_dx) * rstd)


def add_terms(acc_ref, b, dy, xhat):
    acc_ref[0:8, b] += fold(dy * xhat)
    acc_ref[8:16, b] += fold(dy)


def open_sums(acc_ref):
    @pl.when(pl.program_id(0) == 0)
    def _():
        acc_ref[...] = jnp.zeros_like(acc_ref)


def close_sums(out_ref, acc_ref):
    @pl.when(pl.program_id(0) == pl.num_programs(0) - 1)
    def _():
        out_ref[0:1, :] = jnp.sum(acc_ref[0:8, :], axis=0, keepdims=True)
        out_ref[1:2, :] = jnp.sum(acc_ref[8:16, :], axis=0, keepdims=True)


def run_copies(copies):
    for copy in copies:
        copy.start()
    for copy in copies:
        copy.wait()


def piece_copies(pieces, full_ref, me, sem, first=0):
    each = full_ref.shape[0] // len(pieces)
    return [
        pltpu.make_async_copy(
            piece.at[0:each, :],
            full_ref.at[pl.ds(pl.multiple_of((me ^ k) * each, SUB), each), :],
            sem.at[first + k],
        )
        for k, piece in enumerate(pieces)
    ]


def out_copies(pieces, full_ref, me, sem, first=0):
    each, width = full_ref.shape[0] // len(pieces), full_ref.shape[1] // 2
    copies = []
    for k, piece in enumerate(pieces):
        rows = pl.ds(pl.multiple_of((me ^ k) * each, SUB), each)
        for side in range(2):
            at = piece.shape[0] - (2 - side) * each
            copies.append(
                pltpu.make_async_copy(
                    piece.at[at : at + each, :],
                    full_ref.at[rows, side * width : (side + 1) * width],
                    sem.at[first + 2 * k + side],
                )
            )
    return copies


def column(row):
    return jnp.transpose(jnp.broadcast_to(row, (LANE, LANE)))


CHUNK = 64
UPDATE_STEPS = 5
TURNED = 2


def norm_a_kernel(tok_ref, np_ref, hid_ref, slope_ref, xhat_ref, rstd_ref):
    def stats(rows, _):
        mean, rstd = row_stats(tok_ref, rows)
        rstd_ref[rows, :] = jnp.broadcast_to(rstd, (CHUNK, LANE))
        return mean, rstd

    def work(rows, kept):
        mean, rstd = kept
        for b in lane_blocks(D):
            xhat = (tok_ref[rows, b].astype(F32) - mean) * rstd
            hidden, slope = gelu_and_slope(xhat * np_ref[0:1, b] + np_ref[1:2, b])
            hid_ref[rows, b] = hidden.astype(BF16)
            slope_ref[rows, b] = slope.astype(BF16)
            xhat_ref[rows, b] = xhat.astype(BF16)

    in_stages(tok_ref.shape[0], [stats, work])


def running_ends(ends_ref, lengths_ref):
    docs, width = lengths_ref.shape[0], ends_ref.shape[1]
    ends_ref[...] = jnp.zeros_like(ends_ref)
    ends_ref[0:1, 0:docs] = lengths_ref[...].reshape(1, -1).astype(F32)
    before = jnp.zeros((1, 1), F32)
    row = lax.broadcasted_iota(jnp.int32, (LANE, LANE), 0)
    lane = lax.broadcasted_iota(jnp.int32, (LANE, LANE), 1)
    for k in range(0, width, LANE):
        line = ends_ref[0:1, k : k + LANE]
        sums = jnp.sum(jnp.where(row <= lane, column(line), 0.0), axis=0, keepdims=True) + before
        ends_ref[0:1, k : k + LANE] = jnp.where(lane[0:1] + k < docs, sums, 1e9)
        before = before + jnp.sum(line, axis=1, keepdims=True)


def in_kernel(pieces, tiles, place_ref, lengths_ref, hid_ref, live_ref, np_ref, *refs):
    piece_refs = refs[:pieces]
    edges = tiles[0] == 0
    outs = refs[-(11 if edges else 9) :]
    mov_ref, slope_ref, xhat_ref, rstd_ref, mask_ref = outs[:5]
    w_ref, pre_ref, ends_ref, sem = outs[-4:]
    step = pl.program_id(0)
    tile = hid_ref.shape[0]

    @pl.when(step == 0)
    def _():
        copies = piece_copies(piece_refs, w_ref, place_ref[0], sem)
        for copy in copies:
            copy.start()
        running_ends(ends_ref, lengths_ref)
        for copy in copies:
            copy.wait()

    for half in halves_of(tile):
        pre_ref[half, :] = lax.dot_general(
            hid_ref[half, :], w_ref[...], NN, preferred_element_type=F32
        )

    at_tile = tiles[0] + step * tiles[1]
    first = place_ref[1] + at_tile * tile
    ends = ends_ref[0:1, :]
    lanes = lax.broadcasted_iota(jnp.int32, (LANE, LANE), 1)
    offsets = ((lanes - MID) * DILATION_STEP).astype(F32)
    for k in range(tile // LANE):
        at = (first + k * LANE + lax.broadcasted_iota(jnp.int32, (LANE, 1), 0)).astype(F32)
        begin = jnp.max(jnp.where(ends <= at, ends, 0.0), axis=1, keepdims=True)
        end = jnp.min(jnp.where(ends > at, ends, 1e9), axis=1, keepdims=True)
        there = at + offsets
        same = jnp.where((there >= begin) & (there < end), 1.0, 0.0)
        live = column(live_ref[pl.ds(at_tile * (tile // LANE) + k, 1), :].astype(F32))
        mask_ref[k * LANE : (k + 1) * LANE, :] = jnp.where(lanes == MID, live, same)

    def stats(rows, _):
        mean, rstd = row_stats(pre_ref, rows)
        rstd_ref[rows, :] = jnp.broadcast_to(rstd, (CHUNK, LANE))
        return mean, rstd

    def work(rows, kept):
        mean, rstd = kept
        live = mask_ref[rows, MID : MID + 1]
        for b in lane_blocks(INNER):
            gains = slice(D + b.start, D + b.stop)
            xhat = (pre_ref[rows, b] - mean) * rstd
            hidden, slope = gelu_and_slope(xhat * np_ref[0:1, gains] + np_ref[1:2, gains])
            mov_ref[rows, b] = (hidden * live).astype(BF16)
            slope_ref[rows, b] = slope.astype(BF16)
            xhat_ref[rows, b] = xhat.astype(BF16)

    in_stages(tile, [stats, work])
    if edges:
        put_edges(place_ref, outs[5], outs[6], mov_ref, step == 0, step == 1)


def load_window(place_ref, inner, mid, outer, ext_ref, sem):
    rows, core = mid.shape[0], lax.rem(place_ref[0], 2)
    near = pl.multiple_of((1 - core) * (REACH + rows), SUB)
    far = pl.multiple_of(core * (REACH + rows), SUB)
    return [
        pltpu.make_async_copy(inner, ext_ref.at[pl.ds(near, REACH), :], sem.at[0]),
        pltpu.make_async_copy(mid, ext_ref.at[REACH : REACH + rows, :], sem.at[1]),
        pltpu.make_async_copy(outer, ext_ref.at[pl.ds(far, REACH), :], sem.at[2]),
    ]


def put_edges(place_ref, inner_ref, outer_ref, tile_ref, at_first, at_last):
    rows, core = tile_ref.shape[0], lax.rem(place_ref[0], 2)
    for at, edge, first in ((at_first, slice(0, REACH), 0), (at_last, slice(rows - REACH, rows), 1)):

        @pl.when(at & (core == first))
        def _(edge=edge):
            outer_ref[...] = tile_ref[edge, :]

        @pl.when(at & (core != first))
        def _(edge=edge):
            inner_ref[...] = tile_ref[edge, :]


def fill_taps(taps_ref, ext_ref, mask_ref, start):
    tile = taps_ref.shape[0]
    for j in range(KERNEL_TAPS):
        rows = pl.ds(pl.multiple_of(start + j * DILATION_STEP, DILATION_STEP), tile)
        picked = ext_ref[rows, :]
        if j != MID:
            picked = picked * mask_ref[:, j : j + 1].astype(BF16)
        taps_ref[:, j * INNER : (j + 1) * INNER] = picked


def conv_kernel(
    pieces, rows_of, place_ref, low_ref, mov_ref, high_ref, mask_ref, cot_ref, before_ref, np_ref, *refs
):
    piece_refs = refs[:pieces]
    hid_ref, dconv_ref, inner_ref, outer_ref, sums_ref, turned_ref = refs[pieces : pieces + 6]
    outs = refs[pieces + 6 : pieces + 10]
    ext_ref, wc_ref, wct_ref, wo_ref, wt_ref, taps_ref, pre_ref, dh_ref, xhat_ref = refs[
        pieces + 10 : pieces + 19
    ]
    dt_ref, ht_ref, gc_ref, go_ref, acc_ref, stage1_ref, stage2_ref, sem = refs[pieces + 19 :]
    step, steps = pl.program_id(0), pl.num_programs(0) - 1
    tile = taps_ref.shape[1]
    slot = lax.rem(step, 2)

    @pl.when(step == 0)
    def _():
        me = place_ref[0]
        outs = out_copies(piece_refs, wo_ref, me, sem, 3)
        rest = load_window(place_ref, low_ref, mov_ref, high_ref, ext_ref, sem)
        rest += piece_copies(piece_refs, wc_ref, me, sem, 3 + 2 * pieces)
        for copy in outs + rest:
            copy.start()
        for ref in (acc_ref, gc_ref, go_ref):
            ref[...] = jnp.zeros_like(ref)
        for copy in outs:
            copy.wait()
        for k in range(0, D, 256):
            wt_ref[k : k + 256, :] = jnp.transpose(wo_ref[:, k : k + 256])
        for copy in rest:
            copy.wait()

    def grad_conv(cols):
        def work():
            gc_ref[:, cols] += lax.dot_general(
                dt_ref[...], taps_ref[1 - slot, :, cols], NN, preferred_element_type=F32
            )

        return work

    def grad_out(cols):
        def work():
            go_ref[:, cols] += lax.dot_general(
                ht_ref[...], before_ref[:, cols], NN, preferred_element_type=F32
            )

        return work

    taps_wide = KERNEL_TAPS * INNER
    products = [grad_conv(slice(k, min(k + 768, taps_wide))) for k in range(0, taps_wide, 768)]
    products += [grad_out(slice(k, min(k + 768, D))) for k in range(0, D, 768)]

    def tile_work(products, turned):
        fill_taps(taps_ref.at[slot], ext_ref, mask_ref, step * tile)
        pre_ref[...] = lax.dot_general(
            taps_ref[slot], wc_ref[...], NN, preferred_element_type=F32
        )
        dh_ref[...] = lax.dot_general(cot_ref[...], wt_ref[...], NN, preferred_element_type=F32)
        for n in range(turned):
            tap = jnp.minimum(turned * (step - 1) + n, KERNEL_TAPS - 1)
            source = wc_ref[pl.ds(pl.multiple_of(tap * INNER, SUB), INNER), :]
            target = pl.multiple_of((KERNEL_TAPS - 1 - tap) * INNER, SUB)
            wct_ref[pl.ds(target, INNER), :] = jnp.transpose(source)

        def stats(rows, _):
            return row_stats(pre_ref, rows)

        def work(rows, kept):
            mean, rstd = kept
            sums = [0.0, 0.0]
            for b in lane_blocks(INNER):
                gains = slice(D + INNER + b.start, D + INNER + b.stop)
                gain = np_ref[0:1, gains]
                xhat = (pre_ref[rows, b] - mean) * rstd
                hidden, slope = gelu_and_slope(xhat * gain + np_ref[1:2, gains])
                hid_ref[rows, b] = hidden.astype(BF16)
                dy = dh_ref[rows, b] * slope
                add_terms(acc_ref, b, dy, xhat)
                dxhat = dy * gain
                xhat_ref[rows, b] = xhat
                dh_ref[rows, b] = dxhat
                sums = [sums[0] + dxhat, sums[1] + dxhat * xhat]
            return row_means(sums, INNER) + [rstd]

        def finish(rows, means):
            def put(b, value):
                dconv_ref[rows, b] = value.astype(BF16)

            norm_back(rows, dh_ref, xhat_ref, means, put)

        in_stages(tile, [stats, work, finish], products)
        dt_ref[...] = jnp.transpose(dconv_ref[...])
        ht_ref[...] = jnp.transpose(hid_ref[...])

    @pl.when(step == 0)
    def _():
        tile_work([], 0)

    @pl.when((step > 0) & (step < steps))
    def _():
        tile_work(products, TURNED)

    put_edges(place_ref, inner_ref, outer_ref, dconv_ref, step == 0, step == steps - 1)

    @pl.when(step == steps)
    def _():
        copy = pltpu.make_async_copy(wct_ref, turned_ref, sem.at[4])
        copy.start()
        for work in products:
            work()
        core = lax.rem(place_ref[0], 2)
        _, rows_conv, rows_out = rows_of
        stage_turned(stage1_ref, core, gc_ref, rows_conv, 0, slice(0, CUT // LANE))
        first_tiles = rows_conv // SUB * (CUT // LANE)
        stage_plain(stage1_ref, core, go_ref, rows_out, first_tiles)
        copies = stage_copies(stage1_ref, outs[0], outs[1], spans(CHUNKS[0], rows_of)[1], sem, 0)
        for each in copies:
            each.start()
        stage_turned(stage2_ref, core, gc_ref, rows_conv, 0, slice(CUT // LANE, INNER // LANE))
        more = stage_copies(stage2_ref, outs[2], outs[3], spans(CHUNKS[1], rows_of)[1], sem, 2)
        for each in more:
            each.start()
        for each in copies + more + [copy]:
            each.wait()
        sums_ref[0:1, :] = jnp.sum(acc_ref[0:8, :], axis=0, keepdims=True)
        sums_ref[1:2, :] = jnp.sum(acc_ref[8:16, :], axis=0, keepdims=True)


def stage_tiles(stage_ref, core, first_row, rows_each, base, block0, blocks, value):
    for g in range(value.shape[0] // SUB):
        row = first_row + g * SUB
        owner, inside = row // rows_each, row % rows_each // SUB
        side = core ^ (owner % 2)
        for b in range(value.shape[1] // LANE):
            tile = value[g * SUB : (g + 1) * SUB, b * LANE : (b + 1) * LANE]
            at = base + inside * blocks + block0 + b
            stage_ref[side, owner // 2, at] = tile.astype(BF16)


def stage_plain(stage_ref, core, grad_ref, rows_each, base):
    blocks = grad_ref.shape[1] // LANE
    for row in range(0, grad_ref.shape[0], SUB):
        part = grad_ref[row : row + SUB, :]
        stage_tiles(stage_ref, core, row, rows_each, base, 0, blocks, part)


def stage_turned(stage_ref, core, turned_ref, rows_each, base, blocks):
    count = blocks.stop - blocks.start
    for row in range(0, turned_ref.shape[1], LANE):
        for b in range(count):
            at = (blocks.start + b) * LANE
            part = jnp.transpose(turned_ref[at : at + LANE, row : row + LANE].astype(BF16))
            stage_tiles(stage_ref, core, row, rows_each, base, b, count, part)


def stage_copies(stage_ref, keep_ref, send_ref, used, sem, first):
    count = stage_ref.shape[2]
    if used < count:
        dims = stage_ref.shape[:2] + (count - used, SUB, LANE)
        stage_ref[:, :, used:] = jnp.zeros(dims, BF16)
    return [
        pltpu.make_async_copy(stage_ref.at[n], ref, sem.at[first + n])
        for n, ref in enumerate((keep_ref, send_ref))
    ]


def back_conv_kernel(
    last, rows_in, place_ref, low_ref, d_ref, high_ref, turned_ref, mask_ref, xhat_ref, rstd_ref, slope_ref, hid_ref, np_ref, *refs
):
    if last:
        before_ref, dpre_ref, sums_ref, keep_ref, send_ref, stage_ref = refs[:6]
    else:
        dpre_ref, sums_ref, part_ref = refs[:3]
    ext_ref, wt_ref, taps_ref, dmov_ref, grad_ref, acc_ref, sem = refs[-7:]
    step, steps = pl.program_id(0), pl.num_programs(0)
    tile = taps_ref.shape[0]
    open_sums(acc_ref)

    @pl.when(step == 0)
    def _():
        copies = load_window(place_ref, low_ref, d_ref, high_ref, ext_ref, sem)
        copies.append(pltpu.make_async_copy(turned_ref, wt_ref, sem.at[3]))
        if last:
            copies.append(pltpu.make_async_copy(before_ref, grad_ref, sem.at[4]))
        for copy in copies:
            copy.start()
        if not last:
            grad_ref[...] = jnp.zeros_like(grad_ref)
        for copy in copies:
            copy.wait()

    fill_taps(taps_ref, ext_ref, mask_ref, (steps * last + step) * tile)
    for half in halves_of(tile):
        dmov_ref[half, :] = lax.dot_general(
            taps_ref[half, :], wt_ref[...], NN, preferred_element_type=F32
        )

    def work(rows, _):
        live = mask_ref[rows, MID : MID + 1]
        sums = [0.0, 0.0]
        for b in lane_blocks(INNER):
            xhat = xhat_ref[rows, b].astype(F32)
            dy = dmov_ref[rows, b] * live * slope_ref[rows, b].astype(F32)
            add_terms(acc_ref, b, dy, xhat)
            dxhat = dy * np_ref[0:1, D + b.start : D + b.stop]
            dmov_ref[rows, b] = dxhat
            sums = [sums[0] + dxhat, sums[1] + dxhat * xhat]
        return row_means(sums, INNER) + [rstd_ref[rows, :]]

    def finish(rows, means):
        def put(b, value):
            dpre_ref[rows, b] = value.astype(BF16)

        norm_back(rows, dmov_ref, xhat_ref, means, put)

    in_stages(tile, [work, finish])
    close_sums(sums_ref, acc_ref)
    grad_ref[...] += lax.dot_general(dpre_ref[...], hid_ref[...], TN, preferred_element_type=F32)

    @pl.when(step == steps - 1)
    def _():
        if last:
            all_blocks = slice(0, INNER // LANE)
            stage_turned(stage_ref, lax.rem(place_ref[0], 2), grad_ref, rows_in, 0, all_blocks)
            used = rows_in // SUB * (INNER // LANE)
            run_copies(stage_copies(stage_ref, keep_ref, send_ref, used, sem, 0))
        else:
            run_copies([pltpu.make_async_copy(grad_ref, part_ref, sem.at[0])])


def back_a_kernel(pieces, half, place_ref, dpre0_ref, dpre1_ref, xhat_ref, rstd_ref, slope_ref, cot_ref, np_ref, *refs):
    piece_refs = refs[:pieces]
    grad_ref, sums_ref, w_ref, wt_ref, dh_ref, acc_ref, sem = refs[-7:]
    open_sums(acc_ref)

    @pl.when(pl.program_id(0) == 0)
    def _():
        run_copies(piece_copies(piece_refs, w_ref, place_ref[0], sem))
        for k in range(0, D, 256):
            wt_ref[:, k : k + 256] = jnp.transpose(w_ref[k : k + 256, :])

    second = (jnp.zeros((1, 1), jnp.int32) + pl.program_id(0)) >= half
    d_pre = jnp.where(second, dpre1_ref[...], dpre0_ref[...])
    dh_ref[...] = lax.dot_general(d_pre, wt_ref[...], NN, preferred_element_type=F32)

    def work(rows, _):
        sums = [0.0, 0.0]
        for b in lane_blocks(D):
            xhat = xhat_ref[rows, b].astype(F32)
            dy = dh_ref[rows, b] * slope_ref[rows, b].astype(F32)
            add_terms(acc_ref, b, dy, xhat)
            dxhat = dy * np_ref[0:1, b]
            dh_ref[rows, b] = dxhat
            sums = [sums[0] + dxhat, sums[1] + dxhat * xhat]
        return row_means(sums, D) + [rstd_ref[rows, :]]

    def finish(rows, means):
        def put(b, value):
            grad_ref[rows, b] = cot_ref[rows, b].astype(F32) + value

        norm_back(rows, dh_ref, xhat_ref, means, put)

    in_stages(dpre0_ref.shape[0], [work, finish])
    close_sums(sums_ref, acc_ref)


def out_kernel(pieces, place_ref, hid_ref, tok_ref, *refs):
    piece_refs = refs[:pieces]
    out_ref, w_ref, sem = refs[pieces:]

    @pl.when(pl.program_id(0) == 0)
    def _():
        run_copies(out_copies(piece_refs, w_ref, place_ref[0], sem))

    branch = lax.dot_general(hid_ref[...], w_ref[...], NN, preferred_element_type=F32)
    out_ref[...] = (tok_ref[...].astype(F32) + branch).astype(BF16)


WIDTHS = (INNER, INNER, D)
LANE0 = (0, INNER, 2 * INNER)
CUT = 2 * LANE
CHUNKS = (((1, 0, CUT), (2, 0, D)), ((1, CUT, INNER - CUT),), ((0, 0, INNER),))


def spans(chunk, rows):
    found, first = [], 0
    for weight, col, cols in chunk:
        tiles = rows[weight] // SUB * (cols // LANE)
        found.append((weight, col // LANE, cols // LANE, first, tiles))
        first += tiles
    return found, first


def column_sums(pack_ref, row, ref, chunk, rows):
    for weight, block0, blocks, first, tiles in spans(chunk, rows)[0]:

        def body(g, carry, first=first, blocks=blocks):
            new = []
            for b in range(blocks):
                value = ref[first + g * blocks + b].astype(F32)
                new.append(carry[b] + fold(value * value + 1e-30))
            return tuple(new)

        zero = tuple(jnp.zeros((8, LANE), F32) for _ in range(blocks))
        cols = lax.fori_loop(0, tiles // blocks, body, zero, unroll=5)
        for b in range(blocks):
            lane = LANE0[weight] + (block0 + b) * LANE
            pack_ref[row : row + 1, lane : lane + LANE] = jnp.sum(cols[b], axis=0, keepdims=True)


def load_full(refs, place_ref, first, full_ref, sem, at):
    pieces = refs[0].shape[0]
    each = full_ref.shape[0] // (len(refs) * pieces)
    outer = pieces if len(refs) == 2 else pieces // 2
    y = place_ref[2] % 2
    copies = []
    for n, (ref, side) in enumerate(zip(refs, (y, 1 - y))):
        for p in range(pieces):
            index = side * outer + p if len(refs) == 2 else p % 2 * outer + p // 2
            target = full_ref.at[pl.ds(index * each, each)]
            source = ref.at[p, first : first + each]
            copies.append(pltpu.make_async_copy(source, target, sem.at[at + n * pieces + p]))
    return copies


def load_list(bits, mine_ref, other_ref, place_ref, full_ref, sem):
    me, copies = place_ref[2], []
    each = full_ref.shape[0] // (1 << len(bits))
    inner = mine_ref.shape[0]
    for n in range(2 * inner):
        ref, at, k = (mine_ref, other_ref)[n // inner], n % inner, 0
        for i, bit in enumerate(bits):
            if n >> (len(bits) - 1 - i) & 1:
                k |= bit
        device, index = me ^ k, 0
        for bit in sorted(bits):
            index = index * 2 + lax.rem(lax.div(device, bit), 2)
        target = full_ref.at[pl.ds(index * each, each)]
        copies.append(pltpu.make_async_copy(ref.at[at], target, sem.at[n]))
    return copies


def pack_kernel(rows, pieces, place_ref, part_ref, *refs):
    states, sums, (pack_ref, acc_ref) = refs[0:3], refs[3:7], refs[7:9]
    pack_ref[...] = jnp.zeros_like(pack_ref)
    lanes_of = ((0, D), (D, D + INNER), (D, D + INNER), (D + INNER, D + 2 * INNER))
    for part, (lane0, lane1) in zip(sums, lanes_of):
        pack_ref[0:2, lane0:lane1] += part[...]
    lanes = lax.broadcasted_iota(jnp.int32, (1, LANE), 1)
    for k in range(3):
        total = jnp.sum(states[k][...].reshape(1, -1), axis=1, keepdims=True)
        pack_ref[3:4, 0:LANE] += jnp.where(lanes == k, total, 0.0)
    acc_ref[...] = jnp.zeros_like(acc_ref)
    spare = acc_ref.shape[0] - 1
    outer = place_ref[3] // 2
    piece = place_ref[2] % 2 * outer + place_ref[2] // 2
    at = 0
    for chunk, each in zip(CHUNKS[:2], pieces):
        found, _ = spans(chunk, rows)
        start = piece * each

        def body(k, carry, found=found, start=start, at=at):
            n = start + k
            slot = spare
            for weight, block0, blocks, first, tiles in found:
                here = LANE0[weight] // LANE + block0 + lax.rem(jnp.maximum(n - first, 0), blocks)
                slot = jnp.where((n >= first) & (n < first + tiles), here, slot)
            value = part_ref[at + k].astype(F32)
            acc_ref[slot] += value * value + 1e-30
            return carry

        lax.fori_loop(0, each, body, 0, unroll=2)
        at += each
    for slot in range(spare):
        pack_ref[2:3, slot * LANE : (slot + 1) * LANE] = jnp.sum(acc_ref[slot], axis=0, keepdims=True)


def pack_in_kernel(rows, bits, place_ref, mine_ref, other_ref, pack_ref, full_ref, sem):
    run_copies(load_list(bits, mine_ref, other_ref, place_ref, full_ref, sem))
    pack_ref[...] = jnp.zeros_like(pack_ref)
    column_sums(pack_ref, 0, full_ref, CHUNKS[2], rows)


def update_weight(
    k, squares, states_sum, source, weight, state, col_state, grad_ref, new, row_new_ref, col_new_ref, scratch, step=0, steps=1
):
    line_ref, state_ref, new_ref, scaled_ref = scratch
    width, fan, rows_here = WIDTHS[k], (D, KERNEL_TAPS * INNER, INNER)[k], state.shape[0]
    whole_rows = rows_here + -rows_here % LANE
    groups = rows_here // SUB // steps
    rate = 0.5 / fan**0.5

    def before():
        col_new = DECAY * col_state[...].reshape(1, -1) + (1.0 - DECAY) * (squares * (1.0 / fan))
        col_new_ref[...] = col_new.reshape(-1)
        total = DECAY * states_sum
        total = total + (1.0 - DECAY) * (1.0 / width) * jnp.sum(squares, axis=1, keepdims=True)
        scaled_ref[0:1, 0:width] = col_new / (total * (1.0 / fan))
        line_ref[0:1, 0:rows_here] = state[...].reshape(1, -1)
        for c in range(0, whole_rows, LANE):
            state_ref[c : c + LANE, :] = column(line_ref[0:1, c : c + LANE])

    def after():
        for c in range(0, whole_rows, LANE):
            line_ref[0:1, c : c + LANE] = jnp.transpose(new_ref[c : c + LANE, :])[0:1, :]
        row_new_ref[...] = line_ref[0:1, 0:rows_here].reshape(-1)

    def body(g, carry):
        here = pl.ds(pl.multiple_of(g * SUB, SUB), SUB)
        at = step * groups + g
        rows = pl.ds(pl.multiple_of(at * SUB, SUB), SUB)
        square = 0.0
        for ref, block0, blocks, first in source:
            for b in range(blocks):
                value = ref[first + at * blocks + b].astype(F32)
                grad_ref[here, (block0 + b) * LANE : (block0 + b + 1) * LANE] = value
                square = square + (value * value + 1e-30)
        mean = jnp.sum(square, axis=1, keepdims=True) * (1.0 / width)
        row_new = DECAY * state_ref[rows, :] + (1.0 - DECAY) * mean
        new_ref[rows, :] = row_new
        for ref, block0, blocks, first in source:
            for b in range(blocks):
                lanes = slice((block0 + b) * LANE, (block0 + b + 1) * LANE)
                value = ref[first + at * blocks + b].astype(F32)
                change = value * lax.rsqrt(row_new * scaled_ref[0:1, lanes])
                new[here, lanes] = weight[here, lanes] - rate * change
        return carry

    if steps == 1:
        before()
        lax.fori_loop(0, groups, body, 0, unroll=5)
        after()
    else:
        pl.when(step == 0)(before)
        lax.fori_loop(0, groups, body, 0, unroll=5)
        pl.when(step == steps - 1)(after)


def sources_of(chunk, ref, rows):
    return {w: (ref, block0, blocks, first) for w, block0, blocks, first, _ in spans(chunk, rows)[0]}


def update_kernel(rows, copies_of, place_ref, mine_ref, other_ref, pack_ref, *refs):
    weights, states, col_states = refs[0:2], refs[2:4], refs[4:6]
    grads, news, rows_new, cols_new = refs[6:8], refs[8:10], refs[10:12], refs[12:14]
    conv_scratch, out_scratch = refs[14:18], refs[18:22]
    full1_ref, full2_ref, sem = refs[22:25]
    both = (mine_ref, other_ref)
    count = 2 * mine_ref.shape[0]
    step, steps = pl.program_id(0), pl.num_programs(0)

    @pl.when(step == 0)
    def _():
        copies = load_full(both, place_ref, 0, full1_ref, sem, 0)
        copies += load_full(both, place_ref, full1_ref.shape[0] // count, full2_ref, sem, count)
        run_copies(copies)

    from1 = sources_of(CHUNKS[0], full1_ref, rows)
    from2 = sources_of(CHUNKS[1], full2_ref, rows)

    def update(n, k, source, scratch, *steps):
        squares = pack_ref[2:3, LANE0[k] : LANE0[k] + WIDTHS[k]]
        update_weight(
            k, squares, pack_ref[3:4, k : k + 1] * (1.0 / copies_of), source, weights[n],
            states[n], col_states[n], grads[n], news[n], rows_new[n], cols_new[n], scratch, *steps,
        )

    update(0, 1, [from1[1], from2[1]], conv_scratch, step, UPDATE_STEPS)

    @pl.when(step == steps - 1)
    def _():
        update(1, 2, [from1[2]], out_scratch)


def update_in_kernel(
    rows, copies_of, bits, place_ref, mine_ref, other_ref, pack_in_ref, pack_ref, np_ref, second_ref, *refs
):
    weight, state, col_state, grad_ref, new_ref, row_new_ref, col_new_ref = refs[0:7]
    ngrad_ref, nsecond_ref, nnew_ref = refs[7:10]
    full_ref, sem = refs[14:16]
    copies = load_list(bits, mine_ref, other_ref, place_ref, full_ref, sem)
    for copy in copies:
        copy.start()
    grad = pack_ref[0:2, :]
    second = DECAY * second_ref[...] + (1.0 - DECAY) * (grad * grad + 1e-30)
    ngrad_ref[...] = grad
    nsecond_ref[...] = second
    nnew_ref[...] = np_ref[...] - 0.2 * grad * lax.rsqrt(second)
    for copy in copies:
        copy.wait()
    update_weight(
        0, pack_in_ref[0:1, :], pack_ref[3:4, 0:1] * (1.0 / copies_of),
        [sources_of(CHUNKS[2], full_ref, rows)[0]], weight, state, col_state, grad_ref, new_ref,
        row_new_ref, col_new_ref, refs[10:14],
    )


class Places:
    def __init__(self):
        self.seq, self.fsdp = lax.axis_size("seq"), lax.axis_size("fsdp")
        self.q = lax.axis_index("fsdp")
        self.s = lax.axis_index("seq")

    def flip(self, x, axis, bit):
        pairs = []
        for s in range(self.seq):
            for f in range(self.fsdp):
                s2, f2 = (s ^ bit, f) if axis == "seq" else (s, f ^ bit)
                pairs.append((s * self.fsdp + f, s2 * self.fsdp + f2))
        return lax.ppermute(x, AXES, pairs)


def bits_of(count):
    return [1 << k for k in range(count.bit_length() - 1)]


def tie(x, *others):
    return lax.optimization_barrier((x, *others))[0]


def gather_pieces(piece, place, after, later=()):
    found = {0: piece}
    for bit in reversed(bits_of(place.fsdp)):
        for k in list(found):
            moving = found[k]
            if bit == 1:
                moving = tie(moving, *((after,) if k == 0 or not later else later))
            found[k | bit] = place.flip(moving, "fsdp", bit)
    return [found[k] for k in range(place.fsdp)]


def sum_over(x, place, *axes):
    for axis in axes:
        for bit in bits_of(getattr(place, axis)):
            x = x + place.flip(x, axis, bit)
    return x


def pick(x, index, axis):
    return lax.dynamic_index_in_dim(x, index, axis=axis, keepdims=False)


class Reduction:
    def __init__(self, place, keep, send):
        self.place, self.near = place, keep
        self.got = place.flip(send, "fsdp", 1)

    def halve(self, axis, side, flip_axis, bit):
        dims = self.near.shape
        parts = dims[:axis] + (2, dims[axis] // 2) + dims[axis + 1 :]
        near, got = self.near.reshape(parts), self.got.reshape(parts)
        away = pick(near, 1 - side, axis).astype(F32) + pick(got, 1 - side, axis).astype(F32)
        self.near = pick(near, side, axis).astype(F32) + pick(got, side, axis).astype(F32)
        away = away.astype(BF16)
        self.got = self.place.flip(away, flip_axis, bit)
        return away

    def x(self):
        bit = self.place.fsdp // 2
        while bit > 1:
            away = self.halve(0, (self.place.q // bit) % 2, "fsdp", bit)
            bit //= 2
        return away

    def y(self):
        return self.halve(1, self.place.s % 2, "seq", 1)

    def seq_bit(self, bit):
        return self.halve(1, (self.place.s // bit) % 2, "seq", bit)

    def piece(self):
        total = (self.near + self.got.astype(F32)).astype(BF16)
        return total.reshape(total.shape[1:])

    def pieces(self):
        total = (self.near + self.got.astype(F32)).astype(BF16)
        return total.reshape((self.place.seq // 2, -1) + total.shape[2:])


def arrive(result, *reductions):
    result, *gots = lax.optimization_barrier((result, *[r.got for r in reductions]))
    for reduction, got in zip(reductions, gots):
        reduction.got = got
    return result


def summed_f32(got):
    return jnp.sum(got.astype(F32), axis=0)


def summed(got):
    return summed_f32(got).astype(BF16)


def exchange(place, sent):
    line = [[y + 2 * z for z in range(place.seq // 2)] for y in range(2)]
    return lax.all_to_all(sent, "seq", 0, 0, axis_index_groups=line)


def on_device(
    tokens, input_mask, doc_lengths, cotangent, w_in, w_conv, w_out, norm_params,
    row_in, col_in, row_conv, col_conv, row_out, col_out, norm_second,
):
    place = Places()
    rows = tokens.shape[0]
    pieces = place.fsdp
    spots = jnp.stack(
        [place.q, (place.s * place.fsdp + place.q) * rows, place.s, place.seq]
    ).astype(jnp.int32)
    docs = doc_lengths.shape[0]
    live = input_mask.reshape(-1, LANE)
    weights = (w_in, w_conv, w_out)
    rows_of = [w.shape[0] for w in weights]

    tile_a, tile = 256, 512
    steps = rows // tile
    params_spec = whole(2, D + 2 * INNER)
    dma = pltpu.SemaphoreType.DMA

    out_sides = (w_out[:, : D // 2], w_out[:, D // 2 :])
    conv_out = jnp.concatenate([w_conv, *out_sides], axis=0).astype(BF16)
    hidden_a, slope_a, xhat_a, rstd_a = call(
        norm_a_kernel,
        (rows // tile_a,),
        [rows_spec(tile_a, D), params_spec],
        [rows_spec(tile_a, D)] * 3 + [rows_spec(tile_a, LANE)],
        [shape((rows, D), BF16)] * 3 + [shape((rows, LANE), F32)],
        us=17,
    )(tokens, tie(norm_params, conv_out))

    in_pieces = gather_pieces(w_in.astype(BF16), place, hidden_a)

    def in_call(tiles, count, before):
        at, stride = tiles

        def here_spec(width):
            return pl.BlockSpec((tile, width), lambda i: (at + stride * i, 0))

        out_shapes = [shape((rows, INNER), BF16)] * 3 + [shape((rows, LANE), F32)] * 2
        out_specs = [here_spec(INNER)] * 3 + [here_spec(LANE)] * 2
        if at == 0:
            out_shapes += [shape((REACH, INNER), BF16)] * 2
            out_specs += [whole(REACH, INNER)] * 2
        return call(
            functools.partial(in_kernel, pieces, tiles),
            (count,),
            [SMEM, whole(docs), here_spec(D), whole(*live.shape), params_spec]
            + [ANY] * (pieces + len(before)),
            out_specs,
            out_shapes,
            [pltpu.VMEM((D, INNER), BF16), pltpu.VMEM((tile, INNER), F32)]
            + [pltpu.VMEM((8, docs + -docs % LANE), F32), dma((pieces,))],
            us=3,
            aliases={5 + pieces + k: k for k in range(len(before))},
        )(spots, doc_lengths, hidden_a, live, norm_params, *in_pieces, *before)

    *kept, m_first, m_last = in_call((0, steps - 1), 2, ())
    moved, slope_b, xhat_b, rstd_b, masks = in_call((1, 1), steps - 2, kept)

    def halo(inner, outer):
        total = place.seq * place.fsdp
        across = [(i, i + 1 if i % 2 else i - 1) for i in range(1, total - 1)]
        return place.flip(inner, "fsdp", 1), lax.ppermute(outer, AXES, across)

    m_inner, m_outer = halo(m_first, m_last)
    conv_pieces = gather_pieces(conv_out, place, m_first, (moved, m_inner, m_outer))

    ext = pltpu.VMEM((rows + 2 * REACH, INNER), BF16)
    taps_wide = KERNEL_TAPS * INNER
    wide = pltpu.VMEM((taps_wide, INNER), BF16)
    shards = place.fsdp // 2

    def half_dims(chunk):
        count = spans(chunk, rows_of)[1]
        return (shards, count + -count % place.seq, SUB, LANE)

    def tile_spec(width, ahead):
        return pl.BlockSpec((tile, width), lambda i: (jnp.clip(i + ahead, 0, steps - 1), 0))

    halves = [half_dims(CHUNKS[0])] * 2 + [half_dims(CHUNKS[1])] * 2
    work = pltpu.VMEM((tile, INNER), F32)
    turned_tile = pltpu.VMEM((INNER, tile), BF16)
    hidden_c, d_conv, d_first, d_last, sums_c, turned, keep1, send1, keep2, send2 = call(
        functools.partial(conv_kernel, pieces, rows_of),
        (steps + 1,),
        [SMEM, ANY, ANY, ANY, tile_spec(LANE, 0), tile_spec(D, 0), tile_spec(D, -1), params_spec]
        + [ANY] * pieces,
        [tile_spec(INNER, 0)] * 2
        + [whole(REACH, INNER), whole(REACH, INNER), whole(2, INNER)]
        + [ANY] * 5,
        [
            shape((rows, INNER), BF16),
            shape((rows, INNER), BF16),
            shape((REACH, INNER), BF16),
            shape((REACH, INNER), BF16),
            shape((2, INNER), F32),
            shape((taps_wide, INNER), BF16),
        ]
        + [shape(dims, BF16) for dims in halves],
        [ext, wide, wide, pltpu.VMEM((INNER, D), BF16), pltpu.VMEM((D, INNER), BF16)]
        + [pltpu.VMEM((2, tile, taps_wide), BF16), work, work, work, turned_tile, turned_tile]
        + [pltpu.VMEM((INNER, taps_wide), F32), pltpu.VMEM((INNER, D), F32)]
        + [pltpu.VMEM((16, INNER), F32)]
        + [pltpu.VMEM((2,) + halves[0], BF16), pltpu.VMEM((2,) + halves[2], BF16)]
        + [dma((3 + 3 * pieces,))],
        us=45,
    )(
        spots, m_inner, moved, m_outer, masks, cotangent, cotangent, norm_params, *conv_pieces
    )
    d_inner, d_outer = halo(d_first, d_last)
    first, second = Reduction(place, keep1, send1), Reduction(place, keep2, send2)
    (block_out,) = call(
        functools.partial(out_kernel, pieces),
        (steps,),
        [SMEM, rows_spec(tile, INNER), rows_spec(tile, D)] + [ANY] * pieces,
        [rows_spec(tile, D)],
        [shape((rows, D), BF16)],
        [pltpu.VMEM((INNER, D), BF16), dma((2 * pieces,))],
        us=9,
    )(spots, hidden_c, tokens, *conv_pieces)

    def back_conv(last, spots, before):
        here = steps // 2
        at = here * last

        def here_spec(width):
            return pl.BlockSpec((tile, width), lambda i: (i + at, 0))

        dims = half_dims(CHUNKS[2])
        return call(
            functools.partial(back_conv_kernel, last, w_in.shape[0]),
            (here,),
            [SMEM] + [ANY] * 4
            + [here_spec(LANE), here_spec(INNER), here_spec(LANE), here_spec(INNER), here_spec(D)]
            + [params_spec]
            + [ANY] * last,
            [rows_spec(tile, INNER), whole(2, INNER)] + [ANY] * (1 + last),
            [shape((rows // 2, INNER), BF16), shape((2, INNER), F32)]
            + ([shape(dims, BF16)] * 2 if last else [shape((INNER, D), F32)]),
            ([pltpu.VMEM((2,) + dims, BF16)] if last else [])
            + [
                ext,
                wide,
                pltpu.VMEM((tile, taps_wide), BF16),
                pltpu.VMEM((tile, INNER), F32),
                pltpu.VMEM((INNER, D), F32),
                pltpu.VMEM((16, INNER), F32),
                dma((5,)),
            ],
            us=16,
        )(
            spots, d_inner, d_conv, d_outer, turned, masks, xhat_b, rstd_b, slope_b, hidden_a,
            norm_params, *before,
        )

    block_out, d_inner, d_outer = arrive((block_out, d_inner, d_outer), first, second)
    away = (first.x(), second.y())
    d_pre0, sums_b0, grad_part = back_conv(0, tie(spots, *away), ())
    d_pre0 = arrive(d_pre0, first, second)
    away = (first.y(), second.x())
    d_pre1, sums_b1, keep, send = back_conv(1, tie(spots, *away), (grad_part,))
    send = arrive(send, first, second)
    third = Reduction(place, keep, send)
    sent = jnp.concatenate([first.pieces(), second.pieces()], axis=1)
    got = exchange(place, sent)
    third.got = tie(third.got, sent)
    away = (sent, third.x())
    input_grad, sums_a = call(
        functools.partial(back_a_kernel, pieces, steps // 2),
        (steps,),
        [SMEM]
        + [
            pl.BlockSpec((tile, INNER), lambda i: (jnp.minimum(i, steps // 2 - 1), 0)),
            pl.BlockSpec((tile, INNER), lambda i: (jnp.maximum(i - steps // 2, 0), 0)),
        ]
        + [rows_spec(tile, D), rows_spec(tile, LANE), rows_spec(tile, D), rows_spec(tile, D)]
        + [params_spec]
        + [ANY] * pieces,
        [rows_spec(tile, D), whole(2, D)],
        [shape((rows, D), F32), shape((2, D), F32)],
        [
            pltpu.VMEM((D, INNER), BF16),
            pltpu.VMEM((INNER, D), BF16),
            pltpu.VMEM((tile, D), F32),
            pltpu.VMEM((16, D), F32),
            dma((pieces,)),
        ],
        us=17,
    )(
        tie(spots, *away), d_pre0, d_pre1, xhat_a, rstd_a, slope_a, cotangent, norm_params, *in_pieces
    )

    row_states, col_states = (row_in, row_conv, row_out), (col_in, col_conv, col_out)
    row_specs = [whole(*r.shape) for r in row_states]
    col_specs = [whole(*c.shape) for c in col_states]
    cols_all = D + 2 * INNER
    pack_spec = whole(4, cols_all)
    fulls = [pltpu.VMEM(half_dims(c)[1:], BF16) for c in CHUNKS]
    sums = (sums_a, sums_b0, sums_b1, sums_c)
    got, third.got, input_grad = lax.optimization_barrier((got, third.got, input_grad))
    part = summed(got)
    sent = jnp.broadcast_to(part[None], (place.seq // 2,) + part.shape)
    mine = exchange(place, sent)
    third.got = tie(third.got, sent)
    away = third.y()
    (pack,) = call(
        functools.partial(pack_kernel, rows_of, [half_dims(c)[1] // place.seq for c in CHUNKS]),
        (1,),
        [SMEM, whole(*part.shape)] + row_specs + [whole(*x.shape) for x in sums],
        [pack_spec],
        [shape((4, cols_all), F32)],
        [pltpu.VMEM((cols_all // LANE + 1, SUB, LANE), F32)],
        us=2,
        mib=16,
    )(tie(spots, away), part, *row_states, *sums)
    core_sum = pack + place.flip(pack, "fsdp", 1)
    third.got, pack = lax.optimization_barrier((third.got, core_sum))
    for bit in bits_of(place.fsdp)[1:]:
        pack = pack + place.flip(pack, "fsdp", bit)
    seq_bits = bits_of(place.seq)
    third.seq_bit(seq_bits[1])
    pack = pack + place.flip(pack, "seq", 1)
    mine, third.got, pack = lax.optimization_barrier((mine, third.got, pack))
    other = place.flip(mine, "seq", 1)
    for bit in seq_bits[2:]:
        third.seq_bit(bit)
    line = third.piece()[None]
    for bit in seq_bits[:0:-1]:
        line = jnp.concatenate([line, place.flip(line, "seq", bit)], axis=0)
    for bit in seq_bits[1:]:
        pack = pack + place.flip(pack, "seq", bit)
    line, other, pack = lax.optimization_barrier((line, other, pack))
    line_other = place.flip(line, "seq", 1)
    list_bits = [1] + seq_bits[1:]

    def update_scratch(weight):
        lines = weight.shape[0] + -weight.shape[0] % LANE
        return (
            [pltpu.VMEM((8, lines), F32)]
            + [pltpu.VMEM((lines, LANE), F32)] * 2
            + [pltpu.VMEM((8, weight.shape[1]), F32)]
        )

    weight_specs = [whole(*w.shape) for w in weights]
    conv_block = pl.BlockSpec((w_conv.shape[0] // UPDATE_STEPS, INNER), lambda i: (i, 0))
    both_specs = [conv_block, weight_specs[2]]
    results = call(
        functools.partial(update_kernel, rows_of, place.seq),
        (UPDATE_STEPS,),
        [SMEM, ANY, ANY, pack_spec] + both_specs + row_specs[1:] + col_specs[1:],
        both_specs * 2 + row_specs[1:] + col_specs[1:],
        [shape(w.shape, F32) for w in weights[1:]] * 2
        + [shape(r.shape, F32) for r in row_states[1:] + col_states[1:]],
        update_scratch(w_conv)
        + update_scratch(w_out)
        + fulls[:2]
        + [dma((2 * place.seq,))],
        us=8,
        mib=32,
    )(spots, mine, other, pack, *weights[1:], *row_states[1:], *col_states[1:])
    grad_conv, grad_out, new_conv, new_out, row_conv_new, row_out_new, col_conv_new, col_out_new = (
        results
    )
    line_other, grad_out = lax.optimization_barrier((line_other, grad_out))
    (pack_in,) = call(
        functools.partial(pack_in_kernel, rows_of, list_bits),
        (1,),
        [SMEM, ANY, ANY],
        [whole(8, INNER)],
        [shape((8, INNER), F32)],
        [fulls[2], dma((place.seq,))],
        us=2,
        mib=16,
    )(spots, line, line_other)
    pack_in = sum_over(pack_in, place, "fsdp")
    grad_in, new_in, row_in_new, col_in_new, *norm_results = call(
        functools.partial(update_in_kernel, rows_of, place.seq, list_bits),
        (1,),
        [SMEM, ANY, ANY, whole(8, INNER), pack_spec, params_spec, params_spec]
        + [weight_specs[0], row_specs[0], col_specs[0]],
        [weight_specs[0]] * 2 + [row_specs[0], col_specs[0]] + [params_spec] * 3,
        [shape(w_in.shape, F32)] * 2
        + [shape(row_in.shape, F32), shape(col_in.shape, F32)]
        + [shape((2, cols_all), F32)] * 3,
        update_scratch(w_in) + [fulls[2], dma((place.seq,))],
        us=4,
        mib=24,
    )(
        spots, line, line_other, pack_in, pack, norm_params, norm_second, w_in, row_in, col_in
    )
    return (
        block_out,
        input_grad,
        grad_in,
        grad_conv,
        grad_out,
        new_in,
        new_conv,
        new_out,
        row_in_new,
        col_in_new,
        row_conv_new,
        col_conv_new,
        row_out_new,
        col_out_new,
        *norm_results,
    )


def solution(mesh):
    both, rows = P(AXES, None), P("fsdp", None)
    in_specs = (
        both, P(AXES), P(), both, rows, rows, rows, P(),
        P("fsdp"), P(), P("fsdp"), P(), P("fsdp"), P(), P(),
    )
    out_specs = (
        both, both, rows, rows, rows, rows, rows, rows,
        P("fsdp"), P(), P("fsdp"), P(), P("fsdp"), P(), P(), P(), P(),
    )
    return jax.shard_map(
        on_device, mesh=mesh, in_specs=in_specs, out_specs=out_specs, check_vma=False
    )
```

```python
import functools
import math

import jax
import jax.numpy as jnp
from jax import lax
from jax.experimental import pallas as pl
from jax.experimental.pallas import tpu as pltpu
from jax.sharding import PartitionSpec as P

D = 1280
INNER = 640
KERNEL_TAPS = 5
DILATION_STEP = 128
STEP = 10
EPSILON = 1e-05
DECAY = 1.0 - STEP ** (-0.8)

REACH = (KERNEL_TAPS - 1) // 2 * DILATION_STEP
MID = (KERNEL_TAPS - 1) // 2
F32 = jnp.float32
BF16 = jnp.bfloat16
SUB, LANE = 16, 128
AXES = ("seq", "fsdp")
NT = (((1,), (1,)), ((), ()))
TN = (((0,), (0,)), ((), ()))
NN = (((1,), (0,)), ((), ()))


def call(kernel, grid, in_specs, out_specs, out_shape, scratch=(), us=1.0, aliases=None, mib=58):
    params = pltpu.CompilerParams(
        vmem_limit_bytes=mib * 1024 * 1024, dimension_semantics=("arbitrary",) * len(grid)
    )
    return pl.pallas_call(
        kernel,
        grid=grid,
        in_specs=in_specs,
        out_specs=out_specs,
        out_shape=out_shape,
        scratch_shapes=list(scratch),
        compiler_params=params,
        input_output_aliases=aliases or {},
        cost_estimate=pl.CostEstimate(
                flops=int(us * 1.1e9), bytes_accessed=int(us * 3.4e6), transcendentals=0
        ),
    )


def shape(dims, dtype):
    return jax.ShapeDtypeStruct(dims, dtype)


def rows_spec(tile, width):
    return pl.BlockSpec((tile, width), lambda i: (i, 0))


def whole(*dims):
    return pl.BlockSpec(dims, lambda *_: (0,) * len(dims))


ANY = pl.BlockSpec(memory_space=pl.ANY)
SMEM = pl.BlockSpec(memory_space=pltpu.SMEM)


ERFC_P = 0.47 / math.sqrt(2.0)
ERFC_C = (
    0.12357219400743558,
    0.1999878668208835,
    -0.08033356004356296,
    0.3660253986657854,
    -0.1092519747040215,
)
LOG2E = 1.4426950408889634


def gelu_and_slope(y):
    t = pltpu.reciprocal(1.0 + ERFC_P * jnp.abs(y), approx=True)
    bell = jnp.exp2(y * y * (-0.5 * LOG2E))
    poly = ERFC_C[4] * t + ERFC_C[3]
    for c in ERFC_C[2::-1]:
        poly = poly * t + c
    tail = poly * t * bell
    cdf = jnp.where(y > 0.0, 1.0 - tail, tail)
    return y * cdf, cdf + y * (bell * (1.0 / math.sqrt(2.0 * math.pi)))


def lane_blocks(width):
    return [slice(k, k + LANE) for k in range(0, width, LANE)]


def row_stats(ref, rows):
    width = ref.shape[-1]
    blocks = lane_blocks(width)
    total = ref[rows, blocks[0]].astype(F32)
    for b in blocks[1:]:
        total = total + ref[rows, b].astype(F32)
    mean = jnp.sum(total, axis=-1, keepdims=True) * (1.0 / width)
    square = None
    for b in blocks:
        centered = ref[rows, b].astype(F32) - mean
        square = centered * centered if square is None else square + centered * centered
    variance = jnp.sum(square, axis=-1, keepdims=True) * (1.0 / width)
    return mean, lax.rsqrt(variance + EPSILON)


def fold(values):
    total = values[0:8]
    for k in range(8, values.shape[0], 8):
        total = total + values[k : k + 8]
    return total


def in_stages(count, stages, between=()):
    chunks = [slice(k, k + CHUNK) for k in range(0, count, CHUNK)]
    kept, rounds = {}, len(chunks) + len(stages) - 1
    for t in range(rounds):
        for n, stage in enumerate(stages):
            if 0 <= t - n < len(chunks):
                kept[n, t - n] = stage(chunks[t - n], kept.get((n - 1, t - n)))
        for work in between[t * len(between) // rounds : (t + 1) * len(between) // rounds]:
            work()


def halves_of(count):
    return (slice(0, count // 2), slice(count // 2, count))


def row_means(sums, width):
    return [jnp.sum(x, axis=-1, keepdims=True) * (1.0 / width) for x in sums]


def norm_back(rows, dxhat_ref, xhat_ref, means, put):
    mean_d, mean_dx, rstd = means
    for b in lane_blocks(dxhat_ref.shape[-1]):
        xhat = xhat_ref[rows, b].astype(F32)
        put(b, (dxhat_ref[rows, b] - mean_d - xhat * mean_dx) * rstd)


def add_terms(acc_ref, b, dy, xhat):
    acc_ref[0:8, b] += fold(dy * xhat)
    acc_ref[8:16, b] += fold(dy)


def open_sums(acc_ref):
    @pl.when(pl.program_id(0) == 0)
    def _():
        acc_ref[...] = jnp.zeros_like(acc_ref)


def close_sums(out_ref, acc_ref):
    @pl.when(pl.program_id(0) == pl.num_programs(0) - 1)
    def _():
        out_ref[0:1, :] = jnp.sum(acc_ref[0:8, :], axis=0, keepdims=True)
        out_ref[1:2, :] = jnp.sum(acc_ref[8:16, :], axis=0, keepdims=True)


def run_copies(copies):
    for copy in copies:
        copy.start()
    for copy in copies:
        copy.wait()


def piece_copies(pieces, full_ref, me, sem, first=0):
    each = full_ref.shape[0] // len(pieces)
    return [
        pltpu.make_async_copy(
            piece.at[0:each, :],
            full_ref.at[pl.ds(pl.multiple_of((me ^ k) * each, SUB), each), :],
            sem.at[first + k],
        )
        for k, piece in enumerate(pieces)
    ]


def out_copies(pieces, full_ref, me, sem, first=0):
    each, width = full_ref.shape[0] // len(pieces), full_ref.shape[1] // 2
    copies = []
    for k, piece in enumerate(pieces):
        rows = pl.ds(pl.multiple_of((me ^ k) * each, SUB), each)
        for side in range(2):
            at = piece.shape[0] - (2 - side) * each
            copies.append(
                pltpu.make_async_copy(
                    piece.at[at : at + each, :],
                    full_ref.at[rows, side * width : (side + 1) * width],
                    sem.at[first + 2 * k + side],
                )
            )
    return copies


def column(row):
    return jnp.transpose(jnp.broadcast_to(row, (LANE, LANE)))


CHUNK = 64
UPDATE_STEPS = 5
TURNED = 2


def norm_a_kernel(tok_ref, np_ref, hid_ref, slope_ref, xhat_ref, rstd_ref):
    def stats(rows, _):
        mean, rstd = row_stats(tok_ref, rows)
        rstd_ref[rows, :] = jnp.broadcast_to(rstd, (CHUNK, LANE))
        return mean, rstd

    def work(rows, kept):
        mean, rstd = kept
        for b in lane_blocks(D):
            xhat = (tok_ref[rows, b].astype(F32) - mean) * rstd
            hidden, slope = gelu_and_slope(xhat * np_ref[0:1, b] + np_ref[1:2, b])
            hid_ref[rows, b] = hidden.astype(BF16)
            slope_ref[rows, b] = slope.astype(BF16)
            xhat_ref[rows, b] = xhat.astype(BF16)

    in_stages(tok_ref.shape[0], [stats, work])


def running_ends(ends_ref, lengths_ref):
    docs, width = lengths_ref.shape[0], ends_ref.shape[1]
    ends_ref[...] = jnp.zeros_like(ends_ref)
    ends_ref[0:1, 0:docs] = lengths_ref[...].reshape(1, -1).astype(F32)
    before = jnp.zeros((1, 1), F32)
    row = lax.broadcasted_iota(jnp.int32, (LANE, LANE), 0)
    lane = lax.broadcasted_iota(jnp.int32, (LANE, LANE), 1)
    for k in range(0, width, LANE):
        line = ends_ref[0:1, k : k + LANE]
        sums = jnp.sum(jnp.where(row <= lane, column(line), 0.0), axis=0, keepdims=True) + before
        ends_ref[0:1, k : k + LANE] = jnp.where(lane[0:1] + k < docs, sums, 1e9)
        before = before + jnp.sum(line, axis=1, keepdims=True)


def in_kernel(pieces, tiles, place_ref, lengths_ref, hid_ref, live_ref, np_ref, *refs):
    piece_refs = refs[:pieces]
    edges = tiles[0] == 0
    outs = refs[-(11 if edges else 9) :]
    mov_ref, slope_ref, xhat_ref, rstd_ref, mask_ref = outs[:5]
    w_ref, pre_ref, ends_ref, sem = outs[-4:]
    step = pl.program_id(0)
    tile = hid_ref.shape[0]

    @pl.when(step == 0)
    def _():
        copies = piece_copies(piece_refs, w_ref, place_ref[0], sem)
        for copy in copies:
            copy.start()
        running_ends(ends_ref, lengths_ref)
        for copy in copies:
            copy.wait()

    for half in halves_of(tile):
        pre_ref[half, :] = lax.dot_general(
            hid_ref[half, :], w_ref[...], NN, preferred_element_type=F32
        )

    at_tile = tiles[0] + step * tiles[1]
    first = place_ref[1] + at_tile * tile
    ends = ends_ref[0:1, :]
    lanes = lax.broadcasted_iota(jnp.int32, (LANE, LANE), 1)
    offsets = ((lanes - MID) * DILATION_STEP).astype(F32)
    for k in range(tile // LANE):
        at = (first + k * LANE + lax.broadcasted_iota(jnp.int32, (LANE, 1), 0)).astype(F32)
        begin = jnp.max(jnp.where(ends <= at, ends, 0.0), axis=1, keepdims=True)
        end = jnp.min(jnp.where(ends > at, ends, 1e9), axis=1, keepdims=True)
        there = at + offsets
        same = jnp.where((there >= begin) & (there < end), 1.0, 0.0)
        live = column(live_ref[pl.ds(at_tile * (tile // LANE) + k, 1), :].astype(F32))
        mask_ref[k * LANE : (k + 1) * LANE, :] = jnp.where(lanes == MID, live, same)

    def stats(rows, _):
        mean, rstd = row_stats(pre_ref, rows)
        rstd_ref[rows, :] = jnp.broadcast_to(rstd, (CHUNK, LANE))
        return mean, rstd

    def work(rows, kept):
        mean, rstd = kept
        live = mask_ref[rows, MID : MID + 1]
        for b in lane_blocks(INNER):
            gains = slice(D + b.start, D + b.stop)
            xhat = (pre_ref[rows, b] - mean) * rstd
            hidden, slope = gelu_and_slope(xhat * np_ref[0:1, gains] + np_ref[1:2, gains])
            mov_ref[rows, b] = (hidden * live).astype(BF16)
            slope_ref[rows, b] = slope.astype(BF16)
            xhat_ref[rows, b] = xhat.astype(BF16)

    in_stages(tile, [stats, work])
    if edges:
        put_edges(place_ref, outs[5], outs[6], mov_ref, step == 0, step == 1)


def load_window(place_ref, inner, mid, outer, ext_ref, sem):
    rows, core = mid.shape[0], lax.rem(place_ref[0], 2)
    near = pl.multiple_of((1 - core) * (REACH + rows), SUB)
    far = pl.multiple_of(core * (REACH + rows), SUB)
    return [
        pltpu.make_async_copy(inner, ext_ref.at[pl.ds(near, REACH), :], sem.at[0]),
        pltpu.make_async_copy(mid, ext_ref.at[REACH : REACH + rows, :], sem.at[1]),
        pltpu.make_async_copy(outer, ext_ref.at[pl.ds(far, REACH), :], sem.at[2]),
    ]


def put_edges(place_ref, inner_ref, outer_ref, tile_ref, at_first, at_last):
    rows, core = tile_ref.shape[0], lax.rem(place_ref[0], 2)
    for at, edge, first in ((at_first, slice(0, REACH), 0), (at_last, slice(rows - REACH, rows), 1)):

        @pl.when(at & (core == first))
        def _(edge=edge):
            outer_ref[...] = tile_ref[edge, :]

        @pl.when(at & (core != first))
        def _(edge=edge):
            inner_ref[...] = tile_ref[edge, :]


def fill_taps(taps_ref, ext_ref, mask_ref, start):
    tile = taps_ref.shape[0]
    for j in range(KERNEL_TAPS):
        rows = pl.ds(pl.multiple_of(start + j * DILATION_STEP, DILATION_STEP), tile)
        picked = ext_ref[rows, :]
        if j != MID:
            picked = picked * mask_ref[:, j : j + 1].astype(BF16)
        taps_ref[:, j * INNER : (j + 1) * INNER] = picked


def conv_kernel(
    pieces, rows_of, place_ref, low_ref, mov_ref, high_ref, mask_ref, cot_ref, before_ref, np_ref, *refs
):
    piece_refs = refs[:pieces]
    hid_ref, dconv_ref, inner_ref, outer_ref, sums_ref, turned_ref = refs[pieces : pieces + 6]
    outs = refs[pieces + 6 : pieces + 10]
    ext_ref, wc_ref, wct_ref, wo_ref, wt_ref, taps_ref, pre_ref, dh_ref, xhat_ref = refs[
        pieces + 10 : pieces + 19
    ]
    dt_ref, ht_ref, gc_ref, go_ref, acc_ref, stage1_ref, stage2_ref, sem = refs[pieces + 19 :]
    step, steps = pl.program_id(0), pl.num_programs(0) - 1
    tile = taps_ref.shape[1]
    slot = lax.rem(step, 2)

    @pl.when(step == 0)
    def _():
        me = place_ref[0]
        outs = out_copies(piece_refs, wo_ref, me, sem, 3)
        rest = load_window(place_ref, low_ref, mov_ref, high_ref, ext_ref, sem)
        rest += piece_copies(piece_refs, wc_ref, me, sem, 3 + 2 * pieces)
        for copy in outs + rest:
            copy.start()
        for ref in (acc_ref, gc_ref, go_ref):
            ref[...] = jnp.zeros_like(ref)
        for copy in outs:
            copy.wait()
        for k in range(0, D, 256):
            wt_ref[k : k + 256, :] = jnp.transpose(wo_ref[:, k : k + 256])
        for copy in rest:
            copy.wait()

    def grad_conv(cols):
        def work():
            gc_ref[:, cols] += lax.dot_general(
                dt_ref[...], taps_ref[1 - slot, :, cols], NN, preferred_element_type=F32
            )

        return work

    def grad_out(cols):
        def work():
            go_ref[:, cols] += lax.dot_general(
                ht_ref[...], before_ref[:, cols], NN, preferred_element_type=F32
            )

        return work

    taps_wide = KERNEL_TAPS * INNER
    products = [grad_conv(slice(k, min(k + 768, taps_wide))) for k in range(0, taps_wide, 768)]
    products += [grad_out(slice(k, min(k + 768, D))) for k in range(0, D, 768)]

    def tile_work(products, turned):
        fill_taps(taps_ref.at[slot], ext_ref, mask_ref, step * tile)
        pre_ref[...] = lax.dot_general(
            taps_ref[slot], wc_ref[...], NN, preferred_element_type=F32
        )
        dh_ref[...] = lax.dot_general(cot_ref[...], wt_ref[...], NN, preferred_element_type=F32)
        for n in range(turned):
            tap = jnp.minimum(turned * (step - 1) + n, KERNEL_TAPS - 1)
            source = wc_ref[pl.ds(pl.multiple_of(tap * INNER, SUB), INNER), :]
            target = pl.multiple_of((KERNEL_TAPS - 1 - tap) * INNER, SUB)
            wct_ref[pl.ds(target, INNER), :] = jnp.transpose(source)

        def stats(rows, _):
            return row_stats(pre_ref, rows)

        def work(rows, kept):
            mean, rstd = kept
            sums = [0.0, 0.0]
            for b in lane_blocks(INNER):
                gains = slice(D + INNER + b.start, D + INNER + b.stop)
                gain = np_ref[0:1, gains]
                xhat = (pre_ref[rows, b] - mean) * rstd
                hidden, slope = gelu_and_slope(xhat * gain + np_ref[1:2, gains])
                hid_ref[rows, b] = hidden.astype(BF16)
                dy = dh_ref[rows, b] * slope
                add_terms(acc_ref, b, dy, xhat)
                dxhat = dy * gain
                xhat_ref[rows, b] = xhat
                dh_ref[rows, b] = dxhat
                sums = [sums[0] + dxhat, sums[1] + dxhat * xhat]
            return row_means(sums, INNER) + [rstd]

        def finish(rows, means):
            def put(b, value):
                dconv_ref[rows, b] = value.astype(BF16)

            norm_back(rows, dh_ref, xhat_ref, means, put)

        in_stages(tile, [stats, work, finish], products)
        dt_ref[...] = jnp.transpose(dconv_ref[...])
        ht_ref[...] = jnp.transpose(hid_ref[...])

    @pl.when(step == 0)
    def _():
        tile_work([], 0)

    @pl.when((step > 0) & (step < steps))
    def _():
        tile_work(products, TURNED)

    put_edges(place_ref, inner_ref, outer_ref, dconv_ref, step == 0, step == steps - 1)

    @pl.when(step == steps)
    def _():
        copy = pltpu.make_async_copy(wct_ref, turned_ref, sem.at[4])
        copy.start()
        for work in products:
            work()
        core = lax.rem(place_ref[0], 2)
        _, rows_conv, rows_out = rows_of
        stage_turned(stage1_ref, core, gc_ref, rows_conv, 0, slice(0, CUT // LANE))
        first_tiles = rows_conv // SUB * (CUT // LANE)
        stage_plain(stage1_ref, core, go_ref, rows_out, first_tiles)
        copies = stage_copies(stage1_ref, outs[0], outs[1], spans(CHUNKS[0], rows_of)[1], sem, 0)
        for each in copies:
            each.start()
        stage_turned(stage2_ref, core, gc_ref, rows_conv, 0, slice(CUT // LANE, INNER // LANE))
        more = stage_copies(stage2_ref, outs[2], outs[3], spans(CHUNKS[1], rows_of)[1], sem, 2)
        for each in more:
            each.start()
        for each in copies + more + [copy]:
            each.wait()
        sums_ref[0:1, :] = jnp.sum(acc_ref[0:8, :], axis=0, keepdims=True)
        sums_ref[1:2, :] = jnp.sum(acc_ref[8:16, :], axis=0, keepdims=True)


def stage_tiles(stage_ref, core, first_row, rows_each, base, block0, blocks, value):
    for g in range(value.shape[0] // SUB):
        row = first_row + g * SUB
        owner, inside = row // rows_each, row % rows_each // SUB
        side = core ^ (owner % 2)
        for b in range(value.shape[1] // LANE):
            tile = value[g * SUB : (g + 1) * SUB, b * LANE : (b + 1) * LANE]
            at = base + inside * blocks + block0 + b
            stage_ref[side, owner // 2, at] = tile.astype(BF16)


def stage_plain(stage_ref, core, grad_ref, rows_each, base):
    blocks = grad_ref.shape[1] // LANE
    for row in range(0, grad_ref.shape[0], SUB):
        part = grad_ref[row : row + SUB, :]
        stage_tiles(stage_ref, core, row, rows_each, base, 0, blocks, part)


def stage_turned(stage_ref, core, turned_ref, rows_each, base, blocks):
    count = blocks.stop - blocks.start
    for row in range(0, turned_ref.shape[1], LANE):
        for b in range(count):
            at = (blocks.start + b) * LANE
            part = jnp.transpose(turned_ref[at : at + LANE, row : row + LANE].astype(BF16))
            stage_tiles(stage_ref, core, row, rows_each, base, b, count, part)


def stage_copies(stage_ref, keep_ref, send_ref, used, sem, first):
    count = stage_ref.shape[2]
    if used < count:
        dims = stage_ref.shape[:2] + (count - used, SUB, LANE)
        stage_ref[:, :, used:] = jnp.zeros(dims, BF16)
    return [
        pltpu.make_async_copy(stage_ref.at[n], ref, sem.at[first + n])
        for n, ref in enumerate((keep_ref, send_ref))
    ]


def back_conv_kernel(
    last, rows_in, place_ref, low_ref, d_ref, high_ref, turned_ref, mask_ref, xhat_ref, rstd_ref, slope_ref, hid_ref, np_ref, *refs
):
    if last:
        before_ref, dpre_ref, sums_ref, keep_ref, send_ref, stage_ref = refs[:6]
    else:
        dpre_ref, sums_ref, part_ref = refs[:3]
    ext_ref, wt_ref, taps_ref, dmov_ref, grad_ref, acc_ref, sem = refs[-7:]
    step, steps = pl.program_id(0), pl.num_programs(0)
    tile = taps_ref.shape[0]
    open_sums(acc_ref)

    @pl.when(step == 0)
    def _():
        copies = load_window(place_ref, low_ref, d_ref, high_ref, ext_ref, sem)
        copies.append(pltpu.make_async_copy(turned_ref, wt_ref, sem.at[3]))
        if last:
            copies.append(pltpu.make_async_copy(before_ref, grad_ref, sem.at[4]))
        for copy in copies:
            copy.start()
        if not last:
            grad_ref[...] = jnp.zeros_like(grad_ref)
        for copy in copies:
            copy.wait()

    fill_taps(taps_ref, ext_ref, mask_ref, (steps * last + step) * tile)
    for half in halves_of(tile):
        dmov_ref[half, :] = lax.dot_general(
            taps_ref[half, :], wt_ref[...], NN, preferred_element_type=F32
        )

    def work(rows, _):
        live = mask_ref[rows, MID : MID + 1]
        sums = [0.0, 0.0]
        for b in lane_blocks(INNER):
            xhat = xhat_ref[rows, b].astype(F32)
            dy = dmov_ref[rows, b] * live * slope_ref[rows, b].astype(F32)
            add_terms(acc_ref, b, dy, xhat)
            dxhat = dy * np_ref[0:1, D + b.start : D + b.stop]
            dmov_ref[rows, b] = dxhat
            sums = [sums[0] + dxhat, sums[1] + dxhat * xhat]
        return row_means(sums, INNER) + [rstd_ref[rows, :]]

    def finish(rows, means):
        def put(b, value):
            dpre_ref[rows, b] = value.astype(BF16)

        norm_back(rows, dmov_ref, xhat_ref, means, put)

    in_stages(tile, [work, finish])
    close_sums(sums_ref, acc_ref)
    grad_ref[...] += lax.dot_general(dpre_ref[...], hid_ref[...], TN, preferred_element_type=F32)

    @pl.when(step == steps - 1)
    def _():
        if last:
            all_blocks = slice(0, INNER // LANE)
            stage_turned(stage_ref, lax.rem(place_ref[0], 2), grad_ref, rows_in, 0, all_blocks)
            used = rows_in // SUB * (INNER // LANE)
            run_copies(stage_copies(stage_ref, keep_ref, send_ref, used, sem, 0))
        else:
            run_copies([pltpu.make_async_copy(grad_ref, part_ref, sem.at[0])])


def back_a_kernel(pieces, half, place_ref, dpre0_ref, dpre1_ref, xhat_ref, rstd_ref, slope_ref, cot_ref, np_ref, *refs):
    piece_refs = refs[:pieces]
    grad_ref, sums_ref, w_ref, wt_ref, dh_ref, acc_ref, sem = refs[-7:]
    open_sums(acc_ref)

    @pl.when(pl.program_id(0) == 0)
    def _():
        run_copies(piece_copies(piece_refs, w_ref, place_ref[0], sem))
        for k in range(0, D, 256):
            wt_ref[:, k : k + 256] = jnp.transpose(w_ref[k : k + 256, :])

    second = (jnp.zeros((1, 1), jnp.int32) + pl.program_id(0)) >= half
    d_pre = jnp.where(second, dpre1_ref[...], dpre0_ref[...])
    dh_ref[...] = lax.dot_general(d_pre, wt_ref[...], NN, preferred_element_type=F32)

    def work(rows, _):
        sums = [0.0, 0.0]
        for b in lane_blocks(D):
            xhat = xhat_ref[rows, b].astype(F32)
            dy = dh_ref[rows, b] * slope_ref[rows, b].astype(F32)
            add_terms(acc_ref, b, dy, xhat)
            dxhat = dy * np_ref[0:1, b]
            dh_ref[rows, b] = dxhat
            sums = [sums[0] + dxhat, sums[1] + dxhat * xhat]
        return row_means(sums, D) + [rstd_ref[rows, :]]

    def finish(rows, means):
        def put(b, value):
            grad_ref[rows, b] = cot_ref[rows, b].astype(F32) + value

        norm_back(rows, dh_ref, xhat_ref, means, put)

    in_stages(dpre0_ref.shape[0], [work, finish])
    close_sums(sums_ref, acc_ref)


def out_kernel(pieces, place_ref, hid_ref, tok_ref, *refs):
    piece_refs = refs[:pieces]
    out_ref, w_ref, sem = refs[pieces:]

    @pl.when(pl.program_id(0) == 0)
    def _():
        run_copies(out_copies(piece_refs, w_ref, place_ref[0], sem))

    branch = lax.dot_general(hid_ref[...], w_ref[...], NN, preferred_element_type=F32)
    out_ref[...] = (tok_ref[...].astype(F32) + branch).astype(BF16)


WIDTHS = (INNER, INNER, D)
LANE0 = (0, INNER, 2 * INNER)
CUT = 2 * LANE
CHUNKS = (((1, 0, CUT), (2, 0, D)), ((1, CUT, INNER - CUT),), ((0, 0, INNER),))


def spans(chunk, rows):
    found, first = [], 0
    for weight, col, cols in chunk:
        tiles = rows[weight] // SUB * (cols // LANE)
        found.append((weight, col // LANE, cols // LANE, first, tiles))
        first += tiles
    return found, first


def column_sums(pack_ref, row, ref, chunk, rows):
    for weight, block0, blocks, first, tiles in spans(chunk, rows)[0]:

        def body(g, carry, first=first, blocks=blocks):
            new = []
            for b in range(blocks):
                value = ref[first + g * blocks + b].astype(F32)
                new.append(carry[b] + fold(value * value + 1e-30))
            return tuple(new)

        zero = tuple(jnp.zeros((8, LANE), F32) for _ in range(blocks))
        cols = lax.fori_loop(0, tiles // blocks, body, zero, unroll=5)
        for b in range(blocks):
            lane = LANE0[weight] + (block0 + b) * LANE
            pack_ref[row : row + 1, lane : lane + LANE] = jnp.sum(cols[b], axis=0, keepdims=True)


def load_full(refs, place_ref, first, full_ref, sem, at):
    pieces = refs[0].shape[0]
    each = full_ref.shape[0] // (len(refs) * pieces)
    outer = pieces if len(refs) == 2 else pieces // 2
    y = place_ref[2] % 2
    copies = []
    for n, (ref, side) in enumerate(zip(refs, (y, 1 - y))):
        for p in range(pieces):
            index = side * outer + p if len(refs) == 2 else p % 2 * outer + p // 2
            target = full_ref.at[pl.ds(index * each, each)]
            source = ref.at[p, first : first + each]
            copies.append(pltpu.make_async_copy(source, target, sem.at[at + n * pieces + p]))
    return copies


def load_list(bits, mine_ref, other_ref, place_ref, full_ref, sem):
    me, copies = place_ref[2], []
    each = full_ref.shape[0] // (1 << len(bits))
    inner = mine_ref.shape[0]
    for n in range(2 * inner):
        ref, at, k = (mine_ref, other_ref)[n // inner], n % inner, 0
        for i, bit in enumerate(bits):
            if n >> (len(bits) - 1 - i) & 1:
                k |= bit
        device, index = me ^ k, 0
        for bit in sorted(bits):
            index = index * 2 + lax.rem(lax.div(device, bit), 2)
        target = full_ref.at[pl.ds(index * each, each)]
        copies.append(pltpu.make_async_copy(ref.at[at], target, sem.at[n]))
    return copies


PACK_BLOCKS = (D + 2 * INNER) // LANE


def pack_line(pack_ref, row, lane0, width):
    parts = []
    for lane in range(lane0, lane0 + width, LANE):
        at = row * PACK_BLOCKS + lane // LANE
        parts.append(pack_ref[at // SUB, at % SUB : at % SUB + 1, :])
    return jnp.concatenate(parts, axis=1)


def pack_kernel(rows, pieces, place_ref, part_ref, *refs):
    states, sums, (pack_ref, acc_ref) = refs[0:3], refs[3:7], refs[7:9]
    pack_ref[...] = jnp.zeros_like(pack_ref)

    def add(row, lane, value):
        at = row * PACK_BLOCKS + lane // LANE
        pack_ref[at // SUB, at % SUB : at % SUB + 1, :] += value

    lanes_of = ((0, D), (D, D + INNER), (D, D + INNER), (D + INNER, D + 2 * INNER))
    for part, (lane0, lane1) in zip(sums, lanes_of):
        for lane in range(lane0, lane1, LANE):
            for row in range(2):
                add(row, lane, part[row : row + 1, lane - lane0 : lane - lane0 + LANE])
    lanes = lax.broadcasted_iota(jnp.int32, (1, LANE), 1)
    for k in range(3):
        total = jnp.sum(states[k][...].reshape(1, -1), axis=1, keepdims=True)
        add(3, 0, jnp.where(lanes == k, total, 0.0))
    acc_ref[...] = jnp.zeros_like(acc_ref)
    spare = acc_ref.shape[0] - 1
    outer = place_ref[3] // 2
    piece = place_ref[2] % 2 * outer + place_ref[2] // 2
    at = 0
    for chunk, each in zip(CHUNKS[:2], pieces):
        found, _ = spans(chunk, rows)
        start = piece * each

        def body(k, carry, found=found, start=start, at=at):
            n = start + k
            slot = spare
            for weight, block0, blocks, first, tiles in found:
                here = LANE0[weight] // LANE + block0 + lax.rem(jnp.maximum(n - first, 0), blocks)
                slot = jnp.where((n >= first) & (n < first + tiles), here, slot)
            value = part_ref[at + k].astype(F32)
            acc_ref[slot] += value * value + 1e-30
            return carry

        lax.fori_loop(0, each, body, 0, unroll=2)
        at += each
    for slot in range(spare):
        add(2, slot * LANE, jnp.sum(acc_ref[slot], axis=0, keepdims=True))


def pack_in_kernel(rows, bits, place_ref, mine_ref, other_ref, pack_ref, full_ref, sem):
    run_copies(load_list(bits, mine_ref, other_ref, place_ref, full_ref, sem))
    pack_ref[...] = jnp.zeros_like(pack_ref)
    column_sums(pack_ref, 0, full_ref, CHUNKS[2], rows)


def update_weight(
    k, squares, states_sum, source, weight, state, col_state, grad_ref, new, row_new_ref, col_new_ref, scratch, step=0, steps=1
):
    line_ref, state_ref, new_ref, scaled_ref = scratch
    width, fan, rows_here = WIDTHS[k], (D, KERNEL_TAPS * INNER, INNER)[k], state.shape[0]
    whole_rows = rows_here + -rows_here % LANE
    groups = rows_here // SUB // steps
    rate = 0.5 / fan**0.5

    def before():
        col_new = DECAY * col_state[...].reshape(1, -1) + (1.0 - DECAY) * (squares * (1.0 / fan))
        col_new_ref[...] = col_new.reshape(-1)
        total = DECAY * states_sum
        total = total + (1.0 - DECAY) * (1.0 / width) * jnp.sum(squares, axis=1, keepdims=True)
        scaled_ref[0:1, 0:width] = col_new / (total * (1.0 / fan))
        line_ref[0:1, 0:rows_here] = state[...].reshape(1, -1)
        for c in range(0, whole_rows, LANE):
            state_ref[c : c + LANE, :] = column(line_ref[0:1, c : c + LANE])

    def after():
        for c in range(0, whole_rows, LANE):
            line_ref[0:1, c : c + LANE] = jnp.transpose(new_ref[c : c + LANE, :])[0:1, :]
        row_new_ref[...] = line_ref[0:1, 0:rows_here].reshape(-1)

    def body(g, carry):
        here = pl.ds(pl.multiple_of(g * SUB, SUB), SUB)
        at = step * groups + g
        rows = pl.ds(pl.multiple_of(at * SUB, SUB), SUB)
        square = 0.0
        for ref, block0, blocks, first in source:
            for b in range(blocks):
                value = ref[first + at * blocks + b].astype(F32)
                grad_ref[here, (block0 + b) * LANE : (block0 + b + 1) * LANE] = value
                square = square + (value * value + 1e-30)
        mean = jnp.sum(square, axis=1, keepdims=True) * (1.0 / width)
        row_new = DECAY * state_ref[rows, :] + (1.0 - DECAY) * mean
        new_ref[rows, :] = row_new
        for ref, block0, blocks, first in source:
            for b in range(blocks):
                lanes = slice((block0 + b) * LANE, (block0 + b + 1) * LANE)
                value = ref[first + at * blocks + b].astype(F32)
                change = value * lax.rsqrt(row_new * scaled_ref[0:1, lanes])
                new[here, lanes] = weight[here, lanes] - rate * change
        return carry

    if steps == 1:
        before()
        lax.fori_loop(0, groups, body, 0, unroll=5)
        after()
    else:
        pl.when(step == 0)(before)
        lax.fori_loop(0, groups, body, 0, unroll=5)
        pl.when(step == steps - 1)(after)


def sources_of(chunk, ref, rows):
    return {w: (ref, block0, blocks, first) for w, block0, blocks, first, _ in spans(chunk, rows)[0]}


def update_kernel(rows, copies_of, place_ref, mine_ref, other_ref, pack_ref, *refs):
    weights, states, col_states = refs[0:2], refs[2:4], refs[4:6]
    grads, news, rows_new, cols_new = refs[6:8], refs[8:10], refs[10:12], refs[12:14]
    conv_scratch, out_scratch = refs[14:18], refs[18:22]
    full1_ref, full2_ref, sem = refs[22:25]
    both = (mine_ref, other_ref)
    count = 2 * mine_ref.shape[0]
    step, steps = pl.program_id(0), pl.num_programs(0)

    @pl.when(step == 0)
    def _():
        copies = load_full(both, place_ref, 0, full1_ref, sem, 0)
        copies += load_full(both, place_ref, full1_ref.shape[0] // count, full2_ref, sem, count)
        run_copies(copies)

    from1 = sources_of(CHUNKS[0], full1_ref, rows)
    from2 = sources_of(CHUNKS[1], full2_ref, rows)

    def update(n, k, source, scratch, *steps):
        squares = pack_line(pack_ref, 2, LANE0[k], WIDTHS[k])
        update_weight(
            k, squares, pack_line(pack_ref, 3, 0, LANE)[:, k : k + 1] * (1.0 / copies_of), source, weights[n],
            states[n], col_states[n], grads[n], news[n], rows_new[n], cols_new[n], scratch, *steps,
        )

    update(0, 1, [from1[1], from2[1]], conv_scratch, step, UPDATE_STEPS)

    @pl.when(step == steps - 1)
    def _():
        update(1, 2, [from1[2]], out_scratch)


def update_in_kernel(
    rows, copies_of, bits, place_ref, mine_ref, other_ref, pack_in_ref, pack_ref, np_ref, second_ref, *refs
):
    weight, state, col_state, grad_ref, new_ref, row_new_ref, col_new_ref = refs[0:7]
    ngrad_ref, nsecond_ref, nnew_ref = refs[7:10]
    full_ref, sem = refs[14:16]
    copies = load_list(bits, mine_ref, other_ref, place_ref, full_ref, sem)
    for copy in copies:
        copy.start()
    lines = [pack_line(pack_ref, row, 0, D + 2 * INNER) for row in range(2)]
    grad = jnp.concatenate(lines, axis=0)
    second = DECAY * second_ref[...] + (1.0 - DECAY) * (grad * grad + 1e-30)
    ngrad_ref[...] = grad
    nsecond_ref[...] = second
    nnew_ref[...] = np_ref[...] - 0.2 * grad * lax.rsqrt(second)
    for copy in copies:
        copy.wait()
    update_weight(
        0, pack_in_ref[0:1, :], pack_line(pack_ref, 3, 0, LANE)[:, 0:1] * (1.0 / copies_of),
        [sources_of(CHUNKS[2], full_ref, rows)[0]], weight, state, col_state, grad_ref, new_ref,
        row_new_ref, col_new_ref, refs[10:14],
    )


class Places:
    def __init__(self):
        self.seq, self.fsdp = lax.axis_size("seq"), lax.axis_size("fsdp")
        self.q = lax.axis_index("fsdp")
        self.s = lax.axis_index("seq")

    def flip(self, x, axis, bit):
        pairs = []
        for s in range(self.seq):
            for f in range(self.fsdp):
                s2, f2 = (s ^ bit, f) if axis == "seq" else (s, f ^ bit)
                pairs.append((s * self.fsdp + f, s2 * self.fsdp + f2))
        return lax.ppermute(x, AXES, pairs)


def bits_of(count):
    return [1 << k for k in range(count.bit_length() - 1)]


def tie(x, *others):
    return lax.optimization_barrier((x, *others))[0]


def gather_pieces(piece, place, after, later=()):
    found = {0: piece}
    for bit in reversed(bits_of(place.fsdp)):
        for k in list(found):
            moving = found[k]
            if bit == 1:
                moving = tie(moving, *((after,) if k == 0 or not later else later))
            found[k | bit] = place.flip(moving, "fsdp", bit)
    return [found[k] for k in range(place.fsdp)]


def sum_over(x, place, *axes):
    for axis in axes:
        for bit in bits_of(getattr(place, axis)):
            x = x + place.flip(x, axis, bit)
    return x


def pick(x, index, axis):
    return lax.dynamic_index_in_dim(x, index, axis=axis, keepdims=False)


class Reduction:
    def __init__(self, place, keep, send):
        self.place, self.near = place, keep
        self.got = place.flip(send, "fsdp", 1)

    def halve(self, axis, side, flip_axis, bit):
        dims = self.near.shape
        parts = dims[:axis] + (2, dims[axis] // 2) + dims[axis + 1 :]
        near, got = self.near.reshape(parts), self.got.reshape(parts)
        away = pick(near, 1 - side, axis).astype(F32) + pick(got, 1 - side, axis).astype(F32)
        self.near = pick(near, side, axis).astype(F32) + pick(got, side, axis).astype(F32)
        away = away.astype(BF16)
        self.got = self.place.flip(away, flip_axis, bit)
        return away

    def x(self):
        bit = self.place.fsdp // 2
        while bit > 1:
            away = self.halve(0, (self.place.q // bit) % 2, "fsdp", bit)
            bit //= 2
        return away

    def y(self):
        return self.halve(1, self.place.s % 2, "seq", 1)

    def seq_bit(self, bit):
        return self.halve(1, (self.place.s // bit) % 2, "seq", bit)

    def piece(self):
        total = self.near + self.got.astype(F32)
        return total.reshape(total.shape[1:])

    def pieces(self):
        total = (self.near + self.got.astype(F32)).astype(BF16)
        return total.reshape((self.place.seq // 2, -1) + total.shape[2:])


def arrive(result, *reductions):
    result, *gots = lax.optimization_barrier((result, *[r.got for r in reductions]))
    for reduction, got in zip(reductions, gots):
        reduction.got = got
    return result


def summed_f32(got):
    return jnp.sum(got.astype(F32), axis=0)


def summed(got):
    return summed_f32(got).astype(BF16)


def exchange(place, sent):
    line = [[y + 2 * z for z in range(place.seq // 2)] for y in range(2)]
    return lax.all_to_all(sent, "seq", 0, 0, axis_index_groups=line)


def on_device(
    tokens, input_mask, doc_lengths, cotangent, w_in, w_conv, w_out, norm_params,
    row_in, col_in, row_conv, col_conv, row_out, col_out, norm_second,
):
    place = Places()
    rows = tokens.shape[0]
    pieces = place.fsdp
    spots = jnp.stack(
        [place.q, (place.s * place.fsdp + place.q) * rows, place.s, place.seq]
    ).astype(jnp.int32)
    docs = doc_lengths.shape[0]
    live = input_mask.reshape(-1, LANE)
    weights = (w_in, w_conv, w_out)
    rows_of = [w.shape[0] for w in weights]

    tile_a, tile = 256, 512
    steps = rows // tile
    params_spec = whole(2, D + 2 * INNER)
    dma = pltpu.SemaphoreType.DMA

    out_sides = (w_out[:, : D // 2], w_out[:, D // 2 :])
    conv_out = jnp.concatenate([w_conv, *out_sides], axis=0).astype(BF16)
    hidden_a, slope_a, xhat_a, rstd_a = call(
        norm_a_kernel,
        (rows // tile_a,),
        [rows_spec(tile_a, D), params_spec],
        [rows_spec(tile_a, D)] * 3 + [rows_spec(tile_a, LANE)],
        [shape((rows, D), BF16)] * 3 + [shape((rows, LANE), F32)],
        us=17,
    )(tokens, tie(norm_params, conv_out))

    in_pieces = gather_pieces(w_in.astype(BF16), place, hidden_a)

    def in_call(tiles, count, before):
        at, stride = tiles

        def here_spec(width):
            return pl.BlockSpec((tile, width), lambda i: (at + stride * i, 0))

        out_shapes = [shape((rows, INNER), BF16)] * 3 + [shape((rows, LANE), F32)] * 2
        out_specs = [here_spec(INNER)] * 3 + [here_spec(LANE)] * 2
        if at == 0:
            out_shapes += [shape((REACH, INNER), BF16)] * 2
            out_specs += [whole(REACH, INNER)] * 2
        return call(
            functools.partial(in_kernel, pieces, tiles),
            (count,),
            [SMEM, whole(docs), here_spec(D), whole(*live.shape), params_spec]
            + [ANY] * (pieces + len(before)),
            out_specs,
            out_shapes,
            [pltpu.VMEM((D, INNER), BF16), pltpu.VMEM((tile, INNER), F32)]
            + [pltpu.VMEM((8, docs + -docs % LANE), F32), dma((pieces,))],
            us=3,
            aliases={5 + pieces + k: k for k in range(len(before))},
        )(spots, doc_lengths, hidden_a, live, norm_params, *in_pieces, *before)

    *kept, m_first, m_last = in_call((0, steps - 1), 2, ())
    moved, slope_b, xhat_b, rstd_b, masks = in_call((1, 1), steps - 2, kept)

    def halo(inner, outer):
        total = place.seq * place.fsdp
        across = [(i, i + 1 if i % 2 else i - 1) for i in range(1, total - 1)]
        return place.flip(inner, "fsdp", 1), lax.ppermute(outer, AXES, across)

    m_inner, m_outer = halo(m_first, m_last)
    conv_pieces = gather_pieces(conv_out, place, m_first, (moved, m_inner, m_outer))

    ext = pltpu.VMEM((rows + 2 * REACH, INNER), BF16)
    taps_wide = KERNEL_TAPS * INNER
    wide = pltpu.VMEM((taps_wide, INNER), BF16)
    shards = place.fsdp // 2

    def half_dims(chunk):
        count = spans(chunk, rows_of)[1]
        return (shards, count + -count % place.seq, SUB, LANE)

    def tile_spec(width, ahead):
        return pl.BlockSpec((tile, width), lambda i: (jnp.clip(i + ahead, 0, steps - 1), 0))

    halves = [half_dims(CHUNKS[0])] * 2 + [half_dims(CHUNKS[1])] * 2
    work = pltpu.VMEM((tile, INNER), F32)
    turned_tile = pltpu.VMEM((INNER, tile), BF16)
    hidden_c, d_conv, d_first, d_last, sums_c, turned, keep1, send1, keep2, send2 = call(
        functools.partial(conv_kernel, pieces, rows_of),
        (steps + 1,),
        [SMEM, ANY, ANY, ANY, tile_spec(LANE, 0), tile_spec(D, 0), tile_spec(D, -1), params_spec]
        + [ANY] * pieces,
        [tile_spec(INNER, 0)] * 2
        + [whole(REACH, INNER), whole(REACH, INNER), whole(2, INNER)]
        + [ANY] * 5,
        [
            shape((rows, INNER), BF16),
            shape((rows, INNER), BF16),
            shape((REACH, INNER), BF16),
            shape((REACH, INNER), BF16),
            shape((2, INNER), F32),
            shape((taps_wide, INNER), BF16),
        ]
        + [shape(dims, BF16) for dims in halves],
        [ext, wide, wide, pltpu.VMEM((INNER, D), BF16), pltpu.VMEM((D, INNER), BF16)]
        + [pltpu.VMEM((2, tile, taps_wide), BF16), work, work, work, turned_tile, turned_tile]
        + [pltpu.VMEM((INNER, taps_wide), F32), pltpu.VMEM((INNER, D), F32)]
        + [pltpu.VMEM((16, INNER), F32)]
        + [pltpu.VMEM((2,) + halves[0], BF16), pltpu.VMEM((2,) + halves[2], BF16)]
        + [dma((3 + 3 * pieces,))],
        us=45,
    )(
        spots, m_inner, moved, m_outer, masks, cotangent, cotangent, norm_params, *conv_pieces
    )
    d_inner, d_outer = halo(d_first, d_last)
    first, second = Reduction(place, keep1, send1), Reduction(place, keep2, send2)
    (block_out,) = call(
        functools.partial(out_kernel, pieces),
        (steps,),
        [SMEM, rows_spec(tile, INNER), rows_spec(tile, D)] + [ANY] * pieces,
        [rows_spec(tile, D)],
        [shape((rows, D), BF16)],
        [pltpu.VMEM((INNER, D), BF16), dma((2 * pieces,))],
        us=9,
    )(spots, hidden_c, tokens, *conv_pieces)

    def back_conv(last, spots, before):
        here = steps // 2
        at = here * last

        def here_spec(width):
            return pl.BlockSpec((tile, width), lambda i: (i + at, 0))

        dims = half_dims(CHUNKS[2])
        return call(
            functools.partial(back_conv_kernel, last, w_in.shape[0]),
            (here,),
            [SMEM] + [ANY] * 4
            + [here_spec(LANE), here_spec(INNER), here_spec(LANE), here_spec(INNER), here_spec(D)]
            + [params_spec]
            + [ANY] * last,
            [rows_spec(tile, INNER), whole(2, INNER)] + [ANY] * (1 + last),
            [shape((rows // 2, INNER), BF16), shape((2, INNER), F32)]
            + ([shape(dims, BF16)] * 2 if last else [shape((INNER, D), F32)]),
            ([pltpu.VMEM((2,) + dims, BF16)] if last else [])
            + [
                ext,
                wide,
                pltpu.VMEM((tile, taps_wide), BF16),
                pltpu.VMEM((tile, INNER), F32),
                pltpu.VMEM((INNER, D), F32),
                pltpu.VMEM((16, INNER), F32),
                dma((5,)),
            ],
            us=16,
        )(
            spots, d_inner, d_conv, d_outer, turned, masks, xhat_b, rstd_b, slope_b, hidden_a,
            norm_params, *before,
        )

    block_out, d_inner, d_outer = arrive((block_out, d_inner, d_outer), first, second)
    away = (first.x(), second.y())
    d_pre0, sums_b0, grad_part = back_conv(0, tie(spots, *away), ())
    d_pre0 = arrive(d_pre0, first, second)
    away = (first.y(), second.x())
    d_pre1, sums_b1, keep, send = back_conv(1, tie(spots, *away), (grad_part,))
    send = arrive(send, first, second)
    third = Reduction(place, keep, send)
    sent = jnp.concatenate([first.pieces(), second.pieces()], axis=1)
    got = exchange(place, sent)
    third.got = tie(third.got, sent)
    away = (sent, third.x())
    input_grad, sums_a = call(
        functools.partial(back_a_kernel, pieces, steps // 2),
        (steps,),
        [SMEM]
        + [
            pl.BlockSpec((tile, INNER), lambda i: (jnp.minimum(i, steps // 2 - 1), 0)),
            pl.BlockSpec((tile, INNER), lambda i: (jnp.maximum(i - steps // 2, 0), 0)),
        ]
        + [rows_spec(tile, D), rows_spec(tile, LANE), rows_spec(tile, D), rows_spec(tile, D)]
        + [params_spec]
        + [ANY] * pieces,
        [rows_spec(tile, D), whole(2, D)],
        [shape((rows, D), F32), shape((2, D), F32)],
        [
            pltpu.VMEM((D, INNER), BF16),
            pltpu.VMEM((INNER, D), BF16),
            pltpu.VMEM((tile, D), F32),
            pltpu.VMEM((16, D), F32),
            dma((pieces,)),
        ],
        us=17,
    )(
        tie(spots, *away), d_pre0, d_pre1, xhat_a, rstd_a, slope_a, cotangent, norm_params, *in_pieces
    )

    row_states, col_states = (row_in, row_conv, row_out), (col_in, col_conv, col_out)
    row_specs = [whole(*r.shape) for r in row_states]
    col_specs = [whole(*c.shape) for c in col_states]
    cols_all = D + 2 * INNER
    pack_dims = (4 * PACK_BLOCKS // SUB, SUB, LANE)
    pack_spec = whole(*pack_dims)
    fulls = [pltpu.VMEM(half_dims(c)[1:], BF16) for c in CHUNKS]
    sums = (sums_a, sums_b0, sums_b1, sums_c)
    got, third.got, input_grad = lax.optimization_barrier((got, third.got, input_grad))
    part = summed(got)
    sent = jnp.broadcast_to(part[None], (place.seq // 2,) + part.shape)
    mine = exchange(place, sent)
    third.got = tie(third.got, sent)
    away = third.y()
    (pack,) = call(
        functools.partial(pack_kernel, rows_of, [half_dims(c)[1] // place.seq for c in CHUNKS]),
        (1,),
        [SMEM, whole(*part.shape)] + row_specs + [whole(*x.shape) for x in sums],
        [pack_spec],
        [shape(pack_dims, F32)],
        [pltpu.VMEM((cols_all // LANE + 1, SUB, LANE), F32)],
        us=2,
        mib=16,
    )(tie(spots, away), part, *row_states, *sums)
    pack = sum_over(pack, place, "fsdp")
    third.got, pack = lax.optimization_barrier((third.got, pack))
    seq_bits = bits_of(place.seq)
    third.seq_bit(seq_bits[1])
    pack = pack + place.flip(pack, "seq", 1)
    mine, third.got, pack = lax.optimization_barrier((mine, third.got, pack))
    other = place.flip(mine, "seq", 1)
    for bit in seq_bits[2:]:
        third.seq_bit(bit)
    line = third.piece()
    piece_tiles = line.shape[0]
    for bit in seq_bits[:0:-1]:
        count = line.shape[0]
        flipped = place.flip(jnp.concatenate([line, pack], axis=0), "seq", bit)
        line = jnp.concatenate([line, flipped[:count]], axis=0)
        pack = pack + flipped[count:]
    line = line.astype(BF16).reshape((-1, piece_tiles) + line.shape[1:])
    line, other, pack = lax.optimization_barrier((line, other, pack))
    line_other = place.flip(line, "seq", 1)
    list_bits = [1] + seq_bits[1:]

    def update_scratch(weight):
        lines = weight.shape[0] + -weight.shape[0] % LANE
        return (
            [pltpu.VMEM((8, lines), F32)]
            + [pltpu.VMEM((lines, LANE), F32)] * 2
            + [pltpu.VMEM((8, weight.shape[1]), F32)]
        )

    weight_specs = [whole(*w.shape) for w in weights]
    conv_block = pl.BlockSpec((w_conv.shape[0] // UPDATE_STEPS, INNER), lambda i: (i, 0))
    both_specs = [conv_block, weight_specs[2]]
    results = call(
        functools.partial(update_kernel, rows_of, place.seq),
        (UPDATE_STEPS,),
        [SMEM, ANY, ANY, pack_spec] + both_specs + row_specs[1:] + col_specs[1:],
        both_specs * 2 + row_specs[1:] + col_specs[1:],
        [shape(w.shape, F32) for w in weights[1:]] * 2
        + [shape(r.shape, F32) for r in row_states[1:] + col_states[1:]],
        update_scratch(w_conv)
        + update_scratch(w_out)
        + fulls[:2]
        + [dma((2 * place.seq,))],
        us=8,
        mib=32,
    )(spots, mine, other, pack, *weights[1:], *row_states[1:], *col_states[1:])
    grad_conv, grad_out, new_conv, new_out, row_conv_new, row_out_new, col_conv_new, col_out_new = (
        results
    )
    line_other, grad_out = lax.optimization_barrier((line_other, grad_out))
    (pack_in,) = call(
        functools.partial(pack_in_kernel, rows_of, list_bits),
        (1,),
        [SMEM, ANY, ANY],
        [whole(8, INNER)],
        [shape((8, INNER), F32)],
        [fulls[2], dma((place.seq,))],
        us=2,
        mib=16,
    )(spots, line, line_other)
    pack_in = sum_over(pack_in, place, "fsdp")
    grad_in, new_in, row_in_new, col_in_new, *norm_results = call(
        functools.partial(update_in_kernel, rows_of, place.seq, list_bits),
        (1,),
        [SMEM, ANY, ANY, whole(8, INNER), pack_spec, params_spec, params_spec]
        + [weight_specs[0], row_specs[0], col_specs[0]],
        [weight_specs[0]] * 2 + [row_specs[0], col_specs[0]] + [params_spec] * 3,
        [shape(w_in.shape, F32)] * 2
        + [shape(row_in.shape, F32), shape(col_in.shape, F32)]
        + [shape((2, cols_all), F32)] * 3,
        update_scratch(w_in) + [fulls[2], dma((place.seq,))],
        us=4,
        mib=24,
    )(
        spots, line, line_other, pack_in, pack, norm_params, norm_second, w_in, row_in, col_in
    )
    return (
        block_out,
        input_grad,
        grad_in,
        grad_conv,
        grad_out,
        new_in,
        new_conv,
        new_out,
        row_in_new,
        col_in_new,
        row_conv_new,
        col_conv_new,
        row_out_new,
        col_out_new,
        *norm_results,
    )


def solution(mesh):
    both, rows = P(AXES, None), P("fsdp", None)
    in_specs = (
        both, P(AXES), P(), both, rows, rows, rows, P(),
        P("fsdp"), P(), P("fsdp"), P(), P("fsdp"), P(), P(),
    )
    out_specs = (
        both, both, rows, rows, rows, rows, rows, rows,
        P("fsdp"), P(), P("fsdp"), P(), P("fsdp"), P(), P(), P(), P(),
    )
    return jax.shard_map(
        on_device, mesh=mesh, in_specs=in_specs, out_specs=out_specs, check_vma=False
    )
```

```python
import functools
import math

import jax
import jax.numpy as jnp
from jax import lax
from jax.experimental import pallas as pl
from jax.experimental.pallas import tpu as pltpu
from jax.sharding import PartitionSpec as P

D = 1280
INNER = 640
KERNEL_TAPS = 5
DILATION_STEP = 128
STEP = 10
EPSILON = 1e-05
DECAY = 1.0 - STEP ** (-0.8)

REACH = (KERNEL_TAPS - 1) // 2 * DILATION_STEP
MID = (KERNEL_TAPS - 1) // 2
F32 = jnp.float32
BF16 = jnp.bfloat16
SUB, LANE = 16, 128
AXES = ("seq", "fsdp")
NT = (((1,), (1,)), ((), ()))
TN = (((0,), (0,)), ((), ()))
NN = (((1,), (0,)), ((), ()))


def call(kernel, grid, in_specs, out_specs, out_shape, scratch=(), us=1.0, aliases=None, mib=58):
    params = pltpu.CompilerParams(
        vmem_limit_bytes=mib * 1024 * 1024, dimension_semantics=("arbitrary",) * len(grid)
    )
    return pl.pallas_call(
        kernel,
        grid=grid,
        in_specs=in_specs,
        out_specs=out_specs,
        out_shape=out_shape,
        scratch_shapes=list(scratch),
        compiler_params=params,
        input_output_aliases=aliases or {},
        cost_estimate=pl.CostEstimate(
                flops=int(us * 1.1e9), bytes_accessed=int(us * 3.4e6), transcendentals=0
        ),
    )


def shape(dims, dtype):
    return jax.ShapeDtypeStruct(dims, dtype)


def rows_spec(tile, width):
    return pl.BlockSpec((tile, width), lambda i: (i, 0))


def whole(*dims):
    return pl.BlockSpec(dims, lambda *_: (0,) * len(dims))


ANY = pl.BlockSpec(memory_space=pl.ANY)
SMEM = pl.BlockSpec(memory_space=pltpu.SMEM)


ERFC_P = 0.47 / math.sqrt(2.0)
ERFC_C = (
    0.12357219400743558,
    0.1999878668208835,
    -0.08033356004356296,
    0.3660253986657854,
    -0.1092519747040215,
)
LOG2E = 1.4426950408889634


def gelu_and_slope(y):
    t = pltpu.reciprocal(1.0 + ERFC_P * jnp.abs(y), approx=True)
    bell = jnp.exp2(y * y * (-0.5 * LOG2E))
    poly = ERFC_C[4] * t + ERFC_C[3]
    for c in ERFC_C[2::-1]:
        poly = poly * t + c
    tail = poly * t * bell
    cdf = jnp.where(y > 0.0, 1.0 - tail, tail)
    return y * cdf, cdf + y * (bell * (1.0 / math.sqrt(2.0 * math.pi)))


def lane_blocks(width):
    return [slice(k, k + LANE) for k in range(0, width, LANE)]


def row_stats(ref, rows):
    width = ref.shape[-1]
    blocks = lane_blocks(width)
    total = ref[rows, blocks[0]].astype(F32)
    for b in blocks[1:]:
        total = total + ref[rows, b].astype(F32)
    mean = jnp.sum(total, axis=-1, keepdims=True) * (1.0 / width)
    square = None
    for b in blocks:
        centered = ref[rows, b].astype(F32) - mean
        square = centered * centered if square is None else square + centered * centered
    variance = jnp.sum(square, axis=-1, keepdims=True) * (1.0 / width)
    return mean, lax.rsqrt(variance + EPSILON)


def fold(values):
    total = values[0:8]
    for k in range(8, values.shape[0], 8):
        total = total + values[k : k + 8]
    return total


def in_stages(count, stages, between=()):
    chunks = [slice(k, k + CHUNK) for k in range(0, count, CHUNK)]
    kept, rounds = {}, len(chunks) + len(stages) - 1
    for t in range(rounds):
        for n, stage in enumerate(stages):
            if 0 <= t - n < len(chunks):
                kept[n, t - n] = stage(chunks[t - n], kept.get((n - 1, t - n)))
        for work in between[t * len(between) // rounds : (t + 1) * len(between) // rounds]:
            work()


def halves_of(count):
    return (slice(0, count // 2), slice(count // 2, count))


def row_means(sums, width):
    return [jnp.sum(x, axis=-1, keepdims=True) * (1.0 / width) for x in sums]


def norm_back(rows, dxhat_ref, xhat_ref, means, put):
    mean_d, mean_dx, rstd = means
    for b in lane_blocks(dxhat_ref.shape[-1]):
        xhat = xhat_ref[rows, b].astype(F32)
        put(b, (dxhat_ref[rows, b] - mean_d - xhat * mean_dx) * rstd)


def add_terms(acc_ref, b, dy, xhat):
    acc_ref[0:8, b] += fold(dy * xhat)
    acc_ref[8:16, b] += fold(dy)


def open_sums(acc_ref):
    @pl.when(pl.program_id(0) == 0)
    def _():
        acc_ref[...] = jnp.zeros_like(acc_ref)


def close_sums(out_ref, acc_ref):
    @pl.when(pl.program_id(0) == pl.num_programs(0) - 1)
    def _():
        out_ref[0:1, :] = jnp.sum(acc_ref[0:8, :], axis=0, keepdims=True)
        out_ref[1:2, :] = jnp.sum(acc_ref[8:16, :], axis=0, keepdims=True)


def run_copies(copies):
    for copy in copies:
        copy.start()
    for copy in copies:
        copy.wait()


def piece_copies(pieces, full_ref, me, sem, first=0):
    each = full_ref.shape[0] // len(pieces)
    return [
        pltpu.make_async_copy(
            piece.at[0:each, :],
            full_ref.at[pl.ds(pl.multiple_of((me ^ k) * each, SUB), each), :],
            sem.at[first + k],
        )
        for k, piece in enumerate(pieces)
    ]


def out_copies(pieces, full_ref, me, sem, first=0):
    each, width = full_ref.shape[0] // len(pieces), full_ref.shape[1] // 2
    copies = []
    for k, piece in enumerate(pieces):
        rows = pl.ds(pl.multiple_of((me ^ k) * each, SUB), each)
        for side in range(2):
            at = piece.shape[0] - (2 - side) * each
            copies.append(
                pltpu.make_async_copy(
                    piece.at[at : at + each, :],
                    full_ref.at[rows, side * width : (side + 1) * width],
                    sem.at[first + 2 * k + side],
                )
            )
    return copies


def column(row):
    return jnp.transpose(jnp.broadcast_to(row, (LANE, LANE)))


CHUNK = 64
UPDATE_STEPS = 5
TURNED = 2


def norm_a_kernel(tok_ref, np_ref, hid_ref, slope_ref, xhat_ref, rstd_ref):
    def stats(rows, _):
        mean, rstd = row_stats(tok_ref, rows)
        rstd_ref[rows, :] = jnp.broadcast_to(rstd, (CHUNK, LANE))
        return mean, rstd

    def work(rows, kept):
        mean, rstd = kept
        for b in lane_blocks(D):
            xhat = (tok_ref[rows, b].astype(F32) - mean) * rstd
            hidden, slope = gelu_and_slope(xhat * np_ref[0:1, b] + np_ref[1:2, b])
            hid_ref[rows, b] = hidden.astype(BF16)
            slope_ref[rows, b] = slope.astype(BF16)
            xhat_ref[rows, b] = xhat.astype(BF16)

    in_stages(tok_ref.shape[0], [stats, work])


def running_ends(ends_ref, lengths_ref):
    docs, width = lengths_ref.shape[0], ends_ref.shape[1]
    ends_ref[...] = jnp.zeros_like(ends_ref)
    ends_ref[0:1, 0:docs] = lengths_ref[...].reshape(1, -1).astype(F32)
    before = jnp.zeros((1, 1), F32)
    row = lax.broadcasted_iota(jnp.int32, (LANE, LANE), 0)
    lane = lax.broadcasted_iota(jnp.int32, (LANE, LANE), 1)
    for k in range(0, width, LANE):
        line = ends_ref[0:1, k : k + LANE]
        sums = jnp.sum(jnp.where(row <= lane, column(line), 0.0), axis=0, keepdims=True) + before
        ends_ref[0:1, k : k + LANE] = jnp.where(lane[0:1] + k < docs, sums, 1e9)
        before = before + jnp.sum(line, axis=1, keepdims=True)


def in_kernel(pieces, tiles, place_ref, lengths_ref, hid_ref, live_ref, np_ref, *refs):
    piece_refs = refs[:pieces]
    edges = tiles[0] == 0
    outs = refs[-(11 if edges else 9) :]
    mov_ref, slope_ref, xhat_ref, rstd_ref, mask_ref = outs[:5]
    w_ref, pre_ref, ends_ref, sem = outs[-4:]
    step = pl.program_id(0)
    tile = hid_ref.shape[0]

    @pl.when(step == 0)
    def _():
        copies = piece_copies(piece_refs, w_ref, place_ref[0], sem)
        for copy in copies:
            copy.start()
        running_ends(ends_ref, lengths_ref)
        for copy in copies:
            copy.wait()

    for half in halves_of(tile):
        pre_ref[half, :] = lax.dot_general(
            hid_ref[half, :], w_ref[...], NN, preferred_element_type=F32
        )

    at_tile = tiles[0] + step * tiles[1]
    first = place_ref[1] + at_tile * tile
    ends = ends_ref[0:1, :]
    lanes = lax.broadcasted_iota(jnp.int32, (LANE, LANE), 1)
    offsets = ((lanes - MID) * DILATION_STEP).astype(F32)
    for k in range(tile // LANE):
        at = (first + k * LANE + lax.broadcasted_iota(jnp.int32, (LANE, 1), 0)).astype(F32)
        begin = jnp.max(jnp.where(ends <= at, ends, 0.0), axis=1, keepdims=True)
        end = jnp.min(jnp.where(ends > at, ends, 1e9), axis=1, keepdims=True)
        there = at + offsets
        same = jnp.where((there >= begin) & (there < end), 1.0, 0.0)
        live = column(live_ref[pl.ds(at_tile * (tile // LANE) + k, 1), :].astype(F32))
        mask_ref[k * LANE : (k + 1) * LANE, :] = jnp.where(lanes == MID, live, same)

    def stats(rows, _):
        mean, rstd = row_stats(pre_ref, rows)
        rstd_ref[rows, :] = jnp.broadcast_to(rstd, (CHUNK, LANE))
        return mean, rstd

    def work(rows, kept):
        mean, rstd = kept
        live = mask_ref[rows, MID : MID + 1]
        for b in lane_blocks(INNER):
            gains = slice(D + b.start, D + b.stop)
            xhat = (pre_ref[rows, b] - mean) * rstd
            hidden, slope = gelu_and_slope(xhat * np_ref[0:1, gains] + np_ref[1:2, gains])
            mov_ref[rows, b] = (hidden * live).astype(BF16)
            slope_ref[rows, b] = slope.astype(BF16)
            xhat_ref[rows, b] = xhat.astype(BF16)

    in_stages(tile, [stats, work])
    if edges:
        put_edges(place_ref, outs[5], outs[6], mov_ref, step == 0, step == 1)


def load_window(place_ref, inner, mid, outer, ext_ref, sem):
    rows, core = mid.shape[0], lax.rem(place_ref[0], 2)
    near = pl.multiple_of((1 - core) * (REACH + rows), SUB)
    far = pl.multiple_of(core * (REACH + rows), SUB)
    return [
        pltpu.make_async_copy(inner, ext_ref.at[pl.ds(near, REACH), :], sem.at[0]),
        pltpu.make_async_copy(mid, ext_ref.at[REACH : REACH + rows, :], sem.at[1]),
        pltpu.make_async_copy(outer, ext_ref.at[pl.ds(far, REACH), :], sem.at[2]),
    ]


def put_edges(place_ref, inner_ref, outer_ref, tile_ref, at_first, at_last):
    rows, core = tile_ref.shape[0], lax.rem(place_ref[0], 2)
    for at, edge, first in ((at_first, slice(0, REACH), 0), (at_last, slice(rows - REACH, rows), 1)):

        @pl.when(at & (core == first))
        def _(edge=edge):
            outer_ref[...] = tile_ref[edge, :]

        @pl.when(at & (core != first))
        def _(edge=edge):
            inner_ref[...] = tile_ref[edge, :]


def fill_taps(taps_ref, ext_ref, mask_ref, start):
    tile = taps_ref.shape[0]
    for j in range(KERNEL_TAPS):
        rows = pl.ds(pl.multiple_of(start + j * DILATION_STEP, DILATION_STEP), tile)
        picked = ext_ref[rows, :]
        if j != MID:
            picked = picked * mask_ref[:, j : j + 1].astype(BF16)
        taps_ref[:, j * INNER : (j + 1) * INNER] = picked


def conv_kernel(
    pieces, rows_of, place_ref, low_ref, mov_ref, high_ref, mask_ref, cot_ref, before_ref, np_ref, *refs
):
    piece_refs = refs[:pieces]
    hid_ref, dconv_ref, inner_ref, outer_ref, sums_ref, turned_ref = refs[pieces : pieces + 6]
    outs = refs[pieces + 6 : pieces + 10]
    ext_ref, wc_ref, wct_ref, wo_ref, wt_ref, taps_ref, pre_ref, dh_ref, xhat_ref = refs[
        pieces + 10 : pieces + 19
    ]
    dt_ref, ht_ref, gc_ref, go_ref, acc_ref, stage1_ref, stage2_ref, sem = refs[pieces + 19 :]
    step, steps = pl.program_id(0), pl.num_programs(0) - 1
    tile = taps_ref.shape[1]
    slot = lax.rem(step, 2)

    @pl.when(step == 0)
    def _():
        me = place_ref[0]
        outs = out_copies(piece_refs, wo_ref, me, sem, 3)
        rest = load_window(place_ref, low_ref, mov_ref, high_ref, ext_ref, sem)
        rest += piece_copies(piece_refs, wc_ref, me, sem, 3 + 2 * pieces)
        for copy in outs + rest:
            copy.start()
        for ref in (acc_ref, gc_ref, go_ref):
            ref[...] = jnp.zeros_like(ref)
        for copy in outs:
            copy.wait()
        for k in range(0, D, 256):
            wt_ref[k : k + 256, :] = jnp.transpose(wo_ref[:, k : k + 256])
        for copy in rest:
            copy.wait()

    def grad_conv(cols):
        def work():
            gc_ref[:, cols] += lax.dot_general(
                dt_ref[...], taps_ref[1 - slot, :, cols], NN, preferred_element_type=F32
            )

        return work

    def grad_out(cols):
        def work():
            go_ref[:, cols] += lax.dot_general(
                ht_ref[...], before_ref[:, cols], NN, preferred_element_type=F32
            )

        return work

    taps_wide = KERNEL_TAPS * INNER
    products = [grad_conv(slice(k, min(k + 768, taps_wide))) for k in range(0, taps_wide, 768)]
    products += [grad_out(slice(k, min(k + 768, D))) for k in range(0, D, 768)]

    def tile_work(products, turned):
        fill_taps(taps_ref.at[slot], ext_ref, mask_ref, step * tile)
        pre_ref[...] = lax.dot_general(
            taps_ref[slot], wc_ref[...], NN, preferred_element_type=F32
        )
        dh_ref[...] = lax.dot_general(cot_ref[...], wt_ref[...], NN, preferred_element_type=F32)
        for n in range(turned):
            tap = jnp.minimum(turned * (step - 1) + n, KERNEL_TAPS - 1)
            source = wc_ref[pl.ds(pl.multiple_of(tap * INNER, SUB), INNER), :]
            target = pl.multiple_of((KERNEL_TAPS - 1 - tap) * INNER, SUB)
            wct_ref[pl.ds(target, INNER), :] = jnp.transpose(source)

        def stats(rows, _):
            return row_stats(pre_ref, rows)

        def work(rows, kept):
            mean, rstd = kept
            sums = [0.0, 0.0]
            for b in lane_blocks(INNER):
                gains = slice(D + INNER + b.start, D + INNER + b.stop)
                gain = np_ref[0:1, gains]
                xhat = (pre_ref[rows, b] - mean) * rstd
                hidden, slope = gelu_and_slope(xhat * gain + np_ref[1:2, gains])
                hid_ref[rows, b] = hidden.astype(BF16)
                dy = dh_ref[rows, b] * slope
                add_terms(acc_ref, b, dy, xhat)
                dxhat = dy * gain
                xhat_ref[rows, b] = xhat
                dh_ref[rows, b] = dxhat
                sums = [sums[0] + dxhat, sums[1] + dxhat * xhat]
            return row_means(sums, INNER) + [rstd]

        def finish(rows, means):
            def put(b, value):
                dconv_ref[rows, b] = value.astype(BF16)

            norm_back(rows, dh_ref, xhat_ref, means, put)

        in_stages(tile, [stats, work, finish], products)
        dt_ref[...] = jnp.transpose(dconv_ref[...])
        ht_ref[...] = jnp.transpose(hid_ref[...])

    @pl.when(step == 0)
    def _():
        tile_work([], 0)

    @pl.when((step > 0) & (step < steps))
    def _():
        tile_work(products, TURNED)

    put_edges(place_ref, inner_ref, outer_ref, dconv_ref, step == 0, step == steps - 1)

    @pl.when(step == steps)
    def _():
        copy = pltpu.make_async_copy(wct_ref, turned_ref, sem.at[4])
        copy.start()
        for work in products:
            work()
        core = lax.rem(place_ref[0], 2)
        _, rows_conv, rows_out = rows_of
        stage_turned(stage1_ref, core, gc_ref, rows_conv, 0, slice(0, CUT // LANE))
        first_tiles = rows_conv // SUB * (CUT // LANE)
        stage_plain(stage1_ref, core, go_ref, rows_out, first_tiles)
        copies = stage_copies(stage1_ref, outs[0], outs[1], spans(CHUNKS[0], rows_of)[1], sem, 0)
        for each in copies:
            each.start()
        stage_turned(stage2_ref, core, gc_ref, rows_conv, 0, slice(CUT // LANE, INNER // LANE))
        more = stage_copies(stage2_ref, outs[2], outs[3], spans(CHUNKS[1], rows_of)[1], sem, 2)
        for each in more:
            each.start()
        for each in copies + more + [copy]:
            each.wait()
        sums_ref[0:1, :] = jnp.sum(acc_ref[0:8, :], axis=0, keepdims=True)
        sums_ref[1:2, :] = jnp.sum(acc_ref[8:16, :], axis=0, keepdims=True)


def stage_tiles(stage_ref, core, first_row, rows_each, base, block0, blocks, value):
    for g in range(value.shape[0] // SUB):
        row = first_row + g * SUB
        owner, inside = row // rows_each, row % rows_each // SUB
        side = core ^ (owner % 2)
        for b in range(value.shape[1] // LANE):
            tile = value[g * SUB : (g + 1) * SUB, b * LANE : (b + 1) * LANE]
            at = base + inside * blocks + block0 + b
            stage_ref[side, owner // 2, at] = tile.astype(BF16)


def stage_plain(stage_ref, core, grad_ref, rows_each, base):
    blocks = grad_ref.shape[1] // LANE
    for row in range(0, grad_ref.shape[0], SUB):
        part = grad_ref[row : row + SUB, :]
        stage_tiles(stage_ref, core, row, rows_each, base, 0, blocks, part)


def stage_turned(stage_ref, core, turned_ref, rows_each, base, blocks):
    count = blocks.stop - blocks.start
    for row in range(0, turned_ref.shape[1], LANE):
        for b in range(count):
            at = (blocks.start + b) * LANE
            part = jnp.transpose(turned_ref[at : at + LANE, row : row + LANE].astype(BF16))
            stage_tiles(stage_ref, core, row, rows_each, base, b, count, part)


def stage_copies(stage_ref, keep_ref, send_ref, used, sem, first):
    count = stage_ref.shape[2]
    if used < count:
        dims = stage_ref.shape[:2] + (count - used, SUB, LANE)
        stage_ref[:, :, used:] = jnp.zeros(dims, BF16)
    return [
        pltpu.make_async_copy(stage_ref.at[n], ref, sem.at[first + n])
        for n, ref in enumerate((keep_ref, send_ref))
    ]


def back_conv_kernel(
    last, rows_in, place_ref, low_ref, d_ref, high_ref, turned_ref, mask_ref, xhat_ref, rstd_ref, slope_ref, hid_ref, np_ref, *refs
):
    if last:
        before_ref, dpre_ref, sums_ref, keep_ref, send_ref, stage_ref = refs[:6]
    else:
        dpre_ref, sums_ref, part_ref = refs[:3]
    ext_ref, wt_ref, taps_ref, dmov_ref, grad_ref, acc_ref, sem = refs[-7:]
    step, steps = pl.program_id(0), pl.num_programs(0)
    tile = taps_ref.shape[0]
    open_sums(acc_ref)

    @pl.when(step == 0)
    def _():
        copies = load_window(place_ref, low_ref, d_ref, high_ref, ext_ref, sem)
        copies.append(pltpu.make_async_copy(turned_ref, wt_ref, sem.at[3]))
        if last:
            copies.append(pltpu.make_async_copy(before_ref, grad_ref, sem.at[4]))
        for copy in copies:
            copy.start()
        if not last:
            grad_ref[...] = jnp.zeros_like(grad_ref)
        for copy in copies:
            copy.wait()

    fill_taps(taps_ref, ext_ref, mask_ref, (steps * last + step) * tile)
    for half in halves_of(tile):
        dmov_ref[half, :] = lax.dot_general(
            taps_ref[half, :], wt_ref[...], NN, preferred_element_type=F32
        )

    def work(rows, _):
        live = mask_ref[rows, MID : MID + 1]
        sums = [0.0, 0.0]
        for b in lane_blocks(INNER):
            xhat = xhat_ref[rows, b].astype(F32)
            dy = dmov_ref[rows, b] * live * slope_ref[rows, b].astype(F32)
            add_terms(acc_ref, b, dy, xhat)
            dxhat = dy * np_ref[0:1, D + b.start : D + b.stop]
            dmov_ref[rows, b] = dxhat
            sums = [sums[0] + dxhat, sums[1] + dxhat * xhat]
        return row_means(sums, INNER) + [rstd_ref[rows, :]]

    def finish(rows, means):
        def put(b, value):
            dpre_ref[rows, b] = value.astype(BF16)

        norm_back(rows, dmov_ref, xhat_ref, means, put)

    in_stages(tile, [work, finish])
    close_sums(sums_ref, acc_ref)
    grad_ref[...] += lax.dot_general(dpre_ref[...], hid_ref[...], TN, preferred_element_type=F32)

    @pl.when(step == steps - 1)
    def _():
        if last:
            all_blocks = slice(0, INNER // LANE)
            stage_turned(stage_ref, lax.rem(place_ref[0], 2), grad_ref, rows_in, 0, all_blocks)
            used = rows_in // SUB * (INNER // LANE)
            run_copies(stage_copies(stage_ref, keep_ref, send_ref, used, sem, 0))
        else:
            run_copies([pltpu.make_async_copy(grad_ref, part_ref, sem.at[0])])


def back_a_kernel(pieces, half, place_ref, dpre0_ref, dpre1_ref, xhat_ref, rstd_ref, slope_ref, cot_ref, np_ref, *refs):
    piece_refs = refs[:pieces]
    grad_ref, sums_ref, w_ref, wt_ref, dh_ref, acc_ref, sem = refs[-7:]
    open_sums(acc_ref)

    @pl.when(pl.program_id(0) == 0)
    def _():
        run_copies(piece_copies(piece_refs, w_ref, place_ref[0], sem))
        for k in range(0, D, 256):
            wt_ref[:, k : k + 256] = jnp.transpose(w_ref[k : k + 256, :])

    second = (jnp.zeros((1, 1), jnp.int32) + pl.program_id(0)) >= half
    d_pre = jnp.where(second, dpre1_ref[...], dpre0_ref[...])
    dh_ref[...] = lax.dot_general(d_pre, wt_ref[...], NN, preferred_element_type=F32)

    def work(rows, _):
        sums = [0.0, 0.0]
        for b in lane_blocks(D):
            xhat = xhat_ref[rows, b].astype(F32)
            dy = dh_ref[rows, b] * slope_ref[rows, b].astype(F32)
            add_terms(acc_ref, b, dy, xhat)
            dxhat = dy * np_ref[0:1, b]
            dh_ref[rows, b] = dxhat
            sums = [sums[0] + dxhat, sums[1] + dxhat * xhat]
        return row_means(sums, D) + [rstd_ref[rows, :]]

    def finish(rows, means):
        def put(b, value):
            grad_ref[rows, b] = cot_ref[rows, b].astype(F32) + value

        norm_back(rows, dh_ref, xhat_ref, means, put)

    in_stages(dpre0_ref.shape[0], [work, finish])
    close_sums(sums_ref, acc_ref)


def out_kernel(pieces, place_ref, hid_ref, tok_ref, *refs):
    piece_refs = refs[:pieces]
    out_ref, w_ref, sem = refs[pieces:]

    @pl.when(pl.program_id(0) == 0)
    def _():
        run_copies(out_copies(piece_refs, w_ref, place_ref[0], sem))

    branch = lax.dot_general(hid_ref[...], w_ref[...], NN, preferred_element_type=F32)
    out_ref[...] = (tok_ref[...].astype(F32) + branch).astype(BF16)


WIDTHS = (INNER, INNER, D)
LANE0 = (0, INNER, 2 * INNER)
CUT = 2 * LANE
CHUNKS = (((1, 0, CUT), (2, 0, D)), ((1, CUT, INNER - CUT),), ((0, 0, INNER),))


def spans(chunk, rows):
    found, first = [], 0
    for weight, col, cols in chunk:
        tiles = rows[weight] // SUB * (cols // LANE)
        found.append((weight, col // LANE, cols // LANE, first, tiles))
        first += tiles
    return found, first


def column_sums(pack_ref, row, ref, chunk, rows):
    for weight, block0, blocks, first, tiles in spans(chunk, rows)[0]:

        def body(g, carry, first=first, blocks=blocks):
            new = []
            for b in range(blocks):
                value = ref[first + g * blocks + b].astype(F32)
                new.append(carry[b] + fold(value * value + 1e-30))
            return tuple(new)

        zero = tuple(jnp.zeros((8, LANE), F32) for _ in range(blocks))
        cols = lax.fori_loop(0, tiles // blocks, body, zero, unroll=5)
        for b in range(blocks):
            lane = LANE0[weight] + (block0 + b) * LANE
            pack_ref[row : row + 1, lane : lane + LANE] = jnp.sum(cols[b], axis=0, keepdims=True)


def load_full(refs, place_ref, first, full_ref, sem, at):
    pieces = refs[0].shape[0]
    each = full_ref.shape[0] // (len(refs) * pieces)
    outer = pieces if len(refs) == 2 else pieces // 2
    y = place_ref[2] % 2
    copies = []
    for n, (ref, side) in enumerate(zip(refs, (y, 1 - y))):
        for p in range(pieces):
            index = side * outer + p if len(refs) == 2 else p % 2 * outer + p // 2
            target = full_ref.at[pl.ds(index * each, each)]
            source = ref.at[p, first : first + each]
            copies.append(pltpu.make_async_copy(source, target, sem.at[at + n * pieces + p]))
    return copies


def load_halves(mine_ref, other_ref, place_ref, full_ref, sem):
    y, each = lax.rem(place_ref[2], 2), mine_ref.shape[0]
    return [
        pltpu.make_async_copy(ref, full_ref.at[pl.ds(side * each, each)], sem.at[n])
        for n, (ref, side) in enumerate(((mine_ref, y), (other_ref, 1 - y)))
    ]


PACK_BLOCKS = (D + 2 * INNER) // LANE


def pack_line(pack_ref, row, lane0, width):
    parts = []
    for lane in range(lane0, lane0 + width, LANE):
        at = row * PACK_BLOCKS + lane // LANE
        parts.append(pack_ref[at // SUB, at % SUB : at % SUB + 1, :])
    return jnp.concatenate(parts, axis=1)


def pack_kernel(rows, pieces, place_ref, part_ref, *refs):
    states, sums, (pack_ref, acc_ref) = refs[0:3], refs[3:7], refs[7:9]
    pack_ref[...] = jnp.zeros_like(pack_ref)

    def add(row, lane, value):
        at = row * PACK_BLOCKS + lane // LANE
        pack_ref[at // SUB, at % SUB : at % SUB + 1, :] += value

    lanes_of = ((0, D), (D, D + INNER), (D, D + INNER), (D + INNER, D + 2 * INNER))
    for part, (lane0, lane1) in zip(sums, lanes_of):
        for lane in range(lane0, lane1, LANE):
            for row in range(2):
                add(row, lane, part[row : row + 1, lane - lane0 : lane - lane0 + LANE])
    lanes = lax.broadcasted_iota(jnp.int32, (1, LANE), 1)
    for k in range(3):
        total = jnp.sum(states[k][...].reshape(1, -1), axis=1, keepdims=True)
        add(3, 0, jnp.where(lanes == k, total, 0.0))
    acc_ref[...] = jnp.zeros_like(acc_ref)
    spare = acc_ref.shape[0] - 1
    outer = place_ref[3] // 2
    piece = place_ref[2] % 2 * outer + place_ref[2] // 2
    at = 0
    for chunk, each in zip(CHUNKS[:2], pieces):
        found, _ = spans(chunk, rows)
        start = piece * each

        def body(k, carry, found=found, start=start, at=at):
            n = start + k
            slot = spare
            for weight, block0, blocks, first, tiles in found:
                here = LANE0[weight] // LANE + block0 + lax.rem(jnp.maximum(n - first, 0), blocks)
                slot = jnp.where((n >= first) & (n < first + tiles), here, slot)
            value = part_ref[at + k].astype(F32)
            acc_ref[slot] += value * value + 1e-30
            return carry

        lax.fori_loop(0, each, body, 0, unroll=2)
        at += each
    for slot in range(spare):
        add(2, slot * LANE, jnp.sum(acc_ref[slot], axis=0, keepdims=True))


def pack_in_kernel(rows, place_ref, mine_ref, other_ref, pack_ref, full_ref, sem):
    run_copies(load_halves(mine_ref, other_ref, place_ref, full_ref, sem))
    pack_ref[...] = jnp.zeros_like(pack_ref)
    column_sums(pack_ref, 0, full_ref, CHUNKS[2], rows)


def update_weight(
    k, squares, states_sum, source, weight, state, col_state, grad_ref, new, row_new_ref, col_new_ref, scratch, step=0, steps=1
):
    line_ref, state_ref, new_ref, scaled_ref = scratch
    width, fan, rows_here = WIDTHS[k], (D, KERNEL_TAPS * INNER, INNER)[k], state.shape[0]
    whole_rows = rows_here + -rows_here % LANE
    groups = rows_here // SUB // steps
    rate = 0.5 / fan**0.5

    def before():
        col_new = DECAY * col_state[...].reshape(1, -1) + (1.0 - DECAY) * (squares * (1.0 / fan))
        col_new_ref[...] = col_new.reshape(-1)
        total = DECAY * states_sum
        total = total + (1.0 - DECAY) * (1.0 / width) * jnp.sum(squares, axis=1, keepdims=True)
        scaled_ref[0:1, 0:width] = col_new / (total * (1.0 / fan))
        line_ref[0:1, 0:rows_here] = state[...].reshape(1, -1)
        for c in range(0, whole_rows, LANE):
            state_ref[c : c + LANE, :] = column(line_ref[0:1, c : c + LANE])

    def after():
        for c in range(0, whole_rows, LANE):
            line_ref[0:1, c : c + LANE] = jnp.transpose(new_ref[c : c + LANE, :])[0:1, :]
        row_new_ref[...] = line_ref[0:1, 0:rows_here].reshape(-1)

    def body(g, carry):
        here = pl.ds(pl.multiple_of(g * SUB, SUB), SUB)
        at = step * groups + g
        rows = pl.ds(pl.multiple_of(at * SUB, SUB), SUB)
        square = 0.0
        for ref, block0, blocks, first in source:
            for b in range(blocks):
                value = ref[first + at * blocks + b].astype(F32)
                grad_ref[here, (block0 + b) * LANE : (block0 + b + 1) * LANE] = value
                square = square + (value * value + 1e-30)
        mean = jnp.sum(square, axis=1, keepdims=True) * (1.0 / width)
        row_new = DECAY * state_ref[rows, :] + (1.0 - DECAY) * mean
        new_ref[rows, :] = row_new
        for ref, block0, blocks, first in source:
            for b in range(blocks):
                lanes = slice((block0 + b) * LANE, (block0 + b + 1) * LANE)
                value = ref[first + at * blocks + b].astype(F32)
                change = value * lax.rsqrt(row_new * scaled_ref[0:1, lanes])
                new[here, lanes] = weight[here, lanes] - rate * change
        return carry

    if steps == 1:
        before()
        lax.fori_loop(0, groups, body, 0, unroll=5)
        after()
    else:
        pl.when(step == 0)(before)
        lax.fori_loop(0, groups, body, 0, unroll=5)
        pl.when(step == steps - 1)(after)


def sources_of(chunk, ref, rows):
    return {w: (ref, block0, blocks, first) for w, block0, blocks, first, _ in spans(chunk, rows)[0]}


def update_kernel(rows, copies_of, place_ref, mine_ref, other_ref, pack_ref, *refs):
    weights, states, col_states = refs[0:2], refs[2:4], refs[4:6]
    grads, news, rows_new, cols_new = refs[6:8], refs[8:10], refs[10:12], refs[12:14]
    conv_scratch, out_scratch = refs[14:18], refs[18:22]
    full1_ref, full2_ref, sem = refs[22:25]
    both = (mine_ref, other_ref)
    count = 2 * mine_ref.shape[0]
    step, steps = pl.program_id(0), pl.num_programs(0)

    @pl.when(step == 0)
    def _():
        copies = load_full(both, place_ref, 0, full1_ref, sem, 0)
        copies += load_full(both, place_ref, full1_ref.shape[0] // count, full2_ref, sem, count)
        run_copies(copies)

    from1 = sources_of(CHUNKS[0], full1_ref, rows)
    from2 = sources_of(CHUNKS[1], full2_ref, rows)

    def update(n, k, source, scratch, *steps):
        squares = pack_line(pack_ref, 2, LANE0[k], WIDTHS[k])
        update_weight(
            k, squares, pack_line(pack_ref, 3, 0, LANE)[:, k : k + 1] * (1.0 / copies_of), source, weights[n],
            states[n], col_states[n], grads[n], news[n], rows_new[n], cols_new[n], scratch, *steps,
        )

    update(0, 1, [from1[1], from2[1]], conv_scratch, step, UPDATE_STEPS)

    @pl.when(step == steps - 1)
    def _():
        update(1, 2, [from1[2]], out_scratch)


def update_in_kernel(
    rows, copies_of, place_ref, mine_ref, other_ref, pack_in_ref, pack_ref, np_ref, second_ref, *refs
):
    weight, state, col_state, grad_ref, new_ref, row_new_ref, col_new_ref = refs[0:7]
    ngrad_ref, nsecond_ref, nnew_ref = refs[7:10]
    full_ref, sem = refs[14:16]
    copies = load_halves(mine_ref, other_ref, place_ref, full_ref, sem)
    for copy in copies:
        copy.start()
    lines = [pack_line(pack_ref, row, 0, D + 2 * INNER) for row in range(2)]
    grad = jnp.concatenate(lines, axis=0)
    second = DECAY * second_ref[...] + (1.0 - DECAY) * (grad * grad + 1e-30)
    ngrad_ref[...] = grad
    nsecond_ref[...] = second
    nnew_ref[...] = np_ref[...] - 0.2 * grad * lax.rsqrt(second)
    for copy in copies:
        copy.wait()
    update_weight(
        0, pack_in_ref[0:1, :], pack_line(pack_ref, 3, 0, LANE)[:, 0:1] * (1.0 / copies_of),
        [sources_of(CHUNKS[2], full_ref, rows)[0]], weight, state, col_state, grad_ref, new_ref,
        row_new_ref, col_new_ref, refs[10:14],
    )


class Places:
    def __init__(self):
        self.seq, self.fsdp = lax.axis_size("seq"), lax.axis_size("fsdp")
        self.q = lax.axis_index("fsdp")
        self.s = lax.axis_index("seq")

    def flip(self, x, axis, bit):
        pairs = []
        for s in range(self.seq):
            for f in range(self.fsdp):
                s2, f2 = (s ^ bit, f) if axis == "seq" else (s, f ^ bit)
                pairs.append((s * self.fsdp + f, s2 * self.fsdp + f2))
        return lax.ppermute(x, AXES, pairs)


def bits_of(count):
    return [1 << k for k in range(count.bit_length() - 1)]


def tie(x, *others):
    return lax.optimization_barrier((x, *others))[0]


def gather_pieces(piece, place, after, later=()):
    found = {0: piece}
    for bit in reversed(bits_of(place.fsdp)):
        for k in list(found):
            moving = found[k]
            if bit == 1:
                moving = tie(moving, *((after,) if k == 0 or not later else later))
            found[k | bit] = place.flip(moving, "fsdp", bit)
    return [found[k] for k in range(place.fsdp)]


def sum_over(x, place, *axes):
    for axis in axes:
        for bit in bits_of(getattr(place, axis)):
            x = x + place.flip(x, axis, bit)
    return x


def sum_along_z(x, place):
    terms = [x] + [place.flip(x, "seq", 2 * k) for k in range(1, place.seq // 2)]
    while len(terms) > 1:
        terms = [a + b for a, b in zip(terms[::2], terms[1::2])]
    return terms[0]


def pick(x, index, axis):
    return lax.dynamic_index_in_dim(x, index, axis=axis, keepdims=False)


class Reduction:
    def __init__(self, place, keep, send):
        self.place, self.near = place, keep
        self.got = place.flip(send, "fsdp", 1)

    def halve(self, axis, side, flip_axis, bit):
        dims = self.near.shape
        parts = dims[:axis] + (2, dims[axis] // 2) + dims[axis + 1 :]
        near, got = self.near.reshape(parts), self.got.reshape(parts)
        away = pick(near, 1 - side, axis).astype(F32) + pick(got, 1 - side, axis).astype(F32)
        self.near = pick(near, side, axis).astype(F32) + pick(got, side, axis).astype(F32)
        away = away.astype(BF16)
        self.got = self.place.flip(away, flip_axis, bit)
        return away

    def x(self):
        bit = self.place.fsdp // 2
        while bit > 1:
            away = self.halve(0, (self.place.q // bit) % 2, "fsdp", bit)
            bit //= 2
        return away

    def y(self):
        return self.halve(1, self.place.s % 2, "seq", 1)

    def whole_half(self):
        self.near = self.rounded(self.near + self.got.astype(F32))

    def rounded(self, total):
        return lax.optimization_barrier(total.astype(BF16))

    def send_half(self, bit):
        self.got = self.place.flip(self.near, "seq", bit)

    def add_half(self):
        self.near = self.rounded(self.near.astype(F32) + self.got.astype(F32))

    def pieces(self):
        total = (self.near + self.got.astype(F32)).astype(BF16)
        return total.reshape((self.place.seq // 2, -1) + total.shape[2:])


def arrive(result, *reductions):
    result, *gots = lax.optimization_barrier((result, *[r.got for r in reductions]))
    for reduction, got in zip(reductions, gots):
        reduction.got = got
    return result


def summed_f32(got):
    return jnp.sum(got.astype(F32), axis=0)


def summed(got):
    return summed_f32(got).astype(BF16)


def exchange(place, sent):
    line = [[y + 2 * z for z in range(place.seq // 2)] for y in range(2)]
    return lax.all_to_all(sent, "seq", 0, 0, axis_index_groups=line)


def on_device(
    tokens, input_mask, doc_lengths, cotangent, w_in, w_conv, w_out, norm_params,
    row_in, col_in, row_conv, col_conv, row_out, col_out, norm_second,
):
    place = Places()
    rows = tokens.shape[0]
    pieces = place.fsdp
    spots = jnp.stack(
        [place.q, (place.s * place.fsdp + place.q) * rows, place.s, place.seq]
    ).astype(jnp.int32)
    docs = doc_lengths.shape[0]
    live = input_mask.reshape(-1, LANE)
    weights = (w_in, w_conv, w_out)
    rows_of = [w.shape[0] for w in weights]

    tile_a, tile = 256, 512
    steps = rows // tile
    params_spec = whole(2, D + 2 * INNER)
    dma = pltpu.SemaphoreType.DMA

    out_sides = (w_out[:, : D // 2], w_out[:, D // 2 :])
    conv_out = jnp.concatenate([w_conv, *out_sides], axis=0).astype(BF16)
    hidden_a, slope_a, xhat_a, rstd_a = call(
        norm_a_kernel,
        (rows // tile_a,),
        [rows_spec(tile_a, D), params_spec],
        [rows_spec(tile_a, D)] * 3 + [rows_spec(tile_a, LANE)],
        [shape((rows, D), BF16)] * 3 + [shape((rows, LANE), F32)],
        us=17,
    )(tokens, tie(norm_params, conv_out))

    in_pieces = gather_pieces(w_in.astype(BF16), place, hidden_a)

    def in_call(tiles, count, before):
        at, stride = tiles

        def here_spec(width):
            return pl.BlockSpec((tile, width), lambda i: (at + stride * i, 0))

        out_shapes = [shape((rows, INNER), BF16)] * 3 + [shape((rows, LANE), F32)] * 2
        out_specs = [here_spec(INNER)] * 3 + [here_spec(LANE)] * 2
        if at == 0:
            out_shapes += [shape((REACH, INNER), BF16)] * 2
            out_specs += [whole(REACH, INNER)] * 2
        return call(
            functools.partial(in_kernel, pieces, tiles),
            (count,),
            [SMEM, whole(docs), here_spec(D), whole(*live.shape), params_spec]
            + [ANY] * (pieces + len(before)),
            out_specs,
            out_shapes,
            [pltpu.VMEM((D, INNER), BF16), pltpu.VMEM((tile, INNER), F32)]
            + [pltpu.VMEM((8, docs + -docs % LANE), F32), dma((pieces,))],
            us=3,
            aliases={5 + pieces + k: k for k in range(len(before))},
        )(spots, doc_lengths, hidden_a, live, norm_params, *in_pieces, *before)

    *kept, m_first, m_last = in_call((0, steps - 1), 2, ())
    moved, slope_b, xhat_b, rstd_b, masks = in_call((1, 1), steps - 2, kept)

    def halo(inner, outer):
        total = place.seq * place.fsdp
        across = [(i, i + 1 if i % 2 else i - 1) for i in range(1, total - 1)]
        return place.flip(inner, "fsdp", 1), lax.ppermute(outer, AXES, across)

    m_inner, m_outer = halo(m_first, m_last)
    conv_pieces = gather_pieces(conv_out, place, m_first, (moved, m_inner, m_outer))

    ext = pltpu.VMEM((rows + 2 * REACH, INNER), BF16)
    taps_wide = KERNEL_TAPS * INNER
    wide = pltpu.VMEM((taps_wide, INNER), BF16)
    shards = place.fsdp // 2

    def half_dims(chunk):
        count = spans(chunk, rows_of)[1]
        return (shards, count + -count % place.seq, SUB, LANE)

    def tile_spec(width, ahead):
        return pl.BlockSpec((tile, width), lambda i: (jnp.clip(i + ahead, 0, steps - 1), 0))

    halves = [half_dims(CHUNKS[0])] * 2 + [half_dims(CHUNKS[1])] * 2
    work = pltpu.VMEM((tile, INNER), F32)
    turned_tile = pltpu.VMEM((INNER, tile), BF16)
    hidden_c, d_conv, d_first, d_last, sums_c, turned, keep1, send1, keep2, send2 = call(
        functools.partial(conv_kernel, pieces, rows_of),
        (steps + 1,),
        [SMEM, ANY, ANY, ANY, tile_spec(LANE, 0), tile_spec(D, 0), tile_spec(D, -1), params_spec]
        + [ANY] * pieces,
        [tile_spec(INNER, 0)] * 2
        + [whole(REACH, INNER), whole(REACH, INNER), whole(2, INNER)]
        + [ANY] * 5,
        [
            shape((rows, INNER), BF16),
            shape((rows, INNER), BF16),
            shape((REACH, INNER), BF16),
            shape((REACH, INNER), BF16),
            shape((2, INNER), F32),
            shape((taps_wide, INNER), BF16),
        ]
        + [shape(dims, BF16) for dims in halves],
        [ext, wide, wide, pltpu.VMEM((INNER, D), BF16), pltpu.VMEM((D, INNER), BF16)]
        + [pltpu.VMEM((2, tile, taps_wide), BF16), work, work, work, turned_tile, turned_tile]
        + [pltpu.VMEM((INNER, taps_wide), F32), pltpu.VMEM((INNER, D), F32)]
        + [pltpu.VMEM((16, INNER), F32)]
        + [pltpu.VMEM((2,) + halves[0], BF16), pltpu.VMEM((2,) + halves[2], BF16)]
        + [dma((3 + 3 * pieces,))],
        us=45,
    )(
        spots, m_inner, moved, m_outer, masks, cotangent, cotangent, norm_params, *conv_pieces
    )
    d_inner, d_outer = halo(d_first, d_last)
    first, second = Reduction(place, keep1, send1), Reduction(place, keep2, send2)
    (block_out,) = call(
        functools.partial(out_kernel, pieces),
        (steps,),
        [SMEM, rows_spec(tile, INNER), rows_spec(tile, D)] + [ANY] * pieces,
        [rows_spec(tile, D)],
        [shape((rows, D), BF16)],
        [pltpu.VMEM((INNER, D), BF16), dma((2 * pieces,))],
        us=9,
    )(spots, hidden_c, tokens, *conv_pieces)

    def back_conv(last, spots, before):
        here = steps // 2
        at = here * last

        def here_spec(width):
            return pl.BlockSpec((tile, width), lambda i: (i + at, 0))

        dims = half_dims(CHUNKS[2])
        return call(
            functools.partial(back_conv_kernel, last, w_in.shape[0]),
            (here,),
            [SMEM] + [ANY] * 4
            + [here_spec(LANE), here_spec(INNER), here_spec(LANE), here_spec(INNER), here_spec(D)]
            + [params_spec]
            + [ANY] * last,
            [rows_spec(tile, INNER), whole(2, INNER)] + [ANY] * (1 + last),
            [shape((rows // 2, INNER), BF16), shape((2, INNER), F32)]
            + ([shape(dims, BF16)] * 2 if last else [shape((INNER, D), F32)]),
            ([pltpu.VMEM((2,) + dims, BF16)] if last else [])
            + [
                ext,
                wide,
                pltpu.VMEM((tile, taps_wide), BF16),
                pltpu.VMEM((tile, INNER), F32),
                pltpu.VMEM((INNER, D), F32),
                pltpu.VMEM((16, INNER), F32),
                dma((5,)),
            ],
            us=16,
        )(
            spots, d_inner, d_conv, d_outer, turned, masks, xhat_b, rstd_b, slope_b, hidden_a,
            norm_params, *before,
        )

    block_out, d_inner, d_outer = arrive((block_out, d_inner, d_outer), first, second)
    away = (first.x(), second.y())
    d_pre0, sums_b0, grad_part = back_conv(0, tie(spots, *away), ())
    d_pre0 = arrive(d_pre0, first, second)
    away = (first.y(), second.x())
    d_pre1, sums_b1, keep, send = back_conv(1, tie(spots, *away), (grad_part,))
    send = arrive(send, first, second)
    third = Reduction(place, keep, send)
    sent = jnp.concatenate([first.pieces(), second.pieces()], axis=1)
    got = exchange(place, sent)
    third.got = tie(third.got, sent)
    away = (sent, third.x())
    input_grad, sums_a = call(
        functools.partial(back_a_kernel, pieces, steps // 2),
        (steps,),
        [SMEM]
        + [
            pl.BlockSpec((tile, INNER), lambda i: (jnp.minimum(i, steps // 2 - 1), 0)),
            pl.BlockSpec((tile, INNER), lambda i: (jnp.maximum(i - steps // 2, 0), 0)),
        ]
        + [rows_spec(tile, D), rows_spec(tile, LANE), rows_spec(tile, D), rows_spec(tile, D)]
        + [params_spec]
        + [ANY] * pieces,
        [rows_spec(tile, D), whole(2, D)],
        [shape((rows, D), F32), shape((2, D), F32)],
        [
            pltpu.VMEM((D, INNER), BF16),
            pltpu.VMEM((INNER, D), BF16),
            pltpu.VMEM((tile, D), F32),
            pltpu.VMEM((16, D), F32),
            dma((pieces,)),
        ],
        us=17,
    )(
        tie(spots, *away), d_pre0, d_pre1, xhat_a, rstd_a, slope_a, cotangent, norm_params, *in_pieces
    )

    row_states, col_states = (row_in, row_conv, row_out), (col_in, col_conv, col_out)
    row_specs = [whole(*r.shape) for r in row_states]
    col_specs = [whole(*c.shape) for c in col_states]
    cols_all = D + 2 * INNER
    pack_dims = (4 * PACK_BLOCKS // SUB, SUB, LANE)
    pack_spec = whole(*pack_dims)
    fulls = [pltpu.VMEM(half_dims(c)[1:], BF16) for c in CHUNKS]
    sums = (sums_a, sums_b0, sums_b1, sums_c)
    got, third.got, input_grad = lax.optimization_barrier((got, third.got, input_grad))
    part = summed(got)
    sent = jnp.broadcast_to(part[None], (place.seq // 2,) + part.shape)
    mine = exchange(place, sent)
    third.got = tie(third.got, sent)
    away = third.y()
    (pack,) = call(
        functools.partial(pack_kernel, rows_of, [half_dims(c)[1] // place.seq for c in CHUNKS]),
        (1,),
        [SMEM, whole(*part.shape)] + row_specs + [whole(*x.shape) for x in sums],
        [pack_spec],
        [shape(pack_dims, F32)],
        [pltpu.VMEM((cols_all // LANE + 1, SUB, LANE), F32)],
        us=2,
        mib=16,
    )(tie(spots, away), part, *row_states, *sums)
    pack = sum_over(pack, place, "fsdp")
    third.got, pack = lax.optimization_barrier((third.got, pack))
    seq_bits = bits_of(place.seq)
    third.whole_half()
    for bit in seq_bits[1:-1]:
        third.send_half(bit)
        pack = pack + place.flip(pack, "seq", 1) if bit == 2 else pack
        if bit != seq_bits[-2]:
            third.add_half()
    mine, third.got, pack = lax.optimization_barrier((mine, third.got, pack))
    other = place.flip(mine, "seq", 1)
    third.add_half()
    third.send_half(seq_bits[-1])
    pack = sum_along_z(pack, place)
    third.got, other, pack = lax.optimization_barrier((third.got, other, pack))
    third.add_half()
    line = third.near.reshape(third.near.shape[1:])
    line_other = place.flip(line, "seq", 1)

    def update_scratch(weight):
        lines = weight.shape[0] + -weight.shape[0] % LANE
        return (
            [pltpu.VMEM((8, lines), F32)]
            + [pltpu.VMEM((lines, LANE), F32)] * 2
            + [pltpu.VMEM((8, weight.shape[1]), F32)]
        )

    weight_specs = [whole(*w.shape) for w in weights]
    conv_block = pl.BlockSpec((w_conv.shape[0] // UPDATE_STEPS, INNER), lambda i: (i, 0))
    both_specs = [conv_block, weight_specs[2]]
    results = call(
        functools.partial(update_kernel, rows_of, place.seq),
        (UPDATE_STEPS,),
        [SMEM, ANY, ANY, pack_spec] + both_specs + row_specs[1:] + col_specs[1:],
        both_specs * 2 + row_specs[1:] + col_specs[1:],
        [shape(w.shape, F32) for w in weights[1:]] * 2
        + [shape(r.shape, F32) for r in row_states[1:] + col_states[1:]],
        update_scratch(w_conv)
        + update_scratch(w_out)
        + fulls[:2]
        + [dma((2 * place.seq,))],
        us=8,
        mib=32,
    )(spots, mine, other, pack, *weights[1:], *row_states[1:], *col_states[1:])
    grad_conv, grad_out, new_conv, new_out, row_conv_new, row_out_new, col_conv_new, col_out_new = (
        results
    )
    line_other, grad_out = lax.optimization_barrier((line_other, grad_out))
    (pack_in,) = call(
        functools.partial(pack_in_kernel, rows_of),
        (1,),
        [SMEM, ANY, ANY],
        [whole(8, INNER)],
        [shape((8, INNER), F32)],
        [fulls[2], dma((place.seq,))],
        us=2,
        mib=16,
    )(spots, line, line_other)
    pack_in = sum_over(pack_in, place, "fsdp")
    grad_in, new_in, row_in_new, col_in_new, *norm_results = call(
        functools.partial(update_in_kernel, rows_of, place.seq),
        (1,),
        [SMEM, ANY, ANY, whole(8, INNER), pack_spec, params_spec, params_spec]
        + [weight_specs[0], row_specs[0], col_specs[0]],
        [weight_specs[0]] * 2 + [row_specs[0], col_specs[0]] + [params_spec] * 3,
        [shape(w_in.shape, F32)] * 2
        + [shape(row_in.shape, F32), shape(col_in.shape, F32)]
        + [shape((2, cols_all), F32)] * 3,
        update_scratch(w_in) + [fulls[2], dma((place.seq,))],
        us=4,
        mib=24,
    )(
        spots, line, line_other, pack_in, pack, norm_params, norm_second, w_in, row_in, col_in
    )
    return (
        block_out,
        input_grad,
        grad_in,
        grad_conv,
        grad_out,
        new_in,
        new_conv,
        new_out,
        row_in_new,
        col_in_new,
        row_conv_new,
        col_conv_new,
        row_out_new,
        col_out_new,
        *norm_results,
    )


def solution(mesh):
    both, rows = P(AXES, None), P("fsdp", None)
    in_specs = (
        both, P(AXES), P(), both, rows, rows, rows, P(),
        P("fsdp"), P(), P("fsdp"), P(), P("fsdp"), P(), P(),
    )
    out_specs = (
        both, both, rows, rows, rows, rows, rows, rows,
        P("fsdp"), P(), P("fsdp"), P(), P("fsdp"), P(), P(), P(), P(),
    )
    return jax.shard_map(
        on_device, mesh=mesh, in_specs=in_specs, out_specs=out_specs, check_vma=False
    )
```

```python
import functools
import math

import jax
import jax.numpy as jnp
from jax import lax
from jax.experimental import pallas as pl
from jax.experimental.pallas import tpu as pltpu
from jax.sharding import PartitionSpec as P

D = 1280
INNER = 640
KERNEL_TAPS = 5
DILATION_STEP = 128
STEP = 10
EPSILON = 1e-05
DECAY = 1.0 - STEP ** (-0.8)

REACH = (KERNEL_TAPS - 1) // 2 * DILATION_STEP
MID = (KERNEL_TAPS - 1) // 2
F32 = jnp.float32
BF16 = jnp.bfloat16
SUB, LANE = 16, 128
AXES = ("seq", "fsdp")
NT = (((1,), (1,)), ((), ()))
TN = (((0,), (0,)), ((), ()))
NN = (((1,), (0,)), ((), ()))


def call(kernel, grid, in_specs, out_specs, out_shape, scratch=(), us=1.0, aliases=None, mib=58):
    params = pltpu.CompilerParams(
        vmem_limit_bytes=mib * 1024 * 1024, dimension_semantics=("arbitrary",) * len(grid)
    )
    return pl.pallas_call(
        kernel,
        grid=grid,
        in_specs=in_specs,
        out_specs=out_specs,
        out_shape=out_shape,
        scratch_shapes=list(scratch),
        compiler_params=params,
        input_output_aliases=aliases or {},
        cost_estimate=pl.CostEstimate(
                flops=int(us * 1.1e9), bytes_accessed=int(us * 3.4e6), transcendentals=0
        ),
    )


def shape(dims, dtype):
    return jax.ShapeDtypeStruct(dims, dtype)


def rows_spec(tile, width):
    return pl.BlockSpec((tile, width), lambda i: (i, 0))


def whole(*dims):
    return pl.BlockSpec(dims, lambda *_: (0,) * len(dims))


ANY = pl.BlockSpec(memory_space=pl.ANY)
SMEM = pl.BlockSpec(memory_space=pltpu.SMEM)


ERFC_P = 0.47 / math.sqrt(2.0)
ERFC_C = (
    0.12357219400743558,
    0.1999878668208835,
    -0.08033356004356296,
    0.3660253986657854,
    -0.1092519747040215,
)
LOG2E = 1.4426950408889634


def gelu_and_slope(y):
    t = pltpu.reciprocal(1.0 + ERFC_P * jnp.abs(y), approx=True)
    bell = jnp.exp2(y * y * (-0.5 * LOG2E))
    poly = ERFC_C[4] * t + ERFC_C[3]
    for c in ERFC_C[2::-1]:
        poly = poly * t + c
    tail = poly * t * bell
    cdf = jnp.where(y > 0.0, 1.0 - tail, tail)
    return y * cdf, cdf + y * (bell * (1.0 / math.sqrt(2.0 * math.pi)))


def lane_blocks(width):
    return [slice(k, k + LANE) for k in range(0, width, LANE)]


def row_stats(ref, rows):
    width = ref.shape[-1]
    blocks = lane_blocks(width)
    total = ref[rows, blocks[0]].astype(F32)
    for b in blocks[1:]:
        total = total + ref[rows, b].astype(F32)
    mean = jnp.sum(total, axis=-1, keepdims=True) * (1.0 / width)
    square = None
    for b in blocks:
        centered = ref[rows, b].astype(F32) - mean
        square = centered * centered if square is None else square + centered * centered
    variance = jnp.sum(square, axis=-1, keepdims=True) * (1.0 / width)
    return mean, lax.rsqrt(variance + EPSILON)


def fold(values):
    total = values[0:8]
    for k in range(8, values.shape[0], 8):
        total = total + values[k : k + 8]
    return total


def in_stages(count, stages, between=(), chunk=None):
    chunk = chunk or CHUNK
    chunks = [slice(k, k + chunk) for k in range(0, count, chunk)]
    kept, rounds = {}, len(chunks) + len(stages) - 1
    for t in range(rounds):
        for n, stage in enumerate(stages):
            if 0 <= t - n < len(chunks):
                kept[n, t - n] = stage(chunks[t - n], kept.get((n - 1, t - n)))
        for work in between[t * len(between) // rounds : (t + 1) * len(between) // rounds]:
            work()


def halves_of(count):
    return (slice(0, count // 2), slice(count // 2, count))


def row_means(sums, width):
    return [jnp.sum(x, axis=-1, keepdims=True) * (1.0 / width) for x in sums]


def norm_back(rows, dxhat_ref, xhat_ref, means, put):
    mean_d, mean_dx, rstd = means
    for b in lane_blocks(dxhat_ref.shape[-1]):
        xhat = xhat_ref[rows, b].astype(F32)
        put(b, (dxhat_ref[rows, b] - mean_d - xhat * mean_dx) * rstd)


def add_terms(acc_ref, b, dy, xhat):
    acc_ref[0:8, b] += fold(dy * xhat)
    acc_ref[8:16, b] += fold(dy)


def open_sums(acc_ref):
    @pl.when(pl.program_id(0) == 0)
    def _():
        acc_ref[...] = jnp.zeros_like(acc_ref)


def close_sums(out_ref, acc_ref):
    @pl.when(pl.program_id(0) == pl.num_programs(0) - 1)
    def _():
        out_ref[0:1, :] = jnp.sum(acc_ref[0:8, :], axis=0, keepdims=True)
        out_ref[1:2, :] = jnp.sum(acc_ref[8:16, :], axis=0, keepdims=True)


def run_copies(copies):
    for copy in copies:
        copy.start()
    for copy in copies:
        copy.wait()


def piece_copies(pieces, full_ref, me, sem, first=0):
    each = full_ref.shape[0] // len(pieces)
    return [
        pltpu.make_async_copy(
            piece.at[0:each, :],
            full_ref.at[pl.ds(pl.multiple_of((me ^ k) * each, SUB), each), :],
            sem.at[first + k],
        )
        for k, piece in enumerate(pieces)
    ]


def out_copies(pieces, full_ref, me, sem, first=0):
    each, width = full_ref.shape[0] // len(pieces), full_ref.shape[1] // 2
    copies = []
    for k, piece in enumerate(pieces):
        rows = pl.ds(pl.multiple_of((me ^ k) * each, SUB), each)
        for side in range(2):
            at = piece.shape[0] - (2 - side) * each
            copies.append(
                pltpu.make_async_copy(
                    piece.at[at : at + each, :],
                    full_ref.at[rows, side * width : (side + 1) * width],
                    sem.at[first + 2 * k + side],
                )
            )
    return copies


def column(row):
    return jnp.transpose(jnp.broadcast_to(row, (LANE, LANE)))


CHUNK = 64
UPDATE_STEPS = 5
TURNED = 2


def norm_a_kernel(tok_ref, np_ref, hid_ref, slope_ref, xhat_ref, rstd_ref):
    def stats(rows, _):
        mean, rstd = row_stats(tok_ref, rows)
        rstd_ref[rows, :] = jnp.broadcast_to(rstd, (rstd.shape[0], LANE))
        return mean, rstd

    def work(rows, kept):
        mean, rstd = kept
        for b in lane_blocks(D):
            xhat = (tok_ref[rows, b].astype(F32) - mean) * rstd
            hidden, slope = gelu_and_slope(xhat * np_ref[0:1, b] + np_ref[1:2, b])
            hid_ref[rows, b] = hidden.astype(BF16)
            slope_ref[rows, b] = slope.astype(BF16)
            xhat_ref[rows, b] = xhat.astype(BF16)

    in_stages(tok_ref.shape[0], [stats, work], chunk=32)


def running_ends(ends_ref, lengths_ref):
    docs, width = lengths_ref.shape[0], ends_ref.shape[1]
    ends_ref[...] = jnp.zeros_like(ends_ref)
    ends_ref[0:1, 0:docs] = lengths_ref[...].reshape(1, -1).astype(F32)
    before = jnp.zeros((1, 1), F32)
    row = lax.broadcasted_iota(jnp.int32, (LANE, LANE), 0)
    lane = lax.broadcasted_iota(jnp.int32, (LANE, LANE), 1)
    for k in range(0, width, LANE):
        line = ends_ref[0:1, k : k + LANE]
        sums = jnp.sum(jnp.where(row <= lane, column(line), 0.0), axis=0, keepdims=True) + before
        ends_ref[0:1, k : k + LANE] = jnp.where(lane[0:1] + k < docs, sums, 1e9)
        before = before + jnp.sum(line, axis=1, keepdims=True)


def in_kernel(pieces, tiles, place_ref, lengths_ref, hid_ref, live_ref, np_ref, *refs):
    piece_refs = refs[:pieces]
    edges = tiles[0] == 0
    outs = refs[-(11 if edges else 9) :]
    mov_ref, slope_ref, xhat_ref, rstd_ref, mask_ref = outs[:5]
    w_ref, pre_ref, ends_ref, sem = outs[-4:]
    step = pl.program_id(0)
    tile = hid_ref.shape[0]

    @pl.when(step == 0)
    def _():
        copies = piece_copies(piece_refs, w_ref, place_ref[0], sem)
        for copy in copies:
            copy.start()
        running_ends(ends_ref, lengths_ref)
        for copy in copies:
            copy.wait()

    for half in halves_of(tile):
        pre_ref[half, :] = lax.dot_general(
            hid_ref[half, :], w_ref[...], NN, preferred_element_type=F32
        )

    at_tile = tiles[0] + step * tiles[1]
    first = place_ref[1] + at_tile * tile
    ends = ends_ref[0:1, :]
    lanes = lax.broadcasted_iota(jnp.int32, (LANE, LANE), 1)
    offsets = ((lanes - MID) * DILATION_STEP).astype(F32)
    for k in range(tile // LANE):
        at = (first + k * LANE + lax.broadcasted_iota(jnp.int32, (LANE, 1), 0)).astype(F32)
        begin = jnp.max(jnp.where(ends <= at, ends, 0.0), axis=1, keepdims=True)
        end = jnp.min(jnp.where(ends > at, ends, 1e9), axis=1, keepdims=True)
        there = at + offsets
        same = jnp.where((there >= begin) & (there < end), 1.0, 0.0)
        live = column(live_ref[pl.ds(at_tile * (tile // LANE) + k, 1), :].astype(F32))
        mask_ref[k * LANE : (k + 1) * LANE, :] = jnp.where(lanes == MID, live, same)

    def stats(rows, _):
        mean, rstd = row_stats(pre_ref, rows)
        rstd_ref[rows, :] = jnp.broadcast_to(rstd, (rstd.shape[0], LANE))
        return mean, rstd

    def work(rows, kept):
        mean, rstd = kept
        live = mask_ref[rows, MID : MID + 1]
        for b in lane_blocks(INNER):
            gains = slice(D + b.start, D + b.stop)
            xhat = (pre_ref[rows, b] - mean) * rstd
            hidden, slope = gelu_and_slope(xhat * np_ref[0:1, gains] + np_ref[1:2, gains])
            mov_ref[rows, b] = (hidden * live).astype(BF16)
            slope_ref[rows, b] = slope.astype(BF16)
            xhat_ref[rows, b] = xhat.astype(BF16)

    in_stages(tile, [stats, work], chunk=32)
    if edges:
        put_edges(place_ref, outs[5], outs[6], mov_ref, step == 0, step == 1)


def load_window(place_ref, inner, mid, outer, ext_ref, sem):
    rows, core = mid.shape[0], lax.rem(place_ref[0], 2)
    near = pl.multiple_of((1 - core) * (REACH + rows), SUB)
    far = pl.multiple_of(core * (REACH + rows), SUB)
    return [
        pltpu.make_async_copy(inner, ext_ref.at[pl.ds(near, REACH), :], sem.at[0]),
        pltpu.make_async_copy(mid, ext_ref.at[REACH : REACH + rows, :], sem.at[1]),
        pltpu.make_async_copy(outer, ext_ref.at[pl.ds(far, REACH), :], sem.at[2]),
    ]


def put_edges(place_ref, inner_ref, outer_ref, tile_ref, at_first, at_last):
    rows, core = tile_ref.shape[0], lax.rem(place_ref[0], 2)
    for at, edge, first in ((at_first, slice(0, REACH), 0), (at_last, slice(rows - REACH, rows), 1)):

        @pl.when(at & (core == first))
        def _(edge=edge):
            outer_ref[...] = tile_ref[edge, :]

        @pl.when(at & (core != first))
        def _(edge=edge):
            inner_ref[...] = tile_ref[edge, :]


def fill_taps(taps_ref, ext_ref, mask_ref, start):
    tile = taps_ref.shape[0]
    for j in range(KERNEL_TAPS):
        rows = pl.ds(pl.multiple_of(start + j * DILATION_STEP, DILATION_STEP), tile)
        picked = ext_ref[rows, :]
        if j != MID:
            picked = picked * mask_ref[:, j : j + 1].astype(BF16)
        taps_ref[:, j * INNER : (j + 1) * INNER] = picked


def conv_kernel(
    pieces, rows_of, place_ref, low_ref, mov_ref, high_ref, mask_ref, cot_ref, before_ref, np_ref, *refs
):
    piece_refs = refs[:pieces]
    hid_ref, dconv_ref, inner_ref, outer_ref, sums_ref, turned_ref = refs[pieces : pieces + 6]
    outs = refs[pieces + 6 : pieces + 10]
    ext_ref, wc_ref, wct_ref, wo_ref, wt_ref, taps_ref, pre_ref, dh_ref, xhat_ref = refs[
        pieces + 10 : pieces + 19
    ]
    dt_ref, ht_ref, gc_ref, go_ref, acc_ref, stage1_ref, stage2_ref, sem = refs[pieces + 19 :]
    step, steps = pl.program_id(0), pl.num_programs(0) - 1
    tile = taps_ref.shape[1]
    slot = lax.rem(step, 2)

    @pl.when(step == 0)
    def _():
        me = place_ref[0]
        outs = out_copies(piece_refs, wo_ref, me, sem, 3)
        rest = load_window(place_ref, low_ref, mov_ref, high_ref, ext_ref, sem)
        rest += piece_copies(piece_refs, wc_ref, me, sem, 3 + 2 * pieces)
        for copy in outs + rest:
            copy.start()
        for ref in (acc_ref, gc_ref, go_ref):
            ref[...] = jnp.zeros_like(ref)
        for copy in outs:
            copy.wait()
        for k in range(0, D, 256):
            wt_ref[k : k + 256, :] = jnp.transpose(wo_ref[:, k : k + 256])
        for copy in rest:
            copy.wait()

    def grad_conv(cols):
        def work():
            gc_ref[:, cols] += lax.dot_general(
                dt_ref[...], taps_ref[1 - slot, :, cols], NN, preferred_element_type=F32
            )

        return work

    def grad_out(cols):
        def work():
            go_ref[:, cols] += lax.dot_general(
                ht_ref[...], before_ref[:, cols], NN, preferred_element_type=F32
            )

        return work

    taps_wide = KERNEL_TAPS * INNER
    products = [grad_conv(slice(k, min(k + 768, taps_wide))) for k in range(0, taps_wide, 768)]
    products += [grad_out(slice(k, min(k + 768, D))) for k in range(0, D, 768)]

    def tile_work(products, turned):
        fill_taps(taps_ref.at[slot], ext_ref, mask_ref, step * tile)
        pre_ref[...] = lax.dot_general(
            taps_ref[slot], wc_ref[...], NN, preferred_element_type=F32
        )
        dh_ref[...] = lax.dot_general(cot_ref[...], wt_ref[...], NN, preferred_element_type=F32)
        for n in range(turned):
            tap = jnp.minimum(turned * (step - 1) + n, KERNEL_TAPS - 1)
            source = wc_ref[pl.ds(pl.multiple_of(tap * INNER, SUB), INNER), :]
            target = pl.multiple_of((KERNEL_TAPS - 1 - tap) * INNER, SUB)
            wct_ref[pl.ds(target, INNER), :] = jnp.transpose(source)

        def stats(rows, _):
            return row_stats(pre_ref, rows)

        def work(rows, kept):
            mean, rstd = kept
            sums = [0.0, 0.0]
            for b in lane_blocks(INNER):
                gains = slice(D + INNER + b.start, D + INNER + b.stop)
                gain = np_ref[0:1, gains]
                xhat = (pre_ref[rows, b] - mean) * rstd
                hidden, slope = gelu_and_slope(xhat * gain + np_ref[1:2, gains])
                hid_ref[rows, b] = hidden.astype(BF16)
                dy = dh_ref[rows, b] * slope
                add_terms(acc_ref, b, dy, xhat)
                dxhat = dy * gain
                xhat_ref[rows, b] = xhat
                dh_ref[rows, b] = dxhat
                sums = [sums[0] + dxhat, sums[1] + dxhat * xhat]
            return row_means(sums, INNER) + [rstd]

        def finish(rows, means):
            def put(b, value):
                dconv_ref[rows, b] = value.astype(BF16)

            norm_back(rows, dh_ref, xhat_ref, means, put)

        in_stages(tile, [stats, work, finish], products)
        dt_ref[...] = jnp.transpose(dconv_ref[...])
        ht_ref[...] = jnp.transpose(hid_ref[...])

    @pl.when(step == 0)
    def _():
        tile_work([], 0)

    @pl.when((step > 0) & (step < steps))
    def _():
        tile_work(products, TURNED)

    put_edges(place_ref, inner_ref, outer_ref, dconv_ref, step == 0, step == steps - 1)

    @pl.when(step == steps)
    def _():
        copy = pltpu.make_async_copy(wct_ref, turned_ref, sem.at[4])
        copy.start()
        for work in products:
            work()
        core = lax.rem(place_ref[0], 2)
        _, rows_conv, rows_out = rows_of
        stage_turned(stage1_ref, core, gc_ref, rows_conv, 0, slice(0, CUT // LANE))
        first_tiles = rows_conv // SUB * (CUT // LANE)
        stage_plain(stage1_ref, core, go_ref, rows_out, first_tiles)
        copies = stage_copies(stage1_ref, outs[0], outs[1], spans(CHUNKS[0], rows_of)[1], sem, 0)
        for each in copies:
            each.start()
        stage_turned(stage2_ref, core, gc_ref, rows_conv, 0, slice(CUT // LANE, INNER // LANE))
        more = stage_copies(stage2_ref, outs[2], outs[3], spans(CHUNKS[1], rows_of)[1], sem, 2)
        for each in more:
            each.start()
        for each in copies + more + [copy]:
            each.wait()
        sums_ref[0:1, :] = jnp.sum(acc_ref[0:8, :], axis=0, keepdims=True)
        sums_ref[1:2, :] = jnp.sum(acc_ref[8:16, :], axis=0, keepdims=True)


def stage_tiles(stage_ref, core, first_row, rows_each, base, block0, blocks, value):
    for g in range(value.shape[0] // SUB):
        row = first_row + g * SUB
        owner, inside = row // rows_each, row % rows_each // SUB
        side = core ^ (owner % 2)
        for b in range(value.shape[1] // LANE):
            tile = value[g * SUB : (g + 1) * SUB, b * LANE : (b + 1) * LANE]
            at = base + inside * blocks + block0 + b
            stage_ref[side, owner // 2, at] = tile.astype(BF16)


def stage_plain(stage_ref, core, grad_ref, rows_each, base):
    blocks = grad_ref.shape[1] // LANE
    for row in range(0, grad_ref.shape[0], SUB):
        part = grad_ref[row : row + SUB, :]
        stage_tiles(stage_ref, core, row, rows_each, base, 0, blocks, part)


def stage_turned(stage_ref, core, turned_ref, rows_each, base, blocks):
    count = blocks.stop - blocks.start
    for row in range(0, turned_ref.shape[1], LANE):
        for b in range(count):
            at = (blocks.start + b) * LANE
            part = jnp.transpose(turned_ref[at : at + LANE, row : row + LANE].astype(BF16))
            stage_tiles(stage_ref, core, row, rows_each, base, b, count, part)


def stage_copies(stage_ref, keep_ref, send_ref, used, sem, first):
    count = stage_ref.shape[2]
    if used < count:
        dims = stage_ref.shape[:2] + (count - used, SUB, LANE)
        stage_ref[:, :, used:] = jnp.zeros(dims, BF16)
    return [
        pltpu.make_async_copy(stage_ref.at[n], ref, sem.at[first + n])
        for n, ref in enumerate((keep_ref, send_ref))
    ]


def back_conv_kernel(
    last, rows_in, place_ref, low_ref, d_ref, high_ref, turned_ref, mask_ref, xhat_ref, rstd_ref, slope_ref, hid_ref, np_ref, *refs
):
    if last:
        before_ref, dpre_ref, sums_ref, keep_ref, send_ref, stage_ref = refs[:6]
    else:
        dpre_ref, sums_ref, part_ref = refs[:3]
    ext_ref, wt_ref, taps_ref, dmov_ref, grad_ref, acc_ref, sem = refs[-7:]
    step, steps = pl.program_id(0), pl.num_programs(0)
    tile = taps_ref.shape[0]
    open_sums(acc_ref)

    @pl.when(step == 0)
    def _():
        copies = load_window(place_ref, low_ref, d_ref, high_ref, ext_ref, sem)
        copies.append(pltpu.make_async_copy(turned_ref, wt_ref, sem.at[3]))
        if last:
            copies.append(pltpu.make_async_copy(before_ref, grad_ref, sem.at[4]))
        for copy in copies:
            copy.start()
        if not last:
            grad_ref[...] = jnp.zeros_like(grad_ref)
        for copy in copies:
            copy.wait()

    fill_taps(taps_ref, ext_ref, mask_ref, (steps * last + step) * tile)
    for half in halves_of(tile):
        dmov_ref[half, :] = lax.dot_general(
            taps_ref[half, :], wt_ref[...], NN, preferred_element_type=F32
        )

    def work(rows, _):
        live = mask_ref[rows, MID : MID + 1]
        sums = [0.0, 0.0]
        for b in lane_blocks(INNER):
            xhat = xhat_ref[rows, b].astype(F32)
            dy = dmov_ref[rows, b] * live * slope_ref[rows, b].astype(F32)
            add_terms(acc_ref, b, dy, xhat)
            dxhat = dy * np_ref[0:1, D + b.start : D + b.stop]
            dmov_ref[rows, b] = dxhat
            sums = [sums[0] + dxhat, sums[1] + dxhat * xhat]
        return row_means(sums, INNER) + [rstd_ref[rows, :]]

    def finish(rows, means):
        def put(b, value):
            dpre_ref[rows, b] = value.astype(BF16)

        norm_back(rows, dmov_ref, xhat_ref, means, put)

    in_stages(tile, [work, finish])
    close_sums(sums_ref, acc_ref)
    grad_ref[...] += lax.dot_general(dpre_ref[...], hid_ref[...], TN, preferred_element_type=F32)

    @pl.when(step == steps - 1)
    def _():
        if last:
            all_blocks = slice(0, INNER // LANE)
            stage_turned(stage_ref, lax.rem(place_ref[0], 2), grad_ref, rows_in, 0, all_blocks)
            used = rows_in // SUB * (INNER // LANE)
            run_copies(stage_copies(stage_ref, keep_ref, send_ref, used, sem, 0))
        else:
            run_copies([pltpu.make_async_copy(grad_ref, part_ref, sem.at[0])])


def back_a_kernel(pieces, half, place_ref, dpre0_ref, dpre1_ref, xhat_ref, rstd_ref, slope_ref, cot_ref, np_ref, *refs):
    piece_refs = refs[:pieces]
    grad_ref, sums_ref, w_ref, wt_ref, dh_ref, acc_ref, sem = refs[-7:]
    open_sums(acc_ref)

    @pl.when(pl.program_id(0) == 0)
    def _():
        run_copies(piece_copies(piece_refs, w_ref, place_ref[0], sem))
        for k in range(0, D, 256):
            wt_ref[:, k : k + 256] = jnp.transpose(w_ref[k : k + 256, :])

    second = (jnp.zeros((1, 1), jnp.int32) + pl.program_id(0)) >= half
    d_pre = jnp.where(second, dpre1_ref[...], dpre0_ref[...])
    dh_ref[...] = lax.dot_general(d_pre, wt_ref[...], NN, preferred_element_type=F32)

    def work(rows, _):
        sums = [0.0, 0.0]
        for b in lane_blocks(D):
            xhat = xhat_ref[rows, b].astype(F32)
            dy = dh_ref[rows, b] * slope_ref[rows, b].astype(F32)
            add_terms(acc_ref, b, dy, xhat)
            dxhat = dy * np_ref[0:1, b]
            dh_ref[rows, b] = dxhat
            sums = [sums[0] + dxhat, sums[1] + dxhat * xhat]
        return row_means(sums, D) + [rstd_ref[rows, :]]

    def finish(rows, means):
        def put(b, value):
            grad_ref[rows, b] = cot_ref[rows, b].astype(F32) + value

        norm_back(rows, dh_ref, xhat_ref, means, put)

    in_stages(dpre0_ref.shape[0], [work, finish])
    close_sums(sums_ref, acc_ref)


def out_kernel(pieces, place_ref, hid_ref, tok_ref, *refs):
    piece_refs = refs[:pieces]
    out_ref, w_ref, sem = refs[pieces:]

    @pl.when(pl.program_id(0) == 0)
    def _():
        run_copies(out_copies(piece_refs, w_ref, place_ref[0], sem))

    branch = lax.dot_general(hid_ref[...], w_ref[...], NN, preferred_element_type=F32)
    out_ref[...] = (tok_ref[...].astype(F32) + branch).astype(BF16)


WIDTHS = (INNER, INNER, D)
LANE0 = (0, INNER, 2 * INNER)
CUT = 2 * LANE
CHUNKS = (((1, 0, CUT), (2, 0, D)), ((1, CUT, INNER - CUT),), ((0, 0, INNER),))


def spans(chunk, rows):
    found, first = [], 0
    for weight, col, cols in chunk:
        tiles = rows[weight] // SUB * (cols // LANE)
        found.append((weight, col // LANE, cols // LANE, first, tiles))
        first += tiles
    return found, first


def column_sums(pack_ref, row, ref, chunk, rows):
    for weight, block0, blocks, first, tiles in spans(chunk, rows)[0]:

        def body(g, carry, first=first, blocks=blocks):
            new = []
            for b in range(blocks):
                value = ref[first + g * blocks + b].astype(F32)
                new.append(carry[b] + fold(value * value + 1e-30))
            return tuple(new)

        zero = tuple(jnp.zeros((8, LANE), F32) for _ in range(blocks))
        cols = lax.fori_loop(0, tiles // blocks, body, zero, unroll=5)
        for b in range(blocks):
            lane = LANE0[weight] + (block0 + b) * LANE
            pack_ref[row : row + 1, lane : lane + LANE] = jnp.sum(cols[b], axis=0, keepdims=True)


def load_full(refs, place_ref, first, full_ref, sem, at):
    pieces = refs[0].shape[0]
    each = full_ref.shape[0] // (len(refs) * pieces)
    outer = pieces if len(refs) == 2 else pieces // 2
    y = place_ref[2] % 2
    copies = []
    for n, (ref, side) in enumerate(zip(refs, (y, 1 - y))):
        for p in range(pieces):
            index = side * outer + p if len(refs) == 2 else p % 2 * outer + p // 2
            target = full_ref.at[pl.ds(index * each, each)]
            source = ref.at[p, first : first + each]
            copies.append(pltpu.make_async_copy(source, target, sem.at[at + n * pieces + p]))
    return copies


def load_halves(mine_ref, other_ref, place_ref, full_ref, sem):
    y, each = lax.rem(place_ref[2], 2), mine_ref.shape[0]
    return [
        pltpu.make_async_copy(ref, full_ref.at[pl.ds(side * each, each)], sem.at[n])
        for n, (ref, side) in enumerate(((mine_ref, y), (other_ref, 1 - y)))
    ]


PACK_BLOCKS = (D + 2 * INNER) // LANE


def pack_line(pack_ref, row, lane0, width):
    parts = []
    for lane in range(lane0, lane0 + width, LANE):
        at = row * PACK_BLOCKS + lane // LANE
        parts.append(pack_ref[at // SUB, at % SUB : at % SUB + 1, :])
    return jnp.concatenate(parts, axis=1)


def pack_kernel(rows, pieces, place_ref, part_ref, *refs):
    states, sums, (pack_ref, acc_ref) = refs[0:3], refs[3:7], refs[7:9]
    pack_ref[...] = jnp.zeros_like(pack_ref)

    def add(row, lane, value):
        at = row * PACK_BLOCKS + lane // LANE
        pack_ref[at // SUB, at % SUB : at % SUB + 1, :] += value

    lanes_of = ((0, D), (D, D + INNER), (D, D + INNER), (D + INNER, D + 2 * INNER))
    for part, (lane0, lane1) in zip(sums, lanes_of):
        for lane in range(lane0, lane1, LANE):
            for row in range(2):
                add(row, lane, part[row : row + 1, lane - lane0 : lane - lane0 + LANE])
    lanes = lax.broadcasted_iota(jnp.int32, (1, LANE), 1)
    for k in range(3):
        total = jnp.sum(states[k][...].reshape(1, -1), axis=1, keepdims=True)
        add(3, 0, jnp.where(lanes == k, total, 0.0))
    acc_ref[...] = jnp.zeros_like(acc_ref)
    spare = acc_ref.shape[0] - 1
    outer = place_ref[3] // 2
    piece = place_ref[2] % 2 * outer + place_ref[2] // 2
    at = 0
    for chunk, each in zip(CHUNKS[:2], pieces):
        found, _ = spans(chunk, rows)
        start = piece * each

        def body(k, carry, found=found, start=start, at=at):
            n = start + k
            slot = spare
            for weight, block0, blocks, first, tiles in found:
                here = LANE0[weight] // LANE + block0 + lax.rem(jnp.maximum(n - first, 0), blocks)
                slot = jnp.where((n >= first) & (n < first + tiles), here, slot)
            value = part_ref[at + k].astype(F32)
            acc_ref[slot] += value * value + 1e-30
            return carry

        lax.fori_loop(0, each, body, 0, unroll=2)
        at += each
    for slot in range(spare):
        add(2, slot * LANE, jnp.sum(acc_ref[slot], axis=0, keepdims=True))


def pack_in_kernel(rows, place_ref, mine_ref, other_ref, pack_ref, full_ref, sem):
    run_copies(load_halves(mine_ref, other_ref, place_ref, full_ref, sem))
    pack_ref[...] = jnp.zeros_like(pack_ref)
    column_sums(pack_ref, 0, full_ref, CHUNKS[2], rows)


def update_weight(
    k, squares, states_sum, source, weight, state, col_state, grad_ref, new, row_new_ref, col_new_ref, scratch, step=0, steps=1
):
    line_ref, state_ref, new_ref, scaled_ref = scratch
    width, fan, rows_here = WIDTHS[k], (D, KERNEL_TAPS * INNER, INNER)[k], state.shape[0]
    whole_rows = rows_here + -rows_here % LANE
    groups = rows_here // SUB // steps
    rate = 0.5 / fan**0.5

    def before():
        col_new = DECAY * col_state[...].reshape(1, -1) + (1.0 - DECAY) * (squares * (1.0 / fan))
        col_new_ref[...] = col_new.reshape(-1)
        total = DECAY * states_sum
        total = total + (1.0 - DECAY) * (1.0 / width) * jnp.sum(squares, axis=1, keepdims=True)
        scaled_ref[0:1, 0:width] = col_new / (total * (1.0 / fan))
        line_ref[0:1, 0:rows_here] = state[...].reshape(1, -1)
        for c in range(0, whole_rows, LANE):
            state_ref[c : c + LANE, :] = column(line_ref[0:1, c : c + LANE])

    def after():
        for c in range(0, whole_rows, LANE):
            line_ref[0:1, c : c + LANE] = jnp.transpose(new_ref[c : c + LANE, :])[0:1, :]
        row_new_ref[...] = line_ref[0:1, 0:rows_here].reshape(-1)

    def body(g, carry):
        here = pl.ds(pl.multiple_of(g * SUB, SUB), SUB)
        at = step * groups + g
        rows = pl.ds(pl.multiple_of(at * SUB, SUB), SUB)
        square = 0.0
        for ref, block0, blocks, first in source:
            for b in range(blocks):
                value = ref[first + at * blocks + b].astype(F32)
                grad_ref[here, (block0 + b) * LANE : (block0 + b + 1) * LANE] = value
                square = square + (value * value + 1e-30)
        mean = jnp.sum(square, axis=1, keepdims=True) * (1.0 / width)
        row_new = DECAY * state_ref[rows, :] + (1.0 - DECAY) * mean
        new_ref[rows, :] = row_new
        for ref, block0, blocks, first in source:
            for b in range(blocks):
                lanes = slice((block0 + b) * LANE, (block0 + b + 1) * LANE)
                value = ref[first + at * blocks + b].astype(F32)
                change = value * lax.rsqrt(row_new * scaled_ref[0:1, lanes])
                new[here, lanes] = weight[here, lanes] - rate * change
        return carry

    if steps == 1:
        before()
        lax.fori_loop(0, groups, body, 0, unroll=5)
        after()
    else:
        pl.when(step == 0)(before)
        lax.fori_loop(0, groups, body, 0, unroll=5)
        pl.when(step == steps - 1)(after)


def sources_of(chunk, ref, rows):
    return {w: (ref, block0, blocks, first) for w, block0, blocks, first, _ in spans(chunk, rows)[0]}


def update_kernel(rows, copies_of, place_ref, mine_ref, other_ref, pack_ref, *refs):
    weights, states, col_states = refs[0:2], refs[2:4], refs[4:6]
    grads, news, rows_new, cols_new = refs[6:8], refs[8:10], refs[10:12], refs[12:14]
    conv_scratch, out_scratch = refs[14:18], refs[18:22]
    full1_ref, full2_ref, sem = refs[22:25]
    both = (mine_ref, other_ref)
    count = 2 * mine_ref.shape[0]
    step, steps = pl.program_id(0), pl.num_programs(0)

    @pl.when(step == 0)
    def _():
        copies = load_full(both, place_ref, 0, full1_ref, sem, 0)
        copies += load_full(both, place_ref, full1_ref.shape[0] // count, full2_ref, sem, count)
        run_copies(copies)

    from1 = sources_of(CHUNKS[0], full1_ref, rows)
    from2 = sources_of(CHUNKS[1], full2_ref, rows)

    def update(n, k, source, scratch, *steps):
        squares = pack_line(pack_ref, 2, LANE0[k], WIDTHS[k])
        update_weight(
            k, squares, pack_line(pack_ref, 3, 0, LANE)[:, k : k + 1] * (1.0 / copies_of), source, weights[n],
            states[n], col_states[n], grads[n], news[n], rows_new[n], cols_new[n], scratch, *steps,
        )

    update(0, 1, [from1[1], from2[1]], conv_scratch, step, UPDATE_STEPS)

    @pl.when(step == steps - 1)
    def _():
        update(1, 2, [from1[2]], out_scratch)


def update_in_kernel(
    rows, copies_of, place_ref, mine_ref, other_ref, pack_in_ref, pack_ref, np_ref, second_ref, *refs
):
    weight, state, col_state, grad_ref, new_ref, row_new_ref, col_new_ref = refs[0:7]
    ngrad_ref, nsecond_ref, nnew_ref = refs[7:10]
    full_ref, sem = refs[14:16]
    copies = load_halves(mine_ref, other_ref, place_ref, full_ref, sem)
    for copy in copies:
        copy.start()
    lines = [pack_line(pack_ref, row, 0, D + 2 * INNER) for row in range(2)]
    grad = jnp.concatenate(lines, axis=0)
    second = DECAY * second_ref[...] + (1.0 - DECAY) * (grad * grad + 1e-30)
    ngrad_ref[...] = grad
    nsecond_ref[...] = second
    nnew_ref[...] = np_ref[...] - 0.2 * grad * lax.rsqrt(second)
    for copy in copies:
        copy.wait()
    update_weight(
        0, pack_in_ref[0:1, :], pack_line(pack_ref, 3, 0, LANE)[:, 0:1] * (1.0 / copies_of),
        [sources_of(CHUNKS[2], full_ref, rows)[0]], weight, state, col_state, grad_ref, new_ref,
        row_new_ref, col_new_ref, refs[10:14],
    )


class Places:
    def __init__(self):
        self.seq, self.fsdp = lax.axis_size("seq"), lax.axis_size("fsdp")
        self.q = lax.axis_index("fsdp")
        self.s = lax.axis_index("seq")

    def flip(self, x, axis, bit):
        pairs = []
        for s in range(self.seq):
            for f in range(self.fsdp):
                s2, f2 = (s ^ bit, f) if axis == "seq" else (s, f ^ bit)
                pairs.append((s * self.fsdp + f, s2 * self.fsdp + f2))
        return lax.ppermute(x, AXES, pairs)


def bits_of(count):
    return [1 << k for k in range(count.bit_length() - 1)]


def tie(x, *others):
    return lax.optimization_barrier((x, *others))[0]


def gather_pieces(piece, place, after, later=()):
    found = {0: piece}
    for bit in reversed(bits_of(place.fsdp)):
        for k in list(found):
            moving = found[k]
            if bit == 1:
                moving = tie(moving, *((after,) if k == 0 or not later else later))
            found[k | bit] = place.flip(moving, "fsdp", bit)
    return [found[k] for k in range(place.fsdp)]


def sum_over(x, place, *axes):
    for axis in axes:
        for bit in bits_of(getattr(place, axis)):
            x = x + place.flip(x, axis, bit)
    return x


def sum_along_z(x, place):
    terms = [x] + [place.flip(x, "seq", 2 * k) for k in range(1, place.seq // 2)]
    while len(terms) > 1:
        terms = [a + b for a, b in zip(terms[::2], terms[1::2])]
    return terms[0]


def pick(x, index, axis):
    return lax.dynamic_index_in_dim(x, index, axis=axis, keepdims=False)


class Reduction:
    def __init__(self, place, keep, send):
        self.place, self.near = place, keep
        self.got = place.flip(send, "fsdp", 1)

    def halve(self, axis, side, flip_axis, bit):
        dims = self.near.shape
        parts = dims[:axis] + (2, dims[axis] // 2) + dims[axis + 1 :]
        near, got = self.near.reshape(parts), self.got.reshape(parts)
        away = pick(near, 1 - side, axis).astype(F32) + pick(got, 1 - side, axis).astype(F32)
        self.near = pick(near, side, axis).astype(F32) + pick(got, side, axis).astype(F32)
        away = away.astype(BF16)
        self.got = self.place.flip(away, flip_axis, bit)
        return away

    def x(self):
        bit = self.place.fsdp // 2
        while bit > 1:
            away = self.halve(0, (self.place.q // bit) % 2, "fsdp", bit)
            bit //= 2
        return away

    def y(self):
        return self.halve(1, self.place.s % 2, "seq", 1)

    def whole_half(self):
        self.near = self.rounded(self.near + self.got.astype(F32))

    def rounded(self, total):
        return lax.optimization_barrier(total.astype(BF16))

    def send_half(self, bit):
        self.got = self.place.flip(self.near, "seq", bit)

    def add_half(self):
        self.near = self.rounded(self.near.astype(F32) + self.got.astype(F32))

    def pieces(self):
        total = (self.near + self.got.astype(F32)).astype(BF16)
        return total.reshape((self.place.seq // 2, -1) + total.shape[2:])


def arrive(result, *reductions):
    result, *gots = lax.optimization_barrier((result, *[r.got for r in reductions]))
    for reduction, got in zip(reductions, gots):
        reduction.got = got
    return result


def summed_f32(got):
    return jnp.sum(got.astype(F32), axis=0)


def summed(got):
    return summed_f32(got).astype(BF16)


def exchange(place, sent):
    line = [[y + 2 * z for z in range(place.seq // 2)] for y in range(2)]
    return lax.all_to_all(sent, "seq", 0, 0, axis_index_groups=line)


def on_device(
    tokens, input_mask, doc_lengths, cotangent, w_in, w_conv, w_out, norm_params,
    row_in, col_in, row_conv, col_conv, row_out, col_out, norm_second,
):
    place = Places()
    rows = tokens.shape[0]
    pieces = place.fsdp
    spots = jnp.stack(
        [place.q, (place.s * place.fsdp + place.q) * rows, place.s, place.seq]
    ).astype(jnp.int32)
    docs = doc_lengths.shape[0]
    live = input_mask.reshape(-1, LANE)
    weights = (w_in, w_conv, w_out)
    rows_of = [w.shape[0] for w in weights]

    tile_a, tile = 256, 512
    steps = rows // tile
    params_spec = whole(2, D + 2 * INNER)
    dma = pltpu.SemaphoreType.DMA

    out_sides = (w_out[:, : D // 2], w_out[:, D // 2 :])
    conv_out = jnp.concatenate([w_conv, *out_sides], axis=0).astype(BF16)
    hidden_a, slope_a, xhat_a, rstd_a = call(
        norm_a_kernel,
        (rows // tile_a,),
        [rows_spec(tile_a, D), params_spec],
        [rows_spec(tile_a, D)] * 3 + [rows_spec(tile_a, LANE)],
        [shape((rows, D), BF16)] * 3 + [shape((rows, LANE), F32)],
        us=17,
    )(tokens, tie(norm_params, conv_out))

    in_pieces = gather_pieces(w_in.astype(BF16), place, hidden_a)

    def in_call(tiles, count, before):
        at, stride = tiles

        def here_spec(width):
            return pl.BlockSpec((tile, width), lambda i: (at + stride * i, 0))

        out_shapes = [shape((rows, INNER), BF16)] * 3 + [shape((rows, LANE), F32)] * 2
        out_specs = [here_spec(INNER)] * 3 + [here_spec(LANE)] * 2
        if at == 0:
            out_shapes += [shape((REACH, INNER), BF16)] * 2
            out_specs += [whole(REACH, INNER)] * 2
        return call(
            functools.partial(in_kernel, pieces, tiles),
            (count,),
            [SMEM, whole(docs), here_spec(D), whole(*live.shape), params_spec]
            + [ANY] * (pieces + len(before)),
            out_specs,
            out_shapes,
            [pltpu.VMEM((D, INNER), BF16), pltpu.VMEM((tile, INNER), F32)]
            + [pltpu.VMEM((8, docs + -docs % LANE), F32), dma((pieces,))],
            us=3,
            aliases={5 + pieces + k: k for k in range(len(before))},
        )(spots, doc_lengths, hidden_a, live, norm_params, *in_pieces, *before)

    *kept, m_first, m_last = in_call((0, steps - 1), 2, ())
    moved, slope_b, xhat_b, rstd_b, masks = in_call((1, 1), steps - 2, kept)

    def halo(inner, outer):
        total = place.seq * place.fsdp
        across = [(i, i + 1 if i % 2 else i - 1) for i in range(1, total - 1)]
        return place.flip(inner, "fsdp", 1), lax.ppermute(outer, AXES, across)

    m_inner, m_outer = halo(m_first, m_last)
    conv_pieces = gather_pieces(conv_out, place, m_first, (moved, m_inner, m_outer))

    ext = pltpu.VMEM((rows + 2 * REACH, INNER), BF16)
    taps_wide = KERNEL_TAPS * INNER
    wide = pltpu.VMEM((taps_wide, INNER), BF16)
    shards = place.fsdp // 2

    def half_dims(chunk):
        count = spans(chunk, rows_of)[1]
        return (shards, count + -count % place.seq, SUB, LANE)

    def tile_spec(width, ahead):
        return pl.BlockSpec((tile, width), lambda i: (jnp.clip(i + ahead, 0, steps - 1), 0))

    halves = [half_dims(CHUNKS[0])] * 2 + [half_dims(CHUNKS[1])] * 2
    work = pltpu.VMEM((tile, INNER), F32)
    turned_tile = pltpu.VMEM((INNER, tile), BF16)
    hidden_c, d_conv, d_first, d_last, sums_c, turned, keep1, send1, keep2, send2 = call(
        functools.partial(conv_kernel, pieces, rows_of),
        (steps + 1,),
        [SMEM, ANY, ANY, ANY, tile_spec(LANE, 0), tile_spec(D, 0), tile_spec(D, -1), params_spec]
        + [ANY] * pieces,
        [tile_spec(INNER, 0)] * 2
        + [whole(REACH, INNER), whole(REACH, INNER), whole(2, INNER)]
        + [ANY] * 5,
        [
            shape((rows, INNER), BF16),
            shape((rows, INNER), BF16),
            shape((REACH, INNER), BF16),
            shape((REACH, INNER), BF16),
            shape((2, INNER), F32),
            shape((taps_wide, INNER), BF16),
        ]
        + [shape(dims, BF16) for dims in halves],
        [ext, wide, wide, pltpu.VMEM((INNER, D), BF16), pltpu.VMEM((D, INNER), BF16)]
        + [pltpu.VMEM((2, tile, taps_wide), BF16), work, work, work, turned_tile, turned_tile]
        + [pltpu.VMEM((INNER, taps_wide), F32), pltpu.VMEM((INNER, D), F32)]
        + [pltpu.VMEM((16, INNER), F32)]
        + [pltpu.VMEM((2,) + halves[0], BF16), pltpu.VMEM((2,) + halves[2], BF16)]
        + [dma((3 + 3 * pieces,))],
        us=45,
    )(
        spots, m_inner, moved, m_outer, masks, cotangent, cotangent, norm_params, *conv_pieces
    )
    d_inner, d_outer = halo(d_first, d_last)
    first, second = Reduction(place, keep1, send1), Reduction(place, keep2, send2)
    def back_conv(last, spots, before):
        here = steps // 2
        at = here * last

        def here_spec(width):
            return pl.BlockSpec((tile, width), lambda i: (i + at, 0))

        dims = half_dims(CHUNKS[2])
        return call(
            functools.partial(back_conv_kernel, last, w_in.shape[0]),
            (here,),
            [SMEM] + [ANY] * 4
            + [here_spec(LANE), here_spec(INNER), here_spec(LANE), here_spec(INNER), here_spec(D)]
            + [params_spec]
            + [ANY] * last,
            [rows_spec(tile, INNER), whole(2, INNER)] + [ANY] * (1 + last),
            [shape((rows // 2, INNER), BF16), shape((2, INNER), F32)]
            + ([shape(dims, BF16)] * 2 if last else [shape((INNER, D), F32)]),
            ([pltpu.VMEM((2,) + dims, BF16)] if last else [])
            + [
                ext,
                wide,
                pltpu.VMEM((tile, taps_wide), BF16),
                pltpu.VMEM((tile, INNER), F32),
                pltpu.VMEM((INNER, D), F32),
                pltpu.VMEM((16, INNER), F32),
                dma((5,)),
            ],
            us=16,
        )(
            spots, d_inner, d_conv, d_outer, turned, masks, xhat_b, rstd_b, slope_b, hidden_a,
            norm_params, *before,
        )

    d_inner, d_outer = arrive((d_inner, d_outer), first, second)
    away = (first.x(), second.y())
    d_pre0, sums_b0, grad_part = back_conv(0, tie(spots, *away), ())
    d_pre0 = arrive(d_pre0, first, second)
    away = (first.y(), second.x())
    d_pre1, sums_b1, keep, send = back_conv(1, tie(spots, *away), (grad_part,))
    send = arrive(send, first, second)
    third = Reduction(place, keep, send)
    sent = jnp.concatenate([first.pieces(), second.pieces()], axis=1)
    got = exchange(place, sent)
    third.got = tie(third.got, sent)
    away = (sent, third.x())
    input_grad, sums_a = call(
        functools.partial(back_a_kernel, pieces, steps // 2),
        (steps,),
        [SMEM]
        + [
            pl.BlockSpec((tile, INNER), lambda i: (jnp.minimum(i, steps // 2 - 1), 0)),
            pl.BlockSpec((tile, INNER), lambda i: (jnp.maximum(i - steps // 2, 0), 0)),
        ]
        + [rows_spec(tile, D), rows_spec(tile, LANE), rows_spec(tile, D), rows_spec(tile, D)]
        + [params_spec]
        + [ANY] * pieces,
        [rows_spec(tile, D), whole(2, D)],
        [shape((rows, D), F32), shape((2, D), F32)],
        [
            pltpu.VMEM((D, INNER), BF16),
            pltpu.VMEM((INNER, D), BF16),
            pltpu.VMEM((tile, D), F32),
            pltpu.VMEM((16, D), F32),
            dma((pieces,)),
        ],
        us=17,
    )(
        tie(spots, *away), d_pre0, d_pre1, xhat_a, rstd_a, slope_a, cotangent, norm_params, *in_pieces
    )

    row_states, col_states = (row_in, row_conv, row_out), (col_in, col_conv, col_out)
    row_specs = [whole(*r.shape) for r in row_states]
    col_specs = [whole(*c.shape) for c in col_states]
    cols_all = D + 2 * INNER
    pack_dims = (4 * PACK_BLOCKS // SUB, SUB, LANE)
    pack_spec = whole(*pack_dims)
    fulls = [pltpu.VMEM(half_dims(c)[1:], BF16) for c in CHUNKS]
    sums = (sums_a, sums_b0, sums_b1, sums_c)
    got, third.got, input_grad = lax.optimization_barrier((got, third.got, input_grad))
    part = summed(got)
    sent = jnp.broadcast_to(part[None], (place.seq // 2,) + part.shape)
    mine = exchange(place, sent)
    third.got = tie(third.got, sent)
    away = third.y()
    (pack,) = call(
        functools.partial(pack_kernel, rows_of, [half_dims(c)[1] // place.seq for c in CHUNKS]),
        (1,),
        [SMEM, whole(*part.shape)] + row_specs + [whole(*x.shape) for x in sums],
        [pack_spec],
        [shape(pack_dims, F32)],
        [pltpu.VMEM((cols_all // LANE + 1, SUB, LANE), F32)],
        us=2,
        mib=16,
    )(tie(spots, away), part, *row_states, *sums)
    pack = sum_over(pack, place, "fsdp")
    third.got, pack = lax.optimization_barrier((third.got, pack))
    seq_bits = bits_of(place.seq)
    third.whole_half()
    for bit in seq_bits[1:-1]:
        third.send_half(bit)
        pack = pack + place.flip(pack, "seq", 1) if bit == 2 else pack
        if bit != seq_bits[-2]:
            third.add_half()
    mine, third.got, pack = lax.optimization_barrier((mine, third.got, pack))
    other = place.flip(mine, "seq", 1)
    third.add_half()
    third.send_half(seq_bits[-1])
    (block_out,) = call(
        functools.partial(out_kernel, pieces),
        (steps,),
        [SMEM, rows_spec(tile, INNER), rows_spec(tile, D)] + [ANY] * pieces,
        [rows_spec(tile, D)],
        [shape((rows, D), BF16)],
        [pltpu.VMEM((INNER, D), BF16), dma((2 * pieces,))],
        us=1,
    )(tie(spots, pack), hidden_c, tokens, *conv_pieces)
    pack = sum_along_z(pack, place)
    third.got, other, pack, block_out = lax.optimization_barrier(
        (third.got, other, pack, block_out)
    )
    third.add_half()
    line = third.near.reshape(third.near.shape[1:])
    line_other = place.flip(line, "seq", 1)

    def update_scratch(weight):
        lines = weight.shape[0] + -weight.shape[0] % LANE
        return (
            [pltpu.VMEM((8, lines), F32)]
            + [pltpu.VMEM((lines, LANE), F32)] * 2
            + [pltpu.VMEM((8, weight.shape[1]), F32)]
        )

    weight_specs = [whole(*w.shape) for w in weights]
    conv_block = pl.BlockSpec((w_conv.shape[0] // UPDATE_STEPS, INNER), lambda i: (i, 0))
    both_specs = [conv_block, weight_specs[2]]
    results = call(
        functools.partial(update_kernel, rows_of, place.seq),
        (UPDATE_STEPS,),
        [SMEM, ANY, ANY, pack_spec] + both_specs + row_specs[1:] + col_specs[1:],
        both_specs * 2 + row_specs[1:] + col_specs[1:],
        [shape(w.shape, F32) for w in weights[1:]] * 2
        + [shape(r.shape, F32) for r in row_states[1:] + col_states[1:]],
        update_scratch(w_conv)
        + update_scratch(w_out)
        + fulls[:2]
        + [dma((2 * place.seq,))],
        us=8,
        mib=32,
    )(spots, mine, other, pack, *weights[1:], *row_states[1:], *col_states[1:])
    grad_conv, grad_out, new_conv, new_out, row_conv_new, row_out_new, col_conv_new, col_out_new = (
        results
    )
    line_other, grad_out = lax.optimization_barrier((line_other, grad_out))
    (pack_in,) = call(
        functools.partial(pack_in_kernel, rows_of),
        (1,),
        [SMEM, ANY, ANY],
        [whole(8, INNER)],
        [shape((8, INNER), F32)],
        [fulls[2], dma((place.seq,))],
        us=2,
        mib=16,
    )(spots, line, line_other)
    pack_in = sum_over(pack_in, place, "fsdp")
    grad_in, new_in, row_in_new, col_in_new, *norm_results = call(
        functools.partial(update_in_kernel, rows_of, place.seq),
        (1,),
        [SMEM, ANY, ANY, whole(8, INNER), pack_spec, params_spec, params_spec]
        + [weight_specs[0], row_specs[0], col_specs[0]],
        [weight_specs[0]] * 2 + [row_specs[0], col_specs[0]] + [params_spec] * 3,
        [shape(w_in.shape, F32)] * 2
        + [shape(row_in.shape, F32), shape(col_in.shape, F32)]
        + [shape((2, cols_all), F32)] * 3,
        update_scratch(w_in) + [fulls[2], dma((place.seq,))],
        us=4,
        mib=24,
    )(
        spots, line, line_other, pack_in, pack, norm_params, norm_second, w_in, row_in, col_in
    )
    return (
        block_out,
        input_grad,
        grad_in,
        grad_conv,
        grad_out,
        new_in,
        new_conv,
        new_out,
        row_in_new,
        col_in_new,
        row_conv_new,
        col_conv_new,
        row_out_new,
        col_out_new,
        *norm_results,
    )


def solution(mesh):
    both, rows = P(AXES, None), P("fsdp", None)
    in_specs = (
        both, P(AXES), P(), both, rows, rows, rows, P(),
        P("fsdp"), P(), P("fsdp"), P(), P("fsdp"), P(), P(),
    )
    out_specs = (
        both, both, rows, rows, rows, rows, rows, rows,
        P("fsdp"), P(), P("fsdp"), P(), P("fsdp"), P(), P(), P(), P(),
    )
    return jax.shard_map(
        on_device, mesh=mesh, in_specs=in_specs, out_specs=out_specs, check_vma=False
    )
```

```python
import functools
import math

import jax
import jax.numpy as jnp
from jax import lax
from jax.experimental import pallas as pl
from jax.experimental.pallas import tpu as pltpu
from jax.sharding import PartitionSpec as P

D = 1280
INNER = 640
KERNEL_TAPS = 5
DILATION_STEP = 128
STEP = 10
EPSILON = 1e-05
DECAY = 1.0 - STEP ** (-0.8)

REACH = (KERNEL_TAPS - 1) // 2 * DILATION_STEP
MID = (KERNEL_TAPS - 1) // 2
F32 = jnp.float32
BF16 = jnp.bfloat16
SUB, LANE = 16, 128
AXES = ("seq", "fsdp")
NT = (((1,), (1,)), ((), ()))
TN = (((0,), (0,)), ((), ()))
NN = (((1,), (0,)), ((), ()))


def call(kernel, grid, in_specs, out_specs, out_shape, scratch=(), us=1.0, aliases=None, mib=58):
    params = pltpu.CompilerParams(
        vmem_limit_bytes=mib * 1024 * 1024, dimension_semantics=("arbitrary",) * len(grid)
    )
    return pl.pallas_call(
        kernel,
        grid=grid,
        in_specs=in_specs,
        out_specs=out_specs,
        out_shape=out_shape,
        scratch_shapes=list(scratch),
        compiler_params=params,
        input_output_aliases=aliases or {},
        cost_estimate=pl.CostEstimate(
                flops=int(us * 1.1e9), bytes_accessed=int(us * 3.4e6), transcendentals=0
        ),
    )


def shape(dims, dtype):
    return jax.ShapeDtypeStruct(dims, dtype)


def rows_spec(tile, width):
    return pl.BlockSpec((tile, width), lambda i: (i, 0))


def whole(*dims):
    return pl.BlockSpec(dims, lambda *_: (0,) * len(dims))


ANY = pl.BlockSpec(memory_space=pl.ANY)
SMEM = pl.BlockSpec(memory_space=pltpu.SMEM)


ERFC_P = 0.47 / math.sqrt(2.0)
ERFC_C = (
    0.12357219400743558,
    0.1999878668208835,
    -0.08033356004356296,
    0.3660253986657854,
    -0.1092519747040215,
)
LOG2E = 1.4426950408889634


def gelu_and_slope(y):
    t = pltpu.reciprocal(1.0 + ERFC_P * jnp.abs(y), approx=True)
    bell = jnp.exp2(y * y * (-0.5 * LOG2E))
    poly = ERFC_C[4] * t + ERFC_C[3]
    for c in ERFC_C[2::-1]:
        poly = poly * t + c
    tail = poly * t * bell
    cdf = jnp.where(y > 0.0, 1.0 - tail, tail)
    return y * cdf, cdf + y * (bell * (1.0 / math.sqrt(2.0 * math.pi)))


def lane_blocks(width):
    return [slice(k, k + LANE) for k in range(0, width, LANE)]


def row_stats(ref, rows):
    width = ref.shape[-1]
    blocks = lane_blocks(width)
    total = ref[rows, blocks[0]].astype(F32)
    for b in blocks[1:]:
        total = total + ref[rows, b].astype(F32)
    mean = jnp.sum(total, axis=-1, keepdims=True) * (1.0 / width)
    square = None
    for b in blocks:
        centered = ref[rows, b].astype(F32) - mean
        square = centered * centered if square is None else square + centered * centered
    variance = jnp.sum(square, axis=-1, keepdims=True) * (1.0 / width)
    return mean, lax.rsqrt(variance + EPSILON)


def fold(values):
    total = values[0:8]
    for k in range(8, values.shape[0], 8):
        total = total + values[k : k + 8]
    return total


def in_stages(count, stages, between=()):
    chunks = [slice(k, k + CHUNK) for k in range(0, count, CHUNK)]
    kept, rounds = {}, len(chunks) + len(stages) - 1
    for t in range(rounds):
        for n, stage in enumerate(stages):
            if 0 <= t - n < len(chunks):
                kept[n, t - n] = stage(chunks[t - n], kept.get((n - 1, t - n)))
        for work in between[t * len(between) // rounds : (t + 1) * len(between) // rounds]:
            work()


def halves_of(count):
    return (slice(0, count // 2), slice(count // 2, count))


def row_means(sums, width):
    return [jnp.sum(x, axis=-1, keepdims=True) * (1.0 / width) for x in sums]


def norm_back(rows, dxhat_ref, xhat_ref, means, put):
    mean_d, mean_dx, rstd = means
    for b in lane_blocks(dxhat_ref.shape[-1]):
        xhat = xhat_ref[rows, b].astype(F32)
        put(b, (dxhat_ref[rows, b] - mean_d - xhat * mean_dx) * rstd)


def add_terms(acc_ref, b, dy, xhat):
    acc_ref[0:8, b] += fold(dy * xhat)
    acc_ref[8:16, b] += fold(dy)


def open_sums(acc_ref):
    @pl.when(pl.program_id(0) == 0)
    def _():
        acc_ref[...] = jnp.zeros_like(acc_ref)


def close_sums(out_ref, acc_ref):
    @pl.when(pl.program_id(0) == pl.num_programs(0) - 1)
    def _():
        out_ref[0:1, :] = jnp.sum(acc_ref[0:8, :], axis=0, keepdims=True)
        out_ref[1:2, :] = jnp.sum(acc_ref[8:16, :], axis=0, keepdims=True)


def run_copies(copies):
    for copy in copies:
        copy.start()
    for copy in copies:
        copy.wait()


def piece_copies(pieces, full_ref, me, sem, first=0):
    each = full_ref.shape[0] // len(pieces)
    return [
        pltpu.make_async_copy(
            piece.at[0:each, :],
            full_ref.at[pl.ds(pl.multiple_of((me ^ k) * each, SUB), each), :],
            sem.at[first + k],
        )
        for k, piece in enumerate(pieces)
    ]


def out_copies(pieces, full_ref, me, sem, first=0):
    each, width = full_ref.shape[0] // len(pieces), full_ref.shape[1] // 2
    copies = []
    for k, piece in enumerate(pieces):
        rows = pl.ds(pl.multiple_of((me ^ k) * each, SUB), each)
        for side in range(2):
            at = piece.shape[0] - (2 - side) * each
            copies.append(
                pltpu.make_async_copy(
                    piece.at[at : at + each, :],
                    full_ref.at[rows, side * width : (side + 1) * width],
                    sem.at[first + 2 * k + side],
                )
            )
    return copies


def column(row):
    return jnp.transpose(jnp.broadcast_to(row, (LANE, LANE)))


CHUNK = 64
UPDATE_STEPS = 5
TURNED = 2


def norm_a_kernel(tok_ref, np_ref, hid_ref, slope_ref, xhat_ref, rstd_ref):
    def stats(rows, _):
        mean, rstd = row_stats(tok_ref, rows)
        rstd_ref[rows, :] = jnp.broadcast_to(rstd, (CHUNK, LANE))
        return mean, rstd

    def work(rows, kept):
        mean, rstd = kept
        for b in lane_blocks(D):
            xhat = (tok_ref[rows, b].astype(F32) - mean) * rstd
            hidden, slope = gelu_and_slope(xhat * np_ref[0:1, b] + np_ref[1:2, b])
            hid_ref[rows, b] = hidden.astype(BF16)
            slope_ref[rows, b] = slope.astype(BF16)
            xhat_ref[rows, b] = xhat.astype(BF16)

    in_stages(tok_ref.shape[0], [stats, work])


def running_ends(ends_ref, lengths_ref):
    docs, width = lengths_ref.shape[0], ends_ref.shape[1]
    ends_ref[...] = jnp.zeros_like(ends_ref)
    ends_ref[0:1, 0:docs] = lengths_ref[...].reshape(1, -1).astype(F32)
    before = jnp.zeros((1, 1), F32)
    row = lax.broadcasted_iota(jnp.int32, (LANE, LANE), 0)
    lane = lax.broadcasted_iota(jnp.int32, (LANE, LANE), 1)
    for k in range(0, width, LANE):
        line = ends_ref[0:1, k : k + LANE]
        sums = jnp.sum(jnp.where(row <= lane, column(line), 0.0), axis=0, keepdims=True) + before
        ends_ref[0:1, k : k + LANE] = jnp.where(lane[0:1] + k < docs, sums, 1e9)
        before = before + jnp.sum(line, axis=1, keepdims=True)


def in_kernel(pieces, tiles, place_ref, lengths_ref, hid_ref, live_ref, np_ref, *refs):
    piece_refs = refs[:pieces]
    edges = tiles[0] == 0
    outs = refs[-(11 if edges else 9) :]
    mov_ref, slope_ref, xhat_ref, rstd_ref, mask_ref = outs[:5]
    w_ref, pre_ref, ends_ref, sem = outs[-4:]
    step = pl.program_id(0)
    tile = hid_ref.shape[0]

    @pl.when(step == 0)
    def _():
        copies = piece_copies(piece_refs, w_ref, place_ref[0], sem)
        for copy in copies:
            copy.start()
        running_ends(ends_ref, lengths_ref)
        for copy in copies:
            copy.wait()

    for half in halves_of(tile):
        pre_ref[half, :] = lax.dot_general(
            hid_ref[half, :], w_ref[...], NN, preferred_element_type=F32
        )

    at_tile = tiles[0] + step * tiles[1]
    first = place_ref[1] + at_tile * tile
    ends = ends_ref[0:1, :]
    lanes = lax.broadcasted_iota(jnp.int32, (LANE, LANE), 1)
    offsets = ((lanes - MID) * DILATION_STEP).astype(F32)
    for k in range(tile // LANE):
        at = (first + k * LANE + lax.broadcasted_iota(jnp.int32, (LANE, 1), 0)).astype(F32)
        begin = jnp.max(jnp.where(ends <= at, ends, 0.0), axis=1, keepdims=True)
        end = jnp.min(jnp.where(ends > at, ends, 1e9), axis=1, keepdims=True)
        there = at + offsets
        same = jnp.where((there >= begin) & (there < end), 1.0, 0.0)
        live = column(live_ref[pl.ds(at_tile * (tile // LANE) + k, 1), :].astype(F32))
        mask_ref[k * LANE : (k + 1) * LANE, :] = jnp.where(lanes == MID, live, same)

    def stats(rows, _):
        mean, rstd = row_stats(pre_ref, rows)
        rstd_ref[rows, :] = jnp.broadcast_to(rstd, (CHUNK, LANE))
        return mean, rstd

    def work(rows, kept):
        mean, rstd = kept
        live = mask_ref[rows, MID : MID + 1]
        for b in lane_blocks(INNER):
            gains = slice(D + b.start, D + b.stop)
            xhat = (pre_ref[rows, b] - mean) * rstd
            hidden, slope = gelu_and_slope(xhat * np_ref[0:1, gains] + np_ref[1:2, gains])
            mov_ref[rows, b] = (hidden * live).astype(BF16)
            slope_ref[rows, b] = slope.astype(BF16)
            xhat_ref[rows, b] = xhat.astype(BF16)

    in_stages(tile, [stats, work])
    if edges:
        put_edges(place_ref, outs[5], outs[6], mov_ref, step == 0, step == 1)


def load_window(place_ref, inner, mid, outer, ext_ref, sem):
    rows, core = mid.shape[0], lax.rem(place_ref[0], 2)
    near = pl.multiple_of((1 - core) * (REACH + rows), SUB)
    far = pl.multiple_of(core * (REACH + rows), SUB)
    return [
        pltpu.make_async_copy(inner, ext_ref.at[pl.ds(near, REACH), :], sem.at[0]),
        pltpu.make_async_copy(mid, ext_ref.at[REACH : REACH + rows, :], sem.at[1]),
        pltpu.make_async_copy(outer, ext_ref.at[pl.ds(far, REACH), :], sem.at[2]),
    ]


def put_edges(place_ref, inner_ref, outer_ref, tile_ref, at_first, at_last):
    rows, core = tile_ref.shape[0], lax.rem(place_ref[0], 2)
    for at, edge, first in ((at_first, slice(0, REACH), 0), (at_last, slice(rows - REACH, rows), 1)):

        @pl.when(at & (core == first))
        def _(edge=edge):
            outer_ref[...] = tile_ref[edge, :]

        @pl.when(at & (core != first))
        def _(edge=edge):
            inner_ref[...] = tile_ref[edge, :]


def fill_taps(taps_ref, ext_ref, mask_ref, start):
    tile = taps_ref.shape[0]
    for j in range(KERNEL_TAPS):
        rows = pl.ds(pl.multiple_of(start + j * DILATION_STEP, DILATION_STEP), tile)
        picked = ext_ref[rows, :]
        if j != MID:
            picked = picked * mask_ref[:, j : j + 1].astype(BF16)
        taps_ref[:, j * INNER : (j + 1) * INNER] = picked


def conv_kernel(
    pieces, rows_of, place_ref, low_ref, mov_ref, high_ref, mask_ref, cot_ref, before_ref, np_ref, *refs
):
    piece_refs = refs[:pieces]
    hid_ref, dconv_ref, inner_ref, outer_ref, sums_ref, turned_ref = refs[pieces : pieces + 6]
    outs = refs[pieces + 6 : pieces + 10]
    ext_ref, wc_ref, wct_ref, wo_ref, wt_ref, taps_ref, pre_ref, dh_ref, xhat_ref = refs[
        pieces + 10 : pieces + 19
    ]
    dt_ref, ht_ref, gc_ref, go_ref, acc_ref, stage1_ref, stage2_ref, sem = refs[pieces + 19 :]
    step, steps = pl.program_id(0), pl.num_programs(0) - 1
    tile = taps_ref.shape[1]
    slot = lax.rem(step, 2)

    @pl.when(step == 0)
    def _():
        me = place_ref[0]
        outs = out_copies(piece_refs, wo_ref, me, sem, 3)
        rest = load_window(place_ref, low_ref, mov_ref, high_ref, ext_ref, sem)
        rest += piece_copies(piece_refs, wc_ref, me, sem, 3 + 2 * pieces)
        for copy in outs + rest:
            copy.start()
        for ref in (acc_ref, gc_ref, go_ref):
            ref[...] = jnp.zeros_like(ref)
        for copy in outs:
            copy.wait()
        for k in range(0, D, 256):
            wt_ref[k : k + 256, :] = jnp.transpose(wo_ref[:, k : k + 256])
        for copy in rest:
            copy.wait()

    def grad_conv(cols):
        def work():
            gc_ref[:, cols] += lax.dot_general(
                dt_ref[...], taps_ref[1 - slot, :, cols], NN, preferred_element_type=F32
            )

        return work

    def grad_out(cols):
        def work():
            go_ref[:, cols] += lax.dot_general(
                ht_ref[...], before_ref[:, cols], NN, preferred_element_type=F32
            )

        return work

    taps_wide = KERNEL_TAPS * INNER
    products = [grad_conv(slice(k, min(k + 768, taps_wide))) for k in range(0, taps_wide, 768)]
    products += [grad_out(slice(k, min(k + 768, D))) for k in range(0, D, 768)]

    def tile_work(products, turned):
        fill_taps(taps_ref.at[slot], ext_ref, mask_ref, step * tile)
        pre_ref[...] = lax.dot_general(
            taps_ref[slot], wc_ref[...], NN, preferred_element_type=F32
        )
        dh_ref[...] = lax.dot_general(cot_ref[...], wt_ref[...], NN, preferred_element_type=F32)
        for n in range(turned):
            tap = jnp.minimum(turned * (step - 1) + n, KERNEL_TAPS - 1)
            source = wc_ref[pl.ds(pl.multiple_of(tap * INNER, SUB), INNER), :]
            target = pl.multiple_of((KERNEL_TAPS - 1 - tap) * INNER, SUB)
            wct_ref[pl.ds(target, INNER), :] = jnp.transpose(source)

        def stats(rows, _):
            return row_stats(pre_ref, rows)

        def work(rows, kept):
            mean, rstd = kept
            sums = [0.0, 0.0]
            for b in lane_blocks(INNER):
                gains = slice(D + INNER + b.start, D + INNER + b.stop)
                gain = np_ref[0:1, gains]
                xhat = (pre_ref[rows, b] - mean) * rstd
                hidden, slope = gelu_and_slope(xhat * gain + np_ref[1:2, gains])
                hid_ref[rows, b] = hidden.astype(BF16)
                dy = dh_ref[rows, b] * slope
                add_terms(acc_ref, b, dy, xhat)
                dxhat = dy * gain
                xhat_ref[rows, b] = xhat
                dh_ref[rows, b] = dxhat
                sums = [sums[0] + dxhat, sums[1] + dxhat * xhat]
            return row_means(sums, INNER) + [rstd]

        def finish(rows, means):
            def put(b, value):
                dconv_ref[rows, b] = value.astype(BF16)

            norm_back(rows, dh_ref, xhat_ref, means, put)

        in_stages(tile, [stats, work, finish], products)
        dt_ref[...] = jnp.transpose(dconv_ref[...])
        ht_ref[...] = jnp.transpose(hid_ref[...])

    @pl.when(step == 0)
    def _():
        tile_work([], 0)

    @pl.when((step > 0) & (step < steps))
    def _():
        tile_work(products, TURNED)

    put_edges(place_ref, inner_ref, outer_ref, dconv_ref, step == 0, step == steps - 1)

    @pl.when(step == steps)
    def _():
        copy = pltpu.make_async_copy(wct_ref, turned_ref, sem.at[4])
        copy.start()
        for work in products:
            work()
        core = lax.rem(place_ref[0], 2)
        _, rows_conv, rows_out = rows_of
        stage_turned(stage1_ref, core, gc_ref, rows_conv, 0, slice(0, CUT // LANE))
        first_tiles = rows_conv // SUB * (CUT // LANE)
        stage_plain(stage1_ref, core, go_ref, rows_out, first_tiles, slice(0, OUT_CUT // LANE))
        copies = stage_copies(stage1_ref, outs[0], outs[1], spans(CHUNKS[0], rows_of)[1], sem, 0)
        for each in copies:
            each.start()
        stage_turned(stage2_ref, core, gc_ref, rows_conv, 0, slice(CUT // LANE, INNER // LANE))
        second_tiles = rows_conv // SUB * ((INNER - CUT) // LANE)
        rest = slice(OUT_CUT // LANE, D // LANE)
        stage_plain(stage2_ref, core, go_ref, rows_out, second_tiles, rest)
        more = stage_copies(stage2_ref, outs[2], outs[3], spans(CHUNKS[1], rows_of)[1], sem, 2)
        for each in more:
            each.start()
        for each in copies + more + [copy]:
            each.wait()
        sums_ref[0:1, :] = jnp.sum(acc_ref[0:8, :], axis=0, keepdims=True)
        sums_ref[1:2, :] = jnp.sum(acc_ref[8:16, :], axis=0, keepdims=True)


def stage_tiles(stage_ref, core, first_row, rows_each, base, block0, blocks, value):
    for g in range(value.shape[0] // SUB):
        row = first_row + g * SUB
        owner, inside = row // rows_each, row % rows_each // SUB
        side = core ^ (owner % 2)
        for b in range(value.shape[1] // LANE):
            tile = value[g * SUB : (g + 1) * SUB, b * LANE : (b + 1) * LANE]
            at = base + inside * blocks + block0 + b
            stage_ref[side, owner // 2, at] = tile.astype(BF16)


def stage_plain(stage_ref, core, grad_ref, rows_each, base, blocks):
    lanes = slice(blocks.start * LANE, blocks.stop * LANE)
    for row in range(0, grad_ref.shape[0], SUB):
        part = grad_ref[row : row + SUB, lanes]
        stage_tiles(stage_ref, core, row, rows_each, base, 0, blocks.stop - blocks.start, part)


def stage_turned(stage_ref, core, turned_ref, rows_each, base, blocks):
    count = blocks.stop - blocks.start
    for row in range(0, turned_ref.shape[1], LANE):
        for b in range(count):
            at = (blocks.start + b) * LANE
            part = jnp.transpose(turned_ref[at : at + LANE, row : row + LANE].astype(BF16))
            stage_tiles(stage_ref, core, row, rows_each, base, b, count, part)


def stage_copies(stage_ref, keep_ref, send_ref, used, sem, first):
    count = stage_ref.shape[2]
    if used < count:
        dims = stage_ref.shape[:2] + (count - used, SUB, LANE)
        stage_ref[:, :, used:] = jnp.zeros(dims, BF16)
    return [
        pltpu.make_async_copy(stage_ref.at[n], ref, sem.at[first + n])
        for n, ref in enumerate((keep_ref, send_ref))
    ]


def back_conv_kernel(
    last, rows_in, place_ref, low_ref, d_ref, high_ref, turned_ref, mask_ref, xhat_ref, rstd_ref, slope_ref, hid_ref, np_ref, *refs
):
    if last:
        before_ref, dpre_ref, sums_ref, keep_ref, send_ref, stage_ref = refs[:6]
    else:
        dpre_ref, sums_ref, part_ref = refs[:3]
    ext_ref, wt_ref, taps_ref, dmov_ref, grad_ref, acc_ref, sem = refs[-7:]
    step, steps = pl.program_id(0), pl.num_programs(0)
    tile = taps_ref.shape[0]
    open_sums(acc_ref)

    @pl.when(step == 0)
    def _():
        copies = load_window(place_ref, low_ref, d_ref, high_ref, ext_ref, sem)
        copies.append(pltpu.make_async_copy(turned_ref, wt_ref, sem.at[3]))
        if last:
            copies.append(pltpu.make_async_copy(before_ref, grad_ref, sem.at[4]))
        for copy in copies:
            copy.start()
        if not last:
            grad_ref[...] = jnp.zeros_like(grad_ref)
        for copy in copies:
            copy.wait()

    fill_taps(taps_ref, ext_ref, mask_ref, (steps * last + step) * tile)
    for half in halves_of(tile):
        dmov_ref[half, :] = lax.dot_general(
            taps_ref[half, :], wt_ref[...], NN, preferred_element_type=F32
        )

    def work(rows, _):
        live = mask_ref[rows, MID : MID + 1]
        sums = [0.0, 0.0]
        for b in lane_blocks(INNER):
            xhat = xhat_ref[rows, b].astype(F32)
            dy = dmov_ref[rows, b] * live * slope_ref[rows, b].astype(F32)
            add_terms(acc_ref, b, dy, xhat)
            dxhat = dy * np_ref[0:1, D + b.start : D + b.stop]
            dmov_ref[rows, b] = dxhat
            sums = [sums[0] + dxhat, sums[1] + dxhat * xhat]
        return row_means(sums, INNER) + [rstd_ref[rows, :]]

    def finish(rows, means):
        def put(b, value):
            dpre_ref[rows, b] = value.astype(BF16)

        norm_back(rows, dmov_ref, xhat_ref, means, put)

    in_stages(tile, [work, finish])
    close_sums(sums_ref, acc_ref)
    grad_ref[...] += lax.dot_general(dpre_ref[...], hid_ref[...], TN, preferred_element_type=F32)

    @pl.when(step == steps - 1)
    def _():
        if last:
            all_blocks = slice(0, INNER // LANE)
            stage_turned(stage_ref, lax.rem(place_ref[0], 2), grad_ref, rows_in, 0, all_blocks)
            used = rows_in // SUB * (INNER // LANE)
            run_copies(stage_copies(stage_ref, keep_ref, send_ref, used, sem, 0))
        else:
            run_copies([pltpu.make_async_copy(grad_ref, part_ref, sem.at[0])])


def back_a_kernel(pieces, half, place_ref, dpre0_ref, dpre1_ref, xhat_ref, rstd_ref, slope_ref, cot_ref, np_ref, *refs):
    piece_refs = refs[:pieces]
    grad_ref, sums_ref, w_ref, wt_ref, dh_ref, acc_ref, sem = refs[-7:]
    open_sums(acc_ref)

    @pl.when(pl.program_id(0) == 0)
    def _():
        run_copies(piece_copies(piece_refs, w_ref, place_ref[0], sem))
        for k in range(0, D, 256):
            wt_ref[:, k : k + 256] = jnp.transpose(w_ref[k : k + 256, :])

    second = (jnp.zeros((1, 1), jnp.int32) + pl.program_id(0)) >= half
    d_pre = jnp.where(second, dpre1_ref[...], dpre0_ref[...])
    dh_ref[...] = lax.dot_general(d_pre, wt_ref[...], NN, preferred_element_type=F32)

    def work(rows, _):
        sums = [0.0, 0.0]
        for b in lane_blocks(D):
            xhat = xhat_ref[rows, b].astype(F32)
            dy = dh_ref[rows, b] * slope_ref[rows, b].astype(F32)
            add_terms(acc_ref, b, dy, xhat)
            dxhat = dy * np_ref[0:1, b]
            dh_ref[rows, b] = dxhat
            sums = [sums[0] + dxhat, sums[1] + dxhat * xhat]
        return row_means(sums, D) + [rstd_ref[rows, :]]

    def finish(rows, means):
        def put(b, value):
            grad_ref[rows, b] = cot_ref[rows, b].astype(F32) + value

        norm_back(rows, dh_ref, xhat_ref, means, put)

    in_stages(dpre0_ref.shape[0], [work, finish])
    close_sums(sums_ref, acc_ref)


def out_kernel(pieces, place_ref, hid_ref, tok_ref, *refs):
    piece_refs = refs[:pieces]
    out_ref, w_ref, sem = refs[pieces:]

    @pl.when(pl.program_id(0) == 0)
    def _():
        run_copies(out_copies(piece_refs, w_ref, place_ref[0], sem))

    branch = lax.dot_general(hid_ref[...], w_ref[...], NN, preferred_element_type=F32)
    out_ref[...] = (tok_ref[...].astype(F32) + branch).astype(BF16)


WIDTHS = (INNER, INNER, D)
LANE0 = (0, INNER, 2 * INNER)
CUT = 2 * LANE
OUT_CUT = 8 * LANE
CHUNKS = (
    ((1, 0, CUT), (2, 0, OUT_CUT)),
    ((1, CUT, INNER - CUT), (2, OUT_CUT, D - OUT_CUT)),
    ((0, 0, INNER),),
)


def spans(chunk, rows):
    found, first = [], 0
    for weight, col, cols in chunk:
        tiles = rows[weight] // SUB * (cols // LANE)
        found.append((weight, col // LANE, cols // LANE, first, tiles))
        first += tiles
    return found, first


def column_sums(pack_ref, row, ref, chunk, rows):
    for weight, block0, blocks, first, tiles in spans(chunk, rows)[0]:

        def body(g, carry, first=first, blocks=blocks):
            new = []
            for b in range(blocks):
                value = ref[first + g * blocks + b].astype(F32)
                new.append(carry[b] + fold(value * value + 1e-30))
            return tuple(new)

        zero = tuple(jnp.zeros((8, LANE), F32) for _ in range(blocks))
        cols = lax.fori_loop(0, tiles // blocks, body, zero, unroll=5)
        for b in range(blocks):
            lane = LANE0[weight] + (block0 + b) * LANE
            pack_ref[row : row + 1, lane : lane + LANE] = jnp.sum(cols[b], axis=0, keepdims=True)


def load_full(refs, place_ref, first, full_ref, sem, at):
    pieces = refs[0].shape[0]
    each = full_ref.shape[0] // (len(refs) * pieces)
    outer = pieces if len(refs) == 2 else pieces // 2
    y = place_ref[2] % 2
    copies = []
    for n, (ref, side) in enumerate(zip(refs, (y, 1 - y))):
        for p in range(pieces):
            index = side * outer + p if len(refs) == 2 else p % 2 * outer + p // 2
            target = full_ref.at[pl.ds(index * each, each)]
            source = ref.at[p, first : first + each]
            copies.append(pltpu.make_async_copy(source, target, sem.at[at + n * pieces + p]))
    return copies


def load_halves(mine_ref, other_ref, place_ref, full_ref, sem):
    y, each = lax.rem(place_ref[2], 2), mine_ref.shape[0]
    return [
        pltpu.make_async_copy(ref, full_ref.at[pl.ds(side * each, each)], sem.at[n])
        for n, (ref, side) in enumerate(((mine_ref, y), (other_ref, 1 - y)))
    ]


PACK_BLOCKS = (D + 2 * INNER) // LANE


def pack_line(pack_ref, row, lane0, width):
    parts = []
    for lane in range(lane0, lane0 + width, LANE):
        at = row * PACK_BLOCKS + lane // LANE
        parts.append(pack_ref[at // SUB, at % SUB : at % SUB + 1, :])
    return jnp.concatenate(parts, axis=1)


def pack_kernel(rows, pieces, place_ref, part_ref, *refs):
    states, sums, (pack_ref, acc_ref) = refs[0:3], refs[3:7], refs[7:9]
    pack_ref[...] = jnp.zeros_like(pack_ref)

    def add(row, lane, value):
        at = row * PACK_BLOCKS + lane // LANE
        pack_ref[at // SUB, at % SUB : at % SUB + 1, :] += value

    lanes_of = ((0, D), (D, D + INNER), (D, D + INNER), (D + INNER, D + 2 * INNER))
    for part, (lane0, lane1) in zip(sums, lanes_of):
        for lane in range(lane0, lane1, LANE):
            for row in range(2):
                add(row, lane, part[row : row + 1, lane - lane0 : lane - lane0 + LANE])
    lanes = lax.broadcasted_iota(jnp.int32, (1, LANE), 1)
    for k in range(3):
        total = jnp.sum(states[k][...].reshape(1, -1), axis=1, keepdims=True)
        add(3, 0, jnp.where(lanes == k, total, 0.0))
    acc_ref[...] = jnp.zeros_like(acc_ref)
    spare = acc_ref.shape[0] - 1
    outer = place_ref[3] // 2
    piece = place_ref[2] % 2 * outer + place_ref[2] // 2
    at = 0
    for chunk, each in zip(CHUNKS[:2], pieces):
        found, _ = spans(chunk, rows)
        start = piece * each

        def body(k, carry, found=found, start=start, at=at):
            n = start + k
            slot = spare
            for weight, block0, blocks, first, tiles in found:
                here = LANE0[weight] // LANE + block0 + lax.rem(jnp.maximum(n - first, 0), blocks)
                slot = jnp.where((n >= first) & (n < first + tiles), here, slot)
            value = part_ref[at + k].astype(F32)
            acc_ref[slot] += value * value + 1e-30
            return carry

        lax.fori_loop(0, each, body, 0, unroll=2)
        at += each
    for slot in range(spare):
        add(2, slot * LANE, jnp.sum(acc_ref[slot], axis=0, keepdims=True))


def pack_in_kernel(rows, place_ref, mine_ref, other_ref, pack_ref, full_ref, sem):
    run_copies(load_halves(mine_ref, other_ref, place_ref, full_ref, sem))
    pack_ref[...] = jnp.zeros_like(pack_ref)
    column_sums(pack_ref, 0, full_ref, CHUNKS[2], rows)


def update_weight(
    k, squares, states_sum, source, weight, state, col_state, grad_ref, new, row_new_ref, col_new_ref, scratch, step=0, steps=1
):
    line_ref, state_ref, new_ref, scaled_ref = scratch
    width, fan, rows_here = WIDTHS[k], (D, KERNEL_TAPS * INNER, INNER)[k], state.shape[0]
    whole_rows = rows_here + -rows_here % LANE
    groups = rows_here // SUB // steps
    rate = 0.5 / fan**0.5

    def before():
        col_new = DECAY * col_state[...].reshape(1, -1) + (1.0 - DECAY) * (squares * (1.0 / fan))
        col_new_ref[...] = col_new.reshape(-1)
        total = DECAY * states_sum
        total = total + (1.0 - DECAY) * (1.0 / width) * jnp.sum(squares, axis=1, keepdims=True)
        scaled_ref[0:1, 0:width] = col_new / (total * (1.0 / fan))
        line_ref[0:1, 0:rows_here] = state[...].reshape(1, -1)
        for c in range(0, whole_rows, LANE):
            state_ref[c : c + LANE, :] = column(line_ref[0:1, c : c + LANE])

    def after():
        for c in range(0, whole_rows, LANE):
            line_ref[0:1, c : c + LANE] = jnp.transpose(new_ref[c : c + LANE, :])[0:1, :]
        row_new_ref[...] = line_ref[0:1, 0:rows_here].reshape(-1)

    def body(g, carry):
        here = pl.ds(pl.multiple_of(g * SUB, SUB), SUB)
        at = step * groups + g
        rows = pl.ds(pl.multiple_of(at * SUB, SUB), SUB)
        square = 0.0
        for ref, block0, blocks, first in source:
            for b in range(blocks):
                value = ref[first + at * blocks + b].astype(F32)
                grad_ref[here, (block0 + b) * LANE : (block0 + b + 1) * LANE] = value
                square = square + (value * value + 1e-30)
        mean = jnp.sum(square, axis=1, keepdims=True) * (1.0 / width)
        row_new = DECAY * state_ref[rows, :] + (1.0 - DECAY) * mean
        new_ref[rows, :] = row_new
        for ref, block0, blocks, first in source:
            for b in range(blocks):
                lanes = slice((block0 + b) * LANE, (block0 + b + 1) * LANE)
                value = ref[first + at * blocks + b].astype(F32)
                change = value * lax.rsqrt(row_new * scaled_ref[0:1, lanes])
                new[here, lanes] = weight[here, lanes] - rate * change
        return carry

    if steps == 1:
        before()
        lax.fori_loop(0, groups, body, 0, unroll=5)
        after()
    else:
        pl.when(step == 0)(before)
        lax.fori_loop(0, groups, body, 0, unroll=5)
        pl.when(step == steps - 1)(after)


def sources_of(chunk, ref, rows):
    return {w: (ref, block0, blocks, first) for w, block0, blocks, first, _ in spans(chunk, rows)[0]}


def update_kernel(rows, copies_of, place_ref, mine_ref, other_ref, pack_ref, *refs):
    weights, states, col_states = refs[0:2], refs[2:4], refs[4:6]
    grads, news, rows_new, cols_new = refs[6:8], refs[8:10], refs[10:12], refs[12:14]
    conv_scratch, out_scratch = refs[14:18], refs[18:22]
    full1_ref, full2_ref, sem = refs[22:25]
    both = (mine_ref, other_ref)
    count = 2 * mine_ref.shape[0]
    step, steps = pl.program_id(0), pl.num_programs(0)

    @pl.when(step == 0)
    def _():
        copies = load_full(both, place_ref, 0, full1_ref, sem, 0)
        copies += load_full(both, place_ref, full1_ref.shape[0] // count, full2_ref, sem, count)
        run_copies(copies)

    from1 = sources_of(CHUNKS[0], full1_ref, rows)
    from2 = sources_of(CHUNKS[1], full2_ref, rows)

    def update(n, k, source, scratch, *steps):
        squares = pack_line(pack_ref, 2, LANE0[k], WIDTHS[k])
        update_weight(
            k, squares, pack_line(pack_ref, 3, 0, LANE)[:, k : k + 1] * (1.0 / copies_of), source, weights[n],
            states[n], col_states[n], grads[n], news[n], rows_new[n], cols_new[n], scratch, *steps,
        )

    update(0, 1, [from1[1], from2[1]], conv_scratch, step, UPDATE_STEPS)

    @pl.when(step == steps - 1)
    def _():
        update(1, 2, [from1[2], from2[2]], out_scratch)


def update_in_kernel(
    rows, copies_of, place_ref, mine_ref, other_ref, pack_in_ref, pack_ref, np_ref, second_ref, *refs
):
    weight, state, col_state, grad_ref, new_ref, row_new_ref, col_new_ref = refs[0:7]
    ngrad_ref, nsecond_ref, nnew_ref = refs[7:10]
    full_ref, sem = refs[14:16]
    copies = load_halves(mine_ref, other_ref, place_ref, full_ref, sem)
    for copy in copies:
        copy.start()
    lines = [pack_line(pack_ref, row, 0, D + 2 * INNER) for row in range(2)]
    grad = jnp.concatenate(lines, axis=0)
    second = DECAY * second_ref[...] + (1.0 - DECAY) * (grad * grad + 1e-30)
    ngrad_ref[...] = grad
    nsecond_ref[...] = second
    nnew_ref[...] = np_ref[...] - 0.2 * grad * lax.rsqrt(second)
    for copy in copies:
        copy.wait()
    update_weight(
        0, pack_in_ref[0:1, :], pack_line(pack_ref, 3, 0, LANE)[:, 0:1] * (1.0 / copies_of),
        [sources_of(CHUNKS[2], full_ref, rows)[0]], weight, state, col_state, grad_ref, new_ref,
        row_new_ref, col_new_ref, refs[10:14],
    )


class Places:
    def __init__(self):
        self.seq, self.fsdp = lax.axis_size("seq"), lax.axis_size("fsdp")
        self.q = lax.axis_index("fsdp")
        self.s = lax.axis_index("seq")

    def flip(self, x, axis, bit):
        pairs = []
        for s in range(self.seq):
            for f in range(self.fsdp):
                s2, f2 = (s ^ bit, f) if axis == "seq" else (s, f ^ bit)
                pairs.append((s * self.fsdp + f, s2 * self.fsdp + f2))
        return lax.ppermute(x, AXES, pairs)


def bits_of(count):
    return [1 << k for k in range(count.bit_length() - 1)]


def tie(x, *others):
    return lax.optimization_barrier((x, *others))[0]


def gather_pieces(piece, place, after, later=()):
    found = {0: piece}
    for bit in reversed(bits_of(place.fsdp)):
        for k in list(found):
            moving = found[k]
            if bit == 1:
                moving = tie(moving, *((after,) if k == 0 or not later else later))
            found[k | bit] = place.flip(moving, "fsdp", bit)
    return [found[k] for k in range(place.fsdp)]


def sum_over(x, place, *axes):
    for axis in axes:
        for bit in bits_of(getattr(place, axis)):
            x = x + place.flip(x, axis, bit)
    return x


def sum_at_once(x, place, axis, bits):
    terms = [x] + [place.flip(x, axis, bits * k) for k in range(1, getattr(place, axis) // bits)]
    while len(terms) > 1:
        terms = [a + b for a, b in zip(terms[::2], terms[1::2])]
    return terms[0]


def pick(x, index, axis):
    return lax.dynamic_index_in_dim(x, index, axis=axis, keepdims=False)


class Reduction:
    def __init__(self, place, keep, send):
        self.place, self.near = place, keep
        self.got = place.flip(send, "fsdp", 1)

    def halve(self, axis, side, flip_axis, bit):
        dims = self.near.shape
        parts = dims[:axis] + (2, dims[axis] // 2) + dims[axis + 1 :]
        near, got = self.near.reshape(parts), self.got.reshape(parts)
        away = pick(near, 1 - side, axis).astype(F32) + pick(got, 1 - side, axis).astype(F32)
        self.near = pick(near, side, axis).astype(F32) + pick(got, side, axis).astype(F32)
        away = away.astype(BF16)
        self.got = self.place.flip(away, flip_axis, bit)
        return away

    def x(self):
        bit = self.place.fsdp // 2
        while bit > 1:
            away = self.halve(0, (self.place.q // bit) % 2, "fsdp", bit)
            bit //= 2
        return away

    def y(self):
        return self.halve(1, self.place.s % 2, "seq", 1)

    def whole_half(self):
        self.near = self.rounded(self.near + self.got.astype(F32))

    def rounded(self, total):
        return lax.optimization_barrier(total.astype(BF16))

    def send_half(self, bit):
        self.got = self.place.flip(self.near, "seq", bit)

    def add_half(self):
        self.near = self.rounded(self.near.astype(F32) + self.got.astype(F32))

    def pieces(self):
        total = (self.near + self.got.astype(F32)).astype(BF16)
        return total.reshape((self.place.seq // 2, -1) + total.shape[2:])


def arrive(result, *reductions):
    result, *gots = lax.optimization_barrier((result, *[r.got for r in reductions]))
    for reduction, got in zip(reductions, gots):
        reduction.got = got
    return result


def summed_f32(got):
    return jnp.sum(got.astype(F32), axis=0)


def summed(got):
    return summed_f32(got).astype(BF16)


def exchange(place, sent):
    line = [[y + 2 * z for z in range(place.seq // 2)] for y in range(2)]
    return lax.all_to_all(sent, "seq", 0, 0, axis_index_groups=line)


def on_device(
    tokens, input_mask, doc_lengths, cotangent, w_in, w_conv, w_out, norm_params,
    row_in, col_in, row_conv, col_conv, row_out, col_out, norm_second,
):
    place = Places()
    rows = tokens.shape[0]
    pieces = place.fsdp
    spots = jnp.stack(
        [place.q, (place.s * place.fsdp + place.q) * rows, place.s, place.seq]
    ).astype(jnp.int32)
    docs = doc_lengths.shape[0]
    live = input_mask.reshape(-1, LANE)
    weights = (w_in, w_conv, w_out)
    rows_of = [w.shape[0] for w in weights]

    tile_a, tile = 256, 512
    steps = rows // tile
    params_spec = whole(2, D + 2 * INNER)
    dma = pltpu.SemaphoreType.DMA

    out_sides = (w_out[:, : D // 2], w_out[:, D // 2 :])
    conv_out = jnp.concatenate([w_conv, *out_sides], axis=0).astype(BF16)
    hidden_a, slope_a, xhat_a, rstd_a = call(
        norm_a_kernel,
        (rows // tile_a,),
        [rows_spec(tile_a, D), params_spec],
        [rows_spec(tile_a, D)] * 3 + [rows_spec(tile_a, LANE)],
        [shape((rows, D), BF16)] * 3 + [shape((rows, LANE), F32)],
        us=17,
    )(tokens, tie(norm_params, conv_out))

    in_pieces = gather_pieces(w_in.astype(BF16), place, hidden_a)

    def in_call(tiles, count, before):
        at, stride = tiles

        def here_spec(width):
            return pl.BlockSpec((tile, width), lambda i: (at + stride * i, 0))

        out_shapes = [shape((rows, INNER), BF16)] * 3 + [shape((rows, LANE), F32)] * 2
        out_specs = [here_spec(INNER)] * 3 + [here_spec(LANE)] * 2
        if at == 0:
            out_shapes += [shape((REACH, INNER), BF16)] * 2
            out_specs += [whole(REACH, INNER)] * 2
        return call(
            functools.partial(in_kernel, pieces, tiles),
            (count,),
            [SMEM, whole(docs), here_spec(D), whole(*live.shape), params_spec]
            + [ANY] * (pieces + len(before)),
            out_specs,
            out_shapes,
            [pltpu.VMEM((D, INNER), BF16), pltpu.VMEM((tile, INNER), F32)]
            + [pltpu.VMEM((8, docs + -docs % LANE), F32), dma((pieces,))],
            us=3,
            aliases={5 + pieces + k: k for k in range(len(before))},
        )(spots, doc_lengths, hidden_a, live, norm_params, *in_pieces, *before)

    *kept, m_first, m_last = in_call((0, steps - 1), 2, ())
    moved, slope_b, xhat_b, rstd_b, masks = in_call((1, 1), steps - 2, kept)

    def halo(inner, outer):
        total = place.seq * place.fsdp
        across = [(i, i + 1 if i % 2 else i - 1) for i in range(1, total - 1)]
        return place.flip(inner, "fsdp", 1), lax.ppermute(outer, AXES, across)

    m_inner, m_outer = halo(m_first, m_last)
    conv_pieces = gather_pieces(conv_out, place, m_first, (moved, m_inner, m_outer))

    ext = pltpu.VMEM((rows + 2 * REACH, INNER), BF16)
    taps_wide = KERNEL_TAPS * INNER
    wide = pltpu.VMEM((taps_wide, INNER), BF16)
    shards = place.fsdp // 2

    def half_dims(chunk):
        count = spans(chunk, rows_of)[1]
        return (shards, count + -count % place.seq, SUB, LANE)

    def tile_spec(width, ahead):
        return pl.BlockSpec((tile, width), lambda i: (jnp.clip(i + ahead, 0, steps - 1), 0))

    halves = [half_dims(CHUNKS[0])] * 2 + [half_dims(CHUNKS[1])] * 2
    work = pltpu.VMEM((tile, INNER), F32)
    turned_tile = pltpu.VMEM((INNER, tile), BF16)
    hidden_c, d_conv, d_first, d_last, sums_c, turned, keep1, send1, keep2, send2 = call(
        functools.partial(conv_kernel, pieces, rows_of),
        (steps + 1,),
        [SMEM, ANY, ANY, ANY, tile_spec(LANE, 0), tile_spec(D, 0), tile_spec(D, -1), params_spec]
        + [ANY] * pieces,
        [tile_spec(INNER, 0)] * 2
        + [whole(REACH, INNER), whole(REACH, INNER), whole(2, INNER)]
        + [ANY] * 5,
        [
            shape((rows, INNER), BF16),
            shape((rows, INNER), BF16),
            shape((REACH, INNER), BF16),
            shape((REACH, INNER), BF16),
            shape((2, INNER), F32),
            shape((taps_wide, INNER), BF16),
        ]
        + [shape(dims, BF16) for dims in halves],
        [ext, wide, wide, pltpu.VMEM((INNER, D), BF16), pltpu.VMEM((D, INNER), BF16)]
        + [pltpu.VMEM((2, tile, taps_wide), BF16), work, work, work, turned_tile, turned_tile]
        + [pltpu.VMEM((INNER, taps_wide), F32), pltpu.VMEM((INNER, D), F32)]
        + [pltpu.VMEM((16, INNER), F32)]
        + [pltpu.VMEM((2,) + halves[0], BF16), pltpu.VMEM((2,) + halves[2], BF16)]
        + [dma((3 + 3 * pieces,))],
        us=45,
    )(
        spots, m_inner, moved, m_outer, masks, cotangent, cotangent, norm_params, *conv_pieces
    )
    d_inner, d_outer = halo(d_first, d_last)
    first, second = Reduction(place, keep1, send1), Reduction(place, keep2, send2)
    (block_out,) = call(
        functools.partial(out_kernel, pieces),
        (steps,),
        [SMEM, rows_spec(tile, INNER), rows_spec(tile, D)] + [ANY] * pieces,
        [rows_spec(tile, D)],
        [shape((rows, D), BF16)],
        [pltpu.VMEM((INNER, D), BF16), dma((2 * pieces,))],
        us=9,
    )(spots, hidden_c, tokens, *conv_pieces)

    def back_conv(last, spots, before):
        here = steps // 2
        at = here * last

        def here_spec(width):
            return pl.BlockSpec((tile, width), lambda i: (i + at, 0))

        dims = half_dims(CHUNKS[2])
        return call(
            functools.partial(back_conv_kernel, last, w_in.shape[0]),
            (here,),
            [SMEM] + [ANY] * 4
            + [here_spec(LANE), here_spec(INNER), here_spec(LANE), here_spec(INNER), here_spec(D)]
            + [params_spec]
            + [ANY] * last,
            [rows_spec(tile, INNER), whole(2, INNER)] + [ANY] * (1 + last),
            [shape((rows // 2, INNER), BF16), shape((2, INNER), F32)]
            + ([shape(dims, BF16)] * 2 if last else [shape((INNER, D), F32)]),
            ([pltpu.VMEM((2,) + dims, BF16)] if last else [])
            + [
                ext,
                wide,
                pltpu.VMEM((tile, taps_wide), BF16),
                pltpu.VMEM((tile, INNER), F32),
                pltpu.VMEM((INNER, D), F32),
                pltpu.VMEM((16, INNER), F32),
                dma((5,)),
            ],
            us=16,
        )(
            spots, d_inner, d_conv, d_outer, turned, masks, xhat_b, rstd_b, slope_b, hidden_a,
            norm_params, *before,
        )

    block_out, d_inner, d_outer = arrive((block_out, d_inner, d_outer), first, second)
    away = (first.x(), second.y())
    d_pre0, sums_b0, grad_part = back_conv(0, tie(spots, *away), ())
    d_pre0 = arrive(d_pre0, first, second)
    away = (first.y(), second.x())
    d_pre1, sums_b1, keep, send = back_conv(1, tie(spots, *away), (grad_part,))
    send = arrive(send, first, second)
    third = Reduction(place, keep, send)
    sent = jnp.concatenate([first.pieces(), second.pieces()], axis=1)
    got = exchange(place, sent)
    third.got = tie(third.got, sent)
    away = (sent, third.x())
    input_grad, sums_a = call(
        functools.partial(back_a_kernel, pieces, steps // 2),
        (steps,),
        [SMEM]
        + [
            pl.BlockSpec((tile, INNER), lambda i: (jnp.minimum(i, steps // 2 - 1), 0)),
            pl.BlockSpec((tile, INNER), lambda i: (jnp.maximum(i - steps // 2, 0), 0)),
        ]
        + [rows_spec(tile, D), rows_spec(tile, LANE), rows_spec(tile, D), rows_spec(tile, D)]
        + [params_spec]
        + [ANY] * pieces,
        [rows_spec(tile, D), whole(2, D)],
        [shape((rows, D), F32), shape((2, D), F32)],
        [
            pltpu.VMEM((D, INNER), BF16),
            pltpu.VMEM((INNER, D), BF16),
            pltpu.VMEM((tile, D), F32),
            pltpu.VMEM((16, D), F32),
            dma((pieces,)),
        ],
        us=17,
    )(
        tie(spots, *away), d_pre0, d_pre1, xhat_a, rstd_a, slope_a, cotangent, norm_params, *in_pieces
    )

    row_states, col_states = (row_in, row_conv, row_out), (col_in, col_conv, col_out)
    row_specs = [whole(*r.shape) for r in row_states]
    col_specs = [whole(*c.shape) for c in col_states]
    cols_all = D + 2 * INNER
    pack_dims = (4 * PACK_BLOCKS // SUB, SUB, LANE)
    pack_spec = whole(*pack_dims)
    fulls = [pltpu.VMEM(half_dims(c)[1:], BF16) for c in CHUNKS]
    sums = (sums_a, sums_b0, sums_b1, sums_c)
    got, third.got, input_grad = lax.optimization_barrier((got, third.got, input_grad))
    part = summed(got)
    sent = jnp.broadcast_to(part[None], (place.seq // 2,) + part.shape)
    mine = exchange(place, sent)
    third.got = tie(third.got, sent)
    away = third.y()
    (pack,) = call(
        functools.partial(pack_kernel, rows_of, [half_dims(c)[1] // place.seq for c in CHUNKS]),
        (1,),
        [SMEM, whole(*part.shape)] + row_specs + [whole(*x.shape) for x in sums],
        [pack_spec],
        [shape(pack_dims, F32)],
        [pltpu.VMEM((cols_all // LANE + 1, SUB, LANE), F32)],
        us=2,
        mib=16,
    )(tie(spots, away), part, *row_states, *sums)
    pack = sum_over(pack, place, "fsdp")
    third.got, pack = lax.optimization_barrier((third.got, pack))
    seq_bits = bits_of(place.seq)
    third.whole_half()
    for bit in seq_bits[1:-1]:
        third.send_half(bit)
        pack = pack + place.flip(pack, "seq", 1) if bit == 2 else pack
        if bit != seq_bits[-2]:
            third.add_half()
    mine, third.got, pack = lax.optimization_barrier((mine, third.got, pack))
    other = place.flip(mine, "seq", 1)
    third.add_half()
    third.send_half(seq_bits[-1])
    pack = sum_at_once(pack, place, "seq", 2)
    third.got, other, pack = lax.optimization_barrier((third.got, other, pack))
    third.add_half()
    line = third.near.reshape(third.near.shape[1:])
    line_other = place.flip(line, "seq", 1)

    def update_scratch(weight):
        lines = weight.shape[0] + -weight.shape[0] % LANE
        return (
            [pltpu.VMEM((8, lines), F32)]
            + [pltpu.VMEM((lines, LANE), F32)] * 2
            + [pltpu.VMEM((8, weight.shape[1]), F32)]
        )

    weight_specs = [whole(*w.shape) for w in weights]
    conv_block = pl.BlockSpec((w_conv.shape[0] // UPDATE_STEPS, INNER), lambda i: (i, 0))
    both_specs = [conv_block, weight_specs[2]]
    results = call(
        functools.partial(update_kernel, rows_of, place.seq),
        (UPDATE_STEPS,),
        [SMEM, ANY, ANY, pack_spec] + both_specs + row_specs[1:] + col_specs[1:],
        both_specs * 2 + row_specs[1:] + col_specs[1:],
        [shape(w.shape, F32) for w in weights[1:]] * 2
        + [shape(r.shape, F32) for r in row_states[1:] + col_states[1:]],
        update_scratch(w_conv)
        + update_scratch(w_out)
        + fulls[:2]
        + [dma((2 * place.seq,))],
        us=8,
        mib=32,
    )(spots, mine, other, pack, *weights[1:], *row_states[1:], *col_states[1:])
    grad_conv, grad_out, new_conv, new_out, row_conv_new, row_out_new, col_conv_new, col_out_new = (
        results
    )
    line_other, grad_out = lax.optimization_barrier((line_other, grad_out))
    (pack_in,) = call(
        functools.partial(pack_in_kernel, rows_of),
        (1,),
        [SMEM, ANY, ANY],
        [whole(8, INNER)],
        [shape((8, INNER), F32)],
        [fulls[2], dma((place.seq,))],
        us=2,
        mib=16,
    )(spots, line, line_other)
    pack_in = sum_at_once(pack_in, place, "fsdp", 1)
    grad_in, new_in, row_in_new, col_in_new, *norm_results = call(
        functools.partial(update_in_kernel, rows_of, place.seq),
        (1,),
        [SMEM, ANY, ANY, whole(8, INNER), pack_spec, params_spec, params_spec]
        + [weight_specs[0], row_specs[0], col_specs[0]],
        [weight_specs[0]] * 2 + [row_specs[0], col_specs[0]] + [params_spec] * 3,
        [shape(w_in.shape, F32)] * 2
        + [shape(row_in.shape, F32), shape(col_in.shape, F32)]
        + [shape((2, cols_all), F32)] * 3,
        update_scratch(w_in) + [fulls[2], dma((place.seq,))],
        us=4,
        mib=24,
    )(
        spots, line, line_other, pack_in, pack, norm_params, norm_second, w_in, row_in, col_in
    )
    return (
        block_out,
        input_grad,
        grad_in,
        grad_conv,
        grad_out,
        new_in,
        new_conv,
        new_out,
        row_in_new,
        col_in_new,
        row_conv_new,
        col_conv_new,
        row_out_new,
        col_out_new,
        *norm_results,
    )


def solution(mesh):
    both, rows = P(AXES, None), P("fsdp", None)
    in_specs = (
        both, P(AXES), P(), both, rows, rows, rows, P(),
        P("fsdp"), P(), P("fsdp"), P(), P("fsdp"), P(), P(),
    )
    out_specs = (
        both, both, rows, rows, rows, rows, rows, rows,
        P("fsdp"), P(), P("fsdp"), P(), P("fsdp"), P(), P(), P(), P(),
    )
    return jax.shard_map(
        on_device, mesh=mesh, in_specs=in_specs, out_specs=out_specs, check_vma=False
    )
```

```python
import functools
import math

import jax
import jax.numpy as jnp
from jax import lax
from jax.experimental import pallas as pl
from jax.experimental.pallas import tpu as pltpu
from jax.sharding import PartitionSpec as P

D = 1280
INNER = 640
KERNEL_TAPS = 5
DILATION_STEP = 128
STEP = 10
EPSILON = 1e-05
DECAY = 1.0 - STEP ** (-0.8)

REACH = (KERNEL_TAPS - 1) // 2 * DILATION_STEP
MID = (KERNEL_TAPS - 1) // 2
F32 = jnp.float32
BF16 = jnp.bfloat16
SUB, LANE = 16, 128
AXES = ("seq", "fsdp")
NT = (((1,), (1,)), ((), ()))
TN = (((0,), (0,)), ((), ()))
NN = (((1,), (0,)), ((), ()))


def call(kernel, grid, in_specs, out_specs, out_shape, scratch=(), us=1.0, aliases=None, mib=58):
    params = pltpu.CompilerParams(
        vmem_limit_bytes=mib * 1024 * 1024, dimension_semantics=("arbitrary",) * len(grid)
    )
    return pl.pallas_call(
        kernel,
        grid=grid,
        in_specs=in_specs,
        out_specs=out_specs,
        out_shape=out_shape,
        scratch_shapes=list(scratch),
        compiler_params=params,
        input_output_aliases=aliases or {},
        cost_estimate=pl.CostEstimate(
                flops=int(us * 1.1e9), bytes_accessed=int(us * 3.4e6), transcendentals=0
        ),
    )


def shape(dims, dtype):
    return jax.ShapeDtypeStruct(dims, dtype)


def rows_spec(tile, width):
    return pl.BlockSpec((tile, width), lambda i: (i, 0))


def whole(*dims):
    return pl.BlockSpec(dims, lambda *_: (0,) * len(dims))


ANY = pl.BlockSpec(memory_space=pl.ANY)
SMEM = pl.BlockSpec(memory_space=pltpu.SMEM)


ERFC_P = 0.47 / math.sqrt(2.0)
ERFC_C = (
    0.12357219400743558,
    0.1999878668208835,
    -0.08033356004356296,
    0.3660253986657854,
    -0.1092519747040215,
)
LOG2E = 1.4426950408889634


def gelu_and_slope(y):
    t = pltpu.reciprocal(1.0 + ERFC_P * jnp.abs(y), approx=True)
    bell = jnp.exp2(y * y * (-0.5 * LOG2E))
    poly = ERFC_C[4] * t + ERFC_C[3]
    for c in ERFC_C[2::-1]:
        poly = poly * t + c
    tail = poly * t * bell
    cdf = jnp.where(y > 0.0, 1.0 - tail, tail)
    return y * cdf, cdf + y * (bell * (1.0 / math.sqrt(2.0 * math.pi)))


def lane_blocks(width):
    return [slice(k, k + LANE) for k in range(0, width, LANE)]


def row_stats(ref, rows):
    width = ref.shape[-1]
    blocks = lane_blocks(width)
    total = ref[rows, blocks[0]].astype(F32)
    for b in blocks[1:]:
        total = total + ref[rows, b].astype(F32)
    mean = jnp.sum(total, axis=-1, keepdims=True) * (1.0 / width)
    square = None
    for b in blocks:
        centered = ref[rows, b].astype(F32) - mean
        square = centered * centered if square is None else square + centered * centered
    variance = jnp.sum(square, axis=-1, keepdims=True) * (1.0 / width)
    return mean, lax.rsqrt(variance + EPSILON)


def fold(values):
    total = values[0:8]
    for k in range(8, values.shape[0], 8):
        total = total + values[k : k + 8]
    return total


def in_stages(count, stages, between=()):
    chunks = [slice(k, k + CHUNK) for k in range(0, count, CHUNK)]
    kept, rounds = {}, len(chunks) + len(stages) - 1
    for t in range(rounds):
        for n, stage in enumerate(stages):
            if 0 <= t - n < len(chunks):
                kept[n, t - n] = stage(chunks[t - n], kept.get((n - 1, t - n)))
        for work in between[t * len(between) // rounds : (t + 1) * len(between) // rounds]:
            work()


def halves_of(count):
    return (slice(0, count // 2), slice(count // 2, count))


def row_means(sums, width):
    return [jnp.sum(x, axis=-1, keepdims=True) * (1.0 / width) for x in sums]


def norm_back(rows, dxhat_ref, xhat_ref, means, put):
    mean_d, mean_dx, rstd = means
    for b in lane_blocks(dxhat_ref.shape[-1]):
        xhat = xhat_ref[rows, b].astype(F32)
        put(b, (dxhat_ref[rows, b] - mean_d - xhat * mean_dx) * rstd)


def add_terms(acc_ref, b, dy, xhat):
    acc_ref[0:8, b] += fold(dy * xhat)
    acc_ref[8:16, b] += fold(dy)


def open_sums(acc_ref):
    @pl.when(pl.program_id(0) == 0)
    def _():
        acc_ref[...] = jnp.zeros_like(acc_ref)


def close_sums(out_ref, acc_ref):
    @pl.when(pl.program_id(0) == pl.num_programs(0) - 1)
    def _():
        out_ref[0:1, :] = jnp.sum(acc_ref[0:8, :], axis=0, keepdims=True)
        out_ref[1:2, :] = jnp.sum(acc_ref[8:16, :], axis=0, keepdims=True)


def run_copies(copies):
    for copy in copies:
        copy.start()
    for copy in copies:
        copy.wait()


def piece_copies(pieces, full_ref, me, sem, first=0):
    each = full_ref.shape[0] // len(pieces)
    return [
        pltpu.make_async_copy(
            piece.at[0:each, :],
            full_ref.at[pl.ds(pl.multiple_of((me ^ k) * each, SUB), each), :],
            sem.at[first + k],
        )
        for k, piece in enumerate(pieces)
    ]


def out_copies(pieces, full_ref, me, sem, first=0):
    each, width = full_ref.shape[0] // len(pieces), full_ref.shape[1] // 2
    copies = []
    for k, piece in enumerate(pieces):
        rows = pl.ds(pl.multiple_of((me ^ k) * each, SUB), each)
        for side in range(2):
            at = piece.shape[0] - (2 - side) * each
            copies.append(
                pltpu.make_async_copy(
                    piece.at[at : at + each, :],
                    full_ref.at[rows, side * width : (side + 1) * width],
                    sem.at[first + 2 * k + side],
                )
            )
    return copies


def column(row):
    return jnp.transpose(jnp.broadcast_to(row, (LANE, LANE)))


CHUNK = 64
UPDATE_STEPS = 5
TURNED = 2


def norm_a_kernel(tok_ref, np_ref, hid_ref, slope_ref, xhat_ref, rstd_ref):
    def stats(rows, _):
        mean, rstd = row_stats(tok_ref, rows)
        rstd_ref[rows, :] = jnp.broadcast_to(rstd, (CHUNK, LANE))
        return mean, rstd

    def work(rows, kept):
        mean, rstd = kept
        for b in lane_blocks(D):
            xhat = (tok_ref[rows, b].astype(F32) - mean) * rstd
            hidden, slope = gelu_and_slope(xhat * np_ref[0:1, b] + np_ref[1:2, b])
            hid_ref[rows, b] = hidden.astype(BF16)
            slope_ref[rows, b] = slope.astype(BF16)
            xhat_ref[rows, b] = xhat.astype(BF16)

    in_stages(tok_ref.shape[0], [stats, work])


def running_ends(ends_ref, lengths_ref):
    docs, width = lengths_ref.shape[0], ends_ref.shape[1]
    ends_ref[...] = jnp.zeros_like(ends_ref)
    ends_ref[0:1, 0:docs] = lengths_ref[...].reshape(1, -1).astype(F32)
    before = jnp.zeros((1, 1), F32)
    row = lax.broadcasted_iota(jnp.int32, (LANE, LANE), 0)
    lane = lax.broadcasted_iota(jnp.int32, (LANE, LANE), 1)
    for k in range(0, width, LANE):
        line = ends_ref[0:1, k : k + LANE]
        sums = jnp.sum(jnp.where(row <= lane, column(line), 0.0), axis=0, keepdims=True) + before
        ends_ref[0:1, k : k + LANE] = jnp.where(lane[0:1] + k < docs, sums, 1e9)
        before = before + jnp.sum(line, axis=1, keepdims=True)


def in_kernel(pieces, tiles, place_ref, lengths_ref, hid_ref, live_ref, np_ref, *refs):
    piece_refs = refs[:pieces]
    edges = tiles[0] == 0
    outs = refs[-(11 if edges else 9) :]
    mov_ref, slope_ref, xhat_ref, rstd_ref, mask_ref = outs[:5]
    w_ref, pre_ref, ends_ref, sem = outs[-4:]
    step = pl.program_id(0)
    tile = hid_ref.shape[0]

    @pl.when(step == 0)
    def _():
        copies = piece_copies(piece_refs, w_ref, place_ref[0], sem)
        for copy in copies:
            copy.start()
        running_ends(ends_ref, lengths_ref)
        for copy in copies:
            copy.wait()

    for half in halves_of(tile):
        pre_ref[half, :] = lax.dot_general(
            hid_ref[half, :], w_ref[...], NN, preferred_element_type=F32
        )

    at_tile = tiles[0] + step * tiles[1]
    first = place_ref[1] + at_tile * tile
    ends = ends_ref[0:1, :]
    lanes = lax.broadcasted_iota(jnp.int32, (LANE, LANE), 1)
    offsets = ((lanes - MID) * DILATION_STEP).astype(F32)
    for k in range(tile // LANE):
        at = (first + k * LANE + lax.broadcasted_iota(jnp.int32, (LANE, 1), 0)).astype(F32)
        begin = jnp.max(jnp.where(ends <= at, ends, 0.0), axis=1, keepdims=True)
        end = jnp.min(jnp.where(ends > at, ends, 1e9), axis=1, keepdims=True)
        there = at + offsets
        same = jnp.where((there >= begin) & (there < end), 1.0, 0.0)
        live = column(live_ref[pl.ds(at_tile * (tile // LANE) + k, 1), :].astype(F32))
        mask_ref[k * LANE : (k + 1) * LANE, :] = jnp.where(lanes == MID, live, same)

    def stats(rows, _):
        mean, rstd = row_stats(pre_ref, rows)
        rstd_ref[rows, :] = jnp.broadcast_to(rstd, (CHUNK, LANE))
        return mean, rstd

    def work(rows, kept):
        mean, rstd = kept
        live = mask_ref[rows, MID : MID + 1]
        for b in lane_blocks(INNER):
            gains = slice(D + b.start, D + b.stop)
            xhat = (pre_ref[rows, b] - mean) * rstd
            hidden, slope = gelu_and_slope(xhat * np_ref[0:1, gains] + np_ref[1:2, gains])
            mov_ref[rows, b] = (hidden * live).astype(BF16)
            slope_ref[rows, b] = slope.astype(BF16)
            xhat_ref[rows, b] = xhat.astype(BF16)

    in_stages(tile, [stats, work])
    if edges:
        put_edges(place_ref, outs[5], outs[6], mov_ref, step == 0, step == 1)


def load_window(place_ref, inner, mid, outer, ext_ref, sem, begin=0, end=None):
    rows, core = mid.shape[0], lax.rem(place_ref[0], 2)
    end = rows if end is None else end
    near = pl.multiple_of((1 - core) * (REACH + rows), SUB)
    far = pl.multiple_of(core * (REACH + rows), SUB)
    return [
        pltpu.make_async_copy(inner, ext_ref.at[pl.ds(near, REACH), :], sem.at[0]),
        pltpu.make_async_copy(
            mid.at[begin:end, :], ext_ref.at[REACH + begin : REACH + end, :], sem.at[1]
        ),
        pltpu.make_async_copy(outer, ext_ref.at[pl.ds(far, REACH), :], sem.at[2]),
    ]


def put_edges(place_ref, inner_ref, outer_ref, tile_ref, at_first, at_last):
    rows, core = tile_ref.shape[0], lax.rem(place_ref[0], 2)
    for at, edge, first in ((at_first, slice(0, REACH), 0), (at_last, slice(rows - REACH, rows), 1)):

        @pl.when(at & (core == first))
        def _(edge=edge):
            outer_ref[...] = tile_ref[edge, :]

        @pl.when(at & (core != first))
        def _(edge=edge):
            inner_ref[...] = tile_ref[edge, :]


def fill_taps(taps_ref, ext_ref, mask_ref, start):
    tile = taps_ref.shape[0]
    for j in range(KERNEL_TAPS):
        rows = pl.ds(pl.multiple_of(start + j * DILATION_STEP, DILATION_STEP), tile)
        picked = ext_ref[rows, :]
        if j != MID:
            picked = picked * mask_ref[:, j : j + 1].astype(BF16)
        taps_ref[:, j * INNER : (j + 1) * INNER] = picked


def conv_kernel(
    pieces, rows_of, place_ref, low_ref, mov_ref, high_ref, mask_ref, cot_ref, before_ref, np_ref, *refs
):
    piece_refs = refs[:pieces]
    hid_ref, dconv_ref, inner_ref, outer_ref, sums_ref, turned_ref = refs[pieces : pieces + 6]
    outs = refs[pieces + 6 : pieces + 10]
    ext_ref, wc_ref, wct_ref, wo_ref, wt_ref, taps_ref, pre_ref, dh_ref, xhat_ref = refs[
        pieces + 10 : pieces + 19
    ]
    dt_ref, ht_ref, gc_ref, go_ref, acc_ref, stage1_ref, stage2_ref, sem = refs[pieces + 19 :]
    step, steps = pl.program_id(0), pl.num_programs(0) - 1
    tile = taps_ref.shape[1]
    slot = lax.rem(step, 2)

    @pl.when(step == 0)
    def _():
        me = place_ref[0]
        outs = out_copies(piece_refs, wo_ref, me, sem, 3)
        rest = load_window(place_ref, low_ref, mov_ref, high_ref, ext_ref, sem)
        rest += piece_copies(piece_refs, wc_ref, me, sem, 3 + 2 * pieces)
        for copy in outs + rest:
            copy.start()
        for ref in (acc_ref, gc_ref, go_ref):
            ref[...] = jnp.zeros_like(ref)
        for copy in outs:
            copy.wait()
        for k in range(0, D, 256):
            wt_ref[k : k + 256, :] = jnp.transpose(wo_ref[:, k : k + 256])
        for copy in rest:
            copy.wait()

    def grad_conv(cols):
        def work():
            gc_ref[:, cols] += lax.dot_general(
                dt_ref[...], taps_ref[1 - slot, :, cols], NN, preferred_element_type=F32
            )

        return work

    def grad_out(cols):
        def work():
            go_ref[:, cols] += lax.dot_general(
                ht_ref[...], before_ref[:, cols], NN, preferred_element_type=F32
            )

        return work

    taps_wide = KERNEL_TAPS * INNER
    products = [grad_conv(slice(k, min(k + 768, taps_wide))) for k in range(0, taps_wide, 768)]
    products += [grad_out(slice(k, min(k + 768, D))) for k in range(0, D, 768)]

    def tile_work(products, turned):
        fill_taps(taps_ref.at[slot], ext_ref, mask_ref, step * tile)
        pre_ref[...] = lax.dot_general(
            taps_ref[slot], wc_ref[...], NN, preferred_element_type=F32
        )
        dh_ref[...] = lax.dot_general(cot_ref[...], wt_ref[...], NN, preferred_element_type=F32)
        for n in range(turned):
            tap = jnp.minimum(turned * (step - 1) + n, KERNEL_TAPS - 1)
            source = wc_ref[pl.ds(pl.multiple_of(tap * INNER, SUB), INNER), :]
            target = pl.multiple_of((KERNEL_TAPS - 1 - tap) * INNER, SUB)
            wct_ref[pl.ds(target, INNER), :] = jnp.transpose(source)

        def stats(rows, _):
            return row_stats(pre_ref, rows)

        def work(rows, kept):
            mean, rstd = kept
            sums = [0.0, 0.0]
            for b in lane_blocks(INNER):
                gains = slice(D + INNER + b.start, D + INNER + b.stop)
                gain = np_ref[0:1, gains]
                xhat = (pre_ref[rows, b] - mean) * rstd
                hidden, slope = gelu_and_slope(xhat * gain + np_ref[1:2, gains])
                hid_ref[rows, b] = hidden.astype(BF16)
                dy = dh_ref[rows, b] * slope
                add_terms(acc_ref, b, dy, xhat)
                dxhat = dy * gain
                xhat_ref[rows, b] = xhat
                dh_ref[rows, b] = dxhat
                sums = [sums[0] + dxhat, sums[1] + dxhat * xhat]
            return row_means(sums, INNER) + [rstd]

        def finish(rows, means):
            def put(b, value):
                dconv_ref[rows, b] = value.astype(BF16)

            norm_back(rows, dh_ref, xhat_ref, means, put)

        in_stages(tile, [stats, work, finish], products)
        dt_ref[...] = jnp.transpose(dconv_ref[...])
        ht_ref[...] = jnp.transpose(hid_ref[...])

    @pl.when(step == 0)
    def _():
        tile_work([], 0)

    @pl.when((step > 0) & (step < steps))
    def _():
        tile_work(products, TURNED)

    put_edges(place_ref, inner_ref, outer_ref, dconv_ref, step == 0, step == steps - 1)

    @pl.when(step == steps)
    def _():
        copy = pltpu.make_async_copy(wct_ref, turned_ref, sem.at[4])
        copy.start()
        for work in products:
            work()
        core = lax.rem(place_ref[0], 2)
        _, rows_conv, rows_out = rows_of
        stage_turned(stage1_ref, core, gc_ref, rows_conv, 0, slice(0, CUT // LANE))
        first_tiles = rows_conv // SUB * (CUT // LANE)
        stage_plain(stage1_ref, core, go_ref, rows_out, first_tiles, slice(0, OUT_CUT // LANE))
        copies = stage_copies(stage1_ref, outs[0], outs[1], spans(CHUNKS[0], rows_of)[1], sem, 0)
        for each in copies:
            each.start()
        stage_turned(stage2_ref, core, gc_ref, rows_conv, 0, slice(CUT // LANE, INNER // LANE))
        second_tiles = rows_conv // SUB * ((INNER - CUT) // LANE)
        rest = slice(OUT_CUT // LANE, D // LANE)
        stage_plain(stage2_ref, core, go_ref, rows_out, second_tiles, rest)
        more = stage_copies(stage2_ref, outs[2], outs[3], spans(CHUNKS[1], rows_of)[1], sem, 2)
        for each in more:
            each.start()
        for each in copies + more + [copy]:
            each.wait()
        sums_ref[0:1, :] = jnp.sum(acc_ref[0:8, :], axis=0, keepdims=True)
        sums_ref[1:2, :] = jnp.sum(acc_ref[8:16, :], axis=0, keepdims=True)


def stage_tiles(stage_ref, core, first_row, rows_each, base, block0, blocks, value):
    for g in range(value.shape[0] // SUB):
        row = first_row + g * SUB
        owner, inside = row // rows_each, row % rows_each // SUB
        side = core ^ (owner % 2)
        for b in range(value.shape[1] // LANE):
            tile = value[g * SUB : (g + 1) * SUB, b * LANE : (b + 1) * LANE]
            at = base + inside * blocks + block0 + b
            stage_ref[side, owner // 2, at] = tile.astype(BF16)


def stage_plain(stage_ref, core, grad_ref, rows_each, base, blocks):
    lanes = slice(blocks.start * LANE, blocks.stop * LANE)
    for row in range(0, grad_ref.shape[0], SUB):
        part = grad_ref[row : row + SUB, lanes]
        stage_tiles(stage_ref, core, row, rows_each, base, 0, blocks.stop - blocks.start, part)


def stage_turned(stage_ref, core, turned_ref, rows_each, base, blocks):
    count = blocks.stop - blocks.start
    for row in range(0, turned_ref.shape[1], LANE):
        for b in range(count):
            at = (blocks.start + b) * LANE
            part = jnp.transpose(turned_ref[at : at + LANE, row : row + LANE].astype(BF16))
            stage_tiles(stage_ref, core, row, rows_each, base, b, count, part)


def stage_copies(stage_ref, keep_ref, send_ref, used, sem, first):
    count = stage_ref.shape[2]
    if used < count:
        dims = stage_ref.shape[:2] + (count - used, SUB, LANE)
        stage_ref[:, :, used:] = jnp.zeros(dims, BF16)
    return [
        pltpu.make_async_copy(stage_ref.at[n], ref, sem.at[first + n])
        for n, ref in enumerate((keep_ref, send_ref))
    ]


def back_conv_kernel(
    last, rows_in, place_ref, low_ref, d_ref, high_ref, turned_ref, mask_ref, xhat_ref, rstd_ref, slope_ref, hid_ref, np_ref, *refs
):
    if last:
        before_ref, dpre_ref, sums_ref, keep_ref, send_ref, stage_ref = refs[:6]
    else:
        dpre_ref, sums_ref, part_ref = refs[:3]
    ext_ref, wt_ref, taps_ref, dmov_ref, grad_ref, acc_ref, sem = refs[-7:]
    step, steps = pl.program_id(0), pl.num_programs(0)
    tile = taps_ref.shape[0]
    open_sums(acc_ref)

    @pl.when(step == 0)
    def _():
        half = d_ref.shape[0] // 2
        begin, end = (half - REACH, 2 * half) if last else (0, half + REACH)
        copies = load_window(place_ref, low_ref, d_ref, high_ref, ext_ref, sem, begin, end)
        copies.append(pltpu.make_async_copy(turned_ref, wt_ref, sem.at[3]))
        if last:
            copies.append(pltpu.make_async_copy(before_ref, grad_ref, sem.at[4]))
        for copy in copies:
            copy.start()
        if not last:
            grad_ref[...] = jnp.zeros_like(grad_ref)
        for copy in copies:
            copy.wait()

    fill_taps(taps_ref, ext_ref, mask_ref, (steps * last + step) * tile)
    for half in halves_of(tile):
        dmov_ref[half, :] = lax.dot_general(
            taps_ref[half, :], wt_ref[...], NN, preferred_element_type=F32
        )

    def work(rows, _):
        live = mask_ref[rows, MID : MID + 1]
        sums = [0.0, 0.0]
        for b in lane_blocks(INNER):
            xhat = xhat_ref[rows, b].astype(F32)
            dy = dmov_ref[rows, b] * live * slope_ref[rows, b].astype(F32)
            add_terms(acc_ref, b, dy, xhat)
            dxhat = dy * np_ref[0:1, D + b.start : D + b.stop]
            dmov_ref[rows, b] = dxhat
            sums = [sums[0] + dxhat, sums[1] + dxhat * xhat]
        return row_means(sums, INNER) + [rstd_ref[rows, :]]

    def finish(rows, means):
        def put(b, value):
            dpre_ref[rows, b] = value.astype(BF16)

        norm_back(rows, dmov_ref, xhat_ref, means, put)

    in_stages(tile, [work, finish])
    close_sums(sums_ref, acc_ref)
    grad_ref[...] += lax.dot_general(dpre_ref[...], hid_ref[...], TN, preferred_element_type=F32)

    @pl.when(step == steps - 1)
    def _():
        if last:
            all_blocks = slice(0, INNER // LANE)
            stage_turned(stage_ref, lax.rem(place_ref[0], 2), grad_ref, rows_in, 0, all_blocks)
            used = rows_in // SUB * (INNER // LANE)
            run_copies(stage_copies(stage_ref, keep_ref, send_ref, used, sem, 0))
        else:
            run_copies([pltpu.make_async_copy(grad_ref, part_ref, sem.at[0])])


def back_a_kernel(pieces, half, place_ref, dpre0_ref, dpre1_ref, xhat_ref, rstd_ref, slope_ref, cot_ref, np_ref, *refs):
    piece_refs = refs[:pieces]
    grad_ref, sums_ref, w_ref, wt_ref, dh_ref, acc_ref, sem = refs[-7:]
    open_sums(acc_ref)

    @pl.when(pl.program_id(0) == 0)
    def _():
        run_copies(piece_copies(piece_refs, w_ref, place_ref[0], sem))
        for k in range(0, D, 256):
            wt_ref[:, k : k + 256] = jnp.transpose(w_ref[k : k + 256, :])

    second = (jnp.zeros((1, 1), jnp.int32) + pl.program_id(0)) >= half
    d_pre = jnp.where(second, dpre1_ref[...], dpre0_ref[...])
    dh_ref[...] = lax.dot_general(d_pre, wt_ref[...], NN, preferred_element_type=F32)

    def work(rows, _):
        sums = [0.0, 0.0]
        for b in lane_blocks(D):
            xhat = xhat_ref[rows, b].astype(F32)
            dy = dh_ref[rows, b] * slope_ref[rows, b].astype(F32)
            add_terms(acc_ref, b, dy, xhat)
            dxhat = dy * np_ref[0:1, b]
            dh_ref[rows, b] = dxhat
            sums = [sums[0] + dxhat, sums[1] + dxhat * xhat]
        return row_means(sums, D) + [rstd_ref[rows, :]]

    def finish(rows, means):
        def put(b, value):
            grad_ref[rows, b] = cot_ref[rows, b].astype(F32) + value

        norm_back(rows, dh_ref, xhat_ref, means, put)

    in_stages(dpre0_ref.shape[0], [work, finish])
    close_sums(sums_ref, acc_ref)


def out_kernel(pieces, place_ref, hid_ref, tok_ref, *refs):
    piece_refs = refs[:pieces]
    out_ref, w_ref, sem = refs[pieces:]

    @pl.when(pl.program_id(0) == 0)
    def _():
        run_copies(out_copies(piece_refs, w_ref, place_ref[0], sem))

    branch = lax.dot_general(hid_ref[...], w_ref[...], NN, preferred_element_type=F32)
    out_ref[...] = (tok_ref[...].astype(F32) + branch).astype(BF16)


WIDTHS = (INNER, INNER, D)
LANE0 = (0, INNER, 2 * INNER)
CUT = 2 * LANE
OUT_CUT = 8 * LANE
CHUNKS = (
    ((1, 0, CUT), (2, 0, OUT_CUT)),
    ((1, CUT, INNER - CUT), (2, OUT_CUT, D - OUT_CUT)),
    ((0, 0, INNER),),
)


def spans(chunk, rows):
    found, first = [], 0
    for weight, col, cols in chunk:
        tiles = rows[weight] // SUB * (cols // LANE)
        found.append((weight, col // LANE, cols // LANE, first, tiles))
        first += tiles
    return found, first


def column_sums(pack_ref, row, ref, chunk, rows):
    for weight, block0, blocks, first, tiles in spans(chunk, rows)[0]:

        def body(g, carry, first=first, blocks=blocks):
            new = []
            for b in range(blocks):
                value = ref[first + g * blocks + b].astype(F32)
                new.append(carry[b] + fold(value * value + 1e-30))
            return tuple(new)

        zero = tuple(jnp.zeros((8, LANE), F32) for _ in range(blocks))
        cols = lax.fori_loop(0, tiles // blocks, body, zero, unroll=5)
        for b in range(blocks):
            lane = LANE0[weight] + (block0 + b) * LANE
            pack_ref[row : row + 1, lane : lane + LANE] = jnp.sum(cols[b], axis=0, keepdims=True)


def load_full(refs, place_ref, first, full_ref, sem, at):
    pieces = refs[0].shape[0]
    each = full_ref.shape[0] // (len(refs) * pieces)
    outer = pieces if len(refs) == 2 else pieces // 2
    y = place_ref[2] % 2
    copies = []
    for n, (ref, side) in enumerate(zip(refs, (y, 1 - y))):
        for p in range(pieces):
            index = side * outer + p if len(refs) == 2 else p % 2 * outer + p // 2
            target = full_ref.at[pl.ds(index * each, each)]
            source = ref.at[p, first : first + each]
            copies.append(pltpu.make_async_copy(source, target, sem.at[at + n * pieces + p]))
    return copies


def load_halves(mine_ref, other_ref, place_ref, full_ref, sem):
    y, each = lax.rem(place_ref[2], 2), mine_ref.shape[0]
    return [
        pltpu.make_async_copy(ref, full_ref.at[pl.ds(side * each, each)], sem.at[n])
        for n, (ref, side) in enumerate(((mine_ref, y), (other_ref, 1 - y)))
    ]


PACK_BLOCKS = (D + 2 * INNER) // LANE


def pack_line(pack_ref, row, lane0, width):
    parts = []
    for lane in range(lane0, lane0 + width, LANE):
        at = row * PACK_BLOCKS + lane // LANE
        parts.append(pack_ref[at // SUB, at % SUB : at % SUB + 1, :])
    return jnp.concatenate(parts, axis=1)


def pack_kernel(rows, pieces, place_ref, part_ref, *refs):
    states, sums, (pack_ref, acc_ref) = refs[0:3], refs[3:7], refs[7:9]
    pack_ref[...] = jnp.zeros_like(pack_ref)

    def add(row, lane, value):
        at = row * PACK_BLOCKS + lane // LANE
        pack_ref[at // SUB, at % SUB : at % SUB + 1, :] += value

    lanes_of = ((0, D), (D, D + INNER), (D, D + INNER), (D + INNER, D + 2 * INNER))
    for part, (lane0, lane1) in zip(sums, lanes_of):
        for lane in range(lane0, lane1, LANE):
            for row in range(2):
                add(row, lane, part[row : row + 1, lane - lane0 : lane - lane0 + LANE])
    lanes = lax.broadcasted_iota(jnp.int32, (1, LANE), 1)
    for k in range(3):
        total = jnp.sum(states[k][...].reshape(1, -1), axis=1, keepdims=True)
        add(3, 0, jnp.where(lanes == k, total, 0.0))
    acc_ref[...] = jnp.zeros_like(acc_ref)
    spare = acc_ref.shape[0] - 1
    outer = place_ref[3] // 2
    piece = place_ref[2] % 2 * outer + place_ref[2] // 2
    at = 0
    for chunk, each in zip(CHUNKS[:2], pieces):
        found, _ = spans(chunk, rows)
        start = piece * each

        def body(k, carry, found=found, start=start, at=at):
            n = start + k
            slot = spare
            for weight, block0, blocks, first, tiles in found:
                here = LANE0[weight] // LANE + block0 + lax.rem(jnp.maximum(n - first, 0), blocks)
                slot = jnp.where((n >= first) & (n < first + tiles), here, slot)
            value = part_ref[at + k].astype(F32)
            acc_ref[slot] += value * value + 1e-30
            return carry

        lax.fori_loop(0, each, body, 0, unroll=2)
        at += each
    for slot in range(spare):
        add(2, slot * LANE, jnp.sum(acc_ref[slot], axis=0, keepdims=True))


def pack_in_kernel(rows, place_ref, mine_ref, other_ref, pack_ref, full_ref, sem):
    run_copies(load_halves(mine_ref, other_ref, place_ref, full_ref, sem))
    pack_ref[...] = jnp.zeros_like(pack_ref)
    column_sums(pack_ref, 0, full_ref, CHUNKS[2], rows)


def update_weight(
    k, squares, states_sum, source, weight, state, col_state, grad_ref, new, row_new_ref, col_new_ref, scratch, step=0, steps=1
):
    line_ref, state_ref, new_ref, scaled_ref = scratch
    width, fan, rows_here = WIDTHS[k], (D, KERNEL_TAPS * INNER, INNER)[k], state.shape[0]
    whole_rows = rows_here + -rows_here % LANE
    groups = rows_here // SUB // steps
    rate = 0.5 / fan**0.5

    def before():
        col_new = DECAY * col_state[...].reshape(1, -1) + (1.0 - DECAY) * (squares * (1.0 / fan))
        col_new_ref[...] = col_new.reshape(-1)
        total = DECAY * states_sum
        total = total + (1.0 - DECAY) * (1.0 / width) * jnp.sum(squares, axis=1, keepdims=True)
        scaled_ref[0:1, 0:width] = col_new / (total * (1.0 / fan))
        line_ref[0:1, 0:rows_here] = state[...].reshape(1, -1)
        for c in range(0, whole_rows, LANE):
            state_ref[c : c + LANE, :] = column(line_ref[0:1, c : c + LANE])

    def after():
        for c in range(0, whole_rows, LANE):
            line_ref[0:1, c : c + LANE] = jnp.transpose(new_ref[c : c + LANE, :])[0:1, :]
        row_new_ref[...] = line_ref[0:1, 0:rows_here].reshape(-1)

    def body(g, carry):
        here = pl.ds(pl.multiple_of(g * SUB, SUB), SUB)
        at = step * groups + g
        rows = pl.ds(pl.multiple_of(at * SUB, SUB), SUB)
        square = 0.0
        for ref, block0, blocks, first in source:
            for b in range(blocks):
                value = ref[first + at * blocks + b].astype(F32)
                grad_ref[here, (block0 + b) * LANE : (block0 + b + 1) * LANE] = value
                square = square + (value * value + 1e-30)
        mean = jnp.sum(square, axis=1, keepdims=True) * (1.0 / width)
        row_new = DECAY * state_ref[rows, :] + (1.0 - DECAY) * mean
        new_ref[rows, :] = row_new
        for ref, block0, blocks, first in source:
            for b in range(blocks):
                lanes = slice((block0 + b) * LANE, (block0 + b + 1) * LANE)
                value = ref[first + at * blocks + b].astype(F32)
                change = value * lax.rsqrt(row_new * scaled_ref[0:1, lanes])
                new[here, lanes] = weight[here, lanes] - rate * change
        return carry

    if steps == 1:
        before()
        lax.fori_loop(0, groups, body, 0, unroll=5)
        after()
    else:
        pl.when(step == 0)(before)
        lax.fori_loop(0, groups, body, 0, unroll=5)
        pl.when(step == steps - 1)(after)


def sources_of(chunk, ref, rows):
    return {w: (ref, block0, blocks, first) for w, block0, blocks, first, _ in spans(chunk, rows)[0]}


def update_kernel(rows, copies_of, place_ref, mine_ref, other_ref, pack_ref, *refs):
    weights, states, col_states = refs[0:2], refs[2:4], refs[4:6]
    grads, news, rows_new, cols_new = refs[6:8], refs[8:10], refs[10:12], refs[12:14]
    conv_scratch, out_scratch = refs[14:18], refs[18:22]
    full1_ref, full2_ref, sem = refs[22:25]
    both = (mine_ref, other_ref)
    count = 2 * mine_ref.shape[0]
    step, steps = pl.program_id(0), pl.num_programs(0)

    @pl.when(step == 0)
    def _():
        copies = load_full(both, place_ref, 0, full1_ref, sem, 0)
        copies += load_full(both, place_ref, full1_ref.shape[0] // count, full2_ref, sem, count)
        run_copies(copies)

    from1 = sources_of(CHUNKS[0], full1_ref, rows)
    from2 = sources_of(CHUNKS[1], full2_ref, rows)

    def update(n, k, source, scratch, *steps):
        squares = pack_line(pack_ref, 2, LANE0[k], WIDTHS[k])
        update_weight(
            k, squares, pack_line(pack_ref, 3, 0, LANE)[:, k : k + 1] * (1.0 / copies_of), source, weights[n],
            states[n], col_states[n], grads[n], news[n], rows_new[n], cols_new[n], scratch, *steps,
        )

    update(0, 1, [from1[1], from2[1]], conv_scratch, step, UPDATE_STEPS)

    @pl.when(step == steps - 1)
    def _():
        update(1, 2, [from1[2], from2[2]], out_scratch)


def update_in_kernel(
    rows, copies_of, place_ref, mine_ref, other_ref, pack_in_ref, pack_ref, np_ref, second_ref, *refs
):
    weight, state, col_state, grad_ref, new_ref, row_new_ref, col_new_ref = refs[0:7]
    ngrad_ref, nsecond_ref, nnew_ref = refs[7:10]
    full_ref, sem = refs[14:16]
    copies = load_halves(mine_ref, other_ref, place_ref, full_ref, sem)
    for copy in copies:
        copy.start()
    lines = [pack_line(pack_ref, row, 0, D + 2 * INNER) for row in range(2)]
    grad = jnp.concatenate(lines, axis=0)
    second = DECAY * second_ref[...] + (1.0 - DECAY) * (grad * grad + 1e-30)
    ngrad_ref[...] = grad
    nsecond_ref[...] = second
    nnew_ref[...] = np_ref[...] - 0.2 * grad * lax.rsqrt(second)
    for copy in copies:
        copy.wait()
    update_weight(
        0, pack_in_ref[0:1, :], pack_line(pack_ref, 3, 0, LANE)[:, 0:1] * (1.0 / copies_of),
        [sources_of(CHUNKS[2], full_ref, rows)[0]], weight, state, col_state, grad_ref, new_ref,
        row_new_ref, col_new_ref, refs[10:14],
    )


class Places:
    def __init__(self):
        self.seq, self.fsdp = lax.axis_size("seq"), lax.axis_size("fsdp")
        self.q = lax.axis_index("fsdp")
        self.s = lax.axis_index("seq")

    def flip(self, x, axis, bit):
        pairs = []
        for s in range(self.seq):
            for f in range(self.fsdp):
                s2, f2 = (s ^ bit, f) if axis == "seq" else (s, f ^ bit)
                pairs.append((s * self.fsdp + f, s2 * self.fsdp + f2))
        return lax.ppermute(x, AXES, pairs)


def bits_of(count):
    return [1 << k for k in range(count.bit_length() - 1)]


def tie(x, *others):
    return lax.optimization_barrier((x, *others))[0]


def gather_pieces(piece, place, after, later=()):
    found = {0: piece}
    for bit in reversed(bits_of(place.fsdp)):
        for k in list(found):
            moving = found[k]
            if bit == 1:
                moving = tie(moving, *((after,) if k == 0 or not later else later))
            found[k | bit] = place.flip(moving, "fsdp", bit)
    return [found[k] for k in range(place.fsdp)]


def sum_over(x, place, *axes):
    for axis in axes:
        for bit in bits_of(getattr(place, axis)):
            x = x + place.flip(x, axis, bit)
    return x


def sum_at_once(x, place, axis, bits):
    terms = [x] + [place.flip(x, axis, bits * k) for k in range(1, getattr(place, axis) // bits)]
    while len(terms) > 1:
        terms = [a + b for a, b in zip(terms[::2], terms[1::2])]
    return terms[0]


def pick(x, index, axis):
    return lax.dynamic_index_in_dim(x, index, axis=axis, keepdims=False)


class Reduction:
    def __init__(self, place, keep, send):
        self.place, self.near = place, keep
        self.got = place.flip(send, "fsdp", 1)

    def halve(self, axis, side, flip_axis, bit):
        dims = self.near.shape
        parts = dims[:axis] + (2, dims[axis] // 2) + dims[axis + 1 :]
        near, got = self.near.reshape(parts), self.got.reshape(parts)
        away = pick(near, 1 - side, axis).astype(F32) + pick(got, 1 - side, axis).astype(F32)
        self.near = pick(near, side, axis).astype(F32) + pick(got, side, axis).astype(F32)
        away = away.astype(BF16)
        self.got = self.place.flip(away, flip_axis, bit)
        return away

    def x(self):
        bit = self.place.fsdp // 2
        while bit > 1:
            away = self.halve(0, (self.place.q // bit) % 2, "fsdp", bit)
            bit //= 2
        return away

    def y(self):
        return self.halve(1, self.place.s % 2, "seq", 1)

    def whole_half(self):
        self.near = self.rounded(self.near + self.got.astype(F32))

    def rounded(self, total):
        return lax.optimization_barrier(total.astype(BF16))

    def send_half(self, bit):
        self.got = self.place.flip(self.near, "seq", bit)

    def add_half(self):
        self.near = self.rounded(self.near.astype(F32) + self.got.astype(F32))

    def pieces(self):
        total = (self.near + self.got.astype(F32)).astype(BF16)
        return total.reshape((self.place.seq // 2, -1) + total.shape[2:])


def arrive(result, *reductions):
    result, *gots = lax.optimization_barrier((result, *[r.got for r in reductions]))
    for reduction, got in zip(reductions, gots):
        reduction.got = got
    return result


def summed_f32(got):
    return jnp.sum(got.astype(F32), axis=0)


def summed(got):
    return summed_f32(got).astype(BF16)


def exchange(place, sent):
    line = [[y + 2 * z for z in range(place.seq // 2)] for y in range(2)]
    return lax.all_to_all(sent, "seq", 0, 0, axis_index_groups=line)


def on_device(
    tokens, input_mask, doc_lengths, cotangent, w_in, w_conv, w_out, norm_params,
    row_in, col_in, row_conv, col_conv, row_out, col_out, norm_second,
):
    place = Places()
    rows = tokens.shape[0]
    pieces = place.fsdp
    spots = jnp.stack(
        [place.q, (place.s * place.fsdp + place.q) * rows, place.s, place.seq]
    ).astype(jnp.int32)
    docs = doc_lengths.shape[0]
    live = input_mask.reshape(-1, LANE)
    weights = (w_in, w_conv, w_out)
    rows_of = [w.shape[0] for w in weights]

    tile_a, tile = 256, 512
    steps = rows // tile
    params_spec = whole(2, D + 2 * INNER)
    dma = pltpu.SemaphoreType.DMA

    out_sides = (w_out[:, : D // 2], w_out[:, D // 2 :])
    conv_out = jnp.concatenate([w_conv, *out_sides], axis=0).astype(BF16)
    hidden_a, slope_a, xhat_a, rstd_a = call(
        norm_a_kernel,
        (rows // tile_a,),
        [rows_spec(tile_a, D), params_spec],
        [rows_spec(tile_a, D)] * 3 + [rows_spec(tile_a, LANE)],
        [shape((rows, D), BF16)] * 3 + [shape((rows, LANE), F32)],
        us=17,
    )(tokens, tie(norm_params, conv_out))

    in_pieces = gather_pieces(w_in.astype(BF16), place, hidden_a)

    def in_call(tiles, count, before):
        at, stride = tiles

        def here_spec(width):
            return pl.BlockSpec((tile, width), lambda i: (at + stride * i, 0))

        out_shapes = [shape((rows, INNER), BF16)] * 3 + [shape((rows, LANE), F32)] * 2
        out_specs = [here_spec(INNER)] * 3 + [here_spec(LANE)] * 2
        if at == 0:
            out_shapes += [shape((REACH, INNER), BF16)] * 2
            out_specs += [whole(REACH, INNER)] * 2
        return call(
            functools.partial(in_kernel, pieces, tiles),
            (count,),
            [SMEM, whole(docs), here_spec(D), whole(*live.shape), params_spec]
            + [ANY] * (pieces + len(before)),
            out_specs,
            out_shapes,
            [pltpu.VMEM((D, INNER), BF16), pltpu.VMEM((tile, INNER), F32)]
            + [pltpu.VMEM((8, docs + -docs % LANE), F32), dma((pieces,))],
            us=3,
            aliases={5 + pieces + k: k for k in range(len(before))},
        )(spots, doc_lengths, hidden_a, live, norm_params, *in_pieces, *before)

    *kept, m_first, m_last = in_call((0, steps - 1), 2, ())
    moved, slope_b, xhat_b, rstd_b, masks = in_call((1, 1), steps - 2, kept)

    def halo(inner, outer):
        total = place.seq * place.fsdp
        across = [(i, i + 1 if i % 2 else i - 1) for i in range(1, total - 1)]
        return place.flip(inner, "fsdp", 1), lax.ppermute(outer, AXES, across)

    m_inner, m_outer = halo(m_first, m_last)
    conv_pieces = gather_pieces(conv_out, place, m_first, (moved, m_inner, m_outer))

    ext = pltpu.VMEM((rows + 2 * REACH, INNER), BF16)
    taps_wide = KERNEL_TAPS * INNER
    wide = pltpu.VMEM((taps_wide, INNER), BF16)
    shards = place.fsdp // 2

    def half_dims(chunk):
        count = spans(chunk, rows_of)[1]
        return (shards, count + -count % place.seq, SUB, LANE)

    def tile_spec(width, ahead):
        return pl.BlockSpec((tile, width), lambda i: (jnp.clip(i + ahead, 0, steps - 1), 0))

    halves = [half_dims(CHUNKS[0])] * 2 + [half_dims(CHUNKS[1])] * 2
    work = pltpu.VMEM((tile, INNER), F32)
    turned_tile = pltpu.VMEM((INNER, tile), BF16)
    hidden_c, d_conv, d_first, d_last, sums_c, turned, keep1, send1, keep2, send2 = call(
        functools.partial(conv_kernel, pieces, rows_of),
        (steps + 1,),
        [SMEM, ANY, ANY, ANY, tile_spec(LANE, 0), tile_spec(D, 0), tile_spec(D, -1), params_spec]
        + [ANY] * pieces,
        [tile_spec(INNER, 0)] * 2
        + [whole(REACH, INNER), whole(REACH, INNER), whole(2, INNER)]
        + [ANY] * 5,
        [
            shape((rows, INNER), BF16),
            shape((rows, INNER), BF16),
            shape((REACH, INNER), BF16),
            shape((REACH, INNER), BF16),
            shape((2, INNER), F32),
            shape((taps_wide, INNER), BF16),
        ]
        + [shape(dims, BF16) for dims in halves],
        [ext, wide, wide, pltpu.VMEM((INNER, D), BF16), pltpu.VMEM((D, INNER), BF16)]
        + [pltpu.VMEM((2, tile, taps_wide), BF16), work, work, work, turned_tile, turned_tile]
        + [pltpu.VMEM((INNER, taps_wide), F32), pltpu.VMEM((INNER, D), F32)]
        + [pltpu.VMEM((16, INNER), F32)]
        + [pltpu.VMEM((2,) + halves[0], BF16), pltpu.VMEM((2,) + halves[2], BF16)]
        + [dma((3 + 3 * pieces,))],
        us=45,
    )(
        spots, m_inner, moved, m_outer, masks, cotangent, cotangent, norm_params, *conv_pieces
    )
    d_inner, d_outer = halo(d_first, d_last)
    first, second = Reduction(place, keep1, send1), Reduction(place, keep2, send2)
    (block_out,) = call(
        functools.partial(out_kernel, pieces),
        (steps,),
        [SMEM, rows_spec(tile, INNER), rows_spec(tile, D)] + [ANY] * pieces,
        [rows_spec(tile, D)],
        [shape((rows, D), BF16)],
        [pltpu.VMEM((INNER, D), BF16), dma((2 * pieces,))],
        us=9,
    )(spots, hidden_c, tokens, *conv_pieces)

    def back_conv(last, spots, before):
        here = steps // 2
        at = here * last

        def here_spec(width):
            return pl.BlockSpec((tile, width), lambda i: (i + at, 0))

        dims = half_dims(CHUNKS[2])
        return call(
            functools.partial(back_conv_kernel, last, w_in.shape[0]),
            (here,),
            [SMEM] + [ANY] * 4
            + [here_spec(LANE), here_spec(INNER), here_spec(LANE), here_spec(INNER), here_spec(D)]
            + [params_spec]
            + [ANY] * last,
            [rows_spec(tile, INNER), whole(2, INNER)] + [ANY] * (1 + last),
            [shape((rows // 2, INNER), BF16), shape((2, INNER), F32)]
            + ([shape(dims, BF16)] * 2 if last else [shape((INNER, D), F32)]),
            ([pltpu.VMEM((2,) + dims, BF16)] if last else [])
            + [
                ext,
                wide,
                pltpu.VMEM((tile, taps_wide), BF16),
                pltpu.VMEM((tile, INNER), F32),
                pltpu.VMEM((INNER, D), F32),
                pltpu.VMEM((16, INNER), F32),
                dma((5,)),
            ],
            us=16,
        )(
            spots, d_inner, d_conv, d_outer, turned, masks, xhat_b, rstd_b, slope_b, hidden_a,
            norm_params, *before,
        )

    block_out, d_inner, d_outer = arrive((block_out, d_inner, d_outer), first, second)
    away = (first.x(), second.y())
    d_pre0, sums_b0, grad_part = back_conv(0, tie(spots, *away), ())
    d_pre0 = arrive(d_pre0, first, second)
    away = (first.y(), second.x())
    d_pre1, sums_b1, keep, send = back_conv(1, tie(spots, *away), (grad_part,))
    send = arrive(send, first, second)
    third = Reduction(place, keep, send)
    sent = jnp.concatenate([first.pieces(), second.pieces()], axis=1)
    got = exchange(place, sent)
    third.got = tie(third.got, sent)
    away = (sent, third.x())
    input_grad, sums_a = call(
        functools.partial(back_a_kernel, pieces, steps // 2),
        (steps,),
        [SMEM]
        + [
            pl.BlockSpec((tile, INNER), lambda i: (jnp.minimum(i, steps // 2 - 1), 0)),
            pl.BlockSpec((tile, INNER), lambda i: (jnp.maximum(i - steps // 2, 0), 0)),
        ]
        + [rows_spec(tile, D), rows_spec(tile, LANE), rows_spec(tile, D), rows_spec(tile, D)]
        + [params_spec]
        + [ANY] * pieces,
        [rows_spec(tile, D), whole(2, D)],
        [shape((rows, D), F32), shape((2, D), F32)],
        [
            pltpu.VMEM((D, INNER), BF16),
            pltpu.VMEM((INNER, D), BF16),
            pltpu.VMEM((tile, D), F32),
            pltpu.VMEM((16, D), F32),
            dma((pieces,)),
        ],
        us=17,
    )(
        tie(spots, *away), d_pre0, d_pre1, xhat_a, rstd_a, slope_a, cotangent, norm_params, *in_pieces
    )

    row_states, col_states = (row_in, row_conv, row_out), (col_in, col_conv, col_out)
    row_specs = [whole(*r.shape) for r in row_states]
    col_specs = [whole(*c.shape) for c in col_states]
    cols_all = D + 2 * INNER
    pack_dims = (4 * PACK_BLOCKS // SUB, SUB, LANE)
    pack_spec = whole(*pack_dims)
    fulls = [pltpu.VMEM(half_dims(c)[1:], BF16) for c in CHUNKS]
    sums = (sums_a, sums_b0, sums_b1, sums_c)
    got, third.got, input_grad = lax.optimization_barrier((got, third.got, input_grad))
    part = summed(got)
    sent = jnp.broadcast_to(part[None], (place.seq // 2,) + part.shape)
    mine = exchange(place, sent)
    third.got = tie(third.got, sent)
    away = third.y()
    (pack,) = call(
        functools.partial(pack_kernel, rows_of, [half_dims(c)[1] // place.seq for c in CHUNKS]),
        (1,),
        [SMEM, whole(*part.shape)] + row_specs + [whole(*x.shape) for x in sums],
        [pack_spec],
        [shape(pack_dims, F32)],
        [pltpu.VMEM((cols_all // LANE + 1, SUB, LANE), F32)],
        us=2,
        mib=16,
    )(tie(spots, away), part, *row_states, *sums)
    pack = sum_over(pack, place, "fsdp")
    third.got, pack = lax.optimization_barrier((third.got, pack))
    seq_bits = bits_of(place.seq)
    third.whole_half()
    for bit in seq_bits[1:-1]:
        third.send_half(bit)
        pack = pack + place.flip(pack, "seq", 1) if bit == 2 else pack
        if bit != seq_bits[-2]:
            third.add_half()
    mine, third.got, pack = lax.optimization_barrier((mine, third.got, pack))
    other = place.flip(mine, "seq", 1)
    third.add_half()
    third.send_half(seq_bits[-1])
    pack = sum_at_once(pack, place, "seq", 2)
    third.got, other, pack = lax.optimization_barrier((third.got, other, pack))
    third.add_half()
    line = third.near.reshape(third.near.shape[1:])
    line_other = place.flip(line, "seq", 1)

    def update_scratch(weight):
        lines = weight.shape[0] + -weight.shape[0] % LANE
        return (
            [pltpu.VMEM((8, lines), F32)]
            + [pltpu.VMEM((lines, LANE), F32)] * 2
            + [pltpu.VMEM((8, weight.shape[1]), F32)]
        )

    weight_specs = [whole(*w.shape) for w in weights]
    conv_block = pl.BlockSpec((w_conv.shape[0] // UPDATE_STEPS, INNER), lambda i: (i, 0))
    both_specs = [conv_block, weight_specs[2]]
    results = call(
        functools.partial(update_kernel, rows_of, place.seq),
        (UPDATE_STEPS,),
        [SMEM, ANY, ANY, pack_spec] + both_specs + row_specs[1:] + col_specs[1:],
        both_specs * 2 + row_specs[1:] + col_specs[1:],
        [shape(w.shape, F32) for w in weights[1:]] * 2
        + [shape(r.shape, F32) for r in row_states[1:] + col_states[1:]],
        update_scratch(w_conv)
        + update_scratch(w_out)
        + fulls[:2]
        + [dma((2 * place.seq,))],
        us=8,
        mib=32,
    )(spots, mine, other, pack, *weights[1:], *row_states[1:], *col_states[1:])
    grad_conv, grad_out, new_conv, new_out, row_conv_new, row_out_new, col_conv_new, col_out_new = (
        results
    )
    line_other, grad_out = lax.optimization_barrier((line_other, grad_out))
    (pack_in,) = call(
        functools.partial(pack_in_kernel, rows_of),
        (1,),
        [SMEM, ANY, ANY],
        [whole(8, INNER)],
        [shape((8, INNER), F32)],
        [fulls[2], dma((place.seq,))],
        us=2,
        mib=16,
    )(spots, line, line_other)
    pack_in = sum_at_once(pack_in, place, "fsdp", 1)
    grad_in, new_in, row_in_new, col_in_new, *norm_results = call(
        functools.partial(update_in_kernel, rows_of, place.seq),
        (1,),
        [SMEM, ANY, ANY, whole(8, INNER), pack_spec, params_spec, params_spec]
        + [weight_specs[0], row_specs[0], col_specs[0]],
        [weight_specs[0]] * 2 + [row_specs[0], col_specs[0]] + [params_spec] * 3,
        [shape(w_in.shape, F32)] * 2
        + [shape(row_in.shape, F32), shape(col_in.shape, F32)]
        + [shape((2, cols_all), F32)] * 3,
        update_scratch(w_in) + [fulls[2], dma((place.seq,))],
        us=4,
        mib=24,
    )(
        spots, line, line_other, pack_in, pack, norm_params, norm_second, w_in, row_in, col_in
    )
    return (
        block_out,
        input_grad,
        grad_in,
        grad_conv,
        grad_out,
        new_in,
        new_conv,
        new_out,
        row_in_new,
        col_in_new,
        row_conv_new,
        col_conv_new,
        row_out_new,
        col_out_new,
        *norm_results,
    )


def solution(mesh):
    both, rows = P(AXES, None), P("fsdp", None)
    in_specs = (
        both, P(AXES), P(), both, rows, rows, rows, P(),
        P("fsdp"), P(), P("fsdp"), P(), P("fsdp"), P(), P(),
    )
    out_specs = (
        both, both, rows, rows, rows, rows, rows, rows,
        P("fsdp"), P(), P("fsdp"), P(), P("fsdp"), P(), P(), P(), P(),
    )
    return jax.shard_map(
        on_device, mesh=mesh, in_specs=in_specs, out_specs=out_specs, check_vma=False
    )
```
